32 devices in a mesh: rep: 8 (over z, x), shard: 4 (over y, core).
Axes of the slice: x: 2, y: 2, z: 4, core: 2. Of those that a mesh axis runs over, the one named last changes fastest.
Arguments:
- patches: bfloat16 [192, 196, 768], P(('rep', 'shard')), may hold values from -6 to 6
- labels: int32 [192], P(('rep', 'shard')), may hold values from 0 to 999
- counts: int32 [32], P(('rep', 'shard')), may hold values from 1 to 6, as said below
- patch_w: float32 [768, 384], P('shard'), may hold values from -0.21875 to 0.21875
- layer_in: float32 [3, 384, 3072], P(None, 'shard')
- layer_down: float32 [3, 1536, 384], P(None, 'shard'), may hold values from -0.15625 to 0.15625
- layer_vecs: float32 [3, 4608], replicated
- glob_vecs: float32 [4, 384], replicated
- pos_embed: float32 [197, 384], replicated, may hold values from -3 to 3
- head: float32 [385, 1000], replicated, may hold values from -0.625 to 0.625
- m_patch: float32 [768, 384], P('shard'), may hold values from -3.0517578e-05 to 3.0517578e-05
- v_patch: float32 [768, 384], P('shard'), may hold values from 2e-13 to 3.3e-12
- m_in: float32 [3, 384, 3072], P(None, 'shard'), may hold values from -3.0517578e-05 to 3.0517578e-05
- v_in: float32 [3, 384, 3072], P(None, 'shard'), may hold values from 2e-13 to 3.3e-12
- m_down: float32 [3, 1536, 384], P(None, 'shard'), may hold values from -3.0517578e-05 to 3.0517578e-05
- v_down: float32 [3, 1536, 384], P(None, 'shard'), may hold values from 2e-13 to 3.3e-12
- m_vecs: float32 [3, 4608], replicated, may hold values from -0.00015258789 to 0.00015258789
- v_vecs: float32 [3, 4608], replicated, may hold values from 5e-12 to 8e-11
- m_glob: float32 [4, 384], replicated, may hold values from -0.00015258789 to 0.00015258789
- v_glob: float32 [4, 384], replicated, may hold values from 5e-12 to 8e-11
- m_pos: float32 [197, 384], replicated, may hold values from -1.5258789e-05 to 1.5258789e-05
- v_pos: float32 [197, 384], replicated, may hold values from 4e-14 to 6.5e-13
- m_head: float32 [385, 1000], replicated, may hold values from -6.1035156e-05 to 6.1035156e-05
- v_head: float32 [385, 1000], replicated, may hold values from 8e-13 to 1.3e-11
Outputs:
- loss: float32 [], replicated
- grad_norm: float32 [], replicated
- new_patch_w: float32 [768, 384], P('shard')
- new_m_patch: float32 [768, 384], P('shard')
- new_v_patch: float32 [768, 384], P('shard')
- new_layer_in: float32 [3, 384, 3072], P(None, 'shard')
- new_m_in: float32 [3, 384, 3072], P(None, 'shard')
- new_v_in: float32 [3, 384, 3072], P(None, 'shard')
- new_layer_down: float32 [3, 1536, 384], P(None, 'shard')
- new_m_down: float32 [3, 1536, 384], P(None, 'shard')
- new_v_down: float32 [3, 1536, 384], P(None, 'shard')
- new_layer_vecs: float32 [3, 4608], replicated
- new_m_vecs: float32 [3, 4608], replicated
- new_v_vecs: float32 [3, 4608], replicated
- new_glob_vecs: float32 [4, 384], replicated
- new_m_glob: float32 [4, 384], replicated
- new_v_glob: float32 [4, 384], replicated
- new_pos_embed: float32 [197, 384], replicated
- new_m_pos: float32 [197, 384], replicated
- new_v_pos: float32 [197, 384], replicated
- new_head: float32 [385, 1000], replicated
- new_m_head: float32 [385, 1000], replicated
- new_v_head: float32 [385, 1000], replicated
The draws below stay inside these ranges and needn't reach their ends.
Inputs may be any that keep to these rules, and one draw needn't show every extreme that they name: `counts`: the last device of the flattened rep, shard order always holds 6 live images; devices of the lower half of that order hold at most 2, those of the upper half at least 3.
All inputs are finite; a program needn't handle non-finite values.
Results may differ from the reference program's by a relative error of at most 0.019.
Values may be sent and summed in bfloat16 or wider, within the bound.
A program may use at most 160 MiB of HBM per device.

```python
import math
import jax
import jax.numpy as jnp
from jax import lax

D = 384
HEADS = 6
HEAD_DIM = 64
FF = 1536
PATCH_DIM = 768
PATCHES = 196
NCLS = 1000
LAYERS = 3
SLOTS = 6
SEQ = 197
IMAGES = 192
N_REP = 8
N_SHARD = 4


def draw_counts(key, part):
    devices = N_REP * N_SHARD
    lower_key = jax.random.fold_in(key, 11)
    upper_key = jax.random.fold_in(key, 23)
    lower = jax.random.randint(lower_key, (devices,), 1, max(1, SLOTS // 3) + 1)
    upper = jax.random.randint(upper_key, (devices,), SLOTS // 2, SLOTS + 1)
    position = jnp.arange(devices)
    values = jnp.where(position < devices // 2, lower, upper)
    return values.at[devices - 1].set(SLOTS).astype(jnp.int32)


def draw_layer_in(key, part):
    columns = 4 * D + FF
    base = jax.random.normal(key, (LAYERS, D, columns), jnp.float32) * D ** (-0.5)
    column = jnp.arange(columns)
    factor = jnp.where(column < 2 * D, 1.4, jnp.where(column < 3 * D, 1.0, jnp.where(column < 4 * D, 3.0, 1.0)))
    return base * factor


def draw_layer_vecs(key, part):
    width = 8 * D + FF
    base = jax.random.normal(key, (LAYERS, width), jnp.float32) * 0.3
    column = jnp.arange(width)
    gains = jnp.logical_or(column < D, jnp.logical_and(column >= 5 * D, column < 6 * D)).astype(jnp.float32)
    return base + gains


def draw_glob_vecs(key, part):
    base = jax.random.normal(key, (4, D), jnp.float32)
    spread = jnp.array([0.3, 1.0, 0.3, 0.3], jnp.float32)
    offset = jnp.array([0.0, 0.0, 1.0, 0.0], jnp.float32)
    return base * spread[:, None] + offset[:, None]


def place_ends(drawn, rng, smallest, top_value):
    index_at = [jax.random.randint(jax.random.fold_in(rng, axis), (), 0, length) for axis, length in enumerate(drawn.shape)]
    main_axis = drawn.shape.index(max(drawn.shape))
    neighbour = index_at[:main_axis] + [(index_at[main_axis] + 1) % drawn.shape[main_axis]] + index_at[main_axis + 1:]
    return drawn.at[tuple(index_at)].set(smallest).at[tuple(neighbour)].set(top_value)


def block_levels(key, shape, split, smallest, top_value):
    def one(dim, blocks):
        draws = jax.random.uniform(jax.random.fold_in(jax.random.fold_in(key, 6), dim), (blocks,), jnp.float32, smallest / len(split), top_value / len(split))
        return jnp.repeat(jnp.exp(draws), shape[dim] // blocks).reshape((-1,) + (1,) * (len(shape) - dim - 1))

    level = one(*split[0])
    for cut in split[1:]:
        level = level * one(*cut)
    return level


def noise(key, shape, scale, bound, pieces=(), kind=jnp.bfloat16):
    loudness = block_levels(key, shape, pieces, -0.22, 0.18) if pieces else 1.0
    entries = jax.random.normal(key, shape, jnp.float32) * scale * loudness
    return jnp.minimum(jnp.maximum(entries, -bound), bound).astype(kind)


def setup_inputs(seed: int = 0) -> dict:
    key_list = jax.random.split(jax.random.key(seed), 25)
    patches = noise(key_list[0], (IMAGES, PATCHES, PATCH_DIM), 1.0, 6.0, ((0, 32),))
    labels = place_ends(jax.random.randint(key_list[1], (IMAGES,), 0, NCLS), jax.random.fold_in(key_list[1], 1), 0, NCLS - 1).astype(jnp.int32)
    counts = draw_counts(jax.random.fold_in(key_list[24], 71), 0)
    patch_w = noise(key_list[3], (PATCH_DIM, D), PATCH_DIM ** -0.5, 0.21875, ((0, 4),), jnp.float32)
    layer_in = draw_layer_in(jax.random.fold_in(key_list[24], 71), 0)
    layer_down = noise(key_list[5], (LAYERS, FF, D), FF ** -0.5, 0.15625, ((1, 4),), jnp.float32)
    layer_vecs = draw_layer_vecs(jax.random.fold_in(key_list[24], 71), 0)
    glob_vecs = draw_glob_vecs(jax.random.fold_in(key_list[24], 71), 0)
    pos_embed = noise(key_list[8], (SEQ, D), 0.5, 3.0, (), jnp.float32)
    head = noise(key_list[9], (D + 1, NCLS), (D // 4) ** -0.5, 0.625, (), jnp.float32)
    m_patch = noise(key_list[10], (PATCH_DIM, D), (2.3e-6), 3.0517578125e-05, ((0, 4),), jnp.float32)
    v_patch = jnp.clip(jnp.exp(math.log(3.3000000301819377e-12) - 2.8033604 * jax.random.uniform(key_list[11], (PATCH_DIM, D), jnp.float32) ** block_levels(key_list[11], (PATCH_DIM, D), ((0, 4),), -0.2, 0.2)), 1.99999996490334e-13, 3.3000000301819377e-12)
    m_in = noise(key_list[12], (LAYERS, D, 4 * D + FF), (2.3e-6), 3.0517578125e-05, ((1, 4),), jnp.float32)
    v_in = jnp.clip(jnp.exp(math.log(3.3000000301819377e-12) - 2.8033604 * jax.random.uniform(key_list[13], (LAYERS, D, 4 * D + FF), jnp.float32) ** block_levels(key_list[13], (LAYERS, D, 4 * D + FF), ((1, 4),), -0.2, 0.2)), 1.99999996490334e-13, 3.3000000301819377e-12)
    m_down = noise(key_list[14], (LAYERS, FF, D), (2.3e-6), 3.0517578125e-05, ((1, 4),), jnp.float32)
    v_down = jnp.clip(jnp.exp(math.log(3.3000000301819377e-12) - 2.8033604 * jax.random.uniform(key_list[15], (LAYERS, FF, D), jnp.float32) ** block_levels(key_list[15], (LAYERS, FF, D), ((1, 4),), -0.2, 0.2)), 1.99999996490334e-13, 3.3000000301819377e-12)
    m_vecs = noise(key_list[16], (LAYERS, 8 * D + FF), (1.1e-5), 0.00015258789, (), jnp.float32)
    v_vecs = jnp.clip(jnp.exp(jax.random.uniform(key_list[17], (LAYERS, 8 * D + FF), jnp.float32, math.log(4.999999980020986e-12), math.log(7.999999968033578e-11))), 4.999999980020986e-12, 7.999999968033578e-11)
    m_glob = noise(key_list[18], (4, D), (1.1e-5), 0.00015258789, (), jnp.float32)
    v_glob = jnp.clip(jnp.exp(jax.random.uniform(key_list[19], (4, D), jnp.float32, math.log(4.999999980020986e-12), math.log(7.999999968033578e-11))), 4.999999980020986e-12, 7.999999968033578e-11)
    m_pos = noise(key_list[20], (SEQ, D), (1.0e-6), 1.52587890625e-05, (), jnp.float32)
    v_pos = jnp.clip(jnp.exp(jax.random.uniform(key_list[21], (SEQ, D), jnp.float32, math.log(3.99999992980668e-14), math.log(6.500000190867716e-13))), 3.99999992980668e-14, 6.500000190867716e-13)
    m_head = noise(key_list[22], (D + 1, NCLS), (4.6e-6), 6.103515625e-05, (), jnp.float32)
    v_head = jnp.clip(jnp.exp(jax.random.uniform(key_list[23], (D + 1, NCLS), jnp.float32, math.log(7.99999985961336e-13), math.log(1.3000000381735433e-11))), 7.99999985961336e-13, 1.3000000381735433e-11)
    return {"patches": patches, "labels": labels, "counts": counts, "patch_w": patch_w, "layer_in": layer_in, "layer_down": layer_down, "layer_vecs": layer_vecs, "glob_vecs": glob_vecs, "pos_embed": pos_embed, "head": head, "m_patch": m_patch, "v_patch": v_patch, "m_in": m_in, "v_in": v_in, "m_down": m_down, "v_down": v_down, "m_vecs": m_vecs, "v_vecs": v_vecs, "m_glob": m_glob, "v_glob": v_glob, "m_pos": m_pos, "v_pos": v_pos, "m_head": m_head, "v_head": v_head}


@jax.custom_vjp
def low(v):
    return lax.optimization_barrier(v.astype(jnp.bfloat16)).astype(jnp.float32)

@jax.custom_vjp
def low_back(v):
    return v

def low_keep(v):
    return (low(v), None)

def low_pass(kept, grad):
    return (grad,)

def back_keep(v):
    return (v, None)

def back_low(kept, grad):
    return (low(grad),)
low.defvjp(low_keep, low_pass)
low_back.defvjp(back_keep, back_low)
HIGHEST = lax.Precision.HIGHEST
NORM_EPS = 1e-06
SMOOTHING = 0.1
CLIP_NORM = 0.05
LEARNING_RATE = 0.05
VECTOR_RATE = 0.5
BETA_FIRST = 0.9
BETA_SECOND = 0.999
ADAM_EPS = 1e-08
WEIGHT_DECAY = 0.05
ADAM_STEP = 10
GROUP_IMAGES = 16

def both_round(values):
    return low(low_back(values))

def product(left, right):
    return jnp.dot(left, right, precision=HIGHEST)

def layer_norm(values, gain, shift):
    centre = values - lax.optimization_barrier(jnp.mean(values, axis=-1, keepdims=True))
    spread = lax.optimization_barrier(jnp.mean(centre * centre, axis=-1, keepdims=True))
    return centre * lax.rsqrt(spread + NORM_EPS) * gain + shift

def layer_forward(stream, w_in, w_down, vectors, images):
    gain_one = vectors[0:D]
    shift_one = vectors[D:2 * D]
    bias_query = vectors[2 * D:3 * D]
    bias_value = vectors[3 * D:4 * D]
    bias_out = vectors[4 * D:5 * D]
    gain_two = vectors[5 * D:6 * D]
    shift_two = vectors[6 * D:7 * D]
    bias_up = vectors[7 * D:7 * D + FF]
    bias_down = vectors[7 * D + FF:]
    normed = low(layer_norm(stream, gain_one, shift_one))
    bias_qkv = jnp.concatenate([bias_query, jnp.zeros_like(bias_query), bias_value])
    joined = both_round(product(normed, w_in[:, :3 * D]) + bias_qkv)
    joined = joined.reshape(images, SEQ, 3, HEADS, HEAD_DIM)
    query, keys, values = (joined[:, :, 0], joined[:, :, 1], joined[:, :, 2])
    scores = low_back(jnp.einsum('bqhd,bkhd->bhqk', query, keys, precision=HIGHEST) * HEAD_DIM ** (-0.5))
    weights = low(jax.nn.softmax(scores, axis=-1))
    heads_out = jnp.einsum('bhqk,bkhd->bqhd', weights, values, precision=HIGHEST)
    heads_out = both_round(heads_out.reshape(images * SEQ, D))
    stream = stream + low_back(product(heads_out, w_in[:, 3 * D:4 * D])) + bias_out
    normed_two = low(layer_norm(stream, gain_two, shift_two))
    hidden = low_back(product(normed_two, w_in[:, 4 * D:]) + bias_up)
    active = low(jax.nn.gelu(hidden, approximate=True))
    return stream + low_back(product(active, w_down)) + bias_down

def group_loss(patch_low, in_low, down_low, layer_vecs, glob_vecs, pos_embed, head_low, head_bias, pixels, labels, alive):
    images = pixels.shape[0]
    embedded = low_back(product(pixels.reshape(-1, PATCH_DIM), patch_low)).reshape(images, PATCHES, D) + glob_vecs[0]
    leading = jnp.broadcast_to(glob_vecs[1], (images, 1, D))
    stream = (jnp.concatenate([leading, embedded], axis=1) + pos_embed).reshape(images * SEQ, D)
    for layer_index in range(LAYERS):
        stream = layer_forward(stream, in_low[layer_index], down_low[layer_index], layer_vecs[layer_index], images)
    first = stream.reshape(images, SEQ, D)[:, 0]
    final = low(layer_norm(first, glob_vecs[2], glob_vecs[3]))
    logits = low_back(product(final, head_low) + head_bias)
    log_probs = jax.nn.log_softmax(logits, axis=-1)
    picked = jnp.take_along_axis(log_probs, labels[:, None], axis=1)[:, 0]
    per_image = -(1.0 - SMOOTHING) * picked - SMOOTHING * lax.optimization_barrier(jnp.mean(log_probs, axis=1))
    return jnp.sum(per_image * alive)

def adam_update(weight, first, second, grad, factor, rate):
    grad = grad * factor
    first = BETA_FIRST * first + (1.0 - BETA_FIRST) * grad
    second = BETA_SECOND * second + (1.0 - BETA_SECOND) * grad * grad
    first_hat = first / (1.0 - BETA_FIRST ** ADAM_STEP)
    second_hat = second / (1.0 - BETA_SECOND ** ADAM_STEP)
    weight = weight - rate * (first_hat / (jnp.sqrt(second_hat) + ADAM_EPS) + WEIGHT_DECAY * weight)
    return (weight, first, second)

def reference(patches, labels, counts, patch_w, layer_in, layer_down, layer_vecs, glob_vecs, pos_embed, head, m_patch, v_patch, m_in, v_in, m_down, v_down, m_vecs, v_vecs, m_glob, v_glob, m_pos, v_pos, m_head, v_head):
    images = patches.shape[0]
    index = jnp.arange(images, dtype=jnp.int32)
    alive = (index % SLOTS < counts[index // SLOTS]).astype(jnp.float32)
    image_sum = jnp.sum(counts).astype(jnp.float32)
    groups = images // GROUP_IMAGES
    pixels = patches.astype(jnp.float32).reshape(groups, GROUP_IMAGES, PATCHES, PATCH_DIM)
    group_labels = labels.reshape(groups, GROUP_IMAGES)
    group_alive = alive.reshape(groups, GROUP_IMAGES)

    def objective(p_w, l_in, l_down, l_vecs, g_vecs, p_embed, hd):
        patch_low = low(p_w)
        in_low = low(l_in)
        down_low = low(l_down)
        head_low = low(hd[:D])
        head_bias = hd[D]

        def step(carry, group):
            part = group_loss(patch_low, in_low, down_low, l_vecs, g_vecs, p_embed, head_low, head_bias, group[0], group[1], group[2])
            return (carry + part, None)
        summed, unused = lax.scan(jax.checkpoint(step), jnp.zeros((), jnp.float32), (pixels, group_labels, group_alive))
        return summed / image_sum
    weights = (patch_w, layer_in, layer_down, layer_vecs, glob_vecs, pos_embed, head)
    loss, pullback = jax.vjp(objective, *weights)
    grads = pullback(jnp.ones((), jnp.float32))
    squares = jnp.zeros((), jnp.float32)
    for grad in grads:
        squares = squares + jnp.sum(grad * grad)
    grad_norm = jnp.sqrt(squares)
    factor = jnp.minimum(1.0, CLIP_NORM / grad_norm)
    states = ((m_patch, v_patch), (m_in, v_in), (m_down, v_down), (m_vecs, v_vecs), (m_glob, v_glob), (m_pos, v_pos), (m_head, v_head))
    rates = (LEARNING_RATE, LEARNING_RATE, LEARNING_RATE, VECTOR_RATE, VECTOR_RATE, VECTOR_RATE, LEARNING_RATE)
    results = []
    for weight, grad, state, rate in zip(weights, grads, states, rates):
        results.extend(adam_update(weight, state[0], state[1], grad, factor, rate))
    return (loss, grad_norm, results[0], results[1], results[2], results[3], results[4], results[5], results[6], results[7], results[8], results[9], results[10], results[11], results[12], results[13], results[14], results[15], results[16], results[17], results[18], results[19], results[20])
```

```python
import functools

import jax
import jax.numpy as jnp
from jax import lax
from jax.experimental import pallas as pl
from jax.experimental.pallas import tpu as pltpu
from jax.sharding import PartitionSpec as P

D = 384
HEADS = 6
HEAD_DIM = 64
FF = 1536
PATCH_DIM = 768
PATCHES = 196
NCLS = 1000
LAYERS = 3
SEQ = 197

BLK = 208
CLS = 200
TAIL = 192
KEPT = 4
ROWS = KEPT * BLK
HALF = 2 * BLK
CROWS = KEPT * 16
CPAD = 1024
WIDE = 8 * D + FF

NORM_EPS = 1e-06
SMOOTHING = 0.1
CLIP_NORM = 0.05
LEARNING_RATE = 0.05
VECTOR_RATE = 0.5
BETA_FIRST = 0.9
BETA_SECOND = 0.999
ADAM_EPS = 1e-08
WEIGHT_DECAY = 0.05
ADAM_STEP = 10
GELU_SCALE = 0.7978845608028654
GELU_CUBIC = 0.044715

F32 = jnp.float32
BF = jnp.bfloat16


def mm(left, right):
    return jnp.dot(left, right, preferred_element_type=F32)


def mm_nt(left, right):
    return lax.dot_general(left, right, (((1,), (1,)), ((), ())), preferred_element_type=F32)


def mm_tn(left, right):
    return lax.dot_general(left, right, (((0,), (0,)), ((), ())), preferred_element_type=F32)


def fold(values):
    return jnp.sum(values.reshape(-1, 8, values.shape[-1]), axis=0)


def down_sum(values):
    return jnp.sum(values, axis=0, keepdims=True)


def norm(values):
    centre = values - jnp.mean(values, axis=-1, keepdims=True)
    inverse = lax.rsqrt(jnp.mean(centre * centre, axis=-1, keepdims=True) + NORM_EPS)
    return centre * inverse, inverse


def norm_back(upstream, normed, inverse, gain):
    scaled = upstream * gain
    first = jnp.mean(scaled, axis=-1, keepdims=True)
    second = jnp.mean(scaled * normed, axis=-1, keepdims=True)
    return inverse * (scaled - first - normed * second)


def gelu_parts(hidden):
    square = hidden * hidden
    tangent = jnp.tanh(hidden * (GELU_SCALE + (GELU_SCALE * GELU_CUBIC) * square))
    share = 0.5 + 0.5 * tangent
    active = hidden * share
    inner = (2.0 * GELU_SCALE) + (6.0 * GELU_SCALE * GELU_CUBIC) * square
    slope = share + active * (1.0 - share) * inner
    return active, slope


def lane_mask(width, low, high):
    lane = lax.broadcasted_iota(jnp.int32, (1, width), 1)
    return jnp.where((lane >= low) & (lane < high), 1.0, 0.0).astype(BF)


STEP = 32


def pieces(total):
    return [(at, min(STEP, total - at)) for at in range(0, total, STEP)]


def compute(
    pix, wp, win, wdn, vecs, glob, addend, head, hbias, lab,
    gin, gdn, gkv, gpatch, gvec, gfin, gpos, left, right,
    X, N1, H1, I1, QKV, ATT, N2, H2, I2, ACT, SLOPE,
    DXB, DH, DMB, DA, DQKV, KV, SUMS,
):
    even = lane_mask(128, 0, 64)
    odd = lane_mask(128, 64, 128)
    low_lane = lax.broadcasted_iota(jnp.int32, (1, 128), 1) < 64
    key_lane = lax.broadcasted_iota(jnp.int32, (1, BLK), 1)
    key_row = jnp.where((key_lane < PATCHES) | (key_lane == CLS), 0.0, -1e30)
    key_sub = lax.broadcasted_iota(jnp.int32, (BLK, 1), 0)
    key_column = jnp.where((key_sub < PATCHES) | (key_sub == CLS), 0.0, -1e30)

    def vector(layer, at, size):
        return vecs[layer, :, at : at + size]

    def embed(half, carry):
        rows = pl.ds(pl.multiple_of(half * HALF, HALF), HALF)
        made = mm(pix[rows, :], wp[...])
        for image in range(2):
            for at, size in pieces(BLK):
                start = pl.multiple_of(half * HALF + image * BLK + at, 16)
                X[pl.ds(start, size), :] = (
                    made[image * BLK + at : image * BLK + at + size] + addend[at : at + size, :]
                )
        return carry

    lax.fori_loop(0, 2, embed, 0)

    def first_norm(layer, half, columns):
        base = half * HALF
        gain, shift = vector(layer, 0, D), vector(layer, D, D)
        for at, size in pieces(HALF):
            rows = pl.ds(pl.multiple_of(base + at, 16), size)
            normed, inverse = norm(X[rows, :])
            N1[layer, rows, :] = normed.astype(BF)
            I1[layer, rows, :] = jnp.broadcast_to(inverse, (size, 128))
            H1[layer, rows, :] = (normed * gain + shift).astype(BF)
        rows = pl.ds(pl.multiple_of(base, HALF), HALF)
        h1 = H1[layer, rows, :]
        for tile in columns:
            made = mm(h1, win[layer, :, tile * D : (tile + 1) * D])
            if tile == 0:
                made = made + vector(layer, 2 * D, D)
            if tile == 2:
                made = made + vector(layer, 3 * D, D)
            if len(columns) == 3:
                QKV[layer, rows, tile * D : (tile + 1) * D] = made.astype(BF)
            else:
                KV[rows, (tile - 1) * D : tile * D] = made.astype(BF)

    def attend(layer, image):
        rows = pl.ds(pl.multiple_of(image * BLK, BLK), BLK)
        for pair in range(3):
            at = pair * 128
            query = QKV[layer, rows, at : at + 128] * BF(0.125)
            keys = QKV[layer, rows, D + at : D + at + 128]
            values = QKV[layer, rows, 2 * D + at : 2 * D + at + 128]
            both = jnp.concatenate([query * even, query * odd], axis=0)
            scores = mm_nt(both, keys) + key_row
            top = jnp.max(scores, axis=-1, keepdims=True)
            raw = jnp.exp(scores - top)
            probs = (raw * (1.0 / jnp.sum(raw, axis=-1, keepdims=True))).astype(BF)
            made = mm(probs[:BLK], values * even) + mm(probs[BLK:], values * odd)
            ATT[layer, rows, at : at + 128] = made.astype(BF)

    def mlp(layer, half):
        base = half * HALF
        whole = pl.ds(pl.multiple_of(base, HALF), HALF)
        made = mm(ATT[layer, whole, :], win[layer, :, 3 * D : 4 * D])
        bias_out = vector(layer, 4 * D, D)
        gain, shift = vector(layer, 5 * D, D), vector(layer, 6 * D, D)
        for at, size in pieces(HALF):
            rows = pl.ds(pl.multiple_of(base + at, 16), size)
            middle = X[rows, :] + made[at : at + size] + bias_out
            X[rows, :] = middle
            normed, inverse = norm(middle)
            N2[layer, rows, :] = normed.astype(BF)
            I2[layer, rows, :] = jnp.broadcast_to(inverse, (size, 128))
            H2[layer, rows, :] = (normed * gain + shift).astype(BF)
        h2 = H2[layer, whole, :]
        for tile in range(4):
            columns = slice(tile * D, (tile + 1) * D)
            made = mm(h2, win[layer, :, (4 + tile) * D : (5 + tile) * D])
            bias = vector(layer, 7 * D + tile * D, D)
            for at, size in pieces(HALF):
                rows = pl.ds(pl.multiple_of(base + at, 16), size)
                active, slope = gelu_parts(made[at : at + size] + bias)
                ACT[layer, rows, columns] = active.astype(BF)
                SLOPE[layer, rows, columns] = slope.astype(BF)
        made = mm(ACT[layer, whole, :], wdn[layer])
        bias = vector(layer, 7 * D + FF, D)
        for at, size in pieces(HALF):
            rows = pl.ds(pl.multiple_of(base + at, 16), size)
            X[rows, :] = X[rows, :] + made[at : at + size] + bias

    def forward(layer, carry):
        def one(half, c):
            first_norm(layer, half, (0, 1, 2))
            return c

        lax.fori_loop(0, 2, one, 0)

        def two(image, c):
            attend(layer, image)
            return c

        lax.fori_loop(0, KEPT, two, 0)

        def three(half, c):
            mlp(layer, half)
            return c

        lax.fori_loop(0, 2, three, 0)
        return carry

    lax.fori_loop(0, LAYERS - 1, forward, 0)

    last = LAYERS - 1

    def last_norm(half, c):
        first_norm(last, half, (1, 2))
        return c

    lax.fori_loop(0, 2, last_norm, 0)

    def tails(ref, layer=None):
        found = []
        for image in range(KEPT):
            rows = slice(image * BLK + TAIL, (image + 1) * BLK)
            found.append(ref[rows, :] if layer is None else ref[layer, rows, :])
        return jnp.concatenate(found, axis=0)

    h1 = tails(H1, last)
    stream = tails(X)
    query = ((mm(h1, win[last, :, 0:D]) + vector(last, 2 * D, D)).astype(BF)) * BF(0.125)
    head_masks = [lane_mask(D, head * 64, (head + 1) * 64) for head in range(HEADS)]

    def spread(values):
        return jnp.concatenate([values * mask for mask in head_masks], axis=0)

    def gather_heads(values):
        total = None
        for index in range(HEADS):
            part = values[index * 16 : (index + 1) * 16] * head_masks[index].astype(F32)
            total = part if total is None else total + part
        return total

    spread_queries, probabilities, outs = [], [], []
    for image in range(KEPT):
        rows = slice(image * BLK, (image + 1) * BLK)
        queries = spread(query[image * 16 : (image + 1) * 16])
        scores = mm_nt(queries, KV[rows, 0:D]) + key_row
        raw = jnp.exp(scores - jnp.max(scores, axis=-1, keepdims=True))
        probs = raw * (1.0 / jnp.sum(raw, axis=-1, keepdims=True))
        spread_queries.append(queries)
        probabilities.append(probs)
        outs.append(gather_heads(mm(probs.astype(BF), KV[rows, D : 2 * D])))
    attended = jnp.concatenate(outs, axis=0).astype(BF)
    middle = stream + mm(attended, win[last, :, 3 * D : 4 * D]) + vector(last, 4 * D, D)
    n2, i2 = norm(middle)
    h2 = (n2 * vector(last, 5 * D, D) + vector(last, 6 * D, D)).astype(BF)
    active, slope = gelu_parts(mm(h2, win[last, :, 4 * D :]) + vector(last, 7 * D, FF))
    active = active.astype(BF)
    top = middle + mm(active, wdn[last]) + vector(last, 7 * D + FF, D)
    gain_final = glob[2:3, :]
    nf, inf = norm(top)
    final = (nf * gain_final + glob[3:4, :]).astype(BF)
    class_lane = lax.broadcasted_iota(jnp.int32, (1, CPAD), 1)
    logits = mm(final, head[...]) + hbias[...]
    logits = jnp.where(class_lane < NCLS, logits, -1e30)
    peak = jnp.max(logits, axis=-1, keepdims=True)
    shifted = logits - peak
    raw = jnp.exp(shifted)
    total = jnp.sum(raw, axis=-1, keepdims=True)
    log_total = jnp.log(total)
    labels = lab[...]
    alive = jnp.where(labels >= 0, 1.0, 0.0)
    target = jnp.where(class_lane == labels, 1.0 - SMOOTHING, 0.0) + jnp.where(
        class_lane < NCLS, SMOOTHING / NCLS, 0.0
    )
    log_probs = jnp.where(class_lane < NCLS, shifted - log_total, 0.0)
    losses = -jnp.sum(target * log_probs, axis=-1, keepdims=True) * alive
    d_logits = ((raw * (1.0 / total) - target) * alive).astype(BF)
    d_final = mm_nt(d_logits, head[...])
    gfin[:, 0:D] = down_sum(d_final * nf)
    gfin[:, D : 2 * D] = down_sum(d_final)
    gfin[:, 2 * D : 2 * D + 128] = jnp.broadcast_to(down_sum(losses), (1, 128))
    d_top = norm_back(d_final, nf, inf, gain_final)
    low_top = d_top.astype(BF)
    gvec[last, :, 7 * D + FF :] = down_sum(d_top)
    d_up = (mm_nt(low_top, wdn[last]) * slope).astype(BF)
    gvec[last, :, 7 * D : 7 * D + FF] = down_sum(d_up.astype(F32))
    d_h2 = mm_nt(d_up, win[last, :, 4 * D :])
    gvec[last, :, 5 * D : 6 * D] = down_sum(d_h2 * n2)
    gvec[last, :, 6 * D : 7 * D] = down_sum(d_h2)
    d_middle = d_top + norm_back(d_h2, n2, i2, vector(last, 5 * D, D))
    low_middle = d_middle.astype(BF)
    gvec[last, :, 4 * D : 5 * D] = down_sum(d_middle)
    d_heads = mm_nt(low_middle, win[last, :, 3 * D : 4 * D]).astype(BF)
    d_queries = []
    for image in range(KEPT):
        rows = slice(image * BLK, (image + 1) * BLK)
        ups = spread(d_heads[image * 16 : (image + 1) * 16])
        probs = probabilities[image]
        d_probs = mm_nt(ups, KV[rows, D : 2 * D])
        inner = jnp.sum(d_probs * probs, axis=-1, keepdims=True)
        d_scores = (probs * (d_probs - inner)).astype(BF)
        d_queries.append(gather_heads(mm(d_scores, KV[rows, 0:D])) * 0.125)
        DQKV[rows, D : 2 * D] = mm_tn(d_scores, spread_queries[image]).astype(BF)
        DQKV[rows, 2 * D : 3 * D] = mm_tn(probs.astype(BF), ups).astype(BF)
    d_query = jnp.concatenate(d_queries, axis=0).astype(BF)
    gvec[last, :, 2 * D : 3 * D] = down_sum(d_query.astype(F32))
    from_query = mm_nt(d_query, win[last, :, 0:D])

    left[:, 0:FF] = active
    left[:, FF : FF + D] = h2
    left[:, FF + D : FF + 2 * D] = attended
    left[:, FF + 2 * D : FF + 3 * D] = h1
    left[:, FF + 3 * D : FF + 4 * D] = final
    right[:, 0:D] = low_top
    right[:, D : D + FF] = d_up
    right[:, D + FF : 2 * D + FF] = low_middle
    right[:, 2 * D + FF : 3 * D + FF] = d_query
    right[:, 3 * D + FF :] = d_logits

    X[...] = jnp.zeros((ROWS, D), F32)
    for image in range(KEPT):
        X[image * BLK + TAIL : (image + 1) * BLK, :] = d_middle[image * 16 : (image + 1) * 16]

    def store_sums(layer, parts):
        for at, part in parts:
            gvec[layer, :, at : at + part.shape[-1]] = down_sum(part)

    def first_back(layer, half, columns, extra, sums):
        base = half * HALF
        whole = pl.ds(pl.multiple_of(base, HALF), HALF)
        width = D * len(columns)
        grads = DQKV[whole, 3 * D - width : 3 * D]
        made = mm_nt(grads, win[layer, :, 3 * D - width : 3 * D])
        gain = vector(layer, 0, D)
        gain_sum, shift_sum = sums
        for at, size in pieces(HALF):
            rows = pl.ds(pl.multiple_of(base + at, 16), size)
            part = made[at : at + size]
            if extra is not None:
                part = part + extra[rows, :]
            normed = N1[layer, rows, :].astype(F32)
            inverse = I1[layer, rows, :][:, 0:1]
            gain_sum = gain_sum + fold(part * normed)
            shift_sum = shift_sum + fold(part)
            X[rows, :] = X[rows, :] + norm_back(part, normed, inverse, gain)
        return gain_sum, shift_sum

    zeros = jnp.zeros((8, D), F32)

    turned = H1[last].T
    for tile in (1, 2):
        gkv[:, (tile - 1) * D : tile * D] = mm(
            turned, DQKV[:, tile * D : (tile + 1) * D]
        ).astype(BF)
    store_sums(last, [(3 * D, fold(DQKV[:, 2 * D : 3 * D].astype(F32)))])
    SUMS[...] = jnp.zeros((ROWS, D), F32)
    for image in range(KEPT):
        SUMS[image * BLK + TAIL : (image + 1) * BLK, :] = from_query[
            image * 16 : (image + 1) * 16
        ]

    def last_back(half, sums):
        return first_back(last, half, (1, 2), SUMS, sums)

    gain_sum, shift_sum = lax.fori_loop(0, 2, last_back, (zeros, zeros))
    store_sums(last, [(0, gain_sum), (D, shift_sum)])

    def mlp_back(layer, half, sums):
        base = half * HALF
        whole = pl.ds(pl.multiple_of(base, HALF), HALF)
        bias_down, bias_up, gain_sum, shift_sum, bias_out = sums
        for at, size in pieces(HALF):
            rows = pl.ds(pl.multiple_of(base + at, 16), size)
            up = X[rows, :]
            DXB[rows, :] = up.astype(BF)
            bias_down = bias_down + fold(up)
        low = DXB[whole, :]
        ups = []
        for tile in range(4):
            columns = slice(tile * D, (tile + 1) * D)
            made = mm_nt(low, wdn[layer, columns, :])
            total = bias_up[tile]
            for at, size in pieces(HALF):
                rows = pl.ds(pl.multiple_of(base + at, 16), size)
                grad = (made[at : at + size] * SLOPE[layer, rows, columns].astype(F32)).astype(BF)
                DH[rows, columns] = grad
                total = total + fold(grad.astype(F32))
            ups.append(total)
        made = mm_nt(DH[whole, :], win[layer, :, 4 * D :])
        gain = vector(layer, 5 * D, D)
        for at, size in pieces(HALF):
            rows = pl.ds(pl.multiple_of(base + at, 16), size)
            part = made[at : at + size]
            normed = N2[layer, rows, :].astype(F32)
            inverse = I2[layer, rows, :][:, 0:1]
            gain_sum = gain_sum + fold(part * normed)
            shift_sum = shift_sum + fold(part)
            grad = X[rows, :] + norm_back(part, normed, inverse, gain)
            X[rows, :] = grad
            DMB[rows, :] = grad.astype(BF)
            bias_out = bias_out + fold(grad)
        DA[whole, :] = mm_nt(DMB[whole, :], win[layer, :, 3 * D : 4 * D]).astype(BF)
        return bias_down, tuple(ups), gain_sum, shift_sum, bias_out

    def attend_back(layer, image):
        rows = pl.ds(pl.multiple_of(image * BLK, BLK), BLK)
        for pair in range(3):
            at = pair * 128
            query = QKV[layer, rows, at : at + 128] * BF(0.125)
            keys = QKV[layer, rows, D + at : D + at + 128]
            values = QKV[layer, rows, 2 * D + at : 2 * D + at + 128]
            ups = DA[rows, at : at + 128]
            keys_both = jnp.concatenate([keys * even, keys * odd], axis=0)
            values_both = jnp.concatenate([values * even, values * odd], axis=0)
            scores = mm_nt(keys_both, query).reshape(2, BLK, BLK) + key_column[None]
            raw = jnp.exp(scores - jnp.max(scores, axis=1, keepdims=True))
            probs = raw * (1.0 / jnp.sum(raw, axis=1, keepdims=True))
            d_probs = mm_nt(values_both, ups).reshape(2, BLK, BLK)
            inner = jnp.sum(d_probs * probs, axis=1, keepdims=True)
            d_scores = (probs * (d_probs - inner)).astype(BF).reshape(2 * BLK, BLK)
            probs = probs.astype(BF).reshape(2 * BLK, BLK)
            d_values = mm(probs, ups)
            d_keys = mm(d_scores, query)
            d_query = mm_tn(d_scores, keys_both) * 0.125
            DQKV[rows, at : at + 128] = d_query.astype(BF)
            DQKV[rows, D + at : D + at + 128] = jnp.where(
                low_lane, d_keys[:BLK], d_keys[BLK:]
            ).astype(BF)
            DQKV[rows, 2 * D + at : 2 * D + at + 128] = jnp.where(
                low_lane, d_values[:BLK], d_values[BLK:]
            ).astype(BF)

    def backward(step, carry):
        layer = LAYERS - 2 - step

        def one(half, sums):
            return mlp_back(layer, half, sums)

        bias_down, bias_up, gain_sum, shift_sum, bias_out = lax.fori_loop(
            0, 2, one, (zeros, (zeros,) * 4, zeros, zeros, zeros)
        )
        store_sums(
            layer,
            [(7 * D + FF, bias_down), (5 * D, gain_sum), (6 * D, shift_sum), (4 * D, bias_out)]
            + [(7 * D + tile * D, bias_up[tile]) for tile in range(4)],
        )
        turned = DXB[...].T
        for tile in range(4):
            columns = slice(tile * D, (tile + 1) * D)
            gdn[layer, :, columns] = mm(turned, ACT[layer, :, columns]).astype(BF)
        turned = H2[layer].T
        for tile in range(4):
            gin[layer, :, (4 + tile) * D : (5 + tile) * D] = mm(
                turned, DH[:, tile * D : (tile + 1) * D]
            ).astype(BF)
        gin[layer, :, 3 * D : 4 * D] = mm(ATT[layer].T, DMB[...]).astype(BF)

        def two(image, c):
            attend_back(layer, image)
            return c

        lax.fori_loop(0, KEPT, two, 0)
        store_sums(
            layer,
            [
                (2 * D, fold(DQKV[:, 0:D].astype(F32))),
                (3 * D, fold(DQKV[:, 2 * D : 3 * D].astype(F32))),
            ],
        )
        turned = H1[layer].T
        for tile in range(3):
            gin[layer, :, tile * D : (tile + 1) * D] = mm(
                turned, DQKV[:, tile * D : (tile + 1) * D]
            ).astype(BF)

        def three(half, sums):
            return first_back(layer, half, (0, 1, 2), None, sums)

        gain_sum, shift_sum = lax.fori_loop(0, 2, three, (zeros, zeros))
        store_sums(layer, [(0, gain_sum), (D, shift_sum)])
        return carry

    lax.fori_loop(0, LAYERS - 1, backward, 0)

    for at, size in pieces(BLK):
        total = None
        for image in range(KEPT):
            part = X[image * BLK + at : image * BLK + at + size, :]
            DXB[image * BLK + at : image * BLK + at + size, :] = part.astype(BF)
            total = part if total is None else total + part
        gpos[at : at + size, :] = total
    low = DXB[...]
    for tile in range(2):
        columns = slice(tile * D, (tile + 1) * D)
        gpatch[columns, :] = mm_tn(pix[:, columns], low).astype(BF)


def run_compute(pix, wp, win, wdn, vecs, glob, addend, head, hbias, lab):
    def buf(*shape, dtype=BF):
        return pltpu.VMEM(shape, dtype)

    full = pl.BlockSpec(memory_space=pltpu.VMEM)
    keep = LAYERS - 1
    return pl.pallas_call(
        compute,
        out_shape=[
            jax.ShapeDtypeStruct((keep, D, 4 * D + FF), BF),
            jax.ShapeDtypeStruct((keep, D, FF), BF),
            jax.ShapeDtypeStruct((D, 2 * D), BF),
            jax.ShapeDtypeStruct((PATCH_DIM, D), BF),
            jax.ShapeDtypeStruct((LAYERS, 1, WIDE), F32),
            jax.ShapeDtypeStruct((1, 2 * D + 128), F32),
            jax.ShapeDtypeStruct((BLK, D), F32),
            jax.ShapeDtypeStruct((CROWS, FF + 4 * D), BF),
            jax.ShapeDtypeStruct((CROWS, FF + 3 * D + CPAD), BF),
        ],
        in_specs=[full] * 10,
        out_specs=[full] * 9,
        scratch_shapes=[
            buf(ROWS, D, dtype=F32),
            buf(LAYERS, ROWS, D),
            buf(LAYERS, ROWS, D),
            buf(LAYERS, ROWS, 128, dtype=F32),
            buf(keep, ROWS, 3 * D),
            buf(keep, ROWS, D),
            buf(keep, ROWS, D),
            buf(keep, ROWS, D),
            buf(keep, ROWS, 128, dtype=F32),
            buf(keep, ROWS, FF),
            buf(keep, ROWS, FF),
            buf(ROWS, D),
            buf(ROWS, FF),
            buf(ROWS, D),
            buf(ROWS, D),
            buf(ROWS, 3 * D),
            buf(ROWS, 2 * D),
            buf(ROWS, D, dtype=F32),
        ],
        compiler_params=pltpu.CompilerParams(vmem_limit_bytes=60 * 1024 * 1024),
        cost_estimate=pl.CostEstimate(
            flops=24_000_000_000, bytes_accessed=30_000_000, transcendentals=10_000_000
        ),
        name="train_step",
    )(pix, wp, win, wdn, vecs, glob, addend, head, hbias, lab)


def adam_update(weight, first, second, grad, factor, rate):
    grad = grad * factor
    first = BETA_FIRST * first + (1.0 - BETA_FIRST) * grad
    second = BETA_SECOND * second + (1.0 - BETA_SECOND) * grad * grad
    first_hat = first / (1.0 - BETA_FIRST**ADAM_STEP)
    second_hat = second / (1.0 - BETA_SECOND**ADAM_STEP)
    weight = weight - rate * (first_hat / (jnp.sqrt(second_hat) + ADAM_EPS) + WEIGHT_DECAY * weight)
    return (weight, first, second)


def tile_rows(values):
    return jnp.concatenate(
        [
            values[1:],
            jnp.zeros((CLS - PATCHES, D), F32),
            values[:1],
            jnp.zeros((BLK - CLS - 1, D), F32),
        ],
        axis=0,
    )


def shards(
    n_rep,
    n_shard,
    patches,
    labels,
    counts,
    patch_w,
    layer_in,
    layer_down,
    layer_vecs,
    glob_vecs,
    pos_embed,
    head,
    m_patch,
    v_patch,
    m_in,
    v_in,
    m_down,
    v_down,
    m_vecs,
    v_vecs,
    m_glob,
    v_glob,
    m_pos,
    v_pos,
    m_head,
    v_head,
):
    rep = lax.axis_index("rep")
    shard = lax.axis_index("shard")
    half = n_rep // 2
    slot_count = patches.shape[0]
    moves = [(source, source - half) for source in range(half, n_rep)]
    lower = rep < half
    marked = jnp.where(jnp.arange(slot_count) < counts[0], labels, -1)
    came = lax.ppermute(patches[KEPT:], "rep", moves)
    came_marked = lax.ppermute(marked[KEPT:], "rep", moves)
    pix = jnp.where(
        lower, jnp.concatenate([patches[: slot_count - KEPT], came], axis=0), patches[:KEPT]
    )
    pix = jnp.pad(pix, ((0, 0), (0, BLK - PATCHES), (0, 0))).reshape(ROWS, PATCH_DIM)
    chosen = jnp.where(
        lower, jnp.concatenate([marked[: slot_count - KEPT], came_marked]), marked[:KEPT]
    )
    lab = jnp.full((KEPT, 16), -1, jnp.int32).at[:, CLS - TAIL].set(chosen).reshape(CROWS, 1)

    wp = lax.all_gather(patch_w.astype(BF), "shard", axis=0, tiled=True)
    win = lax.all_gather(layer_in.astype(BF), "shard", axis=1, tiled=True)
    wdn = lax.all_gather(layer_down.astype(BF), "shard", axis=1, tiled=True)

    rows = jnp.arange(BLK)[:, None]
    addend = tile_rows(pos_embed) + jnp.where(rows < PATCHES, glob_vecs[0][None], 0.0)
    addend = addend + jnp.where(rows == CLS, glob_vecs[1][None], 0.0)
    head_low = jnp.pad(head[:D].astype(BF), ((0, 0), (0, CPAD - NCLS)))
    head_bias = jnp.pad(head[D:], ((0, 0), (0, CPAD - NCLS)))

    gin, gdn, gkv, gpatch, gvec, gfin, gpos, left, right = run_compute(
        pix, wp, win, wdn, layer_vecs[:, None, :], glob_vecs, addend, head_low, head_bias, lab
    )

    own_in = D // n_shard
    own_down = FF // n_shard
    own_patch = PATCH_DIM // n_shard
    keep = LAYERS - 1
    flat = jnp.concatenate(
        [
            gin.reshape(keep, n_shard, own_in, 4 * D + FF).swapaxes(0, 1).reshape(n_shard, -1),
            gkv.reshape(n_shard, -1),
            gpatch.reshape(n_shard, -1),
            gdn.reshape(keep, D, n_shard, own_down).transpose(2, 0, 1, 3).reshape(n_shard, -1),
        ],
        axis=1,
    )
    mine = lax.psum_scatter(flat, "shard", scatter_dimension=0, tiled=True)
    mine = lax.psum(mine, "rep").reshape(-1).astype(F32)
    sizes = [keep * own_in * (4 * D + FF), own_in * 2 * D, own_patch * D, keep * D * own_down]
    cut = [sum(sizes[:index]) for index in range(5)]
    sum_in = mine[cut[0] : cut[1]].reshape(keep, own_in, 4 * D + FF)
    sum_kv = mine[cut[1] : cut[2]].reshape(own_in, 2 * D)
    grad_patch = mine[cut[2] : cut[3]].reshape(own_patch, D)
    sum_down = mine[cut[3] : cut[4]].reshape(keep, D, own_down).swapaxes(1, 2)
    gvec, gfin, gpos, total = lax.psum(
        (gvec.reshape(LAYERS, WIDE), gfin[0], gpos, counts.astype(F32)), ("rep", "shard")
    )

    picked = slice(CLS - TAIL, None, 16)
    left = lax.all_gather(left[picked], ("rep", "shard"), axis=0, tiled=True)
    right = lax.all_gather(right[picked], ("rep", "shard"), axis=0, tiled=True)

    def rows_of(at, width, count):
        block = lax.dynamic_slice_in_dim(left[:, at : at + width], shard * count, count, axis=1)
        return block

    last_down = mm_tn(rows_of(0, FF, own_down), right[:, 0:D])
    last_up = mm_tn(rows_of(FF, D, own_in), right[:, D : D + FF])
    last_out = mm_tn(rows_of(FF + D, D, own_in), right[:, D + FF : 2 * D + FF])
    last_query = mm_tn(rows_of(FF + 2 * D, D, own_in), right[:, 2 * D + FF : 3 * D + FF])
    d_logits = right[:, 3 * D + FF : 3 * D + FF + NCLS]
    grad_head = jnp.concatenate(
        [
            mm_tn(left[:, FF + 3 * D :], d_logits),
            jnp.sum(d_logits.astype(F32), axis=0, keepdims=True),
        ],
        axis=0,
    )
    last_in = jnp.concatenate([last_query, sum_kv, last_out, last_up], axis=1)
    grad_in = jnp.concatenate([sum_in, last_in[None]], axis=0)
    grad_down = jnp.concatenate([sum_down, last_down[None]], axis=0)
    grad_pos = jnp.concatenate([gpos[CLS : CLS + 1], gpos[:PATCHES]], axis=0)
    grad_glob = jnp.stack(
        [jnp.sum(gpos[:PATCHES], axis=0), gpos[CLS], gfin[:D], gfin[D : 2 * D]]
    )

    inv_count = 1.0 / total[0]
    own_squares = (
        jnp.sum(grad_patch * grad_patch)
        + jnp.sum(grad_in * grad_in)
        + jnp.sum(grad_down * grad_down)
    )
    small_squares = (
        jnp.sum(gvec * gvec)
        + jnp.sum(grad_glob * grad_glob)
        + jnp.sum(grad_pos * grad_pos)
        + jnp.sum(grad_head * grad_head)
    )
    grad_norm = jnp.sqrt(lax.psum(own_squares, "shard") + small_squares) * inv_count
    factor = jnp.minimum(1.0, CLIP_NORM / grad_norm) * inv_count
    loss = gfin[2 * D] * inv_count
    new_patch = adam_update(patch_w, m_patch, v_patch, grad_patch, factor, LEARNING_RATE)
    new_in = adam_update(layer_in, m_in, v_in, grad_in, factor, LEARNING_RATE)
    new_down = adam_update(layer_down, m_down, v_down, grad_down, factor, LEARNING_RATE)
    new_vecs = adam_update(layer_vecs, m_vecs, v_vecs, gvec, factor, VECTOR_RATE)
    new_glob = adam_update(glob_vecs, m_glob, v_glob, grad_glob, factor, VECTOR_RATE)
    new_pos = adam_update(pos_embed, m_pos, v_pos, grad_pos, factor, VECTOR_RATE)
    new_head = adam_update(head, m_head, v_head, grad_head, factor, LEARNING_RATE)
    return (
        loss, grad_norm, *new_patch, *new_in, *new_down, *new_vecs, *new_glob, *new_pos, *new_head
    )


def solution(mesh):
    everywhere = P()
    rows = P("shard", None)
    middle = P(None, "shard", None)
    return jax.shard_map(
        functools.partial(shards, mesh.shape["rep"], mesh.shape["shard"]),
        mesh=mesh,
        in_specs=(
            P(("rep", "shard"), None, None),
            P(("rep", "shard")),
            P(("rep", "shard")),
            rows,
            middle,
            middle,
            *(everywhere,) * 4,
            *(rows,) * 2,
            *(middle,) * 4,
            *(everywhere,) * 8,
        ),
        out_specs=(
            *(everywhere,) * 2,
            *(rows,) * 3,
            *(middle,) * 6,
            *(everywhere,) * 12,
        ),
        check_vma=False,
    )
```

```python
import functools

import jax
import jax.numpy as jnp
from jax import lax
from jax.experimental import pallas as pl
from jax.experimental.pallas import tpu as pltpu
from jax.sharding import PartitionSpec as P

D = 384
HEADS = 6
HEAD_DIM = 64
FF = 1536
PATCH_DIM = 768
PATCHES = 196
NCLS = 1000
LAYERS = 3
SEQ = 197

BLK = 208
CLS = 200
TAIL = 192
KEPT = 4
ROWS = KEPT * BLK
HALF = 2 * BLK
CROWS = KEPT * 16
CPAD = 1024
WIDE = 8 * D + FF

NORM_EPS = 1e-06
SMOOTHING = 0.1
CLIP_NORM = 0.05
LEARNING_RATE = 0.05
VECTOR_RATE = 0.5
BETA_FIRST = 0.9
BETA_SECOND = 0.999
ADAM_EPS = 1e-08
WEIGHT_DECAY = 0.05
ADAM_STEP = 10
GELU_SCALE = 0.7978845608028654
GELU_CUBIC = 0.044715

F32 = jnp.float32
BF = jnp.bfloat16


def mm(left, right):
    return jnp.dot(left, right, preferred_element_type=F32)


def mm_nt(left, right):
    return lax.dot_general(left, right, (((1,), (1,)), ((), ())), preferred_element_type=F32)


def mm_tn(left, right):
    return lax.dot_general(left, right, (((0,), (0,)), ((), ())), preferred_element_type=F32)


def fold(values):
    return jnp.sum(values.reshape(-1, 8, values.shape[-1]), axis=0)


def down_sum(values):
    return jnp.sum(values, axis=0, keepdims=True)


def norm(values):
    centre = values - jnp.mean(values, axis=-1, keepdims=True)
    inverse = lax.rsqrt(jnp.mean(centre * centre, axis=-1, keepdims=True) + NORM_EPS)
    return centre * inverse, inverse


def norm_back(upstream, normed, inverse, gain):
    scaled = upstream * gain
    first = jnp.mean(scaled, axis=-1, keepdims=True)
    second = jnp.mean(scaled * normed, axis=-1, keepdims=True)
    return inverse * (scaled - first - normed * second)


def gelu_parts(hidden):
    square = hidden * hidden
    tangent = jnp.tanh(hidden * (GELU_SCALE + (GELU_SCALE * GELU_CUBIC) * square))
    share = 0.5 + 0.5 * tangent
    active = hidden * share
    inner = (2.0 * GELU_SCALE) + (6.0 * GELU_SCALE * GELU_CUBIC) * square
    slope = share + active * (1.0 - share) * inner
    return active, slope


def lane_mask(width, low, high):
    lane = lax.broadcasted_iota(jnp.int32, (1, width), 1)
    return jnp.where((lane >= low) & (lane < high), 1.0, 0.0).astype(BF)


STEP = 32


def pieces(total):
    return [(at, min(STEP, total - at)) for at in range(0, total, STEP)]


WFAC = FF + 5 * D
VEC_ROWS = 256
VEC_AT = BLK
VEC_WIDE = D + 128
MESH = pl.DeviceIdType.MESH
CHUNKS = 6


class Place:
    def __init__(self, n_rep, n_shard):
        self.n_rep, self.n_shard = n_rep, n_shard
        self.n_x = 2 ** ((n_rep.bit_length() - 2) // 2)
        self.n_z = n_rep // self.n_x
        self.n_y = n_shard // 2
        rep, shard = lax.axis_index("rep"), lax.axis_index("shard")
        self.rep, self.shard = rep, shard
        self.z, self.x = rep // self.n_x, rep % self.n_x
        self.y, self.c = shard // 2, shard % 2

    def to(self, x=None, y=None, z=None, c=None):
        x = self.x if x is None else x
        y = self.y if y is None else y
        z = self.z if z is None else z
        c = self.c if c is None else c
        return {"rep": z * self.n_x + x, "shard": y * 2 + c}


def cut(rows, parts, unit):
    return parts if rows % (parts * unit) == 0 else 1


def aligned(value, unit):
    return pl.multiple_of(value, unit)


def train(
    n_rep, n_shard,
    patches, lab_pairs, own_patch, own_in, own_down, vecs, glob, pos, head, count,
    res_out, small_out, vec_out, all_factors,
    X, N1, I1, QKV, ATT, N2, I2, ACT, SLOPE, DXB, DMB, DA,
    pix, lab, wp, win, wdn, low_head, head_bias,
    G, RC, RY, RX, RZ, RES, GS, SC, SY, SX, SZ, SRES,
    FAC, FC, FY, FALL, V, VC, VY, VX, VZ, VF, SQ, SQS, square_sum,
    ag_send, ag_recv, ag_local, rs_send, rs_recv, f_send, f_recv, v_send, v_recv,
    img_send, img_recv, img_local, out_local,
):
    here = Place(n_rep, n_shard)
    n_x, n_y, n_z = here.n_x, here.n_y, here.n_z
    x, y, z, c = here.x, here.y, here.z, here.c
    rows_in, rows_down, rows_patch = D // n_shard, FF // n_shard, PATCH_DIM // n_shard
    block = 4 * rows_in
    mate = here.to(c=1 - c)

    def push(src, dst, send, recv, device):
        pltpu.make_async_remote_copy(
            src_ref=src, dst_ref=dst, send_sem=send, recv_sem=recv,
            device_id=device, device_id_type=MESH,
        ).start()

    def arrived(dst, recv, send):
        pltpu.make_async_remote_copy(
            src_ref=dst, dst_ref=dst, send_sem=send, recv_sem=recv,
            device_id=mate, device_id_type=MESH,
        ).wait_recv()

    def left_here(src, recv, send):
        pltpu.make_async_remote_copy(
            src_ref=src, dst_ref=src, send_sem=send, recv_sem=recv,
            device_id=mate, device_id_type=MESH,
        ).wait_send()

    sent = {}

    def go(source, dst, sems, index, device):
        name, send, recv = sems
        push(source(), dst, send.at[index], recv.at[index], device)
        sent[name, index] = (source, send, recv, index)

    def gone(sems, index):
        source, send, recv, at = sent.pop((sems[0], index))
        left_here(source(), recv.at[at], send.at[at])

    def turn(at, by, size):
        return lax.rem(at + by, size)

    barrier = pltpu.get_barrier_semaphore()
    others = (
        [mate]
        + [here.to(y=turn(y, o, n_y)) for o in range(1, n_y)]
        + [here.to(x=turn(x, o, n_x)) for o in range(1, n_x)]
        + [here.to(z=turn(z, o, n_z)) for o in range(1, n_z)]
    )
    for other in others:
        pl.semaphore_signal(barrier, inc=1, device_id=other, device_id_type=MESH)
    pl.semaphore_wait(barrier, len(others))

    def weight(kind, layer, shard, part=None):
        if kind == "patch":
            parts = cut(rows_patch, n_x, 16)
            rows = rows_patch // parts
            if part is None:
                return wp.at[pl.ds(aligned(shard * rows_patch, 16), rows_patch), :]
            return wp.at[pl.ds(aligned(shard * rows_patch + part * rows, 16), rows), :]
        if kind == "down":
            parts = cut(rows_down, n_x, 16)
            rows = rows_down // parts
            if part is None:
                return wdn.at[layer, pl.ds(aligned(shard * rows_down, 16), rows_down), :]
            return wdn.at[layer, pl.ds(aligned(shard * rows_down + part * rows, 16), rows), :]
        base = 0 if kind == "attn" else 4 * D
        rows = pl.ds(aligned(shard * rows_in, 16), rows_in)
        if part is None:
            return win.at[layer, rows, pl.ds(base, 4 * D)]
        wide = 4 * D // n_x
        return win.at[layer, rows, pl.ds(aligned(base + part * wide, 128), wide)]

    def owned(kind, layer, part=None):
        if kind == "patch":
            if part is None:
                return own_patch
            rows = rows_patch // cut(rows_patch, n_x, 16)
            return own_patch.at[pl.ds(aligned(part * rows, 16), rows), :]
        if kind == "down":
            if part is None:
                return own_down.at[layer]
            rows = rows_down // cut(rows_down, n_x, 16)
            return own_down.at[layer, pl.ds(aligned(part * rows, 16), rows), :]
        base = 0 if kind == "attn" else 4 * D
        if part is None:
            return own_in.at[layer, :, pl.ds(base, 4 * D)]
        wide = 4 * D // n_x
        return own_in.at[layer, :, pl.ds(aligned(base + part * wide, 128), wide)]

    units = [("patch", 0)] + [
        (kind, layer) for layer in range(LAYERS) for kind in ("attn", "up", "down")
    ]

    def parts_of(kind):
        if kind == "patch":
            return cut(rows_patch, n_x, 16)
        if kind == "down":
            return cut(rows_down, n_x, 16)
        return n_x

    ag = ("ag", ag_send, ag_recv)
    base_x = n_y
    base_my = base_x + (n_y - 1) * (n_x - 1)
    base_mx = base_my + (n_y - 1)

    def weights_start(unit):
        kind, layer = units[unit]
        me = here.shard
        part = x if parts_of(kind) > 1 else 0
        for o in range(1, n_y):
            go(
                lambda: owned(kind, layer, part), weight(kind, layer, me, part), ag, (unit, o),
                here.to(y=turn(y, o, n_y)),
            )
        go(lambda: owned(kind, layer), weight(kind, layer, me), ag, (unit, 0), mate)
        pltpu.make_async_copy(
            owned(kind, layer), weight(kind, layer, me), ag_local.at[unit]
        ).start()

    def weights_forward(unit):
        kind, layer = units[unit]
        split = parts_of(kind) > 1
        part = x if split else 0
        for o in range(1, n_y):
            def make(o=o):
                return weight(kind, layer, turn(y, n_y - o, n_y) * 2 + c, part)

            arrived(make(), ag_recv.at[unit, o], ag_send.at[unit, o])
            if split:
                for p in range(1, n_x):
                    index = base_x + (o - 1) * (n_x - 1) + p - 1
                    go(make, make(), ag, (unit, index), here.to(x=turn(x, p, n_x)))
            go(make, make(), ag, (unit, base_my + o - 1), mate)

    def weights_ready(unit):
        kind, layer = units[unit]
        split = parts_of(kind) > 1
        part = x if split else 0
        if split:
            for o in range(1, n_y):
                for p in range(1, n_x):
                    index = (o - 1) * (n_x - 1) + p - 1

                    def make(o=o, p=p):
                        shard = turn(y, n_y - o, n_y) * 2 + c
                        return weight(kind, layer, shard, turn(x, n_x - p, n_x))

                    arrived(
                        make(), ag_recv.at[unit, base_x + index], ag_send.at[unit, base_x + index]
                    )
                    go(make, make(), ag, (unit, base_mx + index), mate)
        pltpu.make_async_copy(
            owned(kind, layer), weight(kind, layer, here.shard), ag_local.at[unit]
        ).wait()
        arrived(weight(kind, layer, y * 2 + 1 - c), ag_recv.at[unit, 0], ag_send.at[unit, 0])
        for o in range(1, n_y):
            shard = turn(y, n_y - o, n_y) * 2 + 1 - c
            index = base_my + o - 1
            arrived(weight(kind, layer, shard, part), ag_recv.at[unit, index], ag_send.at[unit, index])
            if split:
                for p in range(1, n_x):
                    index = base_mx + (o - 1) * (n_x - 1) + p - 1
                    piece = weight(kind, layer, shard, turn(x, n_x - p, n_x))
                    arrived(piece, ag_recv.at[unit, index], ag_send.at[unit, index])

    lower = here.rep < n_rep // 2
    partner = here.to(z=turn(z, n_z // 2, n_z))
    back_half = pix.at[pl.ds(2, 2)]
    given = patches.at[pl.ds(KEPT, 2)]

    def local_half(half):
        return pltpu.make_async_copy(
            patches.at[pl.ds(2 * half, 2)], pix.at[pl.ds(2 * half, 2)], img_local.at[half]
        )

    def local_lab(half):
        return pltpu.make_async_copy(lab_pairs.at[half], lab.at[half], img_local.at[2 + half])

    local_half(0).start()
    local_lab(0).start()

    @pl.when(jnp.logical_not(lower))
    def _():
        push(given, back_half, img_send.at[0], img_recv.at[0], partner)
        push(lab_pairs.at[2], lab.at[1], img_send.at[1], img_recv.at[1], partner)
        local_half(1).start()
        local_lab(1).start()

    for unit in range(4):
        weights_start(unit)

    even = lane_mask(128, 0, 64)
    odd = lane_mask(128, 64, 128)
    low_lane = lax.broadcasted_iota(jnp.int32, (1, 128), 1) < 64
    key_lane = lax.broadcasted_iota(jnp.int32, (1, BLK), 1)
    key_row = jnp.where((key_lane < PATCHES) | (key_lane == CLS), 0.0, -1e30)
    key_sub = lax.broadcasted_iota(jnp.int32, (BLK, 1), 0)
    key_column = jnp.where((key_sub < PATCHES) | (key_sub == CLS), 0.0, -1e30)
    whole_lanes = NCLS // 128 * 128
    low_head[:, 0:whole_lanes] = head[0:D, 0:whole_lanes].astype(BF)
    low_head[:, whole_lanes:] = jnp.zeros((D, CPAD - whole_lanes), BF)
    low_head[:, whole_lanes:NCLS] = head[0:D, whole_lanes:NCLS].astype(BF)
    head_bias[...] = jnp.zeros((1, CPAD), F32)
    head_bias[:, 0:NCLS] = head[D : D + 1, :]
    V[...] = jnp.zeros((VEC_ROWS, VEC_WIDE), F32)
    square_sum[...] = jnp.zeros((8, 128), F32)
    zeros = jnp.zeros((8, D), F32)
    patch_bias = glob[0:1, :]

    def vector(layer, at, size):
        return vecs[pl.ds(layer, 1), at : at + size]

    def store_vector(layer, at, row):
        for piece in range(row.shape[-1] // D):
            V[pl.ds(VEC_AT + 12 * layer + at // D + piece, 1), 0:D] = row[
                :, piece * D : (piece + 1) * D
            ]

    def store_sums(layer, parts):
        for at, part in parts:
            store_vector(layer, at, down_sum(part))

    def embed(half):
        made = mm(pix[pl.ds(2 * half, 2)].reshape(HALF, PATCH_DIM), wp[...])
        for image in range(2):
            start = aligned(half * HALF + image * BLK, 16)
            for at, size in pieces(PATCHES - 4):
                X[pl.ds(start + at, size), :] = (
                    made[image * BLK + at : image * BLK + at + size]
                    + pos[1 + at : 1 + at + size, :]
                    + patch_bias
                )
            X[pl.ds(start + TAIL, 16), :] = jnp.zeros((16, D), F32)
            X[pl.ds(start + TAIL, 4), :] = (
                made[image * BLK + TAIL : image * BLK + PATCHES]
                + pos[1 + TAIL : 1 + PATCHES, :]
                + patch_bias
            )
            X[pl.ds(start + CLS, 1), :] = glob[1:2, :] + pos[0:1, :]

    def first_norm(layer, half, columns):
        base = half * HALF
        gain, shift = vector(layer, 0, D), vector(layer, D, D)
        for at, size in pieces(HALF):
            rows = pl.ds(aligned(base + at, 16), size)
            normed, inverse = norm(X[rows, :])
            N1[layer, rows, :] = normed.astype(BF)
            I1[layer, rows, :] = jnp.broadcast_to(inverse, (size, 128))
            DXB[rows, :] = (normed * gain + shift).astype(BF)
        rows = pl.ds(aligned(base, 16), HALF)
        h1 = DXB[rows, :]
        for tile in columns:
            made = mm(h1, win[layer, :, tile * D : (tile + 1) * D])
            if tile == 0:
                made = made + vector(layer, 2 * D, D)
            if tile == 2:
                made = made + vector(layer, 3 * D, D)
            if len(columns) == 3:
                QKV[layer, rows, tile * D : (tile + 1) * D] = made.astype(BF)
            else:
                (DMB if tile == 1 else DA)[rows, :] = made.astype(BF)

    def attend(layer, image):
        rows = pl.ds(aligned(image * BLK, 16), BLK)
        for pair in range(3):
            at = pair * 128
            query = QKV[layer, rows, at : at + 128] * BF(0.125)
            keys = QKV[layer, rows, D + at : D + at + 128]
            values = QKV[layer, rows, 2 * D + at : 2 * D + at + 128]
            both = jnp.concatenate([query * even, query * odd], axis=0)
            scores = mm_nt(both, keys) + key_row
            top = jnp.max(scores, axis=-1, keepdims=True)
            raw = jnp.exp(scores - top)
            probs = (raw * (1.0 / jnp.sum(raw, axis=-1, keepdims=True))).astype(BF)
            made = mm(probs[:BLK], values * even) + mm(probs[BLK:], values * odd)
            ATT[layer, rows, at : at + 128] = made.astype(BF)

    def mlp(layer, half):
        base = half * HALF
        whole = pl.ds(aligned(base, 16), HALF)
        made = mm(ATT[layer, whole, :], win[layer, :, 3 * D : 4 * D])
        bias_out = vector(layer, 4 * D, D)
        gain, shift = vector(layer, 5 * D, D), vector(layer, 6 * D, D)
        for at, size in pieces(HALF):
            rows = pl.ds(aligned(base + at, 16), size)
            middle = X[rows, :] + made[at : at + size] + bias_out
            X[rows, :] = middle
            normed, inverse = norm(middle)
            N2[layer, rows, :] = normed.astype(BF)
            I2[layer, rows, :] = jnp.broadcast_to(inverse, (size, 128))
            DXB[rows, :] = (normed * gain + shift).astype(BF)
        h2 = DXB[whole, :]
        for tile in range(4):
            columns = slice(tile * D, (tile + 1) * D)
            made = mm(h2, win[layer, :, (4 + tile) * D : (5 + tile) * D])
            bias = vector(layer, 7 * D + tile * D, D)
            for at, size in pieces(HALF):
                rows = pl.ds(aligned(base + at, 16), size)
                active, slope = gelu_parts(made[at : at + size] + bias)
                ACT[layer, rows, columns] = active.astype(BF)
                SLOPE[layer, rows, columns] = slope.astype(BF)
        made = mm(ACT[layer, whole, :], wdn[layer])
        bias = vector(layer, 7 * D + FF, D)
        for at, size in pieces(HALF):
            rows = pl.ds(aligned(base + at, 16), size)
            X[rows, :] = X[rows, :] + made[at : at + size] + bias

    def when(condition, *steps):
        @pl.when(condition)
        def _():
            for step, unit in steps:
                step(unit)

    weights_forward(0)
    weights_ready(0)

    def forward_half(half, carry):
        start = half == 0

        @pl.when(start)
        def _():
            local_half(0).wait()

        @pl.when(jnp.logical_and(half == 1, lower))
        def _():
            arrived(back_half, img_recv.at[0], img_send.at[0])

        @pl.when(jnp.logical_and(half == 1, jnp.logical_not(lower)))
        def _():
            local_half(1).wait()

        embed(half)

        def forward_layer(layer, inner):
            first = jnp.logical_and(start, layer == 0)
            second = jnp.logical_and(start, layer == 1)
            when(first, (weights_forward, 1), (weights_start, 4), (weights_ready, 1))
            when(second, (weights_ready, 4))
            first_norm(layer, half, (0, 1, 2))
            when(first, (weights_forward, 2), (weights_start, 5))
            when(second, (weights_forward, 6), (weights_start, 9))

            def attend_one(index, nothing):
                attend(layer, 2 * half + index)
                begin = index == 0
                when(
                    jnp.logical_and(first, begin), (weights_forward, 3), (weights_start, 6)
                )
                when(jnp.logical_and(second, begin), (weights_forward, 7))
                return nothing

            lax.fori_loop(0, 2, attend_one, 0)
            when(
                first, (weights_forward, 4), (weights_start, 7), (weights_ready, 2),
                (weights_ready, 3),
            )
            when(second, (weights_forward, 8), (weights_ready, 5), (weights_ready, 6))
            mlp(layer, half)
            when(first, (weights_forward, 5), (weights_start, 8))
            when(second, (weights_forward, 9))
            return inner

        return lax.fori_loop(0, LAYERS - 1, forward_layer, carry)

    lax.fori_loop(0, 2, forward_half, 0)
    for unit in (7, 8, 9):
        weights_ready(unit)

    last = LAYERS - 1

    def last_norm(half, nothing):
        first_norm(last, half, (1, 2))
        return nothing

    lax.fori_loop(0, 2, last_norm, 0)

    fac = ("f", f_send, f_recv)
    f_y, f_x = 1, n_y
    f_z = f_x + n_x - 1
    f_m = f_z + n_z - 1
    group = KEPT * n_shard

    def factors_core():
        go(lambda: FAC.at[1 - c], FC, fac, 0, mate)

    def factors_y():
        arrived(FC, f_recv.at[0], f_send.at[0])
        FAC[c] = FAC[c] + FC[...]
        for o in range(1, n_y):
            go(lambda: FAC.at[c], FY.at[o - 1], fac, f_y + o - 1, here.to(y=turn(y, o, n_y)))

    def factors_x():
        total = FAC[c]
        for o in range(1, n_y):
            arrived(FY.at[o - 1], f_recv.at[f_y + o - 1], f_send.at[f_y + o - 1])
            total = total + FY[o - 1]
        FALL[x] = total
        for o in range(1, n_x):
            go(lambda: FALL.at[x], FALL.at[x], fac, f_x + o - 1, here.to(x=turn(x, o, n_x)))

    def all_rows(at):
        return all_factors.at[c, pl.ds(at * n_x, n_x)]

    def factors_z():
        for o in range(1, n_x):
            index = f_x + o - 1
            arrived(FALL.at[turn(x, n_x - o, n_x)], f_recv.at[index], f_send.at[index])
        pltpu.make_async_copy(FALL, all_rows(z), out_local.at[0]).start()
        for o in range(1, n_z):
            go(lambda: FALL, all_rows(z), fac, f_z + o - 1, here.to(z=turn(z, o, n_z)))

    def factors_mate():
        for o in range(1, n_z):
            index = f_z + o - 1
            arrived(all_rows(turn(z, n_z - o, n_z)), f_recv.at[index], f_send.at[index])
        pltpu.make_async_copy(FALL, all_rows(z), out_local.at[0]).wait()
        go(lambda: all_factors.at[c], all_factors.at[c], fac, f_m, mate)

    def factors_done():
        arrived(all_factors.at[1 - c], f_recv.at[f_m], f_send.at[f_m])

    rs = ("rs", rs_send, rs_recv)
    r_y, r_x = 1, n_y
    r_z = r_x + n_x - 1
    r_gz = r_z + n_z - 1
    r_gx = r_gz + n_z - 1

    def chunk(k):
        if k < CHUNKS:
            return G.at[k], RC.at[k % 3], RY.at[k % 3], RX.at[k], RZ.at[k], RES.at[k], block
        k = k - CHUNKS
        return GS.at[k], SC.at[k], SY.at[k], SX.at[k], SZ.at[k], SRES.at[k], block // 2

    def splits(rows):
        by_x = cut(rows, n_x, 16)
        by_z = cut(rows // by_x, n_z, 16)
        return by_x, rows // by_x, by_z, rows // by_x // by_z

    def add_rows(rows, target, target_at, sources):
        step = 48 if rows % 48 == 0 else 16

        def one(index, nothing):
            at = index * step
            to = pl.ds(aligned(target_at + at, 16), step)
            total = target[to, :]
            if len(sources) == 1:
                total = total + sources[0][pl.ds(aligned(at, 16), step), :]
            else:
                total = total.astype(F32)
                for source in sources:
                    total = total + source[pl.ds(aligned(at, 16), step), :].astype(F32)
                total = total.astype(BF)
            target[to, :] = total
            return nothing

        lax.fori_loop(0, rows // step, one, 0)

    def reduce_core(k):
        g, rc = chunk(k)[0:2]
        go(lambda: chunk(k)[0].at[:, 1 - c], rc, rs, (k, 0), mate)

    def reduce_y(k):
        g, rc, ry, _, _, _, rows = chunk(k)
        arrived(rc, rs_recv.at[k, 0], rs_send.at[k, 0])
        for o in list(range(1, n_y)) + [0]:
            at = turn(y, o, n_y)
            add_rows(rows, g.at[at, c], 0, [rc.at[at]])
            if o:
                go(
                    lambda o=o: chunk(k)[0].at[turn(y, o, n_y), c], ry.at[o - 1], rs,
                    (k, r_y + o - 1), here.to(y=at),
                )

    def total_of(slots, count, at, step):
        total = None
        for index in range(count):
            value = slots[index, pl.ds(aligned(at, 16), step), :].astype(F32)
            total = value if total is None else total + value
        return total

    def reduce_x(k):
        g, _, ry, rx, _, _, rows = chunk(k)
        by_x, rows_x = splits(rows)[0:2]
        for o in range(1, n_y):
            arrived(ry.at[o - 1], rs_recv.at[k, r_y + o - 1], rs_send.at[k, r_y + o - 1])
        mine = g.at[y, c]
        add_rows(rows, mine, 0, [ry.at[o - 1] for o in range(1, n_y)])
        for o in range(1, n_x):
            to = turn(x, o, n_x)
            if by_x > 1:

                def make(o=o):
                    at = turn(x, o, n_x) * rows_x
                    return chunk(k)[0].at[y, c, pl.ds(aligned(at, 16), rows_x), :]

                go(make, rx.at[o - 1], rs, (k, r_x + o - 1), here.to(x=to))
            else:
                go(lambda: chunk(k)[0].at[y, c], rx.at[x], rs, (k, r_x + o - 1), here.to(x=to))

    def reduce_z(k):
        g, _, _, rx, rz, _, rows = chunk(k)
        by_x, rows_x, by_z, rows_z = splits(rows)
        mine = g.at[y, c]
        for o in range(1, n_x):
            slot = rx.at[o - 1] if by_x > 1 else rx.at[turn(x, n_x - o, n_x)]
            arrived(slot, rs_recv.at[k, r_x + o - 1], rs_send.at[k, r_x + o - 1])
        if by_x > 1:
            start = x * rows_x
            add_rows(rows_x, mine, start, [rx.at[o - 1] for o in range(1, n_x)])
        else:
            start = 0
            rx[x] = mine[...]
            for o in range(1, n_x):
                gone(rs, (k, r_x + o - 1))
            step = 48 if rows % 48 == 0 else 16

            def one(index, nothing):
                at = pl.ds(aligned(index * step, 16), step)
                g[y, c, at, :] = total_of(rx, n_x, index * step, step).astype(BF)
                return nothing

            lax.fori_loop(0, rows // step, one, 0)
        for o in range(1, n_z):

            def make(o=o):
                at = x * rows_x if by_x > 1 else 0
                if by_z > 1:
                    at = at + turn(z, o, n_z) * rows_z
                return chunk(k)[0].at[y, c, pl.ds(aligned(at, 16), rows_z), :]

            slot = rz.at[o - 1] if by_z > 1 else rz.at[z]
            go(make, slot, rs, (k, r_z + o - 1), here.to(z=turn(z, o, n_z)))

    def gather_z(k):
        g, _, _, _, rz, res, rows = chunk(k)
        by_x, rows_x, by_z, rows_z = splits(rows)
        start = x * rows_x if by_x > 1 else 0
        if by_z > 1:
            start = start + z * rows_z
        for o in range(1, n_z):
            slot = rz.at[o - 1] if by_z > 1 else rz.at[turn(z, n_z - o, n_z)]
            arrived(slot, rs_recv.at[k, r_z + o - 1], rs_send.at[k, r_z + o - 1])
        own_slot = n_z - 1 if by_z > 1 else z
        rz[own_slot] = g[y, c, pl.ds(aligned(start, 16), rows_z), :]
        share = 1.0 / ((1 if by_x > 1 else n_x) * (1 if by_z > 1 else n_z))
        step = 48 if rows_z % 48 == 0 else 16

        def one(index, total):
            low = total_of(rz, n_z, index * step, step).astype(BF)
            res[pl.ds(aligned(start + index * step, 16), step), :] = low
            wide = low.astype(F32)
            return total + fold(wide * wide)

        total = lax.fori_loop(0, rows_z // step, one, zeros) * share
        for at in range(0, D, 128):
            square_sum[...] = square_sum[...] + total[:, at : at + 128]
        if by_z > 1:

            def make():
                at = x * rows_x if by_x > 1 else 0
                return chunk(k)[5].at[pl.ds(aligned(at + z * rows_z, 16), rows_z), :]

            for o in range(1, n_z):
                go(make, make(), rs, (k, r_gz + o - 1), here.to(z=turn(z, o, n_z)))

    def gather_x(k):
        res, rows = chunk(k)[5:7]
        by_x, rows_x, by_z, rows_z = splits(rows)
        if by_z > 1:
            for o in range(1, n_z):
                start = turn(z, n_z - o, n_z) * rows_z
                if by_x > 1:
                    start = start + x * rows_x
                arrived(
                    res.at[pl.ds(aligned(start, 16), rows_z), :],
                    rs_recv.at[k, r_gz + o - 1], rs_send.at[k, r_gz + o - 1],
                )
        if by_x > 1:

            def make():
                return chunk(k)[5].at[pl.ds(aligned(x * rows_x, 16), rows_x), :]

            for o in range(1, n_x):
                go(make, make(), rs, (k, r_gx + o - 1), here.to(x=turn(x, o, n_x)))

    def result(k):
        if k < CHUNKS:
            return pltpu.make_async_copy(RES.at[k], res_out.at[k], out_local.at[1 + k])
        return pltpu.make_async_copy(
            SRES.at[k - CHUNKS], small_out.at[k - CHUNKS], out_local.at[1 + k]
        )

    def gather_done(k):
        res, rows = chunk(k)[5:7]
        by_x, rows_x = splits(rows)[0:2]
        if by_x > 1:
            for o in range(1, n_x):
                start = turn(x, n_x - o, n_x) * rows_x
                arrived(
                    res.at[pl.ds(aligned(start, 16), rows_x), :],
                    rs_recv.at[k, r_gx + o - 1], rs_send.at[k, r_gx + o - 1],
                )
        result(k).start()

    def tails(ref, layer=None):
        found = []
        for image in range(KEPT):
            rows = slice(image * BLK + TAIL, (image + 1) * BLK)
            found.append(ref[rows, :] if layer is None else ref[layer, rows, :])
        return jnp.concatenate(found, axis=0)

    @pl.when(lower)
    def _():
        arrived(lab.at[1], img_recv.at[1], img_send.at[1])

    @pl.when(jnp.logical_not(lower))
    def _():
        local_lab(1).wait()

    local_lab(0).wait()
    labels = lab[...].reshape(CROWS, 128)[:, 0:1]

    h1 = tails(DXB)
    stream = tails(X)
    query = ((mm(h1, win[last, :, 0:D]) + vector(last, 2 * D, D)).astype(BF)) * BF(0.125)
    head_masks = [lane_mask(D, index * 64, (index + 1) * 64) for index in range(HEADS)]

    def spread(values):
        return jnp.concatenate([values * mask for mask in head_masks], axis=0)

    def gather_heads(values):
        total = None
        for index in range(HEADS):
            part = values[index * 16 : (index + 1) * 16] * head_masks[index].astype(F32)
            total = part if total is None else total + part
        return total

    spread_queries, probabilities, outs = [], [], []
    for image in range(KEPT):
        rows = slice(image * BLK, (image + 1) * BLK)
        queries = spread(query[image * 16 : (image + 1) * 16])
        scores = mm_nt(queries, DMB[rows, :]) + key_row
        raw = jnp.exp(scores - jnp.max(scores, axis=-1, keepdims=True))
        probs = raw * (1.0 / jnp.sum(raw, axis=-1, keepdims=True))
        spread_queries.append(queries)
        probabilities.append(probs)
        outs.append(gather_heads(mm(probs.astype(BF), DA[rows, :])))
    attended = jnp.concatenate(outs, axis=0).astype(BF)
    middle = stream + mm(attended, win[last, :, 3 * D : 4 * D]) + vector(last, 4 * D, D)
    n2, i2 = norm(middle)
    h2 = (n2 * vector(last, 5 * D, D) + vector(last, 6 * D, D)).astype(BF)
    active, slope = gelu_parts(mm(h2, win[last, :, 4 * D :]) + vector(last, 7 * D, FF))
    active = active.astype(BF)
    top = middle + mm(active, wdn[last]) + vector(last, 7 * D + FF, D)
    gain_final = glob[2:3, :]
    nf, inf = norm(top)
    final = (nf * gain_final + glob[3:4, :]).astype(BF)
    class_lane = lax.broadcasted_iota(jnp.int32, (1, CPAD), 1)
    logits = mm(final, low_head[...]) + head_bias[...]
    logits = jnp.where(class_lane < NCLS, logits, -1e30)
    peak = jnp.max(logits, axis=-1, keepdims=True)
    shifted = logits - peak
    raw = jnp.exp(shifted)
    total = jnp.sum(raw, axis=-1, keepdims=True)
    alive = jnp.where(labels >= 0.0, 1.0, 0.0)
    target = jnp.where(class_lane.astype(F32) == labels, 1.0 - SMOOTHING, 0.0) + jnp.where(
        class_lane < NCLS, SMOOTHING / NCLS, 0.0
    )
    log_probs = jnp.where(class_lane < NCLS, shifted - jnp.log(total), 0.0)
    losses = -jnp.sum(target * log_probs, axis=-1, keepdims=True) * alive
    d_logits = ((raw * (1.0 / total) - target) * alive).astype(BF)
    d_final = mm_nt(d_logits, low_head[...])
    last_row = VEC_AT + 12 * LAYERS
    V[last_row : last_row + 1, 0:D] = down_sum(d_final * nf)
    V[last_row + 1 : last_row + 2, 0:D] = down_sum(d_final)
    V[last_row + 2 : last_row + 3, 0:128] = jnp.broadcast_to(down_sum(losses), (1, 128))
    V[last_row + 3 : last_row + 4, 0:128] = count[...]
    d_top = norm_back(d_final, nf, inf, gain_final)
    low_top = d_top.astype(BF)
    store_vector(last, 7 * D + FF, down_sum(d_top))
    d_up = (mm_nt(low_top, wdn[last]) * slope).astype(BF)
    store_vector(last, 7 * D, down_sum(d_up.astype(F32)))
    d_h2 = mm_nt(d_up, win[last, :, 4 * D :])
    store_vector(last, 5 * D, down_sum(d_h2 * n2))
    store_vector(last, 6 * D, down_sum(d_h2))
    d_middle = d_top + norm_back(d_h2, n2, i2, vector(last, 5 * D, D))
    low_middle = d_middle.astype(BF)
    store_vector(last, 4 * D, down_sum(d_middle))
    d_heads = mm_nt(low_middle, win[last, :, 3 * D : 4 * D]).astype(BF)
    d_queries = []
    for image in range(KEPT):
        rows = slice(image * BLK, (image + 1) * BLK)
        ups = spread(d_heads[image * 16 : (image + 1) * 16])
        probs = probabilities[image]
        d_probs = mm_nt(ups, DA[rows, :])
        inner = jnp.sum(d_probs * probs, axis=-1, keepdims=True)
        d_scores = (probs * (d_probs - inner)).astype(BF)
        d_queries.append(gather_heads(mm(d_scores, DMB[rows, :])) * 0.125)
        DMB[rows, :] = mm_tn(d_scores, spread_queries[image]).astype(BF)
        DA[rows, :] = mm_tn(probs.astype(BF), ups).astype(BF)
    d_query = jnp.concatenate(d_queries, axis=0).astype(BF)
    store_vector(last, 2 * D, down_sum(d_query.astype(F32)))
    from_query = mm_nt(d_query, win[last, :, 0:D])

    pick_row = lax.broadcasted_iota(jnp.int32, (group, CROWS), 0)
    pick_lane = lax.broadcasted_iota(jnp.int32, (group, CROWS), 1)
    pick = jnp.where(
        ((pick_row - KEPT * here.shard) * 16 + (CLS - TAIL)) == pick_lane, 1.0, 0.0
    ).astype(BF)
    at = 0
    for piece in (active, h2, attended, h1, final, low_top):
        FAC[0, :, at : at + piece.shape[-1]] = mm(pick, piece).astype(BF)
        at += piece.shape[-1]
    at = 0
    for piece in (d_up, low_middle, d_query, d_logits):
        FAC[1, :, at : at + piece.shape[-1]] = mm(pick, piece).astype(BF)
        at += piece.shape[-1]
    FAC[1, :, at:] = jnp.zeros((group, WFAC - at), BF)
    factors_core()

    turned = DXB[...].T
    for tile, grads in enumerate((DMB, DA)):
        made = mm(turned, grads[...]).astype(BF)
        for shard in range(n_shard):
            GS[0, shard // 2, shard % 2, tile * rows_in : (tile + 1) * rows_in, :] = made[
                shard * rows_in : (shard + 1) * rows_in
            ]
    reduce_core(CHUNKS)
    factors_y()
    store_sums(last, [(3 * D, fold(DA[...].astype(F32)))])

    X[...] = jnp.zeros((ROWS, D), F32)
    gain = vector(last, 0, D)
    gain_sum, shift_sum = zeros, zeros
    for image in range(KEPT):
        rows = slice(image * BLK + TAIL, (image + 1) * BLK)
        part = from_query[image * 16 : (image + 1) * 16]
        normed = N1[last, rows, :].astype(F32)
        gain_sum = gain_sum + fold(part * normed)
        shift_sum = shift_sum + fold(part)
        X[rows, :] = d_middle[image * 16 : (image + 1) * 16] + norm_back(
            part, normed, I1[last, rows, :][:, 0:1], gain
        )

    def first_back(layer, half, made, sums):
        base = half * HALF
        gain = vector(layer, 0, D)
        gain_sum, shift_sum = sums
        for at, size in pieces(HALF):
            rows = pl.ds(aligned(base + at, 16), size)
            part = made[at : at + size]
            normed = N1[layer, rows, :].astype(F32)
            inverse = I1[layer, rows, :][:, 0:1]
            gain_sum = gain_sum + fold(part * normed)
            shift_sum = shift_sum + fold(part)
            X[rows, :] = X[rows, :] + norm_back(part, normed, inverse, gain)
        return gain_sum, shift_sum

    def last_back(half, sums):
        rows = pl.ds(aligned(half * HALF, 16), HALF)
        made = mm_nt(DMB[rows, :], win[last, :, D : 2 * D])
        made = made + mm_nt(DA[rows, :], win[last, :, 2 * D : 3 * D])
        return first_back(last, half, made, sums)

    gain_sum, shift_sum = lax.fori_loop(0, 2, last_back, (gain_sum, shift_sum))
    store_sums(last, [(0, gain_sum), (D, shift_sum)])
    reduce_y(CHUNKS)
    factors_x()

    def mlp_back(layer, half, sums):
        base = half * HALF
        whole = pl.ds(aligned(base, 16), HALF)
        bias_down, bias_up, gain_sum, shift_sum, bias_out = sums
        for at, size in pieces(HALF):
            rows = pl.ds(aligned(base + at, 16), size)
            up = X[rows, :]
            DXB[rows, :] = up.astype(BF)
            bias_down = bias_down + fold(up)
        low = DXB[whole, :]
        ups = []
        for tile in range(4):
            columns = slice(tile * D, (tile + 1) * D)
            made = mm_nt(low, wdn[layer, columns, :])
            total = bias_up[tile]
            for at, size in pieces(HALF):
                rows = pl.ds(aligned(base + at, 16), size)
                grad = (made[at : at + size] * SLOPE[layer, rows, columns].astype(F32)).astype(BF)
                SLOPE[layer, rows, columns] = grad
                total = total + fold(grad.astype(F32))
            ups.append(total)
        made = mm_nt(SLOPE[layer, whole, :], win[layer, :, 4 * D :])
        gain = vector(layer, 5 * D, D)
        for at, size in pieces(HALF):
            rows = pl.ds(aligned(base + at, 16), size)
            part = made[at : at + size]
            normed = N2[layer, rows, :].astype(F32)
            inverse = I2[layer, rows, :][:, 0:1]
            gain_sum = gain_sum + fold(part * normed)
            shift_sum = shift_sum + fold(part)
            grad = X[rows, :] + norm_back(part, normed, inverse, gain)
            X[rows, :] = grad
            DMB[rows, :] = grad.astype(BF)
            bias_out = bias_out + fold(grad)
        DA[whole, :] = mm_nt(DMB[whole, :], win[layer, :, 3 * D : 4 * D]).astype(BF)
        return bias_down, tuple(ups), gain_sum, shift_sum, bias_out

    def attend_back(layer, image):
        rows = pl.ds(aligned(image * BLK, 16), BLK)
        for pair in range(3):
            at = pair * 128
            query = QKV[layer, rows, at : at + 128] * BF(0.125)
            keys = QKV[layer, rows, D + at : D + at + 128]
            values = QKV[layer, rows, 2 * D + at : 2 * D + at + 128]
            ups = DA[rows, at : at + 128]
            keys_both = jnp.concatenate([keys * even, keys * odd], axis=0)
            values_both = jnp.concatenate([values * even, values * odd], axis=0)
            scores = mm_nt(keys_both, query).reshape(2, BLK, BLK) + key_column[None]
            raw = jnp.exp(scores - jnp.max(scores, axis=1, keepdims=True))
            probs = raw * (1.0 / jnp.sum(raw, axis=1, keepdims=True))
            d_probs = mm_nt(values_both, ups).reshape(2, BLK, BLK)
            inner = jnp.sum(d_probs * probs, axis=1, keepdims=True)
            d_scores = (probs * (d_probs - inner)).astype(BF).reshape(2 * BLK, BLK)
            probs = probs.astype(BF).reshape(2 * BLK, BLK)
            d_values = mm(probs, ups)
            d_keys = mm(d_scores, query)
            d_query = mm_tn(d_scores, keys_both) * 0.125
            QKV[layer, rows, at : at + 128] = d_query.astype(BF)
            QKV[layer, rows, D + at : D + at + 128] = jnp.where(
                low_lane, d_keys[:BLK], d_keys[BLK:]
            ).astype(BF)
            QKV[layer, rows, 2 * D + at : 2 * D + at + 128] = jnp.where(
                low_lane, d_values[:BLK], d_values[BLK:]
            ).astype(BF)

    def renew(ref, layer, at):
        gain, shift = vector(layer, at, D), vector(layer, at + D, D)

        def one(index, nothing):
            rows = pl.ds(aligned(index * 64, 16), 64)
            DXB[rows, :] = (ref[layer, rows, :].astype(F32) * gain + shift).astype(BF)
            return nothing

        lax.fori_loop(0, ROWS // 64, one, 0)
        return DXB[...].T

    def keep_in(k, tile, made):
        for shard in range(n_shard):
            G[k, shard // 2, shard % 2, tile * rows_in : (tile + 1) * rows_in, :] = made[
                shard * rows_in : (shard + 1) * rows_in
            ]

    def backward(step, carry):
        layer = LAYERS - 2 - step
        kd, ku, kq = 3 * step, 3 * step + 1, 3 * step + 2
        upper_layer, bottom = step == 0, step == 1

        def one(half, sums):
            sums = mlp_back(layer, half, sums)
            begin = half == 0

            @pl.when(jnp.logical_and(upper_layer, begin))
            def _():
                factors_z()

            @pl.when(jnp.logical_and(bottom, begin))
            def _():
                reduce_x(2)
                gather_x(1)

            return sums

        bias_down, bias_up, gain_sum, shift_sum, bias_out = lax.fori_loop(
            0, 2, one, (zeros, (zeros,) * 4, zeros, zeros, zeros)
        )
        when(upper_layer, (reduce_x, CHUNKS))
        when(bottom, (reduce_z, 2), (gather_done, 0))
        store_sums(
            layer,
            [(7 * D + FF, bias_down), (5 * D, gain_sum), (6 * D, shift_sum), (4 * D, bias_out)]
            + [(7 * D + tile * D, bias_up[tile]) for tile in range(4)],
        )
        turned = DXB[...].T
        per = min(rows_down, D)
        for tile in range(4):
            columns = slice(tile * D, (tile + 1) * D)
            made = mm(turned, ACT[layer, :, columns]).astype(BF).T
            for piece in range(D // per):
                shard, at = divmod(tile * D + piece * per, rows_down)
                G[kd, shard // 2, shard % 2, at : at + per, :] = made[
                    piece * per : (piece + 1) * per
                ]
        when(upper_layer, (reduce_core, 0))
        when(bottom, (reduce_core, 3), (gather_z, 2))
        turned = renew(N2, layer, 5 * D)
        for tile in range(4):
            keep_in(
                ku, tile, mm(turned, SLOPE[layer, :, tile * D : (tile + 1) * D]).astype(BF)
            )
        when(upper_layer, (reduce_core, 1), (reduce_y, 0), (reduce_z, CHUNKS))
        when(bottom, (reduce_core, 4), (reduce_y, 3), (gather_x, 2), (gather_done, 1))
        keep_in(kq, 3, mm(ATT[layer].T, DMB[...]).astype(BF))

        def two(image, nothing):
            attend_back(layer, image)
            first = jnp.logical_and(upper_layer, image == 0)
            when(first, (gather_z, CHUNKS))

            @pl.when(first)
            def _():
                factors_mate()

            when(jnp.logical_and(upper_layer, image == 1), (reduce_y, 1), (reduce_x, 0))
            when(jnp.logical_and(upper_layer, image == 2), (reduce_z, 0), (gather_x, CHUNKS))
            when(jnp.logical_and(upper_layer, image == 3), (reduce_x, 1), (gather_done, CHUNKS))
            when(jnp.logical_and(bottom, image == 0), (reduce_x, 3))
            when(jnp.logical_and(bottom, image == 1), (reduce_y, 4), (gather_done, 2))
            when(jnp.logical_and(bottom, image == 2), (reduce_z, 3), (reduce_x, 4))
            when(jnp.logical_and(bottom, image == 3), (gather_z, 3), (reduce_z, 4))
            return nothing

        lax.fori_loop(0, KEPT, two, 0)
        turned = renew(N1, layer, 0)
        for tile in range(3):
            keep_in(
                kq, tile, mm(turned, QKV[layer, :, tile * D : (tile + 1) * D]).astype(BF)
            )
        when(upper_layer, (reduce_core, 2), (gather_z, 0), (reduce_z, 1))
        when(bottom, (reduce_core, 5), (gather_x, 3), (gather_z, 4))
        store_sums(
            layer,
            [
                (2 * D, fold(QKV[layer, :, 0:D].astype(F32))),
                (3 * D, fold(QKV[layer, :, 2 * D : 3 * D].astype(F32))),
            ],
        )

        def three(half, sums):
            rows = pl.ds(aligned(half * HALF, 16), HALF)
            made = mm_nt(QKV[layer, rows, :], win[layer, :, 0 : 3 * D])
            return first_back(layer, half, made, sums)

        gain_sum, shift_sum = lax.fori_loop(0, 2, three, (zeros, zeros))
        store_sums(layer, [(0, gain_sum), (D, shift_sum)])
        when(upper_layer, (reduce_y, 2), (gather_x, 0), (gather_z, 1))
        when(bottom, (reduce_y, 5), (gather_done, 3), (gather_x, 4))
        return carry

    lax.fori_loop(0, LAYERS - 1, backward, 0)
    factors_done()

    for at, size in pieces(BLK):
        total = None
        for image in range(KEPT):
            part = X[image * BLK + at : image * BLK + at + size, :]
            DXB[image * BLK + at : image * BLK + at + size, :] = part.astype(BF)
            total = part if total is None else total + part
        V[at : at + size, 0:D] = total

    vec = ("v", v_send, v_recv)
    v_y, v_x = 1, n_y
    v_z = v_x + n_x - 1
    v_gz = v_z + n_z - 1
    v_q = v_gz + n_z - 1
    v_gx = v_q + n_z - 1
    v_gy = v_gx + n_x - 1
    v_gc = v_gy + n_y - 1
    rows_c = VEC_ROWS // 2
    rows_y = rows_c // n_y
    rows_x = rows_y // n_x
    split_z = cut(rows_x, n_z, 8)
    rows_z = rows_x // split_z
    at_c = c * rows_c
    at_y = at_c + y * rows_y
    at_x = at_y + x * rows_x
    at_z = at_x + z * rows_z if split_z > 1 else at_x

    def vrows(ref, at, rows):
        return ref.at[pl.ds(aligned(at, 8), rows), :]

    def narrow(at, rows):
        return VF.at[pl.ds(aligned(at, 8), rows), pl.ds(0, D)]

    def vadd(at, rows, sources):
        target = pl.ds(aligned(at, 8), rows)
        total = V[target, :]
        for source in sources:
            total = total + source
        V[target, :] = total

    def vectors_core():
        go(lambda: vrows(V, (1 - c) * rows_c, rows_c), VC, vec, 0, mate)

    def vectors_y():
        arrived(VC, v_recv.at[0], v_send.at[0])
        vadd(at_c, rows_c, [VC[...]])
        for o in range(1, n_y):
            to = turn(y, o, n_y)
            go(
                lambda o=o: vrows(V, at_c + turn(y, o, n_y) * rows_y, rows_y), VY.at[o - 1],
                vec, v_y + o - 1, here.to(y=to),
            )

    def vectors_x():
        for o in range(1, n_y):
            arrived(VY.at[o - 1], v_recv.at[v_y + o - 1], v_send.at[v_y + o - 1])
        vadd(at_y, rows_y, [VY[o - 1] for o in range(1, n_y)])
        for o in range(1, n_x):
            to = turn(x, o, n_x)
            go(
                lambda o=o: vrows(V, at_y + turn(x, o, n_x) * rows_x, rows_x), VX.at[o - 1],
                vec, v_x + o - 1, here.to(x=to),
            )

    def vectors_z():
        for o in range(1, n_x):
            arrived(VX.at[o - 1], v_recv.at[v_x + o - 1], v_send.at[v_x + o - 1])
        vadd(at_x, rows_x, [VX[o - 1] for o in range(1, n_x)])
        for o in range(1, n_z):

            def make(o=o):
                at = at_x + turn(z, o, n_z) * rows_z if split_z > 1 else at_x
                return vrows(V, at, rows_z)

            go(make, VZ.at[z], vec, v_z + o - 1, here.to(z=turn(z, o, n_z)))

    def vectors_gather_z():
        for o in range(1, n_z):
            arrived(
                VZ.at[turn(z, n_z - o, n_z)], v_recv.at[v_z + o - 1], v_send.at[v_z + o - 1]
            )
        target = pl.ds(aligned(at_z, 8), rows_z)
        VZ[z] = V[target, :]
        total = VZ[0]
        for index in range(1, n_z):
            total = total + VZ[index]
        VF[target, 0:D] = total[:, 0:D]
        if split_z > 1:
            for o in range(1, n_z):
                go(
                    lambda: narrow(at_z, rows_z), narrow(at_z, rows_z), vec, v_gz + o - 1,
                    here.to(z=turn(z, o, n_z)),
                )

    def squares_send():
        SQ[...] = square_sum[...]
        SQS[z] = square_sum[...]
        for o in range(1, n_z):
            go(lambda: SQ, SQS.at[z], vec, v_q + o - 1, here.to(z=turn(z, o, n_z)))

    def vectors_gather_x():
        for o in range(1, n_z):
            came = turn(z, n_z - o, n_z)
            if split_z > 1:
                arrived(
                    narrow(at_x + came * rows_z, rows_z), v_recv.at[v_gz + o - 1],
                    v_send.at[v_gz + o - 1],
                )
            arrived(SQS.at[came], v_recv.at[v_q + o - 1], v_send.at[v_q + o - 1])
        total = SQS[0]
        for index in range(1, n_z):
            total = total + SQS[index]
        for at in range(0, rows_x, 8):
            VF[pl.ds(aligned(at_x + at, 8), 8), D:] = total
        for o in range(1, n_x):
            go(
                lambda: vrows(VF, at_x, rows_x), vrows(VF, at_x, rows_x), vec, v_gx + o - 1,
                here.to(x=turn(x, o, n_x)),
            )

    def vectors_gather_y():
        for o in range(1, n_x):
            at = at_y + turn(x, n_x - o, n_x) * rows_x
            arrived(vrows(VF, at, rows_x), v_recv.at[v_gx + o - 1], v_send.at[v_gx + o - 1])
        for o in range(1, n_y):
            go(
                lambda: vrows(VF, at_y, rows_y), vrows(VF, at_y, rows_y), vec, v_gy + o - 1,
                here.to(y=turn(y, o, n_y)),
            )

    def vectors_gather_core():
        for o in range(1, n_y):
            at = at_c + turn(y, n_y - o, n_y) * rows_y
            arrived(vrows(VF, at, rows_y), v_recv.at[v_gy + o - 1], v_send.at[v_gy + o - 1])
        go(lambda: vrows(VF, at_c, rows_c), vrows(VF, at_c, rows_c), vec, v_gc, mate)

    def vectors_done():
        arrived(vrows(VF, (1 - c) * rows_c, rows_c), v_recv.at[v_gc], v_send.at[v_gc])

    vectors_core()
    low = DXB[...]
    for tile in range(2):
        made = mm_tn(pix[:, :, tile * D : (tile + 1) * D].reshape(ROWS, D), low).astype(BF)
        for piece in range(D // rows_patch):
            shard = tile * (D // rows_patch) + piece
            GS[1, shard // 2, shard % 2] = made[piece * rows_patch : (piece + 1) * rows_patch]

    kp = CHUNKS + 1
    reduce_core(kp)
    reduce_x(5)
    vectors_y()
    gather_done(4)
    reduce_y(kp)
    reduce_z(5)
    vectors_x()
    reduce_x(kp)
    gather_z(5)
    vectors_z()
    reduce_z(kp)
    vectors_gather_z()
    gather_x(5)
    gather_z(kp)
    squares_send()
    gather_x(kp)
    vectors_gather_x()
    gather_done(5)
    gather_done(kp)
    vectors_gather_y()
    vectors_gather_core()
    vectors_done()
    last_copy = pltpu.make_async_copy(VF, vec_out, out_local.at[1 + CHUNKS + 2])
    last_copy.start()
    for source, send, recv, at in list(sent.values()):
        left_here(source(), recv.at[at], send.at[at])
    for k in range(CHUNKS + 2):
        result(k).wait()
    last_copy.wait()

    @pl.when(jnp.logical_not(lower))
    def _():
        left_here(given, img_recv.at[0], img_send.at[0])
        left_here(lab_pairs.at[2], img_recv.at[1], img_send.at[1])


def run_train(n_rep, n_shard, patches, lab_pairs, own_patch, own_in, own_down, vecs, glob, pos, head, count):
    n_x = 2 ** ((n_rep.bit_length() - 2) // 2)
    n_z, n_y = n_rep // n_x, n_shard // 2
    block = 4 * (D // n_shard)
    group = KEPT * n_shard
    keep = LAYERS - 1
    units = 1 + 3 * LAYERS
    chunks = CHUNKS + 2

    def buf(*shape, dtype=BF):
        return pltpu.VMEM(shape, dtype)

    def sems(*shape):
        return pltpu.SemaphoreType.DMA(shape)

    def reduction(count, rows):
        by_x = cut(rows, n_x, 16)
        by_z = cut(rows // by_x, n_z, 16)
        return [
            buf(count, n_y, 2, rows, D),
            buf(min(count, 3), n_y, rows, D),
            buf(min(count, 3), n_y - 1, rows, D),
            buf(count, n_x - 1 if by_x > 1 else n_x, rows // by_x, D),
            buf(count, n_z, rows // by_x // by_z, D),
            buf(count, rows, D),
        ]

    rows_y = VEC_ROWS // 2 // n_y
    rows_x = rows_y // n_x
    rows_z = rows_x // cut(rows_x, n_z, 8)
    ag_count = n_y + (n_y - 1) * (n_x - 1) * 2 + n_y - 1
    rs_count = 1 + (n_y - 1) + 2 * (n_x - 1) + 2 * (n_z - 1)
    f_count = 1 + (n_y - 1) + (n_x - 1) + (n_z - 1) + 1
    v_count = 1 + 2 * (n_y - 1) + 2 * (n_x - 1) + 3 * (n_z - 1) + 1
    whole = pl.BlockSpec(memory_space=pltpu.VMEM)
    there = pl.BlockSpec(memory_space=pl.ANY)
    return pl.pallas_call(
        functools.partial(train, n_rep, n_shard),
        out_shape=[
            jax.ShapeDtypeStruct((CHUNKS, block, D), BF),
            jax.ShapeDtypeStruct((2, block // 2, D), BF),
            jax.ShapeDtypeStruct((VEC_ROWS, VEC_WIDE), F32),
            jax.ShapeDtypeStruct((2, n_rep, group, WFAC), BF),
        ],
        in_specs=[there] * 5 + [whole] * 5,
        out_specs=[there] * 4,
        scratch_shapes=[
            buf(ROWS, D, dtype=F32),
            buf(LAYERS, ROWS, D),
            buf(LAYERS, ROWS, 128, dtype=F32),
            buf(keep, ROWS, 3 * D),
            buf(keep, ROWS, D),
            buf(keep, ROWS, D),
            buf(keep, ROWS, 128, dtype=F32),
            buf(keep, ROWS, FF),
            buf(keep, ROWS, FF),
            buf(ROWS, D),
            buf(ROWS, D),
            buf(ROWS, D),
            buf(KEPT, BLK, PATCH_DIM),
            buf(2, 32, 128, dtype=F32),
            buf(PATCH_DIM, D),
            buf(LAYERS, D, 4 * D + FF),
            buf(LAYERS, FF, D),
            buf(D, CPAD),
            buf(1, CPAD, dtype=F32),
            *reduction(CHUNKS, block),
            *reduction(2, block // 2),
            buf(2, group, WFAC),
            buf(group, WFAC),
            buf(n_y - 1, group, WFAC),
            buf(n_x, group, WFAC),
            buf(VEC_ROWS, VEC_WIDE, dtype=F32),
            buf(VEC_ROWS // 2, VEC_WIDE, dtype=F32),
            buf(n_y - 1, rows_y, VEC_WIDE, dtype=F32),
            buf(n_x - 1, rows_x, VEC_WIDE, dtype=F32),
            buf(n_z, rows_z, VEC_WIDE, dtype=F32),
            buf(VEC_ROWS, VEC_WIDE, dtype=F32),
            buf(8, 128, dtype=F32),
            buf(n_z, 8, 128, dtype=F32),
            buf(8, 128, dtype=F32),
            sems(units, ag_count),
            sems(units, ag_count),
            sems(units),
            sems(chunks, rs_count),
            sems(chunks, rs_count),
            sems(f_count),
            sems(f_count),
            sems(v_count),
            sems(v_count),
            sems(2),
            sems(2),
            sems(4),
            sems(2 + chunks),
        ],
        compiler_params=pltpu.CompilerParams(
            vmem_limit_bytes=65400 * 1024, collective_id=0, has_side_effects=True
        ),
        cost_estimate=pl.CostEstimate(
            flops=24_000_000_000, bytes_accessed=30_000_000, transcendentals=10_000_000
        ),
        name="train_step",
    )(patches, lab_pairs, own_patch, own_in, own_down, vecs, glob, pos, head, count)


def adam(weight, first, second, grad, factor, rate):
    grad = grad * factor
    first = BETA_FIRST * first + (1.0 - BETA_FIRST) * grad
    second = BETA_SECOND * second + (1.0 - BETA_SECOND) * grad * grad
    first_hat = first * (1.0 / (1.0 - BETA_FIRST**ADAM_STEP))
    second_hat = second * (1.0 / (1.0 - BETA_SECOND**ADAM_STEP))
    step = first_hat / (jnp.sqrt(second_hat) + ADAM_EPS) + WEIGHT_DECAY * weight
    return weight - rate * step, first, second


def update(n_rep, n_shard, *refs):
    res, small, vec, factors = refs[0:4]
    sources = refs[4:25]
    loss_out, norm_out = refs[25:27]
    targets = refs[27:48]
    buffers = refs[48:69]
    last_in, last_down, grad_head, in_sems, out_sems = refs[69:]
    shard = lax.axis_index("shard")
    rows_in = D // n_shard
    rows_down = FF // n_shard
    keep = LAYERS - 1

    def moves(array, layer=None, out=False):
        found = []
        for kind in range(3):
            index = 3 * array + kind
            if out:
                src, dst, sem = buffers[index], targets[index], out_sems
            else:
                src, dst, sem = sources[index], buffers[index], in_sems
            slot = 0 if layer is None else layer
            if layer is not None:
                src, dst = src.at[layer], dst.at[layer]
            found.append(pltpu.make_async_copy(src, dst, sem.at[index, slot]))
        return found

    layered = [(1, layer) for layer in range(LAYERS)] + [(2, layer) for layer in range(LAYERS)]
    order = layered + [(0, None), (6, None), (5, None), (3, None), (4, None)]
    for array, layer in order:
        for move in moves(array, layer):
            move.start()

    n_rows = factors.shape[1] * factors.shape[2]

    def factor(half, at, size):
        return factors[half, :, :, at : at + size].reshape(n_rows, size)

    def squares(values):
        return fold(values * values)

    total = jnp.zeros((8, D), F32)
    h2 = factor(0, FF, D)
    for tile in range(4):
        made = mm_tn(h2, factor(1, tile * D, D))
        last_in[:, (2 + tile) * D : (3 + tile) * D] = made
        total = total + squares(made)
    made = mm_tn(factor(0, FF + 2 * D, D), factor(1, FF + D, D))
    last_in[:, 0:D] = made
    total = total + squares(made)
    made = mm_tn(factor(0, FF + D, D), factor(1, FF, D))
    last_in[:, D : 2 * D] = made
    total = total + squares(made)
    d_top = factor(0, FF + 4 * D, D)
    for tile in range(4):
        made = mm_tn(factor(0, tile * D, D), d_top)
        last_down[tile * D : (tile + 1) * D, :] = made
        total = total + squares(made)
    final = factor(0, FF + 3 * D, D)
    wide = jnp.zeros((8, 128), F32)
    for at in range(0, CPAD, 512):
        d_logits = factor(1, FF + 2 * D + at, 512)
        made = mm_tn(final, d_logits)
        grad_head[0:D, at : at + 512] = made
        bias = down_sum(d_logits.astype(F32))
        grad_head[D : D + 1, at : at + 512] = bias
        sums = squares(made)
        for lane in range(0, 512, 128):
            wide = wide + sums[:, lane : lane + 128]
            row = bias[:, lane : lane + 128]
            wide = wide + (row * row) * 0.125
    for lane in range(0, D, 128):
        wide = wide + total[:, lane : lane + 128]
    used = VEC_AT + 12 * LAYERS + 2
    parts = jnp.zeros((8, D), F32)
    kept_rows = lax.broadcasted_iota(jnp.int32, (8, 1), 0)
    for at in range(0, used, 8):
        value = vec[at : at + 8, 0:D]
        if at + 8 > used:
            value = jnp.where(kept_rows + at < used, value, 0.0)
        parts = parts + value * value
    patch_bias = down_sum(vec[0:PATCHES, 0:D])
    class_row = vec[CLS : CLS + 1, 0:D]
    rest = (patch_bias * patch_bias + class_row * class_row) * 0.125
    parts = parts + rest
    for lane in range(0, D, 128):
        wide = wide + parts[:, lane : lane + 128]
    n_x = 2 ** ((n_rep.bit_length() - 2) // 2)
    rows_x = VEC_ROWS // n_shard // n_x
    wide = wide + fold(vec[:, D:]) * (8.0 / rows_x)
    sum_squares = jnp.sum(jnp.sum(wide, axis=1, keepdims=True), axis=0, keepdims=True)
    inv_count = 1.0 / vec[used + 1 : used + 2, 0:1]
    grad_norm = jnp.sqrt(sum_squares) * inv_count
    norm_out[...] = grad_norm
    loss_out[...] = vec[used : used + 1, 0:1] * inv_count
    scale = jnp.minimum(1.0, CLIP_NORM / grad_norm) * inv_count

    def apply(array, where, grad, rate):
        refs = [buffers[3 * array + kind] for kind in range(3)]
        made = adam(refs[0][where], refs[1][where], refs[2][where], grad, scale, rate)
        for ref, value in zip(refs, made):
            ref[where] = value

    def begin(array, layer=None):
        for move in moves(array, layer):
            move.wait()

    def finish(array, layer=None):
        for move in moves(array, layer, out=True):
            move.start()

    def in_place(layer, column, at, size):
        return (layer, slice(at, at + size), slice(column * D, (column + 1) * D))

    def in_step(tile_rows):
        return 32 if tile_rows % 32 == 0 else 16

    step = in_step(rows_in)
    own_rows = pl.multiple_of(shard * rows_in, 8)
    for layer in range(LAYERS):
        begin(1, layer)
        for column in range(8):
            for at in range(0, rows_in, step):
                if layer < keep:
                    k = 3 * (keep - 1 - layer) + (2 if column < 4 else 1)
                    row = (column % 4) * rows_in + at
                    grad = res[k, row : row + step, :].astype(F32)
                elif column in (1, 2):
                    row = (column - 1) * rows_in + at
                    grad = small[0, row : row + step, :].astype(F32)
                else:
                    held = 0 if column == 0 else column - 2
                    grad = last_in[
                        pl.ds(own_rows + at, step), held * D : (held + 1) * D
                    ]
                apply(1, in_place(layer, column, at, step), grad, LEARNING_RATE)
        finish(1, layer)
    down_rows = pl.multiple_of(shard * rows_down, 8)
    for layer in range(LAYERS):
        begin(2, layer)
        for at in range(0, rows_down, 32):
            if layer < keep:
                grad = res[3 * (keep - 1 - layer), at : at + 32, :].astype(F32)
            else:
                grad = last_down[pl.ds(down_rows + at, 32), :]
            apply(2, (layer, slice(at, at + 32), slice(0, D)), grad, LEARNING_RATE)
        finish(2, layer)
    begin(0)
    for at in range(0, PATCH_DIM // n_shard, 32):
        grad = small[1, at : at + 32, :].astype(F32)
        apply(0, (slice(at, at + 32), slice(0, D)), grad, LEARNING_RATE)
    finish(0)
    begin(6)
    for at in range(0, D, 32):
        rows = slice(at, at + 32)
        apply(6, (rows, slice(0, NCLS)), grad_head[rows, 0:NCLS], LEARNING_RATE)
    apply(6, (slice(D, D + 1), slice(0, NCLS)), grad_head[D : D + 1, 0:NCLS], LEARNING_RATE)
    finish(6)
    begin(5)
    apply(5, (slice(0, 1), slice(0, D)), class_row, VECTOR_RATE)
    for at in range(0, PATCHES, 28):
        apply(
            5, (slice(1 + at, 29 + at), slice(0, D)), vec[at : at + 28, 0:D], VECTOR_RATE
        )
    finish(5)
    begin(3)
    for layer in range(LAYERS):
        for piece in range(12):
            row = VEC_AT + 12 * layer + piece
            where = (slice(layer, layer + 1), slice(piece * D, (piece + 1) * D))
            apply(3, where, vec[row : row + 1, 0:D], VECTOR_RATE)
    finish(3)
    begin(4)
    rows = [patch_bias, class_row, vec[used - 2 : used - 1, 0:D], vec[used - 1 : used, 0:D]]
    for index, row in enumerate(rows):
        apply(4, (slice(index, index + 1), slice(0, D)), row, VECTOR_RATE)
    finish(4)
    for array, layer in order:
        for move in moves(array, layer, out=True):
            move.wait()


def run_update(n_rep, n_shard, res, small, vec, factors, arrays):
    whole = pl.BlockSpec(memory_space=pltpu.VMEM)
    there = pl.BlockSpec(memory_space=pl.ANY)
    one = jax.ShapeDtypeStruct((1, 1), F32)
    made = pl.pallas_call(
        functools.partial(update, n_rep, n_shard),
        out_shape=[one, one] + [jax.ShapeDtypeStruct(a.shape, F32) for a in arrays],
        in_specs=[whole] * 4 + [there] * 21,
        out_specs=[whole] * 2 + [there] * 21,
        scratch_shapes=[pltpu.VMEM(a.shape, F32) for a in arrays]
        + [
            pltpu.VMEM((D, 2 * D + FF), F32),
            pltpu.VMEM((FF, D), F32),
            pltpu.VMEM((D + 8, CPAD), F32),
            pltpu.SemaphoreType.DMA((21, LAYERS)),
            pltpu.SemaphoreType.DMA((21, LAYERS)),
        ],
        compiler_params=pltpu.CompilerParams(vmem_limit_bytes=62 * 1024 * 1024),
        cost_estimate=pl.CostEstimate(
            flops=200_000_000, bytes_accessed=50_000_000, transcendentals=4_000_000
        ),
        name="adamw",
    )(res, small, vec, factors, *arrays)
    return made[0].reshape(()), made[1].reshape(()), made[2:]


def shards(
    n_rep, n_shard,
    patches, labels, counts, patch_w, layer_in, layer_down, layer_vecs, glob_vecs, pos_embed, head,
    m_patch, v_patch, m_in, v_in, m_down, v_down, m_vecs, v_vecs, m_glob, v_glob, m_pos, v_pos,
    m_head, v_head,
):
    slots = patches.shape[0]
    marked = jnp.where(jnp.arange(slots) < counts[0], labels, -1).astype(F32)
    lab_pairs = jnp.where(
        jnp.arange(16)[None, :, None] == CLS - TAIL, marked[:, None, None], -1.0
    )
    lab_pairs = jnp.broadcast_to(lab_pairs, (slots, 16, 128)).reshape(slots // 2, 32, 128)
    count = jnp.broadcast_to(counts.astype(F32)[None], (1, 128))
    padded = jnp.pad(patches, ((0, 0), (0, BLK - PATCHES), (0, 0)))
    res, small, vec, factors = run_train(
        n_rep, n_shard, padded, lab_pairs, patch_w.astype(BF), layer_in.astype(BF),
        layer_down.astype(BF), layer_vecs, glob_vecs, pos_embed, head, count,
    )
    arrays = [
        patch_w, m_patch, v_patch, layer_in, m_in, v_in, layer_down, m_down, v_down,
        layer_vecs, m_vecs, v_vecs, glob_vecs, m_glob, v_glob, pos_embed, m_pos, v_pos,
        head, m_head, v_head,
    ]
    loss, grad_norm, new = run_update(n_rep, n_shard, res, small, vec, factors, arrays)
    return (loss, grad_norm, *new)


def solution(mesh):
    everywhere = P()
    rows = P("shard", None)
    middle = P(None, "shard", None)
    return jax.shard_map(
        functools.partial(shards, mesh.shape["rep"], mesh.shape["shard"]),
        mesh=mesh,
        in_specs=(
            P(("rep", "shard"), None, None),
            P(("rep", "shard")),
            P(("rep", "shard")),
            rows,
            middle,
            middle,
            *(everywhere,) * 4,
            *(rows,) * 2,
            *(middle,) * 4,
            *(everywhere,) * 8,
        ),
        out_specs=(
            *(everywhere,) * 2,
            *(rows,) * 3,
            *(middle,) * 6,
            *(everywhere,) * 12,
        ),
        check_vma=False,
    )
```

```python
import functools

import jax
import jax.numpy as jnp
from jax import lax
from jax.experimental import pallas as pl
from jax.experimental.pallas import tpu as pltpu
from jax.sharding import PartitionSpec as P

D = 384
HEADS = 6
HEAD_DIM = 64
FF = 1536
PATCH_DIM = 768
PATCHES = 196
NCLS = 1000
LAYERS = 3
SEQ = 197

BLK = 208
CLS = 200
TAIL = 192
KEPT = 4
ROWS = KEPT * BLK
HALF = 2 * BLK
CROWS = KEPT * 16
CPAD = 1024
WIDE = 8 * D + FF

NORM_EPS = 1e-06
SMOOTHING = 0.1
CLIP_NORM = 0.05
LEARNING_RATE = 0.05
VECTOR_RATE = 0.5
BETA_FIRST = 0.9
BETA_SECOND = 0.999
ADAM_EPS = 1e-08
WEIGHT_DECAY = 0.05
ADAM_STEP = 10
GELU_SCALE = 0.7978845608028654
GELU_CUBIC = 0.044715

F32 = jnp.float32
BF = jnp.bfloat16


def mm(left, right):
    return jnp.dot(left, right, preferred_element_type=F32)


def mm_nt(left, right):
    return lax.dot_general(left, right, (((1,), (1,)), ((), ())), preferred_element_type=F32)


def mm_tn(left, right):
    return lax.dot_general(left, right, (((0,), (0,)), ((), ())), preferred_element_type=F32)


def fold(values):
    return jnp.sum(values.reshape(-1, 8, values.shape[-1]), axis=0)


def down_sum(values):
    return jnp.sum(values, axis=0, keepdims=True)


def norm(values):
    centre = values - jnp.mean(values, axis=-1, keepdims=True)
    inverse = lax.rsqrt(jnp.mean(centre * centre, axis=-1, keepdims=True) + NORM_EPS)
    return centre * inverse, inverse


def norm_back(upstream, normed, inverse, gain):
    scaled = upstream * gain
    first = jnp.mean(scaled, axis=-1, keepdims=True)
    second = jnp.mean(scaled * normed, axis=-1, keepdims=True)
    return inverse * (scaled - first - normed * second)


def gelu_parts(hidden):
    square = hidden * hidden
    tangent = jnp.tanh(hidden * (GELU_SCALE + (GELU_SCALE * GELU_CUBIC) * square))
    share = 0.5 + 0.5 * tangent
    active = hidden * share
    inner = (2.0 * GELU_SCALE) + (6.0 * GELU_SCALE * GELU_CUBIC) * square
    slope = share + active * (1.0 - share) * inner
    return active, slope


def lane_mask(width, low, high):
    lane = lax.broadcasted_iota(jnp.int32, (1, width), 1)
    return jnp.where((lane >= low) & (lane < high), 1.0, 0.0).astype(BF)


STEP = 32


def pieces(total):
    return [(at, min(STEP, total - at)) for at in range(0, total, STEP)]


WFAC = FF + 5 * D
VEC_ROWS = 256
VEC_AT = BLK
VEC_WIDE = D + 128
MESH = pl.DeviceIdType.MESH
CHUNKS = 6


class Place:
    def __init__(self, n_rep, n_shard):
        self.n_rep, self.n_shard = n_rep, n_shard
        self.n_x = 2 ** ((n_rep.bit_length() - 2) // 2)
        self.n_z = n_rep // self.n_x
        self.n_y = n_shard // 2
        rep, shard = lax.axis_index("rep"), lax.axis_index("shard")
        self.rep, self.shard = rep, shard
        self.z, self.x = rep // self.n_x, rep % self.n_x
        self.y, self.c = shard // 2, shard % 2

    def to(self, x=None, y=None, z=None, c=None):
        x = self.x if x is None else x
        y = self.y if y is None else y
        z = self.z if z is None else z
        c = self.c if c is None else c
        return {"rep": z * self.n_x + x, "shard": y * 2 + c}


def cut(rows, parts, unit):
    return parts if rows % (parts * unit) == 0 else 1


def aligned(value, unit):
    return pl.multiple_of(value, unit)


def train(
    n_rep, n_shard,
    patches, lab_pairs, own_patch, own_in, own_down, vecs, glob, pos, head, count,
    res_out, small_out, vec_out, all_factors,
    X, N1, I1, QKV, ATT, N2, I2, ACT, SLOPE, DXB, DMB, DA,
    pix, lab, wp, win, wdn, low_head, head_bias,
    G, RC, RY, RX, RZ, RES, GS, SC, SY, SX, SZ, SRES,
    FAC, FC, FY, FALL, V, VC, VY, VX, VZ, VF, SQ, SQS, square_sum,
    ag_send, ag_recv, ag_local, rs_send, rs_recv, f_send, f_recv, v_send, v_recv,
    img_send, img_recv, img_local, out_local,
):
    here = Place(n_rep, n_shard)
    n_x, n_y, n_z = here.n_x, here.n_y, here.n_z
    x, y, z, c = here.x, here.y, here.z, here.c
    rows_in, rows_down, rows_patch = D // n_shard, FF // n_shard, PATCH_DIM // n_shard
    block = 4 * rows_in
    mate = here.to(c=1 - c)

    def push(src, dst, send, recv, device):
        pltpu.make_async_remote_copy(
            src_ref=src, dst_ref=dst, send_sem=send, recv_sem=recv,
            device_id=device, device_id_type=MESH,
        ).start()

    def arrived(dst, recv, send):
        pltpu.make_async_remote_copy(
            src_ref=dst, dst_ref=dst, send_sem=send, recv_sem=recv,
            device_id=mate, device_id_type=MESH,
        ).wait_recv()

    def left_here(src, recv, send):
        pltpu.make_async_remote_copy(
            src_ref=src, dst_ref=src, send_sem=send, recv_sem=recv,
            device_id=mate, device_id_type=MESH,
        ).wait_send()

    sent = {}

    def go(source, dst, sems, index, device):
        name, send, recv = sems
        push(source(), dst, send.at[index], recv.at[index], device)
        sent[name, index] = (source, send, recv, index)

    def gone(sems, index):
        source, send, recv, at = sent.pop((sems[0], index))
        left_here(source(), recv.at[at], send.at[at])

    def turn(at, by, size):
        return lax.rem(at + by, size)

    barrier = pltpu.get_barrier_semaphore()
    others = (
        [mate]
        + [here.to(y=turn(y, o, n_y)) for o in range(1, n_y)]
        + [here.to(x=turn(x, o, n_x)) for o in range(1, n_x)]
        + [here.to(z=turn(z, o, n_z)) for o in range(1, n_z)]
    )
    for other in others:
        pl.semaphore_signal(barrier, inc=1, device_id=other, device_id_type=MESH)
    pl.semaphore_wait(barrier, len(others))

    def weight(kind, layer, shard, part=None):
        if kind == "patch":
            parts = cut(rows_patch, n_x, 16)
            rows = rows_patch // parts
            if part is None:
                return wp.at[pl.ds(aligned(shard * rows_patch, 16), rows_patch), :]
            return wp.at[pl.ds(aligned(shard * rows_patch + part * rows, 16), rows), :]
        if kind == "down":
            parts = cut(rows_down, n_x, 16)
            rows = rows_down // parts
            if part is None:
                return wdn.at[layer, pl.ds(aligned(shard * rows_down, 16), rows_down), :]
            return wdn.at[layer, pl.ds(aligned(shard * rows_down + part * rows, 16), rows), :]
        base = 0 if kind == "attn" else 4 * D
        rows = pl.ds(aligned(shard * rows_in, 16), rows_in)
        if part is None:
            return win.at[layer, rows, pl.ds(base, 4 * D)]
        wide = 4 * D // n_x
        return win.at[layer, rows, pl.ds(aligned(base + part * wide, 128), wide)]

    def owned(kind, layer, part=None):
        if kind == "patch":
            if part is None:
                return own_patch
            rows = rows_patch // cut(rows_patch, n_x, 16)
            return own_patch.at[pl.ds(aligned(part * rows, 16), rows), :]
        if kind == "down":
            if part is None:
                return own_down.at[layer]
            rows = rows_down // cut(rows_down, n_x, 16)
            return own_down.at[layer, pl.ds(aligned(part * rows, 16), rows), :]
        base = 0 if kind == "attn" else 4 * D
        if part is None:
            return own_in.at[layer, :, pl.ds(base, 4 * D)]
        wide = 4 * D // n_x
        return own_in.at[layer, :, pl.ds(aligned(base + part * wide, 128), wide)]

    units = [("patch", 0)] + [
        (kind, layer) for layer in range(LAYERS) for kind in ("attn", "up", "down")
    ]

    def parts_of(kind):
        if kind == "patch":
            return cut(rows_patch, n_x, 16)
        if kind == "down":
            return cut(rows_down, n_x, 16)
        return n_x

    ag = ("ag", ag_send, ag_recv)
    base_x = n_y
    base_my = base_x + (n_y - 1) * (n_x - 1)
    base_mx = base_my + (n_y - 1)

    def weights_start(unit):
        kind, layer = units[unit]
        me = here.shard
        part = x if parts_of(kind) > 1 else 0
        for o in range(1, n_y):
            go(
                lambda: owned(kind, layer, part), weight(kind, layer, me, part), ag, (unit, o),
                here.to(y=turn(y, o, n_y)),
            )
        go(lambda: owned(kind, layer), weight(kind, layer, me), ag, (unit, 0), mate)
        pltpu.make_async_copy(
            owned(kind, layer), weight(kind, layer, me), ag_local.at[unit]
        ).start()

    def weights_forward(unit):
        kind, layer = units[unit]
        split = parts_of(kind) > 1
        part = x if split else 0
        for o in range(1, n_y):
            def make(o=o):
                return weight(kind, layer, turn(y, n_y - o, n_y) * 2 + c, part)

            arrived(make(), ag_recv.at[unit, o], ag_send.at[unit, o])
            if split:
                for p in range(1, n_x):
                    index = base_x + (o - 1) * (n_x - 1) + p - 1
                    go(make, make(), ag, (unit, index), here.to(x=turn(x, p, n_x)))
            go(make, make(), ag, (unit, base_my + o - 1), mate)

    def weights_ready(unit):
        kind, layer = units[unit]
        split = parts_of(kind) > 1
        part = x if split else 0
        if split:
            for o in range(1, n_y):
                for p in range(1, n_x):
                    index = (o - 1) * (n_x - 1) + p - 1

                    def make(o=o, p=p):
                        shard = turn(y, n_y - o, n_y) * 2 + c
                        return weight(kind, layer, shard, turn(x, n_x - p, n_x))

                    arrived(
                        make(), ag_recv.at[unit, base_x + index], ag_send.at[unit, base_x + index]
                    )
                    go(make, make(), ag, (unit, base_mx + index), mate)
        pltpu.make_async_copy(
            owned(kind, layer), weight(kind, layer, here.shard), ag_local.at[unit]
        ).wait()
        arrived(weight(kind, layer, y * 2 + 1 - c), ag_recv.at[unit, 0], ag_send.at[unit, 0])
        for o in range(1, n_y):
            shard = turn(y, n_y - o, n_y) * 2 + 1 - c
            index = base_my + o - 1
            arrived(weight(kind, layer, shard, part), ag_recv.at[unit, index], ag_send.at[unit, index])
            if split:
                for p in range(1, n_x):
                    index = base_mx + (o - 1) * (n_x - 1) + p - 1
                    piece = weight(kind, layer, shard, turn(x, n_x - p, n_x))
                    arrived(piece, ag_recv.at[unit, index], ag_send.at[unit, index])

    lower = here.rep < n_rep // 2
    partner = here.to(z=turn(z, n_z // 2, n_z))
    back_half = pix.at[pl.ds(2, 2)]
    given = patches.at[pl.ds(KEPT, 2)]

    def local_half(half):
        return pltpu.make_async_copy(
            patches.at[pl.ds(2 * half, 2)], pix.at[pl.ds(2 * half, 2)], img_local.at[half]
        )

    def local_lab(half):
        return pltpu.make_async_copy(lab_pairs.at[half], lab.at[half], img_local.at[2 + half])

    local_half(0).start()
    local_lab(0).start()

    @pl.when(jnp.logical_not(lower))
    def _():
        push(given, back_half, img_send.at[0], img_recv.at[0], partner)
        push(lab_pairs.at[2], lab.at[1], img_send.at[1], img_recv.at[1], partner)
        local_half(1).start()
        local_lab(1).start()

    for unit in range(4):
        weights_start(unit)

    even = lane_mask(128, 0, 64)
    odd = lane_mask(128, 64, 128)
    low_lane = lax.broadcasted_iota(jnp.int32, (1, 128), 1) < 64
    key_lane = lax.broadcasted_iota(jnp.int32, (1, BLK), 1)
    key_row = jnp.where((key_lane < PATCHES) | (key_lane == CLS), 0.0, -1e30)
    key_sub = lax.broadcasted_iota(jnp.int32, (BLK, 1), 0)
    key_column = jnp.where((key_sub < PATCHES) | (key_sub == CLS), 0.0, -1e30)
    whole_lanes = NCLS // 128 * 128
    low_head[:, 0:whole_lanes] = head[0:D, 0:whole_lanes].astype(BF)
    low_head[:, whole_lanes:] = jnp.zeros((D, CPAD - whole_lanes), BF)
    low_head[:, whole_lanes:NCLS] = head[0:D, whole_lanes:NCLS].astype(BF)
    head_bias[...] = jnp.zeros((1, CPAD), F32)
    head_bias[:, 0:NCLS] = head[D : D + 1, :]
    V[...] = jnp.zeros((VEC_ROWS, VEC_WIDE), F32)
    square_sum[...] = jnp.zeros((8, 128), F32)
    zeros = jnp.zeros((8, D), F32)
    patch_bias = glob[0:1, :]

    def vector(layer, at, size):
        return vecs[pl.ds(layer, 1), at : at + size]

    def store_vector(layer, at, row):
        for piece in range(row.shape[-1] // D):
            V[pl.ds(VEC_AT + 12 * layer + at // D + piece, 1), 0:D] = row[
                :, piece * D : (piece + 1) * D
            ]

    def store_sums(layer, parts):
        for at, part in parts:
            store_vector(layer, at, down_sum(part))

    def embed(half):
        made = mm(pix[pl.ds(2 * half, 2)].reshape(HALF, PATCH_DIM), wp[...])
        for image in range(2):
            start = aligned(half * HALF + image * BLK, 16)
            for at, size in pieces(PATCHES - 4):
                X[pl.ds(start + at, size), :] = (
                    made[image * BLK + at : image * BLK + at + size]
                    + pos[1 + at : 1 + at + size, :]
                    + patch_bias
                )
            X[pl.ds(start + TAIL, 16), :] = jnp.zeros((16, D), F32)
            X[pl.ds(start + TAIL, 4), :] = (
                made[image * BLK + TAIL : image * BLK + PATCHES]
                + pos[1 + TAIL : 1 + PATCHES, :]
                + patch_bias
            )
            X[pl.ds(start + CLS, 1), :] = glob[1:2, :] + pos[0:1, :]

    def first_norm(layer, half, columns):
        base = half * HALF
        gain, shift = vector(layer, 0, D), vector(layer, D, D)
        for at, size in pieces(HALF):
            rows = pl.ds(aligned(base + at, 16), size)
            normed, inverse = norm(X[rows, :])
            N1[layer, rows, :] = normed.astype(BF)
            I1[layer, rows, :] = jnp.broadcast_to(inverse, (size, 128))
            DXB[rows, :] = (normed * gain + shift).astype(BF)
        rows = pl.ds(aligned(base, 16), HALF)
        h1 = DXB[rows, :]
        for tile in columns:
            made = mm(h1, win[layer, :, tile * D : (tile + 1) * D])
            if tile == 0:
                made = made + vector(layer, 2 * D, D)
            if tile == 2:
                made = made + vector(layer, 3 * D, D)
            if len(columns) == 3:
                QKV[layer, rows, tile * D : (tile + 1) * D] = made.astype(BF)
            else:
                (DMB if tile == 1 else DA)[rows, :] = made.astype(BF)

    def attend(layer, image):
        rows = pl.ds(aligned(image * BLK, 16), BLK)
        for pair in range(3):
            at = pair * 128
            query = QKV[layer, rows, at : at + 128] * BF(0.125)
            keys = QKV[layer, rows, D + at : D + at + 128]
            values = QKV[layer, rows, 2 * D + at : 2 * D + at + 128]
            both = jnp.concatenate([query * even, query * odd], axis=0)
            scores = mm_nt(both, keys)
            probs = []
            for row, size in pieces(HALF):
                part = scores[row : row + size] + key_row
                raw = jnp.exp(part - jnp.max(part, axis=-1, keepdims=True))
                share = 1.0 / jnp.sum(raw, axis=-1, keepdims=True)
                probs.append((raw * share).astype(BF))
            probs = jnp.concatenate(probs, axis=0)
            made = mm(probs[:BLK], values * even) + mm(probs[BLK:], values * odd)
            ATT[layer, rows, at : at + 128] = made.astype(BF)

    def mlp(layer, half):
        base = half * HALF
        whole = pl.ds(aligned(base, 16), HALF)
        made = mm(ATT[layer, whole, :], win[layer, :, 3 * D : 4 * D])
        bias_out = vector(layer, 4 * D, D)
        gain, shift = vector(layer, 5 * D, D), vector(layer, 6 * D, D)
        for at, size in pieces(HALF):
            rows = pl.ds(aligned(base + at, 16), size)
            middle = X[rows, :] + made[at : at + size] + bias_out
            X[rows, :] = middle
            normed, inverse = norm(middle)
            N2[layer, rows, :] = normed.astype(BF)
            I2[layer, rows, :] = jnp.broadcast_to(inverse, (size, 128))
            DXB[rows, :] = (normed * gain + shift).astype(BF)
        h2 = DXB[whole, :]
        for tile in range(4):
            columns = slice(tile * D, (tile + 1) * D)
            made = mm(h2, win[layer, :, (4 + tile) * D : (5 + tile) * D])
            bias = vector(layer, 7 * D + tile * D, D)
            for at, size in pieces(HALF):
                rows = pl.ds(aligned(base + at, 16), size)
                active, slope = gelu_parts(made[at : at + size] + bias)
                ACT[layer, rows, columns] = active.astype(BF)
                SLOPE[layer, rows, columns] = slope.astype(BF)
        made = mm(ACT[layer, whole, :], wdn[layer])
        bias = vector(layer, 7 * D + FF, D)
        for at, size in pieces(HALF):
            rows = pl.ds(aligned(base + at, 16), size)
            X[rows, :] = X[rows, :] + made[at : at + size] + bias

    def when(condition, *steps):
        @pl.when(condition)
        def _():
            for step, unit in steps:
                step(unit)

    weights_forward(0)
    weights_ready(0)

    def forward_half(half, carry):
        start = half == 0

        @pl.when(start)
        def _():
            local_half(0).wait()

        @pl.when(jnp.logical_and(half == 1, lower))
        def _():
            arrived(back_half, img_recv.at[0], img_send.at[0])

        @pl.when(jnp.logical_and(half == 1, jnp.logical_not(lower)))
        def _():
            local_half(1).wait()

        embed(half)

        def forward_layer(layer, inner):
            first = jnp.logical_and(start, layer == 0)
            second = jnp.logical_and(start, layer == 1)
            when(first, (weights_forward, 1), (weights_start, 4), (weights_ready, 1))
            when(second, (weights_ready, 4))
            first_norm(layer, half, (0, 1, 2))
            when(first, (weights_forward, 2), (weights_start, 5))
            when(second, (weights_forward, 6), (weights_start, 9))

            def attend_one(index, nothing):
                attend(layer, 2 * half + index)
                begin = index == 0
                when(
                    jnp.logical_and(first, begin), (weights_forward, 3), (weights_start, 6)
                )
                when(jnp.logical_and(second, begin), (weights_forward, 7))
                return nothing

            lax.fori_loop(0, 2, attend_one, 0)
            when(
                first, (weights_forward, 4), (weights_start, 7), (weights_ready, 2),
                (weights_ready, 3),
            )
            when(second, (weights_forward, 8), (weights_ready, 5), (weights_ready, 6))
            mlp(layer, half)
            when(first, (weights_forward, 5), (weights_start, 8))
            when(second, (weights_forward, 9))
            return inner

        return lax.fori_loop(0, LAYERS - 1, forward_layer, carry)

    lax.fori_loop(0, 2, forward_half, 0)
    for unit in (7, 8, 9):
        weights_ready(unit)

    last = LAYERS - 1

    def last_norm(half, nothing):
        first_norm(last, half, (1, 2))
        return nothing

    lax.fori_loop(0, 2, last_norm, 0)

    fac = ("f", f_send, f_recv)
    f_y, f_x = 1, n_y
    f_z = f_x + n_x - 1
    f_m = f_z + n_z - 1
    group = KEPT * n_shard

    def factors_core():
        go(lambda: FAC.at[1 - c], FC, fac, 0, mate)

    def factors_y():
        arrived(FC, f_recv.at[0], f_send.at[0])
        FAC[c] = FAC[c] + FC[...]
        for o in range(1, n_y):
            go(lambda: FAC.at[c], FY.at[o - 1], fac, f_y + o - 1, here.to(y=turn(y, o, n_y)))

    def factors_x():
        total = FAC[c]
        for o in range(1, n_y):
            arrived(FY.at[o - 1], f_recv.at[f_y + o - 1], f_send.at[f_y + o - 1])
            total = total + FY[o - 1]
        FALL[x] = total
        for o in range(1, n_x):
            go(lambda: FALL.at[x], FALL.at[x], fac, f_x + o - 1, here.to(x=turn(x, o, n_x)))

    def all_rows(at):
        return all_factors.at[c, pl.ds(at * n_x, n_x)]

    def factors_z():
        for o in range(1, n_x):
            index = f_x + o - 1
            arrived(FALL.at[turn(x, n_x - o, n_x)], f_recv.at[index], f_send.at[index])
        pltpu.make_async_copy(FALL, all_rows(z), out_local.at[0]).start()
        for o in range(1, n_z):
            go(lambda: FALL, all_rows(z), fac, f_z + o - 1, here.to(z=turn(z, o, n_z)))

    def factors_mate():
        for o in range(1, n_z):
            index = f_z + o - 1
            arrived(all_rows(turn(z, n_z - o, n_z)), f_recv.at[index], f_send.at[index])
        pltpu.make_async_copy(FALL, all_rows(z), out_local.at[0]).wait()
        go(lambda: all_factors.at[c], all_factors.at[c], fac, f_m, mate)

    def factors_done():
        arrived(all_factors.at[1 - c], f_recv.at[f_m], f_send.at[f_m])

    rs = ("rs", rs_send, rs_recv)
    r_y, r_x = 1, n_y
    r_z = r_x + n_x - 1
    r_gz = r_z + n_z - 1
    r_gx = r_gz + n_z - 1

    def chunk(k):
        if k < CHUNKS:
            return G.at[k], RC.at[k % 3], RY.at[k % 3], RX.at[k], RZ.at[k], RES.at[k], block
        k = k - CHUNKS
        return GS.at[k], SC.at[k], SY.at[k], SX.at[k], SZ.at[k], SRES.at[k], block // 2

    def splits(rows):
        by_x = cut(rows, n_x, 16)
        by_z = cut(rows // by_x, n_z, 16)
        return by_x, rows // by_x, by_z, rows // by_x // by_z

    def add_rows(rows, target, target_at, sources):
        step = 48 if rows % 48 == 0 else 16

        def one(index, nothing):
            at = index * step
            to = pl.ds(aligned(target_at + at, 16), step)
            total = target[to, :]
            if len(sources) == 1:
                total = total + sources[0][pl.ds(aligned(at, 16), step), :]
            else:
                total = total.astype(F32)
                for source in sources:
                    total = total + source[pl.ds(aligned(at, 16), step), :].astype(F32)
                total = total.astype(BF)
            target[to, :] = total
            return nothing

        lax.fori_loop(0, rows // step, one, 0)

    def reduce_core(k):
        g, rc = chunk(k)[0:2]
        go(lambda: chunk(k)[0].at[:, 1 - c], rc, rs, (k, 0), mate)

    def reduce_y(k):
        g, rc, ry, _, _, _, rows = chunk(k)
        arrived(rc, rs_recv.at[k, 0], rs_send.at[k, 0])
        for o in list(range(1, n_y)) + [0]:
            at = turn(y, o, n_y)
            add_rows(rows, g.at[at, c], 0, [rc.at[at]])
            if o:
                go(
                    lambda o=o: chunk(k)[0].at[turn(y, o, n_y), c], ry.at[o - 1], rs,
                    (k, r_y + o - 1), here.to(y=at),
                )

    def total_of(slots, count, at, step):
        total = None
        for index in range(count):
            value = slots[index, pl.ds(aligned(at, 16), step), :].astype(F32)
            total = value if total is None else total + value
        return total

    def reduce_x(k):
        g, _, ry, rx, _, _, rows = chunk(k)
        by_x, rows_x = splits(rows)[0:2]
        for o in range(1, n_y):
            arrived(ry.at[o - 1], rs_recv.at[k, r_y + o - 1], rs_send.at[k, r_y + o - 1])
        mine = g.at[y, c]
        add_rows(rows, mine, 0, [ry.at[o - 1] for o in range(1, n_y)])
        for o in range(1, n_x):
            to = turn(x, o, n_x)
            if by_x > 1:

                def make(o=o):
                    at = turn(x, o, n_x) * rows_x
                    return chunk(k)[0].at[y, c, pl.ds(aligned(at, 16), rows_x), :]

                go(make, rx.at[o - 1], rs, (k, r_x + o - 1), here.to(x=to))
            else:
                go(lambda: chunk(k)[0].at[y, c], rx.at[x], rs, (k, r_x + o - 1), here.to(x=to))

    def reduce_z(k):
        g, _, _, rx, rz, _, rows = chunk(k)
        by_x, rows_x, by_z, rows_z = splits(rows)
        mine = g.at[y, c]
        for o in range(1, n_x):
            slot = rx.at[o - 1] if by_x > 1 else rx.at[turn(x, n_x - o, n_x)]
            arrived(slot, rs_recv.at[k, r_x + o - 1], rs_send.at[k, r_x + o - 1])
        if by_x > 1:
            start = x * rows_x
            add_rows(rows_x, mine, start, [rx.at[o - 1] for o in range(1, n_x)])
        else:
            start = 0
            rx[x] = mine[...]
            for o in range(1, n_x):
                gone(rs, (k, r_x + o - 1))
            step = 48 if rows % 48 == 0 else 16

            def one(index, nothing):
                at = pl.ds(aligned(index * step, 16), step)
                g[y, c, at, :] = total_of(rx, n_x, index * step, step).astype(BF)
                return nothing

            lax.fori_loop(0, rows // step, one, 0)
        for o in range(1, n_z):

            def make(o=o):
                at = x * rows_x if by_x > 1 else 0
                if by_z > 1:
                    at = at + turn(z, o, n_z) * rows_z
                return chunk(k)[0].at[y, c, pl.ds(aligned(at, 16), rows_z), :]

            slot = rz.at[o - 1] if by_z > 1 else rz.at[z]
            go(make, slot, rs, (k, r_z + o - 1), here.to(z=turn(z, o, n_z)))

    def gather_z(k):
        g, _, _, _, rz, res, rows = chunk(k)
        by_x, rows_x, by_z, rows_z = splits(rows)
        start = x * rows_x if by_x > 1 else 0
        if by_z > 1:
            start = start + z * rows_z
        for o in range(1, n_z):
            slot = rz.at[o - 1] if by_z > 1 else rz.at[turn(z, n_z - o, n_z)]
            arrived(slot, rs_recv.at[k, r_z + o - 1], rs_send.at[k, r_z + o - 1])
        own_slot = n_z - 1 if by_z > 1 else z
        rz[own_slot] = g[y, c, pl.ds(aligned(start, 16), rows_z), :]
        share = 1.0 / ((1 if by_x > 1 else n_x) * (1 if by_z > 1 else n_z))
        step = 48 if rows_z % 48 == 0 else 16

        def one(index, total):
            low = total_of(rz, n_z, index * step, step).astype(BF)
            res[pl.ds(aligned(start + index * step, 16), step), :] = low
            wide = low.astype(F32)
            return total + fold(wide * wide)

        total = lax.fori_loop(0, rows_z // step, one, zeros) * share
        for at in range(0, D, 128):
            square_sum[...] = square_sum[...] + total[:, at : at + 128]
        if by_z > 1:

            def make():
                at = x * rows_x if by_x > 1 else 0
                return chunk(k)[5].at[pl.ds(aligned(at + z * rows_z, 16), rows_z), :]

            for o in range(1, n_z):
                go(make, make(), rs, (k, r_gz + o - 1), here.to(z=turn(z, o, n_z)))

    def gather_x(k):
        res, rows = chunk(k)[5:7]
        by_x, rows_x, by_z, rows_z = splits(rows)
        if by_z > 1:
            for o in range(1, n_z):
                start = turn(z, n_z - o, n_z) * rows_z
                if by_x > 1:
                    start = start + x * rows_x
                arrived(
                    res.at[pl.ds(aligned(start, 16), rows_z), :],
                    rs_recv.at[k, r_gz + o - 1], rs_send.at[k, r_gz + o - 1],
                )
        if by_x > 1:

            def make():
                return chunk(k)[5].at[pl.ds(aligned(x * rows_x, 16), rows_x), :]

            for o in range(1, n_x):
                go(make, make(), rs, (k, r_gx + o - 1), here.to(x=turn(x, o, n_x)))

    def result(k):
        if k < CHUNKS:
            return pltpu.make_async_copy(RES.at[k], res_out.at[k], out_local.at[1 + k])
        return pltpu.make_async_copy(
            SRES.at[k - CHUNKS], small_out.at[k - CHUNKS], out_local.at[1 + k]
        )

    def gather_done(k):
        res, rows = chunk(k)[5:7]
        by_x, rows_x = splits(rows)[0:2]
        if by_x > 1:
            for o in range(1, n_x):
                start = turn(x, n_x - o, n_x) * rows_x
                arrived(
                    res.at[pl.ds(aligned(start, 16), rows_x), :],
                    rs_recv.at[k, r_gx + o - 1], rs_send.at[k, r_gx + o - 1],
                )
        result(k).start()

    def tails(ref, layer=None):
        found = []
        for image in range(KEPT):
            rows = slice(image * BLK + TAIL, (image + 1) * BLK)
            found.append(ref[rows, :] if layer is None else ref[layer, rows, :])
        return jnp.concatenate(found, axis=0)

    @pl.when(lower)
    def _():
        arrived(lab.at[1], img_recv.at[1], img_send.at[1])

    @pl.when(jnp.logical_not(lower))
    def _():
        local_lab(1).wait()

    local_lab(0).wait()
    labels = lab[...].reshape(CROWS, 128)[:, 0:1]

    h1 = tails(DXB)
    stream = tails(X)
    query = ((mm(h1, win[last, :, 0:D]) + vector(last, 2 * D, D)).astype(BF)) * BF(0.125)
    head_masks = [lane_mask(D, index * 64, (index + 1) * 64) for index in range(HEADS)]

    def spread(values):
        return jnp.concatenate([values * mask for mask in head_masks], axis=0)

    def gather_heads(values):
        total = None
        for index in range(HEADS):
            part = values[index * 16 : (index + 1) * 16] * head_masks[index].astype(F32)
            total = part if total is None else total + part
        return total

    spread_queries, probabilities, outs = [], [], []
    for image in range(KEPT):
        rows = slice(image * BLK, (image + 1) * BLK)
        queries = spread(query[image * 16 : (image + 1) * 16])
        scores = mm_nt(queries, DMB[rows, :]) + key_row
        raw = jnp.exp(scores - jnp.max(scores, axis=-1, keepdims=True))
        probs = raw * (1.0 / jnp.sum(raw, axis=-1, keepdims=True))
        spread_queries.append(queries)
        probabilities.append(probs)
        outs.append(gather_heads(mm(probs.astype(BF), DA[rows, :])))
    attended = jnp.concatenate(outs, axis=0).astype(BF)
    middle = stream + mm(attended, win[last, :, 3 * D : 4 * D]) + vector(last, 4 * D, D)
    n2, i2 = norm(middle)
    h2 = (n2 * vector(last, 5 * D, D) + vector(last, 6 * D, D)).astype(BF)
    active, slope = gelu_parts(mm(h2, win[last, :, 4 * D :]) + vector(last, 7 * D, FF))
    active = active.astype(BF)
    top = middle + mm(active, wdn[last]) + vector(last, 7 * D + FF, D)
    gain_final = glob[2:3, :]
    nf, inf = norm(top)
    final = (nf * gain_final + glob[3:4, :]).astype(BF)
    class_lane = lax.broadcasted_iota(jnp.int32, (1, CPAD), 1)
    logits = mm(final, low_head[...]) + head_bias[...]
    logits = jnp.where(class_lane < NCLS, logits, -1e30)
    peak = jnp.max(logits, axis=-1, keepdims=True)
    shifted = logits - peak
    raw = jnp.exp(shifted)
    total = jnp.sum(raw, axis=-1, keepdims=True)
    alive = jnp.where(labels >= 0.0, 1.0, 0.0)
    target = jnp.where(class_lane.astype(F32) == labels, 1.0 - SMOOTHING, 0.0) + jnp.where(
        class_lane < NCLS, SMOOTHING / NCLS, 0.0
    )
    log_probs = jnp.where(class_lane < NCLS, shifted - jnp.log(total), 0.0)
    losses = -jnp.sum(target * log_probs, axis=-1, keepdims=True) * alive
    d_logits = ((raw * (1.0 / total) - target) * alive).astype(BF)
    d_final = mm_nt(d_logits, low_head[...])
    last_row = VEC_AT + 12 * LAYERS
    V[last_row : last_row + 1, 0:D] = down_sum(d_final * nf)
    V[last_row + 1 : last_row + 2, 0:D] = down_sum(d_final)
    V[last_row + 2 : last_row + 3, 0:128] = jnp.broadcast_to(down_sum(losses), (1, 128))
    V[last_row + 3 : last_row + 4, 0:128] = count[...]
    d_top = norm_back(d_final, nf, inf, gain_final)
    low_top = d_top.astype(BF)
    store_vector(last, 7 * D + FF, down_sum(d_top))
    d_up = (mm_nt(low_top, wdn[last]) * slope).astype(BF)
    store_vector(last, 7 * D, down_sum(d_up.astype(F32)))
    d_h2 = mm_nt(d_up, win[last, :, 4 * D :])
    store_vector(last, 5 * D, down_sum(d_h2 * n2))
    store_vector(last, 6 * D, down_sum(d_h2))
    d_middle = d_top + norm_back(d_h2, n2, i2, vector(last, 5 * D, D))
    low_middle = d_middle.astype(BF)
    store_vector(last, 4 * D, down_sum(d_middle))
    d_heads = mm_nt(low_middle, win[last, :, 3 * D : 4 * D]).astype(BF)
    d_queries = []
    for image in range(KEPT):
        rows = slice(image * BLK, (image + 1) * BLK)
        ups = spread(d_heads[image * 16 : (image + 1) * 16])
        probs = probabilities[image]
        d_probs = mm_nt(ups, DA[rows, :])
        inner = jnp.sum(d_probs * probs, axis=-1, keepdims=True)
        d_scores = (probs * (d_probs - inner)).astype(BF)
        d_queries.append(gather_heads(mm(d_scores, DMB[rows, :])) * 0.125)
        DMB[rows, :] = mm_tn(d_scores, spread_queries[image]).astype(BF)
        DA[rows, :] = mm_tn(probs.astype(BF), ups).astype(BF)
    d_query = jnp.concatenate(d_queries, axis=0).astype(BF)
    store_vector(last, 2 * D, down_sum(d_query.astype(F32)))
    from_query = mm_nt(d_query, win[last, :, 0:D])

    pick_row = lax.broadcasted_iota(jnp.int32, (group, CROWS), 0)
    pick_lane = lax.broadcasted_iota(jnp.int32, (group, CROWS), 1)
    pick = jnp.where(
        ((pick_row - KEPT * here.shard) * 16 + (CLS - TAIL)) == pick_lane, 1.0, 0.0
    ).astype(BF)
    at = 0
    for piece in (active, h2, attended, h1, final, low_top):
        FAC[0, :, at : at + piece.shape[-1]] = mm(pick, piece).astype(BF)
        at += piece.shape[-1]
    at = 0
    for piece in (d_up, low_middle, d_query, d_logits):
        FAC[1, :, at : at + piece.shape[-1]] = mm(pick, piece).astype(BF)
        at += piece.shape[-1]
    FAC[1, :, at:] = jnp.zeros((group, WFAC - at), BF)
    factors_core()

    turned = DXB[...].T
    for tile, grads in enumerate((DMB, DA)):
        made = mm(turned, grads[...]).astype(BF)
        for shard in range(n_shard):
            GS[0, shard // 2, shard % 2, tile * rows_in : (tile + 1) * rows_in, :] = made[
                shard * rows_in : (shard + 1) * rows_in
            ]
    reduce_core(CHUNKS)
    factors_y()
    store_sums(last, [(3 * D, fold(DA[...].astype(F32)))])

    X[...] = jnp.zeros((ROWS, D), F32)
    gain = vector(last, 0, D)
    gain_sum, shift_sum = zeros, zeros
    for image in range(KEPT):
        rows = slice(image * BLK + TAIL, (image + 1) * BLK)
        part = from_query[image * 16 : (image + 1) * 16]
        normed = N1[last, rows, :].astype(F32)
        gain_sum = gain_sum + fold(part * normed)
        shift_sum = shift_sum + fold(part)
        X[rows, :] = d_middle[image * 16 : (image + 1) * 16] + norm_back(
            part, normed, I1[last, rows, :][:, 0:1], gain
        )

    def first_back(layer, half, made, sums):
        base = half * HALF
        gain = vector(layer, 0, D)
        gain_sum, shift_sum = sums
        for at, size in pieces(HALF):
            rows = pl.ds(aligned(base + at, 16), size)
            part = made[at : at + size]
            normed = N1[layer, rows, :].astype(F32)
            inverse = I1[layer, rows, :][:, 0:1]
            gain_sum = gain_sum + fold(part * normed)
            shift_sum = shift_sum + fold(part)
            X[rows, :] = X[rows, :] + norm_back(part, normed, inverse, gain)
        return gain_sum, shift_sum

    def last_back(half, sums):
        rows = pl.ds(aligned(half * HALF, 16), HALF)
        made = mm_nt(DMB[rows, :], win[last, :, D : 2 * D])
        made = made + mm_nt(DA[rows, :], win[last, :, 2 * D : 3 * D])
        return first_back(last, half, made, sums)

    gain_sum, shift_sum = lax.fori_loop(0, 2, last_back, (gain_sum, shift_sum))
    store_sums(last, [(0, gain_sum), (D, shift_sum)])
    reduce_y(CHUNKS)
    factors_x()

    def mlp_back(layer, half, sums):
        base = half * HALF
        whole = pl.ds(aligned(base, 16), HALF)
        bias_down, bias_up, gain_sum, shift_sum, bias_out = sums
        for at, size in pieces(HALF):
            rows = pl.ds(aligned(base + at, 16), size)
            up = X[rows, :]
            DXB[rows, :] = up.astype(BF)
            bias_down = bias_down + fold(up)
        low = DXB[whole, :]
        ups = []
        for tile in range(4):
            columns = slice(tile * D, (tile + 1) * D)
            made = mm_nt(low, wdn[layer, columns, :])
            total = bias_up[tile]
            for at, size in pieces(HALF):
                rows = pl.ds(aligned(base + at, 16), size)
                grad = (made[at : at + size] * SLOPE[layer, rows, columns].astype(F32)).astype(BF)
                SLOPE[layer, rows, columns] = grad
                total = total + fold(grad.astype(F32))
            ups.append(total)
        made = mm_nt(SLOPE[layer, whole, :], win[layer, :, 4 * D :])
        gain = vector(layer, 5 * D, D)
        for at, size in pieces(HALF):
            rows = pl.ds(aligned(base + at, 16), size)
            part = made[at : at + size]
            normed = N2[layer, rows, :].astype(F32)
            inverse = I2[layer, rows, :][:, 0:1]
            gain_sum = gain_sum + fold(part * normed)
            shift_sum = shift_sum + fold(part)
            grad = X[rows, :] + norm_back(part, normed, inverse, gain)
            X[rows, :] = grad
            DMB[rows, :] = grad.astype(BF)
            bias_out = bias_out + fold(grad)
        DA[whole, :] = mm_nt(DMB[whole, :], win[layer, :, 3 * D : 4 * D]).astype(BF)
        return bias_down, tuple(ups), gain_sum, shift_sum, bias_out

    def attend_back(layer, image):
        rows = pl.ds(aligned(image * BLK, 16), BLK)
        for pair in range(3):
            at = pair * 128
            query = QKV[layer, rows, at : at + 128] * BF(0.125)
            keys = QKV[layer, rows, D + at : D + at + 128]
            values = QKV[layer, rows, 2 * D + at : 2 * D + at + 128]
            ups = DA[rows, at : at + 128]
            keys_both = jnp.concatenate([keys * even, keys * odd], axis=0)
            values_both = jnp.concatenate([values * even, values * odd], axis=0)
            scores = mm_nt(keys_both, query)
            d_probs = mm_nt(values_both, ups)
            probs, d_scores = [], []
            for base in (0, BLK):
                low_probs, low_grads = [], []
                for first, end in ((0, 128), (128, BLK)):
                    part = jnp.concatenate(
                        [
                            scores[base : base + TAIL, first:end],
                            scores[base + TAIL : base + BLK, first:end] + key_column[TAIL:],
                        ],
                        axis=0,
                    )
                    raw = jnp.exp(part - jnp.max(part, axis=0, keepdims=True))
                    prob = raw * (1.0 / jnp.sum(raw, axis=0, keepdims=True))
                    grad = d_probs[base : base + BLK, first:end]
                    inner = jnp.sum(grad * prob, axis=0, keepdims=True)
                    low_grads.append((prob * (grad - inner)).astype(BF))
                    low_probs.append(prob.astype(BF))
                probs.append(jnp.concatenate(low_probs, axis=1))
                d_scores.append(jnp.concatenate(low_grads, axis=1))
            probs = jnp.concatenate(probs, axis=0)
            d_scores = jnp.concatenate(d_scores, axis=0)
            d_values = mm(probs, ups)
            d_keys = mm(d_scores, query)
            d_query = mm_tn(d_scores, keys_both) * 0.125
            QKV[layer, rows, at : at + 128] = d_query.astype(BF)
            QKV[layer, rows, D + at : D + at + 128] = jnp.where(
                low_lane, d_keys[:BLK], d_keys[BLK:]
            ).astype(BF)
            QKV[layer, rows, 2 * D + at : 2 * D + at + 128] = jnp.where(
                low_lane, d_values[:BLK], d_values[BLK:]
            ).astype(BF)

    def renew(ref, layer, at):
        gain, shift = vector(layer, at, D), vector(layer, at + D, D)

        def one(index, nothing):
            rows = pl.ds(aligned(index * 64, 16), 64)
            DXB[rows, :] = (ref[layer, rows, :].astype(F32) * gain + shift).astype(BF)
            return nothing

        lax.fori_loop(0, ROWS // 64, one, 0)
        return DXB[...].T

    def keep_in(k, tile, made):
        for shard in range(n_shard):
            G[k, shard // 2, shard % 2, tile * rows_in : (tile + 1) * rows_in, :] = made[
                shard * rows_in : (shard + 1) * rows_in
            ]

    def backward(step, carry):
        layer = LAYERS - 2 - step
        kd, ku, kq = 3 * step, 3 * step + 1, 3 * step + 2
        upper_layer, bottom = step == 0, step == 1

        def one(half, sums):
            sums = mlp_back(layer, half, sums)
            begin = half == 0

            @pl.when(jnp.logical_and(upper_layer, begin))
            def _():
                factors_z()

            when(jnp.logical_and(bottom, begin), (gather_z, CHUNKS))
            return sums

        bias_down, bias_up, gain_sum, shift_sum, bias_out = lax.fori_loop(
            0, 2, one, (zeros, (zeros,) * 4, zeros, zeros, zeros)
        )
        when(upper_layer, (reduce_x, CHUNKS))
        when(bottom, (reduce_x, 2), (reduce_z, 1))
        store_sums(
            layer,
            [(7 * D + FF, bias_down), (5 * D, gain_sum), (6 * D, shift_sum), (4 * D, bias_out)]
            + [(7 * D + tile * D, bias_up[tile]) for tile in range(4)],
        )
        turned = DXB[...].T
        per = min(rows_down, D)
        for tile in range(4):
            columns = slice(tile * D, (tile + 1) * D)
            made = mm(turned, ACT[layer, :, columns]).astype(BF).T
            for piece in range(D // per):
                shard, at = divmod(tile * D + piece * per, rows_down)
                G[kd, shard // 2, shard % 2, at : at + per, :] = made[
                    piece * per : (piece + 1) * per
                ]
        when(upper_layer, (reduce_core, 0))
        when(bottom, (reduce_core, 3), (gather_z, 0), (gather_x, CHUNKS))
        turned = renew(N2, layer, 5 * D)
        for tile in range(4):
            keep_in(
                ku, tile, mm(turned, SLOPE[layer, :, tile * D : (tile + 1) * D]).astype(BF)
            )
        when(upper_layer, (reduce_core, 1), (reduce_y, 0), (reduce_z, CHUNKS))
        when(bottom, (reduce_core, 4), (reduce_y, 3), (reduce_z, 2))
        keep_in(kq, 3, mm(ATT[layer].T, DMB[...]).astype(BF))

        def two(image, nothing):
            attend_back(layer, image)
            when(jnp.logical_and(upper_layer, image == 0), (reduce_y, 1))
            when(jnp.logical_and(upper_layer, image == 2), (reduce_x, 0))
            when(jnp.logical_and(bottom, image == 0), (reduce_y, 4), (gather_z, 1))

            @pl.when(jnp.logical_and(bottom, image == 1))
            def _():
                factors_mate()
                gather_done(CHUNKS)
                gather_x(0)

            when(jnp.logical_and(bottom, image == 2), (reduce_x, 3), (gather_z, 2))
            when(jnp.logical_and(bottom, image == 3), (gather_x, 1), (reduce_z, 3))
            return nothing

        lax.fori_loop(0, KEPT, two, 0)
        turned = renew(N1, layer, 0)
        for tile in range(3):
            keep_in(
                kq, tile, mm(turned, QKV[layer, :, tile * D : (tile + 1) * D]).astype(BF)
            )
        when(upper_layer, (reduce_core, 2))
        when(bottom, (reduce_core, 5), (gather_x, 2), (gather_done, 0))
        store_sums(
            layer,
            [
                (2 * D, fold(QKV[layer, :, 0:D].astype(F32))),
                (3 * D, fold(QKV[layer, :, 2 * D : 3 * D].astype(F32))),
            ],
        )

        def three(half, sums):
            rows = pl.ds(aligned(half * HALF, 16), HALF)
            made = mm_nt(QKV[layer, rows, :], win[layer, :, 0 : 3 * D])
            return first_back(layer, half, made, sums)

        gain_sum, shift_sum = lax.fori_loop(0, 2, three, (zeros, zeros))
        store_sums(layer, [(0, gain_sum), (D, shift_sum)])
        when(upper_layer, (reduce_x, 1), (reduce_y, 2), (reduce_z, 0))
        when(bottom, (reduce_y, 5), (reduce_x, 4), (gather_z, 3), (gather_done, 1))
        return carry

    lax.fori_loop(0, LAYERS - 1, backward, 0)

    for at, size in pieces(BLK):
        total = None
        for image in range(KEPT):
            part = X[image * BLK + at : image * BLK + at + size, :]
            DXB[image * BLK + at : image * BLK + at + size, :] = part.astype(BF)
            total = part if total is None else total + part
        V[at : at + size, 0:D] = total

    vec = ("v", v_send, v_recv)
    v_y, v_x = 1, n_y
    v_z = v_x + n_x - 1
    v_gz = v_z + n_z - 1
    v_q = v_gz + n_z - 1
    v_gx = v_q + n_z - 1
    v_gy = v_gx + n_x - 1
    v_gc = v_gy + n_y - 1
    rows_c = VEC_ROWS // 2
    rows_y = rows_c // n_y
    rows_x = rows_y // n_x
    split_z = cut(rows_x, n_z, 8)
    rows_z = rows_x // split_z
    at_c = c * rows_c
    at_y = at_c + y * rows_y
    at_x = at_y + x * rows_x
    at_z = at_x + z * rows_z if split_z > 1 else at_x

    def vrows(ref, at, rows):
        return ref.at[pl.ds(aligned(at, 8), rows), :]

    def narrow(at, rows):
        return VF.at[pl.ds(aligned(at, 8), rows), pl.ds(0, D)]

    def vadd(at, rows, sources):
        target = pl.ds(aligned(at, 8), rows)
        total = V[target, :]
        for source in sources:
            total = total + source
        V[target, :] = total

    def vectors_core():
        go(lambda: vrows(V, (1 - c) * rows_c, rows_c), VC, vec, 0, mate)

    def vectors_y():
        arrived(VC, v_recv.at[0], v_send.at[0])
        vadd(at_c, rows_c, [VC[...]])
        for o in range(1, n_y):
            to = turn(y, o, n_y)
            go(
                lambda o=o: vrows(V, at_c + turn(y, o, n_y) * rows_y, rows_y), VY.at[o - 1],
                vec, v_y + o - 1, here.to(y=to),
            )

    def vectors_x():
        for o in range(1, n_y):
            arrived(VY.at[o - 1], v_recv.at[v_y + o - 1], v_send.at[v_y + o - 1])
        vadd(at_y, rows_y, [VY[o - 1] for o in range(1, n_y)])
        for o in range(1, n_x):
            to = turn(x, o, n_x)
            go(
                lambda o=o: vrows(V, at_y + turn(x, o, n_x) * rows_x, rows_x), VX.at[o - 1],
                vec, v_x + o - 1, here.to(x=to),
            )

    def vectors_z():
        for o in range(1, n_x):
            arrived(VX.at[o - 1], v_recv.at[v_x + o - 1], v_send.at[v_x + o - 1])
        vadd(at_x, rows_x, [VX[o - 1] for o in range(1, n_x)])
        for o in range(1, n_z):

            def make(o=o):
                at = at_x + turn(z, o, n_z) * rows_z if split_z > 1 else at_x
                return vrows(V, at, rows_z)

            go(make, VZ.at[z], vec, v_z + o - 1, here.to(z=turn(z, o, n_z)))

    def vectors_gather_z():
        for o in range(1, n_z):
            arrived(
                VZ.at[turn(z, n_z - o, n_z)], v_recv.at[v_z + o - 1], v_send.at[v_z + o - 1]
            )
        target = pl.ds(aligned(at_z, 8), rows_z)
        VZ[z] = V[target, :]
        total = VZ[0]
        for index in range(1, n_z):
            total = total + VZ[index]
        VF[target, 0:D] = total[:, 0:D]
        if split_z > 1:
            for o in range(1, n_z):
                go(
                    lambda: narrow(at_z, rows_z), narrow(at_z, rows_z), vec, v_gz + o - 1,
                    here.to(z=turn(z, o, n_z)),
                )

    def squares_send():
        SQ[...] = square_sum[...]
        SQS[z] = square_sum[...]
        for o in range(1, n_z):
            go(lambda: SQ, SQS.at[z], vec, v_q + o - 1, here.to(z=turn(z, o, n_z)))

    def vectors_gather_x():
        for o in range(1, n_z):
            came = turn(z, n_z - o, n_z)
            if split_z > 1:
                arrived(
                    narrow(at_x + came * rows_z, rows_z), v_recv.at[v_gz + o - 1],
                    v_send.at[v_gz + o - 1],
                )
            arrived(SQS.at[came], v_recv.at[v_q + o - 1], v_send.at[v_q + o - 1])
        total = SQS[0]
        for index in range(1, n_z):
            total = total + SQS[index]
        for at in range(0, rows_x, 8):
            VF[pl.ds(aligned(at_x + at, 8), 8), D:] = total
        for o in range(1, n_x):
            go(
                lambda: vrows(VF, at_x, rows_x), vrows(VF, at_x, rows_x), vec, v_gx + o - 1,
                here.to(x=turn(x, o, n_x)),
            )

    def vectors_gather_y():
        for o in range(1, n_x):
            at = at_y + turn(x, n_x - o, n_x) * rows_x
            arrived(vrows(VF, at, rows_x), v_recv.at[v_gx + o - 1], v_send.at[v_gx + o - 1])
        for o in range(1, n_y):
            go(
                lambda: vrows(VF, at_y, rows_y), vrows(VF, at_y, rows_y), vec, v_gy + o - 1,
                here.to(y=turn(y, o, n_y)),
            )

    def vectors_gather_core():
        for o in range(1, n_y):
            at = at_c + turn(y, n_y - o, n_y) * rows_y
            arrived(vrows(VF, at, rows_y), v_recv.at[v_gy + o - 1], v_send.at[v_gy + o - 1])
        go(lambda: vrows(VF, at_c, rows_c), vrows(VF, at_c, rows_c), vec, v_gc, mate)

    def vectors_done():
        arrived(vrows(VF, (1 - c) * rows_c, rows_c), v_recv.at[v_gc], v_send.at[v_gc])

    vectors_core()
    low = DXB[...]
    for tile in range(2):
        made = mm_tn(pix[:, :, tile * D : (tile + 1) * D].reshape(ROWS, D), low).astype(BF)
        for piece in range(D // rows_patch):
            shard = tile * (D // rows_patch) + piece
            GS[1, shard // 2, shard % 2] = made[piece * rows_patch : (piece + 1) * rows_patch]

    kp = CHUNKS + 1
    reduce_core(kp)
    reduce_z(4)
    vectors_y()
    reduce_y(kp)
    gather_x(3)
    reduce_x(5)
    vectors_x()
    gather_z(4)
    reduce_x(kp)
    reduce_z(5)
    vectors_z()
    gather_done(2)
    gather_x(4)
    gather_done(3)
    reduce_z(kp)
    gather_z(5)
    vectors_gather_z()
    gather_z(kp)
    squares_send()
    gather_x(5)
    gather_x(kp)
    vectors_gather_x()
    gather_done(4)
    vectors_gather_y()
    gather_done(5)
    gather_done(kp)
    vectors_gather_core()
    factors_done()
    vectors_done()
    last_copy = pltpu.make_async_copy(VF, vec_out, out_local.at[1 + CHUNKS + 2])
    last_copy.start()
    for source, send, recv, at in list(sent.values()):
        left_here(source(), recv.at[at], send.at[at])
    for k in range(CHUNKS + 2):
        result(k).wait()
    last_copy.wait()

    @pl.when(jnp.logical_not(lower))
    def _():
        left_here(given, img_recv.at[0], img_send.at[0])
        left_here(lab_pairs.at[2], img_recv.at[1], img_send.at[1])


def run_train(n_rep, n_shard, patches, lab_pairs, own_patch, own_in, own_down, vecs, glob, pos, head, count):
    n_x = 2 ** ((n_rep.bit_length() - 2) // 2)
    n_z, n_y = n_rep // n_x, n_shard // 2
    block = 4 * (D // n_shard)
    group = KEPT * n_shard
    keep = LAYERS - 1
    units = 1 + 3 * LAYERS
    chunks = CHUNKS + 2

    def buf(*shape, dtype=BF):
        return pltpu.VMEM(shape, dtype)

    def sems(*shape):
        return pltpu.SemaphoreType.DMA(shape)

    def reduction(count, rows):
        by_x = cut(rows, n_x, 16)
        by_z = cut(rows // by_x, n_z, 16)
        return [
            buf(count, n_y, 2, rows, D),
            buf(min(count, 3), n_y, rows, D),
            buf(min(count, 3), n_y - 1, rows, D),
            buf(count, n_x - 1 if by_x > 1 else n_x, rows // by_x, D),
            buf(count, n_z, rows // by_x // by_z, D),
            buf(count, rows, D),
        ]

    rows_y = VEC_ROWS // 2 // n_y
    rows_x = rows_y // n_x
    rows_z = rows_x // cut(rows_x, n_z, 8)
    ag_count = n_y + (n_y - 1) * (n_x - 1) * 2 + n_y - 1
    rs_count = 1 + (n_y - 1) + 2 * (n_x - 1) + 2 * (n_z - 1)
    f_count = 1 + (n_y - 1) + (n_x - 1) + (n_z - 1) + 1
    v_count = 1 + 2 * (n_y - 1) + 2 * (n_x - 1) + 3 * (n_z - 1) + 1
    whole = pl.BlockSpec(memory_space=pltpu.VMEM)
    there = pl.BlockSpec(memory_space=pl.ANY)
    return pl.pallas_call(
        functools.partial(train, n_rep, n_shard),
        out_shape=[
            jax.ShapeDtypeStruct((CHUNKS, block, D), BF),
            jax.ShapeDtypeStruct((2, block // 2, D), BF),
            jax.ShapeDtypeStruct((VEC_ROWS, VEC_WIDE), F32),
            jax.ShapeDtypeStruct((2, n_rep, group, WFAC), BF),
        ],
        in_specs=[there] * 5 + [whole] * 5,
        out_specs=[there] * 4,
        scratch_shapes=[
            buf(ROWS, D, dtype=F32),
            buf(LAYERS, ROWS, D),
            buf(LAYERS, ROWS, 128, dtype=F32),
            buf(keep, ROWS, 3 * D),
            buf(keep, ROWS, D),
            buf(keep, ROWS, D),
            buf(keep, ROWS, 128, dtype=F32),
            buf(keep, ROWS, FF),
            buf(keep, ROWS, FF),
            buf(ROWS, D),
            buf(ROWS, D),
            buf(ROWS, D),
            buf(KEPT, BLK, PATCH_DIM),
            buf(2, 32, 128, dtype=F32),
            buf(PATCH_DIM, D),
            buf(LAYERS, D, 4 * D + FF),
            buf(LAYERS, FF, D),
            buf(D, CPAD),
            buf(1, CPAD, dtype=F32),
            *reduction(CHUNKS, block),
            *reduction(2, block // 2),
            buf(2, group, WFAC),
            buf(group, WFAC),
            buf(n_y - 1, group, WFAC),
            buf(n_x, group, WFAC),
            buf(VEC_ROWS, VEC_WIDE, dtype=F32),
            buf(VEC_ROWS // 2, VEC_WIDE, dtype=F32),
            buf(n_y - 1, rows_y, VEC_WIDE, dtype=F32),
            buf(n_x - 1, rows_x, VEC_WIDE, dtype=F32),
            buf(n_z, rows_z, VEC_WIDE, dtype=F32),
            buf(VEC_ROWS, VEC_WIDE, dtype=F32),
            buf(8, 128, dtype=F32),
            buf(n_z, 8, 128, dtype=F32),
            buf(8, 128, dtype=F32),
            sems(units, ag_count),
            sems(units, ag_count),
            sems(units),
            sems(chunks, rs_count),
            sems(chunks, rs_count),
            sems(f_count),
            sems(f_count),
            sems(v_count),
            sems(v_count),
            sems(2),
            sems(2),
            sems(4),
            sems(2 + chunks),
        ],
        compiler_params=pltpu.CompilerParams(
            vmem_limit_bytes=65400 * 1024, collective_id=0, has_side_effects=True
        ),
        cost_estimate=pl.CostEstimate(
            flops=24_000_000_000, bytes_accessed=30_000_000, transcendentals=10_000_000
        ),
        name="train_step",
    )(patches, lab_pairs, own_patch, own_in, own_down, vecs, glob, pos, head, count)


def adam(weight, first, second, grad, factor, rate):
    grad = grad * factor
    first = BETA_FIRST * first + (1.0 - BETA_FIRST) * grad
    second = BETA_SECOND * second + (1.0 - BETA_SECOND) * grad * grad
    first_hat = first * (1.0 / (1.0 - BETA_FIRST**ADAM_STEP))
    second_hat = second * (1.0 / (1.0 - BETA_SECOND**ADAM_STEP))
    step = first_hat / (jnp.sqrt(second_hat) + ADAM_EPS) + WEIGHT_DECAY * weight
    return weight - rate * step, first, second


def update(n_rep, n_shard, *refs):
    res, small, vec, factors = refs[0:4]
    sources = refs[4:25]
    loss_out, norm_out = refs[25:27]
    targets = refs[27:48]
    buffers = refs[48:69]
    last_in, last_down, grad_head, in_sems, out_sems = refs[69:]
    shard = lax.axis_index("shard")
    rows_in = D // n_shard
    rows_down = FF // n_shard
    keep = LAYERS - 1

    def moves(array, layer=None, out=False):
        found = []
        for kind in range(3):
            index = 3 * array + kind
            if out:
                src, dst, sem = buffers[index], targets[index], out_sems
            else:
                src, dst, sem = sources[index], buffers[index], in_sems
            slot = 0 if layer is None else layer
            if layer is not None:
                src, dst = src.at[layer], dst.at[layer]
            found.append(pltpu.make_async_copy(src, dst, sem.at[index, slot]))
        return found

    layered = [(1, layer) for layer in range(LAYERS)] + [(2, layer) for layer in range(LAYERS)]
    order = layered + [(0, None), (6, None), (5, None), (3, None), (4, None)]
    for array, layer in order:
        for move in moves(array, layer):
            move.start()

    n_rows = factors.shape[1] * factors.shape[2]

    def factor(half, at, size):
        return factors[half, :, :, at : at + size].reshape(n_rows, size)

    def squares(values):
        return fold(values * values)

    total = jnp.zeros((8, D), F32)
    h2 = factor(0, FF, D)
    for tile in range(4):
        made = mm_tn(h2, factor(1, tile * D, D))
        last_in[:, (2 + tile) * D : (3 + tile) * D] = made
        total = total + squares(made)
    made = mm_tn(factor(0, FF + 2 * D, D), factor(1, FF + D, D))
    last_in[:, 0:D] = made
    total = total + squares(made)
    made = mm_tn(factor(0, FF + D, D), factor(1, FF, D))
    last_in[:, D : 2 * D] = made
    total = total + squares(made)
    d_top = factor(0, FF + 4 * D, D)
    for tile in range(4):
        made = mm_tn(factor(0, tile * D, D), d_top)
        last_down[tile * D : (tile + 1) * D, :] = made
        total = total + squares(made)
    final = factor(0, FF + 3 * D, D)
    wide = jnp.zeros((8, 128), F32)
    for at in range(0, CPAD, 512):
        d_logits = factor(1, FF + 2 * D + at, 512)
        made = mm_tn(final, d_logits)
        grad_head[0:D, at : at + 512] = made
        bias = down_sum(d_logits.astype(F32))
        grad_head[D : D + 1, at : at + 512] = bias
        sums = squares(made)
        for lane in range(0, 512, 128):
            wide = wide + sums[:, lane : lane + 128]
            row = bias[:, lane : lane + 128]
            wide = wide + (row * row) * 0.125
    for lane in range(0, D, 128):
        wide = wide + total[:, lane : lane + 128]
    used = VEC_AT + 12 * LAYERS + 2
    parts = jnp.zeros((8, D), F32)
    kept_rows = lax.broadcasted_iota(jnp.int32, (8, 1), 0)
    for at in range(0, used, 8):
        value = vec[at : at + 8, 0:D]
        if at + 8 > used:
            value = jnp.where(kept_rows + at < used, value, 0.0)
        parts = parts + value * value
    patch_bias = down_sum(vec[0:PATCHES, 0:D])
    class_row = vec[CLS : CLS + 1, 0:D]
    rest = (patch_bias * patch_bias + class_row * class_row) * 0.125
    parts = parts + rest
    for lane in range(0, D, 128):
        wide = wide + parts[:, lane : lane + 128]
    n_x = 2 ** ((n_rep.bit_length() - 2) // 2)
    rows_x = VEC_ROWS // n_shard // n_x
    wide = wide + fold(vec[:, D:]) * (8.0 / rows_x)
    sum_squares = jnp.sum(jnp.sum(wide, axis=1, keepdims=True), axis=0, keepdims=True)
    inv_count = 1.0 / vec[used + 1 : used + 2, 0:1]
    grad_norm = jnp.sqrt(sum_squares) * inv_count
    norm_out[...] = grad_norm
    loss_out[...] = vec[used : used + 1, 0:1] * inv_count
    scale = jnp.minimum(1.0, CLIP_NORM / grad_norm) * inv_count

    def apply(array, where, grad, rate):
        refs = [buffers[3 * array + kind] for kind in range(3)]
        made = adam(refs[0][where], refs[1][where], refs[2][where], grad, scale, rate)
        for ref, value in zip(refs, made):
            ref[where] = value

    def begin(array, layer=None):
        for move in moves(array, layer):
            move.wait()

    def finish(array, layer=None):
        for move in moves(array, layer, out=True):
            move.start()

    def in_place(layer, column, at, size):
        return (layer, slice(at, at + size), slice(column * D, (column + 1) * D))

    def in_step(tile_rows):
        return 32 if tile_rows % 32 == 0 else 16

    step = in_step(rows_in)
    own_rows = pl.multiple_of(shard * rows_in, 8)
    for layer in range(LAYERS):
        begin(1, layer)
        for column in range(8):
            for at in range(0, rows_in, step):
                if layer < keep:
                    k = 3 * (keep - 1 - layer) + (2 if column < 4 else 1)
                    row = (column % 4) * rows_in + at
                    grad = res[k, row : row + step, :].astype(F32)
                elif column in (1, 2):
                    row = (column - 1) * rows_in + at
                    grad = small[0, row : row + step, :].astype(F32)
                else:
                    held = 0 if column == 0 else column - 2
                    grad = last_in[
                        pl.ds(own_rows + at, step), held * D : (held + 1) * D
                    ]
                apply(1, in_place(layer, column, at, step), grad, LEARNING_RATE)
        finish(1, layer)
    down_rows = pl.multiple_of(shard * rows_down, 8)
    for layer in range(LAYERS):
        begin(2, layer)
        for at in range(0, rows_down, 32):
            if layer < keep:
                grad = res[3 * (keep - 1 - layer), at : at + 32, :].astype(F32)
            else:
                grad = last_down[pl.ds(down_rows + at, 32), :]
            apply(2, (layer, slice(at, at + 32), slice(0, D)), grad, LEARNING_RATE)
        finish(2, layer)
    begin(0)
    for at in range(0, PATCH_DIM // n_shard, 32):
        grad = small[1, at : at + 32, :].astype(F32)
        apply(0, (slice(at, at + 32), slice(0, D)), grad, LEARNING_RATE)
    finish(0)
    begin(6)
    for at in range(0, D, 32):
        rows = slice(at, at + 32)
        apply(6, (rows, slice(0, NCLS)), grad_head[rows, 0:NCLS], LEARNING_RATE)
    apply(6, (slice(D, D + 1), slice(0, NCLS)), grad_head[D : D + 1, 0:NCLS], LEARNING_RATE)
    finish(6)
    begin(5)
    apply(5, (slice(0, 1), slice(0, D)), class_row, VECTOR_RATE)
    for at in range(0, PATCHES, 28):
        apply(
            5, (slice(1 + at, 29 + at), slice(0, D)), vec[at : at + 28, 0:D], VECTOR_RATE
        )
    finish(5)
    begin(3)
    for layer in range(LAYERS):
        for piece in range(12):
            row = VEC_AT + 12 * layer + piece
            where = (slice(layer, layer + 1), slice(piece * D, (piece + 1) * D))
            apply(3, where, vec[row : row + 1, 0:D], VECTOR_RATE)
    finish(3)
    begin(4)
    rows = [patch_bias, class_row, vec[used - 2 : used - 1, 0:D], vec[used - 1 : used, 0:D]]
    for index, row in enumerate(rows):
        apply(4, (slice(index, index + 1), slice(0, D)), row, VECTOR_RATE)
    finish(4)
    for array, layer in order:
        for move in moves(array, layer, out=True):
            move.wait()


def run_update(n_rep, n_shard, res, small, vec, factors, arrays):
    whole = pl.BlockSpec(memory_space=pltpu.VMEM)
    there = pl.BlockSpec(memory_space=pl.ANY)
    one = jax.ShapeDtypeStruct((1, 1), F32)
    made = pl.pallas_call(
        functools.partial(update, n_rep, n_shard),
        out_shape=[one, one] + [jax.ShapeDtypeStruct(a.shape, F32) for a in arrays],
        in_specs=[whole] * 4 + [there] * 21,
        out_specs=[whole] * 2 + [there] * 21,
        scratch_shapes=[pltpu.VMEM(a.shape, F32) for a in arrays]
        + [
            pltpu.VMEM((D, 2 * D + FF), F32),
            pltpu.VMEM((FF, D), F32),
            pltpu.VMEM((D + 8, CPAD), F32),
            pltpu.SemaphoreType.DMA((21, LAYERS)),
            pltpu.SemaphoreType.DMA((21, LAYERS)),
        ],
        compiler_params=pltpu.CompilerParams(vmem_limit_bytes=62 * 1024 * 1024),
        cost_estimate=pl.CostEstimate(
            flops=200_000_000, bytes_accessed=50_000_000, transcendentals=4_000_000
        ),
        name="adamw",
    )(res, small, vec, factors, *arrays)
    return made[0].reshape(()), made[1].reshape(()), made[2:]


def shards(
    n_rep, n_shard,
    patches, labels, counts, patch_w, layer_in, layer_down, layer_vecs, glob_vecs, pos_embed, head,
    m_patch, v_patch, m_in, v_in, m_down, v_down, m_vecs, v_vecs, m_glob, v_glob, m_pos, v_pos,
    m_head, v_head,
):
    slots = patches.shape[0]
    marked = jnp.where(jnp.arange(slots) < counts[0], labels, -1).astype(F32)
    lab_pairs = jnp.where(
        jnp.arange(16)[None, :, None] == CLS - TAIL, marked[:, None, None], -1.0
    )
    lab_pairs = jnp.broadcast_to(lab_pairs, (slots, 16, 128)).reshape(slots // 2, 32, 128)
    count = jnp.broadcast_to(counts.astype(F32)[None], (1, 128))
    padded = jnp.pad(patches, ((0, 0), (0, BLK - PATCHES), (0, 0)))
    res, small, vec, factors = run_train(
        n_rep, n_shard, padded, lab_pairs, patch_w.astype(BF), layer_in.astype(BF),
        layer_down.astype(BF), layer_vecs, glob_vecs, pos_embed, head, count,
    )
    arrays = [
        patch_w, m_patch, v_patch, layer_in, m_in, v_in, layer_down, m_down, v_down,
        layer_vecs, m_vecs, v_vecs, glob_vecs, m_glob, v_glob, pos_embed, m_pos, v_pos,
        head, m_head, v_head,
    ]
    loss, grad_norm, new = run_update(n_rep, n_shard, res, small, vec, factors, arrays)
    return (loss, grad_norm, *new)


def solution(mesh):
    everywhere = P()
    rows = P("shard", None)
    middle = P(None, "shard", None)
    return jax.shard_map(
        functools.partial(shards, mesh.shape["rep"], mesh.shape["shard"]),
        mesh=mesh,
        in_specs=(
            P(("rep", "shard"), None, None),
            P(("rep", "shard")),
            P(("rep", "shard")),
            rows,
            middle,
            middle,
            *(everywhere,) * 4,
            *(rows,) * 2,
            *(middle,) * 4,
            *(everywhere,) * 8,
        ),
        out_specs=(
            *(everywhere,) * 2,
            *(rows,) * 3,
            *(middle,) * 6,
            *(everywhere,) * 12,
        ),
        check_vma=False,
    )
```

```python
import functools

import jax
import jax.numpy as jnp
from jax import lax
from jax.experimental import pallas as pl
from jax.experimental.pallas import tpu as pltpu
from jax.sharding import PartitionSpec as P

D = 384
HEADS = 6
HEAD_DIM = 64
FF = 1536
PATCH_DIM = 768
PATCHES = 196
NCLS = 1000
LAYERS = 3
SEQ = 197

BLK = 208
CLS = 200
TAIL = 192
KEPT = 4
ROWS = KEPT * BLK
HALF = 2 * BLK
CROWS = KEPT * 16
CPAD = 1024
WIDE = 8 * D + FF

NORM_EPS = 1e-06
SMOOTHING = 0.1
CLIP_NORM = 0.05
LEARNING_RATE = 0.05
VECTOR_RATE = 0.5
BETA_FIRST = 0.9
BETA_SECOND = 0.999
ADAM_EPS = 1e-08
WEIGHT_DECAY = 0.05
ADAM_STEP = 10
GELU_SCALE = 0.7978845608028654
GELU_CUBIC = 0.044715

F32 = jnp.float32
BF = jnp.bfloat16


def mm(left, right):
    return jnp.dot(left, right, preferred_element_type=F32)


def mm_nt(left, right):
    return lax.dot_general(left, right, (((1,), (1,)), ((), ())), preferred_element_type=F32)


def mm_tn(left, right):
    return lax.dot_general(left, right, (((0,), (0,)), ((), ())), preferred_element_type=F32)


def fold(values):
    return jnp.sum(values.reshape(-1, 8, values.shape[-1]), axis=0)


def down_sum(values):
    return jnp.sum(values, axis=0, keepdims=True)


def norm(values):
    centre = values - jnp.mean(values, axis=-1, keepdims=True)
    inverse = lax.rsqrt(jnp.mean(centre * centre, axis=-1, keepdims=True) + NORM_EPS)
    return centre * inverse, inverse


def norm_back(upstream, normed, inverse, gain):
    scaled = upstream * gain
    first = jnp.mean(scaled, axis=-1, keepdims=True)
    second = jnp.mean(scaled * normed, axis=-1, keepdims=True)
    return inverse * (scaled - first - normed * second)


def gelu_parts(hidden):
    square = hidden * hidden
    tangent = jnp.tanh(hidden * (GELU_SCALE + (GELU_SCALE * GELU_CUBIC) * square))
    share = 0.5 + 0.5 * tangent
    active = hidden * share
    inner = (2.0 * GELU_SCALE) + (6.0 * GELU_SCALE * GELU_CUBIC) * square
    slope = share + active * (1.0 - share) * inner
    return active, slope


def lane_mask(width, low, high):
    lane = lax.broadcasted_iota(jnp.int32, (1, width), 1)
    return jnp.where((lane >= low) & (lane < high), 1.0, 0.0).astype(BF)


STEP = 32


def pieces(total):
    return [(at, min(STEP, total - at)) for at in range(0, total, STEP)]


WFAC = FF + 5 * D
VEC_ROWS = 256
VEC_AT = BLK
VEC_WIDE = D + 128
MESH = pl.DeviceIdType.MESH
CHUNKS = 6


class Place:
    def __init__(self, n_rep, n_shard):
        self.n_rep, self.n_shard = n_rep, n_shard
        self.n_x = 2 ** ((n_rep.bit_length() - 2) // 2)
        self.n_z = n_rep // self.n_x
        self.n_y = n_shard // 2
        rep, shard = lax.axis_index("rep"), lax.axis_index("shard")
        self.rep, self.shard = rep, shard
        self.z, self.x = rep // self.n_x, rep % self.n_x
        self.y, self.c = shard // 2, shard % 2

    def to(self, x=None, y=None, z=None, c=None):
        x = self.x if x is None else x
        y = self.y if y is None else y
        z = self.z if z is None else z
        c = self.c if c is None else c
        return {"rep": z * self.n_x + x, "shard": y * 2 + c}


def cut(rows, parts, unit):
    return parts if rows % (parts * unit) == 0 else 1


def aligned(value, unit):
    return pl.multiple_of(value, unit)


def train(
    n_rep, n_shard,
    patches, labels, counts, own_patch, own_in, own_down, vecs, glob, pos, head,
    res_out, small_out, vec_out, all_factors,
    X, N1, I1, QKV, ATT, N2, I2, ACT, SLOPE, DXB, DMB, DA,
    pix, lab, lab_given, wp, win, wdn, low_head, head_bias,
    G, RC, RY, RX, RZ, RES, GS, SC, SY, SX, SZ, SRES,
    FAC, FC, FY, FALL, V, VC, VY, VX, VZ, VF, SQ, SQS, square_sum,
    ag_send, ag_recv, ag_local, rs_send, rs_recv, f_send, f_recv, v_send, v_recv,
    img_send, img_recv, img_local, out_local,
):
    here = Place(n_rep, n_shard)
    n_x, n_y, n_z = here.n_x, here.n_y, here.n_z
    x, y, z, c = here.x, here.y, here.z, here.c
    rows_in, rows_down, rows_patch = D // n_shard, FF // n_shard, PATCH_DIM // n_shard
    block = 4 * rows_in
    mate = here.to(c=1 - c)

    def push(src, dst, send, recv, device):
        pltpu.make_async_remote_copy(
            src_ref=src, dst_ref=dst, send_sem=send, recv_sem=recv,
            device_id=device, device_id_type=MESH,
        ).start()

    def arrived(dst, recv, send):
        pltpu.make_async_remote_copy(
            src_ref=dst, dst_ref=dst, send_sem=send, recv_sem=recv,
            device_id=mate, device_id_type=MESH,
        ).wait_recv()

    def left_here(src, recv, send):
        pltpu.make_async_remote_copy(
            src_ref=src, dst_ref=src, send_sem=send, recv_sem=recv,
            device_id=mate, device_id_type=MESH,
        ).wait_send()

    sent = {}

    def go(source, dst, sems, index, device):
        name, send, recv = sems
        push(source(), dst, send.at[index], recv.at[index], device)
        sent[name, index] = (source, send, recv, index)

    def gone(sems, index):
        source, send, recv, at = sent.pop((sems[0], index))
        left_here(source(), recv.at[at], send.at[at])

    def turn(at, by, size):
        return lax.rem(at + by, size)

    barrier = pltpu.get_barrier_semaphore()
    others = (
        [mate]
        + [here.to(y=turn(y, o, n_y)) for o in range(1, n_y)]
        + [here.to(x=turn(x, o, n_x)) for o in range(1, n_x)]
        + [here.to(z=turn(z, o, n_z)) for o in range(1, n_z)]
    )
    for other in others:
        pl.semaphore_signal(barrier, inc=1, device_id=other, device_id_type=MESH)
    pl.semaphore_wait(barrier, len(others))

    def weight(kind, layer, shard, part=None):
        if kind == "patch":
            parts = cut(rows_patch, n_x, 16)
            rows = rows_patch // parts
            if part is None:
                return wp.at[pl.ds(aligned(shard * rows_patch, 16), rows_patch), :]
            return wp.at[pl.ds(aligned(shard * rows_patch + part * rows, 16), rows), :]
        if kind == "down":
            parts = cut(rows_down, n_x, 16)
            rows = rows_down // parts
            if part is None:
                return wdn.at[layer, pl.ds(aligned(shard * rows_down, 16), rows_down), :]
            return wdn.at[layer, pl.ds(aligned(shard * rows_down + part * rows, 16), rows), :]
        base = 0 if kind == "attn" else 4 * D
        rows = pl.ds(aligned(shard * rows_in, 16), rows_in)
        if part is None:
            return win.at[layer, rows, pl.ds(base, 4 * D)]
        wide = 4 * D // n_x
        return win.at[layer, rows, pl.ds(aligned(base + part * wide, 128), wide)]

    units = [("patch", 0)] + [
        (kind, layer) for layer in range(LAYERS) for kind in ("attn", "up", "down")
    ]

    def parts_of(kind):
        if kind == "patch":
            return cut(rows_patch, n_x, 16)
        if kind == "down":
            return cut(rows_down, n_x, 16)
        return n_x

    ag = ("ag", ag_send, ag_recv)
    base_x = n_y
    base_my = base_x + (n_y - 1) * (n_x - 1)
    base_mx = base_my + (n_y - 1)

    stage = 4 * rows_in

    def weights_copies(unit):
        kind, layer = units[unit]
        base = (unit % 2) * stage
        if kind == "patch":
            pairs = [(own_patch, X.at[pl.ds(base, rows_patch)])]
        elif kind == "down":
            pairs = [(own_down.at[layer], X.at[pl.ds(base, rows_down)])]
        else:
            start = 0 if kind == "attn" else 4 * D
            pairs = [
                (
                    own_in.at[layer, :, pl.ds(start + tile * D, D)],
                    X.at[pl.ds(base + tile * rows_in, rows_in)],
                )
                for tile in range(4)
            ]
        return [
            pltpu.make_async_copy(src, dst, ag_local.at[unit, index])
            for index, (src, dst) in enumerate(pairs)
        ]

    def weights_cast(unit):
        kind, layer = units[unit]
        base = (unit % 2) * stage
        for copy in weights_copies(unit):
            copy.wait()
        if kind == "patch":
            rows = pl.ds(aligned(here.shard * rows_patch, 16), rows_patch)
            wp[rows, :] = X[base : base + rows_patch, :].astype(BF)
        elif kind == "down":
            rows = pl.ds(aligned(here.shard * rows_down, 16), rows_down)
            wdn[layer, rows, :] = X[base : base + rows_down, :].astype(BF)
        else:
            start = 0 if kind == "attn" else 4 * D
            rows = pl.ds(aligned(here.shard * rows_in, 16), rows_in)
            for tile in range(4):
                win[layer, rows, start + tile * D : start + (tile + 1) * D] = X[
                    base + tile * rows_in : base + (tile + 1) * rows_in, :
                ].astype(BF)
        if unit + 2 < len(units):
            for copy in weights_copies(unit + 2):
                copy.start()

    def weights_start(unit):
        kind, layer = units[unit]
        part = x if parts_of(kind) > 1 else 0
        for o in range(1, n_y):
            go(
                lambda: weight(kind, layer, here.shard, part),
                weight(kind, layer, here.shard, part), ag, (unit, o),
                here.to(y=turn(y, o, n_y)),
            )
        go(
            lambda: weight(kind, layer, here.shard), weight(kind, layer, here.shard), ag,
            (unit, 0), mate,
        )

    def weights_forward(unit):
        kind, layer = units[unit]
        split = parts_of(kind) > 1
        part = x if split else 0
        for o in range(1, n_y):
            def make(o=o):
                return weight(kind, layer, turn(y, n_y - o, n_y) * 2 + c, part)

            arrived(make(), ag_recv.at[unit, o], ag_send.at[unit, o])
            if split:
                for p in range(1, n_x):
                    index = base_x + (o - 1) * (n_x - 1) + p - 1
                    go(make, make(), ag, (unit, index), here.to(x=turn(x, p, n_x)))
            go(make, make(), ag, (unit, base_my + o - 1), mate)

    def weights_ready(unit):
        kind, layer = units[unit]
        split = parts_of(kind) > 1
        part = x if split else 0
        if split:
            for o in range(1, n_y):
                for p in range(1, n_x):
                    index = (o - 1) * (n_x - 1) + p - 1

                    def make(o=o, p=p):
                        shard = turn(y, n_y - o, n_y) * 2 + c
                        return weight(kind, layer, shard, turn(x, n_x - p, n_x))

                    arrived(
                        make(), ag_recv.at[unit, base_x + index], ag_send.at[unit, base_x + index]
                    )
                    go(make, make(), ag, (unit, base_mx + index), mate)
        arrived(weight(kind, layer, y * 2 + 1 - c), ag_recv.at[unit, 0], ag_send.at[unit, 0])
        for o in range(1, n_y):
            shard = turn(y, n_y - o, n_y) * 2 + 1 - c
            index = base_my + o - 1
            arrived(weight(kind, layer, shard, part), ag_recv.at[unit, index], ag_send.at[unit, index])
            if split:
                for p in range(1, n_x):
                    index = base_mx + (o - 1) * (n_x - 1) + p - 1
                    piece = weight(kind, layer, shard, turn(x, n_x - p, n_x))
                    arrived(piece, ag_recv.at[unit, index], ag_send.at[unit, index])

    lower = here.rep < n_rep // 2
    partner = here.to(z=turn(z, n_z // 2, n_z))
    back_half = pix.at[pl.ds(2, 2)]
    given = patches.at[pl.ds(KEPT, 2)]

    def local_half(half):
        return pltpu.make_async_copy(
            patches.at[pl.ds(2 * half, 2)], pix.at[pl.ds(2 * half, 2)], img_local.at[half]
        )

    def marks(pair):
        row = lax.broadcasted_iota(jnp.int32, (32, 128), 0)
        found = jnp.full((32, 128), -1.0, F32)
        for index in range(2):
            slot = 2 * pair + index
            value = jnp.where(slot < counts[0], labels[slot], -1).astype(F32)
            found = jnp.where(row == CLS - TAIL + 16 * index, value, found)
        return found

    local_half(0).start()
    for unit in range(2):
        for copy in weights_copies(unit):
            copy.start()
    lab[0] = marks(0)
    lab_given[...] = marks(2)

    @pl.when(jnp.logical_not(lower))
    def _():
        push(given, back_half, img_send.at[0], img_recv.at[0], partner)
        push(lab_given, lab.at[1], img_send.at[1], img_recv.at[1], partner)
        local_half(1).start()
        lab[1] = marks(1)

    for unit in range(4):
        weights_cast(unit)
        weights_start(unit)
    weights_forward(0)
    for unit in range(4, len(units)):
        weights_cast(unit)

    even = lane_mask(128, 0, 64)
    odd = lane_mask(128, 64, 128)
    low_lane = lax.broadcasted_iota(jnp.int32, (1, 128), 1) < 64
    key_lane = lax.broadcasted_iota(jnp.int32, (1, BLK), 1)
    key_row = jnp.where((key_lane < PATCHES) | (key_lane == CLS), 0.0, -1e30)
    key_sub = lax.broadcasted_iota(jnp.int32, (BLK, 1), 0)
    key_column = jnp.where((key_sub < PATCHES) | (key_sub == CLS), 0.0, -1e30)
    whole_lanes = NCLS // 128 * 128
    low_head[:, 0:whole_lanes] = head[0:D, 0:whole_lanes].astype(BF)
    low_head[:, whole_lanes:] = jnp.zeros((D, CPAD - whole_lanes), BF)
    low_head[:, whole_lanes:NCLS] = head[0:D, whole_lanes:NCLS].astype(BF)
    head_bias[...] = jnp.zeros((1, CPAD), F32)
    head_bias[:, 0:NCLS] = head[D : D + 1, :]
    V[...] = jnp.zeros((VEC_ROWS, VEC_WIDE), F32)
    square_sum[...] = jnp.zeros((8, 128), F32)
    zeros = jnp.zeros((8, D), F32)
    patch_bias = glob[0:1, :]

    def vector(layer, at, size):
        return vecs[pl.ds(layer, 1), at : at + size]

    def store_vector(layer, at, row):
        for piece in range(row.shape[-1] // D):
            V[pl.ds(VEC_AT + 12 * layer + at // D + piece, 1), 0:D] = row[
                :, piece * D : (piece + 1) * D
            ]

    def store_sums(layer, parts):
        for at, part in parts:
            store_vector(layer, at, down_sum(part))

    def embed(half):
        made = mm(pix[pl.ds(2 * half, 2)].reshape(HALF, PATCH_DIM), wp[...])
        for image in range(2):
            start = aligned(half * HALF + image * BLK, 16)
            for at, size in pieces(PATCHES - 4):
                X[pl.ds(start + at, size), :] = (
                    made[image * BLK + at : image * BLK + at + size]
                    + pos[1 + at : 1 + at + size, :]
                    + patch_bias
                )
            X[pl.ds(start + TAIL, 16), :] = jnp.zeros((16, D), F32)
            X[pl.ds(start + TAIL, 4), :] = (
                made[image * BLK + TAIL : image * BLK + PATCHES]
                + pos[1 + TAIL : 1 + PATCHES, :]
                + patch_bias
            )
            X[pl.ds(start + CLS, 1), :] = glob[1:2, :] + pos[0:1, :]

    def first_norm(layer, half, columns):
        base = half * HALF
        gain, shift = vector(layer, 0, D), vector(layer, D, D)
        for at, size in pieces(HALF):
            rows = pl.ds(aligned(base + at, 16), size)
            normed, inverse = norm(X[rows, :])
            N1[layer, rows, :] = normed.astype(BF)
            I1[layer, rows, :] = jnp.broadcast_to(inverse, (size, 128))
            DXB[rows, :] = (normed * gain + shift).astype(BF)
        rows = pl.ds(aligned(base, 16), HALF)
        h1 = DXB[rows, :]
        for tile in columns:
            made = mm(h1, win[layer, :, tile * D : (tile + 1) * D])
            if tile == 0:
                made = made + vector(layer, 2 * D, D)
            if tile == 2:
                made = made + vector(layer, 3 * D, D)
            if len(columns) == 3:
                QKV[layer, rows, tile * D : (tile + 1) * D] = made.astype(BF)
            else:
                (DMB if tile == 1 else DA)[rows, :] = made.astype(BF)

    def attend(layer, image):
        rows = pl.ds(aligned(image * BLK, 16), BLK)
        for pair in range(3):
            at = pair * 128
            query = QKV[layer, rows, at : at + 128] * BF(0.125)
            keys = QKV[layer, rows, D + at : D + at + 128]
            values = QKV[layer, rows, 2 * D + at : 2 * D + at + 128]
            both = jnp.concatenate([query * even, query * odd], axis=0)
            scores = mm_nt(both, keys)
            probs = []
            for row, size in pieces(HALF):
                part = scores[row : row + size] + key_row
                raw = jnp.exp(part - jnp.max(part, axis=-1, keepdims=True))
                share = 1.0 / jnp.sum(raw, axis=-1, keepdims=True)
                probs.append((raw * share).astype(BF))
            probs = jnp.concatenate(probs, axis=0)
            made = mm(probs[:BLK], values * even) + mm(probs[BLK:], values * odd)
            ATT[layer, rows, at : at + 128] = made.astype(BF)

    def mlp(layer, half):
        base = half * HALF
        whole = pl.ds(aligned(base, 16), HALF)
        made = mm(ATT[layer, whole, :], win[layer, :, 3 * D : 4 * D])
        bias_out = vector(layer, 4 * D, D)
        gain, shift = vector(layer, 5 * D, D), vector(layer, 6 * D, D)
        for at, size in pieces(HALF):
            rows = pl.ds(aligned(base + at, 16), size)
            middle = X[rows, :] + made[at : at + size] + bias_out
            X[rows, :] = middle
            normed, inverse = norm(middle)
            N2[layer, rows, :] = normed.astype(BF)
            I2[layer, rows, :] = jnp.broadcast_to(inverse, (size, 128))
            DXB[rows, :] = (normed * gain + shift).astype(BF)
        h2 = DXB[whole, :]
        for tile in range(4):
            columns = slice(tile * D, (tile + 1) * D)
            made = mm(h2, win[layer, :, (4 + tile) * D : (5 + tile) * D])
            bias = vector(layer, 7 * D + tile * D, D)
            for at, size in pieces(HALF):
                rows = pl.ds(aligned(base + at, 16), size)
                active, slope = gelu_parts(made[at : at + size] + bias)
                ACT[layer, rows, columns] = active.astype(BF)
                SLOPE[layer, rows, columns] = slope.astype(BF)
        made = mm(ACT[layer, whole, :], wdn[layer])
        bias = vector(layer, 7 * D + FF, D)
        for at, size in pieces(HALF):
            rows = pl.ds(aligned(base + at, 16), size)
            X[rows, :] = X[rows, :] + made[at : at + size] + bias

    def when(condition, *steps):
        @pl.when(condition)
        def _():
            for step, unit in steps:
                step(unit)

    weights_ready(0)

    def forward_half(half, carry):
        start = half == 0

        @pl.when(start)
        def _():
            local_half(0).wait()

        @pl.when(jnp.logical_and(half == 1, lower))
        def _():
            arrived(back_half, img_recv.at[0], img_send.at[0])

        @pl.when(jnp.logical_and(half == 1, jnp.logical_not(lower)))
        def _():
            local_half(1).wait()

        embed(half)

        def forward_layer(layer, inner):
            first = jnp.logical_and(start, layer == 0)
            second = jnp.logical_and(start, layer == 1)
            when(first, (weights_forward, 1), (weights_start, 4), (weights_ready, 1))
            when(second, (weights_ready, 4))
            first_norm(layer, half, (0, 1, 2))
            when(first, (weights_forward, 2), (weights_start, 5))
            when(second, (weights_forward, 6), (weights_start, 9))

            def attend_one(index, nothing):
                attend(layer, 2 * half + index)
                begin = index == 0
                when(
                    jnp.logical_and(first, begin), (weights_forward, 3), (weights_start, 6)
                )
                when(jnp.logical_and(second, begin), (weights_forward, 7))
                return nothing

            lax.fori_loop(0, 2, attend_one, 0)
            when(
                first, (weights_forward, 4), (weights_start, 7), (weights_ready, 2),
                (weights_ready, 3),
            )
            when(second, (weights_forward, 8), (weights_ready, 5), (weights_ready, 6))
            mlp(layer, half)
            when(first, (weights_forward, 5), (weights_start, 8))
            when(second, (weights_forward, 9))
            return inner

        return lax.fori_loop(0, LAYERS - 1, forward_layer, carry)

    lax.fori_loop(0, 2, forward_half, 0)
    for unit in (7, 8, 9):
        weights_ready(unit)

    last = LAYERS - 1

    def last_norm(half, nothing):
        first_norm(last, half, (1, 2))
        return nothing

    lax.fori_loop(0, 2, last_norm, 0)

    fac = ("f", f_send, f_recv)
    f_y, f_x = 1, n_y
    f_z = f_x + n_x - 1
    f_m = f_z + n_z - 1
    group = KEPT * n_shard

    def factors_core():
        go(lambda: FAC.at[1 - c], FC, fac, 0, mate)

    def factors_y():
        arrived(FC, f_recv.at[0], f_send.at[0])
        FAC[c] = FAC[c] + FC[...]
        for o in range(1, n_y):
            go(lambda: FAC.at[c], FY.at[o - 1], fac, f_y + o - 1, here.to(y=turn(y, o, n_y)))

    def factors_x():
        total = FAC[c]
        for o in range(1, n_y):
            arrived(FY.at[o - 1], f_recv.at[f_y + o - 1], f_send.at[f_y + o - 1])
            total = total + FY[o - 1]
        FALL[x] = total
        for o in range(1, n_x):
            go(lambda: FALL.at[x], FALL.at[x], fac, f_x + o - 1, here.to(x=turn(x, o, n_x)))

    def all_rows(at):
        return all_factors.at[c, pl.ds(at * n_x, n_x)]

    def factors_z():
        for o in range(1, n_x):
            index = f_x + o - 1
            arrived(FALL.at[turn(x, n_x - o, n_x)], f_recv.at[index], f_send.at[index])
        pltpu.make_async_copy(FALL, all_rows(z), out_local.at[0]).start()
        for o in range(1, n_z):
            go(lambda: FALL, all_rows(z), fac, f_z + o - 1, here.to(z=turn(z, o, n_z)))

    def factors_mate():
        for o in range(1, n_z):
            index = f_z + o - 1
            arrived(all_rows(turn(z, n_z - o, n_z)), f_recv.at[index], f_send.at[index])
        pltpu.make_async_copy(FALL, all_rows(z), out_local.at[0]).wait()
        go(lambda: all_factors.at[c], all_factors.at[c], fac, f_m, mate)

    def factors_done():
        arrived(all_factors.at[1 - c], f_recv.at[f_m], f_send.at[f_m])

    rs = ("rs", rs_send, rs_recv)
    r_y, r_x = 1, n_y
    r_z = r_x + n_x - 1
    r_gz = r_z + n_z - 1
    r_gx = r_gz + n_z - 1

    def chunk(k):
        if k < CHUNKS:
            return G.at[k], RC.at[k % 3], RY.at[k % 3], RX.at[k], RZ.at[k], RES.at[k], block
        k = k - CHUNKS
        return GS.at[k], SC.at[k], SY.at[k], SX.at[k], SZ.at[k], SRES.at[k], block // 2

    def splits(rows):
        by_x = cut(rows, n_x, 16)
        by_z = cut(rows // by_x, n_z, 16)
        return by_x, rows // by_x, by_z, rows // by_x // by_z

    def add_rows(rows, target, target_at, sources):
        step = 48 if rows % 48 == 0 else 16

        def one(index, nothing):
            at = index * step
            to = pl.ds(aligned(target_at + at, 16), step)
            total = target[to, :]
            if len(sources) == 1:
                total = total + sources[0][pl.ds(aligned(at, 16), step), :]
            else:
                total = total.astype(F32)
                for source in sources:
                    total = total + source[pl.ds(aligned(at, 16), step), :].astype(F32)
                total = total.astype(BF)
            target[to, :] = total
            return nothing

        lax.fori_loop(0, rows // step, one, 0)

    def reduce_core(k):
        g, rc = chunk(k)[0:2]
        go(lambda: chunk(k)[0].at[:, 1 - c], rc, rs, (k, 0), mate)

    def reduce_y(k):
        g, rc, ry, _, _, _, rows = chunk(k)
        arrived(rc, rs_recv.at[k, 0], rs_send.at[k, 0])
        for o in list(range(1, n_y)) + [0]:
            at = turn(y, o, n_y)
            add_rows(rows, g.at[at, c], 0, [rc.at[at]])
            if o:
                go(
                    lambda o=o: chunk(k)[0].at[turn(y, o, n_y), c], ry.at[o - 1], rs,
                    (k, r_y + o - 1), here.to(y=at),
                )

    def total_of(slots, count, at, step):
        total = None
        for index in range(count):
            value = slots[index, pl.ds(aligned(at, 16), step), :].astype(F32)
            total = value if total is None else total + value
        return total

    def reduce_x(k):
        g, _, ry, rx, _, _, rows = chunk(k)
        by_x, rows_x = splits(rows)[0:2]
        for o in range(1, n_y):
            arrived(ry.at[o - 1], rs_recv.at[k, r_y + o - 1], rs_send.at[k, r_y + o - 1])
        mine = g.at[y, c]
        add_rows(rows, mine, 0, [ry.at[o - 1] for o in range(1, n_y)])
        for o in range(1, n_x):
            to = turn(x, o, n_x)
            if by_x > 1:

                def make(o=o):
                    at = turn(x, o, n_x) * rows_x
                    return chunk(k)[0].at[y, c, pl.ds(aligned(at, 16), rows_x), :]

                go(make, rx.at[o - 1], rs, (k, r_x + o - 1), here.to(x=to))
            else:
                go(lambda: chunk(k)[0].at[y, c], rx.at[x], rs, (k, r_x + o - 1), here.to(x=to))

    def reduce_z(k):
        g, _, _, rx, rz, _, rows = chunk(k)
        by_x, rows_x, by_z, rows_z = splits(rows)
        mine = g.at[y, c]
        for o in range(1, n_x):
            slot = rx.at[o - 1] if by_x > 1 else rx.at[turn(x, n_x - o, n_x)]
            arrived(slot, rs_recv.at[k, r_x + o - 1], rs_send.at[k, r_x + o - 1])
        if by_x > 1:
            start = x * rows_x
            add_rows(rows_x, mine, start, [rx.at[o - 1] for o in range(1, n_x)])
        else:
            start = 0
            rx[x] = mine[...]
            for o in range(1, n_x):
                gone(rs, (k, r_x + o - 1))
            step = 48 if rows % 48 == 0 else 16

            def one(index, nothing):
                at = pl.ds(aligned(index * step, 16), step)
                g[y, c, at, :] = total_of(rx, n_x, index * step, step).astype(BF)
                return nothing

            lax.fori_loop(0, rows // step, one, 0)
        for o in range(1, n_z):

            def make(o=o):
                at = x * rows_x if by_x > 1 else 0
                if by_z > 1:
                    at = at + turn(z, o, n_z) * rows_z
                return chunk(k)[0].at[y, c, pl.ds(aligned(at, 16), rows_z), :]

            slot = rz.at[o - 1] if by_z > 1 else rz.at[z]
            go(make, slot, rs, (k, r_z + o - 1), here.to(z=turn(z, o, n_z)))

    def gather_z(k):
        g, _, _, _, rz, res, rows = chunk(k)
        by_x, rows_x, by_z, rows_z = splits(rows)
        start = x * rows_x if by_x > 1 else 0
        if by_z > 1:
            start = start + z * rows_z
        for o in range(1, n_z):
            slot = rz.at[o - 1] if by_z > 1 else rz.at[turn(z, n_z - o, n_z)]
            arrived(slot, rs_recv.at[k, r_z + o - 1], rs_send.at[k, r_z + o - 1])
        own_slot = n_z - 1 if by_z > 1 else z
        rz[own_slot] = g[y, c, pl.ds(aligned(start, 16), rows_z), :]
        share = 1.0 / ((1 if by_x > 1 else n_x) * (1 if by_z > 1 else n_z))
        step = 48 if rows_z % 48 == 0 else 16

        def one(index, total):
            low = total_of(rz, n_z, index * step, step).astype(BF)
            res[pl.ds(aligned(start + index * step, 16), step), :] = low
            wide = low.astype(F32)
            return total + fold(wide * wide)

        total = lax.fori_loop(0, rows_z // step, one, zeros) * share
        for at in range(0, D, 128):
            square_sum[...] = square_sum[...] + total[:, at : at + 128]
        if by_z > 1:

            def make():
                at = x * rows_x if by_x > 1 else 0
                return chunk(k)[5].at[pl.ds(aligned(at + z * rows_z, 16), rows_z), :]

            for o in range(1, n_z):
                go(make, make(), rs, (k, r_gz + o - 1), here.to(z=turn(z, o, n_z)))

    def gather_x(k):
        res, rows = chunk(k)[5:7]
        by_x, rows_x, by_z, rows_z = splits(rows)
        if by_z > 1:
            for o in range(1, n_z):
                start = turn(z, n_z - o, n_z) * rows_z
                if by_x > 1:
                    start = start + x * rows_x
                arrived(
                    res.at[pl.ds(aligned(start, 16), rows_z), :],
                    rs_recv.at[k, r_gz + o - 1], rs_send.at[k, r_gz + o - 1],
                )
        if by_x > 1:

            def make():
                return chunk(k)[5].at[pl.ds(aligned(x * rows_x, 16), rows_x), :]

            for o in range(1, n_x):
                go(make, make(), rs, (k, r_gx + o - 1), here.to(x=turn(x, o, n_x)))

    def result(k):
        if k < CHUNKS:
            return pltpu.make_async_copy(RES.at[k], res_out.at[k], out_local.at[1 + k])
        return pltpu.make_async_copy(
            SRES.at[k - CHUNKS], small_out.at[k - CHUNKS], out_local.at[1 + k]
        )

    def gather_done(k):
        res, rows = chunk(k)[5:7]
        by_x, rows_x = splits(rows)[0:2]
        if by_x > 1:
            for o in range(1, n_x):
                start = turn(x, n_x - o, n_x) * rows_x
                arrived(
                    res.at[pl.ds(aligned(start, 16), rows_x), :],
                    rs_recv.at[k, r_gx + o - 1], rs_send.at[k, r_gx + o - 1],
                )
        result(k).start()

    def tails(ref, layer=None):
        found = []
        for image in range(KEPT):
            rows = slice(image * BLK + TAIL, (image + 1) * BLK)
            found.append(ref[rows, :] if layer is None else ref[layer, rows, :])
        return jnp.concatenate(found, axis=0)

    @pl.when(lower)
    def _():
        arrived(lab.at[1], img_recv.at[1], img_send.at[1])

    marked = lab[...].reshape(CROWS, 128)[:, 0:1]

    h1 = tails(DXB)
    stream = tails(X)
    query = ((mm(h1, win[last, :, 0:D]) + vector(last, 2 * D, D)).astype(BF)) * BF(0.125)
    head_masks = [lane_mask(D, index * 64, (index + 1) * 64) for index in range(HEADS)]

    def spread(values):
        return jnp.concatenate([values * mask for mask in head_masks], axis=0)

    def gather_heads(values):
        total = None
        for index in range(HEADS):
            part = values[index * 16 : (index + 1) * 16] * head_masks[index].astype(F32)
            total = part if total is None else total + part
        return total

    spread_queries, probabilities, outs = [], [], []
    for image in range(KEPT):
        rows = slice(image * BLK, (image + 1) * BLK)
        queries = spread(query[image * 16 : (image + 1) * 16])
        scores = mm_nt(queries, DMB[rows, :]) + key_row
        raw = jnp.exp(scores - jnp.max(scores, axis=-1, keepdims=True))
        probs = raw * (1.0 / jnp.sum(raw, axis=-1, keepdims=True))
        spread_queries.append(queries)
        probabilities.append(probs)
        outs.append(gather_heads(mm(probs.astype(BF), DA[rows, :])))
    attended = jnp.concatenate(outs, axis=0).astype(BF)
    middle = stream + mm(attended, win[last, :, 3 * D : 4 * D]) + vector(last, 4 * D, D)
    n2, i2 = norm(middle)
    h2 = (n2 * vector(last, 5 * D, D) + vector(last, 6 * D, D)).astype(BF)
    active, slope = gelu_parts(mm(h2, win[last, :, 4 * D :]) + vector(last, 7 * D, FF))
    active = active.astype(BF)
    top = middle + mm(active, wdn[last]) + vector(last, 7 * D + FF, D)
    gain_final = glob[2:3, :]
    nf, inf = norm(top)
    final = (nf * gain_final + glob[3:4, :]).astype(BF)
    class_lane = lax.broadcasted_iota(jnp.int32, (1, CPAD), 1)
    logits = mm(final, low_head[...]) + head_bias[...]
    logits = jnp.where(class_lane < NCLS, logits, -1e30)
    peak = jnp.max(logits, axis=-1, keepdims=True)
    shifted = logits - peak
    raw = jnp.exp(shifted)
    total = jnp.sum(raw, axis=-1, keepdims=True)
    alive = jnp.where(marked >= 0.0, 1.0, 0.0)
    target = jnp.where(class_lane.astype(F32) == marked, 1.0 - SMOOTHING, 0.0) + jnp.where(
        class_lane < NCLS, SMOOTHING / NCLS, 0.0
    )
    log_probs = jnp.where(class_lane < NCLS, shifted - jnp.log(total), 0.0)
    losses = -jnp.sum(target * log_probs, axis=-1, keepdims=True) * alive
    d_logits = ((raw * (1.0 / total) - target) * alive).astype(BF)
    d_final = mm_nt(d_logits, low_head[...])
    last_row = VEC_AT + 12 * LAYERS
    V[last_row : last_row + 1, 0:D] = down_sum(d_final * nf)
    V[last_row + 1 : last_row + 2, 0:D] = down_sum(d_final)
    V[last_row + 2 : last_row + 3, 0:128] = jnp.broadcast_to(down_sum(losses), (1, 128))
    V[last_row + 3 : last_row + 4, 0:128] = jnp.full((1, 128), counts[0].astype(F32), F32)
    d_top = norm_back(d_final, nf, inf, gain_final)
    low_top = d_top.astype(BF)
    store_vector(last, 7 * D + FF, down_sum(d_top))
    d_up = (mm_nt(low_top, wdn[last]) * slope).astype(BF)
    store_vector(last, 7 * D, down_sum(d_up.astype(F32)))
    d_h2 = mm_nt(d_up, win[last, :, 4 * D :])
    store_vector(last, 5 * D, down_sum(d_h2 * n2))
    store_vector(last, 6 * D, down_sum(d_h2))
    d_middle = d_top + norm_back(d_h2, n2, i2, vector(last, 5 * D, D))
    low_middle = d_middle.astype(BF)
    store_vector(last, 4 * D, down_sum(d_middle))
    d_heads = mm_nt(low_middle, win[last, :, 3 * D : 4 * D]).astype(BF)
    d_queries = []
    for image in range(KEPT):
        rows = slice(image * BLK, (image + 1) * BLK)
        ups = spread(d_heads[image * 16 : (image + 1) * 16])
        probs = probabilities[image]
        d_probs = mm_nt(ups, DA[rows, :])
        inner = jnp.sum(d_probs * probs, axis=-1, keepdims=True)
        d_scores = (probs * (d_probs - inner)).astype(BF)
        d_queries.append(gather_heads(mm(d_scores, DMB[rows, :])) * 0.125)
        DMB[rows, :] = mm_tn(d_scores, spread_queries[image]).astype(BF)
        DA[rows, :] = mm_tn(probs.astype(BF), ups).astype(BF)
    d_query = jnp.concatenate(d_queries, axis=0).astype(BF)
    store_vector(last, 2 * D, down_sum(d_query.astype(F32)))
    from_query = mm_nt(d_query, win[last, :, 0:D])

    pick_row = lax.broadcasted_iota(jnp.int32, (group, CROWS), 0)
    pick_lane = lax.broadcasted_iota(jnp.int32, (group, CROWS), 1)
    pick = jnp.where(
        ((pick_row - KEPT * here.shard) * 16 + (CLS - TAIL)) == pick_lane, 1.0, 0.0
    ).astype(BF)
    at = 0
    for piece in (active, h2, attended, h1, final, low_top):
        FAC[0, :, at : at + piece.shape[-1]] = mm(pick, piece).astype(BF)
        at += piece.shape[-1]
    at = 0
    for piece in (d_up, low_middle, d_query, d_logits):
        FAC[1, :, at : at + piece.shape[-1]] = mm(pick, piece).astype(BF)
        at += piece.shape[-1]
    FAC[1, :, at:] = jnp.zeros((group, WFAC - at), BF)
    factors_core()

    turned = DXB[...].T
    for tile, grads in enumerate((DMB, DA)):
        made = mm(turned, grads[...]).astype(BF)
        for shard in range(n_shard):
            GS[0, shard // 2, shard % 2, tile * rows_in : (tile + 1) * rows_in, :] = made[
                shard * rows_in : (shard + 1) * rows_in
            ]
    reduce_core(CHUNKS)
    factors_y()
    store_sums(last, [(3 * D, fold(DA[...].astype(F32)))])

    X[...] = jnp.zeros((ROWS, D), F32)
    gain = vector(last, 0, D)
    gain_sum, shift_sum = zeros, zeros
    for image in range(KEPT):
        rows = slice(image * BLK + TAIL, (image + 1) * BLK)
        part = from_query[image * 16 : (image + 1) * 16]
        normed = N1[last, rows, :].astype(F32)
        gain_sum = gain_sum + fold(part * normed)
        shift_sum = shift_sum + fold(part)
        X[rows, :] = d_middle[image * 16 : (image + 1) * 16] + norm_back(
            part, normed, I1[last, rows, :][:, 0:1], gain
        )

    def first_back(layer, half, made, sums):
        base = half * HALF
        gain = vector(layer, 0, D)
        gain_sum, shift_sum = sums
        for at, size in pieces(HALF):
            rows = pl.ds(aligned(base + at, 16), size)
            part = made[at : at + size]
            normed = N1[layer, rows, :].astype(F32)
            inverse = I1[layer, rows, :][:, 0:1]
            gain_sum = gain_sum + fold(part * normed)
            shift_sum = shift_sum + fold(part)
            X[rows, :] = X[rows, :] + norm_back(part, normed, inverse, gain)
        return gain_sum, shift_sum

    def last_back(half, sums):
        rows = pl.ds(aligned(half * HALF, 16), HALF)
        made = mm_nt(DMB[rows, :], win[last, :, D : 2 * D])
        made = made + mm_nt(DA[rows, :], win[last, :, 2 * D : 3 * D])
        return first_back(last, half, made, sums)

    gain_sum, shift_sum = lax.fori_loop(0, 2, last_back, (gain_sum, shift_sum))
    store_sums(last, [(0, gain_sum), (D, shift_sum)])
    reduce_y(CHUNKS)
    factors_x()

    def mlp_back(layer, half, sums):
        base = half * HALF
        whole = pl.ds(aligned(base, 16), HALF)
        bias_down, bias_up, gain_sum, shift_sum, bias_out = sums
        for at, size in pieces(HALF):
            rows = pl.ds(aligned(base + at, 16), size)
            up = X[rows, :]
            DXB[rows, :] = up.astype(BF)
            bias_down = bias_down + fold(up)
        low = DXB[whole, :]
        ups = []
        for tile in range(4):
            columns = slice(tile * D, (tile + 1) * D)
            made = mm_nt(low, wdn[layer, columns, :])
            total = bias_up[tile]
            for at, size in pieces(HALF):
                rows = pl.ds(aligned(base + at, 16), size)
                grad = (made[at : at + size] * SLOPE[layer, rows, columns].astype(F32)).astype(BF)
                SLOPE[layer, rows, columns] = grad
                total = total + fold(grad.astype(F32))
            ups.append(total)
        made = mm_nt(SLOPE[layer, whole, :], win[layer, :, 4 * D :])
        gain = vector(layer, 5 * D, D)
        for at, size in pieces(HALF):
            rows = pl.ds(aligned(base + at, 16), size)
            part = made[at : at + size]
            normed = N2[layer, rows, :].astype(F32)
            inverse = I2[layer, rows, :][:, 0:1]
            gain_sum = gain_sum + fold(part * normed)
            shift_sum = shift_sum + fold(part)
            grad = X[rows, :] + norm_back(part, normed, inverse, gain)
            X[rows, :] = grad
            DMB[rows, :] = grad.astype(BF)
            bias_out = bias_out + fold(grad)
        DA[whole, :] = mm_nt(DMB[whole, :], win[layer, :, 3 * D : 4 * D]).astype(BF)
        return bias_down, tuple(ups), gain_sum, shift_sum, bias_out

    def attend_back(layer, image):
        rows = pl.ds(aligned(image * BLK, 16), BLK)
        for pair in range(3):
            at = pair * 128
            query = QKV[layer, rows, at : at + 128] * BF(0.125)
            keys = QKV[layer, rows, D + at : D + at + 128]
            values = QKV[layer, rows, 2 * D + at : 2 * D + at + 128]
            ups = DA[rows, at : at + 128]
            keys_both = jnp.concatenate([keys * even, keys * odd], axis=0)
            values_both = jnp.concatenate([values * even, values * odd], axis=0)
            scores = mm_nt(keys_both, query)
            d_probs = mm_nt(values_both, ups)
            probs, d_scores = [], []
            for base in (0, BLK):
                low_probs, low_grads = [], []
                for first, end in ((0, 128), (128, BLK)):
                    part = jnp.concatenate(
                        [
                            scores[base : base + TAIL, first:end],
                            scores[base + TAIL : base + BLK, first:end] + key_column[TAIL:],
                        ],
                        axis=0,
                    )
                    raw = jnp.exp(part - jnp.max(part, axis=0, keepdims=True))
                    prob = raw * (1.0 / jnp.sum(raw, axis=0, keepdims=True))
                    grad = d_probs[base : base + BLK, first:end]
                    inner = jnp.sum(grad * prob, axis=0, keepdims=True)
                    low_grads.append((prob * (grad - inner)).astype(BF))
                    low_probs.append(prob.astype(BF))
                probs.append(jnp.concatenate(low_probs, axis=1))
                d_scores.append(jnp.concatenate(low_grads, axis=1))
            probs = jnp.concatenate(probs, axis=0)
            d_scores = jnp.concatenate(d_scores, axis=0)
            d_values = mm(probs, ups)
            d_keys = mm(d_scores, query)
            d_query = mm_tn(d_scores, keys_both) * 0.125
            QKV[layer, rows, at : at + 128] = d_query.astype(BF)
            QKV[layer, rows, D + at : D + at + 128] = jnp.where(
                low_lane, d_keys[:BLK], d_keys[BLK:]
            ).astype(BF)
            QKV[layer, rows, 2 * D + at : 2 * D + at + 128] = jnp.where(
                low_lane, d_values[:BLK], d_values[BLK:]
            ).astype(BF)

    def renew(ref, layer, at):
        gain, shift = vector(layer, at, D), vector(layer, at + D, D)

        def one(index, nothing):
            rows = pl.ds(aligned(index * 64, 16), 64)
            DXB[rows, :] = (ref[layer, rows, :].astype(F32) * gain + shift).astype(BF)
            return nothing

        lax.fori_loop(0, ROWS // 64, one, 0)
        return DXB[...].T

    def keep_in(k, tile, made):
        for shard in range(n_shard):
            G[k, shard // 2, shard % 2, tile * rows_in : (tile + 1) * rows_in, :] = made[
                shard * rows_in : (shard + 1) * rows_in
            ]

    def backward(step, carry):
        layer = LAYERS - 2 - step
        kd, ku, kq = 3 * step, 3 * step + 1, 3 * step + 2
        upper_layer, bottom = step == 0, step == 1

        def one(half, sums):
            sums = mlp_back(layer, half, sums)
            begin = half == 0

            @pl.when(jnp.logical_and(upper_layer, begin))
            def _():
                factors_z()

            when(jnp.logical_and(bottom, begin), (gather_z, CHUNKS))
            return sums

        bias_down, bias_up, gain_sum, shift_sum, bias_out = lax.fori_loop(
            0, 2, one, (zeros, (zeros,) * 4, zeros, zeros, zeros)
        )
        when(upper_layer, (reduce_x, CHUNKS))
        when(bottom, (reduce_x, 2), (reduce_z, 1))
        store_sums(
            layer,
            [(7 * D + FF, bias_down), (5 * D, gain_sum), (6 * D, shift_sum), (4 * D, bias_out)]
            + [(7 * D + tile * D, bias_up[tile]) for tile in range(4)],
        )
        turned = DXB[...].T
        per = min(rows_down, D)
        for tile in range(4):
            columns = slice(tile * D, (tile + 1) * D)
            made = mm(turned, ACT[layer, :, columns]).astype(BF).T
            for piece in range(D // per):
                shard, at = divmod(tile * D + piece * per, rows_down)
                G[kd, shard // 2, shard % 2, at : at + per, :] = made[
                    piece * per : (piece + 1) * per
                ]
        when(upper_layer, (reduce_core, 0))
        when(bottom, (reduce_core, 3), (gather_z, 0), (gather_x, CHUNKS))
        turned = renew(N2, layer, 5 * D)
        for tile in range(4):
            keep_in(
                ku, tile, mm(turned, SLOPE[layer, :, tile * D : (tile + 1) * D]).astype(BF)
            )
        when(upper_layer, (reduce_core, 1), (reduce_y, 0), (reduce_z, CHUNKS))
        when(bottom, (reduce_core, 4), (reduce_y, 3), (reduce_z, 2))
        keep_in(kq, 3, mm(ATT[layer].T, DMB[...]).astype(BF))

        def two(image, nothing):
            attend_back(layer, image)
            when(jnp.logical_and(upper_layer, image == 0), (reduce_y, 1))
            when(jnp.logical_and(upper_layer, image == 2), (reduce_x, 0))
            when(jnp.logical_and(bottom, image == 0), (reduce_y, 4), (gather_z, 1))

            @pl.when(jnp.logical_and(bottom, image == 1))
            def _():
                factors_mate()
                gather_done(CHUNKS)
                gather_x(0)

            when(jnp.logical_and(bottom, image == 2), (reduce_x, 3), (gather_z, 2))
            when(jnp.logical_and(bottom, image == 3), (gather_x, 1), (reduce_z, 3))
            return nothing

        lax.fori_loop(0, KEPT, two, 0)
        turned = renew(N1, layer, 0)
        for tile in range(3):
            keep_in(
                kq, tile, mm(turned, QKV[layer, :, tile * D : (tile + 1) * D]).astype(BF)
            )
        when(upper_layer, (reduce_core, 2))
        when(bottom, (reduce_core, 5), (gather_x, 2), (gather_done, 0))
        store_sums(
            layer,
            [
                (2 * D, fold(QKV[layer, :, 0:D].astype(F32))),
                (3 * D, fold(QKV[layer, :, 2 * D : 3 * D].astype(F32))),
            ],
        )

        def three(half, sums):
            rows = pl.ds(aligned(half * HALF, 16), HALF)
            made = mm_nt(QKV[layer, rows, :], win[layer, :, 0 : 3 * D])
            return first_back(layer, half, made, sums)

        gain_sum, shift_sum = lax.fori_loop(0, 2, three, (zeros, zeros))
        store_sums(layer, [(0, gain_sum), (D, shift_sum)])
        when(upper_layer, (reduce_x, 1), (reduce_y, 2), (reduce_z, 0))
        when(bottom, (reduce_y, 5), (reduce_x, 4), (gather_z, 3), (gather_done, 1))
        return carry

    lax.fori_loop(0, LAYERS - 1, backward, 0)

    for at, size in pieces(BLK):
        total = None
        for image in range(KEPT):
            part = X[image * BLK + at : image * BLK + at + size, :]
            DXB[image * BLK + at : image * BLK + at + size, :] = part.astype(BF)
            total = part if total is None else total + part
        V[at : at + size, 0:D] = total

    vec = ("v", v_send, v_recv)
    v_y, v_x = 1, n_y
    v_z = v_x + n_x - 1
    v_gz = v_z + n_z - 1
    v_q = v_gz + n_z - 1
    v_gx = v_q + n_z - 1
    v_gy = v_gx + n_x - 1
    v_gc = v_gy + n_y - 1
    rows_c = VEC_ROWS // 2
    rows_y = rows_c // n_y
    rows_x = rows_y // n_x
    split_z = cut(rows_x, n_z, 8)
    rows_z = rows_x // split_z
    at_c = c * rows_c
    at_y = at_c + y * rows_y
    at_x = at_y + x * rows_x
    at_z = at_x + z * rows_z if split_z > 1 else at_x

    def vrows(ref, at, rows):
        return ref.at[pl.ds(aligned(at, 8), rows), :]

    def narrow(at, rows):
        return VF.at[pl.ds(aligned(at, 8), rows), pl.ds(0, D)]

    def vadd(at, rows, sources):
        target = pl.ds(aligned(at, 8), rows)
        total = V[target, :]
        for source in sources:
            total = total + source
        V[target, :] = total

    def vectors_core():
        go(lambda: vrows(V, (1 - c) * rows_c, rows_c), VC, vec, 0, mate)

    def vectors_y():
        arrived(VC, v_recv.at[0], v_send.at[0])
        vadd(at_c, rows_c, [VC[...]])
        for o in range(1, n_y):
            to = turn(y, o, n_y)
            go(
                lambda o=o: vrows(V, at_c + turn(y, o, n_y) * rows_y, rows_y), VY.at[o - 1],
                vec, v_y + o - 1, here.to(y=to),
            )

    def vectors_x():
        for o in range(1, n_y):
            arrived(VY.at[o - 1], v_recv.at[v_y + o - 1], v_send.at[v_y + o - 1])
        vadd(at_y, rows_y, [VY[o - 1] for o in range(1, n_y)])
        for o in range(1, n_x):
            to = turn(x, o, n_x)
            go(
                lambda o=o: vrows(V, at_y + turn(x, o, n_x) * rows_x, rows_x), VX.at[o - 1],
                vec, v_x + o - 1, here.to(x=to),
            )

    def vectors_z():
        for o in range(1, n_x):
            arrived(VX.at[o - 1], v_recv.at[v_x + o - 1], v_send.at[v_x + o - 1])
        vadd(at_x, rows_x, [VX[o - 1] for o in range(1, n_x)])
        for o in range(1, n_z):

            def make(o=o):
                at = at_x + turn(z, o, n_z) * rows_z if split_z > 1 else at_x
                return vrows(V, at, rows_z)

            go(make, VZ.at[z], vec, v_z + o - 1, here.to(z=turn(z, o, n_z)))

    def vectors_gather_z():
        for o in range(1, n_z):
            arrived(
                VZ.at[turn(z, n_z - o, n_z)], v_recv.at[v_z + o - 1], v_send.at[v_z + o - 1]
            )
        target = pl.ds(aligned(at_z, 8), rows_z)
        VZ[z] = V[target, :]
        total = VZ[0]
        for index in range(1, n_z):
            total = total + VZ[index]
        VF[target, 0:D] = total[:, 0:D]
        if split_z > 1:
            for o in range(1, n_z):
                go(
                    lambda: narrow(at_z, rows_z), narrow(at_z, rows_z), vec, v_gz + o - 1,
                    here.to(z=turn(z, o, n_z)),
                )

    def squares_send():
        SQ[...] = square_sum[...]
        SQS[z] = square_sum[...]
        for o in range(1, n_z):
            go(lambda: SQ, SQS.at[z], vec, v_q + o - 1, here.to(z=turn(z, o, n_z)))

    def vectors_gather_x():
        for o in range(1, n_z):
            came = turn(z, n_z - o, n_z)
            if split_z > 1:
                arrived(
                    narrow(at_x + came * rows_z, rows_z), v_recv.at[v_gz + o - 1],
                    v_send.at[v_gz + o - 1],
                )
            arrived(SQS.at[came], v_recv.at[v_q + o - 1], v_send.at[v_q + o - 1])
        total = SQS[0]
        for index in range(1, n_z):
            total = total + SQS[index]
        for at in range(0, rows_x, 8):
            VF[pl.ds(aligned(at_x + at, 8), 8), D:] = total
        for o in range(1, n_x):
            go(
                lambda: vrows(VF, at_x, rows_x), vrows(VF, at_x, rows_x), vec, v_gx + o - 1,
                here.to(x=turn(x, o, n_x)),
            )

    def vectors_gather_y():
        for o in range(1, n_x):
            at = at_y + turn(x, n_x - o, n_x) * rows_x
            arrived(vrows(VF, at, rows_x), v_recv.at[v_gx + o - 1], v_send.at[v_gx + o - 1])
        for o in range(1, n_y):
            go(
                lambda: vrows(VF, at_y, rows_y), vrows(VF, at_y, rows_y), vec, v_gy + o - 1,
                here.to(y=turn(y, o, n_y)),
            )

    def vectors_gather_core():
        for o in range(1, n_y):
            at = at_c + turn(y, n_y - o, n_y) * rows_y
            arrived(vrows(VF, at, rows_y), v_recv.at[v_gy + o - 1], v_send.at[v_gy + o - 1])
        go(lambda: vrows(VF, at_c, rows_c), vrows(VF, at_c, rows_c), vec, v_gc, mate)

    def vectors_done():
        arrived(vrows(VF, (1 - c) * rows_c, rows_c), v_recv.at[v_gc], v_send.at[v_gc])

    vectors_core()
    low = DXB[...]
    for tile in range(2):
        made = mm_tn(pix[:, :, tile * D : (tile + 1) * D].reshape(ROWS, D), low).astype(BF)
        for piece in range(D // rows_patch):
            shard = tile * (D // rows_patch) + piece
            GS[1, shard // 2, shard % 2] = made[piece * rows_patch : (piece + 1) * rows_patch]

    kp = CHUNKS + 1
    reduce_core(kp)
    reduce_z(4)
    vectors_y()
    reduce_y(kp)
    gather_x(3)
    reduce_x(5)
    vectors_x()
    gather_z(4)
    reduce_x(kp)
    reduce_z(5)
    vectors_z()
    gather_done(2)
    gather_x(4)
    gather_done(3)
    reduce_z(kp)
    gather_z(5)
    vectors_gather_z()
    gather_z(kp)
    squares_send()
    gather_x(5)
    gather_x(kp)
    vectors_gather_x()
    gather_done(4)
    vectors_gather_y()
    gather_done(5)
    gather_done(kp)
    vectors_gather_core()
    factors_done()
    vectors_done()
    last_copy = pltpu.make_async_copy(VF, vec_out, out_local.at[1 + CHUNKS + 2])
    last_copy.start()
    for source, send, recv, at in list(sent.values()):
        left_here(source(), recv.at[at], send.at[at])
    for k in range(CHUNKS + 2):
        result(k).wait()
    last_copy.wait()

    @pl.when(jnp.logical_not(lower))
    def _():
        left_here(given, img_recv.at[0], img_send.at[0])
        left_here(lab_given, img_recv.at[1], img_send.at[1])


def run_train(
    n_rep, n_shard, patches, labels, counts, own_patch, own_in, own_down, vecs, glob, pos, head
):
    n_x = 2 ** ((n_rep.bit_length() - 2) // 2)
    n_z, n_y = n_rep // n_x, n_shard // 2
    block = 4 * (D // n_shard)
    group = KEPT * n_shard
    keep = LAYERS - 1
    units = 1 + 3 * LAYERS
    chunks = CHUNKS + 2

    def buf(*shape, dtype=BF):
        return pltpu.VMEM(shape, dtype)

    def sems(*shape):
        return pltpu.SemaphoreType.DMA(shape)

    def reduction(count, rows):
        by_x = cut(rows, n_x, 16)
        by_z = cut(rows // by_x, n_z, 16)
        return [
            buf(count, n_y, 2, rows, D),
            buf(min(count, 3), n_y, rows, D),
            buf(min(count, 3), n_y - 1, rows, D),
            buf(count, n_x - 1 if by_x > 1 else n_x, rows // by_x, D),
            buf(count, n_z, rows // by_x // by_z, D),
            buf(count, rows, D),
        ]

    rows_y = VEC_ROWS // 2 // n_y
    rows_x = rows_y // n_x
    rows_z = rows_x // cut(rows_x, n_z, 8)
    ag_count = n_y + (n_y - 1) * (n_x - 1) * 2 + n_y - 1
    rs_count = 1 + (n_y - 1) + 2 * (n_x - 1) + 2 * (n_z - 1)
    f_count = 1 + (n_y - 1) + (n_x - 1) + (n_z - 1) + 1
    v_count = 1 + 2 * (n_y - 1) + 2 * (n_x - 1) + 3 * (n_z - 1) + 1
    whole = pl.BlockSpec(memory_space=pltpu.VMEM)
    there = pl.BlockSpec(memory_space=pl.ANY)
    return pl.pallas_call(
        functools.partial(train, n_rep, n_shard),
        out_shape=[
            jax.ShapeDtypeStruct((CHUNKS, block, D), BF),
            jax.ShapeDtypeStruct((2, block // 2, D), BF),
            jax.ShapeDtypeStruct((VEC_ROWS, VEC_WIDE), F32),
            jax.ShapeDtypeStruct((2, n_rep, group, WFAC), BF),
        ],
        in_specs=[there] + [pl.BlockSpec(memory_space=pltpu.SMEM)] * 2 + [there] * 3 + [whole] * 4,
        out_specs=[there] * 4,
        scratch_shapes=[
            buf(ROWS, D, dtype=F32),
            buf(LAYERS, ROWS, D),
            buf(LAYERS, ROWS, 128, dtype=F32),
            buf(keep, ROWS, 3 * D),
            buf(keep, ROWS, D),
            buf(keep, ROWS, D),
            buf(keep, ROWS, 128, dtype=F32),
            buf(keep, ROWS, FF),
            buf(keep, ROWS, FF),
            buf(ROWS, D),
            buf(ROWS, D),
            buf(ROWS, D),
            buf(KEPT, BLK, PATCH_DIM),
            buf(2, 32, 128, dtype=F32),
            buf(32, 128, dtype=F32),
            buf(PATCH_DIM, D),
            buf(LAYERS, D, 4 * D + FF),
            buf(LAYERS, FF, D),
            buf(D, CPAD),
            buf(1, CPAD, dtype=F32),
            *reduction(CHUNKS, block),
            *reduction(2, block // 2),
            buf(2, group, WFAC),
            buf(group, WFAC),
            buf(n_y - 1, group, WFAC),
            buf(n_x, group, WFAC),
            buf(VEC_ROWS, VEC_WIDE, dtype=F32),
            buf(VEC_ROWS // 2, VEC_WIDE, dtype=F32),
            buf(n_y - 1, rows_y, VEC_WIDE, dtype=F32),
            buf(n_x - 1, rows_x, VEC_WIDE, dtype=F32),
            buf(n_z, rows_z, VEC_WIDE, dtype=F32),
            buf(VEC_ROWS, VEC_WIDE, dtype=F32),
            buf(8, 128, dtype=F32),
            buf(n_z, 8, 128, dtype=F32),
            buf(8, 128, dtype=F32),
            sems(units, ag_count),
            sems(units, ag_count),
            sems(units, 4),
            sems(chunks, rs_count),
            sems(chunks, rs_count),
            sems(f_count),
            sems(f_count),
            sems(v_count),
            sems(v_count),
            sems(2),
            sems(2),
            sems(4),
            sems(2 + chunks),
        ],
        compiler_params=pltpu.CompilerParams(
            vmem_limit_bytes=65400 * 1024, collective_id=0, has_side_effects=True
        ),
        cost_estimate=pl.CostEstimate(
            flops=24_000_000_000, bytes_accessed=30_000_000, transcendentals=10_000_000
        ),
        name="train_step",
    )(patches, labels, counts, own_patch, own_in, own_down, vecs, glob, pos, head)


def adam(weight, first, second, grad, factor, rate):
    grad = grad * factor
    first = BETA_FIRST * first + (1.0 - BETA_FIRST) * grad
    second = BETA_SECOND * second + (1.0 - BETA_SECOND) * (grad * grad)
    first_scale = 1.0 / (1.0 - BETA_FIRST**ADAM_STEP)
    root_scale = (1.0 / (1.0 - BETA_SECOND**ADAM_STEP)) ** 0.5
    bottom = second * lax.rsqrt(second) * root_scale + ADAM_EPS
    step = first * lax.rsqrt(bottom * bottom)
    weight = weight * (1.0 - rate * WEIGHT_DECAY) - step * (rate * first_scale)
    return weight, first, second


def update(n_rep, n_shard, *refs):
    res, small, vec, factors = refs[0:4]
    sources = refs[4:25]
    loss_out, norm_out = refs[25:27]
    targets = refs[27:48]
    buffers = refs[48:69]
    last_in, last_down, grad_head, in_sems, out_sems = refs[69:]
    shard = lax.axis_index("shard")
    rows_in = D // n_shard
    rows_down = FF // n_shard
    keep = LAYERS - 1

    def moves(array, layer=None, out=False):
        found = []
        for kind in range(3):
            index = 3 * array + kind
            if out:
                src, dst, sem = buffers[index], targets[index], out_sems
            else:
                src, dst, sem = sources[index], buffers[index], in_sems
            slot = 0 if layer is None else layer
            if layer is not None:
                src, dst = src.at[layer], dst.at[layer]
            found.append(pltpu.make_async_copy(src, dst, sem.at[index, slot]))
        return found

    layered = [(1, layer) for layer in range(LAYERS)] + [(2, layer) for layer in range(LAYERS)]
    order = layered + [(0, None), (6, None), (5, None), (3, None), (4, None)]
    for array, layer in order:
        for move in moves(array, layer):
            move.start()

    n_rows = factors.shape[1] * factors.shape[2]

    def factor(half, at, size):
        return factors[half, :, :, at : at + size].reshape(n_rows, size)

    def squares(values):
        return fold(values * values)

    total = jnp.zeros((8, D), F32)
    h2 = factor(0, FF, D)
    for tile in range(4):
        made = mm_tn(h2, factor(1, tile * D, D))
        last_in[:, (4 + tile) * D : (5 + tile) * D] = made
        total = total + squares(made)
    own_rows = pl.multiple_of(shard * rows_in, 8)
    for tile in range(2):
        last_in[pl.ds(own_rows, rows_in), (1 + tile) * D : (2 + tile) * D] = small[
            0, tile * rows_in : (tile + 1) * rows_in, :
        ].astype(F32)
    made = mm_tn(factor(0, FF + 2 * D, D), factor(1, FF + D, D))
    last_in[:, 0:D] = made
    total = total + squares(made)
    made = mm_tn(factor(0, FF + D, D), factor(1, FF, D))
    last_in[:, 3 * D : 4 * D] = made
    total = total + squares(made)
    d_top = factor(0, FF + 4 * D, D)
    for tile in range(4):
        made = mm_tn(factor(0, tile * D, D), d_top)
        last_down[tile * D : (tile + 1) * D, :] = made
        total = total + squares(made)
    final = factor(0, FF + 3 * D, D)
    wide = jnp.zeros((8, 128), F32)
    for at in range(0, CPAD, 512):
        d_logits = factor(1, FF + 2 * D + at, 512)
        made = mm_tn(final, d_logits)
        grad_head[0:D, at : at + 512] = made
        bias = down_sum(d_logits.astype(F32))
        grad_head[D : D + 1, at : at + 512] = bias
        sums = squares(made)
        for lane in range(0, 512, 128):
            wide = wide + sums[:, lane : lane + 128]
            row = bias[:, lane : lane + 128]
            wide = wide + (row * row) * 0.125
    for lane in range(0, D, 128):
        wide = wide + total[:, lane : lane + 128]
    used = VEC_AT + 12 * LAYERS + 2
    parts = jnp.zeros((8, D), F32)
    kept_rows = lax.broadcasted_iota(jnp.int32, (8, 1), 0)
    for at in range(0, used, 8):
        value = vec[at : at + 8, 0:D]
        if at + 8 > used:
            value = jnp.where(kept_rows + at < used, value, 0.0)
        parts = parts + value * value
    patch_bias = down_sum(vec[0:PATCHES, 0:D])
    class_row = vec[CLS : CLS + 1, 0:D]
    rest = (patch_bias * patch_bias + class_row * class_row) * 0.125
    parts = parts + rest
    for lane in range(0, D, 128):
        wide = wide + parts[:, lane : lane + 128]
    n_x = 2 ** ((n_rep.bit_length() - 2) // 2)
    rows_x = VEC_ROWS // n_shard // n_x
    wide = wide + fold(vec[:, D:]) * (8.0 / rows_x)
    sum_squares = jnp.sum(jnp.sum(wide, axis=1, keepdims=True), axis=0, keepdims=True)
    inv_count = 1.0 / vec[used + 1 : used + 2, 0:1]
    grad_norm = jnp.sqrt(sum_squares) * inv_count
    norm_out[...] = grad_norm
    loss_out[...] = vec[used : used + 1, 0:1] * inv_count
    scale = jnp.minimum(1.0, CLIP_NORM / grad_norm) * inv_count

    def apply(array, where, grad, rate):
        refs = [buffers[3 * array + kind] for kind in range(3)]
        made = adam(refs[0][where], refs[1][where], refs[2][where], grad, scale, rate)
        for ref, value in zip(refs, made):
            ref[where] = value

    def begin(array, layer=None):
        for move in moves(array, layer):
            move.wait()

    def finish(array, layer=None):
        for move in moves(array, layer, out=True):
            move.start()

    def loop(count, body):
        def one(index, nothing):
            body(index)
            return nothing

        lax.fori_loop(0, count, one, 0)

    step = 32 if rows_in % 32 == 0 else 16
    own_rows = pl.multiple_of(shard * rows_in, 8)
    for layer in range(LAYERS):
        begin(1, layer)

        def column_of(column):
            lanes = pl.ds(pl.multiple_of(column * D, 128), D)
            for at in range(0, rows_in, step):
                if layer < keep:
                    k = 3 * (keep - 1 - layer) + jnp.where(column < 4, 2, 1)
                    row = pl.multiple_of(lax.rem(column, 4) * rows_in + at, 16)
                    grad = res[k, pl.ds(row, step), :].astype(F32)
                else:
                    grad = last_in[pl.ds(own_rows + at, step), lanes]
                apply(1, (layer, slice(at, at + step), lanes), grad, LEARNING_RATE)

        loop(8, column_of)
        finish(1, layer)
    down_rows = pl.multiple_of(shard * rows_down, 8)
    for layer in range(LAYERS):
        begin(2, layer)

        def rows_of(index):
            for half in range(2):
                at = pl.multiple_of(index * 64 + half * 32, 16)
                if layer < keep:
                    grad = res[3 * (keep - 1 - layer), pl.ds(at, 32), :].astype(F32)
                else:
                    grad = last_down[pl.ds(down_rows + at, 32), :]
                apply(2, (layer, pl.ds(at, 32), slice(0, D)), grad, LEARNING_RATE)

        loop(rows_down // 64, rows_of)
        finish(2, layer)
    begin(0)

    def patch_rows(index):
        at = pl.multiple_of(index * 32, 16)
        grad = small[1, pl.ds(at, 32), :].astype(F32)
        apply(0, (pl.ds(at, 32), slice(0, D)), grad, LEARNING_RATE)

    loop(PATCH_DIM // n_shard // 32, patch_rows)
    finish(0)
    begin(6)

    def head_rows(index):
        rows = pl.ds(pl.multiple_of(index * 16, 16), 16)
        apply(6, (rows, slice(0, NCLS)), grad_head[rows, 0:NCLS], LEARNING_RATE)

    loop(D // 16, head_rows)
    apply(6, (slice(D, D + 1), slice(0, NCLS)), grad_head[D : D + 1, 0:NCLS], LEARNING_RATE)
    finish(6)
    begin(5)
    apply(5, (slice(0, 1), slice(0, D)), class_row, VECTOR_RATE)
    for at in range(0, PATCHES, 28):
        apply(
            5, (slice(1 + at, 29 + at), slice(0, D)), vec[at : at + 28, 0:D], VECTOR_RATE
        )
    finish(5)
    begin(3)
    for layer in range(LAYERS):
        for piece in range(12):
            row = VEC_AT + 12 * layer + piece
            where = (slice(layer, layer + 1), slice(piece * D, (piece + 1) * D))
            apply(3, where, vec[row : row + 1, 0:D], VECTOR_RATE)
    finish(3)
    begin(4)
    rows = [patch_bias, class_row, vec[used - 2 : used - 1, 0:D], vec[used - 1 : used, 0:D]]
    for index, row in enumerate(rows):
        apply(4, (slice(index, index + 1), slice(0, D)), row, VECTOR_RATE)
    finish(4)
    for array, layer in order:
        for move in moves(array, layer, out=True):
            move.wait()


def run_update(n_rep, n_shard, res, small, vec, factors, arrays):
    whole = pl.BlockSpec(memory_space=pltpu.VMEM)
    there = pl.BlockSpec(memory_space=pl.ANY)
    one = jax.ShapeDtypeStruct((1, 1), F32)
    made = pl.pallas_call(
        functools.partial(update, n_rep, n_shard),
        out_shape=[one, one] + [jax.ShapeDtypeStruct(a.shape, F32) for a in arrays],
        in_specs=[whole] * 4 + [there] * 21,
        out_specs=[whole] * 2 + [there] * 21,
        scratch_shapes=[pltpu.VMEM(a.shape, F32) for a in arrays]
        + [
            pltpu.VMEM((D, 4 * D + FF), F32),
            pltpu.VMEM((FF, D), F32),
            pltpu.VMEM((D + 8, CPAD), F32),
            pltpu.SemaphoreType.DMA((21, LAYERS)),
            pltpu.SemaphoreType.DMA((21, LAYERS)),
        ],
        compiler_params=pltpu.CompilerParams(vmem_limit_bytes=62 * 1024 * 1024),
        cost_estimate=pl.CostEstimate(
            flops=200_000_000, bytes_accessed=50_000_000, transcendentals=4_000_000
        ),
        name="adamw",
    )(res, small, vec, factors, *arrays)
    return made[0].reshape(()), made[1].reshape(()), made[2:]


def shards(
    n_rep, n_shard,
    patches, labels, counts, patch_w, layer_in, layer_down, layer_vecs, glob_vecs, pos_embed, head,
    m_patch, v_patch, m_in, v_in, m_down, v_down, m_vecs, v_vecs, m_glob, v_glob, m_pos, v_pos,
    m_head, v_head,
):
    padded = jnp.pad(patches, ((0, 0), (0, BLK - PATCHES), (0, 0)))
    res, small, vec, factors = run_train(
        n_rep, n_shard, padded, labels, counts, patch_w, layer_in, layer_down, layer_vecs,
        glob_vecs, pos_embed, head,
    )
    arrays = [
        patch_w, m_patch, v_patch, layer_in, m_in, v_in, layer_down, m_down, v_down,
        layer_vecs, m_vecs, v_vecs, glob_vecs, m_glob, v_glob, pos_embed, m_pos, v_pos,
        head, m_head, v_head,
    ]
    loss, grad_norm, new = run_update(n_rep, n_shard, res, small, vec, factors, arrays)
    return (loss, grad_norm, *new)


def solution(mesh):
    everywhere = P()
    rows = P("shard", None)
    middle = P(None, "shard", None)
    return jax.shard_map(
        functools.partial(shards, mesh.shape["rep"], mesh.shape["shard"]),
        mesh=mesh,
        in_specs=(
            P(("rep", "shard"), None, None),
            P(("rep", "shard")),
            P(("rep", "shard")),
            rows,
            middle,
            middle,
            *(everywhere,) * 4,
            *(rows,) * 2,
            *(middle,) * 4,
            *(everywhere,) * 8,
        ),
        out_specs=(
            *(everywhere,) * 2,
            *(rows,) * 3,
            *(middle,) * 6,
            *(everywhere,) * 12,
        ),
        check_vma=False,
    )
```

```python
import functools

import jax
import jax.numpy as jnp
from jax import lax
from jax.experimental import pallas as pl
from jax.experimental.pallas import tpu as pltpu
from jax.sharding import PartitionSpec as P

D = 384
HEADS = 6
HEAD_DIM = 64
FF = 1536
PATCH_DIM = 768
PATCHES = 196
NCLS = 1000
LAYERS = 3
SEQ = 197

BLK = 208
CLS = 200
TAIL = 192
KEPT = 4
ROWS = KEPT * BLK
HALF = 2 * BLK
CROWS = KEPT * 16
CPAD = 1024
WIDE = 8 * D + FF

NORM_EPS = 1e-06
SMOOTHING = 0.1
CLIP_NORM = 0.05
LEARNING_RATE = 0.05
VECTOR_RATE = 0.5
BETA_FIRST = 0.9
BETA_SECOND = 0.999
ADAM_EPS = 1e-08
WEIGHT_DECAY = 0.05
ADAM_STEP = 10
GELU_SCALE = 0.7978845608028654
GELU_CUBIC = 0.044715

F32 = jnp.float32
BF = jnp.bfloat16


def mm(left, right):
    return jnp.dot(left, right, preferred_element_type=F32)


def mm_nt(left, right):
    return lax.dot_general(left, right, (((1,), (1,)), ((), ())), preferred_element_type=F32)


def mm_tn(left, right):
    return lax.dot_general(left, right, (((0,), (0,)), ((), ())), preferred_element_type=F32)


def fold(values):
    return jnp.sum(values.reshape(-1, 8, values.shape[-1]), axis=0)


def down_sum(values):
    return jnp.sum(values, axis=0, keepdims=True)


def norm(values):
    centre = values - jnp.mean(values, axis=-1, keepdims=True)
    inverse = lax.rsqrt(jnp.mean(centre * centre, axis=-1, keepdims=True) + NORM_EPS)
    return centre * inverse, inverse


def norm_back(upstream, normed, inverse, gain):
    scaled = upstream * gain
    first = jnp.mean(scaled, axis=-1, keepdims=True)
    second = jnp.mean(scaled * normed, axis=-1, keepdims=True)
    return inverse * (scaled - first - normed * second)


def gelu_parts(hidden):
    square = hidden * hidden
    tangent = jnp.tanh(hidden * (GELU_SCALE + (GELU_SCALE * GELU_CUBIC) * square))
    share = 0.5 + 0.5 * tangent
    active = hidden * share
    inner = (2.0 * GELU_SCALE) + (6.0 * GELU_SCALE * GELU_CUBIC) * square
    slope = share + active * (1.0 - share) * inner
    return active, slope


def lane_mask(width, low, high):
    lane = lax.broadcasted_iota(jnp.int32, (1, width), 1)
    return jnp.where((lane >= low) & (lane < high), 1.0, 0.0).astype(BF)


STEP = 32


def pieces(total):
    return [(at, min(STEP, total - at)) for at in range(0, total, STEP)]


WFAC = FF + 5 * D
VEC_ROWS = 256
VEC_AT = BLK
VEC_WIDE = D
MESH = pl.DeviceIdType.MESH
CHUNKS = 6


class Place:
    def __init__(self, n_rep, n_shard):
        self.n_rep, self.n_shard = n_rep, n_shard
        self.n_x = 2 ** ((n_rep.bit_length() - 2) // 2)
        self.n_z = n_rep // self.n_x
        self.n_y = n_shard // 2
        rep, shard = lax.axis_index("rep"), lax.axis_index("shard")
        self.rep, self.shard = rep, shard
        self.z, self.x = rep // self.n_x, rep % self.n_x
        self.y, self.c = shard // 2, shard % 2

    def to(self, x=None, y=None, z=None, c=None):
        x = self.x if x is None else x
        y = self.y if y is None else y
        z = self.z if z is None else z
        c = self.c if c is None else c
        return {"rep": z * self.n_x + x, "shard": y * 2 + c}


def cut(rows, parts, unit):
    return parts if rows % (parts * unit) == 0 else 1


def aligned(value, unit):
    return pl.multiple_of(value, unit)


def train(
    n_rep, n_shard,
    patches, labels, counts, own_patch, own_in, own_down, vecs, glob, pos, head,
    res_out, small_out, vec_out, square_out, all_factors,
    X, N1, I1, QKV, ATT, N2, I2, ACT, SLOPE, DXB, DMB, DA, DH,
    pix, lab, lab_given, wp, win, wdn, low_head, head_bias,
    G, RC, RY, RX, RZ, RES, GS, SC, SY, SX, SZ, SRES,
    FAC, FC, FY, FALL, V, VC, VY, VX, VZ, VF, SQ, SQZ, SQP, square_sum,
    ag_send, ag_recv, ag_local, rs_send, rs_recv, f_send, f_recv, v_send, v_recv,
    q_send, q_recv,
    img_send, img_recv, img_local, out_local,
):
    here = Place(n_rep, n_shard)
    n_x, n_y, n_z = here.n_x, here.n_y, here.n_z
    x, y, z, c = here.x, here.y, here.z, here.c
    rows_in, rows_down, rows_patch = D // n_shard, FF // n_shard, PATCH_DIM // n_shard
    block = 4 * rows_in
    mate = here.to(c=1 - c)

    def push(src, dst, send, recv, device):
        pltpu.make_async_remote_copy(
            src_ref=src, dst_ref=dst, send_sem=send, recv_sem=recv,
            device_id=device, device_id_type=MESH,
        ).start()

    def arrived(dst, recv, send):
        pltpu.make_async_remote_copy(
            src_ref=dst, dst_ref=dst, send_sem=send, recv_sem=recv,
            device_id=mate, device_id_type=MESH,
        ).wait_recv()

    def left_here(src, recv, send):
        pltpu.make_async_remote_copy(
            src_ref=src, dst_ref=src, send_sem=send, recv_sem=recv,
            device_id=mate, device_id_type=MESH,
        ).wait_send()

    sent = {}

    def go(source, dst, sems, index, device):
        name, send, recv = sems
        push(source(), dst, send.at[index], recv.at[index], device)
        sent[name, index] = (source, send, recv, index)

    def gone(sems, index):
        source, send, recv, at = sent.pop((sems[0], index))
        left_here(source(), recv.at[at], send.at[at])

    def turn(at, by, size):
        return lax.rem(at + by, size)

    barrier = pltpu.get_barrier_semaphore()
    plane = [
        (i, j, k) for i in range(n_x) for j in range(n_y) for k in range(2) if i or j or k
    ]

    def in_plane(step):
        i, j, k = step
        return here.to(x=turn(x, i, n_x), y=turn(y, j, n_y), c=lax.rem(c + k, 2))

    others = [in_plane(step) for step in plane]
    others += [here.to(z=turn(z, o, n_z)) for o in range(1, n_z)]
    for other in others:
        pl.semaphore_signal(barrier, inc=1, device_id=other, device_id_type=MESH)
    pl.semaphore_wait(barrier, len(others))

    def weight(kind, layer, shard, part=None):
        if kind == "patch":
            parts = cut(rows_patch, n_x, 16)
            rows = rows_patch // parts
            if part is None:
                return wp.at[pl.ds(aligned(shard * rows_patch, 16), rows_patch), :]
            return wp.at[pl.ds(aligned(shard * rows_patch + part * rows, 16), rows), :]
        if kind == "down":
            parts = cut(rows_down, n_x, 16)
            rows = rows_down // parts
            if part is None:
                return wdn.at[layer, pl.ds(aligned(shard * rows_down, 16), rows_down), :]
            return wdn.at[layer, pl.ds(aligned(shard * rows_down + part * rows, 16), rows), :]
        base = 0 if kind == "attn" else 4 * D
        rows = pl.ds(aligned(shard * rows_in, 16), rows_in)
        if part is None:
            return win.at[layer, rows, pl.ds(base, 4 * D)]
        wide = 4 * D // n_x
        return win.at[layer, rows, pl.ds(aligned(base + part * wide, 128), wide)]

    units = [("patch", 0)] + [
        (kind, layer) for layer in range(LAYERS) for kind in ("attn", "up", "down")
    ]

    def parts_of(kind):
        if kind == "patch":
            return cut(rows_patch, n_x, 16)
        if kind == "down":
            return cut(rows_down, n_x, 16)
        return n_x

    ag = ("ag", ag_send, ag_recv)
    base_x = n_y
    base_my = base_x + (n_y - 1) * (n_x - 1)
    base_mx = base_my + (n_y - 1)

    stage = 4 * rows_in

    def weights_copies(unit):
        kind, layer = units[unit]
        base = (unit % 2) * stage
        if kind == "patch":
            pairs = [(own_patch, X.at[pl.ds(base, rows_patch)])]
        elif kind == "down":
            pairs = [(own_down.at[layer], X.at[pl.ds(base, rows_down)])]
        else:
            start = 0 if kind == "attn" else 4 * D
            pairs = [
                (
                    own_in.at[layer, :, pl.ds(start + tile * D, D)],
                    X.at[pl.ds(base + tile * rows_in, rows_in)],
                )
                for tile in range(4)
            ]
        return [
            pltpu.make_async_copy(src, dst, ag_local.at[unit, index])
            for index, (src, dst) in enumerate(pairs)
        ]

    def weights_cast(unit):
        kind, layer = units[unit]
        base = (unit % 2) * stage
        for copy in weights_copies(unit):
            copy.wait()
        if kind == "patch":
            rows = pl.ds(aligned(here.shard * rows_patch, 16), rows_patch)
            wp[rows, :] = X[base : base + rows_patch, :].astype(BF)
        elif kind == "down":
            rows = pl.ds(aligned(here.shard * rows_down, 16), rows_down)
            wdn[layer, rows, :] = X[base : base + rows_down, :].astype(BF)
        else:
            start = 0 if kind == "attn" else 4 * D
            rows = pl.ds(aligned(here.shard * rows_in, 16), rows_in)
            for tile in range(4):
                win[layer, rows, start + tile * D : start + (tile + 1) * D] = X[
                    base + tile * rows_in : base + (tile + 1) * rows_in, :
                ].astype(BF)
        if unit + 2 < len(units):
            for copy in weights_copies(unit + 2):
                copy.start()

    def weights_start(unit):
        kind, layer = units[unit]
        part = x if parts_of(kind) > 1 else 0
        for o in range(1, n_y):
            go(
                lambda: weight(kind, layer, here.shard, part),
                weight(kind, layer, here.shard, part), ag, (unit, o),
                here.to(y=turn(y, o, n_y)),
            )
        go(
            lambda: weight(kind, layer, here.shard), weight(kind, layer, here.shard), ag,
            (unit, 0), mate,
        )

    def weights_forward(unit):
        kind, layer = units[unit]
        split = parts_of(kind) > 1
        part = x if split else 0
        for o in range(1, n_y):
            def make(o=o):
                return weight(kind, layer, turn(y, n_y - o, n_y) * 2 + c, part)

            arrived(make(), ag_recv.at[unit, o], ag_send.at[unit, o])
            if split:
                for p in range(1, n_x):
                    index = base_x + (o - 1) * (n_x - 1) + p - 1
                    go(make, make(), ag, (unit, index), here.to(x=turn(x, p, n_x)))
            go(make, make(), ag, (unit, base_my + o - 1), mate)

    def weights_ready(unit):
        kind, layer = units[unit]
        split = parts_of(kind) > 1
        part = x if split else 0
        if split:
            for o in range(1, n_y):
                for p in range(1, n_x):
                    index = (o - 1) * (n_x - 1) + p - 1

                    def make(o=o, p=p):
                        shard = turn(y, n_y - o, n_y) * 2 + c
                        return weight(kind, layer, shard, turn(x, n_x - p, n_x))

                    arrived(
                        make(), ag_recv.at[unit, base_x + index], ag_send.at[unit, base_x + index]
                    )
                    go(make, make(), ag, (unit, base_mx + index), mate)
        arrived(weight(kind, layer, y * 2 + 1 - c), ag_recv.at[unit, 0], ag_send.at[unit, 0])
        for o in range(1, n_y):
            shard = turn(y, n_y - o, n_y) * 2 + 1 - c
            index = base_my + o - 1
            arrived(weight(kind, layer, shard, part), ag_recv.at[unit, index], ag_send.at[unit, index])
            if split:
                for p in range(1, n_x):
                    index = base_mx + (o - 1) * (n_x - 1) + p - 1
                    piece = weight(kind, layer, shard, turn(x, n_x - p, n_x))
                    arrived(piece, ag_recv.at[unit, index], ag_send.at[unit, index])

    lower = here.rep < n_rep // 2
    partner = here.to(z=turn(z, n_z // 2, n_z))
    back_half = pix.at[pl.ds(2, 2)]
    given = patches.at[pl.ds(KEPT, 2)]

    def local_half(half):
        return pltpu.make_async_copy(
            patches.at[pl.ds(2 * half, 2)], pix.at[pl.ds(2 * half, 2)], img_local.at[half]
        )

    def marks(pair):
        row = lax.broadcasted_iota(jnp.int32, (32, 128), 0)
        found = jnp.full((32, 128), -1.0, F32)
        for index in range(2):
            slot = 2 * pair + index
            value = jnp.where(slot < counts[0], labels[slot], -1).astype(F32)
            found = jnp.where(row == CLS - TAIL + 16 * index, value, found)
        return found

    local_half(0).start()
    for unit in range(2):
        for copy in weights_copies(unit):
            copy.start()
    lab[0] = marks(0)
    lab_given[...] = marks(2)

    @pl.when(jnp.logical_not(lower))
    def _():
        push(given, back_half, img_send.at[0], img_recv.at[0], partner)
        push(lab_given, lab.at[1], img_send.at[1], img_recv.at[1], partner)
        local_half(1).start()
        lab[1] = marks(1)

    for unit in range(4):
        weights_cast(unit)
        weights_start(unit)
    weights_forward(0)
    for unit in range(4, len(units)):
        weights_cast(unit)

    even = lane_mask(128, 0, 64)
    odd = lane_mask(128, 64, 128)
    low_lane = lax.broadcasted_iota(jnp.int32, (1, 128), 1) < 64
    key_lane = lax.broadcasted_iota(jnp.int32, (1, BLK), 1)
    key_row = jnp.where((key_lane < PATCHES) | (key_lane == CLS), 0.0, -1e30)
    key_sub = lax.broadcasted_iota(jnp.int32, (BLK, 1), 0)
    key_column = jnp.where((key_sub < PATCHES) | (key_sub == CLS), 0.0, -1e30)
    whole_lanes = NCLS // 128 * 128
    low_head[:, 0:whole_lanes] = head[0:D, 0:whole_lanes].astype(BF)
    low_head[:, whole_lanes:] = jnp.zeros((D, CPAD - whole_lanes), BF)
    low_head[:, whole_lanes:NCLS] = head[0:D, whole_lanes:NCLS].astype(BF)
    head_bias[...] = jnp.zeros((1, CPAD), F32)
    head_bias[:, 0:NCLS] = head[D : D + 1, :]
    V[...] = jnp.zeros((VEC_ROWS, VEC_WIDE), F32)
    square_sum[...] = jnp.zeros((8, 128), F32)
    zeros = jnp.zeros((8, D), F32)
    patch_bias = glob[0:1, :]

    def whole_lanes_of(tile):
        return jnp.concatenate([tile] * (D // 128), axis=1)

    def vector(layer, at, size):
        return vecs[pl.ds(layer, 1), at : at + size]

    def store_vector(layer, at, row):
        for piece in range(row.shape[-1] // D):
            V[pl.ds(VEC_AT + 12 * layer + at // D + piece, 1), 0:D] = row[
                :, piece * D : (piece + 1) * D
            ]

    def store_sums(layer, parts):
        for at, part in parts:
            store_vector(layer, at, down_sum(part))

    def embed(half):
        made = mm(pix[pl.ds(2 * half, 2)].reshape(HALF, PATCH_DIM), wp[...])
        for image in range(2):
            start = aligned(half * HALF + image * BLK, 16)
            for at, size in pieces(PATCHES - 4):
                X[pl.ds(start + at, size), :] = (
                    made[image * BLK + at : image * BLK + at + size]
                    + pos[1 + at : 1 + at + size, :]
                    + patch_bias
                )
            X[pl.ds(start + TAIL, 16), :] = jnp.zeros((16, D), F32)
            X[pl.ds(start + TAIL, 4), :] = (
                made[image * BLK + TAIL : image * BLK + PATCHES]
                + pos[1 + TAIL : 1 + PATCHES, :]
                + patch_bias
            )
            X[pl.ds(start + CLS, 1), :] = glob[1:2, :] + pos[0:1, :]

    def first_norm(layer, half, columns):
        base = half * HALF
        gain, shift = vector(layer, 0, D), vector(layer, D, D)
        for at, size in pieces(HALF):
            rows = pl.ds(aligned(base + at, 16), size)
            normed, inverse = norm(X[rows, :])
            N1[layer, rows, :] = normed.astype(BF)
            I1[layer, rows, :] = jnp.broadcast_to(inverse, (size, 128))
            DXB[rows, :] = (normed * gain + shift).astype(BF)
        rows = pl.ds(aligned(base, 16), HALF)
        h1 = DXB[rows, :]
        for tile in columns:
            made = mm(h1, win[layer, :, tile * D : (tile + 1) * D])
            if tile == 0:
                made = made + vector(layer, 2 * D, D)
            if tile == 2:
                made = made + vector(layer, 3 * D, D)
            if len(columns) == 3:
                QKV[layer, rows, tile * D : (tile + 1) * D] = made.astype(BF)
            else:
                (DMB if tile == 1 else DA)[rows, :] = made.astype(BF)

    ones = jnp.full((BLK, 128), 1.0, BF)

    def attend(layer, image):
        rows = pl.ds(aligned(image * BLK, 16), BLK)
        for pair in range(3):
            at = pair * 128
            query = QKV[layer, rows, at : at + 128] * BF(0.125)
            keys = QKV[layer, rows, D + at : D + at + 128]
            values = QKV[layer, rows, 2 * D + at : 2 * D + at + 128]
            both = jnp.concatenate([query * even, query * odd], axis=0)
            scores = mm_nt(both, keys)
            probs = []
            for row, size in pieces(HALF):
                part = scores[row : row + size] + key_row
                probs.append(jnp.exp(part - jnp.max(part, axis=-1, keepdims=True)).astype(BF))
            probs = jnp.concatenate(probs, axis=0)
            first = mm(probs[:BLK], jnp.concatenate([values * even, ones], axis=1))
            second = mm(probs[BLK:], jnp.concatenate([values * odd, ones], axis=1))
            made = first[:, :128] * (1.0 / first[:, 128:])
            made = made + second[:, :128] * (1.0 / second[:, 128:])
            ATT[layer, rows, at : at + 128] = made.astype(BF)

    def mlp(layer, half):
        base = half * HALF
        whole = pl.ds(aligned(base, 16), HALF)
        made = mm(ATT[layer, whole, :], win[layer, :, 3 * D : 4 * D])
        bias_out = vector(layer, 4 * D, D)
        gain, shift = vector(layer, 5 * D, D), vector(layer, 6 * D, D)
        for at, size in pieces(HALF):
            rows = pl.ds(aligned(base + at, 16), size)
            middle = X[rows, :] + made[at : at + size] + bias_out
            X[rows, :] = middle
            normed, inverse = norm(middle)
            N2[layer, rows, :] = normed.astype(BF)
            I2[layer, rows, :] = jnp.broadcast_to(inverse, (size, 128))
            DXB[rows, :] = (normed * gain + shift).astype(BF)
        h2 = DXB[whole, :]
        for tile in range(4):
            columns = slice(tile * D, (tile + 1) * D)
            made = mm(h2, win[layer, :, (4 + tile) * D : (5 + tile) * D])
            bias = vector(layer, 7 * D + tile * D, D)
            for at, size in pieces(HALF):
                rows = pl.ds(aligned(base + at, 16), size)
                active, slope = gelu_parts(made[at : at + size] + bias)
                ACT[layer, rows, columns] = active.astype(BF)
                SLOPE[layer, rows, columns] = slope.astype(BF)
        made = mm(ACT[layer, whole, :], wdn[layer])
        bias = vector(layer, 7 * D + FF, D)
        for at, size in pieces(HALF):
            rows = pl.ds(aligned(base + at, 16), size)
            X[rows, :] = X[rows, :] + made[at : at + size] + bias

    def when(condition, *steps):
        @pl.when(condition)
        def _():
            for step, unit in steps:
                step(unit)

    weights_ready(0)

    def forward_half(half, carry):
        start = half == 0

        @pl.when(start)
        def _():
            local_half(0).wait()

        @pl.when(jnp.logical_and(half == 1, lower))
        def _():
            arrived(back_half, img_recv.at[0], img_send.at[0])

        @pl.when(jnp.logical_and(half == 1, jnp.logical_not(lower)))
        def _():
            local_half(1).wait()

        embed(half)

        def forward_layer(layer, inner):
            first = jnp.logical_and(start, layer == 0)
            second = jnp.logical_and(start, layer == 1)
            when(first, (weights_forward, 1), (weights_start, 4), (weights_ready, 1))
            when(second, (weights_ready, 4))
            first_norm(layer, half, (0, 1, 2))
            when(first, (weights_forward, 2), (weights_start, 5))
            when(second, (weights_forward, 6), (weights_start, 9))

            def attend_one(index, nothing):
                attend(layer, 2 * half + index)
                begin = index == 0
                when(
                    jnp.logical_and(first, begin), (weights_forward, 3), (weights_start, 6)
                )
                when(jnp.logical_and(second, begin), (weights_forward, 7))
                return nothing

            lax.fori_loop(0, 2, attend_one, 0)
            when(
                first, (weights_forward, 4), (weights_start, 7), (weights_ready, 2),
                (weights_ready, 3),
            )
            when(second, (weights_forward, 8), (weights_ready, 5), (weights_ready, 6))
            mlp(layer, half)
            when(first, (weights_forward, 5), (weights_start, 8))
            when(second, (weights_forward, 9))
            return inner

        return lax.fori_loop(0, LAYERS - 1, forward_layer, carry)

    lax.fori_loop(0, 2, forward_half, 0)
    for unit in (7, 8, 9):
        weights_ready(unit)

    last = LAYERS - 1

    def last_norm(half, nothing):
        first_norm(last, half, (1, 2))
        return nothing

    lax.fori_loop(0, 2, last_norm, 0)

    fac = ("f", f_send, f_recv)
    f_y, f_x = 1, n_y
    f_z = f_x + n_x - 1
    f_m = f_z + n_z - 1
    group = KEPT * n_shard

    def factors_core():
        go(lambda: FAC.at[1 - c], FC, fac, 0, mate)

    def factors_y():
        arrived(FC, f_recv.at[0], f_send.at[0])
        FAC[c] = FAC[c] + FC[...]
        for o in range(1, n_y):
            go(lambda: FAC.at[c], FY.at[o - 1], fac, f_y + o - 1, here.to(y=turn(y, o, n_y)))

    def factors_x():
        total = FAC[c]
        for o in range(1, n_y):
            arrived(FY.at[o - 1], f_recv.at[f_y + o - 1], f_send.at[f_y + o - 1])
            total = total + FY[o - 1]
        FALL[x] = total
        for o in range(1, n_x):
            go(lambda: FALL.at[x], FALL.at[x], fac, f_x + o - 1, here.to(x=turn(x, o, n_x)))

    def all_rows(at):
        return all_factors.at[c, pl.ds(at * n_x, n_x)]

    def factors_z():
        for o in range(1, n_x):
            index = f_x + o - 1
            arrived(FALL.at[turn(x, n_x - o, n_x)], f_recv.at[index], f_send.at[index])
        pltpu.make_async_copy(FALL, all_rows(z), out_local.at[0]).start()
        for o in range(1, n_z):
            go(lambda: FALL, all_rows(z), fac, f_z + o - 1, here.to(z=turn(z, o, n_z)))

    def factors_mate():
        for o in range(1, n_z):
            index = f_z + o - 1
            arrived(all_rows(turn(z, n_z - o, n_z)), f_recv.at[index], f_send.at[index])
        pltpu.make_async_copy(FALL, all_rows(z), out_local.at[0]).wait()
        go(lambda: all_factors.at[c], all_factors.at[c], fac, f_m, mate)

    def factors_done():
        arrived(all_factors.at[1 - c], f_recv.at[f_m], f_send.at[f_m])

    rs = ("rs", rs_send, rs_recv)
    r_y, r_x = 1, n_y
    r_z = r_x + n_x - 1
    r_gz = r_z + n_z - 1
    r_gx = r_gz + n_z - 1

    def chunk(k):
        if k < CHUNKS:
            slot = k % 3
            return (
                G.at[k], RC.at[slot], RY.at[slot], RX.at[slot], RZ.at[slot], RES.at[k], block
            )
        k = k - CHUNKS
        return GS.at[k], SC.at[0], SY.at[0], SX.at[0], SZ.at[0], SRES.at[k], block // 2

    def splits(rows):
        by_x = cut(rows, n_x, 16)
        by_z = cut(rows // by_x, n_z, 16)
        return by_x, rows // by_x, by_z, rows // by_x // by_z

    def add_rows(rows, target, target_at, sources):
        step = 48 if rows % 48 == 0 else 16

        def one(index, nothing):
            at = index * step
            to = pl.ds(aligned(target_at + at, 16), step)
            total = target[to, :]
            if len(sources) == 1:
                total = total + sources[0][pl.ds(aligned(at, 16), step), :]
            else:
                total = total.astype(F32)
                for source in sources:
                    total = total + source[pl.ds(aligned(at, 16), step), :].astype(F32)
                total = total.astype(BF)
            target[to, :] = total
            return nothing

        lax.fori_loop(0, rows // step, one, 0)

    def reduce_core(k):
        g, rc = chunk(k)[0:2]
        go(lambda: chunk(k)[0].at[:, 1 - c], rc, rs, (k, 0), mate)

    def reduce_y(k):
        g, rc, ry, _, _, _, rows = chunk(k)
        arrived(rc, rs_recv.at[k, 0], rs_send.at[k, 0])
        for o in list(range(1, n_y)) + [0]:
            at = turn(y, o, n_y)
            add_rows(rows, g.at[at, c], 0, [rc.at[at]])
            if o:
                go(
                    lambda o=o: chunk(k)[0].at[turn(y, o, n_y), c], ry.at[o - 1], rs,
                    (k, r_y + o - 1), here.to(y=at),
                )

    def total_of(slots, count, at, step):
        total = None
        for index in range(count):
            value = slots[index, pl.ds(aligned(at, 16), step), :].astype(F32)
            total = value if total is None else total + value
        return total

    def reduce_x(k):
        g, _, ry, rx, _, _, rows = chunk(k)
        by_x, rows_x = splits(rows)[0:2]
        for o in range(1, n_y):
            arrived(ry.at[o - 1], rs_recv.at[k, r_y + o - 1], rs_send.at[k, r_y + o - 1])
        mine = g.at[y, c]
        add_rows(rows, mine, 0, [ry.at[o - 1] for o in range(1, n_y)])
        for o in range(1, n_x):
            to = turn(x, o, n_x)
            if by_x > 1:

                def make(o=o):
                    at = turn(x, o, n_x) * rows_x
                    return chunk(k)[0].at[y, c, pl.ds(aligned(at, 16), rows_x), :]

                go(make, rx.at[o - 1], rs, (k, r_x + o - 1), here.to(x=to))
            else:
                go(lambda: chunk(k)[0].at[y, c], rx.at[x], rs, (k, r_x + o - 1), here.to(x=to))

    def reduce_z(k):
        g, _, _, rx, rz, _, rows = chunk(k)
        by_x, rows_x, by_z, rows_z = splits(rows)
        mine = g.at[y, c]
        for o in range(1, n_x):
            slot = rx.at[o - 1] if by_x > 1 else rx.at[turn(x, n_x - o, n_x)]
            arrived(slot, rs_recv.at[k, r_x + o - 1], rs_send.at[k, r_x + o - 1])
        if by_x > 1:
            start = x * rows_x
            add_rows(rows_x, mine, start, [rx.at[o - 1] for o in range(1, n_x)])
        else:
            start = 0
            rx[x] = mine[...]
            for o in range(1, n_x):
                gone(rs, (k, r_x + o - 1))
            step = 48 if rows % 48 == 0 else 16

            def one(index, nothing):
                at = pl.ds(aligned(index * step, 16), step)
                g[y, c, at, :] = total_of(rx, n_x, index * step, step).astype(BF)
                return nothing

            lax.fori_loop(0, rows // step, one, 0)
        for o in range(1, n_z):

            def make(o=o):
                at = x * rows_x if by_x > 1 else 0
                if by_z > 1:
                    at = at + turn(z, o, n_z) * rows_z
                return chunk(k)[0].at[y, c, pl.ds(aligned(at, 16), rows_z), :]

            slot = rz.at[o - 1] if by_z > 1 else rz.at[z]
            go(make, slot, rs, (k, r_z + o - 1), here.to(z=turn(z, o, n_z)))

    def gather_z(k):
        g, _, _, _, rz, res, rows = chunk(k)
        by_x, rows_x, by_z, rows_z = splits(rows)
        start = x * rows_x if by_x > 1 else 0
        if by_z > 1:
            start = start + z * rows_z
        for o in range(1, n_z):
            slot = rz.at[o - 1] if by_z > 1 else rz.at[turn(z, n_z - o, n_z)]
            arrived(slot, rs_recv.at[k, r_z + o - 1], rs_send.at[k, r_z + o - 1])
        own_slot = n_z - 1 if by_z > 1 else z
        rz[own_slot] = g[y, c, pl.ds(aligned(start, 16), rows_z), :]
        share = 1.0 / ((1 if by_x > 1 else n_x) * (1 if by_z > 1 else n_z))
        step = 48 if rows_z % 48 == 0 else 16

        def one(index, total):
            low = total_of(rz, n_z, index * step, step).astype(BF)
            res[pl.ds(aligned(start + index * step, 16), step), :] = low
            wide = low.astype(F32)
            return total + fold(wide * wide)

        total = lax.fori_loop(0, rows_z // step, one, zeros) * share
        for at in range(0, D, 128):
            square_sum[...] = square_sum[...] + total[:, at : at + 128]
        if by_z > 1:

            def make():
                at = x * rows_x if by_x > 1 else 0
                return chunk(k)[5].at[pl.ds(aligned(at + z * rows_z, 16), rows_z), :]

            for o in range(1, n_z):
                go(make, make(), rs, (k, r_gz + o - 1), here.to(z=turn(z, o, n_z)))

    def gather_x(k):
        res, rows = chunk(k)[5:7]
        by_x, rows_x, by_z, rows_z = splits(rows)
        if by_z > 1:
            for o in range(1, n_z):
                start = turn(z, n_z - o, n_z) * rows_z
                if by_x > 1:
                    start = start + x * rows_x
                arrived(
                    res.at[pl.ds(aligned(start, 16), rows_z), :],
                    rs_recv.at[k, r_gz + o - 1], rs_send.at[k, r_gz + o - 1],
                )
        if by_x > 1:

            def make():
                return chunk(k)[5].at[pl.ds(aligned(x * rows_x, 16), rows_x), :]

            for o in range(1, n_x):
                go(make, make(), rs, (k, r_gx + o - 1), here.to(x=turn(x, o, n_x)))

    def result(k):
        if k < CHUNKS:
            return pltpu.make_async_copy(RES.at[k], res_out.at[k], out_local.at[1 + k])
        return pltpu.make_async_copy(
            SRES.at[k - CHUNKS], small_out.at[k - CHUNKS], out_local.at[1 + k]
        )

    def gather_done(k):
        res, rows = chunk(k)[5:7]
        by_x, rows_x = splits(rows)[0:2]
        if by_x > 1:
            for o in range(1, n_x):
                start = turn(x, n_x - o, n_x) * rows_x
                arrived(
                    res.at[pl.ds(aligned(start, 16), rows_x), :],
                    rs_recv.at[k, r_gx + o - 1], rs_send.at[k, r_gx + o - 1],
                )
        result(k).start()

    def tails(ref, layer=None):
        found = []
        for image in range(KEPT):
            rows = slice(image * BLK + TAIL, (image + 1) * BLK)
            found.append(ref[rows, :] if layer is None else ref[layer, rows, :])
        return jnp.concatenate(found, axis=0)

    @pl.when(lower)
    def _():
        arrived(lab.at[1], img_recv.at[1], img_send.at[1])

    marked = lab[...].reshape(CROWS, 128)[:, 0:1]

    h1 = tails(DXB)
    stream = tails(X)
    query = ((mm(h1, win[last, :, 0:D]) + vector(last, 2 * D, D)).astype(BF)) * BF(0.125)
    head_masks = [lane_mask(D, index * 64, (index + 1) * 64) for index in range(HEADS)]

    def spread(values):
        return jnp.concatenate([values * mask for mask in head_masks], axis=0)

    def gather_heads(values):
        total = None
        for index in range(HEADS):
            part = values[index * 16 : (index + 1) * 16] * head_masks[index].astype(F32)
            total = part if total is None else total + part
        return total

    spread_queries, probabilities, outs = [], [], []
    for image in range(KEPT):
        rows = slice(image * BLK, (image + 1) * BLK)
        queries = spread(query[image * 16 : (image + 1) * 16])
        scores = mm_nt(queries, DMB[rows, :]) + key_row
        raw = jnp.exp(scores - jnp.max(scores, axis=-1, keepdims=True))
        probs = raw * (1.0 / jnp.sum(raw, axis=-1, keepdims=True))
        spread_queries.append(queries)
        probabilities.append(probs)
        outs.append(gather_heads(mm(probs.astype(BF), DA[rows, :])))
    attended = jnp.concatenate(outs, axis=0).astype(BF)
    middle = stream + mm(attended, win[last, :, 3 * D : 4 * D]) + vector(last, 4 * D, D)
    n2, i2 = norm(middle)
    h2 = (n2 * vector(last, 5 * D, D) + vector(last, 6 * D, D)).astype(BF)
    active, slope = gelu_parts(mm(h2, win[last, :, 4 * D :]) + vector(last, 7 * D, FF))
    active = active.astype(BF)
    top = middle + mm(active, wdn[last]) + vector(last, 7 * D + FF, D)
    gain_final = glob[2:3, :]
    nf, inf = norm(top)
    final = (nf * gain_final + glob[3:4, :]).astype(BF)
    class_lane = lax.broadcasted_iota(jnp.int32, (1, CPAD), 1)
    logits = mm(final, low_head[...]) + head_bias[...]
    logits = jnp.where(class_lane < NCLS, logits, -1e30)
    peak = jnp.max(logits, axis=-1, keepdims=True)
    shifted = logits - peak
    raw = jnp.exp(shifted)
    total = jnp.sum(raw, axis=-1, keepdims=True)
    alive = jnp.where(marked >= 0.0, 1.0, 0.0)
    target = jnp.where(class_lane.astype(F32) == marked, 1.0 - SMOOTHING, 0.0) + jnp.where(
        class_lane < NCLS, SMOOTHING / NCLS, 0.0
    )
    log_probs = jnp.where(class_lane < NCLS, shifted - jnp.log(total), 0.0)
    losses = -jnp.sum(target * log_probs, axis=-1, keepdims=True) * alive
    d_logits = ((raw * (1.0 / total) - target) * alive).astype(BF)
    d_final = mm_nt(d_logits, low_head[...])
    last_row = VEC_AT + 12 * LAYERS
    V[last_row : last_row + 1, 0:D] = down_sum(d_final * nf)
    V[last_row + 1 : last_row + 2, 0:D] = down_sum(d_final)
    V[last_row + 2 : last_row + 3, 0:128] = jnp.broadcast_to(down_sum(losses), (1, 128))
    V[last_row + 3 : last_row + 4, 0:128] = jnp.full((1, 128), counts[0].astype(F32), F32)
    d_top = norm_back(d_final, nf, inf, gain_final)
    low_top = d_top.astype(BF)
    store_vector(last, 7 * D + FF, down_sum(d_top))
    d_up = (mm_nt(low_top, wdn[last]) * slope).astype(BF)
    store_vector(last, 7 * D, down_sum(d_up.astype(F32)))
    d_h2 = mm_nt(d_up, win[last, :, 4 * D :])
    store_vector(last, 5 * D, down_sum(d_h2 * n2))
    store_vector(last, 6 * D, down_sum(d_h2))
    d_middle = d_top + norm_back(d_h2, n2, i2, vector(last, 5 * D, D))
    low_middle = d_middle.astype(BF)
    store_vector(last, 4 * D, down_sum(d_middle))
    d_heads = mm_nt(low_middle, win[last, :, 3 * D : 4 * D]).astype(BF)
    d_queries = []
    for image in range(KEPT):
        rows = slice(image * BLK, (image + 1) * BLK)
        ups = spread(d_heads[image * 16 : (image + 1) * 16])
        probs = probabilities[image]
        d_probs = mm_nt(ups, DA[rows, :])
        inner = jnp.sum(d_probs * probs, axis=-1, keepdims=True)
        d_scores = (probs * (d_probs - inner)).astype(BF)
        d_queries.append(gather_heads(mm(d_scores, DMB[rows, :])) * 0.125)
        DMB[rows, :] = mm_tn(d_scores, spread_queries[image]).astype(BF)
        DA[rows, :] = mm_tn(probs.astype(BF), ups).astype(BF)
    d_query = jnp.concatenate(d_queries, axis=0).astype(BF)
    store_vector(last, 2 * D, down_sum(d_query.astype(F32)))
    from_query = mm_nt(d_query, win[last, :, 0:D])

    pick_row = lax.broadcasted_iota(jnp.int32, (group, CROWS), 0)
    pick_lane = lax.broadcasted_iota(jnp.int32, (group, CROWS), 1)
    pick = jnp.where(
        ((pick_row - KEPT * here.shard) * 16 + (CLS - TAIL)) == pick_lane, 1.0, 0.0
    ).astype(BF)
    at = 0
    for piece in (active, h2, attended, h1, final, low_top):
        FAC[0, :, at : at + piece.shape[-1]] = mm(pick, piece).astype(BF)
        at += piece.shape[-1]
    at = 0
    for piece in (d_up, low_middle, d_query, d_logits):
        FAC[1, :, at : at + piece.shape[-1]] = mm(pick, piece).astype(BF)
        at += piece.shape[-1]
    FAC[1, :, at:] = jnp.zeros((group, WFAC - at), BF)
    factors_core()

    turned = DXB[...].T
    for tile, grads in enumerate((DMB, DA)):
        made = mm(turned, grads[...]).astype(BF)
        for shard in range(n_shard):
            GS[0, shard // 2, shard % 2, tile * rows_in : (tile + 1) * rows_in, :] = made[
                shard * rows_in : (shard + 1) * rows_in
            ]
    reduce_core(CHUNKS)
    factors_y()
    store_sums(last, [(3 * D, fold(DA[...].astype(F32)))])

    X[...] = jnp.zeros((ROWS, D), F32)
    gain = vector(last, 0, D)
    gain_sum, shift_sum = zeros, zeros
    for image in range(KEPT):
        rows = slice(image * BLK + TAIL, (image + 1) * BLK)
        part = from_query[image * 16 : (image + 1) * 16]
        normed = N1[last, rows, :].astype(F32)
        gain_sum = gain_sum + fold(part * normed)
        shift_sum = shift_sum + fold(part)
        X[rows, :] = d_middle[image * 16 : (image + 1) * 16] + norm_back(
            part, normed, whole_lanes_of(I1[last, rows, :]), gain
        )

    def first_back(layer, half, made, sums):
        base = half * HALF
        gain = vector(layer, 0, D)
        gain_sum, shift_sum = sums
        for at, size in pieces(HALF):
            rows = pl.ds(aligned(base + at, 16), size)
            part = made[at : at + size]
            normed = N1[layer, rows, :].astype(F32)
            inverse = whole_lanes_of(I1[layer, rows, :])
            gain_sum = gain_sum + fold(part * normed)
            shift_sum = shift_sum + fold(part)
            X[rows, :] = X[rows, :] + norm_back(part, normed, inverse, gain)
        return gain_sum, shift_sum

    def last_back(half, sums):
        rows = pl.ds(aligned(half * HALF, 16), HALF)
        made = mm_nt(DMB[rows, :], win[last, :, D : 2 * D])
        made = made + mm_nt(DA[rows, :], win[last, :, 2 * D : 3 * D])
        return first_back(last, half, made, sums)

    gain_sum, shift_sum = lax.fori_loop(0, 2, last_back, (gain_sum, shift_sum))
    store_sums(last, [(0, gain_sum), (D, shift_sum)])
    reduce_y(CHUNKS)
    factors_x()

    def round_up(half, total):
        for at, size in pieces(HALF):
            rows = pl.ds(aligned(half * HALF + at, 16), size)
            up = X[rows, :]
            DXB[rows, :] = up.astype(BF)
            total = total + fold(up)
        return total

    def act_back(layer, half, totals):
        base = half * HALF
        low = DXB[pl.ds(aligned(base, 16), HALF), :]
        ups = []
        for tile in range(4):
            columns = slice(tile * D, (tile + 1) * D)
            made = mm_nt(low, wdn[layer, columns, :])
            total = totals[tile]
            for at, size in pieces(HALF):
                rows = pl.ds(aligned(base + at, 16), size)
                grad = (made[at : at + size] * SLOPE[layer, rows, columns].astype(F32)).astype(BF)
                DH[rows, columns] = grad
                total = total + fold(grad.astype(F32))
            ups.append(total)
        return tuple(ups)

    def mlp_back(layer, half, sums):
        base = half * HALF
        whole = pl.ds(aligned(base, 16), HALF)
        gain_sum, shift_sum, bias_out = sums
        made = mm_nt(DH[whole, :], win[layer, :, 4 * D :])
        gain = vector(layer, 5 * D, D)
        for at, size in pieces(HALF):
            rows = pl.ds(aligned(base + at, 16), size)
            part = made[at : at + size]
            normed = N2[layer, rows, :].astype(F32)
            inverse = whole_lanes_of(I2[layer, rows, :])
            gain_sum = gain_sum + fold(part * normed)
            shift_sum = shift_sum + fold(part)
            grad = X[rows, :] + norm_back(part, normed, inverse, gain)
            X[rows, :] = grad
            DMB[rows, :] = grad.astype(BF)
            bias_out = bias_out + fold(grad)
        DA[whole, :] = mm_nt(DMB[whole, :], win[layer, :, 3 * D : 4 * D]).astype(BF)
        return gain_sum, shift_sum, bias_out

    def attend_back(layer, image):
        rows = pl.ds(aligned(image * BLK, 16), BLK)
        for pair in range(3):
            at = pair * 128
            query = QKV[layer, rows, at : at + 128] * BF(0.125)
            keys = QKV[layer, rows, D + at : D + at + 128]
            values = QKV[layer, rows, 2 * D + at : 2 * D + at + 128]
            ups = DA[rows, at : at + 128]
            keys_both = jnp.concatenate([keys * even, keys * odd], axis=0)
            values_both = jnp.concatenate([values * even, values * odd], axis=0)
            scores = mm_nt(keys_both, query)
            d_probs = mm_nt(values_both, ups)
            probs, d_scores = [], []
            for base in (0, BLK):
                low_probs, low_grads = [], []
                for first, end in ((0, 128), (128, BLK)):
                    part = jnp.concatenate(
                        [
                            scores[base : base + TAIL, first:end],
                            scores[base + TAIL : base + BLK, first:end] + key_column[TAIL:],
                        ],
                        axis=0,
                    )
                    raw = jnp.exp(part - jnp.max(part, axis=0, keepdims=True))
                    prob = raw * (1.0 / jnp.sum(raw, axis=0, keepdims=True))
                    grad = d_probs[base : base + BLK, first:end]
                    inner = jnp.sum(grad * prob, axis=0, keepdims=True)
                    low_grads.append((prob * (grad - inner)).astype(BF))
                    low_probs.append(prob.astype(BF))
                probs.append(jnp.concatenate(low_probs, axis=1))
                d_scores.append(jnp.concatenate(low_grads, axis=1))
            probs = jnp.concatenate(probs, axis=0)
            d_scores = jnp.concatenate(d_scores, axis=0)
            d_values = mm(probs, ups)
            d_keys = mm(d_scores, query)
            d_query = mm_tn(d_scores, keys_both) * 0.125
            DH[rows, at : at + 128] = d_query.astype(BF)
            DH[rows, D + at : D + at + 128] = jnp.where(
                low_lane, d_keys[:BLK], d_keys[BLK:]
            ).astype(BF)
            DH[rows, 2 * D + at : 2 * D + at + 128] = jnp.where(
                low_lane, d_values[:BLK], d_values[BLK:]
            ).astype(BF)

    def renew(ref, layer, at):
        gain, shift = vector(layer, at, D), vector(layer, at + D, D)

        def one(index, nothing):
            rows = pl.ds(aligned(index * 64, 16), 64)
            DXB[rows, :] = (ref[layer, rows, :].astype(F32) * gain + shift).astype(BF)
            return nothing

        lax.fori_loop(0, ROWS // 64, one, 0)
        return DXB[...].T

    def keep_in(k, tile, made):
        for shard in range(n_shard):
            G[k, shard // 2, shard % 2, tile * rows_in : (tile + 1) * rows_in, :] = made[
                shard * rows_in : (shard + 1) * rows_in
            ]

    def backward(step, carry):
        layer = LAYERS - 2 - step
        kd, ku, kq = 3 * step, 3 * step + 1, 3 * step + 2
        upper_layer, bottom = step == 0, step == 1

        bias_down = lax.fori_loop(0, 2, round_up, zeros)
        when(upper_layer, (reduce_x, CHUNKS))

        @pl.when(upper_layer)
        def _():
            factors_z()

        turned = DXB[...].T
        per = min(rows_down, D)
        for tile in range(4):
            columns = slice(tile * D, (tile + 1) * D)
            made = mm(turned, ACT[layer, :, columns]).astype(BF).T
            for piece in range(D // per):
                shard, at = divmod(tile * D + piece * per, rows_down)
                G[kd, shard // 2, shard % 2, at : at + per, :] = made[
                    piece * per : (piece + 1) * per
                ]
        when(upper_layer, (reduce_core, 0))
        when(bottom, (reduce_core, 3), (gather_z, CHUNKS))

        def one(half, totals):
            return act_back(layer, half, totals)

        bias_up = lax.fori_loop(0, 2, one, (zeros,) * 4)
        when(upper_layer, (reduce_y, 0))
        when(bottom, (reduce_x, 2), (reduce_y, 3), (reduce_z, 1))
        turned = renew(N2, layer, 5 * D)
        for tile in range(4):
            keep_in(ku, tile, mm(turned, DH[:, tile * D : (tile + 1) * D]).astype(BF))
        when(upper_layer, (reduce_core, 1))
        when(bottom, (reduce_core, 4), (gather_z, 0), (gather_x, CHUNKS))

        def one_more(half, sums):
            return mlp_back(layer, half, sums)

        gain_sum, shift_sum, bias_out = lax.fori_loop(0, 2, one_more, (zeros, zeros, zeros))
        when(upper_layer, (reduce_y, 1), (reduce_z, CHUNKS))
        when(bottom, (reduce_y, 4), (reduce_z, 2), (gather_z, 1))
        store_sums(
            layer,
            [(7 * D + FF, bias_down), (5 * D, gain_sum), (6 * D, shift_sum), (4 * D, bias_out)]
            + [(7 * D + tile * D, bias_up[tile]) for tile in range(4)],
        )
        keep_in(kq, 3, mm(ATT[layer].T, DMB[...]).astype(BF))

        def two(image, nothing):
            attend_back(layer, image)
            when(jnp.logical_and(upper_layer, image == 0), (reduce_x, 0))
            when(jnp.logical_and(upper_layer, image == 2), (reduce_x, 1))
            when(jnp.logical_and(upper_layer, image == 3), (reduce_z, 0))

            @pl.when(jnp.logical_and(bottom, image == 0))
            def _():
                factors_mate()
                gather_done(CHUNKS)
                gather_x(0)

            when(jnp.logical_and(bottom, image == 1), (reduce_x, 3), (gather_z, 2))
            when(jnp.logical_and(bottom, image == 2), (gather_x, 1), (reduce_z, 3))
            when(jnp.logical_and(bottom, image == 3), (reduce_x, 4), (gather_x, 2), (gather_done, 0))
            return nothing

        lax.fori_loop(0, KEPT, two, 0)
        turned = renew(N1, layer, 0)
        for tile in range(3):
            keep_in(
                kq, tile, mm(turned, DH[:, tile * D : (tile + 1) * D]).astype(BF)
            )
        when(upper_layer, (reduce_core, 2))
        when(bottom, (reduce_core, 5), (gather_z, 3))
        store_sums(
            layer,
            [
                (2 * D, fold(DH[:, 0:D].astype(F32))),
                (3 * D, fold(DH[:, 2 * D : 3 * D].astype(F32))),
            ],
        )

        def three(half, sums):
            rows = pl.ds(aligned(half * HALF, 16), HALF)
            made = mm_nt(DH[rows, 0 : 3 * D], win[layer, :, 0 : 3 * D])
            return first_back(layer, half, made, sums)

        gain_sum, shift_sum = lax.fori_loop(0, 2, three, (zeros, zeros))
        store_sums(layer, [(0, gain_sum), (D, shift_sum)])
        when(upper_layer, (reduce_y, 2))
        when(bottom, (reduce_y, 5), (reduce_z, 4), (gather_done, 1))
        return carry

    lax.fori_loop(0, LAYERS - 1, backward, 0)

    for at, size in pieces(BLK):
        total = None
        for image in range(KEPT):
            part = X[image * BLK + at : image * BLK + at + size, :]
            DXB[image * BLK + at : image * BLK + at + size, :] = part.astype(BF)
            total = part if total is None else total + part
        V[at : at + size, 0:D] = total

    vec = ("v", v_send, v_recv)
    v_y, v_x = 1, n_y
    v_z = v_x + n_x - 1
    v_gz = v_z + n_z - 1
    v_gx = v_gz + n_z - 1
    v_gy = v_gx + n_x - 1
    v_gc = v_gy + n_y - 1
    rows_c = VEC_ROWS // 2
    rows_y = rows_c // n_y
    rows_x = rows_y // n_x
    split_z = cut(rows_x, n_z, 8)
    rows_z = rows_x // split_z
    at_c = c * rows_c
    at_y = at_c + y * rows_y
    at_x = at_y + x * rows_x
    at_z = at_x + z * rows_z if split_z > 1 else at_x

    def vrows(ref, at, rows):
        return ref.at[pl.ds(aligned(at, 8), rows), :]

    def vadd(at, rows, sources):
        target = pl.ds(aligned(at, 8), rows)
        total = V[target, :]
        for source in sources:
            total = total + source
        V[target, :] = total

    def vectors_core():
        go(lambda: vrows(V, (1 - c) * rows_c, rows_c), VC, vec, 0, mate)

    def vectors_y():
        arrived(VC, v_recv.at[0], v_send.at[0])
        vadd(at_c, rows_c, [VC[...]])
        for o in range(1, n_y):
            to = turn(y, o, n_y)
            go(
                lambda o=o: vrows(V, at_c + turn(y, o, n_y) * rows_y, rows_y), VY.at[o - 1],
                vec, v_y + o - 1, here.to(y=to),
            )

    def vectors_x():
        for o in range(1, n_y):
            arrived(VY.at[o - 1], v_recv.at[v_y + o - 1], v_send.at[v_y + o - 1])
        vadd(at_y, rows_y, [VY[o - 1] for o in range(1, n_y)])
        for o in range(1, n_x):
            to = turn(x, o, n_x)
            go(
                lambda o=o: vrows(V, at_y + turn(x, o, n_x) * rows_x, rows_x), VX.at[o - 1],
                vec, v_x + o - 1, here.to(x=to),
            )

    def vectors_z():
        for o in range(1, n_x):
            arrived(VX.at[o - 1], v_recv.at[v_x + o - 1], v_send.at[v_x + o - 1])
        vadd(at_x, rows_x, [VX[o - 1] for o in range(1, n_x)])
        for o in range(1, n_z):

            def make(o=o):
                at = at_x + turn(z, o, n_z) * rows_z if split_z > 1 else at_x
                return vrows(V, at, rows_z)

            go(make, VZ.at[z], vec, v_z + o - 1, here.to(z=turn(z, o, n_z)))

    def vectors_gather_z():
        for o in range(1, n_z):
            arrived(
                VZ.at[turn(z, n_z - o, n_z)], v_recv.at[v_z + o - 1], v_send.at[v_z + o - 1]
            )
        target = pl.ds(aligned(at_z, 8), rows_z)
        VZ[z] = V[target, :]
        total = VZ[0]
        for index in range(1, n_z):
            total = total + VZ[index]
        VF[target, :] = total
        if split_z > 1:
            for o in range(1, n_z):
                go(
                    lambda: vrows(VF, at_z, rows_z), vrows(VF, at_z, rows_z), vec, v_gz + o - 1,
                    here.to(z=turn(z, o, n_z)),
                )

    def vectors_gather_x():
        if split_z > 1:
            for o in range(1, n_z):
                came = turn(z, n_z - o, n_z)
                arrived(
                    vrows(VF, at_x + came * rows_z, rows_z), v_recv.at[v_gz + o - 1],
                    v_send.at[v_gz + o - 1],
                )
        for o in range(1, n_x):
            go(
                lambda: vrows(VF, at_x, rows_x), vrows(VF, at_x, rows_x), vec, v_gx + o - 1,
                here.to(x=turn(x, o, n_x)),
            )

    sq = ("q", q_send, q_recv)

    def squares_z():
        SQ[0] = square_sum[...]
        SQZ[z] = square_sum[...]
        for o in range(1, n_z):
            go(lambda: SQ.at[0], SQZ.at[z], sq, o - 1, here.to(z=turn(z, o, n_z)))

    def slot_of(i, j, k):
        return (i * n_y + j) * 2 + k

    def squares_plane():
        for o in range(1, n_z):
            arrived(SQZ.at[turn(z, n_z - o, n_z)], q_recv.at[o - 1], q_send.at[o - 1])
        total = SQZ[0]
        for index in range(1, n_z):
            total = total + SQZ[index]
        SQ[1] = total
        SQP[slot_of(x, y, c)] = total
        for index, step in enumerate(plane):
            go(
                lambda: SQ.at[1], SQP.at[slot_of(x, y, c)], sq, n_z - 1 + index,
                in_plane(step),
            )

    def squares_done():
        for index, (i, j, k) in enumerate(plane):
            slot = slot_of(
                turn(x, n_x - i, n_x), turn(y, n_y - j, n_y), lax.rem(c + k, 2)
            )
            arrived(SQP.at[slot], q_recv.at[n_z - 1 + index], q_send.at[n_z - 1 + index])
        total = SQP[0]
        for index in range(1, 2 * n_x * n_y):
            total = total + SQP[index]
        SQ[2] = total

    def vectors_gather_y():
        for o in range(1, n_x):
            at = at_y + turn(x, n_x - o, n_x) * rows_x
            arrived(vrows(VF, at, rows_x), v_recv.at[v_gx + o - 1], v_send.at[v_gx + o - 1])
        for o in range(1, n_y):
            go(
                lambda: vrows(VF, at_y, rows_y), vrows(VF, at_y, rows_y), vec, v_gy + o - 1,
                here.to(y=turn(y, o, n_y)),
            )

    def vectors_gather_core():
        for o in range(1, n_y):
            at = at_c + turn(y, n_y - o, n_y) * rows_y
            arrived(vrows(VF, at, rows_y), v_recv.at[v_gy + o - 1], v_send.at[v_gy + o - 1])
        go(lambda: vrows(VF, at_c, rows_c), vrows(VF, at_c, rows_c), vec, v_gc, mate)

    def vectors_done():
        arrived(vrows(VF, (1 - c) * rows_c, rows_c), v_recv.at[v_gc], v_send.at[v_gc])

    vectors_core()
    low = DXB[...]
    for tile in range(2):
        made = mm_tn(pix[:, :, tile * D : (tile + 1) * D].reshape(ROWS, D), low).astype(BF)
        for piece in range(D // rows_patch):
            shard = tile * (D // rows_patch) + piece
            GS[1, shard // 2, shard % 2] = made[piece * rows_patch : (piece + 1) * rows_patch]

    kp = CHUNKS + 1
    reduce_core(kp)
    vectors_y()
    gather_done(2)
    gather_x(3)
    reduce_y(kp)
    vectors_x()
    gather_z(4)
    reduce_x(5)
    vectors_z()
    reduce_x(kp)
    gather_x(4)
    vectors_gather_z()
    reduce_z(5)
    reduce_z(kp)
    vectors_gather_x()
    gather_done(3)
    gather_z(5)
    vectors_gather_y()
    gather_done(4)
    gather_x(5)
    gather_z(kp)
    squares_z()
    gather_x(kp)
    vectors_gather_core()
    factors_done()
    squares_plane()
    vectors_done()
    gather_done(5)
    gather_done(kp)
    squares_done()
    last_copies = [
        pltpu.make_async_copy(VF, vec_out, out_local.at[1 + CHUNKS + 2]),
        pltpu.make_async_copy(SQ.at[2], square_out, out_local.at[2 + CHUNKS + 2]),
    ]
    for copy in last_copies:
        copy.start()
    for source, send, recv, at in list(sent.values()):
        left_here(source(), recv.at[at], send.at[at])
    for k in range(CHUNKS + 2):
        result(k).wait()
    for copy in last_copies:
        copy.wait()

    @pl.when(jnp.logical_not(lower))
    def _():
        left_here(given, img_recv.at[0], img_send.at[0])
        left_here(lab_given, img_recv.at[1], img_send.at[1])


def run_train(
    n_rep, n_shard, patches, labels, counts, own_patch, own_in, own_down, vecs, glob, pos, head
):
    n_x = 2 ** ((n_rep.bit_length() - 2) // 2)
    n_z, n_y = n_rep // n_x, n_shard // 2
    block = 4 * (D // n_shard)
    group = KEPT * n_shard
    keep = LAYERS - 1
    units = 1 + 3 * LAYERS
    chunks = CHUNKS + 2

    def buf(*shape, dtype=BF):
        return pltpu.VMEM(shape, dtype)

    def sems(*shape):
        return pltpu.SemaphoreType.DMA(shape)

    def reduction(count, slots, rows):
        by_x = cut(rows, n_x, 16)
        by_z = cut(rows // by_x, n_z, 16)
        return [
            buf(count, n_y, 2, rows, D),
            buf(slots, n_y, rows, D),
            buf(slots, n_y - 1, rows, D),
            buf(slots, n_x - 1 if by_x > 1 else n_x, rows // by_x, D),
            buf(slots, n_z, rows // by_x // by_z, D),
            buf(count, rows, D),
        ]

    rows_y = VEC_ROWS // 2 // n_y
    rows_x = rows_y // n_x
    rows_z = rows_x // cut(rows_x, n_z, 8)
    ag_count = n_y + (n_y - 1) * (n_x - 1) * 2 + n_y - 1
    rs_count = 1 + (n_y - 1) + 2 * (n_x - 1) + 2 * (n_z - 1)
    f_count = 1 + (n_y - 1) + (n_x - 1) + (n_z - 1) + 1
    v_count = 1 + 2 * (n_y - 1) + 2 * (n_x - 1) + 2 * (n_z - 1) + 1
    q_count = n_z - 1 + 2 * n_x * n_y - 1
    whole = pl.BlockSpec(memory_space=pltpu.VMEM)
    there = pl.BlockSpec(memory_space=pl.ANY)
    return pl.pallas_call(
        functools.partial(train, n_rep, n_shard),
        out_shape=[
            jax.ShapeDtypeStruct((CHUNKS, block, D), BF),
            jax.ShapeDtypeStruct((2, block // 2, D), BF),
            jax.ShapeDtypeStruct((VEC_ROWS, VEC_WIDE), F32),
            jax.ShapeDtypeStruct((8, 128), F32),
            jax.ShapeDtypeStruct((2, n_rep, group, WFAC), BF),
        ],
        in_specs=[there] + [pl.BlockSpec(memory_space=pltpu.SMEM)] * 2 + [there] * 3 + [whole] * 4,
        out_specs=[there] * 5,
        scratch_shapes=[
            buf(ROWS, D, dtype=F32),
            buf(LAYERS, ROWS, D),
            buf(LAYERS, ROWS, 128, dtype=F32),
            buf(keep, ROWS, 3 * D),
            buf(keep, ROWS, D),
            buf(keep, ROWS, D),
            buf(keep, ROWS, 128, dtype=F32),
            buf(keep, ROWS, FF),
            buf(keep, ROWS, FF),
            buf(ROWS, D),
            buf(ROWS, D),
            buf(ROWS, D),
            buf(ROWS, FF),
            buf(KEPT, BLK, PATCH_DIM),
            buf(2, 32, 128, dtype=F32),
            buf(32, 128, dtype=F32),
            buf(PATCH_DIM, D),
            buf(LAYERS, D, 4 * D + FF),
            buf(LAYERS, FF, D),
            buf(D, CPAD),
            buf(1, CPAD, dtype=F32),
            *reduction(CHUNKS, 3, block),
            *reduction(2, 1, block // 2),
            buf(2, group, WFAC),
            buf(group, WFAC),
            buf(n_y - 1, group, WFAC),
            buf(n_x, group, WFAC),
            buf(VEC_ROWS, VEC_WIDE, dtype=F32),
            buf(VEC_ROWS // 2, VEC_WIDE, dtype=F32),
            buf(n_y - 1, rows_y, VEC_WIDE, dtype=F32),
            buf(n_x - 1, rows_x, VEC_WIDE, dtype=F32),
            buf(n_z, rows_z, VEC_WIDE, dtype=F32),
            buf(VEC_ROWS, VEC_WIDE, dtype=F32),
            buf(3, 8, 128, dtype=F32),
            buf(n_z, 8, 128, dtype=F32),
            buf(2 * n_x * n_y, 8, 128, dtype=F32),
            buf(8, 128, dtype=F32),
            sems(units, ag_count),
            sems(units, ag_count),
            sems(units, 4),
            sems(chunks, rs_count),
            sems(chunks, rs_count),
            sems(f_count),
            sems(f_count),
            sems(v_count),
            sems(v_count),
            sems(q_count),
            sems(q_count),
            sems(2),
            sems(2),
            sems(4),
            sems(3 + chunks),
        ],
        compiler_params=pltpu.CompilerParams(
            vmem_limit_bytes=65400 * 1024, collective_id=0, has_side_effects=True
        ),
        cost_estimate=pl.CostEstimate(
            flops=24_000_000_000, bytes_accessed=30_000_000, transcendentals=10_000_000
        ),
        name="train_step",
    )(patches, labels, counts, own_patch, own_in, own_down, vecs, glob, pos, head)


def adam(weight, first, second, grad, factor, rate):
    grad = grad * factor
    first = BETA_FIRST * first + (1.0 - BETA_FIRST) * grad
    second = BETA_SECOND * second + (1.0 - BETA_SECOND) * (grad * grad)
    first_scale = 1.0 / (1.0 - BETA_FIRST**ADAM_STEP)
    root_scale = (1.0 / (1.0 - BETA_SECOND**ADAM_STEP)) ** 0.5
    bottom = second * lax.rsqrt(second) * root_scale + ADAM_EPS
    step = first * lax.rsqrt(bottom * bottom)
    weight = weight * (1.0 - rate * WEIGHT_DECAY) - step * (rate * first_scale)
    return weight, first, second


def update(n_rep, n_shard, *refs):
    res, small, vec, exchanged, factors = refs[0:5]
    sources = refs[5:26]
    loss_out, norm_out = refs[26:28]
    targets = refs[28:49]
    buffers = refs[49:70]
    results = refs[70:91]
    last_in, last_down, passing, grad_head, in_sems, out_sems = refs[91:]
    shard = lax.axis_index("shard")
    rows_in = D // n_shard
    rows_down = FF // n_shard
    keep = LAYERS - 1

    def moves(array, layer=None, out=False):
        found = []
        for kind in range(3):
            index = 3 * array + kind
            if out:
                src, dst, sem = results[index], targets[index], out_sems
            else:
                src, dst, sem = sources[index], buffers[index], in_sems
            slot = 0 if layer is None else layer
            if layer is not None:
                src, dst = src.at[layer], dst.at[layer]
            found.append(pltpu.make_async_copy(src, dst, sem.at[index, slot]))
        return found

    layered = [(1, layer) for layer in range(LAYERS)] + [(2, layer) for layer in range(LAYERS)]
    order = layered + [(0, None), (6, None), (5, None), (3, None), (4, None)]
    for array, layer in order:
        for move in moves(array, layer):
            move.start()

    n_rows = factors.shape[1] * factors.shape[2]

    def factor(half, at, size):
        return factors[half, :, :, at : at + size].reshape(n_rows, size)

    def squares(values):
        return fold(values * values)

    total = jnp.zeros((8, D), F32)
    own_rows = pl.multiple_of(shard * rows_in, 8)

    def keep_in(column, made):
        slot = column % 2
        passing[slot] = made
        last_in[:, column * D : (column + 1) * D] = passing[slot, pl.ds(own_rows, rows_in), :]

    h2 = factor(0, FF, D)
    for tile in range(4):
        made = mm_tn(h2, factor(1, tile * D, D))
        keep_in(4 + tile, made)
        total = total + squares(made)
    for tile in range(2):
        last_in[:, (1 + tile) * D : (2 + tile) * D] = small[
            0, tile * rows_in : (tile + 1) * rows_in, :
        ].astype(F32)
    made = mm_tn(factor(0, FF + 2 * D, D), factor(1, FF + D, D))
    keep_in(0, made)
    total = total + squares(made)
    made = mm_tn(factor(0, FF + D, D), factor(1, FF, D))
    keep_in(3, made)
    total = total + squares(made)
    d_top = factor(0, FF + 4 * D, D)
    per = min(rows_down, D)
    for tile in range(4):
        made = mm_tn(factor(0, tile * D, D), d_top)
        total = total + squares(made)
        for piece in range(D // per):
            owner, at = divmod(tile * D + piece * per, rows_down)

            def keep_down(made=made, piece=piece, at=at):
                last_down[at : at + per, :] = made[piece * per : (piece + 1) * per]

            pl.when(shard == owner)(keep_down)
    final = factor(0, FF + 3 * D, D)
    wide = jnp.zeros((8, 128), F32)
    for at in range(0, CPAD, 512):
        d_logits = factor(1, FF + 2 * D + at, 512)
        made = mm_tn(final, d_logits)
        grad_head[0:D, at : at + 512] = made
        bias = down_sum(d_logits.astype(F32))
        grad_head[D : D + 1, at : at + 512] = bias
        sums = squares(made)
        for lane in range(0, 512, 128):
            wide = wide + sums[:, lane : lane + 128]
            row = bias[:, lane : lane + 128]
            wide = wide + (row * row) * 0.125
    for lane in range(0, D, 128):
        wide = wide + total[:, lane : lane + 128]
    used = VEC_AT + 12 * LAYERS + 2
    parts = jnp.zeros((8, D), F32)
    kept_rows = lax.broadcasted_iota(jnp.int32, (8, 1), 0)
    for at in range(0, used, 8):
        value = vec[at : at + 8, 0:D]
        if at + 8 > used:
            value = jnp.where(kept_rows + at < used, value, 0.0)
        parts = parts + value * value
    patch_bias = down_sum(vec[0:PATCHES, 0:D])
    class_row = vec[CLS : CLS + 1, 0:D]
    rest = (patch_bias * patch_bias + class_row * class_row) * 0.125
    parts = parts + rest
    for lane in range(0, D, 128):
        wide = wide + parts[:, lane : lane + 128]
    wide = wide + exchanged[...]
    sum_squares = jnp.sum(jnp.sum(wide, axis=1, keepdims=True), axis=0, keepdims=True)
    inv_count = 1.0 / vec[used + 1 : used + 2, 0:1]
    grad_norm = jnp.sqrt(sum_squares) * inv_count
    norm_out[...] = grad_norm
    loss_out[...] = vec[used : used + 1, 0:1] * inv_count
    scale = jnp.minimum(1.0, CLIP_NORM / grad_norm) * inv_count

    def apply(array, where, grad, rate):
        refs = [buffers[3 * array + kind] for kind in range(3)]
        made = adam(refs[0][where], refs[1][where], refs[2][where], grad, scale, rate)
        for kind, value in enumerate(made):
            results[3 * array + kind][where] = value

    def begin(array, layer=None):
        for move in moves(array, layer):
            move.wait()

    def finish(array, layer=None):
        for move in moves(array, layer, out=True):
            move.start()

    def loop(count, body):
        def one(index, nothing):
            body(index)
            return nothing

        lax.fori_loop(0, count, one, 0)

    step = 32 if rows_in % 32 == 0 else 16
    for layer in range(LAYERS):
        begin(1, layer)

        def column_of(column):
            lanes = pl.ds(pl.multiple_of(column * D, 128), D)
            for at in range(0, rows_in, step):
                if layer < keep:
                    k = 3 * (keep - 1 - layer) + jnp.where(column < 4, 2, 1)
                    row = pl.multiple_of(lax.rem(column, 4) * rows_in + at, 16)
                    grad = res[k, pl.ds(row, step), :].astype(F32)
                else:
                    grad = last_in[at : at + step, lanes]
                apply(1, (layer, slice(at, at + step), lanes), grad, LEARNING_RATE)

        loop(8, column_of)
        finish(1, layer)
    for layer in range(LAYERS):
        begin(2, layer)

        def rows_of(index):
            for part in range(3):
                at = pl.multiple_of(index * 96 + part * 32, 16)
                if layer < keep:
                    grad = res[3 * (keep - 1 - layer), pl.ds(at, 32), :].astype(F32)
                else:
                    grad = last_down[pl.ds(at, 32), :]
                apply(2, (layer, pl.ds(at, 32), slice(0, D)), grad, LEARNING_RATE)

        loop(rows_down // 96, rows_of)
        finish(2, layer)
    begin(0)

    def patch_rows(index):
        for part in range(3):
            at = pl.multiple_of(index * 96 + part * 32, 16)
            grad = small[1, pl.ds(at, 32), :].astype(F32)
            apply(0, (pl.ds(at, 32), slice(0, D)), grad, LEARNING_RATE)

    loop(PATCH_DIM // n_shard // 96, patch_rows)
    finish(0)
    begin(6)

    def head_rows(index):
        for part in range(3):
            rows = pl.ds(pl.multiple_of(index * 48 + part * 16, 16), 16)
            apply(6, (rows, slice(0, NCLS)), grad_head[rows, 0:NCLS], LEARNING_RATE)

    loop(D // 48, head_rows)
    apply(6, (slice(D, D + 1), slice(0, NCLS)), grad_head[D : D + 1, 0:NCLS], LEARNING_RATE)
    finish(6)
    begin(5)
    apply(5, (slice(0, 1), slice(0, D)), class_row, VECTOR_RATE)
    for at in range(0, PATCHES, 28):
        apply(
            5, (slice(1 + at, 29 + at), slice(0, D)), vec[at : at + 28, 0:D], VECTOR_RATE
        )
    finish(5)
    begin(3)
    for layer in range(LAYERS):
        for piece in range(12):
            row = VEC_AT + 12 * layer + piece
            where = (slice(layer, layer + 1), slice(piece * D, (piece + 1) * D))
            apply(3, where, vec[row : row + 1, 0:D], VECTOR_RATE)
    finish(3)
    begin(4)
    rows = [patch_bias, class_row, vec[used - 2 : used - 1, 0:D], vec[used - 1 : used, 0:D]]
    for index, row in enumerate(rows):
        apply(4, (slice(index, index + 1), slice(0, D)), row, VECTOR_RATE)
    finish(4)
    for array, layer in order:
        for move in moves(array, layer, out=True):
            move.wait()


def run_update(n_rep, n_shard, res, small, vec, squares, factors, arrays):
    whole = pl.BlockSpec(memory_space=pltpu.VMEM)
    there = pl.BlockSpec(memory_space=pl.ANY)
    one = jax.ShapeDtypeStruct((1, 1), F32)
    made = pl.pallas_call(
        functools.partial(update, n_rep, n_shard),
        out_shape=[one, one] + [jax.ShapeDtypeStruct(a.shape, F32) for a in arrays],
        in_specs=[whole] * 5 + [there] * 21,
        out_specs=[whole] * 2 + [there] * 21,
        scratch_shapes=[pltpu.VMEM(a.shape, F32) for a in (*arrays, *arrays)]
        + [
            pltpu.VMEM((D // n_shard, 4 * D + FF), F32),
            pltpu.VMEM((FF // n_shard, D), F32),
            pltpu.VMEM((2, D, D), F32),
            pltpu.VMEM((D + 8, CPAD), F32),
            pltpu.SemaphoreType.DMA((21, LAYERS)),
            pltpu.SemaphoreType.DMA((21, LAYERS)),
        ],
        compiler_params=pltpu.CompilerParams(vmem_limit_bytes=62 * 1024 * 1024),
        cost_estimate=pl.CostEstimate(
            flops=200_000_000, bytes_accessed=50_000_000, transcendentals=4_000_000
        ),
        name="adamw",
    )(res, small, vec, squares, factors, *arrays)
    return made[0].reshape(()), made[1].reshape(()), made[2:]


def shards(
    n_rep, n_shard,
    patches, labels, counts, patch_w, layer_in, layer_down, layer_vecs, glob_vecs, pos_embed, head,
    m_patch, v_patch, m_in, v_in, m_down, v_down, m_vecs, v_vecs, m_glob, v_glob, m_pos, v_pos,
    m_head, v_head,
):
    padded = jnp.pad(patches, ((0, 0), (0, BLK - PATCHES), (0, 0)))
    res, small, vec, squares, factors = run_train(
        n_rep, n_shard, padded, labels, counts, patch_w, layer_in, layer_down, layer_vecs,
        glob_vecs, pos_embed, head,
    )
    arrays = [
        patch_w, m_patch, v_patch, layer_in, m_in, v_in, layer_down, m_down, v_down,
        layer_vecs, m_vecs, v_vecs, glob_vecs, m_glob, v_glob, pos_embed, m_pos, v_pos,
        head, m_head, v_head,
    ]
    loss, grad_norm, new = run_update(n_rep, n_shard, res, small, vec, squares, factors, arrays)
    return (loss, grad_norm, *new)


def solution(mesh):
    everywhere = P()
    rows = P("shard", None)
    middle = P(None, "shard", None)
    return jax.shard_map(
        functools.partial(shards, mesh.shape["rep"], mesh.shape["shard"]),
        mesh=mesh,
        in_specs=(
            P(("rep", "shard"), None, None),
            P(("rep", "shard")),
            P(("rep", "shard")),
            rows,
            middle,
            middle,
            *(everywhere,) * 4,
            *(rows,) * 2,
            *(middle,) * 4,
            *(everywhere,) * 8,
        ),
        out_specs=(
            *(everywhere,) * 2,
            *(rows,) * 3,
            *(middle,) * 6,
            *(everywhere,) * 12,
        ),
        check_vma=False,
    )
```

```python
import functools

import jax
import jax.numpy as jnp
from jax import lax
from jax.experimental import pallas as pl
from jax.experimental.pallas import tpu as pltpu
from jax.sharding import PartitionSpec as P

D = 384
HEADS = 6
HEAD_DIM = 64
FF = 1536
PATCH_DIM = 768
PATCHES = 196
NCLS = 1000
LAYERS = 3
SEQ = 197

BLK = 208
CLS = 200
TAIL = 192
KEPT = 4
ROWS = KEPT * BLK
HALF = 2 * BLK
CROWS = KEPT * 16
CPAD = 1024
WIDE = 8 * D + FF

NORM_EPS = 1e-06
SMOOTHING = 0.1
CLIP_NORM = 0.05
LEARNING_RATE = 0.05
VECTOR_RATE = 0.5
BETA_FIRST = 0.9
BETA_SECOND = 0.999
ADAM_EPS = 1e-08
WEIGHT_DECAY = 0.05
ADAM_STEP = 10
GELU_SCALE = 0.7978845608028654
GELU_CUBIC = 0.044715

F32 = jnp.float32
BF = jnp.bfloat16


def mm(left, right):
    return jnp.dot(left, right, preferred_element_type=F32)


def mm_nt(left, right):
    return lax.dot_general(left, right, (((1,), (1,)), ((), ())), preferred_element_type=F32)


def mm_tn(left, right):
    return lax.dot_general(left, right, (((0,), (0,)), ((), ())), preferred_element_type=F32)


def fold(values):
    return jnp.sum(values.reshape(-1, 8, values.shape[-1]), axis=0)


def down_sum(values):
    return jnp.sum(values, axis=0, keepdims=True)


def norm(values):
    centre = values - jnp.mean(values, axis=-1, keepdims=True)
    inverse = lax.rsqrt(jnp.mean(centre * centre, axis=-1, keepdims=True) + NORM_EPS)
    return centre * inverse, inverse


def norm_back(upstream, normed, inverse, gain):
    scaled = upstream * gain
    first = jnp.mean(scaled, axis=-1, keepdims=True)
    second = jnp.mean(scaled * normed, axis=-1, keepdims=True)
    return inverse * (scaled - first - normed * second)


def gelu_parts(hidden):
    square = hidden * hidden
    tangent = jnp.tanh(hidden * (GELU_SCALE + (GELU_SCALE * GELU_CUBIC) * square))
    share = 0.5 + 0.5 * tangent
    active = hidden * share
    inner = (2.0 * GELU_SCALE) + (6.0 * GELU_SCALE * GELU_CUBIC) * square
    slope = share + active * (1.0 - share) * inner
    return active, slope


def lane_mask(width, low, high):
    lane = lax.broadcasted_iota(jnp.int32, (1, width), 1)
    return jnp.where((lane >= low) & (lane < high), 1.0, 0.0).astype(BF)


STEP = 32


def pieces(total):
    return [(at, min(STEP, total - at)) for at in range(0, total, STEP)]


SCHEDULE = {
    ("cast", 0): ("ws0",),
    ("cast", 1): ("ws1",),
    ("cast", 2): ("ws2",),
    ("b_start",): ("wf0", "ws3", "wf1", "wr0", "ws4", "we0",),
    ("embed", 0): ("wf2", "ws5",),
    ("b_norm", 0, 0): ("wr1", "wf3", "ws6", "we1",),
    ("norm", 0, 0): ("wr2", "wf4", "ws7",),
    ("att", 0, 0, 1): ("wr3",),
    ("mid", 0, 0): ("wf5", "ws8",),
    ("b_up", 0, 0): ("we2",),
    ("up", 0, 0): ("wr4", "wf6", "ws9",),
    ("b_down", 0, 0): ("we3",),
    ("b_norm", 0, 1): ("wr5", "we4",),
    ("norm", 0, 1): ("wf7",),
    ("att", 0, 1, 0): ("wr6",),
    ("att", 0, 1, 1): ("wf8",),
    ("b_up", 0, 1): ("we5",),
    ("up", 0, 1): ("wr7", "wf9",),
    ("b_down", 0, 1): ("we6",),
    ("norm", 1, 0): ("wr8",),
    ("att", 1, 0, 1): ("wr9",),
    ("b_last",): ("we7", "we8", "we9",),
    ("class",): ("fc",),
    ("kv",): ("core6",),
    ("lb", 1): ("fy",),
    ("dn", 1): ("y6", "core0",),
    ("act", 1, 1): ("fz",),
    ("ups", 1): ("core1", "y0",),
    ("mlpb", 1, 0): ("x6",),
    ("attb", 1, 0): ("y1", "z6",),
    ("attb", 1, 3): ("x0",),
    ("qkv", 1): ("fx", "core2",),
    ("dn", 0): ("z0", "y2", "x1", "core3",),
    ("act", 0, 0): ("gz6", "gx6",),
    ("mlpb", 0, 0): ("gz0",),
    ("attb", 0, 0): ("x2", "y3", "core4", "fm",),
    ("attb", 0, 1): ("gx0",),
    ("attb", 0, 2): ("z1",),
    ("attb", 0, 3): ("gd6",),
    ("fb", 0, 1): ("z2", "fd",),
    ("emb",): ("x3", "y4", "core5", "gz1", "vc",),
    ("patch",): ("gd0", "core7",),
    ("tail",): ("gz2", "z3", "vy", "y7", "gx1", "x4", "y5", "gx2", "vx", "gd1", "gz3", "x7", "z4", "gd2", "gx3", "vz", "x5", "z7", "gz4", "vgz", "gd3", "z5", "gz7", "gx7", "gx4", "gd7", "vgx", "gz5", "qz", "gd4", "vgy", "gx5", "qp", "vgc", "vd", "gd5", "qd",),
}


WFAC = FF + 5 * D
VEC_ROWS = 256
VEC_AT = BLK
VEC_WIDE = D
MESH = pl.DeviceIdType.MESH
CHUNKS = 6


class Place:
    def __init__(self, n_rep, n_shard):
        self.n_rep, self.n_shard = n_rep, n_shard
        self.n_x = 2 ** ((n_rep.bit_length() - 2) // 2)
        self.n_z = n_rep // self.n_x
        self.n_y = n_shard // 2
        rep, shard = lax.axis_index("rep"), lax.axis_index("shard")
        self.rep, self.shard = rep, shard
        self.z, self.x = rep // self.n_x, rep % self.n_x
        self.y, self.c = shard // 2, shard % 2

    def to(self, x=None, y=None, z=None, c=None):
        x = self.x if x is None else x
        y = self.y if y is None else y
        z = self.z if z is None else z
        c = self.c if c is None else c
        return {"rep": z * self.n_x + x, "shard": y * 2 + c}


def cut(rows, parts, unit):
    return parts if rows % (parts * unit) == 0 else 1


def aligned(value, unit):
    return pl.multiple_of(value, unit)


def train(
    n_rep, n_shard,
    patches, labels, counts, own_patch, own_in, own_down, vecs, glob, pos, head,
    res_out, small_out, vec_out, square_out, all_factors,
    X, N1, I1, QKV, ATT, N2, I2, ACT, SLOPE, DXB, DMB, DA, DH,
    pix, lab, lab_given, wp, win, wdn, low_head, head_bias,
    G, RC, RY, RX, RZ, RES, GS, SC, SY, SX, SZ, SRES,
    FAC, FC, FY, FALL, V, VC, VY, VX, VZ, VF, SQ, SQZ, SQP, square_sum,
    ag_send, ag_recv, ag_local, rs_send, rs_recv, f_send, f_recv, v_send, v_recv,
    q_send, q_recv,
    img_send, img_recv, img_local, out_local,
):
    here = Place(n_rep, n_shard)
    n_x, n_y, n_z = here.n_x, here.n_y, here.n_z
    x, y, z, c = here.x, here.y, here.z, here.c
    rows_in, rows_down, rows_patch = D // n_shard, FF // n_shard, PATCH_DIM // n_shard
    block = 4 * rows_in
    mate = here.to(c=1 - c)

    def push(src, dst, send, recv, device):
        pltpu.make_async_remote_copy(
            src_ref=src, dst_ref=dst, send_sem=send, recv_sem=recv,
            device_id=device, device_id_type=MESH,
        ).start()

    def arrived(dst, recv, send):
        pltpu.make_async_remote_copy(
            src_ref=dst, dst_ref=dst, send_sem=send, recv_sem=recv,
            device_id=mate, device_id_type=MESH,
        ).wait_recv()

    def left_here(src, recv, send):
        pltpu.make_async_remote_copy(
            src_ref=src, dst_ref=src, send_sem=send, recv_sem=recv,
            device_id=mate, device_id_type=MESH,
        ).wait_send()

    sent = {}

    def go(source, dst, sems, index, device):
        name, send, recv = sems
        push(source(), dst, send.at[index], recv.at[index], device)
        sent[name, index] = (source, send, recv, index)

    def gone(sems, index):
        source, send, recv, at = sent.pop((sems[0], index))
        left_here(source(), recv.at[at], send.at[at])

    def turn(at, by, size):
        return lax.rem(at + by, size)

    barrier = pltpu.get_barrier_semaphore()
    plane = [
        (i, j, k) for i in range(n_x) for j in range(n_y) for k in range(2) if i or j or k
    ]

    def in_plane(step):
        i, j, k = step
        return here.to(x=turn(x, i, n_x), y=turn(y, j, n_y), c=lax.rem(c + k, 2))

    others = [in_plane(step) for step in plane]
    others += [here.to(z=turn(z, o, n_z)) for o in range(1, n_z)]
    for other in others:
        pl.semaphore_signal(barrier, inc=1, device_id=other, device_id_type=MESH)
    pl.semaphore_wait(barrier, len(others))

    def weight(kind, layer, shard, part=None):
        if kind == "patch":
            parts = cut(rows_patch, n_x, 16)
            rows = rows_patch // parts
            if part is None:
                return wp.at[pl.ds(aligned(shard * rows_patch, 16), rows_patch), :]
            return wp.at[pl.ds(aligned(shard * rows_patch + part * rows, 16), rows), :]
        if kind == "down":
            parts = cut(rows_down, n_x, 16)
            rows = rows_down // parts
            if part is None:
                return wdn.at[layer, pl.ds(aligned(shard * rows_down, 16), rows_down), :]
            return wdn.at[layer, pl.ds(aligned(shard * rows_down + part * rows, 16), rows), :]
        base = 0 if kind == "attn" else 4 * D
        rows = pl.ds(aligned(shard * rows_in, 16), rows_in)
        if part is None:
            return win.at[layer, rows, pl.ds(base, 4 * D)]
        wide = 4 * D // n_x
        return win.at[layer, rows, pl.ds(aligned(base + part * wide, 128), wide)]

    units = [("patch", 0)] + [
        (kind, layer) for layer in range(LAYERS) for kind in ("attn", "up", "down")
    ]

    def parts_of(kind):
        if kind == "patch":
            return cut(rows_patch, n_x, 16)
        if kind == "down":
            return cut(rows_down, n_x, 16)
        return n_x

    ag = ("ag", ag_send, ag_recv)
    base_x = n_y
    base_my = base_x + (n_y - 1) * (n_x - 1)
    base_mx = base_my + (n_y - 1)

    stage = 4 * rows_in

    def weights_copies(unit):
        kind, layer = units[unit]
        base = (unit % 2) * stage
        if kind == "patch":
            pairs = [(own_patch, X.at[pl.ds(base, rows_patch)])]
        elif kind == "down":
            pairs = [(own_down.at[layer], X.at[pl.ds(base, rows_down)])]
        else:
            start = 0 if kind == "attn" else 4 * D
            pairs = [
                (
                    own_in.at[layer, :, pl.ds(start + tile * D, D)],
                    X.at[pl.ds(base + tile * rows_in, rows_in)],
                )
                for tile in range(4)
            ]
        return [
            pltpu.make_async_copy(src, dst, ag_local.at[unit, index])
            for index, (src, dst) in enumerate(pairs)
        ]

    def weights_cast(unit):
        kind, layer = units[unit]
        base = (unit % 2) * stage
        for copy in weights_copies(unit):
            copy.wait()
        if kind == "patch":
            rows = pl.ds(aligned(here.shard * rows_patch, 16), rows_patch)
            wp[rows, :] = X[base : base + rows_patch, :].astype(BF)
        elif kind == "down":
            rows = pl.ds(aligned(here.shard * rows_down, 16), rows_down)
            wdn[layer, rows, :] = X[base : base + rows_down, :].astype(BF)
        else:
            start = 0 if kind == "attn" else 4 * D
            rows = pl.ds(aligned(here.shard * rows_in, 16), rows_in)
            for tile in range(4):
                win[layer, rows, start + tile * D : start + (tile + 1) * D] = X[
                    base + tile * rows_in : base + (tile + 1) * rows_in, :
                ].astype(BF)
        if unit + 2 < len(units):
            for copy in weights_copies(unit + 2):
                copy.start()

    def weights_start(unit):
        kind, layer = units[unit]
        part = x if parts_of(kind) > 1 else 0
        for o in range(1, n_y):
            go(
                lambda: weight(kind, layer, here.shard, part),
                weight(kind, layer, here.shard, part), ag, (unit, o),
                here.to(y=turn(y, o, n_y)),
            )
        go(
            lambda: weight(kind, layer, here.shard), weight(kind, layer, here.shard), ag,
            (unit, 0), mate,
        )

    def weights_forward(unit):
        kind, layer = units[unit]
        split = parts_of(kind) > 1
        part = x if split else 0
        for o in range(1, n_y):
            def make(o=o):
                return weight(kind, layer, turn(y, n_y - o, n_y) * 2 + c, part)

            arrived(make(), ag_recv.at[unit, o], ag_send.at[unit, o])
            if split:
                for p in range(1, n_x):
                    index = base_x + (o - 1) * (n_x - 1) + p - 1
                    go(make, make(), ag, (unit, index), here.to(x=turn(x, p, n_x)))
            go(make, make(), ag, (unit, base_my + o - 1), mate)

    def weights_pass(unit):
        kind, layer = units[unit]
        split = parts_of(kind) > 1
        part = x if split else 0
        if split:
            for o in range(1, n_y):
                for p in range(1, n_x):
                    index = (o - 1) * (n_x - 1) + p - 1

                    def make(o=o, p=p):
                        shard = turn(y, n_y - o, n_y) * 2 + c
                        return weight(kind, layer, shard, turn(x, n_x - p, n_x))

                    arrived(
                        make(), ag_recv.at[unit, base_x + index], ag_send.at[unit, base_x + index]
                    )
                    go(make, make(), ag, (unit, base_mx + index), mate)

    def weights_whole(unit):
        kind, layer = units[unit]
        split = parts_of(kind) > 1
        part = x if split else 0
        arrived(weight(kind, layer, y * 2 + 1 - c), ag_recv.at[unit, 0], ag_send.at[unit, 0])
        for o in range(1, n_y):
            shard = turn(y, n_y - o, n_y) * 2 + 1 - c
            index = base_my + o - 1
            arrived(weight(kind, layer, shard, part), ag_recv.at[unit, index], ag_send.at[unit, index])
            if split:
                for p in range(1, n_x):
                    index = base_mx + (o - 1) * (n_x - 1) + p - 1
                    piece = weight(kind, layer, shard, turn(x, n_x - p, n_x))
                    arrived(piece, ag_recv.at[unit, index], ag_send.at[unit, index])

    actions = {}

    def perform(names):
        for name in names:
            actions[name]()

    def at_place(place, *indices):
        for key, names in SCHEDULE.items():
            if key[0] != place:
                continue
            held = None
            for index, value in zip(indices, key[1:], strict=True):
                if not isinstance(index, int):
                    same = index == value
                    held = same if held is None else jnp.logical_and(held, same)
                elif index != value:
                    break
            else:
                if held is None:
                    perform(names)
                else:
                    pl.when(held)(functools.partial(perform, names))

    for unit in range(len(units)):
        actions[f"ws{unit}"] = functools.partial(weights_start, unit)
        actions[f"wf{unit}"] = functools.partial(weights_forward, unit)
        actions[f"wr{unit}"] = functools.partial(weights_pass, unit)
        actions[f"we{unit}"] = functools.partial(weights_whole, unit)

    lower = here.rep < n_rep // 2
    partner = here.to(z=turn(z, n_z // 2, n_z))
    back_half = pix.at[pl.ds(2, 2)]
    given = patches.at[pl.ds(KEPT, 2)]

    def local_half(half):
        return pltpu.make_async_copy(
            patches.at[pl.ds(2 * half, 2)], pix.at[pl.ds(2 * half, 2)], img_local.at[half]
        )

    def marks(pair):
        row = lax.broadcasted_iota(jnp.int32, (32, 128), 0)
        found = jnp.full((32, 128), -1.0, F32)
        for index in range(2):
            slot = 2 * pair + index
            value = jnp.where(slot < counts[0], labels[slot], -1).astype(F32)
            found = jnp.where(row == CLS - TAIL + 16 * index, value, found)
        return found

    local_half(0).start()
    for unit in range(2):
        for copy in weights_copies(unit):
            copy.start()
    lab[0] = marks(0)
    lab_given[...] = marks(2)

    @pl.when(jnp.logical_not(lower))
    def _():
        push(given, back_half, img_send.at[0], img_recv.at[0], partner)
        push(lab_given, lab.at[1], img_send.at[1], img_recv.at[1], partner)
        local_half(1).start()
        lab[1] = marks(1)

    for unit in range(len(units)):
        weights_cast(unit)
        at_place("cast", unit)

    even = lane_mask(128, 0, 64)
    odd = lane_mask(128, 64, 128)
    low_lane = lax.broadcasted_iota(jnp.int32, (1, 128), 1) < 64
    key_lane = lax.broadcasted_iota(jnp.int32, (1, BLK), 1)
    key_row = jnp.where((key_lane < PATCHES) | (key_lane == CLS), 0.0, -1e30)
    key_sub = lax.broadcasted_iota(jnp.int32, (BLK, 1), 0)
    key_column = jnp.where((key_sub < PATCHES) | (key_sub == CLS), 0.0, -1e30)
    whole_lanes = NCLS // 128 * 128
    low_head[:, 0:whole_lanes] = head[0:D, 0:whole_lanes].astype(BF)
    low_head[:, whole_lanes:] = jnp.zeros((D, CPAD - whole_lanes), BF)
    low_head[:, whole_lanes:NCLS] = head[0:D, whole_lanes:NCLS].astype(BF)
    head_bias[...] = jnp.zeros((1, CPAD), F32)
    head_bias[:, 0:NCLS] = head[D : D + 1, :]
    V[...] = jnp.zeros((VEC_ROWS, VEC_WIDE), F32)
    square_sum[...] = jnp.zeros((8, 128), F32)
    zeros = jnp.zeros((8, D), F32)
    patch_bias = glob[0:1, :]

    def whole_lanes_of(tile):
        return jnp.concatenate([tile] * (D // 128), axis=1)

    def vector(layer, at, size):
        return vecs[pl.ds(layer, 1), at : at + size]

    def store_vector(layer, at, row):
        for piece in range(row.shape[-1] // D):
            V[pl.ds(VEC_AT + 12 * layer + at // D + piece, 1), 0:D] = row[
                :, piece * D : (piece + 1) * D
            ]

    def store_sums(layer, parts):
        for at, part in parts:
            store_vector(layer, at, down_sum(part))

    def embed(half):
        made = mm(pix[pl.ds(2 * half, 2)].reshape(HALF, PATCH_DIM), wp[...])
        for image in range(2):
            start = aligned(half * HALF + image * BLK, 16)
            for at, size in pieces(PATCHES - 4):
                X[pl.ds(start + at, size), :] = (
                    made[image * BLK + at : image * BLK + at + size]
                    + pos[1 + at : 1 + at + size, :]
                    + patch_bias
                )
            X[pl.ds(start + TAIL, 16), :] = jnp.zeros((16, D), F32)
            X[pl.ds(start + TAIL, 4), :] = (
                made[image * BLK + TAIL : image * BLK + PATCHES]
                + pos[1 + TAIL : 1 + PATCHES, :]
                + patch_bias
            )
            X[pl.ds(start + CLS, 1), :] = glob[1:2, :] + pos[0:1, :]

    def first_norm(layer, half, columns):
        base = half * HALF
        gain, shift = vector(layer, 0, D), vector(layer, D, D)
        for at, size in pieces(HALF):
            rows = pl.ds(aligned(base + at, 16), size)
            normed, inverse = norm(X[rows, :])
            N1[layer, rows, :] = normed.astype(BF)
            I1[layer, rows, :] = jnp.broadcast_to(inverse, (size, 128))
            DXB[rows, :] = (normed * gain + shift).astype(BF)
        rows = pl.ds(aligned(base, 16), HALF)
        h1 = DXB[rows, :]
        for tile in columns:
            made = mm(h1, win[layer, :, tile * D : (tile + 1) * D])
            if tile == 0:
                made = made + vector(layer, 2 * D, D)
            if tile == 2:
                made = made + vector(layer, 3 * D, D)
            if len(columns) == 3:
                QKV[layer, rows, tile * D : (tile + 1) * D] = made.astype(BF)
            else:
                (DMB if tile == 1 else DA)[rows, :] = made.astype(BF)

    ones = jnp.full((BLK, 128), 1.0, BF)

    def attend(layer, image):
        rows = pl.ds(aligned(image * BLK, 16), BLK)
        for pair in range(3):
            at = pair * 128
            query = QKV[layer, rows, at : at + 128] * BF(0.125)
            keys = QKV[layer, rows, D + at : D + at + 128]
            values = QKV[layer, rows, 2 * D + at : 2 * D + at + 128]
            both = jnp.concatenate([query * even, query * odd], axis=0)
            scores = mm_nt(both, keys)
            probs = []
            for row, size in pieces(HALF):
                part = scores[row : row + size] + key_row
                probs.append(jnp.exp(part - jnp.max(part, axis=-1, keepdims=True)).astype(BF))
            probs = jnp.concatenate(probs, axis=0)
            first = mm(probs[:BLK], jnp.concatenate([values * even, ones], axis=1))
            second = mm(probs[BLK:], jnp.concatenate([values * odd, ones], axis=1))
            made = first[:, :128] * (1.0 / first[:, 128:])
            made = made + second[:, :128] * (1.0 / second[:, 128:])
            ATT[layer, rows, at : at + 128] = made.astype(BF)

    def mlp(layer, half):
        base = half * HALF
        whole = pl.ds(aligned(base, 16), HALF)
        made = mm(ATT[layer, whole, :], win[layer, :, 3 * D : 4 * D])
        bias_out = vector(layer, 4 * D, D)
        gain, shift = vector(layer, 5 * D, D), vector(layer, 6 * D, D)
        for at, size in pieces(HALF):
            rows = pl.ds(aligned(base + at, 16), size)
            middle = X[rows, :] + made[at : at + size] + bias_out
            X[rows, :] = middle
            normed, inverse = norm(middle)
            N2[layer, rows, :] = normed.astype(BF)
            I2[layer, rows, :] = jnp.broadcast_to(inverse, (size, 128))
            DXB[rows, :] = (normed * gain + shift).astype(BF)
        at_place("mid", half, layer)
        at_place("b_up", half, layer)
        h2 = DXB[whole, :]
        for tile in range(4):
            columns = slice(tile * D, (tile + 1) * D)
            made = mm(h2, win[layer, :, (4 + tile) * D : (5 + tile) * D])
            bias = vector(layer, 7 * D + tile * D, D)
            for at, size in pieces(HALF):
                rows = pl.ds(aligned(base + at, 16), size)
                active, slope = gelu_parts(made[at : at + size] + bias)
                ACT[layer, rows, columns] = active.astype(BF)
                SLOPE[layer, rows, columns] = slope.astype(BF)
        at_place("up", half, layer)
        at_place("b_down", half, layer)
        made = mm(ACT[layer, whole, :], wdn[layer])
        bias = vector(layer, 7 * D + FF, D)
        for at, size in pieces(HALF):
            rows = pl.ds(aligned(base + at, 16), size)
            X[rows, :] = X[rows, :] + made[at : at + size] + bias
        at_place("down", half, layer)

    at_place("b_start")

    def forward_half(half, carry):
        @pl.when(half == 0)
        def _():
            local_half(0).wait()

        @pl.when(jnp.logical_and(half == 1, lower))
        def _():
            arrived(back_half, img_recv.at[0], img_send.at[0])

        @pl.when(jnp.logical_and(half == 1, jnp.logical_not(lower)))
        def _():
            local_half(1).wait()

        embed(half)
        at_place("embed", half)

        def forward_layer(layer, inner):
            at_place("b_norm", half, layer)
            first_norm(layer, half, (0, 1, 2))
            at_place("norm", half, layer)

            def attend_one(index, nothing):
                attend(layer, 2 * half + index)
                at_place("att", half, layer, index)
                return nothing

            lax.fori_loop(0, 2, attend_one, 0)
            mlp(layer, half)
            return inner

        return lax.fori_loop(0, LAYERS - 1, forward_layer, carry)

    lax.fori_loop(0, 2, forward_half, 0)
    at_place("b_last")

    last = LAYERS - 1

    def last_norm(half, nothing):
        first_norm(last, half, (1, 2))
        at_place("ln", half)
        return nothing

    lax.fori_loop(0, 2, last_norm, 0)

    fac = ("f", f_send, f_recv)
    f_y, f_z = 1, n_y
    f_x = f_z + n_z - 1
    f_m = f_x + n_x - 1
    group = KEPT * n_shard

    def factors_core():
        go(lambda: FAC.at[1 - c], FC, fac, 0, mate)

    def factors_y():
        arrived(FC, f_recv.at[0], f_send.at[0])
        FAC[c] = FAC[c] + FC[...]
        for o in range(1, n_y):
            go(lambda: FAC.at[c], FY.at[o - 1], fac, f_y + o - 1, here.to(y=turn(y, o, n_y)))

    def factors_z():
        total = FAC[c]
        for o in range(1, n_y):
            arrived(FY.at[o - 1], f_recv.at[f_y + o - 1], f_send.at[f_y + o - 1])
            total = total + FY[o - 1]
        FALL[z] = total
        for o in range(1, n_z):
            go(
                lambda: FALL.at[z], FALL.at[z], fac, f_z + o - 1,
                here.to(z=turn(z, o, n_z)),
            )

    def factors_x():
        for o in range(1, n_z):
            index = f_z + o - 1
            arrived(FALL.at[turn(z, n_z - o, n_z)], f_recv.at[index], f_send.at[index])
        pltpu.make_async_copy(FALL, all_factors.at[c, x], out_local.at[0]).start()
        for o in range(1, n_x):
            go(
                lambda: FALL, all_factors.at[c, x], fac, f_x + o - 1,
                here.to(x=turn(x, o, n_x)),
            )

    def factors_mate():
        for o in range(1, n_x):
            index = f_x + o - 1
            came = all_factors.at[c, turn(x, n_x - o, n_x)]
            arrived(came, f_recv.at[index], f_send.at[index])
        pltpu.make_async_copy(FALL, all_factors.at[c, x], out_local.at[0]).wait()
        go(lambda: all_factors.at[c], all_factors.at[c], fac, f_m, mate)

    def factors_done():
        arrived(all_factors.at[1 - c], f_recv.at[f_m], f_send.at[f_m])

    rs = ("rs", rs_send, rs_recv)
    r_y, r_x = 1, n_y
    r_z = r_x + n_x - 1
    r_gz = r_z + n_z - 1
    r_gx = r_gz + n_z - 1

    def chunk(k):
        if k < CHUNKS:
            slot = k % 3
            return (
                G.at[k], RC.at[slot], RY.at[slot], RX.at[slot], RZ.at[slot], RES.at[k], block
            )
        k = k - CHUNKS
        return GS.at[k], SC.at[0], SY.at[0], SX.at[0], SZ.at[0], SRES.at[k], block // 2

    def splits(rows):
        by_x = cut(rows, n_x, 16)
        by_z = cut(rows // by_x, n_z, 16)
        return by_x, rows // by_x, by_z, rows // by_x // by_z

    def add_rows(rows, target, target_at, sources):
        step = 48 if rows % 48 == 0 else 16

        def one(index, nothing):
            at = index * step
            to = pl.ds(aligned(target_at + at, 16), step)
            total = target[to, :]
            if len(sources) == 1:
                total = total + sources[0][pl.ds(aligned(at, 16), step), :]
            else:
                total = total.astype(F32)
                for source in sources:
                    total = total + source[pl.ds(aligned(at, 16), step), :].astype(F32)
                total = total.astype(BF)
            target[to, :] = total
            return nothing

        lax.fori_loop(0, rows // step, one, 0)

    def reduce_core(k):
        g, rc = chunk(k)[0:2]
        go(lambda: chunk(k)[0].at[:, 1 - c], rc, rs, (k, 0), mate)

    def reduce_y(k):
        g, rc, ry, _, _, _, rows = chunk(k)
        arrived(rc, rs_recv.at[k, 0], rs_send.at[k, 0])
        for o in list(range(1, n_y)) + [0]:
            at = turn(y, o, n_y)
            add_rows(rows, g.at[at, c], 0, [rc.at[at]])
            if o:
                go(
                    lambda o=o: chunk(k)[0].at[turn(y, o, n_y), c], ry.at[o - 1], rs,
                    (k, r_y + o - 1), here.to(y=at),
                )

    def total_of(slots, count, at, step):
        total = None
        for index in range(count):
            value = slots[index, pl.ds(aligned(at, 16), step), :].astype(F32)
            total = value if total is None else total + value
        return total

    def reduce_x(k):
        g, _, ry, rx, _, _, rows = chunk(k)
        by_x, rows_x = splits(rows)[0:2]
        for o in range(1, n_y):
            arrived(ry.at[o - 1], rs_recv.at[k, r_y + o - 1], rs_send.at[k, r_y + o - 1])
        mine = g.at[y, c]
        add_rows(rows, mine, 0, [ry.at[o - 1] for o in range(1, n_y)])
        for o in range(1, n_x):
            to = turn(x, o, n_x)
            if by_x > 1:

                def make(o=o):
                    at = turn(x, o, n_x) * rows_x
                    return chunk(k)[0].at[y, c, pl.ds(aligned(at, 16), rows_x), :]

                go(make, rx.at[o - 1], rs, (k, r_x + o - 1), here.to(x=to))
            else:
                go(lambda: chunk(k)[0].at[y, c], rx.at[x], rs, (k, r_x + o - 1), here.to(x=to))

    def reduce_z(k):
        g, _, _, rx, rz, _, rows = chunk(k)
        by_x, rows_x, by_z, rows_z = splits(rows)
        mine = g.at[y, c]
        for o in range(1, n_x):
            slot = rx.at[o - 1] if by_x > 1 else rx.at[turn(x, n_x - o, n_x)]
            arrived(slot, rs_recv.at[k, r_x + o - 1], rs_send.at[k, r_x + o - 1])
        if by_x > 1:
            start = x * rows_x
            add_rows(rows_x, mine, start, [rx.at[o - 1] for o in range(1, n_x)])
        else:
            start = 0
            rx[x] = mine[...]
            for o in range(1, n_x):
                gone(rs, (k, r_x + o - 1))
            step = 48 if rows % 48 == 0 else 16

            def one(index, nothing):
                at = pl.ds(aligned(index * step, 16), step)
                g[y, c, at, :] = total_of(rx, n_x, index * step, step).astype(BF)
                return nothing

            lax.fori_loop(0, rows // step, one, 0)
        for o in range(1, n_z):

            def make(o=o):
                at = x * rows_x if by_x > 1 else 0
                if by_z > 1:
                    at = at + turn(z, o, n_z) * rows_z
                return chunk(k)[0].at[y, c, pl.ds(aligned(at, 16), rows_z), :]

            slot = rz.at[o - 1] if by_z > 1 else rz.at[z]
            go(make, slot, rs, (k, r_z + o - 1), here.to(z=turn(z, o, n_z)))

    def gather_z(k):
        g, _, _, _, rz, res, rows = chunk(k)
        by_x, rows_x, by_z, rows_z = splits(rows)
        start = x * rows_x if by_x > 1 else 0
        if by_z > 1:
            start = start + z * rows_z
        for o in range(1, n_z):
            slot = rz.at[o - 1] if by_z > 1 else rz.at[turn(z, n_z - o, n_z)]
            arrived(slot, rs_recv.at[k, r_z + o - 1], rs_send.at[k, r_z + o - 1])
        own_slot = n_z - 1 if by_z > 1 else z
        rz[own_slot] = g[y, c, pl.ds(aligned(start, 16), rows_z), :]
        share = 1.0 / ((1 if by_x > 1 else n_x) * (1 if by_z > 1 else n_z))
        step = 48 if rows_z % 48 == 0 else 16

        def one(index, total):
            low = total_of(rz, n_z, index * step, step).astype(BF)
            res[pl.ds(aligned(start + index * step, 16), step), :] = low
            wide = low.astype(F32)
            return total + fold(wide * wide)

        total = lax.fori_loop(0, rows_z // step, one, zeros) * share
        for at in range(0, D, 128):
            square_sum[...] = square_sum[...] + total[:, at : at + 128]
        if by_z > 1:

            def make():
                at = x * rows_x if by_x > 1 else 0
                return chunk(k)[5].at[pl.ds(aligned(at + z * rows_z, 16), rows_z), :]

            for o in range(1, n_z):
                go(make, make(), rs, (k, r_gz + o - 1), here.to(z=turn(z, o, n_z)))

    def gather_x(k):
        res, rows = chunk(k)[5:7]
        by_x, rows_x, by_z, rows_z = splits(rows)
        if by_z > 1:
            for o in range(1, n_z):
                start = turn(z, n_z - o, n_z) * rows_z
                if by_x > 1:
                    start = start + x * rows_x
                arrived(
                    res.at[pl.ds(aligned(start, 16), rows_z), :],
                    rs_recv.at[k, r_gz + o - 1], rs_send.at[k, r_gz + o - 1],
                )
        if by_x > 1:

            def make():
                return chunk(k)[5].at[pl.ds(aligned(x * rows_x, 16), rows_x), :]

            for o in range(1, n_x):
                go(make, make(), rs, (k, r_gx + o - 1), here.to(x=turn(x, o, n_x)))

    def result(k):
        if k < CHUNKS:
            return pltpu.make_async_copy(RES.at[k], res_out.at[k], out_local.at[1 + k])
        return pltpu.make_async_copy(
            SRES.at[k - CHUNKS], small_out.at[k - CHUNKS], out_local.at[1 + k]
        )

    def gather_done(k):
        res, rows = chunk(k)[5:7]
        by_x, rows_x = splits(rows)[0:2]
        if by_x > 1:
            for o in range(1, n_x):
                start = turn(x, n_x - o, n_x) * rows_x
                arrived(
                    res.at[pl.ds(aligned(start, 16), rows_x), :],
                    rs_recv.at[k, r_gx + o - 1], rs_send.at[k, r_gx + o - 1],
                )
        result(k).start()

    for k in range(CHUNKS + 2):
        actions[f"core{k}"] = functools.partial(reduce_core, k)
        actions[f"y{k}"] = functools.partial(reduce_y, k)
        actions[f"x{k}"] = functools.partial(reduce_x, k)
        actions[f"z{k}"] = functools.partial(reduce_z, k)
        actions[f"gz{k}"] = functools.partial(gather_z, k)
        actions[f"gx{k}"] = functools.partial(gather_x, k)
        actions[f"gd{k}"] = functools.partial(gather_done, k)
    actions.update(
        fc=factors_core, fy=factors_y, fz=factors_z, fx=factors_x, fm=factors_mate,
        fd=factors_done,
    )

    def tails(ref, layer=None):
        found = []
        for image in range(KEPT):
            rows = slice(image * BLK + TAIL, (image + 1) * BLK)
            found.append(ref[rows, :] if layer is None else ref[layer, rows, :])
        return jnp.concatenate(found, axis=0)

    @pl.when(lower)
    def _():
        arrived(lab.at[1], img_recv.at[1], img_send.at[1])

    marked = lab[...].reshape(CROWS, 128)[:, 0:1]

    h1 = tails(DXB)
    stream = tails(X)
    query = ((mm(h1, win[last, :, 0:D]) + vector(last, 2 * D, D)).astype(BF)) * BF(0.125)
    head_masks = [lane_mask(D, index * 64, (index + 1) * 64) for index in range(HEADS)]

    def spread(values):
        return jnp.concatenate([values * mask for mask in head_masks], axis=0)

    def gather_heads(values):
        total = None
        for index in range(HEADS):
            part = values[index * 16 : (index + 1) * 16] * head_masks[index].astype(F32)
            total = part if total is None else total + part
        return total

    spread_queries, probabilities, outs = [], [], []
    for image in range(KEPT):
        rows = slice(image * BLK, (image + 1) * BLK)
        queries = spread(query[image * 16 : (image + 1) * 16])
        scores = mm_nt(queries, DMB[rows, :]) + key_row
        raw = jnp.exp(scores - jnp.max(scores, axis=-1, keepdims=True))
        probs = raw * (1.0 / jnp.sum(raw, axis=-1, keepdims=True))
        spread_queries.append(queries)
        probabilities.append(probs)
        outs.append(gather_heads(mm(probs.astype(BF), DA[rows, :])))
    attended = jnp.concatenate(outs, axis=0).astype(BF)
    middle = stream + mm(attended, win[last, :, 3 * D : 4 * D]) + vector(last, 4 * D, D)
    n2, i2 = norm(middle)
    h2 = (n2 * vector(last, 5 * D, D) + vector(last, 6 * D, D)).astype(BF)
    active, slope = gelu_parts(mm(h2, win[last, :, 4 * D :]) + vector(last, 7 * D, FF))
    active = active.astype(BF)
    top = middle + mm(active, wdn[last]) + vector(last, 7 * D + FF, D)
    gain_final = glob[2:3, :]
    nf, inf = norm(top)
    final = (nf * gain_final + glob[3:4, :]).astype(BF)
    class_lane = lax.broadcasted_iota(jnp.int32, (1, CPAD), 1)
    logits = mm(final, low_head[...]) + head_bias[...]
    logits = jnp.where(class_lane < NCLS, logits, -1e30)
    peak = jnp.max(logits, axis=-1, keepdims=True)
    shifted = logits - peak
    raw = jnp.exp(shifted)
    total = jnp.sum(raw, axis=-1, keepdims=True)
    alive = jnp.where(marked >= 0.0, 1.0, 0.0)
    target = jnp.where(class_lane.astype(F32) == marked, 1.0 - SMOOTHING, 0.0) + jnp.where(
        class_lane < NCLS, SMOOTHING / NCLS, 0.0
    )
    log_probs = jnp.where(class_lane < NCLS, shifted - jnp.log(total), 0.0)
    losses = -jnp.sum(target * log_probs, axis=-1, keepdims=True) * alive
    d_logits = ((raw * (1.0 / total) - target) * alive).astype(BF)
    d_final = mm_nt(d_logits, low_head[...])
    last_row = VEC_AT + 12 * LAYERS
    V[last_row : last_row + 1, 0:D] = down_sum(d_final * nf)
    V[last_row + 1 : last_row + 2, 0:D] = down_sum(d_final)
    V[last_row + 2 : last_row + 3, 0:128] = jnp.broadcast_to(down_sum(losses), (1, 128))
    V[last_row + 3 : last_row + 4, 0:128] = jnp.full((1, 128), counts[0].astype(F32), F32)
    d_top = norm_back(d_final, nf, inf, gain_final)
    low_top = d_top.astype(BF)
    store_vector(last, 7 * D + FF, down_sum(d_top))
    d_up = (mm_nt(low_top, wdn[last]) * slope).astype(BF)
    store_vector(last, 7 * D, down_sum(d_up.astype(F32)))
    d_h2 = mm_nt(d_up, win[last, :, 4 * D :])
    store_vector(last, 5 * D, down_sum(d_h2 * n2))
    store_vector(last, 6 * D, down_sum(d_h2))
    d_middle = d_top + norm_back(d_h2, n2, i2, vector(last, 5 * D, D))
    low_middle = d_middle.astype(BF)
    store_vector(last, 4 * D, down_sum(d_middle))
    d_heads = mm_nt(low_middle, win[last, :, 3 * D : 4 * D]).astype(BF)
    d_queries = []
    for image in range(KEPT):
        rows = slice(image * BLK, (image + 1) * BLK)
        ups = spread(d_heads[image * 16 : (image + 1) * 16])
        probs = probabilities[image]
        d_probs = mm_nt(ups, DA[rows, :])
        inner = jnp.sum(d_probs * probs, axis=-1, keepdims=True)
        d_scores = (probs * (d_probs - inner)).astype(BF)
        d_queries.append(gather_heads(mm(d_scores, DMB[rows, :])) * 0.125)
        DMB[rows, :] = mm_tn(d_scores, spread_queries[image]).astype(BF)
        DA[rows, :] = mm_tn(probs.astype(BF), ups).astype(BF)
    d_query = jnp.concatenate(d_queries, axis=0).astype(BF)
    store_vector(last, 2 * D, down_sum(d_query.astype(F32)))
    from_query = mm_nt(d_query, win[last, :, 0:D])

    pick_row = lax.broadcasted_iota(jnp.int32, (group, CROWS), 0)
    pick_lane = lax.broadcasted_iota(jnp.int32, (group, CROWS), 1)
    pick = jnp.where(
        ((pick_row - KEPT * here.shard) * 16 + (CLS - TAIL)) == pick_lane, 1.0, 0.0
    ).astype(BF)
    at = 0
    for piece in (active, h2, attended, h1, final, low_top):
        FAC[0, :, at : at + piece.shape[-1]] = mm(pick, piece).astype(BF)
        at += piece.shape[-1]
    at = 0
    for piece in (d_up, low_middle, d_query, d_logits):
        FAC[1, :, at : at + piece.shape[-1]] = mm(pick, piece).astype(BF)
        at += piece.shape[-1]
    FAC[1, :, at:] = jnp.zeros((group, WFAC - at), BF)
    at_place("class")

    turned = DXB[...].T
    for tile, grads in enumerate((DMB, DA)):
        made = mm(turned, grads[...]).astype(BF)
        for shard in range(n_shard):
            GS[0, shard // 2, shard % 2, tile * rows_in : (tile + 1) * rows_in, :] = made[
                shard * rows_in : (shard + 1) * rows_in
            ]
    at_place("kv")
    store_sums(last, [(3 * D, fold(DA[...].astype(F32)))])

    X[...] = jnp.zeros((ROWS, D), F32)
    gain = vector(last, 0, D)
    gain_sum, shift_sum = zeros, zeros
    for image in range(KEPT):
        rows = slice(image * BLK + TAIL, (image + 1) * BLK)
        part = from_query[image * 16 : (image + 1) * 16]
        normed = N1[last, rows, :].astype(F32)
        gain_sum = gain_sum + fold(part * normed)
        shift_sum = shift_sum + fold(part)
        X[rows, :] = d_middle[image * 16 : (image + 1) * 16] + norm_back(
            part, normed, whole_lanes_of(I1[last, rows, :]), gain
        )

    def first_back(layer, half, made, sums):
        base = half * HALF
        gain = vector(layer, 0, D)
        gain_sum, shift_sum = sums
        for at, size in pieces(HALF):
            rows = pl.ds(aligned(base + at, 16), size)
            part = made[at : at + size]
            normed = N1[layer, rows, :].astype(F32)
            inverse = whole_lanes_of(I1[layer, rows, :])
            gain_sum = gain_sum + fold(part * normed)
            shift_sum = shift_sum + fold(part)
            X[rows, :] = X[rows, :] + norm_back(part, normed, inverse, gain)
        return gain_sum, shift_sum

    def last_back(half, sums):
        rows = pl.ds(aligned(half * HALF, 16), HALF)
        made = mm_nt(DMB[rows, :], win[last, :, D : 2 * D])
        made = made + mm_nt(DA[rows, :], win[last, :, 2 * D : 3 * D])
        sums = first_back(last, half, made, sums)
        at_place("lb", half)
        return sums

    gain_sum, shift_sum = lax.fori_loop(0, 2, last_back, (gain_sum, shift_sum))
    store_sums(last, [(0, gain_sum), (D, shift_sum)])

    def round_up(half, total):
        for at, size in pieces(HALF):
            rows = pl.ds(aligned(half * HALF + at, 16), size)
            up = X[rows, :]
            DXB[rows, :] = up.astype(BF)
            total = total + fold(up)
        return total

    def act_back(layer, half, totals):
        base = half * HALF
        low = DXB[pl.ds(aligned(base, 16), HALF), :]
        ups = []
        for tile in range(4):
            columns = slice(tile * D, (tile + 1) * D)
            made = mm_nt(low, wdn[layer, columns, :])
            total = totals[tile]
            for at, size in pieces(HALF):
                rows = pl.ds(aligned(base + at, 16), size)
                grad = (made[at : at + size] * SLOPE[layer, rows, columns].astype(F32)).astype(BF)
                DH[rows, columns] = grad
                total = total + fold(grad.astype(F32))
            ups.append(total)
        return tuple(ups)

    def mlp_back(layer, half, sums):
        base = half * HALF
        whole = pl.ds(aligned(base, 16), HALF)
        gain_sum, shift_sum, bias_out = sums
        made = mm_nt(DH[whole, :], win[layer, :, 4 * D :])
        gain = vector(layer, 5 * D, D)
        for at, size in pieces(HALF):
            rows = pl.ds(aligned(base + at, 16), size)
            part = made[at : at + size]
            normed = N2[layer, rows, :].astype(F32)
            inverse = whole_lanes_of(I2[layer, rows, :])
            gain_sum = gain_sum + fold(part * normed)
            shift_sum = shift_sum + fold(part)
            grad = X[rows, :] + norm_back(part, normed, inverse, gain)
            X[rows, :] = grad
            DMB[rows, :] = grad.astype(BF)
            bias_out = bias_out + fold(grad)
        DA[whole, :] = mm_nt(DMB[whole, :], win[layer, :, 3 * D : 4 * D]).astype(BF)
        return gain_sum, shift_sum, bias_out

    def attend_back(layer, image):
        rows = pl.ds(aligned(image * BLK, 16), BLK)
        for pair in range(3):
            at = pair * 128
            query = QKV[layer, rows, at : at + 128] * BF(0.125)
            keys = QKV[layer, rows, D + at : D + at + 128]
            values = QKV[layer, rows, 2 * D + at : 2 * D + at + 128]
            ups = DA[rows, at : at + 128]
            keys_both = jnp.concatenate([keys * even, keys * odd], axis=0)
            values_both = jnp.concatenate([values * even, values * odd], axis=0)
            scores = mm_nt(keys_both, query)
            d_probs = mm_nt(values_both, ups)
            probs, d_scores = [], []
            for base in (0, BLK):
                low_probs, low_grads = [], []
                for first, end in ((0, 128), (128, BLK)):
                    part = jnp.concatenate(
                        [
                            scores[base : base + TAIL, first:end],
                            scores[base + TAIL : base + BLK, first:end] + key_column[TAIL:],
                        ],
                        axis=0,
                    )
                    raw = jnp.exp(part - jnp.max(part, axis=0, keepdims=True))
                    prob = raw * (1.0 / jnp.sum(raw, axis=0, keepdims=True))
                    grad = d_probs[base : base + BLK, first:end]
                    inner = jnp.sum(grad * prob, axis=0, keepdims=True)
                    low_grads.append((prob * (grad - inner)).astype(BF))
                    low_probs.append(prob.astype(BF))
                probs.append(jnp.concatenate(low_probs, axis=1))
                d_scores.append(jnp.concatenate(low_grads, axis=1))
            probs = jnp.concatenate(probs, axis=0)
            d_scores = jnp.concatenate(d_scores, axis=0)
            d_values = mm(probs, ups)
            d_keys = mm(d_scores, query)
            d_query = mm_tn(d_scores, keys_both) * 0.125
            DH[rows, at : at + 128] = d_query.astype(BF)
            DH[rows, D + at : D + at + 128] = jnp.where(
                low_lane, d_keys[:BLK], d_keys[BLK:]
            ).astype(BF)
            DH[rows, 2 * D + at : 2 * D + at + 128] = jnp.where(
                low_lane, d_values[:BLK], d_values[BLK:]
            ).astype(BF)

    def renew(ref, layer, at):
        gain, shift = vector(layer, at, D), vector(layer, at + D, D)

        def one(index, nothing):
            rows = pl.ds(aligned(index * 64, 16), 64)
            DXB[rows, :] = (ref[layer, rows, :].astype(F32) * gain + shift).astype(BF)
            return nothing

        lax.fori_loop(0, ROWS // 64, one, 0)
        return DXB[...].T

    def keep_in(k, tile, made):
        for shard in range(n_shard):
            G[k, shard // 2, shard % 2, tile * rows_in : (tile + 1) * rows_in, :] = made[
                shard * rows_in : (shard + 1) * rows_in
            ]

    def backward(step, carry):
        layer = LAYERS - 2 - step
        kd, ku, kq = 3 * step, 3 * step + 1, 3 * step + 2
        bias_down = lax.fori_loop(0, 2, round_up, zeros)
        at_place("round", layer)
        turned = DXB[...].T
        per = min(rows_down, D)
        for tile in range(4):
            columns = slice(tile * D, (tile + 1) * D)
            made = mm(turned, ACT[layer, :, columns]).astype(BF).T
            for piece in range(D // per):
                shard, at = divmod(tile * D + piece * per, rows_down)
                G[kd, shard // 2, shard % 2, at : at + per, :] = made[
                    piece * per : (piece + 1) * per
                ]
        at_place("dn", layer)

        def one(half, totals):
            totals = act_back(layer, half, totals)
            at_place("act", layer, half)
            return totals

        bias_up = lax.fori_loop(0, 2, one, (zeros,) * 4)
        turned = renew(N2, layer, 5 * D)
        for tile in range(4):
            keep_in(ku, tile, mm(turned, DH[:, tile * D : (tile + 1) * D]).astype(BF))
        at_place("ups", layer)

        def one_more(half, sums):
            sums = mlp_back(layer, half, sums)
            at_place("mlpb", layer, half)
            return sums

        gain_sum, shift_sum, bias_out = lax.fori_loop(0, 2, one_more, (zeros, zeros, zeros))
        store_sums(
            layer,
            [(7 * D + FF, bias_down), (5 * D, gain_sum), (6 * D, shift_sum), (4 * D, bias_out)]
            + [(7 * D + tile * D, bias_up[tile]) for tile in range(4)],
        )
        keep_in(kq, 3, mm(ATT[layer].T, DMB[...]).astype(BF))
        at_place("out", layer)

        def two(image, nothing):
            attend_back(layer, image)
            at_place("attb", layer, image)
            return nothing

        lax.fori_loop(0, KEPT, two, 0)
        turned = renew(N1, layer, 0)
        for tile in range(3):
            keep_in(
                kq, tile, mm(turned, DH[:, tile * D : (tile + 1) * D]).astype(BF)
            )
        at_place("qkv", layer)
        store_sums(
            layer,
            [
                (2 * D, fold(DH[:, 0:D].astype(F32))),
                (3 * D, fold(DH[:, 2 * D : 3 * D].astype(F32))),
            ],
        )

        def three(half, sums):
            rows = pl.ds(aligned(half * HALF, 16), HALF)
            made = mm_nt(DH[rows, 0 : 3 * D], win[layer, :, 0 : 3 * D])
            sums = first_back(layer, half, made, sums)
            at_place("fb", layer, half)
            return sums

        gain_sum, shift_sum = lax.fori_loop(0, 2, three, (zeros, zeros))
        store_sums(layer, [(0, gain_sum), (D, shift_sum)])
        return carry

    lax.fori_loop(0, LAYERS - 1, backward, 0)

    for at, size in pieces(BLK):
        total = None
        for image in range(KEPT):
            part = X[image * BLK + at : image * BLK + at + size, :]
            DXB[image * BLK + at : image * BLK + at + size, :] = part.astype(BF)
            total = part if total is None else total + part
        V[at : at + size, 0:D] = total

    vec = ("v", v_send, v_recv)
    v_y, v_x = 1, n_y
    v_z = v_x + n_x - 1
    v_gz = v_z + n_z - 1
    v_gx = v_gz + n_z - 1
    v_gy = v_gx + n_x - 1
    v_gc = v_gy + n_y - 1
    rows_c = VEC_ROWS // 2
    rows_y = rows_c // n_y
    rows_x = rows_y // n_x
    split_z = cut(rows_x, n_z, 8)
    rows_z = rows_x // split_z
    at_c = c * rows_c
    at_y = at_c + y * rows_y
    at_x = at_y + x * rows_x
    at_z = at_x + z * rows_z if split_z > 1 else at_x

    def vrows(ref, at, rows):
        return ref.at[pl.ds(aligned(at, 8), rows), :]

    def vadd(at, rows, sources):
        target = pl.ds(aligned(at, 8), rows)
        total = V[target, :]
        for source in sources:
            total = total + source
        V[target, :] = total

    def vectors_core():
        go(lambda: vrows(V, (1 - c) * rows_c, rows_c), VC, vec, 0, mate)

    def vectors_y():
        arrived(VC, v_recv.at[0], v_send.at[0])
        vadd(at_c, rows_c, [VC[...]])
        for o in range(1, n_y):
            to = turn(y, o, n_y)
            go(
                lambda o=o: vrows(V, at_c + turn(y, o, n_y) * rows_y, rows_y), VY.at[o - 1],
                vec, v_y + o - 1, here.to(y=to),
            )

    def vectors_x():
        for o in range(1, n_y):
            arrived(VY.at[o - 1], v_recv.at[v_y + o - 1], v_send.at[v_y + o - 1])
        vadd(at_y, rows_y, [VY[o - 1] for o in range(1, n_y)])
        for o in range(1, n_x):
            to = turn(x, o, n_x)
            go(
                lambda o=o: vrows(V, at_y + turn(x, o, n_x) * rows_x, rows_x), VX.at[o - 1],
                vec, v_x + o - 1, here.to(x=to),
            )

    def vectors_z():
        for o in range(1, n_x):
            arrived(VX.at[o - 1], v_recv.at[v_x + o - 1], v_send.at[v_x + o - 1])
        vadd(at_x, rows_x, [VX[o - 1] for o in range(1, n_x)])
        for o in range(1, n_z):

            def make(o=o):
                at = at_x + turn(z, o, n_z) * rows_z if split_z > 1 else at_x
                return vrows(V, at, rows_z)

            go(make, VZ.at[z], vec, v_z + o - 1, here.to(z=turn(z, o, n_z)))

    def vectors_gather_z():
        for o in range(1, n_z):
            arrived(
                VZ.at[turn(z, n_z - o, n_z)], v_recv.at[v_z + o - 1], v_send.at[v_z + o - 1]
            )
        target = pl.ds(aligned(at_z, 8), rows_z)
        VZ[z] = V[target, :]
        total = VZ[0]
        for index in range(1, n_z):
            total = total + VZ[index]
        VF[target, :] = total
        if split_z > 1:
            for o in range(1, n_z):
                go(
                    lambda: vrows(VF, at_z, rows_z), vrows(VF, at_z, rows_z), vec, v_gz + o - 1,
                    here.to(z=turn(z, o, n_z)),
                )

    def vectors_gather_x():
        if split_z > 1:
            for o in range(1, n_z):
                came = turn(z, n_z - o, n_z)
                arrived(
                    vrows(VF, at_x + came * rows_z, rows_z), v_recv.at[v_gz + o - 1],
                    v_send.at[v_gz + o - 1],
                )
        for o in range(1, n_x):
            go(
                lambda: vrows(VF, at_x, rows_x), vrows(VF, at_x, rows_x), vec, v_gx + o - 1,
                here.to(x=turn(x, o, n_x)),
            )

    sq = ("q", q_send, q_recv)

    def squares_z():
        SQ[0] = square_sum[...]
        SQZ[z] = square_sum[...]
        for o in range(1, n_z):
            go(lambda: SQ.at[0], SQZ.at[z], sq, o - 1, here.to(z=turn(z, o, n_z)))

    def slot_of(i, j, k):
        return (i * n_y + j) * 2 + k

    def squares_plane():
        for o in range(1, n_z):
            arrived(SQZ.at[turn(z, n_z - o, n_z)], q_recv.at[o - 1], q_send.at[o - 1])
        total = SQZ[0]
        for index in range(1, n_z):
            total = total + SQZ[index]
        SQ[1] = total
        SQP[slot_of(x, y, c)] = total
        for index, step in enumerate(plane):
            go(
                lambda: SQ.at[1], SQP.at[slot_of(x, y, c)], sq, n_z - 1 + index,
                in_plane(step),
            )

    def squares_done():
        for index, (i, j, k) in enumerate(plane):
            slot = slot_of(
                turn(x, n_x - i, n_x), turn(y, n_y - j, n_y), lax.rem(c + k, 2)
            )
            arrived(SQP.at[slot], q_recv.at[n_z - 1 + index], q_send.at[n_z - 1 + index])
        total = SQP[0]
        for index in range(1, 2 * n_x * n_y):
            total = total + SQP[index]
        SQ[2] = total

    def vectors_gather_y():
        for o in range(1, n_x):
            at = at_y + turn(x, n_x - o, n_x) * rows_x
            arrived(vrows(VF, at, rows_x), v_recv.at[v_gx + o - 1], v_send.at[v_gx + o - 1])
        for o in range(1, n_y):
            go(
                lambda: vrows(VF, at_y, rows_y), vrows(VF, at_y, rows_y), vec, v_gy + o - 1,
                here.to(y=turn(y, o, n_y)),
            )

    def vectors_gather_core():
        for o in range(1, n_y):
            at = at_c + turn(y, n_y - o, n_y) * rows_y
            arrived(vrows(VF, at, rows_y), v_recv.at[v_gy + o - 1], v_send.at[v_gy + o - 1])
        go(lambda: vrows(VF, at_c, rows_c), vrows(VF, at_c, rows_c), vec, v_gc, mate)

    def vectors_done():
        arrived(vrows(VF, (1 - c) * rows_c, rows_c), v_recv.at[v_gc], v_send.at[v_gc])

    actions.update(
        vc=vectors_core, vy=vectors_y, vx=vectors_x, vz=vectors_z, vgz=vectors_gather_z,
        vgx=vectors_gather_x, vgy=vectors_gather_y, vgc=vectors_gather_core, vd=vectors_done,
        qz=squares_z, qp=squares_plane, qd=squares_done,
    )
    at_place("emb")
    low = DXB[...]
    for tile in range(2):
        made = mm_tn(pix[:, :, tile * D : (tile + 1) * D].reshape(ROWS, D), low).astype(BF)
        for piece in range(D // rows_patch):
            shard = tile * (D // rows_patch) + piece
            GS[1, shard // 2, shard % 2] = made[piece * rows_patch : (piece + 1) * rows_patch]

    at_place("patch")
    at_place("tail")
    last_copies = [
        pltpu.make_async_copy(VF, vec_out, out_local.at[1 + CHUNKS + 2]),
        pltpu.make_async_copy(SQ.at[2], square_out, out_local.at[2 + CHUNKS + 2]),
    ]
    for copy in last_copies:
        copy.start()
    for source, send, recv, at in list(sent.values()):
        left_here(source(), recv.at[at], send.at[at])
    for k in range(CHUNKS + 2):
        result(k).wait()
    for copy in last_copies:
        copy.wait()

    @pl.when(jnp.logical_not(lower))
    def _():
        left_here(given, img_recv.at[0], img_send.at[0])
        left_here(lab_given, img_recv.at[1], img_send.at[1])


def run_train(
    n_rep, n_shard, patches, labels, counts, own_patch, own_in, own_down, vecs, glob, pos, head
):
    n_x = 2 ** ((n_rep.bit_length() - 2) // 2)
    n_z, n_y = n_rep // n_x, n_shard // 2
    block = 4 * (D // n_shard)
    group = KEPT * n_shard
    keep = LAYERS - 1
    units = 1 + 3 * LAYERS
    chunks = CHUNKS + 2

    def buf(*shape, dtype=BF):
        return pltpu.VMEM(shape, dtype)

    def sems(*shape):
        return pltpu.SemaphoreType.DMA(shape)

    def reduction(count, slots, rows):
        by_x = cut(rows, n_x, 16)
        by_z = cut(rows // by_x, n_z, 16)
        return [
            buf(count, n_y, 2, rows, D),
            buf(slots, n_y, rows, D),
            buf(slots, n_y - 1, rows, D),
            buf(slots, n_x - 1 if by_x > 1 else n_x, rows // by_x, D),
            buf(slots, n_z, rows // by_x // by_z, D),
            buf(count, rows, D),
        ]

    rows_y = VEC_ROWS // 2 // n_y
    rows_x = rows_y // n_x
    rows_z = rows_x // cut(rows_x, n_z, 8)
    ag_count = n_y + (n_y - 1) * (n_x - 1) * 2 + n_y - 1
    rs_count = 1 + (n_y - 1) + 2 * (n_x - 1) + 2 * (n_z - 1)
    f_count = 1 + (n_y - 1) + (n_x - 1) + (n_z - 1) + 1
    v_count = 1 + 2 * (n_y - 1) + 2 * (n_x - 1) + 2 * (n_z - 1) + 1
    q_count = n_z - 1 + 2 * n_x * n_y - 1
    whole = pl.BlockSpec(memory_space=pltpu.VMEM)
    there = pl.BlockSpec(memory_space=pl.ANY)
    return pl.pallas_call(
        functools.partial(train, n_rep, n_shard),
        out_shape=[
            jax.ShapeDtypeStruct((CHUNKS, block, D), BF),
            jax.ShapeDtypeStruct((2, block // 2, D), BF),
            jax.ShapeDtypeStruct((VEC_ROWS, VEC_WIDE), F32),
            jax.ShapeDtypeStruct((8, 128), F32),
            jax.ShapeDtypeStruct((2, n_x, n_z, group, WFAC), BF),
        ],
        in_specs=[there] + [pl.BlockSpec(memory_space=pltpu.SMEM)] * 2 + [there] * 3 + [whole] * 4,
        out_specs=[there] * 5,
        scratch_shapes=[
            buf(ROWS, D, dtype=F32),
            buf(LAYERS, ROWS, D),
            buf(LAYERS, ROWS, 128, dtype=F32),
            buf(keep, ROWS, 3 * D),
            buf(keep, ROWS, D),
            buf(keep, ROWS, D),
            buf(keep, ROWS, 128, dtype=F32),
            buf(keep, ROWS, FF),
            buf(keep, ROWS, FF),
            buf(ROWS, D),
            buf(ROWS, D),
            buf(ROWS, D),
            buf(ROWS, FF),
            buf(KEPT, BLK, PATCH_DIM),
            buf(2, 32, 128, dtype=F32),
            buf(32, 128, dtype=F32),
            buf(PATCH_DIM, D),
            buf(LAYERS, D, 4 * D + FF),
            buf(LAYERS, FF, D),
            buf(D, CPAD),
            buf(1, CPAD, dtype=F32),
            *reduction(CHUNKS, 3, block),
            *reduction(2, 1, block // 2),
            buf(2, group, WFAC),
            buf(group, WFAC),
            buf(n_y - 1, group, WFAC),
            buf(n_z, group, WFAC),
            buf(VEC_ROWS, VEC_WIDE, dtype=F32),
            buf(VEC_ROWS // 2, VEC_WIDE, dtype=F32),
            buf(n_y - 1, rows_y, VEC_WIDE, dtype=F32),
            buf(n_x - 1, rows_x, VEC_WIDE, dtype=F32),
            buf(n_z, rows_z, VEC_WIDE, dtype=F32),
            buf(VEC_ROWS, VEC_WIDE, dtype=F32),
            buf(3, 8, 128, dtype=F32),
            buf(n_z, 8, 128, dtype=F32),
            buf(2 * n_x * n_y, 8, 128, dtype=F32),
            buf(8, 128, dtype=F32),
            sems(units, ag_count),
            sems(units, ag_count),
            sems(units, 4),
            sems(chunks, rs_count),
            sems(chunks, rs_count),
            sems(f_count),
            sems(f_count),
            sems(v_count),
            sems(v_count),
            sems(q_count),
            sems(q_count),
            sems(2),
            sems(2),
            sems(4),
            sems(3 + chunks),
        ],
        compiler_params=pltpu.CompilerParams(
            vmem_limit_bytes=65400 * 1024, collective_id=0, has_side_effects=True
        ),
        cost_estimate=pl.CostEstimate(
            flops=24_000_000_000, bytes_accessed=30_000_000, transcendentals=10_000_000
        ),
        name="train_step",
    )(patches, labels, counts, own_patch, own_in, own_down, vecs, glob, pos, head)


def adam(weight, first, second, grad, factor, rate):
    grad = grad * factor
    first = BETA_FIRST * first + (1.0 - BETA_FIRST) * grad
    second = BETA_SECOND * second + (1.0 - BETA_SECOND) * (grad * grad)
    first_scale = 1.0 / (1.0 - BETA_FIRST**ADAM_STEP)
    root_scale = (1.0 / (1.0 - BETA_SECOND**ADAM_STEP)) ** 0.5
    bottom = second * lax.rsqrt(second) * root_scale + ADAM_EPS
    step = first * lax.rsqrt(bottom * bottom)
    weight = weight * (1.0 - rate * WEIGHT_DECAY) - step * (rate * first_scale)
    return weight, first, second


def update(n_rep, n_shard, *refs):
    res, small, vec, exchanged, factors = refs[0:5]
    sources = refs[5:26]
    loss_out, norm_out = refs[26:28]
    targets = refs[28:49]
    buffers = refs[49:70]
    results = refs[70:91]
    last_in, last_down, passing, grad_head, in_sems, out_sems = refs[91:]
    shard = lax.axis_index("shard")
    rows_in = D // n_shard
    rows_down = FF // n_shard
    keep = LAYERS - 1

    def moves(array, layer=None, out=False):
        found = []
        for kind in range(3):
            index = 3 * array + kind
            if out:
                src, dst, sem = results[index], targets[index], out_sems
            else:
                src, dst, sem = sources[index], buffers[index], in_sems
            slot = 0 if layer is None else layer
            if layer is not None:
                src, dst = src.at[layer], dst.at[layer]
            found.append(pltpu.make_async_copy(src, dst, sem.at[index, slot]))
        return found

    layered = [(1, layer) for layer in range(LAYERS)] + [(2, layer) for layer in range(LAYERS)]
    order = layered + [(0, None), (6, None), (5, None), (3, None), (4, None)]
    for array, layer in order:
        for move in moves(array, layer):
            move.start()

    n_rows = factors.shape[1] * factors.shape[2] * factors.shape[3]

    def factor(half, at, size):
        return factors[half, :, :, :, at : at + size].reshape(n_rows, size)

    def squares(values):
        return fold(values * values)

    total = jnp.zeros((8, D), F32)
    own_rows = pl.multiple_of(shard * rows_in, 8)

    def keep_in(column, made):
        slot = column % 2
        passing[slot] = made
        last_in[:, column * D : (column + 1) * D] = passing[slot, pl.ds(own_rows, rows_in), :]

    h2 = factor(0, FF, D)
    for tile in range(4):
        made = mm_tn(h2, factor(1, tile * D, D))
        keep_in(4 + tile, made)
        total = total + squares(made)
    for tile in range(2):
        last_in[:, (1 + tile) * D : (2 + tile) * D] = small[
            0, tile * rows_in : (tile + 1) * rows_in, :
        ].astype(F32)
    made = mm_tn(factor(0, FF + 2 * D, D), factor(1, FF + D, D))
    keep_in(0, made)
    total = total + squares(made)
    made = mm_tn(factor(0, FF + D, D), factor(1, FF, D))
    keep_in(3, made)
    total = total + squares(made)
    d_top = factor(0, FF + 4 * D, D)
    per = min(rows_down, D)
    for tile in range(4):
        made = mm_tn(factor(0, tile * D, D), d_top)
        total = total + squares(made)
        for piece in range(D // per):
            owner, at = divmod(tile * D + piece * per, rows_down)

            def keep_down(made=made, piece=piece, at=at):
                last_down[at : at + per, :] = made[piece * per : (piece + 1) * per]

            pl.when(shard == owner)(keep_down)
    final = factor(0, FF + 3 * D, D)
    wide = jnp.zeros((8, 128), F32)
    for at in range(0, CPAD, 512):
        d_logits = factor(1, FF + 2 * D + at, 512)
        made = mm_tn(final, d_logits)
        grad_head[0:D, at : at + 512] = made
        bias = down_sum(d_logits.astype(F32))
        grad_head[D : D + 1, at : at + 512] = bias
        sums = squares(made)
        for lane in range(0, 512, 128):
            wide = wide + sums[:, lane : lane + 128]
            row = bias[:, lane : lane + 128]
            wide = wide + (row * row) * 0.125
    for lane in range(0, D, 128):
        wide = wide + total[:, lane : lane + 128]
    used = VEC_AT + 12 * LAYERS + 2
    parts = jnp.zeros((8, D), F32)
    kept_rows = lax.broadcasted_iota(jnp.int32, (8, 1), 0)
    for at in range(0, used, 8):
        value = vec[at : at + 8, 0:D]
        if at + 8 > used:
            value = jnp.where(kept_rows + at < used, value, 0.0)
        parts = parts + value * value
    patch_bias = down_sum(vec[0:PATCHES, 0:D])
    class_row = vec[CLS : CLS + 1, 0:D]
    rest = (patch_bias * patch_bias + class_row * class_row) * 0.125
    parts = parts + rest
    for lane in range(0, D, 128):
        wide = wide + parts[:, lane : lane + 128]
    wide = wide + exchanged[...]
    sum_squares = jnp.sum(jnp.sum(wide, axis=1, keepdims=True), axis=0, keepdims=True)
    inv_count = 1.0 / vec[used + 1 : used + 2, 0:1]
    grad_norm = jnp.sqrt(sum_squares) * inv_count
    norm_out[...] = grad_norm
    loss_out[...] = vec[used : used + 1, 0:1] * inv_count
    scale = jnp.minimum(1.0, CLIP_NORM / grad_norm) * inv_count

    def apply(array, where, grad, rate):
        refs = [buffers[3 * array + kind] for kind in range(3)]
        made = adam(refs[0][where], refs[1][where], refs[2][where], grad, scale, rate)
        for kind, value in enumerate(made):
            results[3 * array + kind][where] = value

    def begin(array, layer=None):
        for move in moves(array, layer):
            move.wait()

    def finish(array, layer=None):
        for move in moves(array, layer, out=True):
            move.start()

    def loop(count, body):
        def one(index, nothing):
            body(index)
            return nothing

        lax.fori_loop(0, count, one, 0)

    step = 32 if rows_in % 32 == 0 else 16
    for layer in range(LAYERS):
        begin(1, layer)

        def column_of(column):
            lanes = pl.ds(pl.multiple_of(column * D, 128), D)
            for at in range(0, rows_in, step):
                if layer < keep:
                    k = 3 * (keep - 1 - layer) + jnp.where(column < 4, 2, 1)
                    row = pl.multiple_of(lax.rem(column, 4) * rows_in + at, 16)
                    grad = res[k, pl.ds(row, step), :].astype(F32)
                else:
                    grad = last_in[at : at + step, lanes]
                apply(1, (layer, slice(at, at + step), lanes), grad, LEARNING_RATE)

        loop(8, column_of)
        finish(1, layer)
    for layer in range(LAYERS):
        begin(2, layer)

        def rows_of(index):
            for part in range(3):
                at = pl.multiple_of(index * 96 + part * 32, 16)
                if layer < keep:
                    grad = res[3 * (keep - 1 - layer), pl.ds(at, 32), :].astype(F32)
                else:
                    grad = last_down[pl.ds(at, 32), :]
                apply(2, (layer, pl.ds(at, 32), slice(0, D)), grad, LEARNING_RATE)

        loop(rows_down // 96, rows_of)
        finish(2, layer)
    begin(0)

    def patch_rows(index):
        for part in range(3):
            at = pl.multiple_of(index * 96 + part * 32, 16)
            grad = small[1, pl.ds(at, 32), :].astype(F32)
            apply(0, (pl.ds(at, 32), slice(0, D)), grad, LEARNING_RATE)

    loop(PATCH_DIM // n_shard // 96, patch_rows)
    finish(0)
    begin(6)

    def head_rows(index):
        for part in range(3):
            rows = pl.ds(pl.multiple_of(index * 48 + part * 16, 16), 16)
            apply(6, (rows, slice(0, NCLS)), grad_head[rows, 0:NCLS], LEARNING_RATE)

    loop(D // 48, head_rows)
    apply(6, (slice(D, D + 1), slice(0, NCLS)), grad_head[D : D + 1, 0:NCLS], LEARNING_RATE)
    finish(6)
    begin(5)
    apply(5, (slice(0, 1), slice(0, D)), class_row, VECTOR_RATE)
    for at in range(0, PATCHES, 28):
        apply(
            5, (slice(1 + at, 29 + at), slice(0, D)), vec[at : at + 28, 0:D], VECTOR_RATE
        )
    finish(5)
    begin(3)
    for layer in range(LAYERS):
        for piece in range(12):
            row = VEC_AT + 12 * layer + piece
            where = (slice(layer, layer + 1), slice(piece * D, (piece + 1) * D))
            apply(3, where, vec[row : row + 1, 0:D], VECTOR_RATE)
    finish(3)
    begin(4)
    rows = [patch_bias, class_row, vec[used - 2 : used - 1, 0:D], vec[used - 1 : used, 0:D]]
    for index, row in enumerate(rows):
        apply(4, (slice(index, index + 1), slice(0, D)), row, VECTOR_RATE)
    finish(4)
    for array, layer in order:
        for move in moves(array, layer, out=True):
            move.wait()


def run_update(n_rep, n_shard, res, small, vec, squares, factors, arrays):
    whole = pl.BlockSpec(memory_space=pltpu.VMEM)
    there = pl.BlockSpec(memory_space=pl.ANY)
    one = jax.ShapeDtypeStruct((1, 1), F32)
    made = pl.pallas_call(
        functools.partial(update, n_rep, n_shard),
        out_shape=[one, one] + [jax.ShapeDtypeStruct(a.shape, F32) for a in arrays],
        in_specs=[whole] * 5 + [there] * 21,
        out_specs=[whole] * 2 + [there] * 21,
        scratch_shapes=[pltpu.VMEM(a.shape, F32) for a in (*arrays, *arrays)]
        + [
            pltpu.VMEM((D // n_shard, 4 * D + FF), F32),
            pltpu.VMEM((FF // n_shard, D), F32),
            pltpu.VMEM((2, D, D), F32),
            pltpu.VMEM((D + 8, CPAD), F32),
            pltpu.SemaphoreType.DMA((21, LAYERS)),
            pltpu.SemaphoreType.DMA((21, LAYERS)),
        ],
        compiler_params=pltpu.CompilerParams(vmem_limit_bytes=62 * 1024 * 1024),
        cost_estimate=pl.CostEstimate(
            flops=200_000_000, bytes_accessed=50_000_000, transcendentals=4_000_000
        ),
        name="adamw",
    )(res, small, vec, squares, factors, *arrays)
    return made[0].reshape(()), made[1].reshape(()), made[2:]


def shards(
    n_rep, n_shard,
    patches, labels, counts, patch_w, layer_in, layer_down, layer_vecs, glob_vecs, pos_embed, head,
    m_patch, v_patch, m_in, v_in, m_down, v_down, m_vecs, v_vecs, m_glob, v_glob, m_pos, v_pos,
    m_head, v_head,
):
    padded = jnp.pad(patches, ((0, 0), (0, BLK - PATCHES), (0, 0)))
    res, small, vec, squares, factors = run_train(
        n_rep, n_shard, padded, labels, counts, patch_w, layer_in, layer_down, layer_vecs,
        glob_vecs, pos_embed, head,
    )
    arrays = [
        patch_w, m_patch, v_patch, layer_in, m_in, v_in, layer_down, m_down, v_down,
        layer_vecs, m_vecs, v_vecs, glob_vecs, m_glob, v_glob, pos_embed, m_pos, v_pos,
        head, m_head, v_head,
    ]
    loss, grad_norm, new = run_update(n_rep, n_shard, res, small, vec, squares, factors, arrays)
    return (loss, grad_norm, *new)


def solution(mesh):
    everywhere = P()
    rows = P("shard", None)
    middle = P(None, "shard", None)
    return jax.shard_map(
        functools.partial(shards, mesh.shape["rep"], mesh.shape["shard"]),
        mesh=mesh,
        in_specs=(
            P(("rep", "shard"), None, None),
            P(("rep", "shard")),
            P(("rep", "shard")),
            rows,
            middle,
            middle,
            *(everywhere,) * 4,
            *(rows,) * 2,
            *(middle,) * 4,
            *(everywhere,) * 8,
        ),
        out_specs=(
            *(everywhere,) * 2,
            *(rows,) * 3,
            *(middle,) * 6,
            *(everywhere,) * 12,
        ),
        check_vma=False,
    )
```

```python
import functools

import jax
import jax.numpy as jnp
from jax import lax
from jax.experimental import pallas as pl
from jax.experimental.pallas import tpu as pltpu
from jax.sharding import PartitionSpec as P

D = 384
HEADS = 6
HEAD_DIM = 64
FF = 1536
PATCH_DIM = 768
PATCHES = 196
NCLS = 1000
LAYERS = 3
SEQ = 197

BLK = 208
CLS = 200
TAIL = 192
KEPT = 4
ROWS = KEPT * BLK
HALF = 2 * BLK
CROWS = KEPT * 16
CPAD = 1024
WIDE = 8 * D + FF

NORM_EPS = 1e-06
SMOOTHING = 0.1
CLIP_NORM = 0.05
LEARNING_RATE = 0.05
VECTOR_RATE = 0.5
BETA_FIRST = 0.9
BETA_SECOND = 0.999
ADAM_EPS = 1e-08
WEIGHT_DECAY = 0.05
ADAM_STEP = 10
GELU_SCALE = 0.7978845608028654
GELU_CUBIC = 0.044715

F32 = jnp.float32
BF = jnp.bfloat16


def mm(left, right):
    return jnp.dot(left, right, preferred_element_type=F32)


def mm_nt(left, right):
    return lax.dot_general(left, right, (((1,), (1,)), ((), ())), preferred_element_type=F32)


def mm_tn(left, right):
    return lax.dot_general(left, right, (((0,), (0,)), ((), ())), preferred_element_type=F32)


def fold(values):
    return jnp.sum(values.reshape(-1, 8, values.shape[-1]), axis=0)


def down_sum(values):
    return jnp.sum(values, axis=0, keepdims=True)


def norm(values):
    centre = values - jnp.mean(values, axis=-1, keepdims=True)
    inverse = lax.rsqrt(jnp.mean(centre * centre, axis=-1, keepdims=True) + NORM_EPS)
    return centre * inverse, inverse


def norm_back(upstream, normed, inverse, gain):
    scaled = upstream * gain
    first = jnp.mean(scaled, axis=-1, keepdims=True)
    second = jnp.mean(scaled * normed, axis=-1, keepdims=True)
    return inverse * (scaled - first - normed * second)


def gelu_parts(hidden):
    square = hidden * hidden
    tangent = jnp.tanh(hidden * (GELU_SCALE + (GELU_SCALE * GELU_CUBIC) * square))
    share = 0.5 + 0.5 * tangent
    active = hidden * share
    inner = (2.0 * GELU_SCALE) + (6.0 * GELU_SCALE * GELU_CUBIC) * square
    slope = share + active * (1.0 - share) * inner
    return active, slope


def lane_mask(width, low, high):
    lane = lax.broadcasted_iota(jnp.int32, (1, width), 1)
    return jnp.where((lane >= low) & (lane < high), 1.0, 0.0).astype(BF)


STEP = 32


def pieces(total):
    return [(at, min(STEP, total - at)) for at in range(0, total, STEP)]


SCHEDULE = {
    ("cast", 0): ("ws0",),
    ("cast", 1): ("ws1",),
    ("cast", 2): ("ws2",),
    ("b_start",): ("wf0", "ws3", "wf1", "wr0", "ws4", "we0",),
    ("embed", 0): ("wf2", "ws5",),
    ("b_norm", 0, 0): ("wr1", "wf3", "ws6", "we1",),
    ("norm", 0, 0): ("wr2", "wf4", "ws7",),
    ("att", 0, 0, 1): ("wr3",),
    ("mid", 0, 0): ("wf5", "ws8",),
    ("b_up", 0, 0): ("we2",),
    ("up", 0, 0): ("wr4", "wf6", "ws9",),
    ("b_down", 0, 0): ("we3",),
    ("b_norm", 0, 1): ("wr5", "we4",),
    ("norm", 0, 1): ("wf7",),
    ("att", 0, 1, 0): ("wr6",),
    ("att", 0, 1, 1): ("wf8",),
    ("b_up", 0, 1): ("we5",),
    ("up", 0, 1): ("wr7", "wf9",),
    ("b_down", 0, 1): ("we6",),
    ("norm", 1, 0): ("wr8",),
    ("att", 1, 0, 1): ("wr9",),
    ("b_last",): ("we7", "we8", "we9",),
    ("class",): ("fc",),
    ("kv",): ("core6",),
    ("lb", 1): ("fy",),
    ("dn", 1): ("y6", "core0",),
    ("act", 1, 1): ("fz",),
    ("ups", 1): ("core1", "y0",),
    ("mlpb", 1, 1): ("x6",),
    ("attb", 1, 0): ("y1",),
    ("attb", 1, 2): ("z6",),
    ("attb", 1, 3): ("x0",),
    ("qkv", 1): ("fx", "core2",),
    ("fb", 1, 1): ("gz6",),
    ("dn", 0): ("y2", "x1", "z0", "core3",),
    ("act", 0, 0): ("gx6",),
    ("mlpb", 0, 0): ("gz0",),
    ("attb", 0, 0): ("x2", "y3", "core4", "fm",),
    ("attb", 0, 1): ("gx0",),
    ("attb", 0, 2): ("z1",),
    ("qkv", 0): ("gd6",),
    ("fb", 0, 1): ("fd",),
    ("emb",): ("z2", "x3", "y4", "core5", "gz1", "vc",),
    ("patch",): ("core7",),
    ("tail",): ("gd0", "gz2", "vy", "z3", "y7", "gx1", "x4", "y5", "vx", "gx2", "gd1", "gz3", "x7", "z4", "vz", "gx3", "gd2", "x5", "z7", "gz4", "vgz", "gd3", "gz7", "z5", "gx4", "vgx", "gx7", "gd4", "vgy", "gz5", "qz", "gd7", "vgc", "gx5", "qp", "vd", "gd5", "qd",),
}


WFAC = FF + 5 * D
VEC_ROWS = 256
VEC_AT = BLK
VEC_WIDE = D
MESH = pl.DeviceIdType.MESH
CHUNKS = 6


class Place:
    def __init__(self, n_rep, n_shard):
        self.n_rep, self.n_shard = n_rep, n_shard
        self.n_x = 2 ** ((n_rep.bit_length() - 2) // 2)
        self.n_z = n_rep // self.n_x
        self.n_y = n_shard // 2
        rep, shard = lax.axis_index("rep"), lax.axis_index("shard")
        self.rep, self.shard = rep, shard
        self.z, self.x = rep // self.n_x, rep % self.n_x
        self.y, self.c = shard // 2, shard % 2

    def to(self, x=None, y=None, z=None, c=None):
        x = self.x if x is None else x
        y = self.y if y is None else y
        z = self.z if z is None else z
        c = self.c if c is None else c
        return {"rep": z * self.n_x + x, "shard": y * 2 + c}


def cut(rows, parts, unit):
    return parts if rows % (parts * unit) == 0 else 1


def small_rows(rows, n_x, n_z):
    unit = 16 * n_x * n_z
    padded = -(-rows // unit) * unit
    return padded if 2 * padded <= 3 * rows else rows


def aligned(value, unit):
    return pl.multiple_of(value, unit)


def train(
    n_rep, n_shard,
    patches, patch_ends, labels, counts, own_patch, own_in, own_down, vecs, glob, pos, head,
    res_out, small_out, vec_out, square_out, all_factors,
    X, N1, I1, QKV, ATT, N2, I2, ACT, SLOPE, DXB, DMB, DA, DH,
    pix, lab, lab_given, wp, win, wdn, low_head, head_bias,
    G, RC, RY, RX, RZ, RES, GS, SC, SY, SX, SZ, SRES,
    FAC, FC, FY, FALL, V, VC, VY, VX, VZ, VF, SQ, SQZ, SQP, square_sum,
    ag_send, ag_recv, ag_local, rs_send, rs_recv, f_send, f_recv, v_send, v_recv,
    q_send, q_recv,
    img_send, img_recv, img_local, out_local,
):
    here = Place(n_rep, n_shard)
    n_x, n_y, n_z = here.n_x, here.n_y, here.n_z
    x, y, z, c = here.x, here.y, here.z, here.c
    rows_in, rows_down, rows_patch = D // n_shard, FF // n_shard, PATCH_DIM // n_shard
    block = 4 * rows_in
    small_block = small_rows(block // 2, n_x, n_z)
    mate = here.to(c=1 - c)

    def push(src, dst, send, recv, device):
        pltpu.make_async_remote_copy(
            src_ref=src, dst_ref=dst, send_sem=send, recv_sem=recv,
            device_id=device, device_id_type=MESH,
        ).start()

    def arrived(dst, recv, send):
        pltpu.make_async_remote_copy(
            src_ref=dst, dst_ref=dst, send_sem=send, recv_sem=recv,
            device_id=mate, device_id_type=MESH,
        ).wait_recv()

    def left_here(src, recv, send):
        pltpu.make_async_remote_copy(
            src_ref=src, dst_ref=src, send_sem=send, recv_sem=recv,
            device_id=mate, device_id_type=MESH,
        ).wait_send()

    sent = {}

    def go(source, dst, sems, index, device):
        name, send, recv = sems
        push(source(), dst, send.at[index], recv.at[index], device)
        sent[name, index] = (source, send, recv, index)

    def gone(sems, index):
        source, send, recv, at = sent.pop((sems[0], index))
        left_here(source(), recv.at[at], send.at[at])

    def turn(at, by, size):
        return lax.rem(at + by, size)

    barrier = pltpu.get_barrier_semaphore()
    plane = [
        (i, j, k) for i in range(n_x) for j in range(n_y) for k in range(2) if i or j or k
    ]

    def in_plane(step):
        i, j, k = step
        return here.to(x=turn(x, i, n_x), y=turn(y, j, n_y), c=lax.rem(c + k, 2))

    others = [in_plane(step) for step in plane]
    others += [here.to(z=turn(z, o, n_z)) for o in range(1, n_z)]
    for other in others:
        pl.semaphore_signal(barrier, inc=1, device_id=other, device_id_type=MESH)
    pl.semaphore_wait(barrier, len(others))

    def weight(kind, layer, shard, part=None):
        if kind == "patch":
            parts = cut(rows_patch, n_x, 16)
            rows = rows_patch // parts
            if part is None:
                return wp.at[pl.ds(aligned(shard * rows_patch, 16), rows_patch), :]
            return wp.at[pl.ds(aligned(shard * rows_patch + part * rows, 16), rows), :]
        if kind == "down":
            parts = cut(rows_down, n_x, 16)
            rows = rows_down // parts
            if part is None:
                return wdn.at[layer, pl.ds(aligned(shard * rows_down, 16), rows_down), :]
            return wdn.at[layer, pl.ds(aligned(shard * rows_down + part * rows, 16), rows), :]
        base = 0 if kind == "attn" else 4 * D
        rows = pl.ds(aligned(shard * rows_in, 16), rows_in)
        if part is None:
            return win.at[layer, rows, pl.ds(base, 4 * D)]
        wide = 4 * D // n_x
        return win.at[layer, rows, pl.ds(aligned(base + part * wide, 128), wide)]

    units = [("patch", 0)] + [
        (kind, layer) for layer in range(LAYERS) for kind in ("attn", "up", "down")
    ]

    def parts_of(kind):
        if kind == "patch":
            return cut(rows_patch, n_x, 16)
        if kind == "down":
            return cut(rows_down, n_x, 16)
        return n_x

    ag = ("ag", ag_send, ag_recv)
    base_x = n_y
    base_my = base_x + (n_y - 1) * (n_x - 1)
    base_mx = base_my + (n_y - 1)

    stage = 4 * rows_in

    def weights_copies(unit):
        kind, layer = units[unit]
        base = (unit % 2) * stage
        if kind == "patch":
            pairs = [(own_patch, X.at[pl.ds(base, rows_patch)])]
        elif kind == "down":
            pairs = [(own_down.at[layer], X.at[pl.ds(base, rows_down)])]
        else:
            start = 0 if kind == "attn" else 4 * D
            pairs = [
                (
                    own_in.at[layer, :, pl.ds(start + tile * D, D)],
                    X.at[pl.ds(base + tile * rows_in, rows_in)],
                )
                for tile in range(4)
            ]
        return [
            pltpu.make_async_copy(src, dst, ag_local.at[unit, index])
            for index, (src, dst) in enumerate(pairs)
        ]

    def weights_cast(unit):
        kind, layer = units[unit]
        base = (unit % 2) * stage
        for copy in weights_copies(unit):
            copy.wait()
        if kind == "patch":
            rows = pl.ds(aligned(here.shard * rows_patch, 16), rows_patch)
            wp[rows, :] = X[base : base + rows_patch, :].astype(BF)
        elif kind == "down":
            rows = pl.ds(aligned(here.shard * rows_down, 16), rows_down)
            wdn[layer, rows, :] = X[base : base + rows_down, :].astype(BF)
        else:
            start = 0 if kind == "attn" else 4 * D
            rows = pl.ds(aligned(here.shard * rows_in, 16), rows_in)
            for tile in range(4):
                win[layer, rows, start + tile * D : start + (tile + 1) * D] = X[
                    base + tile * rows_in : base + (tile + 1) * rows_in, :
                ].astype(BF)
        if unit + 2 < len(units):
            for copy in weights_copies(unit + 2):
                copy.start()

    def weights_start(unit):
        kind, layer = units[unit]
        part = x if parts_of(kind) > 1 else 0
        for o in range(1, n_y):
            go(
                lambda: weight(kind, layer, here.shard, part),
                weight(kind, layer, here.shard, part), ag, (unit, o),
                here.to(y=turn(y, o, n_y)),
            )
        go(
            lambda: weight(kind, layer, here.shard), weight(kind, layer, here.shard), ag,
            (unit, 0), mate,
        )

    def weights_forward(unit):
        kind, layer = units[unit]
        split = parts_of(kind) > 1
        part = x if split else 0
        for o in range(1, n_y):
            def make(o=o):
                return weight(kind, layer, turn(y, n_y - o, n_y) * 2 + c, part)

            arrived(make(), ag_recv.at[unit, o], ag_send.at[unit, o])
            if split:
                for p in range(1, n_x):
                    index = base_x + (o - 1) * (n_x - 1) + p - 1
                    go(make, make(), ag, (unit, index), here.to(x=turn(x, p, n_x)))
            go(make, make(), ag, (unit, base_my + o - 1), mate)

    def weights_pass(unit):
        kind, layer = units[unit]
        split = parts_of(kind) > 1
        part = x if split else 0
        if split:
            for o in range(1, n_y):
                for p in range(1, n_x):
                    index = (o - 1) * (n_x - 1) + p - 1

                    def make(o=o, p=p):
                        shard = turn(y, n_y - o, n_y) * 2 + c
                        return weight(kind, layer, shard, turn(x, n_x - p, n_x))

                    arrived(
                        make(), ag_recv.at[unit, base_x + index], ag_send.at[unit, base_x + index]
                    )
                    go(make, make(), ag, (unit, base_mx + index), mate)

    def weights_whole(unit):
        kind, layer = units[unit]
        split = parts_of(kind) > 1
        part = x if split else 0
        arrived(weight(kind, layer, y * 2 + 1 - c), ag_recv.at[unit, 0], ag_send.at[unit, 0])
        for o in range(1, n_y):
            shard = turn(y, n_y - o, n_y) * 2 + 1 - c
            index = base_my + o - 1
            arrived(weight(kind, layer, shard, part), ag_recv.at[unit, index], ag_send.at[unit, index])
            if split:
                for p in range(1, n_x):
                    index = base_mx + (o - 1) * (n_x - 1) + p - 1
                    piece = weight(kind, layer, shard, turn(x, n_x - p, n_x))
                    arrived(piece, ag_recv.at[unit, index], ag_send.at[unit, index])

    actions = {}

    def perform(names):
        for name in names:
            actions[name]()

    def at_place(place, *indices):
        for key, names in SCHEDULE.items():
            if key[0] != place:
                continue
            held = None
            for index, value in zip(indices, key[1:], strict=True):
                if not isinstance(index, int):
                    same = index == value
                    held = same if held is None else jnp.logical_and(held, same)
                elif index != value:
                    break
            else:
                if held is None:
                    perform(names)
                else:
                    pl.when(held)(functools.partial(perform, names))

    for unit in range(len(units)):
        actions[f"ws{unit}"] = functools.partial(weights_start, unit)
        actions[f"wf{unit}"] = functools.partial(weights_forward, unit)
        actions[f"wr{unit}"] = functools.partial(weights_pass, unit)
        actions[f"we{unit}"] = functools.partial(weights_whole, unit)

    lower = here.rep < n_rep // 2
    partner = here.to(z=turn(z, n_z // 2, n_z))
    back_parts = (
        pix.at[pl.ds(2, 2), pl.ds(0, TAIL)], pix.at[pl.ds(2, 2), pl.ds(TAIL, BLK - TAIL)]
    )
    given = (patches.at[pl.ds(KEPT, 2), pl.ds(0, TAIL)], patch_ends.at[pl.ds(KEPT, 2)])

    def local_half(half):
        pair = pl.ds(2 * half, 2)
        return (
            pltpu.make_async_copy(
                patches.at[pair, pl.ds(0, TAIL)], pix.at[pair, pl.ds(0, TAIL)],
                img_local.at[half],
            ),
            pltpu.make_async_copy(
                patch_ends.at[pair], pix.at[pair, pl.ds(TAIL, BLK - TAIL)],
                img_local.at[2 + half],
            ),
        )

    def marks(pair):
        row = lax.broadcasted_iota(jnp.int32, (32, 128), 0)
        found = jnp.full((32, 128), -1.0, F32)
        for index in range(2):
            slot = 2 * pair + index
            value = jnp.where(slot < counts[0], labels[slot], -1).astype(F32)
            found = jnp.where(row == CLS - TAIL + 16 * index, value, found)
        return found

    for copy in local_half(0):
        copy.start()
    for unit in range(2):
        for copy in weights_copies(unit):
            copy.start()
    lab[0] = marks(0)
    lab_given[...] = marks(2)

    @pl.when(jnp.logical_not(lower))
    def _():
        for index in range(2):
            push(
                given[index], back_parts[index], img_send.at[index], img_recv.at[index],
                partner,
            )
        push(lab_given, lab.at[1], img_send.at[2], img_recv.at[2], partner)
        for copy in local_half(1):
            copy.start()
        lab[1] = marks(1)

    for unit in range(len(units)):
        weights_cast(unit)
        at_place("cast", unit)

    even = lane_mask(128, 0, 64)
    odd = lane_mask(128, 64, 128)
    low_lane = lax.broadcasted_iota(jnp.int32, (1, 128), 1) < 64
    key_lane = lax.broadcasted_iota(jnp.int32, (1, BLK), 1)
    key_row = jnp.where((key_lane < PATCHES) | (key_lane == CLS), 0.0, -1e30)
    key_sub = lax.broadcasted_iota(jnp.int32, (BLK, 1), 0)
    key_column = jnp.where((key_sub < PATCHES) | (key_sub == CLS), 0.0, -1e30)
    whole_lanes = NCLS // 128 * 128
    low_head[:, 0:whole_lanes] = head[0:D, 0:whole_lanes].astype(BF)
    low_head[:, whole_lanes:] = jnp.zeros((D, CPAD - whole_lanes), BF)
    low_head[:, whole_lanes:NCLS] = head[0:D, whole_lanes:NCLS].astype(BF)
    head_bias[...] = jnp.zeros((1, CPAD), F32)
    head_bias[:, 0:NCLS] = head[D : D + 1, :]
    V[...] = jnp.zeros((VEC_ROWS, VEC_WIDE), F32)
    square_sum[...] = jnp.zeros((8, 128), F32)
    if small_block > block // 2:
        spare = small_block - block // 2
        GS[:, :, :, block // 2 :, :] = jnp.zeros((2, n_y, 2, spare, D), BF)
    zeros = jnp.zeros((8, D), F32)
    patch_bias = glob[0:1, :]

    def whole_lanes_of(tile):
        return jnp.concatenate([tile] * (D // 128), axis=1)

    def vector(layer, at, size):
        return vecs[pl.ds(layer, 1), at : at + size]

    def store_vector(layer, at, row):
        for piece in range(row.shape[-1] // D):
            V[pl.ds(VEC_AT + 12 * layer + at // D + piece, 1), 0:D] = row[
                :, piece * D : (piece + 1) * D
            ]

    def store_sums(layer, parts):
        for at, part in parts:
            store_vector(layer, at, down_sum(part))

    def embed(half):
        made = mm(pix[pl.ds(2 * half, 2)].reshape(HALF, PATCH_DIM), wp[...])
        for image in range(2):
            start = aligned(half * HALF + image * BLK, 16)
            for at, size in pieces(PATCHES - 4):
                X[pl.ds(start + at, size), :] = (
                    made[image * BLK + at : image * BLK + at + size]
                    + pos[1 + at : 1 + at + size, :]
                    + patch_bias
                )
            X[pl.ds(start + TAIL, 16), :] = jnp.zeros((16, D), F32)
            X[pl.ds(start + TAIL, 4), :] = (
                made[image * BLK + TAIL : image * BLK + PATCHES]
                + pos[1 + TAIL : 1 + PATCHES, :]
                + patch_bias
            )
            X[pl.ds(start + CLS, 1), :] = glob[1:2, :] + pos[0:1, :]

    def first_norm(layer, half, columns):
        base = half * HALF
        gain, shift = vector(layer, 0, D), vector(layer, D, D)
        for at, size in pieces(HALF):
            rows = pl.ds(aligned(base + at, 16), size)
            normed, inverse = norm(X[rows, :])
            N1[layer, rows, :] = normed.astype(BF)
            I1[layer, rows, :] = jnp.broadcast_to(inverse, (size, 128))
            DXB[rows, :] = (normed * gain + shift).astype(BF)
        rows = pl.ds(aligned(base, 16), HALF)
        h1 = DXB[rows, :]
        if len(columns) == 3:
            made = mm(h1, win[layer, :, 0 : 2 * D])
            QKV[layer, rows, 0:D] = (made[:, 0:D] + vector(layer, 2 * D, D)).astype(BF)
            QKV[layer, rows, D : 2 * D] = made[:, D:].astype(BF)
            made = mm(h1, win[layer, :, 2 * D : 3 * D])
            QKV[layer, rows, 2 * D :] = (made + vector(layer, 3 * D, D)).astype(BF)
        else:
            made = mm(h1, win[layer, :, D : 3 * D])
            DMB[rows, :] = made[:, 0:D].astype(BF)
            DA[rows, :] = (made[:, D:] + vector(layer, 3 * D, D)).astype(BF)

    ones = jnp.full((BLK, 128), 1.0, BF)

    def attend(layer, image):
        rows = pl.ds(aligned(image * BLK, 16), BLK)
        for pair in range(3):
            at = pair * 128
            query = QKV[layer, rows, at : at + 128] * BF(0.125)
            keys = QKV[layer, rows, D + at : D + at + 128]
            values = QKV[layer, rows, 2 * D + at : 2 * D + at + 128]
            both = jnp.concatenate([query * even, query * odd], axis=0)
            scores = mm_nt(both, keys)
            probs = []
            for row, size in pieces(HALF):
                part = scores[row : row + size] + key_row
                probs.append(jnp.exp(part - jnp.max(part, axis=-1, keepdims=True)).astype(BF))
            probs = jnp.concatenate(probs, axis=0)
            first = mm(probs[:BLK], jnp.concatenate([values * even, ones], axis=1))
            second = mm(probs[BLK:], jnp.concatenate([values * odd, ones], axis=1))
            made = first[:, :128] * (1.0 / first[:, 128:])
            made = made + second[:, :128] * (1.0 / second[:, 128:])
            ATT[layer, rows, at : at + 128] = made.astype(BF)

    def mlp(layer, half):
        base = half * HALF
        whole = pl.ds(aligned(base, 16), HALF)
        made = mm(ATT[layer, whole, :], win[layer, :, 3 * D : 4 * D])
        bias_out = vector(layer, 4 * D, D)
        gain, shift = vector(layer, 5 * D, D), vector(layer, 6 * D, D)
        for at, size in pieces(HALF):
            rows = pl.ds(aligned(base + at, 16), size)
            middle = X[rows, :] + made[at : at + size] + bias_out
            X[rows, :] = middle
            normed, inverse = norm(middle)
            N2[layer, rows, :] = normed.astype(BF)
            I2[layer, rows, :] = jnp.broadcast_to(inverse, (size, 128))
            DXB[rows, :] = (normed * gain + shift).astype(BF)
        at_place("mid", half, layer)
        at_place("b_up", half, layer)
        h2 = DXB[whole, :]
        for pair in range(2):
            made = mm(h2, win[layer, :, (4 + 2 * pair) * D : (6 + 2 * pair) * D])
            for tile in range(2):
                start = (2 * pair + tile) * D
                columns = slice(start, start + D)
                bias = vector(layer, 7 * D + start, D)
                for at, size in pieces(HALF):
                    rows = pl.ds(aligned(base + at, 16), size)
                    active, slope = gelu_parts(
                        made[at : at + size, tile * D : (tile + 1) * D] + bias
                    )
                    ACT[layer, rows, columns] = active.astype(BF)
                    SLOPE[layer, rows, columns] = slope.astype(BF)
        at_place("up", half, layer)
        at_place("b_down", half, layer)
        made = mm(ACT[layer, whole, :], wdn[layer])
        bias = vector(layer, 7 * D + FF, D)
        for at, size in pieces(HALF):
            rows = pl.ds(aligned(base + at, 16), size)
            X[rows, :] = X[rows, :] + made[at : at + size] + bias
        at_place("down", half, layer)

    at_place("b_start")

    def forward_half(half, carry):
        @pl.when(half == 0)
        def _():
            for copy in local_half(0):
                copy.wait()

        @pl.when(jnp.logical_and(half == 1, lower))
        def _():
            for index in range(2):
                arrived(back_parts[index], img_recv.at[index], img_send.at[index])

        @pl.when(jnp.logical_and(half == 1, jnp.logical_not(lower)))
        def _():
            for copy in local_half(1):
                copy.wait()

        embed(half)
        at_place("embed", half)

        def forward_layer(layer, inner):
            at_place("b_norm", half, layer)
            first_norm(layer, half, (0, 1, 2))
            at_place("norm", half, layer)

            def attend_one(index, nothing):
                attend(layer, 2 * half + index)
                at_place("att", half, layer, index)
                return nothing

            lax.fori_loop(0, 2, attend_one, 0)
            mlp(layer, half)
            return inner

        return lax.fori_loop(0, LAYERS - 1, forward_layer, carry)

    lax.fori_loop(0, 2, forward_half, 0)
    at_place("b_last")

    last = LAYERS - 1

    def last_norm(half, nothing):
        first_norm(last, half, (1, 2))
        at_place("ln", half)
        return nothing

    lax.fori_loop(0, 2, last_norm, 0)

    fac = ("f", f_send, f_recv)
    f_y, f_z = 1, n_y
    f_x = f_z + n_z - 1
    f_m = f_x + n_x - 1
    group = KEPT * n_shard

    def factors_core():
        go(lambda: FAC.at[1 - c], FC, fac, 0, mate)

    def factors_y():
        arrived(FC, f_recv.at[0], f_send.at[0])
        FAC[c] = FAC[c] + FC[...]
        for o in range(1, n_y):
            go(lambda: FAC.at[c], FY.at[o - 1], fac, f_y + o - 1, here.to(y=turn(y, o, n_y)))

    def factors_z():
        total = FAC[c]
        for o in range(1, n_y):
            arrived(FY.at[o - 1], f_recv.at[f_y + o - 1], f_send.at[f_y + o - 1])
            total = total + FY[o - 1]
        FALL[z] = total
        for o in range(1, n_z):
            go(
                lambda: FALL.at[z], FALL.at[z], fac, f_z + o - 1,
                here.to(z=turn(z, o, n_z)),
            )

    def factors_x():
        for o in range(1, n_z):
            index = f_z + o - 1
            arrived(FALL.at[turn(z, n_z - o, n_z)], f_recv.at[index], f_send.at[index])
        pltpu.make_async_copy(FALL, all_factors.at[c, x], out_local.at[0]).start()
        for o in range(1, n_x):
            go(
                lambda: FALL, all_factors.at[c, x], fac, f_x + o - 1,
                here.to(x=turn(x, o, n_x)),
            )

    def factors_mate():
        for o in range(1, n_x):
            index = f_x + o - 1
            came = all_factors.at[c, turn(x, n_x - o, n_x)]
            arrived(came, f_recv.at[index], f_send.at[index])
        pltpu.make_async_copy(FALL, all_factors.at[c, x], out_local.at[0]).wait()
        go(lambda: all_factors.at[c], all_factors.at[c], fac, f_m, mate)

    def factors_done():
        arrived(all_factors.at[1 - c], f_recv.at[f_m], f_send.at[f_m])

    rs = ("rs", rs_send, rs_recv)
    r_y, r_x = 1, n_y
    r_z = r_x + n_x - 1
    r_gz = r_z + n_z - 1
    r_gx = r_gz + n_z - 1

    def chunk(k):
        if k < CHUNKS:
            slot = k % 3
            return (
                G.at[k], RC.at[slot], RY.at[slot], RX.at[slot], RZ.at[slot], RES.at[k], block
            )
        k = k - CHUNKS
        return GS.at[k], SC.at[0], SY.at[0], SX.at[0], SZ.at[0], SRES.at[k], small_block

    def splits(rows):
        by_x = cut(rows, n_x, 16)
        by_z = cut(rows // by_x, n_z, 16)
        return by_x, rows // by_x, by_z, rows // by_x // by_z

    def step_of(rows, most=192):
        return max(step for step in range(16, most + 1, 16) if rows % step == 0)

    def add_rows(rows, target, target_at, sources):
        step = step_of(rows)

        def one(index, nothing):
            at = index * step
            to = pl.ds(aligned(target_at + at, 16), step)
            total = target[to, :]
            if len(sources) == 1:
                total = total + sources[0][pl.ds(aligned(at, 16), step), :]
            else:
                total = total.astype(F32)
                for source in sources:
                    total = total + source[pl.ds(aligned(at, 16), step), :].astype(F32)
                total = total.astype(BF)
            target[to, :] = total
            return nothing

        lax.fori_loop(0, rows // step, one, 0)

    def reduce_core(k):
        g, rc = chunk(k)[0:2]
        go(lambda: chunk(k)[0].at[:, 1 - c], rc, rs, (k, 0), mate)

    def reduce_y(k):
        g, rc, ry, _, _, _, rows = chunk(k)
        arrived(rc, rs_recv.at[k, 0], rs_send.at[k, 0])
        for o in list(range(1, n_y)) + [0]:
            at = turn(y, o, n_y)
            add_rows(rows, g.at[at, c], 0, [rc.at[at]])
            if o:
                go(
                    lambda o=o: chunk(k)[0].at[turn(y, o, n_y), c], ry.at[o - 1], rs,
                    (k, r_y + o - 1), here.to(y=at),
                )

    def total_of(slots, count, at, step):
        total = None
        for index in range(count):
            value = slots[index, pl.ds(aligned(at, 16), step), :].astype(F32)
            total = value if total is None else total + value
        return total

    def reduce_x(k):
        g, _, ry, rx, _, _, rows = chunk(k)
        by_x, rows_x = splits(rows)[0:2]
        for o in range(1, n_y):
            arrived(ry.at[o - 1], rs_recv.at[k, r_y + o - 1], rs_send.at[k, r_y + o - 1])
        mine = g.at[y, c]
        add_rows(rows, mine, 0, [ry.at[o - 1] for o in range(1, n_y)])
        for o in range(1, n_x):
            to = turn(x, o, n_x)
            if by_x > 1:

                def make(o=o):
                    at = turn(x, o, n_x) * rows_x
                    return chunk(k)[0].at[y, c, pl.ds(aligned(at, 16), rows_x), :]

                go(make, rx.at[o - 1], rs, (k, r_x + o - 1), here.to(x=to))
            else:
                go(lambda: chunk(k)[0].at[y, c], rx.at[x], rs, (k, r_x + o - 1), here.to(x=to))

    def reduce_z(k):
        g, _, _, rx, rz, _, rows = chunk(k)
        by_x, rows_x, by_z, rows_z = splits(rows)
        mine = g.at[y, c]
        for o in range(1, n_x):
            slot = rx.at[o - 1] if by_x > 1 else rx.at[turn(x, n_x - o, n_x)]
            arrived(slot, rs_recv.at[k, r_x + o - 1], rs_send.at[k, r_x + o - 1])
        if by_x > 1:
            start = x * rows_x
            add_rows(rows_x, mine, start, [rx.at[o - 1] for o in range(1, n_x)])
        else:
            start = 0
            rx[x] = mine[...]
            for o in range(1, n_x):
                gone(rs, (k, r_x + o - 1))
            step = step_of(rows)

            def one(index, nothing):
                at = pl.ds(aligned(index * step, 16), step)
                g[y, c, at, :] = total_of(rx, n_x, index * step, step).astype(BF)
                return nothing

            lax.fori_loop(0, rows // step, one, 0)
        for o in range(1, n_z):

            def make(o=o):
                at = x * rows_x if by_x > 1 else 0
                if by_z > 1:
                    at = at + turn(z, o, n_z) * rows_z
                return chunk(k)[0].at[y, c, pl.ds(aligned(at, 16), rows_z), :]

            slot = rz.at[o - 1] if by_z > 1 else rz.at[z]
            go(make, slot, rs, (k, r_z + o - 1), here.to(z=turn(z, o, n_z)))

    def gather_z(k):
        g, _, _, _, rz, res, rows = chunk(k)
        by_x, rows_x, by_z, rows_z = splits(rows)
        start = x * rows_x if by_x > 1 else 0
        if by_z > 1:
            start = start + z * rows_z
        for o in range(1, n_z):
            slot = rz.at[o - 1] if by_z > 1 else rz.at[turn(z, n_z - o, n_z)]
            arrived(slot, rs_recv.at[k, r_z + o - 1], rs_send.at[k, r_z + o - 1])
        own_slot = n_z - 1 if by_z > 1 else z
        rz[own_slot] = g[y, c, pl.ds(aligned(start, 16), rows_z), :]
        share = 1.0 / ((1 if by_x > 1 else n_x) * (1 if by_z > 1 else n_z))
        step = step_of(rows_z, 96)

        def one(index, total):
            low = total_of(rz, n_z, index * step, step).astype(BF)
            res[pl.ds(aligned(start + index * step, 16), step), :] = low
            wide = low.astype(F32)
            return total + fold(wide * wide)

        total = lax.fori_loop(0, rows_z // step, one, zeros) * share
        for at in range(0, D, 128):
            square_sum[...] = square_sum[...] + total[:, at : at + 128]
        if by_z > 1:

            def make():
                at = x * rows_x if by_x > 1 else 0
                return chunk(k)[5].at[pl.ds(aligned(at + z * rows_z, 16), rows_z), :]

            for o in range(1, n_z):
                go(make, make(), rs, (k, r_gz + o - 1), here.to(z=turn(z, o, n_z)))

    def gather_x(k):
        res, rows = chunk(k)[5:7]
        by_x, rows_x, by_z, rows_z = splits(rows)
        if by_z > 1:
            for o in range(1, n_z):
                start = turn(z, n_z - o, n_z) * rows_z
                if by_x > 1:
                    start = start + x * rows_x
                arrived(
                    res.at[pl.ds(aligned(start, 16), rows_z), :],
                    rs_recv.at[k, r_gz + o - 1], rs_send.at[k, r_gz + o - 1],
                )
        if by_x > 1:

            def make():
                return chunk(k)[5].at[pl.ds(aligned(x * rows_x, 16), rows_x), :]

            for o in range(1, n_x):
                go(make, make(), rs, (k, r_gx + o - 1), here.to(x=turn(x, o, n_x)))

    def result(k):
        if k < CHUNKS:
            return pltpu.make_async_copy(RES.at[k], res_out.at[k], out_local.at[1 + k])
        return pltpu.make_async_copy(
            SRES.at[k - CHUNKS], small_out.at[k - CHUNKS], out_local.at[1 + k]
        )

    def gather_done(k):
        res, rows = chunk(k)[5:7]
        by_x, rows_x = splits(rows)[0:2]
        if by_x > 1:
            for o in range(1, n_x):
                start = turn(x, n_x - o, n_x) * rows_x
                arrived(
                    res.at[pl.ds(aligned(start, 16), rows_x), :],
                    rs_recv.at[k, r_gx + o - 1], rs_send.at[k, r_gx + o - 1],
                )
        result(k).start()

    for k in range(CHUNKS + 2):
        actions[f"core{k}"] = functools.partial(reduce_core, k)
        actions[f"y{k}"] = functools.partial(reduce_y, k)
        actions[f"x{k}"] = functools.partial(reduce_x, k)
        actions[f"z{k}"] = functools.partial(reduce_z, k)
        actions[f"gz{k}"] = functools.partial(gather_z, k)
        actions[f"gx{k}"] = functools.partial(gather_x, k)
        actions[f"gd{k}"] = functools.partial(gather_done, k)
    actions.update(
        fc=factors_core, fy=factors_y, fz=factors_z, fx=factors_x, fm=factors_mate,
        fd=factors_done,
    )

    def tails(ref, layer=None):
        found = []
        for image in range(KEPT):
            rows = slice(image * BLK + TAIL, (image + 1) * BLK)
            found.append(ref[rows, :] if layer is None else ref[layer, rows, :])
        return jnp.concatenate(found, axis=0)

    @pl.when(lower)
    def _():
        arrived(lab.at[1], img_recv.at[2], img_send.at[2])

    marked = lab[...].reshape(CROWS, 128)[:, 0:1]

    h1 = tails(DXB)
    stream = tails(X)
    query = ((mm(h1, win[last, :, 0:D]) + vector(last, 2 * D, D)).astype(BF)) * BF(0.125)
    head_masks = [lane_mask(D, index * 64, (index + 1) * 64) for index in range(HEADS)]

    def spread(values):
        return jnp.concatenate([values * mask for mask in head_masks], axis=0)

    def gather_heads(values):
        total = None
        for index in range(HEADS):
            part = values[index * 16 : (index + 1) * 16] * head_masks[index].astype(F32)
            total = part if total is None else total + part
        return total

    spread_queries, probabilities, outs = [], [], []
    for image in range(KEPT):
        rows = slice(image * BLK, (image + 1) * BLK)
        queries = spread(query[image * 16 : (image + 1) * 16])
        scores = mm_nt(queries, DMB[rows, :]) + key_row
        raw = jnp.exp(scores - jnp.max(scores, axis=-1, keepdims=True))
        probs = raw * (1.0 / jnp.sum(raw, axis=-1, keepdims=True))
        spread_queries.append(queries)
        probabilities.append(probs)
        outs.append(gather_heads(mm(probs.astype(BF), DA[rows, :])))
    attended = jnp.concatenate(outs, axis=0).astype(BF)
    middle = stream + mm(attended, win[last, :, 3 * D : 4 * D]) + vector(last, 4 * D, D)
    n2, i2 = norm(middle)
    h2 = (n2 * vector(last, 5 * D, D) + vector(last, 6 * D, D)).astype(BF)
    active, slope = gelu_parts(mm(h2, win[last, :, 4 * D :]) + vector(last, 7 * D, FF))
    active = active.astype(BF)
    top = middle + mm(active, wdn[last]) + vector(last, 7 * D + FF, D)
    gain_final = glob[2:3, :]
    nf, inf = norm(top)
    final = (nf * gain_final + glob[3:4, :]).astype(BF)
    class_lane = lax.broadcasted_iota(jnp.int32, (1, CPAD), 1)
    logits = mm(final, low_head[...]) + head_bias[...]
    logits = jnp.where(class_lane < NCLS, logits, -1e30)
    peak = jnp.max(logits, axis=-1, keepdims=True)
    shifted = logits - peak
    raw = jnp.exp(shifted)
    total = jnp.sum(raw, axis=-1, keepdims=True)
    alive = jnp.where(marked >= 0.0, 1.0, 0.0)
    target = jnp.where(class_lane.astype(F32) == marked, 1.0 - SMOOTHING, 0.0) + jnp.where(
        class_lane < NCLS, SMOOTHING / NCLS, 0.0
    )
    log_probs = jnp.where(class_lane < NCLS, shifted - jnp.log(total), 0.0)
    losses = -jnp.sum(target * log_probs, axis=-1, keepdims=True) * alive
    d_logits = ((raw * (1.0 / total) - target) * alive).astype(BF)
    d_final = mm_nt(d_logits, low_head[...])
    last_row = VEC_AT + 12 * LAYERS
    V[last_row : last_row + 1, 0:D] = down_sum(d_final * nf)
    V[last_row + 1 : last_row + 2, 0:D] = down_sum(d_final)
    V[last_row + 2 : last_row + 3, 0:128] = jnp.broadcast_to(down_sum(losses), (1, 128))
    V[last_row + 3 : last_row + 4, 0:128] = jnp.full((1, 128), counts[0].astype(F32), F32)
    d_top = norm_back(d_final, nf, inf, gain_final)
    low_top = d_top.astype(BF)
    store_vector(last, 7 * D + FF, down_sum(d_top))
    d_up = (mm_nt(low_top, wdn[last]) * slope).astype(BF)
    store_vector(last, 7 * D, down_sum(d_up.astype(F32)))
    d_h2 = mm_nt(d_up, win[last, :, 4 * D :])
    store_vector(last, 5 * D, down_sum(d_h2 * n2))
    store_vector(last, 6 * D, down_sum(d_h2))
    d_middle = d_top + norm_back(d_h2, n2, i2, vector(last, 5 * D, D))
    low_middle = d_middle.astype(BF)
    store_vector(last, 4 * D, down_sum(d_middle))
    d_heads = mm_nt(low_middle, win[last, :, 3 * D : 4 * D]).astype(BF)
    d_queries = []
    for image in range(KEPT):
        rows = slice(image * BLK, (image + 1) * BLK)
        ups = spread(d_heads[image * 16 : (image + 1) * 16])
        probs = probabilities[image]
        d_probs = mm_nt(ups, DA[rows, :])
        inner = jnp.sum(d_probs * probs, axis=-1, keepdims=True)
        d_scores = (probs * (d_probs - inner)).astype(BF)
        d_queries.append(gather_heads(mm(d_scores, DMB[rows, :])) * 0.125)
        DMB[rows, :] = mm_tn(d_scores, spread_queries[image]).astype(BF)
        DA[rows, :] = mm_tn(probs.astype(BF), ups).astype(BF)
    d_query = jnp.concatenate(d_queries, axis=0).astype(BF)
    store_vector(last, 2 * D, down_sum(d_query.astype(F32)))
    from_query = mm_nt(d_query, win[last, :, 0:D])

    pick_row = lax.broadcasted_iota(jnp.int32, (group, CROWS), 0)
    pick_lane = lax.broadcasted_iota(jnp.int32, (group, CROWS), 1)
    pick = jnp.where(
        ((pick_row - KEPT * here.shard) * 16 + (CLS - TAIL)) == pick_lane, 1.0, 0.0
    ).astype(BF)
    at = 0
    for piece in (active, h2, attended, h1, final, low_top):
        FAC[0, :, at : at + piece.shape[-1]] = mm(pick, piece).astype(BF)
        at += piece.shape[-1]
    at = 0
    for piece in (d_up, low_middle, d_query, d_logits):
        FAC[1, :, at : at + piece.shape[-1]] = mm(pick, piece).astype(BF)
        at += piece.shape[-1]
    FAC[1, :, at:] = jnp.zeros((group, WFAC - at), BF)
    at_place("class")

    turned = DXB[...].T
    for tile, grads in enumerate((DMB, DA)):
        made = mm(turned, grads[...]).astype(BF)
        for shard in range(n_shard):
            GS[0, shard // 2, shard % 2, tile * rows_in : (tile + 1) * rows_in, :] = made[
                shard * rows_in : (shard + 1) * rows_in
            ]
    at_place("kv")
    store_sums(last, [(3 * D, fold(DA[...].astype(F32)))])

    X[...] = jnp.zeros((ROWS, D), F32)
    gain = vector(last, 0, D)
    gain_sum, shift_sum = zeros, zeros
    for image in range(KEPT):
        rows = slice(image * BLK + TAIL, (image + 1) * BLK)
        part = from_query[image * 16 : (image + 1) * 16]
        normed = N1[last, rows, :].astype(F32)
        gain_sum = gain_sum + fold(part * normed)
        shift_sum = shift_sum + fold(part)
        X[rows, :] = d_middle[image * 16 : (image + 1) * 16] + norm_back(
            part, normed, whole_lanes_of(I1[last, rows, :]), gain
        )

    def first_back(layer, half, made, sums):
        base = half * HALF
        gain = vector(layer, 0, D)
        gain_sum, shift_sum = sums
        for at, size in pieces(HALF):
            rows = pl.ds(aligned(base + at, 16), size)
            part = made[at : at + size]
            normed = N1[layer, rows, :].astype(F32)
            inverse = whole_lanes_of(I1[layer, rows, :])
            gain_sum = gain_sum + fold(part * normed)
            shift_sum = shift_sum + fold(part)
            X[rows, :] = X[rows, :] + norm_back(part, normed, inverse, gain)
        return gain_sum, shift_sum

    def last_back(half, sums):
        rows = pl.ds(aligned(half * HALF, 16), HALF)
        made = mm_nt(DMB[rows, :], win[last, :, D : 2 * D])
        made = made + mm_nt(DA[rows, :], win[last, :, 2 * D : 3 * D])
        sums = first_back(last, half, made, sums)
        at_place("lb", half)
        return sums

    gain_sum, shift_sum = lax.fori_loop(0, 2, last_back, (gain_sum, shift_sum))
    store_sums(last, [(0, gain_sum), (D, shift_sum)])

    def round_up(half, total):
        for at, size in pieces(HALF):
            rows = pl.ds(aligned(half * HALF + at, 16), size)
            up = X[rows, :]
            DXB[rows, :] = up.astype(BF)
            total = total + fold(up)
        return total

    def act_back(layer, half, totals):
        base = half * HALF
        low = DXB[pl.ds(aligned(base, 16), HALF), :]
        ups = []
        for pair in range(2):
            made = mm_nt(low, wdn[layer, 2 * pair * D : 2 * (pair + 1) * D, :])
            for tile in range(2):
                start = (2 * pair + tile) * D
                columns = slice(start, start + D)
                total = totals[2 * pair + tile]
                for at, size in pieces(HALF):
                    rows = pl.ds(aligned(base + at, 16), size)
                    part = made[at : at + size, tile * D : (tile + 1) * D]
                    grad = (part * SLOPE[layer, rows, columns].astype(F32)).astype(BF)
                    DH[rows, columns] = grad
                    total = total + fold(grad.astype(F32))
                ups.append(total)
        return tuple(ups)

    def mlp_back(layer, half, sums):
        base = half * HALF
        whole = pl.ds(aligned(base, 16), HALF)
        gain_sum, shift_sum, bias_out = sums
        made = mm_nt(DH[whole, :], win[layer, :, 4 * D :])
        gain = vector(layer, 5 * D, D)
        for at, size in pieces(HALF):
            rows = pl.ds(aligned(base + at, 16), size)
            part = made[at : at + size]
            normed = N2[layer, rows, :].astype(F32)
            inverse = whole_lanes_of(I2[layer, rows, :])
            gain_sum = gain_sum + fold(part * normed)
            shift_sum = shift_sum + fold(part)
            grad = X[rows, :] + norm_back(part, normed, inverse, gain)
            X[rows, :] = grad
            DMB[rows, :] = grad.astype(BF)
            bias_out = bias_out + fold(grad)
        DA[whole, :] = mm_nt(DMB[whole, :], win[layer, :, 3 * D : 4 * D]).astype(BF)
        return gain_sum, shift_sum, bias_out

    def attend_back(layer, image):
        rows = pl.ds(aligned(image * BLK, 16), BLK)
        for pair in range(3):
            at = pair * 128
            query = QKV[layer, rows, at : at + 128] * BF(0.125)
            keys = QKV[layer, rows, D + at : D + at + 128]
            values = QKV[layer, rows, 2 * D + at : 2 * D + at + 128]
            ups = DA[rows, at : at + 128]
            keys_both = jnp.concatenate([keys * even, keys * odd], axis=0)
            values_both = jnp.concatenate([values * even, values * odd], axis=0)
            scores = mm_nt(keys_both, query)
            d_probs = mm_nt(values_both, ups)
            probs, d_scores = [], []
            for base in (0, BLK):
                low_probs, low_grads = [], []
                for first, end in ((0, 128), (128, BLK)):
                    part = jnp.concatenate(
                        [
                            scores[base : base + TAIL, first:end],
                            scores[base + TAIL : base + BLK, first:end] + key_column[TAIL:],
                        ],
                        axis=0,
                    )
                    raw = jnp.exp(part - jnp.max(part, axis=0, keepdims=True))
                    prob = raw * (1.0 / jnp.sum(raw, axis=0, keepdims=True))
                    grad = d_probs[base : base + BLK, first:end]
                    inner = jnp.sum(grad * prob, axis=0, keepdims=True)
                    low_grads.append((prob * (grad - inner)).astype(BF))
                    low_probs.append(prob.astype(BF))
                probs.append(jnp.concatenate(low_probs, axis=1))
                d_scores.append(jnp.concatenate(low_grads, axis=1))
            probs = jnp.concatenate(probs, axis=0)
            d_scores = jnp.concatenate(d_scores, axis=0)
            d_values = mm(probs, ups)
            d_keys = mm(d_scores, query)
            d_query = mm_tn(d_scores, keys_both) * 0.125
            DH[rows, at : at + 128] = d_query.astype(BF)
            DH[rows, D + at : D + at + 128] = jnp.where(
                low_lane, d_keys[:BLK], d_keys[BLK:]
            ).astype(BF)
            DH[rows, 2 * D + at : 2 * D + at + 128] = jnp.where(
                low_lane, d_values[:BLK], d_values[BLK:]
            ).astype(BF)

    def renew(ref, layer, at):
        gain, shift = vector(layer, at, D), vector(layer, at + D, D)

        def one(index, nothing):
            for at, size in pieces(BLK):
                rows = pl.ds(aligned(index * BLK + at, 16), size)
                DXB[rows, :] = (ref[layer, rows, :].astype(F32) * gain + shift).astype(BF)
            return nothing

        lax.fori_loop(0, KEPT, one, 0)
        return DXB[...].T

    def keep_in(k, tile, made):
        for shard in range(n_shard):
            G[k, shard // 2, shard % 2, tile * rows_in : (tile + 1) * rows_in, :] = made[
                shard * rows_in : (shard + 1) * rows_in
            ]

    def backward(step, carry):
        layer = LAYERS - 2 - step
        kd, ku, kq = 3 * step, 3 * step + 1, 3 * step + 2
        bias_down = lax.fori_loop(0, 2, round_up, zeros)
        at_place("round", layer)
        turned = DXB[...].T
        per = min(rows_down, D)
        for pair in range(2):
            start = 2 * pair * D
            wide = mm(turned, ACT[layer, :, start : start + 2 * D]).astype(BF)
            for tile in range(2):
                made = wide[:, tile * D : (tile + 1) * D].T
                for piece in range(D // per):
                    shard, at = divmod(start + tile * D + piece * per, rows_down)
                    G[kd, shard // 2, shard % 2, at : at + per, :] = made[
                        piece * per : (piece + 1) * per
                    ]
        at_place("dn", layer)

        def one(half, totals):
            totals = act_back(layer, half, totals)
            at_place("act", layer, half)
            return totals

        bias_up = lax.fori_loop(0, 2, one, (zeros,) * 4)
        turned = renew(N2, layer, 5 * D)
        for pair in range(2):
            made = mm(turned, DH[:, 2 * pair * D : 2 * (pair + 1) * D]).astype(BF)
            keep_in(ku, 2 * pair, made[:, :D])
            keep_in(ku, 2 * pair + 1, made[:, D:])
        at_place("ups", layer)

        def one_more(half, sums):
            sums = mlp_back(layer, half, sums)
            at_place("mlpb", layer, half)
            return sums

        gain_sum, shift_sum, bias_out = lax.fori_loop(0, 2, one_more, (zeros, zeros, zeros))
        store_sums(
            layer,
            [(7 * D + FF, bias_down), (5 * D, gain_sum), (6 * D, shift_sum), (4 * D, bias_out)]
            + [(7 * D + tile * D, bias_up[tile]) for tile in range(4)],
        )
        keep_in(kq, 3, mm(ATT[layer].T, DMB[...]).astype(BF))
        at_place("out", layer)

        def two(image, nothing):
            attend_back(layer, image)
            at_place("attb", layer, image)
            return nothing

        lax.fori_loop(0, KEPT, two, 0)
        turned = renew(N1, layer, 0)
        made = mm(turned, DH[:, 0 : 2 * D]).astype(BF)
        keep_in(kq, 0, made[:, :D])
        keep_in(kq, 1, made[:, D:])
        keep_in(kq, 2, mm(turned, DH[:, 2 * D : 3 * D]).astype(BF))
        at_place("qkv", layer)
        store_sums(
            layer,
            [
                (2 * D, fold(DH[:, 0:D].astype(F32))),
                (3 * D, fold(DH[:, 2 * D : 3 * D].astype(F32))),
            ],
        )

        def three(half, sums):
            rows = pl.ds(aligned(half * HALF, 16), HALF)
            made = mm_nt(DH[rows, 0 : 3 * D], win[layer, :, 0 : 3 * D])
            sums = first_back(layer, half, made, sums)
            at_place("fb", layer, half)
            return sums

        gain_sum, shift_sum = lax.fori_loop(0, 2, three, (zeros, zeros))
        store_sums(layer, [(0, gain_sum), (D, shift_sum)])
        return carry

    lax.fori_loop(0, LAYERS - 1, backward, 0)

    for at, size in pieces(BLK):
        total = None
        for image in range(KEPT):
            part = X[image * BLK + at : image * BLK + at + size, :]
            DXB[image * BLK + at : image * BLK + at + size, :] = part.astype(BF)
            total = part if total is None else total + part
        V[at : at + size, 0:D] = total

    vec = ("v", v_send, v_recv)
    v_y, v_x = 1, n_y
    v_z = v_x + n_x - 1
    v_gz = v_z + n_z - 1
    v_gx = v_gz + n_z - 1
    v_gy = v_gx + n_x - 1
    v_gc = v_gy + n_y - 1
    rows_c = VEC_ROWS // 2
    rows_y = rows_c // n_y
    rows_x = rows_y // n_x
    split_z = cut(rows_x, n_z, 8)
    rows_z = rows_x // split_z
    at_c = c * rows_c
    at_y = at_c + y * rows_y
    at_x = at_y + x * rows_x
    at_z = at_x + z * rows_z if split_z > 1 else at_x

    def vrows(ref, at, rows):
        return ref.at[pl.ds(aligned(at, 8), rows), :]

    def vadd(at, rows, sources):
        target = pl.ds(aligned(at, 8), rows)
        total = V[target, :]
        for source in sources:
            total = total + source
        V[target, :] = total

    def vectors_core():
        go(lambda: vrows(V, (1 - c) * rows_c, rows_c), VC, vec, 0, mate)

    def vectors_y():
        arrived(VC, v_recv.at[0], v_send.at[0])
        vadd(at_c, rows_c, [VC[...]])
        for o in range(1, n_y):
            to = turn(y, o, n_y)
            go(
                lambda o=o: vrows(V, at_c + turn(y, o, n_y) * rows_y, rows_y), VY.at[o - 1],
                vec, v_y + o - 1, here.to(y=to),
            )

    def vectors_x():
        for o in range(1, n_y):
            arrived(VY.at[o - 1], v_recv.at[v_y + o - 1], v_send.at[v_y + o - 1])
        vadd(at_y, rows_y, [VY[o - 1] for o in range(1, n_y)])
        for o in range(1, n_x):
            to = turn(x, o, n_x)
            go(
                lambda o=o: vrows(V, at_y + turn(x, o, n_x) * rows_x, rows_x), VX.at[o - 1],
                vec, v_x + o - 1, here.to(x=to),
            )

    def vectors_z():
        for o in range(1, n_x):
            arrived(VX.at[o - 1], v_recv.at[v_x + o - 1], v_send.at[v_x + o - 1])
        vadd(at_x, rows_x, [VX[o - 1] for o in range(1, n_x)])
        for o in range(1, n_z):

            def make(o=o):
                at = at_x + turn(z, o, n_z) * rows_z if split_z > 1 else at_x
                return vrows(V, at, rows_z)

            go(make, VZ.at[z], vec, v_z + o - 1, here.to(z=turn(z, o, n_z)))

    def vectors_gather_z():
        for o in range(1, n_z):
            arrived(
                VZ.at[turn(z, n_z - o, n_z)], v_recv.at[v_z + o - 1], v_send.at[v_z + o - 1]
            )
        target = pl.ds(aligned(at_z, 8), rows_z)
        VZ[z] = V[target, :]
        total = VZ[0]
        for index in range(1, n_z):
            total = total + VZ[index]
        VF[target, :] = total
        if split_z > 1:
            for o in range(1, n_z):
                go(
                    lambda: vrows(VF, at_z, rows_z), vrows(VF, at_z, rows_z), vec, v_gz + o - 1,
                    here.to(z=turn(z, o, n_z)),
                )

    def vectors_gather_x():
        if split_z > 1:
            for o in range(1, n_z):
                came = turn(z, n_z - o, n_z)
                arrived(
                    vrows(VF, at_x + came * rows_z, rows_z), v_recv.at[v_gz + o - 1],
                    v_send.at[v_gz + o - 1],
                )
        for o in range(1, n_x):
            go(
                lambda: vrows(VF, at_x, rows_x), vrows(VF, at_x, rows_x), vec, v_gx + o - 1,
                here.to(x=turn(x, o, n_x)),
            )

    sq = ("q", q_send, q_recv)

    def squares_z():
        SQ[0] = square_sum[...]
        SQZ[z] = square_sum[...]
        for o in range(1, n_z):
            go(lambda: SQ.at[0], SQZ.at[z], sq, o - 1, here.to(z=turn(z, o, n_z)))

    def slot_of(i, j, k):
        return (i * n_y + j) * 2 + k

    def squares_plane():
        for o in range(1, n_z):
            arrived(SQZ.at[turn(z, n_z - o, n_z)], q_recv.at[o - 1], q_send.at[o - 1])
        total = SQZ[0]
        for index in range(1, n_z):
            total = total + SQZ[index]
        SQ[1] = total
        SQP[slot_of(x, y, c)] = total
        for index, step in enumerate(plane):
            go(
                lambda: SQ.at[1], SQP.at[slot_of(x, y, c)], sq, n_z - 1 + index,
                in_plane(step),
            )

    def squares_done():
        for index, (i, j, k) in enumerate(plane):
            slot = slot_of(
                turn(x, n_x - i, n_x), turn(y, n_y - j, n_y), lax.rem(c + k, 2)
            )
            arrived(SQP.at[slot], q_recv.at[n_z - 1 + index], q_send.at[n_z - 1 + index])
        total = SQP[0]
        for index in range(1, 2 * n_x * n_y):
            total = total + SQP[index]
        SQ[2] = total

    def vectors_gather_y():
        for o in range(1, n_x):
            at = at_y + turn(x, n_x - o, n_x) * rows_x
            arrived(vrows(VF, at, rows_x), v_recv.at[v_gx + o - 1], v_send.at[v_gx + o - 1])
        for o in range(1, n_y):
            go(
                lambda: vrows(VF, at_y, rows_y), vrows(VF, at_y, rows_y), vec, v_gy + o - 1,
                here.to(y=turn(y, o, n_y)),
            )

    def vectors_gather_core():
        for o in range(1, n_y):
            at = at_c + turn(y, n_y - o, n_y) * rows_y
            arrived(vrows(VF, at, rows_y), v_recv.at[v_gy + o - 1], v_send.at[v_gy + o - 1])
        go(lambda: vrows(VF, at_c, rows_c), vrows(VF, at_c, rows_c), vec, v_gc, mate)

    def vectors_done():
        arrived(vrows(VF, (1 - c) * rows_c, rows_c), v_recv.at[v_gc], v_send.at[v_gc])

    actions.update(
        vc=vectors_core, vy=vectors_y, vx=vectors_x, vz=vectors_z, vgz=vectors_gather_z,
        vgx=vectors_gather_x, vgy=vectors_gather_y, vgc=vectors_gather_core, vd=vectors_done,
        qz=squares_z, qp=squares_plane, qd=squares_done,
    )
    at_place("emb")
    low = DXB[...]
    for tile in range(2):
        made = mm_tn(pix[:, :, tile * D : (tile + 1) * D].reshape(ROWS, D), low).astype(BF)
        for piece in range(D // rows_patch):
            shard = tile * (D // rows_patch) + piece
            GS[1, shard // 2, shard % 2, 0:rows_patch, :] = made[piece * rows_patch : (piece + 1) * rows_patch]

    at_place("patch")
    ending = SCHEDULE["tail",]
    perform(ending[:-6])
    early = [
        key for key in sent
        if key[0] in ("ag", "f") or (key[0] == "rs" and key[1][0] not in (4, 5, 7))
    ]
    for key in early:
        source, send, recv, at = sent.pop(key)
        left_here(source(), recv.at[at], send.at[at])
    perform(ending[-6:])
    last_copies = [
        pltpu.make_async_copy(VF, vec_out, out_local.at[1 + CHUNKS + 2]),
        pltpu.make_async_copy(SQ.at[2], square_out, out_local.at[2 + CHUNKS + 2]),
    ]
    for copy in last_copies:
        copy.start()
    for source, send, recv, at in list(sent.values()):
        left_here(source(), recv.at[at], send.at[at])
    for k in range(CHUNKS + 2):
        result(k).wait()
    for copy in last_copies:
        copy.wait()

    @pl.when(jnp.logical_not(lower))
    def _():
        for index in range(2):
            left_here(given[index], img_recv.at[index], img_send.at[index])
        left_here(lab_given, img_recv.at[2], img_send.at[2])


def run_train(
    n_rep, n_shard, patches, patch_ends, labels, counts, own_patch, own_in, own_down, vecs, glob, pos, head
):
    n_x = 2 ** ((n_rep.bit_length() - 2) // 2)
    n_z, n_y = n_rep // n_x, n_shard // 2
    block = 4 * (D // n_shard)
    small_block = small_rows(block // 2, n_x, n_z)
    group = KEPT * n_shard
    keep = LAYERS - 1
    units = 1 + 3 * LAYERS
    chunks = CHUNKS + 2

    def buf(*shape, dtype=BF):
        return pltpu.VMEM(shape, dtype)

    def sems(*shape):
        return pltpu.SemaphoreType.DMA(shape)

    def reduction(count, slots, rows):
        by_x = cut(rows, n_x, 16)
        by_z = cut(rows // by_x, n_z, 16)
        return [
            buf(count, n_y, 2, rows, D),
            buf(slots, n_y, rows, D),
            buf(slots, n_y - 1, rows, D),
            buf(slots, n_x - 1 if by_x > 1 else n_x, rows // by_x, D),
            buf(slots, n_z, rows // by_x // by_z, D),
            buf(count, rows, D),
        ]

    rows_y = VEC_ROWS // 2 // n_y
    rows_x = rows_y // n_x
    rows_z = rows_x // cut(rows_x, n_z, 8)
    ag_count = n_y + (n_y - 1) * (n_x - 1) * 2 + n_y - 1
    rs_count = 1 + (n_y - 1) + 2 * (n_x - 1) + 2 * (n_z - 1)
    f_count = 1 + (n_y - 1) + (n_x - 1) + (n_z - 1) + 1
    v_count = 1 + 2 * (n_y - 1) + 2 * (n_x - 1) + 2 * (n_z - 1) + 1
    q_count = n_z - 1 + 2 * n_x * n_y - 1
    whole = pl.BlockSpec(memory_space=pltpu.VMEM)
    there = pl.BlockSpec(memory_space=pl.ANY)
    return pl.pallas_call(
        functools.partial(train, n_rep, n_shard),
        out_shape=[
            jax.ShapeDtypeStruct((CHUNKS, block, D), BF),
            jax.ShapeDtypeStruct((2, small_block, D), BF),
            jax.ShapeDtypeStruct((VEC_ROWS, VEC_WIDE), F32),
            jax.ShapeDtypeStruct((8, 128), F32),
            jax.ShapeDtypeStruct((2, n_x, n_z, group, WFAC), BF),
        ],
        in_specs=[there] * 2 + [pl.BlockSpec(memory_space=pltpu.SMEM)] * 2 + [there] * 3 + [whole] * 4,
        out_specs=[there] * 5,
        scratch_shapes=[
            buf(ROWS, D, dtype=F32),
            buf(LAYERS, ROWS, D),
            buf(LAYERS, ROWS, 128, dtype=F32),
            buf(keep, ROWS, 3 * D),
            buf(keep, ROWS, D),
            buf(keep, ROWS, D),
            buf(keep, ROWS, 128, dtype=F32),
            buf(keep, ROWS, FF),
            buf(keep, ROWS, FF),
            buf(ROWS, D),
            buf(ROWS, D),
            buf(ROWS, D),
            buf(ROWS, FF),
            buf(KEPT, BLK, PATCH_DIM),
            buf(2, 32, 128, dtype=F32),
            buf(32, 128, dtype=F32),
            buf(PATCH_DIM, D),
            buf(LAYERS, D, 4 * D + FF),
            buf(LAYERS, FF, D),
            buf(D, CPAD),
            buf(1, CPAD, dtype=F32),
            *reduction(CHUNKS, 3, block),
            *reduction(2, 1, small_block),
            buf(2, group, WFAC),
            buf(group, WFAC),
            buf(n_y - 1, group, WFAC),
            buf(n_z, group, WFAC),
            buf(VEC_ROWS, VEC_WIDE, dtype=F32),
            buf(VEC_ROWS // 2, VEC_WIDE, dtype=F32),
            buf(n_y - 1, rows_y, VEC_WIDE, dtype=F32),
            buf(n_x - 1, rows_x, VEC_WIDE, dtype=F32),
            buf(n_z, rows_z, VEC_WIDE, dtype=F32),
            buf(VEC_ROWS, VEC_WIDE, dtype=F32),
            buf(3, 8, 128, dtype=F32),
            buf(n_z, 8, 128, dtype=F32),
            buf(2 * n_x * n_y, 8, 128, dtype=F32),
            buf(8, 128, dtype=F32),
            sems(units, ag_count),
            sems(units, ag_count),
            sems(units, 4),
            sems(chunks, rs_count),
            sems(chunks, rs_count),
            sems(f_count),
            sems(f_count),
            sems(v_count),
            sems(v_count),
            sems(q_count),
            sems(q_count),
            sems(3),
            sems(3),
            sems(4),
            sems(3 + chunks),
        ],
        compiler_params=pltpu.CompilerParams(
            vmem_limit_bytes=65400 * 1024, collective_id=0, has_side_effects=True
        ),
        cost_estimate=pl.CostEstimate(
            flops=24_000_000_000, bytes_accessed=30_000_000, transcendentals=10_000_000
        ),
        name="train_step",
    )(patches, patch_ends, labels, counts, own_patch, own_in, own_down, vecs, glob, pos, head)


def adam(weight, first, second, grad, factor, rate):
    grad = grad * factor
    first = BETA_FIRST * first + (1.0 - BETA_FIRST) * grad
    second = BETA_SECOND * second + (1.0 - BETA_SECOND) * (grad * grad)
    first_scale = 1.0 / (1.0 - BETA_FIRST**ADAM_STEP)
    root_scale = (1.0 / (1.0 - BETA_SECOND**ADAM_STEP)) ** 0.5
    bottom = second * lax.rsqrt(second) * root_scale + ADAM_EPS
    step = first * lax.rsqrt(bottom * bottom)
    weight = weight * (1.0 - rate * WEIGHT_DECAY) - step * (rate * first_scale)
    return weight, first, second


def update(n_rep, n_shard, *refs):
    res, small, vec, exchanged, factors = refs[0:5]
    sources = refs[5:26]
    loss_out, norm_out = refs[26:28]
    targets = refs[28:49]
    buffers = refs[49:70]
    results = refs[70:91]
    last_in, last_down, passing, grad_head, in_sems, out_sems = refs[91:]
    shard = lax.axis_index("shard")
    rows_in = D // n_shard
    rows_down = FF // n_shard
    keep = LAYERS - 1

    def moves(array, layer=None, out=False):
        found = []
        for kind in range(3):
            index = 3 * array + kind
            if out:
                src, dst, sem = results[index], targets[index], out_sems
            else:
                src, dst, sem = sources[index], buffers[index], in_sems
            slot = 0 if layer is None else layer
            if layer is not None:
                src, dst = src.at[layer], dst.at[layer]
            found.append(pltpu.make_async_copy(src, dst, sem.at[index, slot]))
        return found

    layered = [(1, layer) for layer in range(LAYERS)] + [(2, layer) for layer in range(LAYERS)]
    order = layered + [(0, None), (6, None), (5, None), (3, None), (4, None)]
    for array, layer in order:
        for move in moves(array, layer):
            move.start()

    n_rows = factors.shape[1] * factors.shape[2] * factors.shape[3]

    def factor(half, at, size):
        return factors[half, :, :, :, at : at + size].reshape(n_rows, size)

    def squares(values):
        return fold(values * values)

    total = jnp.zeros((8, D), F32)
    own_rows = pl.multiple_of(shard * rows_in, 8)

    def keep_in(column, made):
        slot = column % 2
        passing[slot] = made
        last_in[:, column * D : (column + 1) * D] = passing[slot, pl.ds(own_rows, rows_in), :]

    h2 = factor(0, FF, D)
    for tile in range(4):
        made = mm_tn(h2, factor(1, tile * D, D))
        keep_in(4 + tile, made)
        total = total + squares(made)
    for tile in range(2):
        last_in[:, (1 + tile) * D : (2 + tile) * D] = small[
            0, tile * rows_in : (tile + 1) * rows_in, :
        ].astype(F32)
    made = mm_tn(factor(0, FF + 2 * D, D), factor(1, FF + D, D))
    keep_in(0, made)
    total = total + squares(made)
    made = mm_tn(factor(0, FF + D, D), factor(1, FF, D))
    keep_in(3, made)
    total = total + squares(made)
    d_top = factor(0, FF + 4 * D, D)
    per = min(rows_down, D)
    for tile in range(4):
        made = mm_tn(factor(0, tile * D, D), d_top)
        total = total + squares(made)
        for piece in range(D // per):
            owner, at = divmod(tile * D + piece * per, rows_down)

            def keep_down(made=made, piece=piece, at=at):
                last_down[at : at + per, :] = made[piece * per : (piece + 1) * per]

            pl.when(shard == owner)(keep_down)
    final = factor(0, FF + 3 * D, D)
    wide = jnp.zeros((8, 128), F32)
    for at in range(0, CPAD, 512):
        d_logits = factor(1, FF + 2 * D + at, 512)
        made = mm_tn(final, d_logits)
        grad_head[0:D, at : at + 512] = made
        bias = down_sum(d_logits.astype(F32))
        grad_head[D : D + 1, at : at + 512] = bias
        sums = squares(made)
        for lane in range(0, 512, 128):
            wide = wide + sums[:, lane : lane + 128]
            row = bias[:, lane : lane + 128]
            wide = wide + (row * row) * 0.125
    for lane in range(0, D, 128):
        wide = wide + total[:, lane : lane + 128]
    used = VEC_AT + 12 * LAYERS + 2
    parts = jnp.zeros((8, D), F32)
    kept_rows = lax.broadcasted_iota(jnp.int32, (8, 1), 0)
    for at in range(0, used, 8):
        value = vec[at : at + 8, 0:D]
        if at + 8 > used:
            value = jnp.where(kept_rows + at < used, value, 0.0)
        parts = parts + value * value
    patch_bias = down_sum(vec[0:PATCHES, 0:D])
    class_row = vec[CLS : CLS + 1, 0:D]
    rest = (patch_bias * patch_bias + class_row * class_row) * 0.125
    parts = parts + rest
    for lane in range(0, D, 128):
        wide = wide + parts[:, lane : lane + 128]
    wide = wide + exchanged[...]
    sum_squares = jnp.sum(jnp.sum(wide, axis=1, keepdims=True), axis=0, keepdims=True)
    inv_count = 1.0 / vec[used + 1 : used + 2, 0:1]
    grad_norm = jnp.sqrt(sum_squares) * inv_count
    norm_out[...] = grad_norm
    loss_out[...] = vec[used : used + 1, 0:1] * inv_count
    scale = jnp.minimum(1.0, CLIP_NORM / grad_norm) * inv_count

    def apply(array, where, grad, rate):
        refs = [buffers[3 * array + kind] for kind in range(3)]
        made = adam(refs[0][where], refs[1][where], refs[2][where], grad, scale, rate)
        for kind, value in enumerate(made):
            results[3 * array + kind][where] = value

    def begin(array, layer=None):
        for move in moves(array, layer):
            move.wait()

    def finish(array, layer=None):
        for move in moves(array, layer, out=True):
            move.start()

    def loop(count, body):
        def one(index, nothing):
            body(index)
            return nothing

        lax.fori_loop(0, count, one, 0)

    step = 32 if rows_in % 32 == 0 else 16
    for layer in range(LAYERS):
        begin(1, layer)

        def column_of(column):
            lanes = pl.ds(pl.multiple_of(column * D, 128), D)
            for at in range(0, rows_in, step):
                if layer < keep:
                    k = 3 * (keep - 1 - layer) + jnp.where(column < 4, 2, 1)
                    row = pl.multiple_of(lax.rem(column, 4) * rows_in + at, 16)
                    grad = res[k, pl.ds(row, step), :].astype(F32)
                else:
                    grad = last_in[at : at + step, lanes]
                apply(1, (layer, slice(at, at + step), lanes), grad, LEARNING_RATE)

        loop(8, column_of)
        finish(1, layer)
    for layer in range(LAYERS):
        begin(2, layer)

        def rows_of(index):
            for part in range(3):
                at = pl.multiple_of(index * 96 + part * 32, 16)
                if layer < keep:
                    grad = res[3 * (keep - 1 - layer), pl.ds(at, 32), :].astype(F32)
                else:
                    grad = last_down[pl.ds(at, 32), :]
                apply(2, (layer, pl.ds(at, 32), slice(0, D)), grad, LEARNING_RATE)

        loop(rows_down // 96, rows_of)
        finish(2, layer)
    begin(0)

    def patch_rows(index):
        for part in range(3):
            at = pl.multiple_of(index * 96 + part * 32, 16)
            grad = small[1, pl.ds(at, 32), :].astype(F32)
            apply(0, (pl.ds(at, 32), slice(0, D)), grad, LEARNING_RATE)

    loop(PATCH_DIM // n_shard // 96, patch_rows)
    finish(0)
    begin(6)

    def head_rows(index):
        for part in range(3):
            rows = pl.ds(pl.multiple_of(index * 48 + part * 16, 16), 16)
            apply(6, (rows, slice(0, NCLS)), grad_head[rows, 0:NCLS], LEARNING_RATE)

    loop(D // 48, head_rows)
    apply(6, (slice(D, D + 1), slice(0, NCLS)), grad_head[D : D + 1, 0:NCLS], LEARNING_RATE)
    finish(6)
    begin(5)
    apply(5, (slice(0, 1), slice(0, D)), class_row, VECTOR_RATE)
    for at in range(0, PATCHES, 28):
        apply(
            5, (slice(1 + at, 29 + at), slice(0, D)), vec[at : at + 28, 0:D], VECTOR_RATE
        )
    finish(5)
    begin(3)
    for layer in range(LAYERS):
        for piece in range(12):
            row = VEC_AT + 12 * layer + piece
            where = (slice(layer, layer + 1), slice(piece * D, (piece + 1) * D))
            apply(3, where, vec[row : row + 1, 0:D], VECTOR_RATE)
    finish(3)
    begin(4)
    rows = [patch_bias, class_row, vec[used - 2 : used - 1, 0:D], vec[used - 1 : used, 0:D]]
    for index, row in enumerate(rows):
        apply(4, (slice(index, index + 1), slice(0, D)), row, VECTOR_RATE)
    finish(4)
    for array, layer in order:
        for move in moves(array, layer, out=True):
            move.wait()


def run_update(n_rep, n_shard, res, small, vec, squares, factors, arrays):
    whole = pl.BlockSpec(memory_space=pltpu.VMEM)
    there = pl.BlockSpec(memory_space=pl.ANY)
    one = jax.ShapeDtypeStruct((1, 1), F32)
    made = pl.pallas_call(
        functools.partial(update, n_rep, n_shard),
        out_shape=[one, one] + [jax.ShapeDtypeStruct(a.shape, F32) for a in arrays],
        in_specs=[whole] * 5 + [there] * 21,
        out_specs=[whole] * 2 + [there] * 21,
        scratch_shapes=[pltpu.VMEM(a.shape, F32) for a in (*arrays, *arrays)]
        + [
            pltpu.VMEM((D // n_shard, 4 * D + FF), F32),
            pltpu.VMEM((FF // n_shard, D), F32),
            pltpu.VMEM((2, D, D), F32),
            pltpu.VMEM((D + 8, CPAD), F32),
            pltpu.SemaphoreType.DMA((21, LAYERS)),
            pltpu.SemaphoreType.DMA((21, LAYERS)),
        ],
        compiler_params=pltpu.CompilerParams(vmem_limit_bytes=62 * 1024 * 1024),
        cost_estimate=pl.CostEstimate(
            flops=200_000_000, bytes_accessed=50_000_000, transcendentals=4_000_000
        ),
        name="adamw",
    )(res, small, vec, squares, factors, *arrays)
    return made[0].reshape(()), made[1].reshape(()), made[2:]


def shards(
    n_rep, n_shard,
    patches, labels, counts, patch_w, layer_in, layer_down, layer_vecs, glob_vecs, pos_embed, head,
    m_patch, v_patch, m_in, v_in, m_down, v_down, m_vecs, v_vecs, m_glob, v_glob, m_pos, v_pos,
    m_head, v_head,
):
    ends = jnp.pad(patches[:, TAIL:], ((0, 0), (0, BLK - PATCHES), (0, 0)))
    res, small, vec, squares, factors = run_train(
        n_rep, n_shard, patches, ends, labels, counts, patch_w, layer_in, layer_down, layer_vecs,
        glob_vecs, pos_embed, head,
    )
    arrays = [
        patch_w, m_patch, v_patch, layer_in, m_in, v_in, layer_down, m_down, v_down,
        layer_vecs, m_vecs, v_vecs, glob_vecs, m_glob, v_glob, pos_embed, m_pos, v_pos,
        head, m_head, v_head,
    ]
    loss, grad_norm, new = run_update(n_rep, n_shard, res, small, vec, squares, factors, arrays)
    return (loss, grad_norm, *new)


def solution(mesh):
    everywhere = P()
    rows = P("shard", None)
    middle = P(None, "shard", None)
    return jax.shard_map(
        functools.partial(shards, mesh.shape["rep"], mesh.shape["shard"]),
        mesh=mesh,
        in_specs=(
            P(("rep", "shard"), None, None),
            P(("rep", "shard")),
            P(("rep", "shard")),
            rows,
            middle,
            middle,
            *(everywhere,) * 4,
            *(rows,) * 2,
            *(middle,) * 4,
            *(everywhere,) * 8,
        ),
        out_specs=(
            *(everywhere,) * 2,
            *(rows,) * 3,
            *(middle,) * 6,
            *(everywhere,) * 12,
        ),
        check_vma=False,
    )
```

```python
import functools

import jax
import jax.numpy as jnp
from jax import lax
from jax.experimental import pallas as pl
from jax.experimental.pallas import tpu as pltpu
from jax.sharding import PartitionSpec as P

D = 384
HEADS = 6
HEAD_DIM = 64
FF = 1536
PATCH_DIM = 768
PATCHES = 196
NCLS = 1000
LAYERS = 3
SEQ = 197

BLK = 208
CLS = 200
TAIL = 192
KEPT = 4
ROWS = KEPT * BLK
HALF = 2 * BLK
CROWS = KEPT * 16
CPAD = 1024
WIDE = 8 * D + FF

NORM_EPS = 1e-06
SMOOTHING = 0.1
CLIP_NORM = 0.05
LEARNING_RATE = 0.05
VECTOR_RATE = 0.5
BETA_FIRST = 0.9
BETA_SECOND = 0.999
ADAM_EPS = 1e-08
WEIGHT_DECAY = 0.05
ADAM_STEP = 10
GELU_SCALE = 0.7978845608028654
GELU_CUBIC = 0.044715

F32 = jnp.float32
BF = jnp.bfloat16


def mm(left, right):
    return jnp.dot(left, right, preferred_element_type=F32)


def mm_nt(left, right):
    return lax.dot_general(left, right, (((1,), (1,)), ((), ())), preferred_element_type=F32)


def mm_tn(left, right):
    return lax.dot_general(left, right, (((0,), (0,)), ((), ())), preferred_element_type=F32)


def fold(values):
    return jnp.sum(values.reshape(-1, 8, values.shape[-1]), axis=0)


def down_sum(values):
    return jnp.sum(values, axis=0, keepdims=True)


def norm(values):
    centre = values - jnp.mean(values, axis=-1, keepdims=True)
    inverse = lax.rsqrt(jnp.mean(centre * centre, axis=-1, keepdims=True) + NORM_EPS)
    return centre * inverse, inverse


def norm_back(upstream, normed, inverse, gain):
    scaled = upstream * gain
    first = jnp.mean(scaled, axis=-1, keepdims=True)
    second = jnp.mean(scaled * normed, axis=-1, keepdims=True)
    return inverse * (scaled - first - normed * second)


def gelu_parts(hidden):
    bent = hidden * (GELU_SCALE + (GELU_SCALE * GELU_CUBIC) * (hidden * hidden))
    tangent = jnp.tanh(bent)
    share = 0.5 + 0.5 * tangent
    slope = share + (1.0 - tangent * tangent) * (1.5 * bent - GELU_SCALE * hidden)
    return hidden * share, slope


def lane_mask(width, low, high):
    lane = lax.broadcasted_iota(jnp.int32, (1, width), 1)
    return jnp.where((lane >= low) & (lane < high), 1.0, 0.0).astype(BF)


STEP = 16


def pieces(total):
    return [(at, min(STEP, total - at)) for at in range(0, total, STEP)]


SCHEDULE = {
    ("cast", 0): ("ws0",),
    ("cast", 1): ("ws1",),
    ("cast", 2): ("ws2",),
    ("b_start",): ("wf0", "ws3", "wf1", "wr0", "ws4", "we0",),
    ("embed", 0): ("wf2", "ws5",),
    ("b_norm", 0, 0): ("wr1", "wf3", "ws6", "we1",),
    ("norm", 0, 0): ("wr2", "wf4", "ws7",),
    ("att", 0, 0, 1): ("wr3",),
    ("mid", 0, 0): ("wf5", "ws8",),
    ("b_up", 0, 0): ("we2",),
    ("up", 0, 0): ("wr4", "wf6", "ws9",),
    ("b_down", 0, 0): ("we3",),
    ("b_norm", 0, 1): ("wr5", "we4",),
    ("norm", 0, 1): ("wf7",),
    ("att", 0, 1, 0): ("wr6",),
    ("att", 0, 1, 1): ("wf8",),
    ("b_up", 0, 1): ("we5",),
    ("up", 0, 1): ("wr7", "wf9",),
    ("b_down", 0, 1): ("we6",),
    ("norm", 1, 0): ("wr8",),
    ("att", 1, 0, 1): ("wr9",),
    ("b_last",): ("we7", "we8", "we9",),
    ("class",): ("fc",),
    ("kv",): ("core6",),
    ("lb", 1): ("fy",),
    ("dn", 1): ("y6", "core0",),
    ("act", 1, 1): ("fz",),
    ("ups", 1): ("core1", "y0",),
    ("mlpb", 1, 1): ("x6",),
    ("attb", 1, 0): ("y1",),
    ("attb", 1, 2): ("z6",),
    ("attb", 1, 3): ("x0",),
    ("qkv", 1): ("fx", "core2",),
    ("fb", 1, 1): ("gz6",),
    ("dn", 0): ("y2", "x1", "z0", "core3",),
    ("act", 0, 0): ("gx6",),
    ("mlpb", 0, 0): ("gz0",),
    ("attb", 0, 0): ("x2", "y3", "core4", "fm",),
    ("attb", 0, 1): ("gx0",),
    ("attb", 0, 2): ("z1",),
    ("qkv", 0): ("gd6",),
    ("fb", 0, 1): ("fd",),
    ("emb",): ("z2", "x3", "y4", "core5", "gz1", "vc",),
    ("patch",): ("core7",),
    ("tail",): ("gd0", "gz2", "vy", "z3", "y7", "gx1", "x4", "y5", "vx", "gx2", "gd1", "gz3", "x7", "z4", "vz", "gx3", "gd2", "x5", "z7", "gz4", "vgz", "gd3", "gz7", "z5", "gx4", "vgx", "gx7", "gd4", "vgy", "gz5", "qz", "gd7", "vgc", "gx5", "qp", "vd", "gd5", "qd",),
}


WFAC = FF + 5 * D
VEC_ROWS = 256
VEC_AT = BLK
VEC_WIDE = D
MESH = pl.DeviceIdType.MESH
CHUNKS = 6


class Place:
    def __init__(self, n_rep, n_shard):
        self.n_rep, self.n_shard = n_rep, n_shard
        self.n_x = 2 ** ((n_rep.bit_length() - 2) // 2)
        self.n_z = n_rep // self.n_x
        self.n_y = n_shard // 2
        rep, shard = lax.axis_index("rep"), lax.axis_index("shard")
        self.rep, self.shard = rep, shard
        self.z, self.x = rep // self.n_x, rep % self.n_x
        self.y, self.c = shard // 2, shard % 2

    def to(self, x=None, y=None, z=None, c=None):
        x = self.x if x is None else x
        y = self.y if y is None else y
        z = self.z if z is None else z
        c = self.c if c is None else c
        return {"rep": z * self.n_x + x, "shard": y * 2 + c}


def cut(rows, parts, unit):
    return parts if rows % (parts * unit) == 0 else 1


def small_rows(rows, n_x, n_z):
    unit = 16 * n_x * n_z
    padded = -(-rows // unit) * unit
    return padded if 2 * padded <= 3 * rows else rows


def aligned(value, unit):
    return pl.multiple_of(value, unit)


def train(
    n_rep, n_shard,
    patches, patch_ends, labels, counts, own_patch, own_in, own_down, vecs, glob, pos, head,
    res_out, small_out, vec_out, square_out, all_factors,
    X, N1, I1, QKV, ATT, N2, I2, ACT, SLOPE, DXB, DMB, DA, DH,
    pix, lab, lab_given, wp, win, wdn, low_head, head_bias,
    G, RC, RY, RX, RZ, RES, GS, SC, SY, SX, SZ, SRES,
    FAC, FC, FY, V, VC, VY, VX, VZ, VF, SQ, SQZ, SQP, square_sum,
    ag_send, ag_recv, ag_local, rs_send, rs_recv, f_send, f_recv, v_send, v_recv,
    q_send, q_recv,
    img_send, img_recv, img_local, out_local,
):
    here = Place(n_rep, n_shard)
    n_x, n_y, n_z = here.n_x, here.n_y, here.n_z
    x, y, z, c = here.x, here.y, here.z, here.c
    rows_in, rows_down, rows_patch = D // n_shard, FF // n_shard, PATCH_DIM // n_shard
    block = 4 * rows_in
    small_block = small_rows(block // 2, n_x, n_z)
    mate = here.to(c=1 - c)

    def push(src, dst, send, recv, device):
        pltpu.make_async_remote_copy(
            src_ref=src, dst_ref=dst, send_sem=send, recv_sem=recv,
            device_id=device, device_id_type=MESH,
        ).start()

    def arrived(dst, recv, send):
        pltpu.make_async_remote_copy(
            src_ref=dst, dst_ref=dst, send_sem=send, recv_sem=recv,
            device_id=mate, device_id_type=MESH,
        ).wait_recv()

    def left_here(src, recv, send):
        pltpu.make_async_remote_copy(
            src_ref=src, dst_ref=src, send_sem=send, recv_sem=recv,
            device_id=mate, device_id_type=MESH,
        ).wait_send()

    sent = {}

    def go(source, dst, sems, index, device):
        name, send, recv = sems
        push(source(), dst, send.at[index], recv.at[index], device)
        sent[name, index] = (source, send, recv, index)

    def gone(sems, index):
        source, send, recv, at = sent.pop((sems[0], index))
        left_here(source(), recv.at[at], send.at[at])

    def turn(at, by, size):
        return lax.rem(at + by, size)

    barrier = pltpu.get_barrier_semaphore()
    plane = [
        (i, j, k) for i in range(n_x) for j in range(n_y) for k in range(2) if i or j or k
    ]

    def in_plane(step):
        i, j, k = step
        return here.to(x=turn(x, i, n_x), y=turn(y, j, n_y), c=lax.rem(c + k, 2))

    others = [in_plane(step) for step in plane]
    others += [here.to(z=turn(z, o, n_z)) for o in range(1, n_z)]
    for other in others:
        pl.semaphore_signal(barrier, inc=1, device_id=other, device_id_type=MESH)
    pl.semaphore_wait(barrier, len(others))

    def weight(kind, layer, shard, part=None):
        if kind == "patch":
            parts = cut(rows_patch, n_x, 16)
            rows = rows_patch // parts
            if part is None:
                return wp.at[pl.ds(aligned(shard * rows_patch, 16), rows_patch), :]
            return wp.at[pl.ds(aligned(shard * rows_patch + part * rows, 16), rows), :]
        if kind == "down":
            parts = cut(rows_down, n_x, 16)
            rows = rows_down // parts
            if part is None:
                return wdn.at[layer, pl.ds(aligned(shard * rows_down, 16), rows_down), :]
            return wdn.at[layer, pl.ds(aligned(shard * rows_down + part * rows, 16), rows), :]
        base = 0 if kind == "attn" else 4 * D
        rows = pl.ds(aligned(shard * rows_in, 16), rows_in)
        if part is None:
            return win.at[layer, rows, pl.ds(base, 4 * D)]
        wide = 4 * D // n_x
        return win.at[layer, rows, pl.ds(aligned(base + part * wide, 128), wide)]

    units = [("patch", 0)] + [
        (kind, layer) for layer in range(LAYERS) for kind in ("attn", "up", "down")
    ]

    def parts_of(kind):
        if kind == "patch":
            return cut(rows_patch, n_x, 16)
        if kind == "down":
            return cut(rows_down, n_x, 16)
        return n_x

    ag = ("ag", ag_send, ag_recv)
    base_x = n_y
    base_my = base_x + (n_y - 1) * (n_x - 1)
    base_mx = base_my + (n_y - 1)

    stage = 4 * rows_in

    def weights_copies(unit):
        kind, layer = units[unit]
        base = (unit % 2) * stage
        if kind == "patch":
            pairs = [(own_patch, X.at[pl.ds(base, rows_patch)])]
        elif kind == "down":
            pairs = [(own_down.at[layer], X.at[pl.ds(base, rows_down)])]
        else:
            start = 0 if kind == "attn" else 4 * D
            pairs = [
                (
                    own_in.at[layer, :, pl.ds(start + tile * D, D)],
                    X.at[pl.ds(base + tile * rows_in, rows_in)],
                )
                for tile in range(4)
            ]
        return [
            pltpu.make_async_copy(src, dst, ag_local.at[unit, index])
            for index, (src, dst) in enumerate(pairs)
        ]

    def weights_cast(unit):
        kind, layer = units[unit]
        base = (unit % 2) * stage
        for copy in weights_copies(unit):
            copy.wait()
        if kind == "patch":
            rows = pl.ds(aligned(here.shard * rows_patch, 16), rows_patch)
            wp[rows, :] = X[base : base + rows_patch, :].astype(BF)
        elif kind == "down":
            rows = pl.ds(aligned(here.shard * rows_down, 16), rows_down)
            wdn[layer, rows, :] = X[base : base + rows_down, :].astype(BF)
        else:
            start = 0 if kind == "attn" else 4 * D
            rows = pl.ds(aligned(here.shard * rows_in, 16), rows_in)
            for tile in range(4):
                win[layer, rows, start + tile * D : start + (tile + 1) * D] = X[
                    base + tile * rows_in : base + (tile + 1) * rows_in, :
                ].astype(BF)
        if unit + 2 < len(units):
            for copy in weights_copies(unit + 2):
                copy.start()

    def weights_start(unit):
        kind, layer = units[unit]
        part = x if parts_of(kind) > 1 else 0
        for o in range(1, n_y):
            go(
                lambda: weight(kind, layer, here.shard, part),
                weight(kind, layer, here.shard, part), ag, (unit, o),
                here.to(y=turn(y, o, n_y)),
            )
        go(
            lambda: weight(kind, layer, here.shard), weight(kind, layer, here.shard), ag,
            (unit, 0), mate,
        )

    def weights_forward(unit):
        kind, layer = units[unit]
        split = parts_of(kind) > 1
        part = x if split else 0
        for o in range(1, n_y):
            def make(o=o):
                return weight(kind, layer, turn(y, n_y - o, n_y) * 2 + c, part)

            arrived(make(), ag_recv.at[unit, o], ag_send.at[unit, o])
            if split:
                for p in range(1, n_x):
                    index = base_x + (o - 1) * (n_x - 1) + p - 1
                    go(make, make(), ag, (unit, index), here.to(x=turn(x, p, n_x)))
            go(make, make(), ag, (unit, base_my + o - 1), mate)

    def weights_pass(unit):
        kind, layer = units[unit]
        split = parts_of(kind) > 1
        part = x if split else 0
        if split:
            for o in range(1, n_y):
                for p in range(1, n_x):
                    index = (o - 1) * (n_x - 1) + p - 1

                    def make(o=o, p=p):
                        shard = turn(y, n_y - o, n_y) * 2 + c
                        return weight(kind, layer, shard, turn(x, n_x - p, n_x))

                    arrived(
                        make(), ag_recv.at[unit, base_x + index], ag_send.at[unit, base_x + index]
                    )
                    go(make, make(), ag, (unit, base_mx + index), mate)

    def weights_whole(unit):
        kind, layer = units[unit]
        split = parts_of(kind) > 1
        part = x if split else 0
        arrived(weight(kind, layer, y * 2 + 1 - c), ag_recv.at[unit, 0], ag_send.at[unit, 0])
        for o in range(1, n_y):
            shard = turn(y, n_y - o, n_y) * 2 + 1 - c
            index = base_my + o - 1
            arrived(weight(kind, layer, shard, part), ag_recv.at[unit, index], ag_send.at[unit, index])
            if split:
                for p in range(1, n_x):
                    index = base_mx + (o - 1) * (n_x - 1) + p - 1
                    piece = weight(kind, layer, shard, turn(x, n_x - p, n_x))
                    arrived(piece, ag_recv.at[unit, index], ag_send.at[unit, index])

    actions = {}

    def perform(names):
        for name in names:
            actions[name]()

    def at_place(place, *indices):
        for key, names in SCHEDULE.items():
            if key[0] != place:
                continue
            held = None
            for index, value in zip(indices, key[1:], strict=True):
                if not isinstance(index, int):
                    same = index == value
                    held = same if held is None else jnp.logical_and(held, same)
                elif index != value:
                    break
            else:
                if held is None:
                    perform(names)
                else:
                    pl.when(held)(functools.partial(perform, names))

    for unit in range(len(units)):
        actions[f"ws{unit}"] = functools.partial(weights_start, unit)
        actions[f"wf{unit}"] = functools.partial(weights_forward, unit)
        actions[f"wr{unit}"] = functools.partial(weights_pass, unit)
        actions[f"we{unit}"] = functools.partial(weights_whole, unit)

    lower = here.rep < n_rep // 2
    partner = here.to(z=turn(z, n_z // 2, n_z))
    back_parts = (
        pix.at[pl.ds(2, 2), pl.ds(0, TAIL)], pix.at[pl.ds(2, 2), pl.ds(TAIL, BLK - TAIL)]
    )
    given = (patches.at[pl.ds(KEPT, 2), pl.ds(0, TAIL)], patch_ends.at[pl.ds(KEPT, 2)])

    def local_half(half):
        pair = pl.ds(2 * half, 2)
        return (
            pltpu.make_async_copy(
                patches.at[pair, pl.ds(0, TAIL)], pix.at[pair, pl.ds(0, TAIL)],
                img_local.at[half],
            ),
            pltpu.make_async_copy(
                patch_ends.at[pair], pix.at[pair, pl.ds(TAIL, BLK - TAIL)],
                img_local.at[2 + half],
            ),
        )

    def marks(pair):
        row = lax.broadcasted_iota(jnp.int32, (32, 128), 0)
        found = jnp.full((32, 128), -1.0, F32)
        for index in range(2):
            slot = 2 * pair + index
            value = jnp.where(slot < counts[0], labels[slot], -1).astype(F32)
            found = jnp.where(row == CLS - TAIL + 16 * index, value, found)
        return found

    for copy in local_half(0):
        copy.start()
    for unit in range(2):
        for copy in weights_copies(unit):
            copy.start()
    lab[0] = marks(0)
    lab_given[...] = marks(2)

    @pl.when(jnp.logical_not(lower))
    def _():
        for index in range(2):
            push(
                given[index], back_parts[index], img_send.at[index], img_recv.at[index],
                partner,
            )
        push(lab_given, lab.at[1], img_send.at[2], img_recv.at[2], partner)
        for copy in local_half(1):
            copy.start()
        lab[1] = marks(1)

    for unit in range(len(units)):
        weights_cast(unit)
        at_place("cast", unit)

    even = lane_mask(128, 0, 64)
    odd = lane_mask(128, 64, 128)
    low_lane = lax.broadcasted_iota(jnp.int32, (1, 128), 1) < 64
    key_lane = lax.broadcasted_iota(jnp.int32, (1, BLK), 1)
    key_row = jnp.where((key_lane < PATCHES) | (key_lane == CLS), 0.0, -1e30)
    key_sub = lax.broadcasted_iota(jnp.int32, (BLK, 1), 0)
    key_column = jnp.where((key_sub < PATCHES) | (key_sub == CLS), 0.0, -1e30)
    whole_lanes = NCLS // 128 * 128
    low_head[:, 0:whole_lanes] = head[0:D, 0:whole_lanes].astype(BF)
    low_head[:, whole_lanes:] = jnp.zeros((D, CPAD - whole_lanes), BF)
    low_head[:, whole_lanes:NCLS] = head[0:D, whole_lanes:NCLS].astype(BF)
    head_bias[...] = jnp.zeros((1, CPAD), F32)
    head_bias[:, 0:NCLS] = head[D : D + 1, :]
    V[...] = jnp.zeros((VEC_ROWS, VEC_WIDE), F32)
    square_sum[...] = jnp.zeros((8, 128), F32)
    if small_block > block // 2:
        spare = small_block - block // 2
        GS[:, :, :, block // 2 :, :] = jnp.zeros((2, n_y, 2, spare, D), BF)
    zeros = jnp.zeros((8, D), F32)
    patch_bias = glob[0:1, :]

    def whole_lanes_of(tile):
        return jnp.concatenate([tile] * (D // 128), axis=1)

    def vector(layer, at, size):
        return vecs[pl.ds(layer, 1), at : at + size]

    def store_vector(layer, at, row):
        for piece in range(row.shape[-1] // D):
            V[pl.ds(VEC_AT + 12 * layer + at // D + piece, 1), 0:D] = row[
                :, piece * D : (piece + 1) * D
            ]

    def store_sums(layer, parts):
        for at, part in parts:
            store_vector(layer, at, down_sum(part))

    def embed(half):
        made = mm(pix[pl.ds(2 * half, 2)].reshape(HALF, PATCH_DIM), wp[...])
        for image in range(2):
            start = aligned(half * HALF + image * BLK, 16)
            for at, size in pieces(PATCHES - 4):
                X[pl.ds(start + at, size), :] = (
                    made[image * BLK + at : image * BLK + at + size]
                    + pos[1 + at : 1 + at + size, :]
                    + patch_bias
                )
            X[pl.ds(start + TAIL, 16), :] = jnp.zeros((16, D), F32)
            X[pl.ds(start + TAIL, 4), :] = (
                made[image * BLK + TAIL : image * BLK + PATCHES]
                + pos[1 + TAIL : 1 + PATCHES, :]
                + patch_bias
            )
            X[pl.ds(start + CLS, 1), :] = glob[1:2, :] + pos[0:1, :]

    def first_norm(layer, half, columns):
        base = half * HALF
        gain, shift = vector(layer, 0, D), vector(layer, D, D)
        for at, size in pieces(HALF):
            rows = pl.ds(aligned(base + at, 16), size)
            normed, inverse = norm(X[rows, :])
            N1[layer, rows, :] = normed.astype(BF)
            I1[layer, rows, :] = jnp.broadcast_to(inverse, (size, 128))
            DXB[rows, :] = (normed * gain + shift).astype(BF)
        rows = pl.ds(aligned(base, 16), HALF)
        h1 = DXB[rows, :]
        if len(columns) == 3:
            made = mm(h1, win[layer, :, 0 : 2 * D])
            QKV[layer, rows, 0:D] = (made[:, 0:D] + vector(layer, 2 * D, D)).astype(BF)
            QKV[layer, rows, D : 2 * D] = made[:, D:].astype(BF)
            made = mm(h1, win[layer, :, 2 * D : 3 * D])
            QKV[layer, rows, 2 * D :] = (made + vector(layer, 3 * D, D)).astype(BF)
        else:
            made = mm(h1, win[layer, :, D : 3 * D])
            DMB[rows, :] = made[:, 0:D].astype(BF)
            DA[rows, :] = (made[:, D:] + vector(layer, 3 * D, D)).astype(BF)

    ones = jnp.full((BLK, 128), 1.0, BF)

    def attend(layer, image):
        rows = pl.ds(aligned(image * BLK, 16), BLK)
        for pair in range(3):
            at = pair * 128
            query = QKV[layer, rows, at : at + 128] * BF(0.125)
            keys = QKV[layer, rows, D + at : D + at + 128]
            values = QKV[layer, rows, 2 * D + at : 2 * D + at + 128]
            both = jnp.concatenate([query * even, query * odd], axis=0)
            scores = mm_nt(both, keys)
            probs = []
            for row, size in pieces(HALF):
                part = scores[row : row + size] + key_row
                probs.append(jnp.exp(part - jnp.max(part, axis=-1, keepdims=True)).astype(BF))
            probs = jnp.concatenate(probs, axis=0)
            first = mm(probs[:BLK], jnp.concatenate([values * even, ones], axis=1))
            second = mm(probs[BLK:], jnp.concatenate([values * odd, ones], axis=1))
            made = first[:, :128] * (1.0 / first[:, 128:])
            made = made + second[:, :128] * (1.0 / second[:, 128:])
            ATT[layer, rows, at : at + 128] = made.astype(BF)

    def mlp(layer, half):
        base = half * HALF
        whole = pl.ds(aligned(base, 16), HALF)
        made = mm(ATT[layer, whole, :], win[layer, :, 3 * D : 4 * D])
        bias_out = vector(layer, 4 * D, D)
        gain, shift = vector(layer, 5 * D, D), vector(layer, 6 * D, D)
        for at, size in pieces(HALF):
            rows = pl.ds(aligned(base + at, 16), size)
            middle = X[rows, :] + made[at : at + size] + bias_out
            X[rows, :] = middle
            normed, inverse = norm(middle)
            N2[layer, rows, :] = normed.astype(BF)
            I2[layer, rows, :] = jnp.broadcast_to(inverse, (size, 128))
            DXB[rows, :] = (normed * gain + shift).astype(BF)
        at_place("mid", half, layer)
        at_place("b_up", half, layer)
        h2 = DXB[whole, :]
        for pair in range(2):
            made = mm(h2, win[layer, :, (4 + 2 * pair) * D : (6 + 2 * pair) * D])
            for tile in range(2):
                start = (2 * pair + tile) * D
                columns = slice(start, start + D)
                bias = vector(layer, 7 * D + start, D)
                for at, size in pieces(HALF):
                    rows = pl.ds(aligned(base + at, 16), size)
                    active, slope = gelu_parts(
                        made[at : at + size, tile * D : (tile + 1) * D] + bias
                    )
                    ACT[layer, rows, columns] = active.astype(BF)
                    SLOPE[layer, rows, columns] = slope.astype(BF)
        at_place("up", half, layer)
        at_place("b_down", half, layer)
        made = mm(ACT[layer, whole, :], wdn[layer])
        bias = vector(layer, 7 * D + FF, D)
        for at, size in pieces(HALF):
            rows = pl.ds(aligned(base + at, 16), size)
            X[rows, :] = X[rows, :] + made[at : at + size] + bias
        at_place("down", half, layer)

    at_place("b_start")

    def forward_half(half, carry):
        @pl.when(half == 0)
        def _():
            for copy in local_half(0):
                copy.wait()

        @pl.when(jnp.logical_and(half == 1, lower))
        def _():
            for index in range(2):
                arrived(back_parts[index], img_recv.at[index], img_send.at[index])

        @pl.when(jnp.logical_and(half == 1, jnp.logical_not(lower)))
        def _():
            for copy in local_half(1):
                copy.wait()

        embed(half)
        at_place("embed", half)

        def forward_layer(layer, inner):
            at_place("b_norm", half, layer)
            first_norm(layer, half, (0, 1, 2))
            at_place("norm", half, layer)

            def attend_one(index, nothing):
                attend(layer, 2 * half + index)
                at_place("att", half, layer, index)
                return nothing

            lax.fori_loop(0, 2, attend_one, 0)
            mlp(layer, half)
            return inner

        return lax.fori_loop(0, LAYERS - 1, forward_layer, carry)

    lax.fori_loop(0, 2, forward_half, 0)
    at_place("b_last")

    last = LAYERS - 1

    def last_norm(half, nothing):
        first_norm(last, half, (1, 2))
        at_place("ln", half)
        return nothing

    lax.fori_loop(0, 2, last_norm, 0)

    fac = ("f", f_send, f_recv)
    f_y, f_z = 1, n_y
    f_x = f_z + n_z - 1
    f_m = f_x + n_x - 1
    group = KEPT * n_shard

    def factors_core():
        go(lambda: FAC.at[1 - c], FC, fac, 0, mate)

    def factors_y():
        arrived(FC, f_recv.at[0], f_send.at[0])
        FAC[c] = FAC[c] + FC[...]
        for o in range(1, n_y):
            go(lambda: FAC.at[c], FY.at[o - 1], fac, f_y + o - 1, here.to(y=turn(y, o, n_y)))

    def line_factors(z_at, x_at):
        return all_factors.at[c, x_at, z_at]

    def factors_z():
        total = FAC[c]
        for o in range(1, n_y):
            arrived(FY.at[o - 1], f_recv.at[f_y + o - 1], f_send.at[f_y + o - 1])
            total = total + FY[o - 1]
        FC[...] = total
        pltpu.make_async_copy(FC, line_factors(z, x), out_local.at[0]).start()
        for o in range(1, n_z):
            go(
                lambda: FC, line_factors(z, x), fac, f_z + o - 1,
                here.to(z=turn(z, o, n_z)),
            )

    def factors_x():
        for o in range(1, n_z):
            index = f_z + o - 1
            arrived(line_factors(turn(z, n_z - o, n_z), x), f_recv.at[index], f_send.at[index])
        pltpu.make_async_copy(FC, line_factors(z, x), out_local.at[0]).wait()
        for o in range(1, n_x):
            go(
                lambda: all_factors.at[c, x], all_factors.at[c, x], fac, f_x + o - 1,
                here.to(x=turn(x, o, n_x)),
            )

    def factors_mate():
        for o in range(1, n_x):
            index = f_x + o - 1
            came = all_factors.at[c, turn(x, n_x - o, n_x)]
            arrived(came, f_recv.at[index], f_send.at[index])
        go(lambda: all_factors.at[c], all_factors.at[c], fac, f_m, mate)

    def factors_done():
        arrived(all_factors.at[1 - c], f_recv.at[f_m], f_send.at[f_m])

    rs = ("rs", rs_send, rs_recv)
    r_y, r_x = 1, n_y
    r_z = r_x + n_x - 1
    r_gz = r_z + n_z - 1
    r_gx = r_gz + n_z - 1

    def chunk(k):
        if k < CHUNKS:
            slot = k % 3
            return (
                G.at[k], RC.at[slot], RY.at[slot], RX.at[slot], RZ.at[slot], RES.at[k], block
            )
        k = k - CHUNKS
        return GS.at[k], SC.at[0], SY.at[0], SX.at[0], SZ.at[0], SRES.at[k], small_block

    def splits(rows):
        by_x = cut(rows, n_x, 16)
        by_z = cut(rows // by_x, n_z, 16)
        return by_x, rows // by_x, by_z, rows // by_x // by_z

    def step_of(rows, most=192):
        return max(step for step in range(16, most + 1, 16) if rows % step == 0)

    def add_rows(rows, target, target_at, sources):
        step = step_of(rows)

        def one(index, nothing):
            at = index * step
            to = pl.ds(aligned(target_at + at, 16), step)
            total = target[to, :]
            if len(sources) == 1:
                total = total + sources[0][pl.ds(aligned(at, 16), step), :]
            else:
                total = total.astype(F32)
                for source in sources:
                    total = total + source[pl.ds(aligned(at, 16), step), :].astype(F32)
                total = total.astype(BF)
            target[to, :] = total
            return nothing

        lax.fori_loop(0, rows // step, one, 0)

    def reduce_core(k):
        g, rc = chunk(k)[0:2]
        go(lambda: chunk(k)[0].at[:, 1 - c], rc, rs, (k, 0), mate)

    def reduce_y(k):
        g, rc, ry, _, _, _, rows = chunk(k)
        arrived(rc, rs_recv.at[k, 0], rs_send.at[k, 0])
        for o in list(range(1, n_y)) + [0]:
            at = turn(y, o, n_y)
            add_rows(rows, g.at[at, c], 0, [rc.at[at]])
            if o:
                go(
                    lambda o=o: chunk(k)[0].at[turn(y, o, n_y), c], ry.at[o - 1], rs,
                    (k, r_y + o - 1), here.to(y=at),
                )

    def total_of(slots, count, at, step):
        total = None
        for index in range(count):
            value = slots[index, pl.ds(aligned(at, 16), step), :].astype(F32)
            total = value if total is None else total + value
        return total

    def reduce_x(k):
        g, _, ry, rx, _, _, rows = chunk(k)
        by_x, rows_x = splits(rows)[0:2]
        for o in range(1, n_y):
            arrived(ry.at[o - 1], rs_recv.at[k, r_y + o - 1], rs_send.at[k, r_y + o - 1])
        mine = g.at[y, c]
        add_rows(rows, mine, 0, [ry.at[o - 1] for o in range(1, n_y)])
        for o in range(1, n_x):
            to = turn(x, o, n_x)
            if by_x > 1:

                def make(o=o):
                    at = turn(x, o, n_x) * rows_x
                    return chunk(k)[0].at[y, c, pl.ds(aligned(at, 16), rows_x), :]

                go(make, rx.at[o - 1], rs, (k, r_x + o - 1), here.to(x=to))
            else:
                go(lambda: chunk(k)[0].at[y, c], rx.at[x], rs, (k, r_x + o - 1), here.to(x=to))

    def reduce_z(k):
        g, _, _, rx, rz, _, rows = chunk(k)
        by_x, rows_x, by_z, rows_z = splits(rows)
        mine = g.at[y, c]
        for o in range(1, n_x):
            slot = rx.at[o - 1] if by_x > 1 else rx.at[turn(x, n_x - o, n_x)]
            arrived(slot, rs_recv.at[k, r_x + o - 1], rs_send.at[k, r_x + o - 1])
        if by_x > 1:
            start = x * rows_x
            add_rows(rows_x, mine, start, [rx.at[o - 1] for o in range(1, n_x)])
        else:
            start = 0
            rx[x] = mine[...]
            for o in range(1, n_x):
                gone(rs, (k, r_x + o - 1))
            step = step_of(rows)

            def one(index, nothing):
                at = pl.ds(aligned(index * step, 16), step)
                g[y, c, at, :] = total_of(rx, n_x, index * step, step).astype(BF)
                return nothing

            lax.fori_loop(0, rows // step, one, 0)
        for o in range(1, n_z):

            def make(o=o):
                at = x * rows_x if by_x > 1 else 0
                if by_z > 1:
                    at = at + turn(z, o, n_z) * rows_z
                return chunk(k)[0].at[y, c, pl.ds(aligned(at, 16), rows_z), :]

            slot = rz.at[o - 1] if by_z > 1 else rz.at[z]
            go(make, slot, rs, (k, r_z + o - 1), here.to(z=turn(z, o, n_z)))

    def gather_z(k):
        g, _, _, _, rz, res, rows = chunk(k)
        by_x, rows_x, by_z, rows_z = splits(rows)
        start = x * rows_x if by_x > 1 else 0
        if by_z > 1:
            start = start + z * rows_z
        for o in range(1, n_z):
            slot = rz.at[o - 1] if by_z > 1 else rz.at[turn(z, n_z - o, n_z)]
            arrived(slot, rs_recv.at[k, r_z + o - 1], rs_send.at[k, r_z + o - 1])
        own_slot = n_z - 1 if by_z > 1 else z
        rz[own_slot] = g[y, c, pl.ds(aligned(start, 16), rows_z), :]
        share = 1.0 / ((1 if by_x > 1 else n_x) * (1 if by_z > 1 else n_z))
        step = step_of(rows_z, 96)

        def one(index, total):
            low = total_of(rz, n_z, index * step, step).astype(BF)
            res[pl.ds(aligned(start + index * step, 16), step), :] = low
            wide = low.astype(F32)
            return total + fold(wide * wide)

        total = lax.fori_loop(0, rows_z // step, one, zeros) * share
        for at in range(0, D, 128):
            square_sum[...] = square_sum[...] + total[:, at : at + 128]
        if by_z > 1:

            def make():
                at = x * rows_x if by_x > 1 else 0
                return chunk(k)[5].at[pl.ds(aligned(at + z * rows_z, 16), rows_z), :]

            for o in range(1, n_z):
                go(make, make(), rs, (k, r_gz + o - 1), here.to(z=turn(z, o, n_z)))

    def gather_x(k):
        res, rows = chunk(k)[5:7]
        by_x, rows_x, by_z, rows_z = splits(rows)
        if by_z > 1:
            for o in range(1, n_z):
                start = turn(z, n_z - o, n_z) * rows_z
                if by_x > 1:
                    start = start + x * rows_x
                arrived(
                    res.at[pl.ds(aligned(start, 16), rows_z), :],
                    rs_recv.at[k, r_gz + o - 1], rs_send.at[k, r_gz + o - 1],
                )
        if by_x > 1:

            def make():
                return chunk(k)[5].at[pl.ds(aligned(x * rows_x, 16), rows_x), :]

            for o in range(1, n_x):
                go(make, make(), rs, (k, r_gx + o - 1), here.to(x=turn(x, o, n_x)))

    def result(k):
        if k < CHUNKS:
            return pltpu.make_async_copy(RES.at[k], res_out.at[k], out_local.at[1 + k])
        return pltpu.make_async_copy(
            SRES.at[k - CHUNKS], small_out.at[k - CHUNKS], out_local.at[1 + k]
        )

    def gather_done(k):
        res, rows = chunk(k)[5:7]
        by_x, rows_x = splits(rows)[0:2]
        if by_x > 1:
            for o in range(1, n_x):
                start = turn(x, n_x - o, n_x) * rows_x
                arrived(
                    res.at[pl.ds(aligned(start, 16), rows_x), :],
                    rs_recv.at[k, r_gx + o - 1], rs_send.at[k, r_gx + o - 1],
                )
        result(k).start()

    for k in range(CHUNKS + 2):
        actions[f"core{k}"] = functools.partial(reduce_core, k)
        actions[f"y{k}"] = functools.partial(reduce_y, k)
        actions[f"x{k}"] = functools.partial(reduce_x, k)
        actions[f"z{k}"] = functools.partial(reduce_z, k)
        actions[f"gz{k}"] = functools.partial(gather_z, k)
        actions[f"gx{k}"] = functools.partial(gather_x, k)
        actions[f"gd{k}"] = functools.partial(gather_done, k)
    actions.update(
        fc=factors_core, fy=factors_y, fz=factors_z, fx=factors_x, fm=factors_mate,
        fd=factors_done,
    )

    def tails(ref, layer=None):
        found = []
        for image in range(KEPT):
            rows = slice(image * BLK + TAIL, (image + 1) * BLK)
            found.append(ref[rows, :] if layer is None else ref[layer, rows, :])
        return jnp.concatenate(found, axis=0)

    @pl.when(lower)
    def _():
        arrived(lab.at[1], img_recv.at[2], img_send.at[2])

    marked = lab[...].reshape(CROWS, 128)[:, 0:1]

    h1 = tails(DXB)
    stream = tails(X)
    query = ((mm(h1, win[last, :, 0:D]) + vector(last, 2 * D, D)).astype(BF)) * BF(0.125)
    head_masks = [lane_mask(D, index * 64, (index + 1) * 64) for index in range(HEADS)]

    def spread(values):
        return jnp.concatenate([values * mask for mask in head_masks], axis=0)

    def gather_heads(values):
        total = None
        for index in range(HEADS):
            part = values[index * 16 : (index + 1) * 16] * head_masks[index].astype(F32)
            total = part if total is None else total + part
        return total

    spread_queries, probabilities, outs = [], [], []
    for image in range(KEPT):
        rows = slice(image * BLK, (image + 1) * BLK)
        queries = spread(query[image * 16 : (image + 1) * 16])
        scores = mm_nt(queries, DMB[rows, :]) + key_row
        raw = jnp.exp(scores - jnp.max(scores, axis=-1, keepdims=True))
        probs = raw * (1.0 / jnp.sum(raw, axis=-1, keepdims=True))
        spread_queries.append(queries)
        probabilities.append(probs)
        outs.append(gather_heads(mm(probs.astype(BF), DA[rows, :])))
    attended = jnp.concatenate(outs, axis=0).astype(BF)
    middle = stream + mm(attended, win[last, :, 3 * D : 4 * D]) + vector(last, 4 * D, D)
    n2, i2 = norm(middle)
    h2 = (n2 * vector(last, 5 * D, D) + vector(last, 6 * D, D)).astype(BF)
    active, slope = gelu_parts(mm(h2, win[last, :, 4 * D :]) + vector(last, 7 * D, FF))
    active = active.astype(BF)
    top = middle + mm(active, wdn[last]) + vector(last, 7 * D + FF, D)
    gain_final = glob[2:3, :]
    nf, inf = norm(top)
    final = (nf * gain_final + glob[3:4, :]).astype(BF)
    class_lane = lax.broadcasted_iota(jnp.int32, (1, CPAD), 1)
    logits = mm(final, low_head[...]) + head_bias[...]
    logits = jnp.where(class_lane < NCLS, logits, -1e30)
    peak = jnp.max(logits, axis=-1, keepdims=True)
    shifted = logits - peak
    raw = jnp.exp(shifted)
    total = jnp.sum(raw, axis=-1, keepdims=True)
    alive = jnp.where(marked >= 0.0, 1.0, 0.0)
    target = jnp.where(class_lane.astype(F32) == marked, 1.0 - SMOOTHING, 0.0) + jnp.where(
        class_lane < NCLS, SMOOTHING / NCLS, 0.0
    )
    log_probs = jnp.where(class_lane < NCLS, shifted - jnp.log(total), 0.0)
    losses = -jnp.sum(target * log_probs, axis=-1, keepdims=True) * alive
    d_logits = ((raw * (1.0 / total) - target) * alive).astype(BF)
    d_final = mm_nt(d_logits, low_head[...])
    last_row = VEC_AT + 12 * LAYERS
    V[last_row : last_row + 1, 0:D] = down_sum(d_final * nf)
    V[last_row + 1 : last_row + 2, 0:D] = down_sum(d_final)
    V[last_row + 2 : last_row + 3, 0:128] = jnp.broadcast_to(down_sum(losses), (1, 128))
    V[last_row + 3 : last_row + 4, 0:128] = jnp.full((1, 128), counts[0].astype(F32), F32)
    d_top = norm_back(d_final, nf, inf, gain_final)
    low_top = d_top.astype(BF)
    store_vector(last, 7 * D + FF, down_sum(d_top))
    d_up = (mm_nt(low_top, wdn[last]) * slope).astype(BF)
    store_vector(last, 7 * D, down_sum(d_up.astype(F32)))
    d_h2 = mm_nt(d_up, win[last, :, 4 * D :])
    store_vector(last, 5 * D, down_sum(d_h2 * n2))
    store_vector(last, 6 * D, down_sum(d_h2))
    d_middle = d_top + norm_back(d_h2, n2, i2, vector(last, 5 * D, D))
    low_middle = d_middle.astype(BF)
    store_vector(last, 4 * D, down_sum(d_middle))
    d_heads = mm_nt(low_middle, win[last, :, 3 * D : 4 * D]).astype(BF)
    d_queries = []
    for image in range(KEPT):
        rows = slice(image * BLK, (image + 1) * BLK)
        ups = spread(d_heads[image * 16 : (image + 1) * 16])
        probs = probabilities[image]
        d_probs = mm_nt(ups, DA[rows, :])
        inner = jnp.sum(d_probs * probs, axis=-1, keepdims=True)
        d_scores = (probs * (d_probs - inner)).astype(BF)
        d_queries.append(gather_heads(mm(d_scores, DMB[rows, :])) * 0.125)
        DMB[rows, :] = mm_tn(d_scores, spread_queries[image]).astype(BF)
        DA[rows, :] = mm_tn(probs.astype(BF), ups).astype(BF)
    d_query = jnp.concatenate(d_queries, axis=0).astype(BF)
    store_vector(last, 2 * D, down_sum(d_query.astype(F32)))
    from_query = mm_nt(d_query, win[last, :, 0:D])

    pick_row = lax.broadcasted_iota(jnp.int32, (group, CROWS), 0)
    pick_lane = lax.broadcasted_iota(jnp.int32, (group, CROWS), 1)
    pick = jnp.where(
        ((pick_row - KEPT * here.shard) * 16 + (CLS - TAIL)) == pick_lane, 1.0, 0.0
    ).astype(BF)
    at = 0
    for piece in (active, h2, attended, h1, final, low_top):
        FAC[0, :, at : at + piece.shape[-1]] = mm(pick, piece).astype(BF)
        at += piece.shape[-1]
    at = 0
    for piece in (d_up, low_middle, d_query, d_logits):
        FAC[1, :, at : at + piece.shape[-1]] = mm(pick, piece).astype(BF)
        at += piece.shape[-1]
    FAC[1, :, at:] = jnp.zeros((group, WFAC - at), BF)
    at_place("class")

    turned = DXB[...].T
    for tile, grads in enumerate((DMB, DA)):
        made = mm(turned, grads[...]).astype(BF)
        for shard in range(n_shard):
            GS[0, shard // 2, shard % 2, tile * rows_in : (tile + 1) * rows_in, :] = made[
                shard * rows_in : (shard + 1) * rows_in
            ]
    at_place("kv")
    store_sums(last, [(3 * D, fold(DA[...].astype(F32)))])

    X[...] = jnp.zeros((ROWS, D), F32)
    gain = vector(last, 0, D)
    gain_sum, shift_sum = zeros, zeros
    for image in range(KEPT):
        rows = slice(image * BLK + TAIL, (image + 1) * BLK)
        part = from_query[image * 16 : (image + 1) * 16]
        normed = N1[last, rows, :].astype(F32)
        gain_sum = gain_sum + fold(part * normed)
        shift_sum = shift_sum + fold(part)
        X[rows, :] = d_middle[image * 16 : (image + 1) * 16] + norm_back(
            part, normed, whole_lanes_of(I1[last, rows, :]), gain
        )

    def first_back(layer, half, made, sums):
        base = half * HALF
        gain = vector(layer, 0, D)
        gain_sum, shift_sum = sums
        for at, size in pieces(HALF):
            rows = pl.ds(aligned(base + at, 16), size)
            part = made[at : at + size]
            normed = N1[layer, rows, :].astype(F32)
            inverse = whole_lanes_of(I1[layer, rows, :])
            gain_sum = gain_sum + fold(part * normed)
            shift_sum = shift_sum + fold(part)
            X[rows, :] = X[rows, :] + norm_back(part, normed, inverse, gain)
        return gain_sum, shift_sum

    def last_back(half, sums):
        rows = pl.ds(aligned(half * HALF, 16), HALF)
        made = mm_nt(DMB[rows, :], win[last, :, D : 2 * D])
        made = made + mm_nt(DA[rows, :], win[last, :, 2 * D : 3 * D])
        sums = first_back(last, half, made, sums)
        at_place("lb", half)
        return sums

    gain_sum, shift_sum = lax.fori_loop(0, 2, last_back, (gain_sum, shift_sum))
    store_sums(last, [(0, gain_sum), (D, shift_sum)])

    def round_up(half, total):
        for at, size in pieces(HALF):
            rows = pl.ds(aligned(half * HALF + at, 16), size)
            up = X[rows, :]
            DXB[rows, :] = up.astype(BF)
            total = total + fold(up)
        return total

    def act_back(layer, half, totals):
        base = half * HALF
        low = DXB[pl.ds(aligned(base, 16), HALF), :]
        ups = []
        for pair in range(2):
            made = mm_nt(low, wdn[layer, 2 * pair * D : 2 * (pair + 1) * D, :])
            for tile in range(2):
                start = (2 * pair + tile) * D
                columns = slice(start, start + D)
                total = totals[2 * pair + tile]
                for at, size in pieces(HALF):
                    rows = pl.ds(aligned(base + at, 16), size)
                    part = made[at : at + size, tile * D : (tile + 1) * D]
                    grad = (part * SLOPE[layer, rows, columns].astype(F32)).astype(BF)
                    DH[rows, columns] = grad
                    total = total + fold(grad.astype(F32))
                ups.append(total)
        return tuple(ups)

    def mlp_back(layer, half, sums):
        base = half * HALF
        whole = pl.ds(aligned(base, 16), HALF)
        gain_sum, shift_sum, bias_out = sums
        made = mm_nt(DH[whole, :], win[layer, :, 4 * D :])
        gain = vector(layer, 5 * D, D)
        for at, size in pieces(HALF):
            rows = pl.ds(aligned(base + at, 16), size)
            part = made[at : at + size]
            normed = N2[layer, rows, :].astype(F32)
            inverse = whole_lanes_of(I2[layer, rows, :])
            gain_sum = gain_sum + fold(part * normed)
            shift_sum = shift_sum + fold(part)
            grad = X[rows, :] + norm_back(part, normed, inverse, gain)
            X[rows, :] = grad
            DMB[rows, :] = grad.astype(BF)
            bias_out = bias_out + fold(grad)
        DA[whole, :] = mm_nt(DMB[whole, :], win[layer, :, 3 * D : 4 * D]).astype(BF)
        return gain_sum, shift_sum, bias_out

    def attend_back(layer, image):
        rows = pl.ds(aligned(image * BLK, 16), BLK)
        for pair in range(3):
            at = pair * 128
            query = QKV[layer, rows, at : at + 128] * BF(0.125)
            keys = QKV[layer, rows, D + at : D + at + 128]
            values = QKV[layer, rows, 2 * D + at : 2 * D + at + 128]
            ups = DA[rows, at : at + 128]
            keys_both = jnp.concatenate([keys * even, keys * odd], axis=0)
            values_both = jnp.concatenate([values * even, values * odd], axis=0)
            scores = mm_nt(keys_both, query)
            d_probs = mm_nt(values_both, ups)
            probs, d_scores = [], []
            for base in (0, BLK):
                low_probs, low_grads = [], []
                for first, end in ((0, 128), (128, BLK)):
                    part = jnp.concatenate(
                        [
                            scores[base : base + TAIL, first:end],
                            scores[base + TAIL : base + BLK, first:end] + key_column[TAIL:],
                        ],
                        axis=0,
                    )
                    raw = jnp.exp(part - jnp.max(part, axis=0, keepdims=True))
                    prob = raw * (1.0 / jnp.sum(raw, axis=0, keepdims=True))
                    grad = d_probs[base : base + BLK, first:end]
                    inner = jnp.sum(grad * prob, axis=0, keepdims=True)
                    low_grads.append((prob * (grad - inner)).astype(BF))
                    low_probs.append(prob.astype(BF))
                probs.append(jnp.concatenate(low_probs, axis=1))
                d_scores.append(jnp.concatenate(low_grads, axis=1))
            probs = jnp.concatenate(probs, axis=0)
            d_scores = jnp.concatenate(d_scores, axis=0)
            d_values = mm(probs, ups)
            d_keys = mm(d_scores, query)
            d_query = mm_tn(d_scores, keys_both) * 0.125
            DH[rows, at : at + 128] = d_query.astype(BF)
            DH[rows, D + at : D + at + 128] = jnp.where(
                low_lane, d_keys[:BLK], d_keys[BLK:]
            ).astype(BF)
            DH[rows, 2 * D + at : 2 * D + at + 128] = jnp.where(
                low_lane, d_values[:BLK], d_values[BLK:]
            ).astype(BF)

    def renew(ref, layer, at):
        gain, shift = vector(layer, at, D), vector(layer, at + D, D)

        def one(index, nothing):
            for at, size in pieces(BLK):
                rows = pl.ds(aligned(index * BLK + at, 16), size)
                DXB[rows, :] = (ref[layer, rows, :].astype(F32) * gain + shift).astype(BF)
            return nothing

        lax.fori_loop(0, KEPT, one, 0)
        return DXB[...].T

    def keep_in(k, tile, made):
        for shard in range(n_shard):
            G[k, shard // 2, shard % 2, tile * rows_in : (tile + 1) * rows_in, :] = made[
                shard * rows_in : (shard + 1) * rows_in
            ]

    def backward(step, carry):
        layer = LAYERS - 2 - step
        kd, ku, kq = 3 * step, 3 * step + 1, 3 * step + 2
        bias_down = lax.fori_loop(0, 2, round_up, zeros)
        at_place("round", layer)
        turned = DXB[...].T
        per = min(rows_down, D)
        for pair in range(2):
            start = 2 * pair * D
            wide = mm(turned, ACT[layer, :, start : start + 2 * D]).astype(BF)
            for tile in range(2):
                made = wide[:, tile * D : (tile + 1) * D].T
                for piece in range(D // per):
                    shard, at = divmod(start + tile * D + piece * per, rows_down)
                    G[kd, shard // 2, shard % 2, at : at + per, :] = made[
                        piece * per : (piece + 1) * per
                    ]
        at_place("dn", layer)

        def one(half, totals):
            totals = act_back(layer, half, totals)
            at_place("act", layer, half)
            return totals

        bias_up = lax.fori_loop(0, 2, one, (zeros,) * 4)
        turned = renew(N2, layer, 5 * D)
        for pair in range(2):
            made = mm(turned, DH[:, 2 * pair * D : 2 * (pair + 1) * D]).astype(BF)
            keep_in(ku, 2 * pair, made[:, :D])
            keep_in(ku, 2 * pair + 1, made[:, D:])
        at_place("ups", layer)

        def one_more(half, sums):
            sums = mlp_back(layer, half, sums)
            at_place("mlpb", layer, half)
            return sums

        gain_sum, shift_sum, bias_out = lax.fori_loop(0, 2, one_more, (zeros, zeros, zeros))
        store_sums(
            layer,
            [(7 * D + FF, bias_down), (5 * D, gain_sum), (6 * D, shift_sum), (4 * D, bias_out)]
            + [(7 * D + tile * D, bias_up[tile]) for tile in range(4)],
        )
        keep_in(kq, 3, mm(ATT[layer].T, DMB[...]).astype(BF))
        at_place("out", layer)

        def two(image, nothing):
            attend_back(layer, image)
            at_place("attb", layer, image)
            return nothing

        lax.fori_loop(0, KEPT, two, 0)
        turned = renew(N1, layer, 0)
        made = mm(turned, DH[:, 0 : 2 * D]).astype(BF)
        keep_in(kq, 0, made[:, :D])
        keep_in(kq, 1, made[:, D:])
        keep_in(kq, 2, mm(turned, DH[:, 2 * D : 3 * D]).astype(BF))
        at_place("qkv", layer)
        store_sums(
            layer,
            [
                (2 * D, fold(DH[:, 0:D].astype(F32))),
                (3 * D, fold(DH[:, 2 * D : 3 * D].astype(F32))),
            ],
        )

        def three(half, sums):
            rows = pl.ds(aligned(half * HALF, 16), HALF)
            made = mm_nt(DH[rows, 0 : 3 * D], win[layer, :, 0 : 3 * D])
            sums = first_back(layer, half, made, sums)
            at_place("fb", layer, half)
            return sums

        gain_sum, shift_sum = lax.fori_loop(0, 2, three, (zeros, zeros))
        store_sums(layer, [(0, gain_sum), (D, shift_sum)])
        return carry

    lax.fori_loop(0, LAYERS - 1, backward, 0)

    for at, size in pieces(BLK):
        total = None
        for image in range(KEPT):
            part = X[image * BLK + at : image * BLK + at + size, :]
            DXB[image * BLK + at : image * BLK + at + size, :] = part.astype(BF)
            total = part if total is None else total + part
        V[at : at + size, 0:D] = total

    vec = ("v", v_send, v_recv)
    v_y, v_x = 1, n_y
    v_z = v_x + n_x - 1
    v_gz = v_z + n_z - 1
    v_gx = v_gz + n_z - 1
    v_gy = v_gx + n_x - 1
    v_gc = v_gy + n_y - 1
    rows_c = VEC_ROWS // 2
    rows_y = rows_c // n_y
    rows_x = rows_y // n_x
    split_z = cut(rows_x, n_z, 8)
    rows_z = rows_x // split_z
    at_c = c * rows_c
    at_y = at_c + y * rows_y
    at_x = at_y + x * rows_x
    at_z = at_x + z * rows_z if split_z > 1 else at_x

    def vrows(ref, at, rows):
        return ref.at[pl.ds(aligned(at, 8), rows), :]

    def vadd(at, rows, sources):
        target = pl.ds(aligned(at, 8), rows)
        total = V[target, :]
        for source in sources:
            total = total + source
        V[target, :] = total

    def vectors_core():
        go(lambda: vrows(V, (1 - c) * rows_c, rows_c), VC, vec, 0, mate)

    def vectors_y():
        arrived(VC, v_recv.at[0], v_send.at[0])
        vadd(at_c, rows_c, [VC[...]])
        for o in range(1, n_y):
            to = turn(y, o, n_y)
            go(
                lambda o=o: vrows(V, at_c + turn(y, o, n_y) * rows_y, rows_y), VY.at[o - 1],
                vec, v_y + o - 1, here.to(y=to),
            )

    def vectors_x():
        for o in range(1, n_y):
            arrived(VY.at[o - 1], v_recv.at[v_y + o - 1], v_send.at[v_y + o - 1])
        vadd(at_y, rows_y, [VY[o - 1] for o in range(1, n_y)])
        for o in range(1, n_x):
            to = turn(x, o, n_x)
            go(
                lambda o=o: vrows(V, at_y + turn(x, o, n_x) * rows_x, rows_x), VX.at[o - 1],
                vec, v_x + o - 1, here.to(x=to),
            )

    def vectors_z():
        for o in range(1, n_x):
            arrived(VX.at[o - 1], v_recv.at[v_x + o - 1], v_send.at[v_x + o - 1])
        vadd(at_x, rows_x, [VX[o - 1] for o in range(1, n_x)])
        for o in range(1, n_z):

            def make(o=o):
                at = at_x + turn(z, o, n_z) * rows_z if split_z > 1 else at_x
                return vrows(V, at, rows_z)

            go(make, VZ.at[z], vec, v_z + o - 1, here.to(z=turn(z, o, n_z)))

    def vectors_gather_z():
        for o in range(1, n_z):
            arrived(
                VZ.at[turn(z, n_z - o, n_z)], v_recv.at[v_z + o - 1], v_send.at[v_z + o - 1]
            )
        target = pl.ds(aligned(at_z, 8), rows_z)
        VZ[z] = V[target, :]
        total = VZ[0]
        for index in range(1, n_z):
            total = total + VZ[index]
        VF[target, :] = total
        if split_z > 1:
            for o in range(1, n_z):
                go(
                    lambda: vrows(VF, at_z, rows_z), vrows(VF, at_z, rows_z), vec, v_gz + o - 1,
                    here.to(z=turn(z, o, n_z)),
                )

    def vectors_gather_x():
        if split_z > 1:
            for o in range(1, n_z):
                came = turn(z, n_z - o, n_z)
                arrived(
                    vrows(VF, at_x + came * rows_z, rows_z), v_recv.at[v_gz + o - 1],
                    v_send.at[v_gz + o - 1],
                )
        for o in range(1, n_x):
            go(
                lambda: vrows(VF, at_x, rows_x), vrows(VF, at_x, rows_x), vec, v_gx + o - 1,
                here.to(x=turn(x, o, n_x)),
            )

    sq = ("q", q_send, q_recv)

    def squares_z():
        SQ[0] = square_sum[...]
        SQZ[z] = square_sum[...]
        for o in range(1, n_z):
            go(lambda: SQ.at[0], SQZ.at[z], sq, o - 1, here.to(z=turn(z, o, n_z)))

    def slot_of(i, j, k):
        return (i * n_y + j) * 2 + k

    def squares_plane():
        for o in range(1, n_z):
            arrived(SQZ.at[turn(z, n_z - o, n_z)], q_recv.at[o - 1], q_send.at[o - 1])
        total = SQZ[0]
        for index in range(1, n_z):
            total = total + SQZ[index]
        SQ[1] = total
        SQP[slot_of(x, y, c)] = total
        for index, step in enumerate(plane):
            go(
                lambda: SQ.at[1], SQP.at[slot_of(x, y, c)], sq, n_z - 1 + index,
                in_plane(step),
            )

    def squares_done():
        for index, (i, j, k) in enumerate(plane):
            slot = slot_of(
                turn(x, n_x - i, n_x), turn(y, n_y - j, n_y), lax.rem(c + k, 2)
            )
            arrived(SQP.at[slot], q_recv.at[n_z - 1 + index], q_send.at[n_z - 1 + index])
        total = SQP[0]
        for index in range(1, 2 * n_x * n_y):
            total = total + SQP[index]
        SQ[2] = total

    def vectors_gather_y():
        for o in range(1, n_x):
            at = at_y + turn(x, n_x - o, n_x) * rows_x
            arrived(vrows(VF, at, rows_x), v_recv.at[v_gx + o - 1], v_send.at[v_gx + o - 1])
        for o in range(1, n_y):
            go(
                lambda: vrows(VF, at_y, rows_y), vrows(VF, at_y, rows_y), vec, v_gy + o - 1,
                here.to(y=turn(y, o, n_y)),
            )

    def vectors_gather_core():
        for o in range(1, n_y):
            at = at_c + turn(y, n_y - o, n_y) * rows_y
            arrived(vrows(VF, at, rows_y), v_recv.at[v_gy + o - 1], v_send.at[v_gy + o - 1])
        go(lambda: vrows(VF, at_c, rows_c), vrows(VF, at_c, rows_c), vec, v_gc, mate)

    def vectors_done():
        arrived(vrows(VF, (1 - c) * rows_c, rows_c), v_recv.at[v_gc], v_send.at[v_gc])

    actions.update(
        vc=vectors_core, vy=vectors_y, vx=vectors_x, vz=vectors_z, vgz=vectors_gather_z,
        vgx=vectors_gather_x, vgy=vectors_gather_y, vgc=vectors_gather_core, vd=vectors_done,
        qz=squares_z, qp=squares_plane, qd=squares_done,
    )
    at_place("emb")
    low = DXB[...]
    for tile in range(2):
        made = mm_tn(pix[:, :, tile * D : (tile + 1) * D].reshape(ROWS, D), low).astype(BF)
        for piece in range(D // rows_patch):
            shard = tile * (D // rows_patch) + piece
            GS[1, shard // 2, shard % 2, 0:rows_patch, :] = made[piece * rows_patch : (piece + 1) * rows_patch]

    at_place("patch")
    ending = SCHEDULE["tail",]
    perform(ending[:-6])
    early = [
        key for key in sent
        if key[0] in ("ag", "f") or (key[0] == "rs" and key[1][0] not in (4, 5, 7))
    ]
    for key in early:
        source, send, recv, at = sent.pop(key)
        left_here(source(), recv.at[at], send.at[at])
    perform(ending[-6:])
    last_copies = [
        pltpu.make_async_copy(VF, vec_out, out_local.at[1 + CHUNKS + 2]),
        pltpu.make_async_copy(SQ.at[2], square_out, out_local.at[2 + CHUNKS + 2]),
    ]
    for copy in last_copies:
        copy.start()
    for source, send, recv, at in list(sent.values()):
        left_here(source(), recv.at[at], send.at[at])
    for k in range(CHUNKS + 2):
        result(k).wait()
    for copy in last_copies:
        copy.wait()

    @pl.when(jnp.logical_not(lower))
    def _():
        for index in range(2):
            left_here(given[index], img_recv.at[index], img_send.at[index])
        left_here(lab_given, img_recv.at[2], img_send.at[2])


def run_train(
    n_rep, n_shard, patches, patch_ends, labels, counts, own_patch, own_in, own_down, vecs, glob, pos, head
):
    n_x = 2 ** ((n_rep.bit_length() - 2) // 2)
    n_z, n_y = n_rep // n_x, n_shard // 2
    block = 4 * (D // n_shard)
    small_block = small_rows(block // 2, n_x, n_z)
    group = KEPT * n_shard
    keep = LAYERS - 1
    units = 1 + 3 * LAYERS
    chunks = CHUNKS + 2

    def buf(*shape, dtype=BF):
        return pltpu.VMEM(shape, dtype)

    def sems(*shape):
        return pltpu.SemaphoreType.DMA(shape)

    def reduction(count, slots, rows):
        by_x = cut(rows, n_x, 16)
        by_z = cut(rows // by_x, n_z, 16)
        return [
            buf(count, n_y, 2, rows, D),
            buf(slots, n_y, rows, D),
            buf(slots, n_y - 1, rows, D),
            buf(slots, n_x - 1 if by_x > 1 else n_x, rows // by_x, D),
            buf(slots, n_z, rows // by_x // by_z, D),
            buf(count, rows, D),
        ]

    rows_y = VEC_ROWS // 2 // n_y
    rows_x = rows_y // n_x
    rows_z = rows_x // cut(rows_x, n_z, 8)
    ag_count = n_y + (n_y - 1) * (n_x - 1) * 2 + n_y - 1
    rs_count = 1 + (n_y - 1) + 2 * (n_x - 1) + 2 * (n_z - 1)
    f_count = 1 + (n_y - 1) + (n_x - 1) + (n_z - 1) + 1
    v_count = 1 + 2 * (n_y - 1) + 2 * (n_x - 1) + 2 * (n_z - 1) + 1
    q_count = n_z - 1 + 2 * n_x * n_y - 1
    whole = pl.BlockSpec(memory_space=pltpu.VMEM)
    there = pl.BlockSpec(memory_space=pl.ANY)
    return pl.pallas_call(
        functools.partial(train, n_rep, n_shard),
        out_shape=[
            jax.ShapeDtypeStruct((CHUNKS, block, D), BF),
            jax.ShapeDtypeStruct((2, small_block, D), BF),
            jax.ShapeDtypeStruct((VEC_ROWS, VEC_WIDE), F32),
            jax.ShapeDtypeStruct((8, 128), F32),
            jax.ShapeDtypeStruct((2, n_x, n_z, group, WFAC), BF),
        ],
        in_specs=[there] * 2 + [pl.BlockSpec(memory_space=pltpu.SMEM)] * 2 + [there] * 3 + [whole] * 4,
        out_specs=[there] * 5,
        scratch_shapes=[
            buf(ROWS, D, dtype=F32),
            buf(LAYERS, ROWS, D),
            buf(LAYERS, ROWS, 128, dtype=F32),
            buf(keep, ROWS, 3 * D),
            buf(keep, ROWS, D),
            buf(keep, ROWS, D),
            buf(keep, ROWS, 128, dtype=F32),
            buf(keep, ROWS, FF),
            buf(keep, ROWS, FF),
            buf(ROWS, D),
            buf(ROWS, D),
            buf(ROWS, D),
            buf(ROWS, FF),
            buf(KEPT, BLK, PATCH_DIM),
            buf(2, 32, 128, dtype=F32),
            buf(32, 128, dtype=F32),
            buf(PATCH_DIM, D),
            buf(LAYERS, D, 4 * D + FF),
            buf(LAYERS, FF, D),
            buf(D, CPAD),
            buf(1, CPAD, dtype=F32),
            *reduction(CHUNKS, 3, block),
            *reduction(2, 1, small_block),
            buf(2, group, WFAC),
            buf(group, WFAC),
            buf(n_y - 1, group, WFAC),
            buf(VEC_ROWS, VEC_WIDE, dtype=F32),
            buf(VEC_ROWS // 2, VEC_WIDE, dtype=F32),
            buf(n_y - 1, rows_y, VEC_WIDE, dtype=F32),
            buf(n_x - 1, rows_x, VEC_WIDE, dtype=F32),
            buf(n_z, rows_z, VEC_WIDE, dtype=F32),
            buf(VEC_ROWS, VEC_WIDE, dtype=F32),
            buf(3, 8, 128, dtype=F32),
            buf(n_z, 8, 128, dtype=F32),
            buf(2 * n_x * n_y, 8, 128, dtype=F32),
            buf(8, 128, dtype=F32),
            sems(units, ag_count),
            sems(units, ag_count),
            sems(units, 4),
            sems(chunks, rs_count),
            sems(chunks, rs_count),
            sems(f_count),
            sems(f_count),
            sems(v_count),
            sems(v_count),
            sems(q_count),
            sems(q_count),
            sems(3),
            sems(3),
            sems(4),
            sems(3 + chunks),
        ],
        compiler_params=pltpu.CompilerParams(
            vmem_limit_bytes=65400 * 1024, collective_id=0, has_side_effects=True
        ),
        cost_estimate=pl.CostEstimate(
            flops=24_000_000_000, bytes_accessed=30_000_000, transcendentals=10_000_000
        ),
        name="train_step",
    )(patches, patch_ends, labels, counts, own_patch, own_in, own_down, vecs, glob, pos, head)


def adam(weight, first, second, grad, factor, rate):
    share = grad * factor
    first = BETA_FIRST * first + share
    square_scale = (1.0 - BETA_SECOND) / (1.0 - BETA_FIRST) ** 2
    second = BETA_SECOND * second + square_scale * (share * share)
    root_scale = (1.0 / (1.0 - BETA_SECOND**ADAM_STEP)) ** 0.5
    step_scale = rate / (1.0 - BETA_FIRST**ADAM_STEP) / root_scale
    bottom = second * lax.rsqrt(second) + ADAM_EPS / root_scale
    step = first * lax.rsqrt(bottom * bottom)
    return weight * (1.0 - rate * WEIGHT_DECAY) - step * step_scale, first, second


def update(n_rep, n_shard, *refs):
    res, small, vec, exchanged, factors = refs[0:5]
    sources = refs[5:26]
    loss_out, norm_out = refs[26:28]
    targets = refs[28:49]
    buffers = refs[49:70]
    results = refs[70:91]
    last_in, last_down, passing, grad_head, in_sems, out_sems = refs[91:]
    shard = lax.axis_index("shard")
    rows_in = D // n_shard
    rows_down = FF // n_shard
    keep = LAYERS - 1

    def moves(array, layer=None, out=False):
        found = []
        for kind in range(3):
            index = 3 * array + kind
            if out:
                src, dst, sem = results[index], targets[index], out_sems
            else:
                src, dst, sem = sources[index], buffers[index], in_sems
            slot = 0 if layer is None else layer
            if layer is not None:
                src, dst = src.at[layer], dst.at[layer]
            found.append(pltpu.make_async_copy(src, dst, sem.at[index, slot]))
        return found

    layered = [(1, layer) for layer in range(LAYERS)] + [(2, layer) for layer in range(LAYERS)]
    order = layered + [(0, None), (6, None), (5, None), (3, None), (4, None)]
    for array, layer in order:
        for move in moves(array, layer):
            move.start()

    n_rows = factors.shape[1] * factors.shape[2] * factors.shape[3]

    def factor(half, at, size):
        return factors[half, :, :, :, at : at + size].reshape(n_rows, size)

    def squares(values):
        return fold(values * values)

    total = jnp.zeros((8, D), F32)
    own_rows = pl.multiple_of(shard * rows_in, 8)

    def keep_in(column, made):
        slot = column % 2
        passing[slot] = made
        last_in[:, column * D : (column + 1) * D] = passing[slot, pl.ds(own_rows, rows_in), :]

    h2 = factor(0, FF, D)
    for tile in range(4):
        made = mm_tn(h2, factor(1, tile * D, D))
        keep_in(4 + tile, made)
        total = total + squares(made)
    for tile in range(2):
        last_in[:, (1 + tile) * D : (2 + tile) * D] = small[
            0, tile * rows_in : (tile + 1) * rows_in, :
        ].astype(F32)
    made = mm_tn(factor(0, FF + 2 * D, D), factor(1, FF + D, D))
    keep_in(0, made)
    total = total + squares(made)
    made = mm_tn(factor(0, FF + D, D), factor(1, FF, D))
    keep_in(3, made)
    total = total + squares(made)
    d_top = factor(0, FF + 4 * D, D)
    per = min(rows_down, D)
    for tile in range(4):
        made = mm_tn(factor(0, tile * D, D), d_top)
        total = total + squares(made)
        for piece in range(D // per):
            owner, at = divmod(tile * D + piece * per, rows_down)

            def keep_down(made=made, piece=piece, at=at):
                last_down[at : at + per, :] = made[piece * per : (piece + 1) * per]

            pl.when(shard == owner)(keep_down)
    final = factor(0, FF + 3 * D, D)
    wide = jnp.zeros((8, 128), F32)
    for at in range(0, CPAD, 512):
        d_logits = factor(1, FF + 2 * D + at, 512)
        made = mm_tn(final, d_logits)
        grad_head[0:D, at : at + 512] = made
        bias = down_sum(d_logits.astype(F32))
        grad_head[D : D + 1, at : at + 512] = bias
        sums = squares(made)
        for lane in range(0, 512, 128):
            wide = wide + sums[:, lane : lane + 128]
            row = bias[:, lane : lane + 128]
            wide = wide + (row * row) * 0.125
    for lane in range(0, D, 128):
        wide = wide + total[:, lane : lane + 128]
    used = VEC_AT + 12 * LAYERS + 2
    parts = jnp.zeros((8, D), F32)
    kept_rows = lax.broadcasted_iota(jnp.int32, (8, 1), 0)
    for at in range(0, used, 8):
        value = vec[at : at + 8, 0:D]
        if at + 8 > used:
            value = jnp.where(kept_rows + at < used, value, 0.0)
        parts = parts + value * value
    patch_bias = down_sum(vec[0:PATCHES, 0:D])
    class_row = vec[CLS : CLS + 1, 0:D]
    rest = (patch_bias * patch_bias + class_row * class_row) * 0.125
    parts = parts + rest
    for lane in range(0, D, 128):
        wide = wide + parts[:, lane : lane + 128]
    wide = wide + exchanged[...]
    sum_squares = jnp.sum(jnp.sum(wide, axis=1, keepdims=True), axis=0, keepdims=True)
    inv_count = 1.0 / vec[used + 1 : used + 2, 0:1]
    grad_norm = jnp.sqrt(sum_squares) * inv_count
    norm_out[...] = grad_norm
    loss_out[...] = vec[used : used + 1, 0:1] * inv_count
    scale = jnp.minimum(1.0, CLIP_NORM / grad_norm) * inv_count * (1.0 - BETA_FIRST)

    def apply(array, where, grad, rate):
        refs = [buffers[3 * array + kind] for kind in range(3)]
        made = adam(refs[0][where], refs[1][where], refs[2][where], grad, scale, rate)
        for kind, value in enumerate(made):
            results[3 * array + kind][where] = value

    def begin(array, layer=None):
        for move in moves(array, layer):
            move.wait()

    def finish(array, layer=None):
        for move in moves(array, layer, out=True):
            move.start()

    def loop(count, body):
        def one(index, nothing):
            body(index)
            return nothing

        lax.fori_loop(0, count, one, 0)

    step = 32 if rows_in % 32 == 0 else 16
    for layer in range(LAYERS):
        begin(1, layer)

        def column_of(column):
            lanes = pl.ds(pl.multiple_of(column * D, 128), D)
            for at in range(0, rows_in, step):
                if layer < keep:
                    k = 3 * (keep - 1 - layer) + jnp.where(column < 4, 2, 1)
                    row = pl.multiple_of(lax.rem(column, 4) * rows_in + at, 16)
                    grad = res[k, pl.ds(row, step), :].astype(F32)
                else:
                    grad = last_in[at : at + step, lanes]
                apply(1, (layer, slice(at, at + step), lanes), grad, LEARNING_RATE)

        loop(8, column_of)
        finish(1, layer)
    for layer in range(LAYERS):
        begin(2, layer)

        def rows_of(index):
            for part in range(3):
                at = pl.multiple_of(index * 96 + part * 32, 16)
                if layer < keep:
                    grad = res[3 * (keep - 1 - layer), pl.ds(at, 32), :].astype(F32)
                else:
                    grad = last_down[pl.ds(at, 32), :]
                apply(2, (layer, pl.ds(at, 32), slice(0, D)), grad, LEARNING_RATE)

        loop(rows_down // 96, rows_of)
        finish(2, layer)
    begin(0)

    def patch_rows(index):
        for part in range(3):
            at = pl.multiple_of(index * 96 + part * 32, 16)
            grad = small[1, pl.ds(at, 32), :].astype(F32)
            apply(0, (pl.ds(at, 32), slice(0, D)), grad, LEARNING_RATE)

    loop(PATCH_DIM // n_shard // 96, patch_rows)
    finish(0)
    begin(6)

    def head_rows(index):
        for part in range(3):
            rows = pl.ds(pl.multiple_of(index * 48 + part * 16, 16), 16)
            apply(6, (rows, slice(0, NCLS)), grad_head[rows, 0:NCLS], LEARNING_RATE)

    loop(D // 48, head_rows)
    apply(6, (slice(D, D + 1), slice(0, NCLS)), grad_head[D : D + 1, 0:NCLS], LEARNING_RATE)
    finish(6)
    begin(5)
    apply(5, (slice(0, 1), slice(0, D)), class_row, VECTOR_RATE)
    for at in range(0, PATCHES, 28):
        apply(
            5, (slice(1 + at, 29 + at), slice(0, D)), vec[at : at + 28, 0:D], VECTOR_RATE
        )
    finish(5)
    begin(3)
    for layer in range(LAYERS):
        for piece in range(12):
            row = VEC_AT + 12 * layer + piece
            where = (slice(layer, layer + 1), slice(piece * D, (piece + 1) * D))
            apply(3, where, vec[row : row + 1, 0:D], VECTOR_RATE)
    finish(3)
    begin(4)
    rows = [patch_bias, class_row, vec[used - 2 : used - 1, 0:D], vec[used - 1 : used, 0:D]]
    for index, row in enumerate(rows):
        apply(4, (slice(index, index + 1), slice(0, D)), row, VECTOR_RATE)
    finish(4)
    for array, layer in order:
        for move in moves(array, layer, out=True):
            move.wait()


def run_update(n_rep, n_shard, res, small, vec, squares, factors, arrays):
    whole = pl.BlockSpec(memory_space=pltpu.VMEM)
    there = pl.BlockSpec(memory_space=pl.ANY)
    one = jax.ShapeDtypeStruct((1, 1), F32)
    made = pl.pallas_call(
        functools.partial(update, n_rep, n_shard),
        out_shape=[one, one] + [jax.ShapeDtypeStruct(a.shape, F32) for a in arrays],
        in_specs=[whole] * 5 + [there] * 21,
        out_specs=[whole] * 2 + [there] * 21,
        scratch_shapes=[pltpu.VMEM(a.shape, F32) for a in (*arrays, *arrays)]
        + [
            pltpu.VMEM((D // n_shard, 4 * D + FF), F32),
            pltpu.VMEM((FF // n_shard, D), F32),
            pltpu.VMEM((2, D, D), F32),
            pltpu.VMEM((D + 8, CPAD), F32),
            pltpu.SemaphoreType.DMA((21, LAYERS)),
            pltpu.SemaphoreType.DMA((21, LAYERS)),
        ],
        compiler_params=pltpu.CompilerParams(vmem_limit_bytes=62 * 1024 * 1024),
        cost_estimate=pl.CostEstimate(
            flops=200_000_000, bytes_accessed=50_000_000, transcendentals=4_000_000
        ),
        name="adamw",
    )(res, small, vec, squares, factors, *arrays)
    return made[0].reshape(()), made[1].reshape(()), made[2:]


def shards(
    n_rep, n_shard,
    patches, labels, counts, patch_w, layer_in, layer_down, layer_vecs, glob_vecs, pos_embed, head,
    m_patch, v_patch, m_in, v_in, m_down, v_down, m_vecs, v_vecs, m_glob, v_glob, m_pos, v_pos,
    m_head, v_head,
):
    ends = jnp.pad(patches[:, TAIL:], ((0, 0), (0, BLK - PATCHES), (0, 0)))
    res, small, vec, squares, factors = run_train(
        n_rep, n_shard, patches, ends, labels, counts, patch_w, layer_in, layer_down, layer_vecs,
        glob_vecs, pos_embed, head,
    )
    arrays = [
        patch_w, m_patch, v_patch, layer_in, m_in, v_in, layer_down, m_down, v_down,
        layer_vecs, m_vecs, v_vecs, glob_vecs, m_glob, v_glob, pos_embed, m_pos, v_pos,
        head, m_head, v_head,
    ]
    loss, grad_norm, new = run_update(n_rep, n_shard, res, small, vec, squares, factors, arrays)
    return (loss, grad_norm, *new)


def solution(mesh):
    everywhere = P()
    rows = P("shard", None)
    middle = P(None, "shard", None)
    return jax.shard_map(
        functools.partial(shards, mesh.shape["rep"], mesh.shape["shard"]),
        mesh=mesh,
        in_specs=(
            P(("rep", "shard"), None, None),
            P(("rep", "shard")),
            P(("rep", "shard")),
            rows,
            middle,
            middle,
            *(everywhere,) * 4,
            *(rows,) * 2,
            *(middle,) * 4,
            *(everywhere,) * 8,
        ),
        out_specs=(
            *(everywhere,) * 2,
            *(rows,) * 3,
            *(middle,) * 6,
            *(everywhere,) * 12,
        ),
        check_vma=False,
    )
```

```python
import functools

import jax
import jax.numpy as jnp
from jax import lax
from jax.experimental import pallas as pl
from jax.experimental.pallas import tpu as pltpu
from jax.sharding import PartitionSpec as P

D = 384
HEADS = 6
HEAD_DIM = 64
FF = 1536
PATCH_DIM = 768
PATCHES = 196
NCLS = 1000
LAYERS = 3
SEQ = 197

BLK = 208
CLS = 200
TAIL = 192
KEPT = 4
ROWS = KEPT * BLK
HALF = 2 * BLK
CROWS = KEPT * 16
CPAD = 1024
WIDE = 8 * D + FF

NORM_EPS = 1e-06
SMOOTHING = 0.1
CLIP_NORM = 0.05
LEARNING_RATE = 0.05
VECTOR_RATE = 0.5
BETA_FIRST = 0.9
BETA_SECOND = 0.999
ADAM_EPS = 1e-08
WEIGHT_DECAY = 0.05
ADAM_STEP = 10
GELU_SCALE = 0.7978845608028654
GELU_CUBIC = 0.044715

F32 = jnp.float32
BF = jnp.bfloat16


def mm(left, right):
    return jnp.dot(left, right, preferred_element_type=F32)


def mm_nt(left, right):
    return lax.dot_general(left, right, (((1,), (1,)), ((), ())), preferred_element_type=F32)


def mm_tn(left, right):
    return lax.dot_general(left, right, (((0,), (0,)), ((), ())), preferred_element_type=F32)


def fold(values):
    return jnp.sum(values.reshape(-1, 8, values.shape[-1]), axis=0)


def down_sum(values):
    return jnp.sum(values, axis=0, keepdims=True)


def norm(values):
    centre = values - jnp.mean(values, axis=-1, keepdims=True)
    inverse = lax.rsqrt(jnp.mean(centre * centre, axis=-1, keepdims=True) + NORM_EPS)
    return centre * inverse, inverse


def norm_back(upstream, normed, inverse, gain):
    scaled = upstream * gain
    first = jnp.mean(scaled, axis=-1, keepdims=True)
    second = jnp.mean(scaled * normed, axis=-1, keepdims=True)
    return inverse * (scaled - first - normed * second)


def gelu_parts(hidden):
    bent = hidden * (GELU_SCALE + (GELU_SCALE * GELU_CUBIC) * (hidden * hidden))
    tangent = jnp.tanh(bent)
    share = 0.5 + 0.5 * tangent
    slope = share + (1.0 - tangent * tangent) * (1.5 * bent - GELU_SCALE * hidden)
    return hidden * share, slope


def lane_mask(width, low, high):
    lane = lax.broadcasted_iota(jnp.int32, (1, width), 1)
    return jnp.where((lane >= low) & (lane < high), 1.0, 0.0).astype(BF)


STEP = 16


def pieces(total):
    return [(at, min(STEP, total - at)) for at in range(0, total, STEP)]


SCHEDULE = {
    ("cast", 0): ("ws0",),
    ("cast", 1): ("ws1",),
    ("cast", 2): ("ws2",),
    ("b_start",): ("wf0", "ws3", "wr0", "wf1", "ws4", "we0",),
    ("b_norm", 0, 0): ("wf2", "ws5", "wr1", "we1",),
    ("norm", 0, 0): ("wr2", "wf3", "ws6",),
    ("mid", 0, 0): ("wf4", "ws7",),
    ("b_up", 0, 0): ("we2",),
    ("up", 0, 0): ("wr3",),
    ("b_down", 0, 0): ("wf5", "ws8", "we3",),
    ("b_norm", 0, 1): ("wr4", "wf6", "ws9", "we4",),
    ("att", 0, 1, 0): ("wr5", "wf7",),
    ("b_up", 0, 1): ("we5",),
    ("up", 0, 1): ("wr6", "wf8",),
    ("b_down", 0, 1): ("we6",),
    ("down", 0, 1): ("wr7",),
    ("embed", 1): ("wf9",),
    ("att", 1, 0, 0): ("wr8",),
    ("up", 1, 0): ("wr9",),
    ("b_last",): ("we7", "we8", "we9",),
    ("class",): ("fc",),
    ("kv",): ("core6",),
    ("lb", 0): ("fy",),
    ("dn", 1): ("y6", "fz", "core0",),
    ("ups", 1): ("y0", "core1",),
    ("mlpb", 1, 1): ("x6",),
    ("out", 1): ("fx",),
    ("attb", 1, 0): ("y1",),
    ("attb", 1, 2): ("z6",),
    ("qkv", 1): ("x0", "core2",),
    ("fb", 1, 0): ("gz6",),
    ("dn", 0): ("y2", "core3",),
    ("act", 0, 0): ("gx6",),
    ("act", 0, 1): ("z0",),
    ("ups", 0): ("x1",),
    ("mlpb", 0, 0): ("gd6",),
    ("attb", 0, 0): ("gz0",),
    ("attb", 0, 1): ("z1",),
    ("attb", 0, 2): ("x2", "y3", "core4",),
    ("qkv", 0): ("gx0",),
    ("emb",): ("z2", "vc",),
    ("patch",): ("gz1", "core7",),
    ("tail",): ("vy", "gd0", "x3", "y4", "core5", "y7", "gz2", "vx", "z3", "gx1", "vz", "gx2", "x4", "y5", "gd1", "fv", "gz3", "vgz", "gd2", "x7", "z4", "gx3", "vgx", "z7", "x5", "gz4", "gd3", "vgy", "gz7", "z5", "gx4", "gx7", "gd4", "fm", "gz5", "qz", "gd7", "vgc", "fd", "vd", "gx5", "qp", "gd5", "qd",),
}


WFAC = FF + 5 * D + 128
VEC_ROWS = 256
VEC_AT = BLK
VEC_WIDE = D
MESH = pl.DeviceIdType.MESH
CHUNKS = 6


class Place:
    def __init__(self, n_rep, n_shard):
        self.n_rep, self.n_shard = n_rep, n_shard
        self.n_x = 2 ** ((n_rep.bit_length() - 2) // 2)
        self.n_z = n_rep // self.n_x
        self.n_y = n_shard // 2
        rep, shard = lax.axis_index("rep"), lax.axis_index("shard")
        self.rep, self.shard = rep, shard
        self.z, self.x = rep // self.n_x, rep % self.n_x
        self.y, self.c = shard // 2, shard % 2

    def to(self, x=None, y=None, z=None, c=None):
        x = self.x if x is None else x
        y = self.y if y is None else y
        z = self.z if z is None else z
        c = self.c if c is None else c
        return {"rep": z * self.n_x + x, "shard": y * 2 + c}


def cut(rows, parts, unit):
    return parts if rows % (parts * unit) == 0 else 1


def small_rows(rows, n_x, n_z):
    unit = 16 * n_x * n_z
    padded = -(-rows // unit) * unit
    return padded if 2 * padded <= 3 * rows else rows


def aligned(value, unit):
    return pl.multiple_of(value, unit)


def train(
    n_rep, n_shard,
    patches, patch_ends, labels, counts, own_patch, own_in, own_down, vecs, glob, pos, head,
    res_out, small_out, vec_out, square_out, all_factors,
    X, N1, I1, QKV, ATT, N2, I2, ACT, SLOPE, DXB, DMB, DA, DH,
    pix, lab, lab_given, wp, win, wdn, low_head, head_bias,
    G, RC, RY, RX, RZ, RES, GS, SC, SY, SX, SZ, SRES,
    FAC, FC, FY, V, VC, VY, VX, VZ, VF, SQ, SQZ, SQP, square_sum,
    ag_send, ag_recv, ag_local, rs_send, rs_recv, f_send, f_recv, v_send, v_recv,
    q_send, q_recv,
    img_send, img_recv, img_local, out_local,
):
    here = Place(n_rep, n_shard)
    n_x, n_y, n_z = here.n_x, here.n_y, here.n_z
    x, y, z, c = here.x, here.y, here.z, here.c
    rows_in, rows_down, rows_patch = D // n_shard, FF // n_shard, PATCH_DIM // n_shard
    block = 4 * rows_in
    small_block = small_rows(block // 2, n_x, n_z)
    mate = here.to(c=1 - c)

    def push(src, dst, send, recv, device):
        pltpu.make_async_remote_copy(
            src_ref=src, dst_ref=dst, send_sem=send, recv_sem=recv,
            device_id=device, device_id_type=MESH,
        ).start()

    def arrived(dst, recv, send):
        pltpu.make_async_remote_copy(
            src_ref=dst, dst_ref=dst, send_sem=send, recv_sem=recv,
            device_id=mate, device_id_type=MESH,
        ).wait_recv()

    def left_here(src, recv, send):
        pltpu.make_async_remote_copy(
            src_ref=src, dst_ref=src, send_sem=send, recv_sem=recv,
            device_id=mate, device_id_type=MESH,
        ).wait_send()

    sent = {}

    def go(source, dst, sems, index, device):
        name, send, recv = sems
        push(source(), dst, send.at[index], recv.at[index], device)
        sent[name, index] = (source, send, recv, index)

    def gone(sems, index):
        source, send, recv, at = sent.pop((sems[0], index))
        left_here(source(), recv.at[at], send.at[at])

    def turn(at, by, size):
        return lax.rem(at + by, size)

    barrier = pltpu.get_barrier_semaphore()
    plane = [
        (i, j, k) for i in range(n_x) for j in range(n_y) for k in range(2) if i or j or k
    ]

    def in_plane(step):
        i, j, k = step
        return here.to(x=turn(x, i, n_x), y=turn(y, j, n_y), c=lax.rem(c + k, 2))

    others = [in_plane(step) for step in plane]
    others += [here.to(z=turn(z, o, n_z)) for o in range(1, n_z)]
    for other in others:
        pl.semaphore_signal(barrier, inc=1, device_id=other, device_id_type=MESH)
    pl.semaphore_wait(barrier, len(others))

    def weight(kind, layer, shard, part=None):
        if kind == "patch":
            parts = cut(rows_patch, n_x, 16)
            rows = rows_patch // parts
            if part is None:
                return wp.at[pl.ds(aligned(shard * rows_patch, 16), rows_patch), :]
            return wp.at[pl.ds(aligned(shard * rows_patch + part * rows, 16), rows), :]
        if kind == "down":
            parts = cut(rows_down, n_x, 16)
            rows = rows_down // parts
            if part is None:
                return wdn.at[layer, pl.ds(aligned(shard * rows_down, 16), rows_down), :]
            return wdn.at[layer, pl.ds(aligned(shard * rows_down + part * rows, 16), rows), :]
        base = 0 if kind == "attn" else 4 * D
        rows = pl.ds(aligned(shard * rows_in, 16), rows_in)
        if part is None:
            return win.at[layer, rows, pl.ds(base, 4 * D)]
        wide = 4 * D // n_x
        return win.at[layer, rows, pl.ds(aligned(base + part * wide, 128), wide)]

    units = [("patch", 0)] + [
        (kind, layer) for layer in range(LAYERS) for kind in ("attn", "up", "down")
    ]

    def parts_of(kind):
        if kind == "patch":
            return cut(rows_patch, n_x, 16)
        if kind == "down":
            return cut(rows_down, n_x, 16)
        return n_x

    ag = ("ag", ag_send, ag_recv)
    base_x = n_y
    base_my = base_x + (n_y - 1) * (n_x - 1)
    base_mx = base_my + (n_y - 1)

    stage = 4 * rows_in

    def weights_copies(unit):
        kind, layer = units[unit]
        base = (unit % 2) * stage
        if kind == "patch":
            pairs = [(own_patch, X.at[pl.ds(base, rows_patch)])]
        elif kind == "down":
            pairs = [(own_down.at[layer], X.at[pl.ds(base, rows_down)])]
        else:
            start = 0 if kind == "attn" else 4 * D
            pairs = [
                (
                    own_in.at[layer, :, pl.ds(start + tile * D, D)],
                    X.at[pl.ds(base + tile * rows_in, rows_in)],
                )
                for tile in range(4)
            ]
        return [
            pltpu.make_async_copy(src, dst, ag_local.at[unit, index])
            for index, (src, dst) in enumerate(pairs)
        ]

    def weights_cast(unit):
        kind, layer = units[unit]
        base = (unit % 2) * stage
        for copy in weights_copies(unit):
            copy.wait()
        if kind == "patch":
            rows = pl.ds(aligned(here.shard * rows_patch, 16), rows_patch)
            wp[rows, :] = X[base : base + rows_patch, :].astype(BF)
        elif kind == "down":
            rows = pl.ds(aligned(here.shard * rows_down, 16), rows_down)
            wdn[layer, rows, :] = X[base : base + rows_down, :].astype(BF)
        else:
            start = 0 if kind == "attn" else 4 * D
            rows = pl.ds(aligned(here.shard * rows_in, 16), rows_in)
            for tile in range(4):
                win[layer, rows, start + tile * D : start + (tile + 1) * D] = X[
                    base + tile * rows_in : base + (tile + 1) * rows_in, :
                ].astype(BF)
        if unit + 2 < len(units):
            for copy in weights_copies(unit + 2):
                copy.start()

    def weights_start(unit):
        kind, layer = units[unit]
        part = x if parts_of(kind) > 1 else 0
        for o in range(1, n_y):
            go(
                lambda: weight(kind, layer, here.shard, part),
                weight(kind, layer, here.shard, part), ag, (unit, o),
                here.to(y=turn(y, o, n_y)),
            )
        go(
            lambda: weight(kind, layer, here.shard), weight(kind, layer, here.shard), ag,
            (unit, 0), mate,
        )

    def weights_forward(unit):
        kind, layer = units[unit]
        split = parts_of(kind) > 1
        part = x if split else 0
        for o in range(1, n_y):
            def make(o=o):
                return weight(kind, layer, turn(y, n_y - o, n_y) * 2 + c, part)

            arrived(make(), ag_recv.at[unit, o], ag_send.at[unit, o])
            if split:
                for p in range(1, n_x):
                    index = base_x + (o - 1) * (n_x - 1) + p - 1
                    go(make, make(), ag, (unit, index), here.to(x=turn(x, p, n_x)))
            go(make, make(), ag, (unit, base_my + o - 1), mate)

    def weights_pass(unit):
        kind, layer = units[unit]
        split = parts_of(kind) > 1
        part = x if split else 0
        if split:
            for o in range(1, n_y):
                for p in range(1, n_x):
                    index = (o - 1) * (n_x - 1) + p - 1

                    def make(o=o, p=p):
                        shard = turn(y, n_y - o, n_y) * 2 + c
                        return weight(kind, layer, shard, turn(x, n_x - p, n_x))

                    arrived(
                        make(), ag_recv.at[unit, base_x + index], ag_send.at[unit, base_x + index]
                    )
                    go(make, make(), ag, (unit, base_mx + index), mate)

    def weights_whole(unit):
        kind, layer = units[unit]
        split = parts_of(kind) > 1
        part = x if split else 0
        arrived(weight(kind, layer, y * 2 + 1 - c), ag_recv.at[unit, 0], ag_send.at[unit, 0])
        for o in range(1, n_y):
            shard = turn(y, n_y - o, n_y) * 2 + 1 - c
            index = base_my + o - 1
            arrived(weight(kind, layer, shard, part), ag_recv.at[unit, index], ag_send.at[unit, index])
            if split:
                for p in range(1, n_x):
                    index = base_mx + (o - 1) * (n_x - 1) + p - 1
                    piece = weight(kind, layer, shard, turn(x, n_x - p, n_x))
                    arrived(piece, ag_recv.at[unit, index], ag_send.at[unit, index])

    actions = {}

    def perform(names):
        for name in names:
            actions[name]()

    def at_place(place, *indices):
        for key, names in SCHEDULE.items():
            if key[0] != place:
                continue
            held = None
            for index, value in zip(indices, key[1:], strict=True):
                if not isinstance(index, int):
                    same = index == value
                    held = same if held is None else jnp.logical_and(held, same)
                elif index != value:
                    break
            else:
                if held is None:
                    perform(names)
                else:
                    pl.when(held)(functools.partial(perform, names))

    for unit in range(len(units)):
        actions[f"ws{unit}"] = functools.partial(weights_start, unit)
        actions[f"wf{unit}"] = functools.partial(weights_forward, unit)
        actions[f"wr{unit}"] = functools.partial(weights_pass, unit)
        actions[f"we{unit}"] = functools.partial(weights_whole, unit)

    lower = here.rep < n_rep // 2
    partner = here.to(z=turn(z, n_z // 2, n_z))
    back_parts = (
        pix.at[pl.ds(2, 2), pl.ds(0, TAIL)], pix.at[pl.ds(2, 2), pl.ds(TAIL, BLK - TAIL)]
    )
    given = (patches.at[pl.ds(KEPT, 2), pl.ds(0, TAIL)], patch_ends.at[pl.ds(KEPT, 2)])

    def local_half(half):
        pair = pl.ds(2 * half, 2)
        return (
            pltpu.make_async_copy(
                patches.at[pair, pl.ds(0, TAIL)], pix.at[pair, pl.ds(0, TAIL)],
                img_local.at[half],
            ),
            pltpu.make_async_copy(
                patch_ends.at[pair], pix.at[pair, pl.ds(TAIL, BLK - TAIL)],
                img_local.at[2 + half],
            ),
        )

    def marks(pair):
        row = lax.broadcasted_iota(jnp.int32, (32, 128), 0)
        found = jnp.full((32, 128), -1.0, F32)
        for index in range(2):
            slot = 2 * pair + index
            value = jnp.where(slot < counts[0], labels[slot], -1).astype(F32)
            found = jnp.where(row == CLS - TAIL + 16 * index, value, found)
        return found

    for copy in local_half(0):
        copy.start()
    for unit in range(2):
        for copy in weights_copies(unit):
            copy.start()
    lab[0] = marks(0)
    lab_given[...] = marks(2)

    @pl.when(jnp.logical_not(lower))
    def _():
        for index in range(2):
            push(
                given[index], back_parts[index], img_send.at[index], img_recv.at[index],
                partner,
            )
        push(lab_given, lab.at[1], img_send.at[2], img_recv.at[2], partner)
        for copy in local_half(1):
            copy.start()
        lab[1] = marks(1)

    for unit in range(len(units)):
        weights_cast(unit)
        at_place("cast", unit)

    even = lane_mask(128, 0, 64)
    odd = lane_mask(128, 64, 128)
    low_lane = lax.broadcasted_iota(jnp.int32, (1, 128), 1) < 64
    key_lane = lax.broadcasted_iota(jnp.int32, (1, BLK), 1)
    key_row = jnp.where((key_lane < PATCHES) | (key_lane == CLS), 0.0, -1e30)
    key_sub = lax.broadcasted_iota(jnp.int32, (BLK, 1), 0)
    key_column = jnp.where((key_sub < PATCHES) | (key_sub == CLS), 0.0, -1e30)
    whole_lanes = NCLS // 128 * 128
    low_head[:, 0:whole_lanes] = head[0:D, 0:whole_lanes].astype(BF)
    low_head[:, whole_lanes:] = jnp.zeros((D, CPAD - whole_lanes), BF)
    low_head[:, whole_lanes:NCLS] = head[0:D, whole_lanes:NCLS].astype(BF)
    head_bias[...] = jnp.zeros((1, CPAD), F32)
    head_bias[:, 0:NCLS] = head[D : D + 1, :]
    V[...] = jnp.zeros((VEC_ROWS, VEC_WIDE), F32)
    square_sum[...] = jnp.zeros((8, 128), F32)
    if small_block > block // 2:
        spare = small_block - block // 2
        GS[:, :, :, block // 2 :, :] = jnp.zeros((2, n_y, 2, spare, D), BF)
    zeros = jnp.zeros((8, D), F32)
    patch_bias = glob[0:1, :]

    def whole_lanes_of(tile):
        return jnp.concatenate([tile] * (D // 128), axis=1)

    def vector(layer, at, size):
        return vecs[pl.ds(layer, 1), at : at + size]

    def store_vector(layer, at, row):
        for piece in range(row.shape[-1] // D):
            V[pl.ds(VEC_AT + 12 * layer + at // D + piece, 1), 0:D] = row[
                :, piece * D : (piece + 1) * D
            ]

    def store_sums(layer, parts):
        for at, part in parts:
            store_vector(layer, at, down_sum(part))

    def embed(half):
        made = mm(pix[pl.ds(2 * half, 2)].reshape(HALF, PATCH_DIM), wp[...])
        for image in range(2):
            start = aligned(half * HALF + image * BLK, 16)
            for at, size in pieces(PATCHES - 4):
                X[pl.ds(start + at, size), :] = (
                    made[image * BLK + at : image * BLK + at + size]
                    + pos[1 + at : 1 + at + size, :]
                    + patch_bias
                )
            X[pl.ds(start + TAIL, 16), :] = jnp.zeros((16, D), F32)
            X[pl.ds(start + TAIL, 4), :] = (
                made[image * BLK + TAIL : image * BLK + PATCHES]
                + pos[1 + TAIL : 1 + PATCHES, :]
                + patch_bias
            )
            X[pl.ds(start + CLS, 1), :] = glob[1:2, :] + pos[0:1, :]

    def first_norm(layer, half, columns):
        base = half * HALF
        gain, shift = vector(layer, 0, D), vector(layer, D, D)
        for at, size in pieces(HALF):
            rows = pl.ds(aligned(base + at, 16), size)
            normed, inverse = norm(X[rows, :])
            N1[layer, rows, :] = normed.astype(BF)
            I1[layer, rows, :] = jnp.broadcast_to(inverse, (size, 128))
            DXB[rows, :] = (normed * gain + shift).astype(BF)
        rows = pl.ds(aligned(base, 16), HALF)
        h1 = DXB[rows, :]
        if len(columns) == 3:
            made = mm(h1, win[layer, :, 0 : 2 * D])
            QKV[layer, rows, 0:D] = (made[:, 0:D] + vector(layer, 2 * D, D)).astype(BF)
            QKV[layer, rows, D : 2 * D] = made[:, D:].astype(BF)
            made = mm(h1, win[layer, :, 2 * D : 3 * D])
            QKV[layer, rows, 2 * D :] = (made + vector(layer, 3 * D, D)).astype(BF)
        else:
            made = mm(h1, win[layer, :, D : 3 * D])
            DMB[rows, :] = made[:, 0:D].astype(BF)
            DA[rows, :] = (made[:, D:] + vector(layer, 3 * D, D)).astype(BF)

    ones = jnp.full((BLK, 128), 1.0, BF)

    def attend(layer, image):
        rows = pl.ds(aligned(image * BLK, 16), BLK)
        for pair in range(3):
            at = pair * 128
            query = QKV[layer, rows, at : at + 128] * BF(0.125)
            keys = QKV[layer, rows, D + at : D + at + 128]
            values = QKV[layer, rows, 2 * D + at : 2 * D + at + 128]
            both = jnp.concatenate([query * even, query * odd], axis=0)
            scores = mm_nt(both, keys)
            probs = []
            for row, size in pieces(HALF):
                part = scores[row : row + size] + key_row
                probs.append(jnp.exp(part - jnp.max(part, axis=-1, keepdims=True)).astype(BF))
            probs = jnp.concatenate(probs, axis=0)
            first = mm(probs[:BLK], jnp.concatenate([values * even, ones], axis=1))
            second = mm(probs[BLK:], jnp.concatenate([values * odd, ones], axis=1))
            made = first[:, :128] * (1.0 / first[:, 128:])
            made = made + second[:, :128] * (1.0 / second[:, 128:])
            ATT[layer, rows, at : at + 128] = made.astype(BF)

    def mlp(layer, half):
        base = half * HALF
        whole = pl.ds(aligned(base, 16), HALF)
        made = mm(ATT[layer, whole, :], win[layer, :, 3 * D : 4 * D])
        bias_out = vector(layer, 4 * D, D)
        gain, shift = vector(layer, 5 * D, D), vector(layer, 6 * D, D)
        for at, size in pieces(HALF):
            rows = pl.ds(aligned(base + at, 16), size)
            middle = X[rows, :] + made[at : at + size] + bias_out
            X[rows, :] = middle
            normed, inverse = norm(middle)
            N2[layer, rows, :] = normed.astype(BF)
            I2[layer, rows, :] = jnp.broadcast_to(inverse, (size, 128))
            DXB[rows, :] = (normed * gain + shift).astype(BF)
        at_place("mid", half, layer)
        at_place("b_up", half, layer)
        h2 = DXB[whole, :]
        for pair in range(2):
            made = mm(h2, win[layer, :, (4 + 2 * pair) * D : (6 + 2 * pair) * D])
            for tile in range(2):
                start = (2 * pair + tile) * D
                columns = slice(start, start + D)
                bias = vector(layer, 7 * D + start, D)
                for at, size in pieces(HALF):
                    rows = pl.ds(aligned(base + at, 16), size)
                    active, slope = gelu_parts(
                        made[at : at + size, tile * D : (tile + 1) * D] + bias
                    )
                    ACT[layer, rows, columns] = active.astype(BF)
                    SLOPE[layer, rows, columns] = slope.astype(BF)
        at_place("up", half, layer)
        at_place("b_down", half, layer)
        made = mm(ACT[layer, whole, :], wdn[layer])
        bias = vector(layer, 7 * D + FF, D)
        for at, size in pieces(HALF):
            rows = pl.ds(aligned(base + at, 16), size)
            X[rows, :] = X[rows, :] + made[at : at + size] + bias
        at_place("down", half, layer)

    at_place("b_start")

    def forward_half(half, carry):
        @pl.when(half == 0)
        def _():
            for copy in local_half(0):
                copy.wait()

        @pl.when(jnp.logical_and(half == 1, lower))
        def _():
            for index in range(2):
                arrived(back_parts[index], img_recv.at[index], img_send.at[index])

        @pl.when(jnp.logical_and(half == 1, jnp.logical_not(lower)))
        def _():
            for copy in local_half(1):
                copy.wait()

        embed(half)
        at_place("embed", half)

        def forward_layer(layer, inner):
            at_place("b_norm", half, layer)
            first_norm(layer, half, (0, 1, 2))
            at_place("norm", half, layer)

            def attend_one(index, nothing):
                attend(layer, 2 * half + index)
                at_place("att", half, layer, index)
                return nothing

            lax.fori_loop(0, 2, attend_one, 0)
            mlp(layer, half)
            return inner

        return lax.fori_loop(0, LAYERS - 1, forward_layer, carry)

    lax.fori_loop(0, 2, forward_half, 0)
    at_place("b_last")

    last = LAYERS - 1

    def last_norm(half, nothing):
        first_norm(last, half, (1, 2))
        at_place("ln", half)
        return nothing

    lax.fori_loop(0, 2, last_norm, 0)

    fac = ("f", f_send, f_recv)
    f_y, f_z = 1, n_y
    f_x = f_z + n_z - 1
    f_v = f_x + n_x - 1
    f_m = f_v + n_y - 1
    part_wide = WFAC // n_y
    group = KEPT * n_shard

    def factors_core():
        go(lambda: FAC.at[1 - c], FC, fac, 0, mate)

    def factors_y():
        arrived(FC, f_recv.at[0], f_send.at[0])
        FAC[c] = FAC[c] + FC[...]
        for o in range(1, n_y):
            go(
                lambda o=o: FAC.at[c, turn(y, o, n_y)], FY.at[o - 1], fac, f_y + o - 1,
                here.to(y=turn(y, o, n_y)),
            )

    def line_factors(z_at, x_at):
        return all_factors.at[c, y, x_at, z_at]

    def factors_z():
        total = FAC[c, y]
        for o in range(1, n_y):
            arrived(FY.at[o - 1], f_recv.at[f_y + o - 1], f_send.at[f_y + o - 1])
            total = total + FY[o - 1]
        FC[0] = total
        pltpu.make_async_copy(FC.at[0], line_factors(z, x), out_local.at[0]).start()
        for o in range(1, n_z):
            go(
                lambda: FC.at[0], line_factors(z, x), fac, f_z + o - 1,
                here.to(z=turn(z, o, n_z)),
            )

    def factors_x():
        for o in range(1, n_z):
            index = f_z + o - 1
            arrived(line_factors(turn(z, n_z - o, n_z), x), f_recv.at[index], f_send.at[index])
        pltpu.make_async_copy(FC.at[0], line_factors(z, x), out_local.at[0]).wait()
        for o in range(1, n_x):
            go(
                lambda: all_factors.at[c, y, x], all_factors.at[c, y, x], fac, f_x + o - 1,
                here.to(x=turn(x, o, n_x)),
            )

    def factors_side():
        for o in range(1, n_x):
            index = f_x + o - 1
            came = all_factors.at[c, y, turn(x, n_x - o, n_x)]
            arrived(came, f_recv.at[index], f_send.at[index])
        for o in range(1, n_y):
            go(
                lambda: all_factors.at[c, y], all_factors.at[c, y], fac, f_v + o - 1,
                here.to(y=turn(y, o, n_y)),
            )

    def factors_mate():
        for o in range(1, n_y):
            index = f_v + o - 1
            came = all_factors.at[c, turn(y, n_y - o, n_y)]
            arrived(came, f_recv.at[index], f_send.at[index])
        go(lambda: all_factors.at[c], all_factors.at[c], fac, f_m, mate)

    def factors_done():
        arrived(all_factors.at[1 - c], f_recv.at[f_m], f_send.at[f_m])

    rs = ("rs", rs_send, rs_recv)
    r_y, r_x = 1, n_y
    r_z = r_x + n_x - 1
    r_gz = r_z + n_z - 1
    r_gx = r_gz + n_z - 1

    def chunk(k):
        if k < CHUNKS:
            slot = k % 3
            return (
                G.at[k], RC.at[slot], RY.at[slot], RX.at[slot], RZ.at[slot], RES.at[k], block
            )
        k = k - CHUNKS
        return GS.at[k], SC.at[0], SY.at[0], SX.at[0], SZ.at[0], SRES.at[k], small_block

    def splits(rows):
        by_x = cut(rows, n_x, 16)
        by_z = cut(rows // by_x, n_z, 16)
        return by_x, rows // by_x, by_z, rows // by_x // by_z

    def step_of(rows, most=192):
        return max(step for step in range(16, most + 1, 16) if rows % step == 0)

    def add_rows(rows, target, target_at, sources):
        step = step_of(rows)

        def one(index, nothing):
            at = index * step
            to = pl.ds(aligned(target_at + at, 16), step)
            total = target[to, :]
            if len(sources) == 1:
                total = total + sources[0][pl.ds(aligned(at, 16), step), :]
            else:
                total = total.astype(F32)
                for source in sources:
                    total = total + source[pl.ds(aligned(at, 16), step), :].astype(F32)
                total = total.astype(BF)
            target[to, :] = total
            return nothing

        lax.fori_loop(0, rows // step, one, 0)

    def reduce_core(k):
        g, rc = chunk(k)[0:2]
        go(lambda: chunk(k)[0].at[:, 1 - c], rc, rs, (k, 0), mate)

    def reduce_y(k):
        g, rc, ry, _, _, _, rows = chunk(k)
        arrived(rc, rs_recv.at[k, 0], rs_send.at[k, 0])
        for o in list(range(1, n_y)) + [0]:
            at = turn(y, o, n_y)
            add_rows(rows, g.at[at, c], 0, [rc.at[at]])
            if o:
                go(
                    lambda o=o: chunk(k)[0].at[turn(y, o, n_y), c], ry.at[o - 1], rs,
                    (k, r_y + o - 1), here.to(y=at),
                )

    def total_of(slots, count, at, step):
        total = None
        for index in range(count):
            value = slots[index, pl.ds(aligned(at, 16), step), :].astype(F32)
            total = value if total is None else total + value
        return total

    def reduce_x(k):
        g, _, ry, rx, _, _, rows = chunk(k)
        by_x, rows_x = splits(rows)[0:2]
        for o in range(1, n_y):
            arrived(ry.at[o - 1], rs_recv.at[k, r_y + o - 1], rs_send.at[k, r_y + o - 1])
        mine = g.at[y, c]
        add_rows(rows, mine, 0, [ry.at[o - 1] for o in range(1, n_y)])
        for o in range(1, n_x):
            to = turn(x, o, n_x)
            if by_x > 1:

                def make(o=o):
                    at = turn(x, o, n_x) * rows_x
                    return chunk(k)[0].at[y, c, pl.ds(aligned(at, 16), rows_x), :]

                go(make, rx.at[o - 1], rs, (k, r_x + o - 1), here.to(x=to))
            else:
                go(lambda: chunk(k)[0].at[y, c], rx.at[x], rs, (k, r_x + o - 1), here.to(x=to))

    def reduce_z(k):
        g, _, _, rx, rz, _, rows = chunk(k)
        by_x, rows_x, by_z, rows_z = splits(rows)
        mine = g.at[y, c]
        for o in range(1, n_x):
            slot = rx.at[o - 1] if by_x > 1 else rx.at[turn(x, n_x - o, n_x)]
            arrived(slot, rs_recv.at[k, r_x + o - 1], rs_send.at[k, r_x + o - 1])
        if by_x > 1:
            start = x * rows_x
            add_rows(rows_x, mine, start, [rx.at[o - 1] for o in range(1, n_x)])
        else:
            start = 0
            rx[x] = mine[...]
            for o in range(1, n_x):
                gone(rs, (k, r_x + o - 1))
            step = step_of(rows)

            def one(index, nothing):
                at = pl.ds(aligned(index * step, 16), step)
                g[y, c, at, :] = total_of(rx, n_x, index * step, step).astype(BF)
                return nothing

            lax.fori_loop(0, rows // step, one, 0)
        for o in range(1, n_z):

            def make(o=o):
                at = x * rows_x if by_x > 1 else 0
                if by_z > 1:
                    at = at + turn(z, o, n_z) * rows_z
                return chunk(k)[0].at[y, c, pl.ds(aligned(at, 16), rows_z), :]

            slot = rz.at[o - 1] if by_z > 1 else rz.at[z]
            go(make, slot, rs, (k, r_z + o - 1), here.to(z=turn(z, o, n_z)))

    def gather_z(k):
        g, _, _, _, rz, res, rows = chunk(k)
        by_x, rows_x, by_z, rows_z = splits(rows)
        start = x * rows_x if by_x > 1 else 0
        if by_z > 1:
            start = start + z * rows_z
        for o in range(1, n_z):
            slot = rz.at[o - 1] if by_z > 1 else rz.at[turn(z, n_z - o, n_z)]
            arrived(slot, rs_recv.at[k, r_z + o - 1], rs_send.at[k, r_z + o - 1])
        own_slot = n_z - 1 if by_z > 1 else z
        rz[own_slot] = g[y, c, pl.ds(aligned(start, 16), rows_z), :]
        share = 1.0 / ((1 if by_x > 1 else n_x) * (1 if by_z > 1 else n_z))
        step = step_of(rows_z, 96)

        def one(index, total):
            low = total_of(rz, n_z, index * step, step).astype(BF)
            res[pl.ds(aligned(start + index * step, 16), step), :] = low
            wide = low.astype(F32)
            return total + fold(wide * wide)

        total = lax.fori_loop(0, rows_z // step, one, zeros) * share
        for at in range(0, D, 128):
            square_sum[...] = square_sum[...] + total[:, at : at + 128]
        if by_z > 1:

            def make():
                at = x * rows_x if by_x > 1 else 0
                return chunk(k)[5].at[pl.ds(aligned(at + z * rows_z, 16), rows_z), :]

            for o in range(1, n_z):
                go(make, make(), rs, (k, r_gz + o - 1), here.to(z=turn(z, o, n_z)))

    def gather_x(k):
        res, rows = chunk(k)[5:7]
        by_x, rows_x, by_z, rows_z = splits(rows)
        if by_z > 1:
            for o in range(1, n_z):
                start = turn(z, n_z - o, n_z) * rows_z
                if by_x > 1:
                    start = start + x * rows_x
                arrived(
                    res.at[pl.ds(aligned(start, 16), rows_z), :],
                    rs_recv.at[k, r_gz + o - 1], rs_send.at[k, r_gz + o - 1],
                )
        if by_x > 1:

            def make():
                return chunk(k)[5].at[pl.ds(aligned(x * rows_x, 16), rows_x), :]

            for o in range(1, n_x):
                go(make, make(), rs, (k, r_gx + o - 1), here.to(x=turn(x, o, n_x)))

    def result(k):
        if k < CHUNKS:
            return pltpu.make_async_copy(RES.at[k], res_out.at[k], out_local.at[1 + k])
        return pltpu.make_async_copy(
            SRES.at[k - CHUNKS], small_out.at[k - CHUNKS], out_local.at[1 + k]
        )

    def gather_done(k):
        res, rows = chunk(k)[5:7]
        by_x, rows_x = splits(rows)[0:2]
        if by_x > 1:
            for o in range(1, n_x):
                start = turn(x, n_x - o, n_x) * rows_x
                arrived(
                    res.at[pl.ds(aligned(start, 16), rows_x), :],
                    rs_recv.at[k, r_gx + o - 1], rs_send.at[k, r_gx + o - 1],
                )
        result(k).start()

    for k in range(CHUNKS + 2):
        actions[f"core{k}"] = functools.partial(reduce_core, k)
        actions[f"y{k}"] = functools.partial(reduce_y, k)
        actions[f"x{k}"] = functools.partial(reduce_x, k)
        actions[f"z{k}"] = functools.partial(reduce_z, k)
        actions[f"gz{k}"] = functools.partial(gather_z, k)
        actions[f"gx{k}"] = functools.partial(gather_x, k)
        actions[f"gd{k}"] = functools.partial(gather_done, k)
    actions.update(
        fc=factors_core, fy=factors_y, fz=factors_z, fx=factors_x, fv=factors_side,
        fm=factors_mate, fd=factors_done,
    )

    def tails(ref, layer=None):
        found = []
        for image in range(KEPT):
            rows = slice(image * BLK + TAIL, (image + 1) * BLK)
            found.append(ref[rows, :] if layer is None else ref[layer, rows, :])
        return jnp.concatenate(found, axis=0)

    @pl.when(lower)
    def _():
        arrived(lab.at[1], img_recv.at[2], img_send.at[2])

    marked = lab[...].reshape(CROWS, 128)[:, 0:1]

    h1 = tails(DXB)
    stream = tails(X)
    query = ((mm(h1, win[last, :, 0:D]) + vector(last, 2 * D, D)).astype(BF)) * BF(0.125)
    head_masks = [lane_mask(D, index * 64, (index + 1) * 64) for index in range(HEADS)]

    def spread(values):
        return jnp.concatenate([values * mask for mask in head_masks], axis=0)

    def gather_heads(values):
        total = None
        for index in range(HEADS):
            part = values[index * 16 : (index + 1) * 16] * head_masks[index].astype(F32)
            total = part if total is None else total + part
        return total

    spread_queries, probabilities, outs = [], [], []
    for image in range(KEPT):
        rows = slice(image * BLK, (image + 1) * BLK)
        queries = spread(query[image * 16 : (image + 1) * 16])
        scores = mm_nt(queries, DMB[rows, :]) + key_row
        raw = jnp.exp(scores - jnp.max(scores, axis=-1, keepdims=True))
        probs = raw * (1.0 / jnp.sum(raw, axis=-1, keepdims=True))
        spread_queries.append(queries)
        probabilities.append(probs)
        outs.append(gather_heads(mm(probs.astype(BF), DA[rows, :])))
    attended = jnp.concatenate(outs, axis=0).astype(BF)
    middle = stream + mm(attended, win[last, :, 3 * D : 4 * D]) + vector(last, 4 * D, D)
    n2, i2 = norm(middle)
    h2 = (n2 * vector(last, 5 * D, D) + vector(last, 6 * D, D)).astype(BF)
    active, slope = gelu_parts(mm(h2, win[last, :, 4 * D :]) + vector(last, 7 * D, FF))
    active = active.astype(BF)
    top = middle + mm(active, wdn[last]) + vector(last, 7 * D + FF, D)
    gain_final = glob[2:3, :]
    nf, inf = norm(top)
    final = (nf * gain_final + glob[3:4, :]).astype(BF)
    class_lane = lax.broadcasted_iota(jnp.int32, (1, CPAD), 1)
    logits = mm(final, low_head[...]) + head_bias[...]
    logits = jnp.where(class_lane < NCLS, logits, -1e30)
    peak = jnp.max(logits, axis=-1, keepdims=True)
    shifted = logits - peak
    raw = jnp.exp(shifted)
    total = jnp.sum(raw, axis=-1, keepdims=True)
    alive = jnp.where(marked >= 0.0, 1.0, 0.0)
    target = jnp.where(class_lane.astype(F32) == marked, 1.0 - SMOOTHING, 0.0) + jnp.where(
        class_lane < NCLS, SMOOTHING / NCLS, 0.0
    )
    log_probs = jnp.where(class_lane < NCLS, shifted - jnp.log(total), 0.0)
    losses = -jnp.sum(target * log_probs, axis=-1, keepdims=True) * alive
    d_logits = ((raw * (1.0 / total) - target) * alive).astype(BF)
    d_final = mm_nt(d_logits, low_head[...])
    last_row = VEC_AT + 12 * LAYERS
    V[last_row : last_row + 1, 0:D] = down_sum(d_final * nf)
    V[last_row + 1 : last_row + 2, 0:D] = down_sum(d_final)
    V[last_row + 2 : last_row + 3, 0:128] = jnp.broadcast_to(down_sum(losses), (1, 128))
    V[last_row + 3 : last_row + 4, 0:128] = jnp.full((1, 128), counts[0].astype(F32), F32)
    d_top = norm_back(d_final, nf, inf, gain_final)
    low_top = d_top.astype(BF)
    store_vector(last, 7 * D + FF, down_sum(d_top))
    d_up = (mm_nt(low_top, wdn[last]) * slope).astype(BF)
    store_vector(last, 7 * D, down_sum(d_up.astype(F32)))
    d_h2 = mm_nt(d_up, win[last, :, 4 * D :])
    store_vector(last, 5 * D, down_sum(d_h2 * n2))
    store_vector(last, 6 * D, down_sum(d_h2))
    d_middle = d_top + norm_back(d_h2, n2, i2, vector(last, 5 * D, D))
    low_middle = d_middle.astype(BF)
    store_vector(last, 4 * D, down_sum(d_middle))
    d_heads = mm_nt(low_middle, win[last, :, 3 * D : 4 * D]).astype(BF)
    d_queries = []
    for image in range(KEPT):
        rows = slice(image * BLK, (image + 1) * BLK)
        ups = spread(d_heads[image * 16 : (image + 1) * 16])
        probs = probabilities[image]
        d_probs = mm_nt(ups, DA[rows, :])
        inner = jnp.sum(d_probs * probs, axis=-1, keepdims=True)
        d_scores = (probs * (d_probs - inner)).astype(BF)
        d_queries.append(gather_heads(mm(d_scores, DMB[rows, :])) * 0.125)
        DMB[rows, :] = mm_tn(d_scores, spread_queries[image]).astype(BF)
        DA[rows, :] = mm_tn(probs.astype(BF), ups).astype(BF)
    d_query = jnp.concatenate(d_queries, axis=0).astype(BF)
    store_vector(last, 2 * D, down_sum(d_query.astype(F32)))
    from_query = mm_nt(d_query, win[last, :, 0:D])

    pick_row = lax.broadcasted_iota(jnp.int32, (group, CROWS), 0)
    pick_lane = lax.broadcasted_iota(jnp.int32, (group, CROWS), 1)
    pick = jnp.where(
        ((pick_row - KEPT * here.shard) * 16 + (CLS - TAIL)) == pick_lane, 1.0, 0.0
    ).astype(BF)
    def keep_factors(half, pieces_of):
        at = 0
        for piece in pieces_of:
            made = None if piece is None else mm(pick, piece).astype(BF)
            for lane in range(0, WFAC - at if made is None else made.shape[-1], 128):
                part, column = divmod(at + lane, part_wide)
                FAC[half, part, :, column : column + 128] = (
                    jnp.zeros((group, 128), BF) if made is None else made[:, lane : lane + 128]
                )
            at += 0 if made is None else made.shape[-1]

    keep_factors(0, (active, h2, attended, h1, final, low_top, None))
    keep_factors(1, (d_up, low_middle, d_query, d_logits, None))
    at_place("class")

    turned = DXB[...].T
    for tile, grads in enumerate((DMB, DA)):
        made = mm(turned, grads[...]).astype(BF)
        for shard in range(n_shard):
            GS[0, shard // 2, shard % 2, tile * rows_in : (tile + 1) * rows_in, :] = made[
                shard * rows_in : (shard + 1) * rows_in
            ]
    at_place("kv")
    store_sums(last, [(3 * D, fold(DA[...].astype(F32)))])

    X[...] = jnp.zeros((ROWS, D), F32)
    gain = vector(last, 0, D)
    gain_sum, shift_sum = zeros, zeros
    for image in range(KEPT):
        rows = slice(image * BLK + TAIL, (image + 1) * BLK)
        part = from_query[image * 16 : (image + 1) * 16]
        normed = N1[last, rows, :].astype(F32)
        gain_sum = gain_sum + fold(part * normed)
        shift_sum = shift_sum + fold(part)
        X[rows, :] = d_middle[image * 16 : (image + 1) * 16] + norm_back(
            part, normed, whole_lanes_of(I1[last, rows, :]), gain
        )

    def first_back(layer, half, made, sums):
        base = half * HALF
        gain = vector(layer, 0, D)
        gain_sum, shift_sum = sums
        for at, size in pieces(HALF):
            rows = pl.ds(aligned(base + at, 16), size)
            part = made[at : at + size]
            normed = N1[layer, rows, :].astype(F32)
            inverse = whole_lanes_of(I1[layer, rows, :])
            gain_sum = gain_sum + fold(part * normed)
            shift_sum = shift_sum + fold(part)
            X[rows, :] = X[rows, :] + norm_back(part, normed, inverse, gain)
        return gain_sum, shift_sum

    def last_back(half, sums):
        rows = pl.ds(aligned(half * HALF, 16), HALF)
        made = mm_nt(DMB[rows, :], win[last, :, D : 2 * D])
        made = made + mm_nt(DA[rows, :], win[last, :, 2 * D : 3 * D])
        sums = first_back(last, half, made, sums)
        at_place("lb", half)
        return sums

    gain_sum, shift_sum = lax.fori_loop(0, 2, last_back, (gain_sum, shift_sum))
    store_sums(last, [(0, gain_sum), (D, shift_sum)])

    def round_up(half, total):
        for at, size in pieces(HALF):
            rows = pl.ds(aligned(half * HALF + at, 16), size)
            up = X[rows, :]
            DXB[rows, :] = up.astype(BF)
            total = total + fold(up)
        return total

    def act_back(layer, half, totals):
        base = half * HALF
        low = DXB[pl.ds(aligned(base, 16), HALF), :]
        ups = []
        for pair in range(2):
            made = mm_nt(low, wdn[layer, 2 * pair * D : 2 * (pair + 1) * D, :])
            for tile in range(2):
                start = (2 * pair + tile) * D
                columns = slice(start, start + D)
                total = totals[2 * pair + tile]
                for at, size in pieces(HALF):
                    rows = pl.ds(aligned(base + at, 16), size)
                    part = made[at : at + size, tile * D : (tile + 1) * D]
                    grad = (part * SLOPE[layer, rows, columns].astype(F32)).astype(BF)
                    DH[rows, columns] = grad
                    total = total + fold(grad.astype(F32))
                ups.append(total)
        return tuple(ups)

    def mlp_back(layer, half, sums):
        base = half * HALF
        whole = pl.ds(aligned(base, 16), HALF)
        gain_sum, shift_sum, bias_out = sums
        made = mm_nt(DH[whole, :], win[layer, :, 4 * D :])
        gain = vector(layer, 5 * D, D)
        for at, size in pieces(HALF):
            rows = pl.ds(aligned(base + at, 16), size)
            part = made[at : at + size]
            normed = N2[layer, rows, :].astype(F32)
            inverse = whole_lanes_of(I2[layer, rows, :])
            gain_sum = gain_sum + fold(part * normed)
            shift_sum = shift_sum + fold(part)
            grad = X[rows, :] + norm_back(part, normed, inverse, gain)
            X[rows, :] = grad
            DMB[rows, :] = grad.astype(BF)
            bias_out = bias_out + fold(grad)
        DA[whole, :] = mm_nt(DMB[whole, :], win[layer, :, 3 * D : 4 * D]).astype(BF)
        return gain_sum, shift_sum, bias_out

    def attend_back(layer, image):
        rows = pl.ds(aligned(image * BLK, 16), BLK)
        for pair in range(3):
            at = pair * 128
            query = QKV[layer, rows, at : at + 128] * BF(0.125)
            keys = QKV[layer, rows, D + at : D + at + 128]
            values = QKV[layer, rows, 2 * D + at : 2 * D + at + 128]
            ups = DA[rows, at : at + 128]
            keys_both = jnp.concatenate([keys * even, keys * odd], axis=0)
            values_both = jnp.concatenate([values * even, values * odd], axis=0)
            scores = mm_nt(keys_both, query)
            d_probs = mm_nt(values_both, ups)
            probs, d_scores = [], []
            for base in (0, BLK):
                low_probs, low_grads = [], []
                for first, end in ((0, 128), (128, BLK)):
                    part = jnp.concatenate(
                        [
                            scores[base : base + TAIL, first:end],
                            scores[base + TAIL : base + BLK, first:end] + key_column[TAIL:],
                        ],
                        axis=0,
                    )
                    raw = jnp.exp(part - jnp.max(part, axis=0, keepdims=True))
                    prob = raw * (1.0 / jnp.sum(raw, axis=0, keepdims=True))
                    grad = d_probs[base : base + BLK, first:end]
                    inner = jnp.sum(grad * prob, axis=0, keepdims=True)
                    low_grads.append((prob * (grad - inner)).astype(BF))
                    low_probs.append(prob.astype(BF))
                probs.append(jnp.concatenate(low_probs, axis=1))
                d_scores.append(jnp.concatenate(low_grads, axis=1))
            probs = jnp.concatenate(probs, axis=0)
            d_scores = jnp.concatenate(d_scores, axis=0)
            d_values = mm(probs, ups)
            d_keys = mm(d_scores, query)
            d_query = mm_tn(d_scores, keys_both) * 0.125
            DH[rows, at : at + 128] = d_query.astype(BF)
            DH[rows, D + at : D + at + 128] = jnp.where(
                low_lane, d_keys[:BLK], d_keys[BLK:]
            ).astype(BF)
            DH[rows, 2 * D + at : 2 * D + at + 128] = jnp.where(
                low_lane, d_values[:BLK], d_values[BLK:]
            ).astype(BF)

    def renew(ref, layer, at):
        gain, shift = vector(layer, at, D), vector(layer, at + D, D)

        def one(index, nothing):
            for at, size in pieces(BLK):
                rows = pl.ds(aligned(index * BLK + at, 16), size)
                DXB[rows, :] = (ref[layer, rows, :].astype(F32) * gain + shift).astype(BF)
            return nothing

        lax.fori_loop(0, KEPT, one, 0)
        return DXB[...].T

    def keep_in(k, tile, made):
        for shard in range(n_shard):
            G[k, shard // 2, shard % 2, tile * rows_in : (tile + 1) * rows_in, :] = made[
                shard * rows_in : (shard + 1) * rows_in
            ]

    def backward(step, carry):
        layer = LAYERS - 2 - step
        kd, ku, kq = 3 * step, 3 * step + 1, 3 * step + 2
        bias_down = lax.fori_loop(0, 2, round_up, zeros)
        at_place("round", layer)
        turned = DXB[...].T
        per = min(rows_down, D)
        for pair in range(2):
            start = 2 * pair * D
            wide = mm(turned, ACT[layer, :, start : start + 2 * D]).astype(BF)
            for tile in range(2):
                made = wide[:, tile * D : (tile + 1) * D].T
                for piece in range(D // per):
                    shard, at = divmod(start + tile * D + piece * per, rows_down)
                    G[kd, shard // 2, shard % 2, at : at + per, :] = made[
                        piece * per : (piece + 1) * per
                    ]
        at_place("dn", layer)

        def one(half, totals):
            totals = act_back(layer, half, totals)
            at_place("act", layer, half)
            return totals

        bias_up = lax.fori_loop(0, 2, one, (zeros,) * 4)
        turned = renew(N2, layer, 5 * D)
        for pair in range(2):
            made = mm(turned, DH[:, 2 * pair * D : 2 * (pair + 1) * D]).astype(BF)
            keep_in(ku, 2 * pair, made[:, :D])
            keep_in(ku, 2 * pair + 1, made[:, D:])
        at_place("ups", layer)

        def one_more(half, sums):
            sums = mlp_back(layer, half, sums)
            at_place("mlpb", layer, half)
            return sums

        gain_sum, shift_sum, bias_out = lax.fori_loop(0, 2, one_more, (zeros, zeros, zeros))
        store_sums(
            layer,
            [(7 * D + FF, bias_down), (5 * D, gain_sum), (6 * D, shift_sum), (4 * D, bias_out)]
            + [(7 * D + tile * D, bias_up[tile]) for tile in range(4)],
        )
        keep_in(kq, 3, mm(ATT[layer].T, DMB[...]).astype(BF))
        at_place("out", layer)

        def two(image, nothing):
            attend_back(layer, image)
            at_place("attb", layer, image)
            return nothing

        lax.fori_loop(0, KEPT, two, 0)
        turned = renew(N1, layer, 0)
        made = mm(turned, DH[:, 0 : 2 * D]).astype(BF)
        keep_in(kq, 0, made[:, :D])
        keep_in(kq, 1, made[:, D:])
        keep_in(kq, 2, mm(turned, DH[:, 2 * D : 3 * D]).astype(BF))
        at_place("qkv", layer)
        store_sums(
            layer,
            [
                (2 * D, fold(DH[:, 0:D].astype(F32))),
                (3 * D, fold(DH[:, 2 * D : 3 * D].astype(F32))),
            ],
        )

        def three(half, sums):
            rows = pl.ds(aligned(half * HALF, 16), HALF)
            made = mm_nt(DH[rows, 0 : 3 * D], win[layer, :, 0 : 3 * D])
            sums = first_back(layer, half, made, sums)
            at_place("fb", layer, half)
            return sums

        gain_sum, shift_sum = lax.fori_loop(0, 2, three, (zeros, zeros))
        store_sums(layer, [(0, gain_sum), (D, shift_sum)])
        return carry

    lax.fori_loop(0, LAYERS - 1, backward, 0)

    for at, size in pieces(BLK):
        total = None
        for image in range(KEPT):
            part = X[image * BLK + at : image * BLK + at + size, :]
            DXB[image * BLK + at : image * BLK + at + size, :] = part.astype(BF)
            total = part if total is None else total + part
        V[at : at + size, 0:D] = total

    vec = ("v", v_send, v_recv)
    v_y, v_x = 1, n_y
    v_z = v_x + n_x - 1
    v_gz = v_z + n_z - 1
    v_gx = v_gz + n_z - 1
    v_gy = v_gx + n_x - 1
    v_gc = v_gy + n_y - 1
    rows_c = VEC_ROWS // 2
    rows_y = rows_c // n_y
    rows_x = rows_y // n_x
    split_z = cut(rows_x, n_z, 8)
    rows_z = rows_x // split_z
    at_c = c * rows_c
    at_y = at_c + y * rows_y
    at_x = at_y + x * rows_x
    at_z = at_x + z * rows_z if split_z > 1 else at_x

    def vrows(ref, at, rows):
        return ref.at[pl.ds(aligned(at, 8), rows), :]

    def vadd(at, rows, sources):
        target = pl.ds(aligned(at, 8), rows)
        total = V[target, :]
        for source in sources:
            total = total + source
        V[target, :] = total

    def vectors_core():
        go(lambda: vrows(V, (1 - c) * rows_c, rows_c), VC, vec, 0, mate)

    def vectors_y():
        arrived(VC, v_recv.at[0], v_send.at[0])
        vadd(at_c, rows_c, [VC[...]])
        for o in range(1, n_y):
            to = turn(y, o, n_y)
            go(
                lambda o=o: vrows(V, at_c + turn(y, o, n_y) * rows_y, rows_y), VY.at[o - 1],
                vec, v_y + o - 1, here.to(y=to),
            )

    def vectors_x():
        for o in range(1, n_y):
            arrived(VY.at[o - 1], v_recv.at[v_y + o - 1], v_send.at[v_y + o - 1])
        vadd(at_y, rows_y, [VY[o - 1] for o in range(1, n_y)])
        for o in range(1, n_x):
            to = turn(x, o, n_x)
            go(
                lambda o=o: vrows(V, at_y + turn(x, o, n_x) * rows_x, rows_x), VX.at[o - 1],
                vec, v_x + o - 1, here.to(x=to),
            )

    def vectors_z():
        for o in range(1, n_x):
            arrived(VX.at[o - 1], v_recv.at[v_x + o - 1], v_send.at[v_x + o - 1])
        vadd(at_x, rows_x, [VX[o - 1] for o in range(1, n_x)])
        for o in range(1, n_z):

            def make(o=o):
                at = at_x + turn(z, o, n_z) * rows_z if split_z > 1 else at_x
                return vrows(V, at, rows_z)

            go(make, VZ.at[z], vec, v_z + o - 1, here.to(z=turn(z, o, n_z)))

    def vectors_gather_z():
        for o in range(1, n_z):
            arrived(
                VZ.at[turn(z, n_z - o, n_z)], v_recv.at[v_z + o - 1], v_send.at[v_z + o - 1]
            )
        target = pl.ds(aligned(at_z, 8), rows_z)
        VZ[z] = V[target, :]
        total = VZ[0]
        for index in range(1, n_z):
            total = total + VZ[index]
        VF[target, :] = total
        if split_z > 1:
            for o in range(1, n_z):
                go(
                    lambda: vrows(VF, at_z, rows_z), vrows(VF, at_z, rows_z), vec, v_gz + o - 1,
                    here.to(z=turn(z, o, n_z)),
                )

    def vectors_gather_x():
        if split_z > 1:
            for o in range(1, n_z):
                came = turn(z, n_z - o, n_z)
                arrived(
                    vrows(VF, at_x + came * rows_z, rows_z), v_recv.at[v_gz + o - 1],
                    v_send.at[v_gz + o - 1],
                )
        for o in range(1, n_x):
            go(
                lambda: vrows(VF, at_x, rows_x), vrows(VF, at_x, rows_x), vec, v_gx + o - 1,
                here.to(x=turn(x, o, n_x)),
            )

    sq = ("q", q_send, q_recv)

    def squares_z():
        SQ[0] = square_sum[...]
        SQZ[z] = square_sum[...]
        for o in range(1, n_z):
            go(lambda: SQ.at[0], SQZ.at[z], sq, o - 1, here.to(z=turn(z, o, n_z)))

    def slot_of(i, j, k):
        return (i * n_y + j) * 2 + k

    def squares_plane():
        for o in range(1, n_z):
            arrived(SQZ.at[turn(z, n_z - o, n_z)], q_recv.at[o - 1], q_send.at[o - 1])
        total = SQZ[0]
        for index in range(1, n_z):
            total = total + SQZ[index]
        SQ[1] = total
        SQP[slot_of(x, y, c)] = total
        for index, step in enumerate(plane):
            go(
                lambda: SQ.at[1], SQP.at[slot_of(x, y, c)], sq, n_z - 1 + index,
                in_plane(step),
            )

    def squares_done():
        for index, (i, j, k) in enumerate(plane):
            slot = slot_of(
                turn(x, n_x - i, n_x), turn(y, n_y - j, n_y), lax.rem(c + k, 2)
            )
            arrived(SQP.at[slot], q_recv.at[n_z - 1 + index], q_send.at[n_z - 1 + index])
        total = SQP[0]
        for index in range(1, 2 * n_x * n_y):
            total = total + SQP[index]
        SQ[2] = total

    def vectors_gather_y():
        for o in range(1, n_x):
            at = at_y + turn(x, n_x - o, n_x) * rows_x
            arrived(vrows(VF, at, rows_x), v_recv.at[v_gx + o - 1], v_send.at[v_gx + o - 1])
        for o in range(1, n_y):
            go(
                lambda: vrows(VF, at_y, rows_y), vrows(VF, at_y, rows_y), vec, v_gy + o - 1,
                here.to(y=turn(y, o, n_y)),
            )

    def vectors_gather_core():
        for o in range(1, n_y):
            at = at_c + turn(y, n_y - o, n_y) * rows_y
            arrived(vrows(VF, at, rows_y), v_recv.at[v_gy + o - 1], v_send.at[v_gy + o - 1])
        go(lambda: vrows(VF, at_c, rows_c), vrows(VF, at_c, rows_c), vec, v_gc, mate)

    def vectors_done():
        arrived(vrows(VF, (1 - c) * rows_c, rows_c), v_recv.at[v_gc], v_send.at[v_gc])

    actions.update(
        vc=vectors_core, vy=vectors_y, vx=vectors_x, vz=vectors_z, vgz=vectors_gather_z,
        vgx=vectors_gather_x, vgy=vectors_gather_y, vgc=vectors_gather_core, vd=vectors_done,
        qz=squares_z, qp=squares_plane, qd=squares_done,
    )
    at_place("emb")
    low = DXB[...]
    for tile in range(2):
        made = mm_tn(pix[:, :, tile * D : (tile + 1) * D].reshape(ROWS, D), low).astype(BF)
        for piece in range(D // rows_patch):
            shard = tile * (D // rows_patch) + piece
            GS[1, shard // 2, shard % 2, 0:rows_patch, :] = made[piece * rows_patch : (piece + 1) * rows_patch]

    at_place("patch")
    ending = SCHEDULE["tail",]
    perform(ending[:-6])
    early = [
        key for key in sent
        if key[0] == "ag" or (key[0] == "rs" and key[1][0] not in (4, 5, 7))
    ]
    for key in early:
        source, send, recv, at = sent.pop(key)
        left_here(source(), recv.at[at], send.at[at])
    perform(ending[-6:])
    last_copies = [
        pltpu.make_async_copy(VF, vec_out, out_local.at[1 + CHUNKS + 2]),
        pltpu.make_async_copy(SQ.at[2], square_out, out_local.at[2 + CHUNKS + 2]),
    ]
    for copy in last_copies:
        copy.start()
    for source, send, recv, at in list(sent.values()):
        left_here(source(), recv.at[at], send.at[at])
    for k in range(CHUNKS + 2):
        result(k).wait()
    for copy in last_copies:
        copy.wait()

    @pl.when(jnp.logical_not(lower))
    def _():
        for index in range(2):
            left_here(given[index], img_recv.at[index], img_send.at[index])
        left_here(lab_given, img_recv.at[2], img_send.at[2])


def run_train(
    n_rep, n_shard, patches, patch_ends, labels, counts, own_patch, own_in, own_down, vecs, glob, pos, head
):
    n_x = 2 ** ((n_rep.bit_length() - 2) // 2)
    n_z, n_y = n_rep // n_x, n_shard // 2
    block = 4 * (D // n_shard)
    small_block = small_rows(block // 2, n_x, n_z)
    group = KEPT * n_shard
    keep = LAYERS - 1
    units = 1 + 3 * LAYERS
    chunks = CHUNKS + 2

    def buf(*shape, dtype=BF):
        return pltpu.VMEM(shape, dtype)

    def sems(*shape):
        return pltpu.SemaphoreType.DMA(shape)

    def reduction(count, slots, rows):
        by_x = cut(rows, n_x, 16)
        by_z = cut(rows // by_x, n_z, 16)
        return [
            buf(count, n_y, 2, rows, D),
            buf(slots, n_y, rows, D),
            buf(slots, n_y - 1, rows, D),
            buf(slots, n_x - 1 if by_x > 1 else n_x, rows // by_x, D),
            buf(slots, n_z, rows // by_x // by_z, D),
            buf(count, rows, D),
        ]

    rows_y = VEC_ROWS // 2 // n_y
    rows_x = rows_y // n_x
    rows_z = rows_x // cut(rows_x, n_z, 8)
    ag_count = n_y + (n_y - 1) * (n_x - 1) * 2 + n_y - 1
    rs_count = 1 + (n_y - 1) + 2 * (n_x - 1) + 2 * (n_z - 1)
    f_count = 1 + 2 * (n_y - 1) + (n_x - 1) + (n_z - 1) + 1
    v_count = 1 + 2 * (n_y - 1) + 2 * (n_x - 1) + 2 * (n_z - 1) + 1
    q_count = n_z - 1 + 2 * n_x * n_y - 1
    whole = pl.BlockSpec(memory_space=pltpu.VMEM)
    there = pl.BlockSpec(memory_space=pl.ANY)
    return pl.pallas_call(
        functools.partial(train, n_rep, n_shard),
        out_shape=[
            jax.ShapeDtypeStruct((CHUNKS, block, D), BF),
            jax.ShapeDtypeStruct((2, small_block, D), BF),
            jax.ShapeDtypeStruct((VEC_ROWS, VEC_WIDE), F32),
            jax.ShapeDtypeStruct((8, 128), F32),
            jax.ShapeDtypeStruct((2, n_y, n_x, n_z, group, WFAC // n_y), BF),
        ],
        in_specs=[there] * 2 + [pl.BlockSpec(memory_space=pltpu.SMEM)] * 2 + [there] * 3 + [whole] * 4,
        out_specs=[there] * 5,
        scratch_shapes=[
            buf(ROWS, D, dtype=F32),
            buf(LAYERS, ROWS, D),
            buf(LAYERS, ROWS, 128, dtype=F32),
            buf(keep, ROWS, 3 * D),
            buf(keep, ROWS, D),
            buf(keep, ROWS, D),
            buf(keep, ROWS, 128, dtype=F32),
            buf(keep, ROWS, FF),
            buf(keep, ROWS, FF),
            buf(ROWS, D),
            buf(ROWS, D),
            buf(ROWS, D),
            buf(ROWS, FF),
            buf(KEPT, BLK, PATCH_DIM),
            buf(2, 32, 128, dtype=F32),
            buf(32, 128, dtype=F32),
            buf(PATCH_DIM, D),
            buf(LAYERS, D, 4 * D + FF),
            buf(LAYERS, FF, D),
            buf(D, CPAD),
            buf(1, CPAD, dtype=F32),
            *reduction(CHUNKS, 3, block),
            *reduction(2, 1, small_block),
            buf(2, n_y, group, WFAC // n_y),
            buf(n_y, group, WFAC // n_y),
            buf(n_y - 1, group, WFAC // n_y),
            buf(VEC_ROWS, VEC_WIDE, dtype=F32),
            buf(VEC_ROWS // 2, VEC_WIDE, dtype=F32),
            buf(n_y - 1, rows_y, VEC_WIDE, dtype=F32),
            buf(n_x - 1, rows_x, VEC_WIDE, dtype=F32),
            buf(n_z, rows_z, VEC_WIDE, dtype=F32),
            buf(VEC_ROWS, VEC_WIDE, dtype=F32),
            buf(3, 8, 128, dtype=F32),
            buf(n_z, 8, 128, dtype=F32),
            buf(2 * n_x * n_y, 8, 128, dtype=F32),
            buf(8, 128, dtype=F32),
            sems(units, ag_count),
            sems(units, ag_count),
            sems(units, 4),
            sems(chunks, rs_count),
            sems(chunks, rs_count),
            sems(f_count),
            sems(f_count),
            sems(v_count),
            sems(v_count),
            sems(q_count),
            sems(q_count),
            sems(3),
            sems(3),
            sems(4),
            sems(3 + chunks),
        ],
        compiler_params=pltpu.CompilerParams(
            vmem_limit_bytes=65400 * 1024, collective_id=0, has_side_effects=True
        ),
        cost_estimate=pl.CostEstimate(
            flops=24_000_000_000, bytes_accessed=30_000_000, transcendentals=10_000_000
        ),
        name="train_step",
    )(patches, patch_ends, labels, counts, own_patch, own_in, own_down, vecs, glob, pos, head)


def adam(weight, first, second, grad, factor, rate):
    share = grad * factor
    first = BETA_FIRST * first + share
    square_scale = (1.0 - BETA_SECOND) / (1.0 - BETA_FIRST) ** 2
    second = BETA_SECOND * second + square_scale * (share * share)
    root_scale = (1.0 / (1.0 - BETA_SECOND**ADAM_STEP)) ** 0.5
    step_scale = rate / (1.0 - BETA_FIRST**ADAM_STEP) / root_scale
    bottom = second * lax.rsqrt(second) + ADAM_EPS / root_scale
    step = first * lax.rsqrt(bottom * bottom)
    return weight * (1.0 - rate * WEIGHT_DECAY) - step * step_scale, first, second


def update(n_rep, n_shard, *refs):
    res, small, vec, exchanged, factors = refs[0:5]
    sources = refs[5:26]
    loss_out, norm_out = refs[26:28]
    targets = refs[28:49]
    buffers = refs[49:70]
    results = refs[70:91]
    last_in, last_down, passing, grad_head, in_sems, out_sems = refs[91:]
    shard = lax.axis_index("shard")
    rows_in = D // n_shard
    rows_down = FF // n_shard
    keep = LAYERS - 1

    def moves(array, layer=None, out=False):
        found = []
        for kind in range(3):
            index = 3 * array + kind
            if out:
                src, dst, sem = results[index], targets[index], out_sems
            else:
                src, dst, sem = sources[index], buffers[index], in_sems
            slot = 0 if layer is None else layer
            if layer is not None:
                src, dst = src.at[layer], dst.at[layer]
            found.append(pltpu.make_async_copy(src, dst, sem.at[index, slot]))
        return found

    layered = [(1, layer) for layer in range(LAYERS)] + [(2, layer) for layer in range(LAYERS)]
    order = layered + [(0, None), (6, None), (5, None), (3, None), (4, None)]
    for array, layer in order:
        for move in moves(array, layer):
            move.start()

    n_rows = factors.shape[2] * factors.shape[3] * factors.shape[4]
    part_wide = factors.shape[5]

    def factor(half, at, size):
        found = []
        while size:
            part, column = divmod(at, part_wide)
            wide = min(size, part_wide - column)
            piece = factors[half, part, :, :, :, column : column + wide]
            found.append(piece.reshape(n_rows, wide))
            at, size = at + wide, size - wide
        return found[0] if len(found) == 1 else jnp.concatenate(found, axis=1)

    def squares(values):
        return fold(values * values)

    total = jnp.zeros((8, D), F32)
    own_rows = pl.multiple_of(shard * rows_in, 8)

    def keep_in(column, made):
        slot = column % 2
        passing[slot] = made
        last_in[:, column * D : (column + 1) * D] = passing[slot, pl.ds(own_rows, rows_in), :]

    h2 = factor(0, FF, D)
    for tile in range(4):
        made = mm_tn(h2, factor(1, tile * D, D))
        keep_in(4 + tile, made)
        total = total + squares(made)
    for tile in range(2):
        last_in[:, (1 + tile) * D : (2 + tile) * D] = small[
            0, tile * rows_in : (tile + 1) * rows_in, :
        ].astype(F32)
    made = mm_tn(factor(0, FF + 2 * D, D), factor(1, FF + D, D))
    keep_in(0, made)
    total = total + squares(made)
    made = mm_tn(factor(0, FF + D, D), factor(1, FF, D))
    keep_in(3, made)
    total = total + squares(made)
    d_top = factor(0, FF + 4 * D, D)
    per = min(rows_down, D)
    for tile in range(4):
        made = mm_tn(factor(0, tile * D, D), d_top)
        total = total + squares(made)
        for piece in range(D // per):
            owner, at = divmod(tile * D + piece * per, rows_down)

            def keep_down(made=made, piece=piece, at=at):
                last_down[at : at + per, :] = made[piece * per : (piece + 1) * per]

            pl.when(shard == owner)(keep_down)
    final = factor(0, FF + 3 * D, D)
    wide = jnp.zeros((8, 128), F32)
    for at in range(0, CPAD, 512):
        d_logits = factor(1, FF + 2 * D + at, 512)
        made = mm_tn(final, d_logits)
        grad_head[0:D, at : at + 512] = made
        bias = down_sum(d_logits.astype(F32))
        grad_head[D : D + 1, at : at + 512] = bias
        sums = squares(made)
        for lane in range(0, 512, 128):
            wide = wide + sums[:, lane : lane + 128]
            row = bias[:, lane : lane + 128]
            wide = wide + (row * row) * 0.125
    for lane in range(0, D, 128):
        wide = wide + total[:, lane : lane + 128]
    used = VEC_AT + 12 * LAYERS + 2
    parts = jnp.zeros((8, D), F32)
    kept_rows = lax.broadcasted_iota(jnp.int32, (8, 1), 0)
    for at in range(0, used, 8):
        value = vec[at : at + 8, 0:D]
        if at + 8 > used:
            value = jnp.where(kept_rows + at < used, value, 0.0)
        parts = parts + value * value
    patch_bias = down_sum(vec[0:PATCHES, 0:D])
    class_row = vec[CLS : CLS + 1, 0:D]
    rest = (patch_bias * patch_bias + class_row * class_row) * 0.125
    parts = parts + rest
    for lane in range(0, D, 128):
        wide = wide + parts[:, lane : lane + 128]
    wide = wide + exchanged[...]
    sum_squares = jnp.sum(jnp.sum(wide, axis=1, keepdims=True), axis=0, keepdims=True)
    inv_count = 1.0 / vec[used + 1 : used + 2, 0:1]
    grad_norm = jnp.sqrt(sum_squares) * inv_count
    norm_out[...] = grad_norm
    loss_out[...] = vec[used : used + 1, 0:1] * inv_count
    scale = jnp.minimum(1.0, CLIP_NORM / grad_norm) * inv_count * (1.0 - BETA_FIRST)

    def apply(array, where, grad, rate):
        refs = [buffers[3 * array + kind] for kind in range(3)]
        made = adam(refs[0][where], refs[1][where], refs[2][where], grad, scale, rate)
        for kind, value in enumerate(made):
            results[3 * array + kind][where] = value

    def begin(array, layer=None):
        for move in moves(array, layer):
            move.wait()

    def finish(array, layer=None):
        for move in moves(array, layer, out=True):
            move.start()

    def loop(count, body):
        def one(index, nothing):
            body(index)
            return nothing

        lax.fori_loop(0, count, one, 0)

    step = 32 if rows_in % 32 == 0 else 16
    for layer in range(LAYERS):
        begin(1, layer)

        def column_of(column):
            lanes = pl.ds(pl.multiple_of(column * D, 128), D)
            for at in range(0, rows_in, step):
                if layer < keep:
                    k = 3 * (keep - 1 - layer) + jnp.where(column < 4, 2, 1)
                    row = pl.multiple_of(lax.rem(column, 4) * rows_in + at, 16)
                    grad = res[k, pl.ds(row, step), :].astype(F32)
                else:
                    grad = last_in[at : at + step, lanes]
                apply(1, (layer, slice(at, at + step), lanes), grad, LEARNING_RATE)

        loop(8, column_of)
        finish(1, layer)
    for layer in range(LAYERS):
        begin(2, layer)

        def rows_of(index):
            for part in range(3):
                at = pl.multiple_of(index * 96 + part * 32, 16)
                if layer < keep:
                    grad = res[3 * (keep - 1 - layer), pl.ds(at, 32), :].astype(F32)
                else:
                    grad = last_down[pl.ds(at, 32), :]
                apply(2, (layer, pl.ds(at, 32), slice(0, D)), grad, LEARNING_RATE)

        loop(rows_down // 96, rows_of)
        finish(2, layer)
    begin(0)

    def patch_rows(index):
        for part in range(3):
            at = pl.multiple_of(index * 96 + part * 32, 16)
            grad = small[1, pl.ds(at, 32), :].astype(F32)
            apply(0, (pl.ds(at, 32), slice(0, D)), grad, LEARNING_RATE)

    loop(PATCH_DIM // n_shard // 96, patch_rows)
    finish(0)
    begin(6)

    def head_rows(index):
        for part in range(3):
            rows = pl.ds(pl.multiple_of(index * 48 + part * 16, 16), 16)
            apply(6, (rows, slice(0, NCLS)), grad_head[rows, 0:NCLS], LEARNING_RATE)

    loop(D // 48, head_rows)
    apply(6, (slice(D, D + 1), slice(0, NCLS)), grad_head[D : D + 1, 0:NCLS], LEARNING_RATE)
    finish(6)
    begin(5)
    apply(5, (slice(0, 1), slice(0, D)), class_row, VECTOR_RATE)
    for at in range(0, PATCHES, 28):
        apply(
            5, (slice(1 + at, 29 + at), slice(0, D)), vec[at : at + 28, 0:D], VECTOR_RATE
        )
    finish(5)
    begin(3)
    for layer in range(LAYERS):
        for piece in range(12):
            row = VEC_AT + 12 * layer + piece
            where = (slice(layer, layer + 1), slice(piece * D, (piece + 1) * D))
            apply(3, where, vec[row : row + 1, 0:D], VECTOR_RATE)
    finish(3)
    begin(4)
    rows = [patch_bias, class_row, vec[used - 2 : used - 1, 0:D], vec[used - 1 : used, 0:D]]
    for index, row in enumerate(rows):
        apply(4, (slice(index, index + 1), slice(0, D)), row, VECTOR_RATE)
    finish(4)
    for array, layer in order:
        for move in moves(array, layer, out=True):
            move.wait()


def run_update(n_rep, n_shard, res, small, vec, squares, factors, arrays):
    whole = pl.BlockSpec(memory_space=pltpu.VMEM)
    there = pl.BlockSpec(memory_space=pl.ANY)
    one = jax.ShapeDtypeStruct((1, 1), F32)
    made = pl.pallas_call(
        functools.partial(update, n_rep, n_shard),
        out_shape=[one, one] + [jax.ShapeDtypeStruct(a.shape, F32) for a in arrays],
        in_specs=[whole] * 5 + [there] * 21,
        out_specs=[whole] * 2 + [there] * 21,
        scratch_shapes=[pltpu.VMEM(a.shape, F32) for a in (*arrays, *arrays)]
        + [
            pltpu.VMEM((D // n_shard, 4 * D + FF), F32),
            pltpu.VMEM((FF // n_shard, D), F32),
            pltpu.VMEM((2, D, D), F32),
            pltpu.VMEM((D + 8, CPAD), F32),
            pltpu.SemaphoreType.DMA((21, LAYERS)),
            pltpu.SemaphoreType.DMA((21, LAYERS)),
        ],
        compiler_params=pltpu.CompilerParams(vmem_limit_bytes=62 * 1024 * 1024),
        cost_estimate=pl.CostEstimate(
            flops=200_000_000, bytes_accessed=50_000_000, transcendentals=4_000_000
        ),
        name="adamw",
    )(res, small, vec, squares, factors, *arrays)
    return made[0].reshape(()), made[1].reshape(()), made[2:]


def shards(
    n_rep, n_shard,
    patches, labels, counts, patch_w, layer_in, layer_down, layer_vecs, glob_vecs, pos_embed, head,
    m_patch, v_patch, m_in, v_in, m_down, v_down, m_vecs, v_vecs, m_glob, v_glob, m_pos, v_pos,
    m_head, v_head,
):
    ends = jnp.pad(patches[:, TAIL:], ((0, 0), (0, BLK - PATCHES), (0, 0)))
    res, small, vec, squares, factors = run_train(
        n_rep, n_shard, patches, ends, labels, counts, patch_w, layer_in, layer_down, layer_vecs,
        glob_vecs, pos_embed, head,
    )
    arrays = [
        patch_w, m_patch, v_patch, layer_in, m_in, v_in, layer_down, m_down, v_down,
        layer_vecs, m_vecs, v_vecs, glob_vecs, m_glob, v_glob, pos_embed, m_pos, v_pos,
        head, m_head, v_head,
    ]
    loss, grad_norm, new = run_update(n_rep, n_shard, res, small, vec, squares, factors, arrays)
    return (loss, grad_norm, *new)


def solution(mesh):
    everywhere = P()
    rows = P("shard", None)
    middle = P(None, "shard", None)
    return jax.shard_map(
        functools.partial(shards, mesh.shape["rep"], mesh.shape["shard"]),
        mesh=mesh,
        in_specs=(
            P(("rep", "shard"), None, None),
            P(("rep", "shard")),
            P(("rep", "shard")),
            rows,
            middle,
            middle,
            *(everywhere,) * 4,
            *(rows,) * 2,
            *(middle,) * 4,
            *(everywhere,) * 8,
        ),
        out_specs=(
            *(everywhere,) * 2,
            *(rows,) * 3,
            *(middle,) * 6,
            *(everywhere,) * 12,
        ),
        check_vma=False,
    )
```

```python
import functools

import jax
import jax.numpy as jnp
from jax import lax
from jax.experimental import pallas as pl
from jax.experimental.pallas import tpu as pltpu
from jax.sharding import PartitionSpec as P

D = 384
HEADS = 6
HEAD_DIM = 64
FF = 1536
PATCH_DIM = 768
PATCHES = 196
NCLS = 1000
LAYERS = 3
SEQ = 197

BLK = 208
CLS = 200
TAIL = 192
KEPT = 4
ROWS = KEPT * BLK
HALF = 2 * BLK
CROWS = KEPT * 16
CPAD = 1024
WIDE = 8 * D + FF

NORM_EPS = 1e-06
SMOOTHING = 0.1
CLIP_NORM = 0.05
LEARNING_RATE = 0.05
VECTOR_RATE = 0.5
BETA_FIRST = 0.9
BETA_SECOND = 0.999
ADAM_EPS = 1e-08
WEIGHT_DECAY = 0.05
ADAM_STEP = 10
GELU_SCALE = 0.7978845608028654
GELU_CUBIC = 0.044715

F32 = jnp.float32
BF = jnp.bfloat16


def mm(left, right):
    return jnp.dot(left, right, preferred_element_type=F32)


def mm_nt(left, right):
    return lax.dot_general(left, right, (((1,), (1,)), ((), ())), preferred_element_type=F32)


def mm_tn(left, right):
    return lax.dot_general(left, right, (((0,), (0,)), ((), ())), preferred_element_type=F32)


def fold(values):
    return jnp.sum(values.reshape(-1, 8, values.shape[-1]), axis=0)


def down_sum(values):
    return jnp.sum(values, axis=0, keepdims=True)


def norm(values):
    centre = values - jnp.mean(values, axis=-1, keepdims=True)
    inverse = lax.rsqrt(jnp.mean(centre * centre, axis=-1, keepdims=True) + NORM_EPS)
    return centre * inverse, inverse


def norm_back(upstream, normed, inverse, gain):
    scaled = upstream * gain
    first = jnp.mean(scaled, axis=-1, keepdims=True)
    second = jnp.mean(scaled * normed, axis=-1, keepdims=True)
    return inverse * (scaled - first - normed * second)


def gelu_parts(hidden):
    bent = hidden * (GELU_SCALE + (GELU_SCALE * GELU_CUBIC) * (hidden * hidden))
    tangent = jnp.tanh(bent)
    share = 0.5 + 0.5 * tangent
    slope = share + (1.0 - tangent * tangent) * (1.5 * bent - GELU_SCALE * hidden)
    return hidden * share, slope


def lane_mask(width, low, high):
    lane = lax.broadcasted_iota(jnp.int32, (1, width), 1)
    return jnp.where((lane >= low) & (lane < high), 1.0, 0.0).astype(BF)


STEP = 16


def pieces(total):
    return [(at, min(STEP, total - at)) for at in range(0, total, STEP)]


SCHEDULE = {
    ("cast", 0): ("ws0",),
    ("cast", 1): ("ws1",),
    ("cast", 2): ("ws2",),
    ("cast", 8): ("wf0", "ws3",),
    ("b_start",): ("wr0", "wf1", "ws4", "we0",),
    ("b_norm", 0, 0): ("wf2", "ws5", "wr1", "wf3", "ws6", "we1",),
    ("norm", 0, 0): ("wr2",),
    ("att", 0, 0, 0): ("wf4", "ws7",),
    ("att", 0, 0, 1): ("wr3",),
    ("b_up", 0, 0): ("we2",),
    ("up", 0, 0): ("wr4", "wf5", "ws8",),
    ("b_down", 0, 0): ("we3",),
    ("down", 0, 0): ("wf6", "ws9",),
    ("b_norm", 0, 1): ("we4",),
    ("norm", 0, 1): ("wf7", "wr5",),
    ("mid", 0, 1): ("wr6", "wf8",),
    ("b_up", 0, 1): ("we5",),
    ("up", 0, 1): ("wf9",),
    ("b_down", 0, 1): ("we6",),
    ("down", 0, 1): ("wr7",),
    ("norm", 1, 0): ("wr8",),
    ("att", 1, 0, 1): ("wr9",),
    ("b_last",): ("we7", "we8", "we9",),
    ("class",): ("fc",),
    ("kv",): ("core6",),
    ("lb", 0): ("fy",),
    ("round", 1): ("y6",),
    ("dn", 1): ("fz", "core0",),
    ("ups", 1): ("y0", "x6", "core1",),
    ("mlpb", 1, 0): ("fx",),
    ("out", 1): ("y1", "z6",),
    ("attb", 1, 2): ("x0", "gz6",),
    ("qkv", 1): ("core2",),
    ("fb", 1, 0): ("gx6",),
    ("fb", 1, 1): ("x1", "z0",),
    ("round", 0): ("y2",),
    ("dn", 0): ("gd6", "core3",),
    ("act", 0, 1): ("z1", "gz0",),
    ("mlpb", 0, 0): ("x2", "y3", "core4",),
    ("mlpb", 0, 1): ("gz1",),
    ("attb", 0, 0): ("gx0",),
    ("attb", 0, 1): ("z2",),
    ("attb", 0, 2): ("gx1",),
    ("attb", 0, 3): ("x3", "y4", "gd0",),
    ("qkv", 0): ("gz2", "core5",),
    ("fb", 0, 0): ("gd1",),
    ("emb",): ("vc",),
    ("patch",): ("z3", "gx2", "core7",),
    ("tail",): ("vy", "x4", "y5", "y7", "fv", "vx", "gz3", "gd2", "z4", "vz", "gx3", "x5", "gz4", "vgz", "gd3", "x7", "z5", "gx4", "vgx", "z7", "gz5", "gd4", "vgy", "gz7", "qz", "fm", "gx5", "vgc", "gx7", "qp", "fd", "vd", "gd5", "gd7", "qd",),
}


WFAC = FF + 5 * D + 128
VEC_ROWS = 256
VEC_AT = BLK
VEC_WIDE = D
MESH = pl.DeviceIdType.MESH
CHUNKS = 6


class Place:
    def __init__(self, n_rep, n_shard):
        self.n_rep, self.n_shard = n_rep, n_shard
        self.n_x = 2 ** ((n_rep.bit_length() - 2) // 2)
        self.n_z = n_rep // self.n_x
        self.n_y = n_shard // 2
        rep, shard = lax.axis_index("rep"), lax.axis_index("shard")
        self.rep, self.shard = rep, shard
        self.z, self.x = rep // self.n_x, rep % self.n_x
        self.y, self.c = shard // 2, shard % 2

    def to(self, x=None, y=None, z=None, c=None):
        x = self.x if x is None else x
        y = self.y if y is None else y
        z = self.z if z is None else z
        c = self.c if c is None else c
        return {"rep": z * self.n_x + x, "shard": y * 2 + c}


def cut(rows, parts, unit):
    return parts if rows % (parts * unit) == 0 else 1


def small_rows(rows, n_x, n_z):
    unit = 16 * n_x * n_z
    padded = -(-rows // unit) * unit
    return padded if 2 * padded <= 3 * rows else rows


def aligned(value, unit):
    return pl.multiple_of(value, unit)


def train(
    n_rep, n_shard,
    patches, patch_ends, labels, counts, own_patch, own_in, own_down, vecs, glob, pos, head,
    res_out, small_out, vec_out, square_out, all_factors,
    X, N1, I1, QKV, ATT, N2, I2, ACT, SLOPE, DXB, DMB, DA, DH,
    pix, lab, lab_given, wp, win, wdn, low_head, head_bias,
    G, RC, RY, RX, RZ, RES, GS, SC, SY, SX, SZ, SRES,
    FAC, FC, FY, V, VC, VY, VX, VZ, VF, SQ, SQZ, SQP, square_sum,
    ag_send, ag_recv, ag_local, rs_send, rs_recv, f_send, f_recv, v_send, v_recv,
    q_send, q_recv,
    img_send, img_recv, img_local, out_local,
):
    here = Place(n_rep, n_shard)
    n_x, n_y, n_z = here.n_x, here.n_y, here.n_z
    x, y, z, c = here.x, here.y, here.z, here.c
    rows_in, rows_down, rows_patch = D // n_shard, FF // n_shard, PATCH_DIM // n_shard
    block = 4 * rows_in
    small_block = small_rows(block // 2, n_x, n_z)
    mate = here.to(c=1 - c)

    def push(src, dst, send, recv, device):
        pltpu.make_async_remote_copy(
            src_ref=src, dst_ref=dst, send_sem=send, recv_sem=recv,
            device_id=device, device_id_type=MESH,
        ).start()

    def arrived(dst, recv, send):
        pltpu.make_async_remote_copy(
            src_ref=dst, dst_ref=dst, send_sem=send, recv_sem=recv,
            device_id=mate, device_id_type=MESH,
        ).wait_recv()

    def left_here(src, recv, send):
        pltpu.make_async_remote_copy(
            src_ref=src, dst_ref=src, send_sem=send, recv_sem=recv,
            device_id=mate, device_id_type=MESH,
        ).wait_send()

    sent = {}

    def go(source, dst, sems, index, device):
        name, send, recv = sems
        push(source(), dst, send.at[index], recv.at[index], device)
        sent[name, index] = (source, send, recv, index)

    def gone(sems, index):
        source, send, recv, at = sent.pop((sems[0], index))
        left_here(source(), recv.at[at], send.at[at])

    def turn(at, by, size):
        return lax.rem(at + by, size)

    barrier = pltpu.get_barrier_semaphore()
    plane = [
        (i, j, k) for i in range(n_x) for j in range(n_y) for k in range(2) if i or j or k
    ]

    def in_plane(step):
        i, j, k = step
        return here.to(x=turn(x, i, n_x), y=turn(y, j, n_y), c=lax.rem(c + k, 2))

    others = [in_plane(step) for step in plane]
    others += [here.to(z=turn(z, o, n_z)) for o in range(1, n_z)]
    for other in others:
        pl.semaphore_signal(barrier, inc=1, device_id=other, device_id_type=MESH)
    pl.semaphore_wait(barrier, len(others))

    def weight(kind, layer, shard, part=None):
        if kind == "patch":
            parts = cut(rows_patch, n_x, 16)
            rows = rows_patch // parts
            if part is None:
                return wp.at[pl.ds(aligned(shard * rows_patch, 16), rows_patch), :]
            return wp.at[pl.ds(aligned(shard * rows_patch + part * rows, 16), rows), :]
        if kind == "down":
            parts = cut(rows_down, n_x, 16)
            rows = rows_down // parts
            if part is None:
                return wdn.at[layer, pl.ds(aligned(shard * rows_down, 16), rows_down), :]
            return wdn.at[layer, pl.ds(aligned(shard * rows_down + part * rows, 16), rows), :]
        base = 0 if kind == "attn" else 4 * D
        rows = pl.ds(aligned(shard * rows_in, 16), rows_in)
        if part is None:
            return win.at[layer, rows, pl.ds(base, 4 * D)]
        wide = 4 * D // n_x
        return win.at[layer, rows, pl.ds(aligned(base + part * wide, 128), wide)]

    units = [("patch", 0)] + [
        (kind, layer) for layer in range(LAYERS) for kind in ("attn", "up", "down")
    ]

    def parts_of(kind):
        if kind == "patch":
            return cut(rows_patch, n_x, 16)
        if kind == "down":
            return cut(rows_down, n_x, 16)
        return n_x

    ag = ("ag", ag_send, ag_recv)
    base_x = n_y
    base_my = base_x + (n_y - 1) * (n_x - 1)
    base_mx = base_my + (n_y - 1)

    stage = 4 * rows_in

    def weights_copies(unit):
        kind, layer = units[unit]
        base = (unit % 2) * stage
        if kind == "patch":
            pairs = [(own_patch, X.at[pl.ds(base, rows_patch)])]
        elif kind == "down":
            pairs = [(own_down.at[layer], X.at[pl.ds(base, rows_down)])]
        else:
            start = 0 if kind == "attn" else 4 * D
            pairs = [
                (
                    own_in.at[layer, :, pl.ds(start + tile * D, D)],
                    X.at[pl.ds(base + tile * rows_in, rows_in)],
                )
                for tile in range(4)
            ]
        return [
            pltpu.make_async_copy(src, dst, ag_local.at[unit, index])
            for index, (src, dst) in enumerate(pairs)
        ]

    def weights_cast(unit):
        kind, layer = units[unit]
        base = (unit % 2) * stage
        for copy in weights_copies(unit):
            copy.wait()
        if kind == "patch":
            rows = pl.ds(aligned(here.shard * rows_patch, 16), rows_patch)
            wp[rows, :] = X[base : base + rows_patch, :].astype(BF)
        elif kind == "down":
            rows = pl.ds(aligned(here.shard * rows_down, 16), rows_down)
            wdn[layer, rows, :] = X[base : base + rows_down, :].astype(BF)
        else:
            start = 0 if kind == "attn" else 4 * D
            rows = pl.ds(aligned(here.shard * rows_in, 16), rows_in)
            for tile in range(4):
                win[layer, rows, start + tile * D : start + (tile + 1) * D] = X[
                    base + tile * rows_in : base + (tile + 1) * rows_in, :
                ].astype(BF)
        if unit + 2 < len(units):
            for copy in weights_copies(unit + 2):
                copy.start()

    def weights_start(unit):
        kind, layer = units[unit]
        part = x if parts_of(kind) > 1 else 0
        for o in range(1, n_y):
            go(
                lambda: weight(kind, layer, here.shard, part),
                weight(kind, layer, here.shard, part), ag, (unit, o),
                here.to(y=turn(y, o, n_y)),
            )
        go(
            lambda: weight(kind, layer, here.shard), weight(kind, layer, here.shard), ag,
            (unit, 0), mate,
        )

    def weights_forward(unit):
        kind, layer = units[unit]
        split = parts_of(kind) > 1
        part = x if split else 0
        for o in range(1, n_y):
            def make(o=o):
                return weight(kind, layer, turn(y, n_y - o, n_y) * 2 + c, part)

            arrived(make(), ag_recv.at[unit, o], ag_send.at[unit, o])
            if split:
                for p in range(1, n_x):
                    index = base_x + (o - 1) * (n_x - 1) + p - 1
                    go(make, make(), ag, (unit, index), here.to(x=turn(x, p, n_x)))
            go(make, make(), ag, (unit, base_my + o - 1), mate)

    def weights_pass(unit):
        kind, layer = units[unit]
        split = parts_of(kind) > 1
        part = x if split else 0
        if split:
            for o in range(1, n_y):
                for p in range(1, n_x):
                    index = (o - 1) * (n_x - 1) + p - 1

                    def make(o=o, p=p):
                        shard = turn(y, n_y - o, n_y) * 2 + c
                        return weight(kind, layer, shard, turn(x, n_x - p, n_x))

                    arrived(
                        make(), ag_recv.at[unit, base_x + index], ag_send.at[unit, base_x + index]
                    )
                    go(make, make(), ag, (unit, base_mx + index), mate)

    def weights_whole(unit):
        kind, layer = units[unit]
        split = parts_of(kind) > 1
        part = x if split else 0
        arrived(weight(kind, layer, y * 2 + 1 - c), ag_recv.at[unit, 0], ag_send.at[unit, 0])
        for o in range(1, n_y):
            shard = turn(y, n_y - o, n_y) * 2 + 1 - c
            index = base_my + o - 1
            arrived(weight(kind, layer, shard, part), ag_recv.at[unit, index], ag_send.at[unit, index])
            if split:
                for p in range(1, n_x):
                    index = base_mx + (o - 1) * (n_x - 1) + p - 1
                    piece = weight(kind, layer, shard, turn(x, n_x - p, n_x))
                    arrived(piece, ag_recv.at[unit, index], ag_send.at[unit, index])

    actions = {}

    def perform(names):
        for name in names:
            actions[name]()

    def at_place(place, *indices):
        for key, names in SCHEDULE.items():
            if key[0] != place:
                continue
            held = None
            for index, value in zip(indices, key[1:], strict=True):
                if not isinstance(index, int):
                    same = index == value
                    held = same if held is None else jnp.logical_and(held, same)
                elif index != value:
                    break
            else:
                if held is None:
                    perform(names)
                else:
                    pl.when(held)(functools.partial(perform, names))

    for unit in range(len(units)):
        actions[f"ws{unit}"] = functools.partial(weights_start, unit)
        actions[f"wf{unit}"] = functools.partial(weights_forward, unit)
        actions[f"wr{unit}"] = functools.partial(weights_pass, unit)
        actions[f"we{unit}"] = functools.partial(weights_whole, unit)

    lower = here.rep < n_rep // 2
    partner = here.to(z=turn(z, n_z // 2, n_z))
    back_parts = (
        pix.at[pl.ds(2, 2), pl.ds(0, TAIL)], pix.at[pl.ds(2, 2), pl.ds(TAIL, BLK - TAIL)]
    )
    given = (patches.at[pl.ds(KEPT, 2), pl.ds(0, TAIL)], patch_ends.at[pl.ds(KEPT, 2)])

    def local_half(half):
        pair = pl.ds(2 * half, 2)
        return (
            pltpu.make_async_copy(
                patches.at[pair, pl.ds(0, TAIL)], pix.at[pair, pl.ds(0, TAIL)],
                img_local.at[half],
            ),
            pltpu.make_async_copy(
                patch_ends.at[pair], pix.at[pair, pl.ds(TAIL, BLK - TAIL)],
                img_local.at[2 + half],
            ),
        )

    def marks(pair):
        row = lax.broadcasted_iota(jnp.int32, (32, 128), 0)
        found = jnp.full((32, 128), -1.0, F32)
        for index in range(2):
            slot = 2 * pair + index
            value = jnp.where(slot < counts[0], labels[slot], -1).astype(F32)
            found = jnp.where(row == CLS - TAIL + 16 * index, value, found)
        return found

    for copy in local_half(0):
        copy.start()
    for unit in range(2):
        for copy in weights_copies(unit):
            copy.start()
    lab[0] = marks(0)
    lab_given[...] = marks(2)

    @pl.when(jnp.logical_not(lower))
    def _():
        for index in range(2):
            push(
                given[index], back_parts[index], img_send.at[index], img_recv.at[index],
                partner,
            )
        push(lab_given, lab.at[1], img_send.at[2], img_recv.at[2], partner)
        for copy in local_half(1):
            copy.start()
        lab[1] = marks(1)

    for unit in range(len(units)):
        weights_cast(unit)
        at_place("cast", unit)

    even = lane_mask(128, 0, 64)
    odd = lane_mask(128, 64, 128)
    low_lane = lax.broadcasted_iota(jnp.int32, (1, 128), 1) < 64
    key_lane = lax.broadcasted_iota(jnp.int32, (1, BLK), 1)
    key_row = jnp.where((key_lane < PATCHES) | (key_lane == CLS), 0.0, -1e30)
    key_sub = lax.broadcasted_iota(jnp.int32, (BLK, 1), 0)
    key_column = jnp.where((key_sub < PATCHES) | (key_sub == CLS), 0.0, -1e30)
    whole_lanes = NCLS // 128 * 128
    low_head[:, 0:whole_lanes] = head[0:D, 0:whole_lanes].astype(BF)
    low_head[:, whole_lanes:] = jnp.zeros((D, CPAD - whole_lanes), BF)
    low_head[:, whole_lanes:NCLS] = head[0:D, whole_lanes:NCLS].astype(BF)
    head_bias[...] = jnp.zeros((1, CPAD), F32)
    head_bias[:, 0:NCLS] = head[D : D + 1, :]
    V[...] = jnp.zeros((VEC_ROWS, VEC_WIDE), F32)
    square_sum[...] = jnp.zeros((8, 128), F32)
    if small_block > block // 2:
        spare = small_block - block // 2
        GS[:, :, :, block // 2 :, :] = jnp.zeros((2, n_y, 2, spare, D), BF)
    zeros = jnp.zeros((8, D), F32)
    patch_bias = glob[0:1, :]

    def whole_lanes_of(tile):
        return jnp.concatenate([tile] * (D // 128), axis=1)

    def vector(layer, at, size):
        return vecs[pl.ds(layer, 1), at : at + size]

    def store_vector(layer, at, row):
        for piece in range(row.shape[-1] // D):
            V[pl.ds(VEC_AT + 12 * layer + at // D + piece, 1), 0:D] = row[
                :, piece * D : (piece + 1) * D
            ]

    def store_sums(layer, parts):
        for at, part in parts:
            store_vector(layer, at, down_sum(part))

    def embed(half):
        made = mm(pix[pl.ds(2 * half, 2)].reshape(HALF, PATCH_DIM), wp[...])
        for image in range(2):
            start = aligned(half * HALF + image * BLK, 16)
            for at, size in pieces(PATCHES - 4):
                X[pl.ds(start + at, size), :] = (
                    made[image * BLK + at : image * BLK + at + size]
                    + pos[1 + at : 1 + at + size, :]
                    + patch_bias
                )
            X[pl.ds(start + TAIL, 16), :] = jnp.zeros((16, D), F32)
            X[pl.ds(start + TAIL, 4), :] = (
                made[image * BLK + TAIL : image * BLK + PATCHES]
                + pos[1 + TAIL : 1 + PATCHES, :]
                + patch_bias
            )
            X[pl.ds(start + CLS, 1), :] = glob[1:2, :] + pos[0:1, :]

    def first_norm(layer, half, columns):
        base = half * HALF
        gain, shift = vector(layer, 0, D), vector(layer, D, D)
        for at, size in pieces(HALF):
            rows = pl.ds(aligned(base + at, 16), size)
            normed, inverse = norm(X[rows, :])
            N1[layer, rows, :] = normed.astype(BF)
            I1[layer, rows, :] = jnp.broadcast_to(inverse, (size, 128))
            DXB[rows, :] = (normed * gain + shift).astype(BF)
        rows = pl.ds(aligned(base, 16), HALF)
        h1 = DXB[rows, :]
        if len(columns) == 3:
            made = mm(h1, win[layer, :, 0 : 2 * D])
            QKV[layer, rows, 0:D] = (made[:, 0:D] + vector(layer, 2 * D, D)).astype(BF)
            QKV[layer, rows, D : 2 * D] = made[:, D:].astype(BF)
            made = mm(h1, win[layer, :, 2 * D : 3 * D])
            QKV[layer, rows, 2 * D :] = (made + vector(layer, 3 * D, D)).astype(BF)
        else:
            made = mm(h1, win[layer, :, D : 3 * D])
            DMB[rows, :] = made[:, 0:D].astype(BF)
            DA[rows, :] = (made[:, D:] + vector(layer, 3 * D, D)).astype(BF)

    ones = jnp.full((BLK, 128), 1.0, BF)

    def attend(layer, image):
        rows = pl.ds(aligned(image * BLK, 16), BLK)
        for pair in range(3):
            at = pair * 128
            query = QKV[layer, rows, at : at + 128] * BF(0.125)
            keys = QKV[layer, rows, D + at : D + at + 128]
            values = QKV[layer, rows, 2 * D + at : 2 * D + at + 128]
            both = jnp.concatenate([query * even, query * odd], axis=0)
            scores = mm_nt(both, keys)
            probs = []
            for row, size in pieces(HALF):
                part = scores[row : row + size] + key_row
                probs.append(jnp.exp(part - jnp.max(part, axis=-1, keepdims=True)).astype(BF))
            probs = jnp.concatenate(probs, axis=0)
            first = mm(probs[:BLK], jnp.concatenate([values * even, ones], axis=1))
            second = mm(probs[BLK:], jnp.concatenate([values * odd, ones], axis=1))
            made = first[:, :128] * (1.0 / first[:, 128:])
            made = made + second[:, :128] * (1.0 / second[:, 128:])
            ATT[layer, rows, at : at + 128] = made.astype(BF)

    def mlp(layer, half):
        base = half * HALF
        whole = pl.ds(aligned(base, 16), HALF)
        made = mm(ATT[layer, whole, :], win[layer, :, 3 * D : 4 * D])
        bias_out = vector(layer, 4 * D, D)
        gain, shift = vector(layer, 5 * D, D), vector(layer, 6 * D, D)
        for at, size in pieces(HALF):
            rows = pl.ds(aligned(base + at, 16), size)
            middle = X[rows, :] + made[at : at + size] + bias_out
            X[rows, :] = middle
            normed, inverse = norm(middle)
            N2[layer, rows, :] = normed.astype(BF)
            I2[layer, rows, :] = jnp.broadcast_to(inverse, (size, 128))
            DXB[rows, :] = (normed * gain + shift).astype(BF)
        at_place("mid", half, layer)
        at_place("b_up", half, layer)
        h2 = DXB[whole, :]
        for pair in range(2):
            made = mm(h2, win[layer, :, (4 + 2 * pair) * D : (6 + 2 * pair) * D])
            for tile in range(2):
                start = (2 * pair + tile) * D
                columns = slice(start, start + D)
                bias = vector(layer, 7 * D + start, D)
                for at, size in pieces(HALF):
                    rows = pl.ds(aligned(base + at, 16), size)
                    active, slope = gelu_parts(
                        made[at : at + size, tile * D : (tile + 1) * D] + bias
                    )
                    ACT[layer, rows, columns] = active.astype(BF)
                    SLOPE[layer, rows, columns] = slope.astype(BF)
        at_place("up", half, layer)
        at_place("b_down", half, layer)
        made = mm(ACT[layer, whole, :], wdn[layer])
        bias = vector(layer, 7 * D + FF, D)
        for at, size in pieces(HALF):
            rows = pl.ds(aligned(base + at, 16), size)
            X[rows, :] = X[rows, :] + made[at : at + size] + bias
        at_place("down", half, layer)

    at_place("b_start")

    def forward_half(half, carry):
        @pl.when(half == 0)
        def _():
            for copy in local_half(0):
                copy.wait()

        @pl.when(jnp.logical_and(half == 1, lower))
        def _():
            for index in range(2):
                arrived(back_parts[index], img_recv.at[index], img_send.at[index])

        @pl.when(jnp.logical_and(half == 1, jnp.logical_not(lower)))
        def _():
            for copy in local_half(1):
                copy.wait()

        embed(half)
        at_place("embed", half)

        def forward_layer(layer, inner):
            at_place("b_norm", half, layer)
            first_norm(layer, half, (0, 1, 2))
            at_place("norm", half, layer)

            def attend_one(index, nothing):
                attend(layer, 2 * half + index)
                at_place("att", half, layer, index)
                return nothing

            lax.fori_loop(0, 2, attend_one, 0)
            mlp(layer, half)
            return inner

        return lax.fori_loop(0, LAYERS - 1, forward_layer, carry)

    lax.fori_loop(0, 2, forward_half, 0)
    at_place("b_last")

    last = LAYERS - 1

    def last_norm(half, nothing):
        first_norm(last, half, (1, 2))
        at_place("ln", half)
        return nothing

    lax.fori_loop(0, 2, last_norm, 0)

    fac = ("f", f_send, f_recv)
    f_y, f_z = 1, n_y
    f_x = f_z + n_z - 1
    f_v = f_x + n_x - 1
    f_m = f_v + n_y - 1
    part_wide = WFAC // n_y
    group = KEPT * n_shard

    def factors_core():
        go(lambda: FAC.at[1 - c], FC, fac, 0, mate)

    def factors_y():
        arrived(FC, f_recv.at[0], f_send.at[0])
        FAC[c] = FAC[c] + FC[...]
        for o in range(1, n_y):
            go(
                lambda o=o: FAC.at[c, turn(y, o, n_y)], FY.at[o - 1], fac, f_y + o - 1,
                here.to(y=turn(y, o, n_y)),
            )

    def line_factors(z_at, x_at):
        return all_factors.at[c, y, x_at, z_at]

    def factors_z():
        total = FAC[c, y]
        for o in range(1, n_y):
            arrived(FY.at[o - 1], f_recv.at[f_y + o - 1], f_send.at[f_y + o - 1])
            total = total + FY[o - 1]
        FC[0] = total
        pltpu.make_async_copy(FC.at[0], line_factors(z, x), out_local.at[0]).start()
        for o in range(1, n_z):
            go(
                lambda: FC.at[0], line_factors(z, x), fac, f_z + o - 1,
                here.to(z=turn(z, o, n_z)),
            )

    def factors_x():
        for o in range(1, n_z):
            index = f_z + o - 1
            arrived(line_factors(turn(z, n_z - o, n_z), x), f_recv.at[index], f_send.at[index])
        pltpu.make_async_copy(FC.at[0], line_factors(z, x), out_local.at[0]).wait()
        for o in range(1, n_x):
            go(
                lambda: all_factors.at[c, y, x], all_factors.at[c, y, x], fac, f_x + o - 1,
                here.to(x=turn(x, o, n_x)),
            )

    def factors_side():
        for o in range(1, n_x):
            index = f_x + o - 1
            came = all_factors.at[c, y, turn(x, n_x - o, n_x)]
            arrived(came, f_recv.at[index], f_send.at[index])
        for o in range(1, n_y):
            go(
                lambda: all_factors.at[c, y], all_factors.at[c, y], fac, f_v + o - 1,
                here.to(y=turn(y, o, n_y)),
            )

    def factors_mate():
        for o in range(1, n_y):
            index = f_v + o - 1
            came = all_factors.at[c, turn(y, n_y - o, n_y)]
            arrived(came, f_recv.at[index], f_send.at[index])
        go(lambda: all_factors.at[c], all_factors.at[c], fac, f_m, mate)

    def factors_done():
        arrived(all_factors.at[1 - c], f_recv.at[f_m], f_send.at[f_m])

    rs = ("rs", rs_send, rs_recv)
    r_y, r_x = 1, n_y
    r_z = r_x + n_x - 1
    r_gz = r_z + n_z - 1
    r_gx = r_gz + n_z - 1

    def chunk(k):
        if k < CHUNKS:
            slot = k % 3
            return (
                G.at[k], RC.at[slot], RY.at[slot], RX.at[slot], RZ.at[slot], RES.at[k], block
            )
        k = k - CHUNKS
        return GS.at[k], SC.at[0], SY.at[0], SX.at[0], SZ.at[0], SRES.at[k], small_block

    def splits(rows):
        by_x = cut(rows, n_x, 16)
        by_z = cut(rows // by_x, n_z, 16)
        return by_x, rows // by_x, by_z, rows // by_x // by_z

    def step_of(rows, most=192):
        return max(step for step in range(16, most + 1, 16) if rows % step == 0)

    def add_rows(rows, target, target_at, sources):
        step = step_of(rows)

        def one(index, nothing):
            at = index * step
            to = pl.ds(aligned(target_at + at, 16), step)
            total = target[to, :]
            if len(sources) == 1:
                total = total + sources[0][pl.ds(aligned(at, 16), step), :]
            else:
                total = total.astype(F32)
                for source in sources:
                    total = total + source[pl.ds(aligned(at, 16), step), :].astype(F32)
                total = total.astype(BF)
            target[to, :] = total
            return nothing

        lax.fori_loop(0, rows // step, one, 0)

    def reduce_core(k):
        g, rc = chunk(k)[0:2]
        go(lambda: chunk(k)[0].at[:, 1 - c], rc, rs, (k, 0), mate)

    def reduce_y(k):
        g, rc, ry, _, _, _, rows = chunk(k)
        arrived(rc, rs_recv.at[k, 0], rs_send.at[k, 0])
        for o in list(range(1, n_y)) + [0]:
            at = turn(y, o, n_y)
            add_rows(rows, g.at[at, c], 0, [rc.at[at]])
            if o:
                go(
                    lambda o=o: chunk(k)[0].at[turn(y, o, n_y), c], ry.at[o - 1], rs,
                    (k, r_y + o - 1), here.to(y=at),
                )

    def total_of(slots, count, at, step):
        total = None
        for index in range(count):
            value = slots[index, pl.ds(aligned(at, 16), step), :].astype(F32)
            total = value if total is None else total + value
        return total

    def reduce_x(k):
        g, _, ry, rx, _, _, rows = chunk(k)
        by_x, rows_x = splits(rows)[0:2]
        for o in range(1, n_y):
            arrived(ry.at[o - 1], rs_recv.at[k, r_y + o - 1], rs_send.at[k, r_y + o - 1])
        mine = g.at[y, c]
        add_rows(rows, mine, 0, [ry.at[o - 1] for o in range(1, n_y)])
        for o in range(1, n_x):
            to = turn(x, o, n_x)
            if by_x > 1:

                def make(o=o):
                    at = turn(x, o, n_x) * rows_x
                    return chunk(k)[0].at[y, c, pl.ds(aligned(at, 16), rows_x), :]

                go(make, rx.at[o - 1], rs, (k, r_x + o - 1), here.to(x=to))
            else:
                go(lambda: chunk(k)[0].at[y, c], rx.at[x], rs, (k, r_x + o - 1), here.to(x=to))

    def reduce_z(k):
        g, _, _, rx, rz, _, rows = chunk(k)
        by_x, rows_x, by_z, rows_z = splits(rows)
        mine = g.at[y, c]
        for o in range(1, n_x):
            slot = rx.at[o - 1] if by_x > 1 else rx.at[turn(x, n_x - o, n_x)]
            arrived(slot, rs_recv.at[k, r_x + o - 1], rs_send.at[k, r_x + o - 1])
        if by_x > 1:
            start = x * rows_x
            add_rows(rows_x, mine, start, [rx.at[o - 1] for o in range(1, n_x)])
        else:
            start = 0
            rx[x] = mine[...]
            for o in range(1, n_x):
                gone(rs, (k, r_x + o - 1))
            step = step_of(rows)

            def one(index, nothing):
                at = pl.ds(aligned(index * step, 16), step)
                g[y, c, at, :] = total_of(rx, n_x, index * step, step).astype(BF)
                return nothing

            lax.fori_loop(0, rows // step, one, 0)
        for o in range(1, n_z):

            def make(o=o):
                at = x * rows_x if by_x > 1 else 0
                if by_z > 1:
                    at = at + turn(z, o, n_z) * rows_z
                return chunk(k)[0].at[y, c, pl.ds(aligned(at, 16), rows_z), :]

            slot = rz.at[o - 1] if by_z > 1 else rz.at[z]
            go(make, slot, rs, (k, r_z + o - 1), here.to(z=turn(z, o, n_z)))

    def gather_z(k):
        g, _, _, _, rz, res, rows = chunk(k)
        by_x, rows_x, by_z, rows_z = splits(rows)
        start = x * rows_x if by_x > 1 else 0
        if by_z > 1:
            start = start + z * rows_z
        for o in range(1, n_z):
            slot = rz.at[o - 1] if by_z > 1 else rz.at[turn(z, n_z - o, n_z)]
            arrived(slot, rs_recv.at[k, r_z + o - 1], rs_send.at[k, r_z + o - 1])
        own_slot = n_z - 1 if by_z > 1 else z
        rz[own_slot] = g[y, c, pl.ds(aligned(start, 16), rows_z), :]
        share = 1.0 / ((1 if by_x > 1 else n_x) * (1 if by_z > 1 else n_z))
        step = step_of(rows_z, 96)

        def one(index, total):
            low = total_of(rz, n_z, index * step, step).astype(BF)
            res[pl.ds(aligned(start + index * step, 16), step), :] = low
            wide = low.astype(F32)
            return total + fold(wide * wide)

        total = lax.fori_loop(0, rows_z // step, one, zeros) * share
        for at in range(0, D, 128):
            square_sum[...] = square_sum[...] + total[:, at : at + 128]
        if by_z > 1:

            def make():
                at = x * rows_x if by_x > 1 else 0
                return chunk(k)[5].at[pl.ds(aligned(at + z * rows_z, 16), rows_z), :]

            for o in range(1, n_z):
                go(make, make(), rs, (k, r_gz + o - 1), here.to(z=turn(z, o, n_z)))

    def gather_x(k):
        res, rows = chunk(k)[5:7]
        by_x, rows_x, by_z, rows_z = splits(rows)
        if by_z > 1:
            for o in range(1, n_z):
                start = turn(z, n_z - o, n_z) * rows_z
                if by_x > 1:
                    start = start + x * rows_x
                arrived(
                    res.at[pl.ds(aligned(start, 16), rows_z), :],
                    rs_recv.at[k, r_gz + o - 1], rs_send.at[k, r_gz + o - 1],
                )
        if by_x > 1:

            def make():
                return chunk(k)[5].at[pl.ds(aligned(x * rows_x, 16), rows_x), :]

            for o in range(1, n_x):
                go(make, make(), rs, (k, r_gx + o - 1), here.to(x=turn(x, o, n_x)))

    def result(k):
        if k < CHUNKS:
            return pltpu.make_async_copy(RES.at[k], res_out.at[k], out_local.at[1 + k])
        return pltpu.make_async_copy(
            SRES.at[k - CHUNKS], small_out.at[k - CHUNKS], out_local.at[1 + k]
        )

    def gather_done(k):
        res, rows = chunk(k)[5:7]
        by_x, rows_x = splits(rows)[0:2]
        if by_x > 1:
            for o in range(1, n_x):
                start = turn(x, n_x - o, n_x) * rows_x
                arrived(
                    res.at[pl.ds(aligned(start, 16), rows_x), :],
                    rs_recv.at[k, r_gx + o - 1], rs_send.at[k, r_gx + o - 1],
                )
        result(k).start()

    for k in range(CHUNKS + 2):
        actions[f"core{k}"] = functools.partial(reduce_core, k)
        actions[f"y{k}"] = functools.partial(reduce_y, k)
        actions[f"x{k}"] = functools.partial(reduce_x, k)
        actions[f"z{k}"] = functools.partial(reduce_z, k)
        actions[f"gz{k}"] = functools.partial(gather_z, k)
        actions[f"gx{k}"] = functools.partial(gather_x, k)
        actions[f"gd{k}"] = functools.partial(gather_done, k)
    actions.update(
        fc=factors_core, fy=factors_y, fz=factors_z, fx=factors_x, fv=factors_side,
        fm=factors_mate, fd=factors_done,
    )

    def tails(ref, layer=None):
        found = []
        for image in range(KEPT):
            rows = slice(image * BLK + TAIL, (image + 1) * BLK)
            found.append(ref[rows, :] if layer is None else ref[layer, rows, :])
        return jnp.concatenate(found, axis=0)

    @pl.when(lower)
    def _():
        arrived(lab.at[1], img_recv.at[2], img_send.at[2])

    marked = lab[...].reshape(CROWS, 128)[:, 0:1]

    h1 = tails(DXB)
    stream = tails(X)
    query = ((mm(h1, win[last, :, 0:D]) + vector(last, 2 * D, D)).astype(BF)) * BF(0.125)
    head_masks = [lane_mask(D, index * 64, (index + 1) * 64) for index in range(HEADS)]

    def spread(values):
        return jnp.concatenate([values * mask for mask in head_masks], axis=0)

    def gather_heads(values):
        total = None
        for index in range(HEADS):
            part = values[index * 16 : (index + 1) * 16] * head_masks[index].astype(F32)
            total = part if total is None else total + part
        return total

    spread_queries, probabilities, outs = [], [], []
    for image in range(KEPT):
        rows = slice(image * BLK, (image + 1) * BLK)
        queries = spread(query[image * 16 : (image + 1) * 16])
        scores = mm_nt(queries, DMB[rows, :]) + key_row
        raw = jnp.exp(scores - jnp.max(scores, axis=-1, keepdims=True))
        probs = raw * (1.0 / jnp.sum(raw, axis=-1, keepdims=True))
        spread_queries.append(queries)
        probabilities.append(probs)
        outs.append(gather_heads(mm(probs.astype(BF), DA[rows, :])))
    attended = jnp.concatenate(outs, axis=0).astype(BF)
    middle = stream + mm(attended, win[last, :, 3 * D : 4 * D]) + vector(last, 4 * D, D)
    n2, i2 = norm(middle)
    h2 = (n2 * vector(last, 5 * D, D) + vector(last, 6 * D, D)).astype(BF)
    active, slope = gelu_parts(mm(h2, win[last, :, 4 * D :]) + vector(last, 7 * D, FF))
    active = active.astype(BF)
    top = middle + mm(active, wdn[last]) + vector(last, 7 * D + FF, D)
    gain_final = glob[2:3, :]
    nf, inf = norm(top)
    final = (nf * gain_final + glob[3:4, :]).astype(BF)
    class_lane = lax.broadcasted_iota(jnp.int32, (1, CPAD), 1)
    logits = mm(final, low_head[...]) + head_bias[...]
    logits = jnp.where(class_lane < NCLS, logits, -1e30)
    peak = jnp.max(logits, axis=-1, keepdims=True)
    shifted = logits - peak
    raw = jnp.exp(shifted)
    total = jnp.sum(raw, axis=-1, keepdims=True)
    alive = jnp.where(marked >= 0.0, 1.0, 0.0)
    target = jnp.where(class_lane.astype(F32) == marked, 1.0 - SMOOTHING, 0.0) + jnp.where(
        class_lane < NCLS, SMOOTHING / NCLS, 0.0
    )
    log_probs = jnp.where(class_lane < NCLS, shifted - jnp.log(total), 0.0)
    losses = -jnp.sum(target * log_probs, axis=-1, keepdims=True) * alive
    d_logits = ((raw * (1.0 / total) - target) * alive).astype(BF)
    d_final = mm_nt(d_logits, low_head[...])
    last_row = VEC_AT + 12 * LAYERS
    V[last_row : last_row + 1, 0:D] = down_sum(d_final * nf)
    V[last_row + 1 : last_row + 2, 0:D] = down_sum(d_final)
    V[last_row + 2 : last_row + 3, 0:128] = jnp.broadcast_to(down_sum(losses), (1, 128))
    V[last_row + 3 : last_row + 4, 0:128] = jnp.full((1, 128), counts[0].astype(F32), F32)
    d_top = norm_back(d_final, nf, inf, gain_final)
    low_top = d_top.astype(BF)
    store_vector(last, 7 * D + FF, down_sum(d_top))
    d_up = (mm_nt(low_top, wdn[last]) * slope).astype(BF)
    store_vector(last, 7 * D, down_sum(d_up.astype(F32)))
    d_h2 = mm_nt(d_up, win[last, :, 4 * D :])
    store_vector(last, 5 * D, down_sum(d_h2 * n2))
    store_vector(last, 6 * D, down_sum(d_h2))
    d_middle = d_top + norm_back(d_h2, n2, i2, vector(last, 5 * D, D))
    low_middle = d_middle.astype(BF)
    store_vector(last, 4 * D, down_sum(d_middle))
    d_heads = mm_nt(low_middle, win[last, :, 3 * D : 4 * D]).astype(BF)
    d_queries = []
    for image in range(KEPT):
        rows = slice(image * BLK, (image + 1) * BLK)
        ups = spread(d_heads[image * 16 : (image + 1) * 16])
        probs = probabilities[image]
        d_probs = mm_nt(ups, DA[rows, :])
        inner = jnp.sum(d_probs * probs, axis=-1, keepdims=True)
        d_scores = (probs * (d_probs - inner)).astype(BF)
        d_queries.append(gather_heads(mm(d_scores, DMB[rows, :])) * 0.125)
        DMB[rows, :] = mm_tn(d_scores, spread_queries[image]).astype(BF)
        DA[rows, :] = mm_tn(probs.astype(BF), ups).astype(BF)
    d_query = jnp.concatenate(d_queries, axis=0).astype(BF)
    store_vector(last, 2 * D, down_sum(d_query.astype(F32)))
    from_query = mm_nt(d_query, win[last, :, 0:D])

    pick_row = lax.broadcasted_iota(jnp.int32, (group, CROWS), 0)
    pick_lane = lax.broadcasted_iota(jnp.int32, (group, CROWS), 1)
    pick = jnp.where(
        ((pick_row - KEPT * here.shard) * 16 + (CLS - TAIL)) == pick_lane, 1.0, 0.0
    ).astype(BF)
    def keep_factors(half, pieces_of):
        at = 0
        for piece in pieces_of:
            made = None if piece is None else mm(pick, piece).astype(BF)
            for lane in range(0, WFAC - at if made is None else made.shape[-1], 128):
                part, column = divmod(at + lane, part_wide)
                FAC[half, part, :, column : column + 128] = (
                    jnp.zeros((group, 128), BF) if made is None else made[:, lane : lane + 128]
                )
            at += 0 if made is None else made.shape[-1]

    keep_factors(0, (active, h2, attended, h1, final, low_top, None))
    keep_factors(1, (d_up, low_middle, d_query, d_logits, None))
    at_place("class")

    turned = DXB[...].T
    for tile, grads in enumerate((DMB, DA)):
        made = mm(turned, grads[...]).astype(BF)
        for shard in range(n_shard):
            GS[0, shard // 2, shard % 2, tile * rows_in : (tile + 1) * rows_in, :] = made[
                shard * rows_in : (shard + 1) * rows_in
            ]
    at_place("kv")
    store_sums(last, [(3 * D, fold(DA[...].astype(F32)))])

    X[...] = jnp.zeros((ROWS, D), F32)
    gain = vector(last, 0, D)
    gain_sum, shift_sum = zeros, zeros
    for image in range(KEPT):
        rows = slice(image * BLK + TAIL, (image + 1) * BLK)
        part = from_query[image * 16 : (image + 1) * 16]
        normed = N1[last, rows, :].astype(F32)
        gain_sum = gain_sum + fold(part * normed)
        shift_sum = shift_sum + fold(part)
        X[rows, :] = d_middle[image * 16 : (image + 1) * 16] + norm_back(
            part, normed, whole_lanes_of(I1[last, rows, :]), gain
        )

    def first_back(layer, half, made, sums):
        base = half * HALF
        gain = vector(layer, 0, D)
        gain_sum, shift_sum = sums
        for at, size in pieces(HALF):
            rows = pl.ds(aligned(base + at, 16), size)
            part = made[at : at + size]
            normed = N1[layer, rows, :].astype(F32)
            inverse = whole_lanes_of(I1[layer, rows, :])
            gain_sum = gain_sum + fold(part * normed)
            shift_sum = shift_sum + fold(part)
            X[rows, :] = X[rows, :] + norm_back(part, normed, inverse, gain)
        return gain_sum, shift_sum

    def last_back(half, sums):
        rows = pl.ds(aligned(half * HALF, 16), HALF)
        made = mm_nt(DMB[rows, :], win[last, :, D : 2 * D])
        made = made + mm_nt(DA[rows, :], win[last, :, 2 * D : 3 * D])
        sums = first_back(last, half, made, sums)
        at_place("lb", half)
        return sums

    gain_sum, shift_sum = lax.fori_loop(0, 2, last_back, (gain_sum, shift_sum))
    store_sums(last, [(0, gain_sum), (D, shift_sum)])

    def round_up(half, total):
        for at, size in pieces(HALF):
            rows = pl.ds(aligned(half * HALF + at, 16), size)
            up = X[rows, :]
            DXB[rows, :] = up.astype(BF)
            total = total + fold(up)
        return total

    def act_back(layer, half, totals):
        base = half * HALF
        low = DXB[pl.ds(aligned(base, 16), HALF), :]
        ups = []
        for pair in range(2):
            made = mm_nt(low, wdn[layer, 2 * pair * D : 2 * (pair + 1) * D, :])
            for tile in range(2):
                start = (2 * pair + tile) * D
                columns = slice(start, start + D)
                total = totals[2 * pair + tile]
                for at, size in pieces(HALF):
                    rows = pl.ds(aligned(base + at, 16), size)
                    part = made[at : at + size, tile * D : (tile + 1) * D]
                    grad = (part * SLOPE[layer, rows, columns].astype(F32)).astype(BF)
                    DH[rows, columns] = grad
                    total = total + fold(grad.astype(F32))
                ups.append(total)
        return tuple(ups)

    def mlp_back(layer, half, sums):
        base = half * HALF
        whole = pl.ds(aligned(base, 16), HALF)
        gain_sum, shift_sum, bias_out = sums
        made = mm_nt(DH[whole, :], win[layer, :, 4 * D :])
        gain = vector(layer, 5 * D, D)
        for at, size in pieces(HALF):
            rows = pl.ds(aligned(base + at, 16), size)
            part = made[at : at + size]
            normed = N2[layer, rows, :].astype(F32)
            inverse = whole_lanes_of(I2[layer, rows, :])
            gain_sum = gain_sum + fold(part * normed)
            shift_sum = shift_sum + fold(part)
            grad = X[rows, :] + norm_back(part, normed, inverse, gain)
            X[rows, :] = grad
            DMB[rows, :] = grad.astype(BF)
            bias_out = bias_out + fold(grad)
        DA[whole, :] = mm_nt(DMB[whole, :], win[layer, :, 3 * D : 4 * D]).astype(BF)
        return gain_sum, shift_sum, bias_out

    def attend_back(layer, image):
        rows = pl.ds(aligned(image * BLK, 16), BLK)
        for pair in range(3):
            at = pair * 128
            query = QKV[layer, rows, at : at + 128] * BF(0.125)
            keys = QKV[layer, rows, D + at : D + at + 128]
            values = QKV[layer, rows, 2 * D + at : 2 * D + at + 128]
            ups = DA[rows, at : at + 128]
            keys_both = jnp.concatenate([keys * even, keys * odd], axis=0)
            values_both = jnp.concatenate([values * even, values * odd], axis=0)
            scores = mm_nt(keys_both, query)
            d_probs = mm_nt(values_both, ups)
            probs, d_scores = [], []
            for base in (0, BLK):
                low_probs, low_grads = [], []
                for first, end in ((0, 128), (128, BLK)):
                    part = jnp.concatenate(
                        [
                            scores[base : base + TAIL, first:end],
                            scores[base + TAIL : base + BLK, first:end] + key_column[TAIL:],
                        ],
                        axis=0,
                    )
                    raw = jnp.exp(part - jnp.max(part, axis=0, keepdims=True))
                    prob = raw * (1.0 / jnp.sum(raw, axis=0, keepdims=True))
                    grad = d_probs[base : base + BLK, first:end]
                    inner = jnp.sum(grad * prob, axis=0, keepdims=True)
                    low_grads.append((prob * (grad - inner)).astype(BF))
                    low_probs.append(prob.astype(BF))
                probs.append(jnp.concatenate(low_probs, axis=1))
                d_scores.append(jnp.concatenate(low_grads, axis=1))
            probs = jnp.concatenate(probs, axis=0)
            d_scores = jnp.concatenate(d_scores, axis=0)
            d_values = mm(probs, ups)
            d_keys = mm(d_scores, query)
            d_query = mm_tn(d_scores, keys_both) * 0.125
            DH[rows, at : at + 128] = d_query.astype(BF)
            DH[rows, D + at : D + at + 128] = jnp.where(
                low_lane, d_keys[:BLK], d_keys[BLK:]
            ).astype(BF)
            DH[rows, 2 * D + at : 2 * D + at + 128] = jnp.where(
                low_lane, d_values[:BLK], d_values[BLK:]
            ).astype(BF)

    def renew(ref, layer, at):
        gain, shift = vector(layer, at, D), vector(layer, at + D, D)

        def one(index, nothing):
            for at, size in pieces(BLK):
                rows = pl.ds(aligned(index * BLK + at, 16), size)
                DXB[rows, :] = (ref[layer, rows, :].astype(F32) * gain + shift).astype(BF)
            return nothing

        lax.fori_loop(0, KEPT, one, 0)
        return DXB[...].T

    def keep_in(k, tile, made):
        for shard in range(n_shard):
            G[k, shard // 2, shard % 2, tile * rows_in : (tile + 1) * rows_in, :] = made[
                shard * rows_in : (shard + 1) * rows_in
            ]

    def backward(step, carry):
        layer = LAYERS - 2 - step
        kd, ku, kq = 3 * step, 3 * step + 1, 3 * step + 2
        bias_down = lax.fori_loop(0, 2, round_up, zeros)
        at_place("round", layer)
        turned = DXB[...].T
        per = min(rows_down, D)
        for pair in range(2):
            start = 2 * pair * D
            wide = mm(turned, ACT[layer, :, start : start + 2 * D]).astype(BF)
            for tile in range(2):
                made = wide[:, tile * D : (tile + 1) * D].T
                for piece in range(D // per):
                    shard, at = divmod(start + tile * D + piece * per, rows_down)
                    G[kd, shard // 2, shard % 2, at : at + per, :] = made[
                        piece * per : (piece + 1) * per
                    ]
        at_place("dn", layer)

        def one(half, totals):
            totals = act_back(layer, half, totals)
            at_place("act", layer, half)
            return totals

        bias_up = lax.fori_loop(0, 2, one, (zeros,) * 4)
        turned = renew(N2, layer, 5 * D)
        for pair in range(2):
            made = mm(turned, DH[:, 2 * pair * D : 2 * (pair + 1) * D]).astype(BF)
            keep_in(ku, 2 * pair, made[:, :D])
            keep_in(ku, 2 * pair + 1, made[:, D:])
        at_place("ups", layer)

        def one_more(half, sums):
            sums = mlp_back(layer, half, sums)
            at_place("mlpb", layer, half)
            return sums

        gain_sum, shift_sum, bias_out = lax.fori_loop(0, 2, one_more, (zeros, zeros, zeros))
        store_sums(
            layer,
            [(7 * D + FF, bias_down), (5 * D, gain_sum), (6 * D, shift_sum), (4 * D, bias_out)]
            + [(7 * D + tile * D, bias_up[tile]) for tile in range(4)],
        )
        keep_in(kq, 3, mm(ATT[layer].T, DMB[...]).astype(BF))
        at_place("out", layer)

        def two(image, nothing):
            attend_back(layer, image)
            at_place("attb", layer, image)
            return nothing

        lax.fori_loop(0, KEPT, two, 0)
        turned = renew(N1, layer, 0)
        made = mm(turned, DH[:, 0 : 2 * D]).astype(BF)
        keep_in(kq, 0, made[:, :D])
        keep_in(kq, 1, made[:, D:])
        keep_in(kq, 2, mm(turned, DH[:, 2 * D : 3 * D]).astype(BF))
        at_place("qkv", layer)
        store_sums(
            layer,
            [
                (2 * D, fold(DH[:, 0:D].astype(F32))),
                (3 * D, fold(DH[:, 2 * D : 3 * D].astype(F32))),
            ],
        )

        def three(half, sums):
            rows = pl.ds(aligned(half * HALF, 16), HALF)
            made = mm_nt(DH[rows, 0 : 3 * D], win[layer, :, 0 : 3 * D])
            sums = first_back(layer, half, made, sums)
            at_place("fb", layer, half)
            return sums

        gain_sum, shift_sum = lax.fori_loop(0, 2, three, (zeros, zeros))
        store_sums(layer, [(0, gain_sum), (D, shift_sum)])
        return carry

    lax.fori_loop(0, LAYERS - 1, backward, 0)

    for at, size in pieces(BLK):
        total = None
        for image in range(KEPT):
            part = X[image * BLK + at : image * BLK + at + size, :]
            DXB[image * BLK + at : image * BLK + at + size, :] = part.astype(BF)
            total = part if total is None else total + part
        V[at : at + size, 0:D] = total

    vec = ("v", v_send, v_recv)
    v_y, v_x = 1, n_y
    v_z = v_x + n_x - 1
    v_gz = v_z + n_z - 1
    v_gx = v_gz + n_z - 1
    v_gy = v_gx + n_x - 1
    v_gc = v_gy + n_y - 1
    rows_c = VEC_ROWS // 2
    rows_y = rows_c // n_y
    rows_x = rows_y // n_x
    split_z = cut(rows_x, n_z, 8)
    rows_z = rows_x // split_z
    at_c = c * rows_c
    at_y = at_c + y * rows_y
    at_x = at_y + x * rows_x
    at_z = at_x + z * rows_z if split_z > 1 else at_x

    def vrows(ref, at, rows):
        return ref.at[pl.ds(aligned(at, 8), rows), :]

    def vadd(at, rows, sources):
        target = pl.ds(aligned(at, 8), rows)
        total = V[target, :]
        for source in sources:
            total = total + source
        V[target, :] = total

    def vectors_core():
        go(lambda: vrows(V, (1 - c) * rows_c, rows_c), VC, vec, 0, mate)

    def vectors_y():
        arrived(VC, v_recv.at[0], v_send.at[0])
        vadd(at_c, rows_c, [VC[...]])
        for o in range(1, n_y):
            to = turn(y, o, n_y)
            go(
                lambda o=o: vrows(V, at_c + turn(y, o, n_y) * rows_y, rows_y), VY.at[o - 1],
                vec, v_y + o - 1, here.to(y=to),
            )

    def vectors_x():
        for o in range(1, n_y):
            arrived(VY.at[o - 1], v_recv.at[v_y + o - 1], v_send.at[v_y + o - 1])
        vadd(at_y, rows_y, [VY[o - 1] for o in range(1, n_y)])
        for o in range(1, n_x):
            to = turn(x, o, n_x)
            go(
                lambda o=o: vrows(V, at_y + turn(x, o, n_x) * rows_x, rows_x), VX.at[o - 1],
                vec, v_x + o - 1, here.to(x=to),
            )

    def vectors_z():
        for o in range(1, n_x):
            arrived(VX.at[o - 1], v_recv.at[v_x + o - 1], v_send.at[v_x + o - 1])
        vadd(at_x, rows_x, [VX[o - 1] for o in range(1, n_x)])
        for o in range(1, n_z):

            def make(o=o):
                at = at_x + turn(z, o, n_z) * rows_z if split_z > 1 else at_x
                return vrows(V, at, rows_z)

            go(make, VZ.at[z], vec, v_z + o - 1, here.to(z=turn(z, o, n_z)))

    def vectors_gather_z():
        for o in range(1, n_z):
            arrived(
                VZ.at[turn(z, n_z - o, n_z)], v_recv.at[v_z + o - 1], v_send.at[v_z + o - 1]
            )
        target = pl.ds(aligned(at_z, 8), rows_z)
        VZ[z] = V[target, :]
        total = VZ[0]
        for index in range(1, n_z):
            total = total + VZ[index]
        VF[target, :] = total
        if split_z > 1:
            for o in range(1, n_z):
                go(
                    lambda: vrows(VF, at_z, rows_z), vrows(VF, at_z, rows_z), vec, v_gz + o - 1,
                    here.to(z=turn(z, o, n_z)),
                )

    def vectors_gather_x():
        if split_z > 1:
            for o in range(1, n_z):
                came = turn(z, n_z - o, n_z)
                arrived(
                    vrows(VF, at_x + came * rows_z, rows_z), v_recv.at[v_gz + o - 1],
                    v_send.at[v_gz + o - 1],
                )
        for o in range(1, n_x):
            go(
                lambda: vrows(VF, at_x, rows_x), vrows(VF, at_x, rows_x), vec, v_gx + o - 1,
                here.to(x=turn(x, o, n_x)),
            )

    sq = ("q", q_send, q_recv)

    def squares_z():
        SQ[0] = square_sum[...]
        SQZ[z] = square_sum[...]
        for o in range(1, n_z):
            go(lambda: SQ.at[0], SQZ.at[z], sq, o - 1, here.to(z=turn(z, o, n_z)))

    def slot_of(i, j, k):
        return (i * n_y + j) * 2 + k

    def squares_plane():
        for o in range(1, n_z):
            arrived(SQZ.at[turn(z, n_z - o, n_z)], q_recv.at[o - 1], q_send.at[o - 1])
        total = SQZ[0]
        for index in range(1, n_z):
            total = total + SQZ[index]
        SQ[1] = total
        SQP[slot_of(x, y, c)] = total
        for index, step in enumerate(plane):
            go(
                lambda: SQ.at[1], SQP.at[slot_of(x, y, c)], sq, n_z - 1 + index,
                in_plane(step),
            )

    def squares_done():
        for index, (i, j, k) in enumerate(plane):
            slot = slot_of(
                turn(x, n_x - i, n_x), turn(y, n_y - j, n_y), lax.rem(c + k, 2)
            )
            arrived(SQP.at[slot], q_recv.at[n_z - 1 + index], q_send.at[n_z - 1 + index])
        total = SQP[0]
        for index in range(1, 2 * n_x * n_y):
            total = total + SQP[index]
        SQ[2] = total

    def vectors_gather_y():
        for o in range(1, n_x):
            at = at_y + turn(x, n_x - o, n_x) * rows_x
            arrived(vrows(VF, at, rows_x), v_recv.at[v_gx + o - 1], v_send.at[v_gx + o - 1])
        for o in range(1, n_y):
            go(
                lambda: vrows(VF, at_y, rows_y), vrows(VF, at_y, rows_y), vec, v_gy + o - 1,
                here.to(y=turn(y, o, n_y)),
            )

    def vectors_gather_core():
        for o in range(1, n_y):
            at = at_c + turn(y, n_y - o, n_y) * rows_y
            arrived(vrows(VF, at, rows_y), v_recv.at[v_gy + o - 1], v_send.at[v_gy + o - 1])
        go(lambda: vrows(VF, at_c, rows_c), vrows(VF, at_c, rows_c), vec, v_gc, mate)

    def vectors_done():
        arrived(vrows(VF, (1 - c) * rows_c, rows_c), v_recv.at[v_gc], v_send.at[v_gc])

    actions.update(
        vc=vectors_core, vy=vectors_y, vx=vectors_x, vz=vectors_z, vgz=vectors_gather_z,
        vgx=vectors_gather_x, vgy=vectors_gather_y, vgc=vectors_gather_core, vd=vectors_done,
        qz=squares_z, qp=squares_plane, qd=squares_done,
    )
    at_place("emb")
    low = DXB[...]
    for tile in range(2):
        made = mm_tn(pix[:, :, tile * D : (tile + 1) * D].reshape(ROWS, D), low).astype(BF)
        for piece in range(D // rows_patch):
            shard = tile * (D // rows_patch) + piece
            GS[1, shard // 2, shard % 2, 0:rows_patch, :] = made[piece * rows_patch : (piece + 1) * rows_patch]

    at_place("patch")
    ending = SCHEDULE["tail",]
    perform(ending[:-6])
    early = [
        key for key in sent
        if key[0] == "ag" or (key[0] == "rs" and key[1][0] not in (4, 5, 7))
    ]
    for key in early:
        source, send, recv, at = sent.pop(key)
        left_here(source(), recv.at[at], send.at[at])
    perform(ending[-6:])
    last_copies = [
        pltpu.make_async_copy(VF, vec_out, out_local.at[1 + CHUNKS + 2]),
        pltpu.make_async_copy(SQ.at[2], square_out, out_local.at[2 + CHUNKS + 2]),
    ]
    for copy in last_copies:
        copy.start()
    for source, send, recv, at in list(sent.values()):
        left_here(source(), recv.at[at], send.at[at])
    for k in range(CHUNKS + 2):
        result(k).wait()
    for copy in last_copies:
        copy.wait()

    @pl.when(jnp.logical_not(lower))
    def _():
        for index in range(2):
            left_here(given[index], img_recv.at[index], img_send.at[index])
        left_here(lab_given, img_recv.at[2], img_send.at[2])


def run_train(
    n_rep, n_shard, patches, patch_ends, labels, counts, own_patch, own_in, own_down, vecs, glob, pos, head
):
    n_x = 2 ** ((n_rep.bit_length() - 2) // 2)
    n_z, n_y = n_rep // n_x, n_shard // 2
    block = 4 * (D // n_shard)
    small_block = small_rows(block // 2, n_x, n_z)
    group = KEPT * n_shard
    keep = LAYERS - 1
    units = 1 + 3 * LAYERS
    chunks = CHUNKS + 2

    def buf(*shape, dtype=BF):
        return pltpu.VMEM(shape, dtype)

    def sems(*shape):
        return pltpu.SemaphoreType.DMA(shape)

    def reduction(count, slots, rows):
        by_x = cut(rows, n_x, 16)
        by_z = cut(rows // by_x, n_z, 16)
        return [
            buf(count, n_y, 2, rows, D),
            buf(slots, n_y, rows, D),
            buf(slots, n_y - 1, rows, D),
            buf(slots, n_x - 1 if by_x > 1 else n_x, rows // by_x, D),
            buf(slots, n_z, rows // by_x // by_z, D),
            buf(count, rows, D),
        ]

    rows_y = VEC_ROWS // 2 // n_y
    rows_x = rows_y // n_x
    rows_z = rows_x // cut(rows_x, n_z, 8)
    ag_count = n_y + (n_y - 1) * (n_x - 1) * 2 + n_y - 1
    rs_count = 1 + (n_y - 1) + 2 * (n_x - 1) + 2 * (n_z - 1)
    f_count = 1 + 2 * (n_y - 1) + (n_x - 1) + (n_z - 1) + 1
    v_count = 1 + 2 * (n_y - 1) + 2 * (n_x - 1) + 2 * (n_z - 1) + 1
    q_count = n_z - 1 + 2 * n_x * n_y - 1
    whole = pl.BlockSpec(memory_space=pltpu.VMEM)
    there = pl.BlockSpec(memory_space=pl.ANY)
    return pl.pallas_call(
        functools.partial(train, n_rep, n_shard),
        out_shape=[
            jax.ShapeDtypeStruct((CHUNKS, block, D), BF),
            jax.ShapeDtypeStruct((2, small_block, D), BF),
            jax.ShapeDtypeStruct((VEC_ROWS, VEC_WIDE), F32),
            jax.ShapeDtypeStruct((8, 128), F32),
            jax.ShapeDtypeStruct((2, n_y, n_x, n_z, group, WFAC // n_y), BF),
        ],
        in_specs=[there] * 2 + [pl.BlockSpec(memory_space=pltpu.SMEM)] * 2 + [there] * 3 + [whole] * 4,
        out_specs=[there] * 5,
        scratch_shapes=[
            buf(ROWS, D, dtype=F32),
            buf(LAYERS, ROWS, D),
            buf(LAYERS, ROWS, 128, dtype=F32),
            buf(keep, ROWS, 3 * D),
            buf(keep, ROWS, D),
            buf(keep, ROWS, D),
            buf(keep, ROWS, 128, dtype=F32),
            buf(keep, ROWS, FF),
            buf(keep, ROWS, FF),
            buf(ROWS, D),
            buf(ROWS, D),
            buf(ROWS, D),
            buf(ROWS, FF),
            buf(KEPT, BLK, PATCH_DIM),
            buf(2, 32, 128, dtype=F32),
            buf(32, 128, dtype=F32),
            buf(PATCH_DIM, D),
            buf(LAYERS, D, 4 * D + FF),
            buf(LAYERS, FF, D),
            buf(D, CPAD),
            buf(1, CPAD, dtype=F32),
            *reduction(CHUNKS, 3, block),
            *reduction(2, 1, small_block),
            buf(2, n_y, group, WFAC // n_y),
            buf(n_y, group, WFAC // n_y),
            buf(n_y - 1, group, WFAC // n_y),
            buf(VEC_ROWS, VEC_WIDE, dtype=F32),
            buf(VEC_ROWS // 2, VEC_WIDE, dtype=F32),
            buf(n_y - 1, rows_y, VEC_WIDE, dtype=F32),
            buf(n_x - 1, rows_x, VEC_WIDE, dtype=F32),
            buf(n_z, rows_z, VEC_WIDE, dtype=F32),
            buf(VEC_ROWS, VEC_WIDE, dtype=F32),
            buf(3, 8, 128, dtype=F32),
            buf(n_z, 8, 128, dtype=F32),
            buf(2 * n_x * n_y, 8, 128, dtype=F32),
            buf(8, 128, dtype=F32),
            sems(units, ag_count),
            sems(units, ag_count),
            sems(units, 4),
            sems(chunks, rs_count),
            sems(chunks, rs_count),
            sems(f_count),
            sems(f_count),
            sems(v_count),
            sems(v_count),
            sems(q_count),
            sems(q_count),
            sems(3),
            sems(3),
            sems(4),
            sems(3 + chunks),
        ],
        compiler_params=pltpu.CompilerParams(
            vmem_limit_bytes=65400 * 1024, collective_id=0, has_side_effects=True
        ),
        cost_estimate=pl.CostEstimate(
            flops=24_000_000_000, bytes_accessed=30_000_000, transcendentals=10_000_000
        ),
        name="train_step",
    )(patches, patch_ends, labels, counts, own_patch, own_in, own_down, vecs, glob, pos, head)


def adam(weight, first, second, grad, factor, rate):
    share = grad * factor
    first = BETA_FIRST * first + share
    square_scale = (1.0 - BETA_SECOND) / (1.0 - BETA_FIRST) ** 2
    second = BETA_SECOND * second + square_scale * (share * share)
    root_scale = (1.0 / (1.0 - BETA_SECOND**ADAM_STEP)) ** 0.5
    step_scale = rate / (1.0 - BETA_FIRST**ADAM_STEP) / root_scale
    bottom = second * lax.rsqrt(second) + ADAM_EPS / root_scale
    step = first * lax.rsqrt(bottom * bottom)
    return weight * (1.0 - rate * WEIGHT_DECAY) - step * step_scale, first, second


def update(n_rep, n_shard, *refs):
    res, small, vec, exchanged, factors = refs[0:5]
    sources = refs[5:26]
    loss_out, norm_out = refs[26:28]
    targets = refs[28:49]
    buffers = refs[49:70]
    results = refs[70:91]
    last_in, last_down, passing, grad_head, in_sems, out_sems = refs[91:]
    shard = lax.axis_index("shard")
    rows_in = D // n_shard
    rows_down = FF // n_shard
    keep = LAYERS - 1

    def moves(array, layer=None, out=False):
        found = []
        for kind in range(3):
            index = 3 * array + kind
            if out:
                src, dst, sem = results[index], targets[index], out_sems
            else:
                src, dst, sem = sources[index], buffers[index], in_sems
            slot = 0 if layer is None else layer
            if layer is not None:
                src, dst = src.at[layer], dst.at[layer]
            found.append(pltpu.make_async_copy(src, dst, sem.at[index, slot]))
        return found

    layered = [(1, layer) for layer in range(LAYERS)] + [(2, layer) for layer in range(LAYERS)]
    order = layered + [(0, None), (6, None), (5, None), (3, None), (4, None)]
    for array, layer in order:
        for move in moves(array, layer):
            move.start()

    n_rows = factors.shape[2] * factors.shape[3] * factors.shape[4]
    part_wide = factors.shape[5]

    def factor(half, at, size):
        found = []
        while size:
            part, column = divmod(at, part_wide)
            wide = min(size, part_wide - column)
            piece = factors[half, part, :, :, :, column : column + wide]
            found.append(piece.reshape(n_rows, wide))
            at, size = at + wide, size - wide
        return found[0] if len(found) == 1 else jnp.concatenate(found, axis=1)

    def squares(values):
        return fold(values * values)

    total = jnp.zeros((8, D), F32)
    own_rows = pl.multiple_of(shard * rows_in, 8)

    def keep_in(column, made):
        slot = column % 2
        passing[slot] = made
        last_in[:, column * D : (column + 1) * D] = passing[slot, pl.ds(own_rows, rows_in), :]

    h2 = factor(0, FF, D)
    for tile in range(4):
        made = mm_tn(h2, factor(1, tile * D, D))
        keep_in(4 + tile, made)
        total = total + squares(made)
    for tile in range(2):
        last_in[:, (1 + tile) * D : (2 + tile) * D] = small[
            0, tile * rows_in : (tile + 1) * rows_in, :
        ].astype(F32)
    made = mm_tn(factor(0, FF + 2 * D, D), factor(1, FF + D, D))
    keep_in(0, made)
    total = total + squares(made)
    made = mm_tn(factor(0, FF + D, D), factor(1, FF, D))
    keep_in(3, made)
    total = total + squares(made)
    d_top = factor(0, FF + 4 * D, D)
    per = min(rows_down, D)
    for tile in range(4):
        made = mm_tn(factor(0, tile * D, D), d_top)
        total = total + squares(made)
        for piece in range(D // per):
            owner, at = divmod(tile * D + piece * per, rows_down)

            def keep_down(made=made, piece=piece, at=at):
                last_down[at : at + per, :] = made[piece * per : (piece + 1) * per]

            pl.when(shard == owner)(keep_down)
    final = factor(0, FF + 3 * D, D)
    wide = jnp.zeros((8, 128), F32)
    for at in range(0, CPAD, 512):
        d_logits = factor(1, FF + 2 * D + at, 512)
        made = mm_tn(final, d_logits)
        grad_head[0:D, at : at + 512] = made
        bias = down_sum(d_logits.astype(F32))
        grad_head[D : D + 1, at : at + 512] = bias
        sums = squares(made)
        for lane in range(0, 512, 128):
            wide = wide + sums[:, lane : lane + 128]
            row = bias[:, lane : lane + 128]
            wide = wide + (row * row) * 0.125
    for lane in range(0, D, 128):
        wide = wide + total[:, lane : lane + 128]
    used = VEC_AT + 12 * LAYERS + 2
    parts = jnp.zeros((8, D), F32)
    kept_rows = lax.broadcasted_iota(jnp.int32, (8, 1), 0)
    for at in range(0, used, 8):
        value = vec[at : at + 8, 0:D]
        if at + 8 > used:
            value = jnp.where(kept_rows + at < used, value, 0.0)
        parts = parts + value * value
    patch_bias = down_sum(vec[0:PATCHES, 0:D])
    class_row = vec[CLS : CLS + 1, 0:D]
    rest = (patch_bias * patch_bias + class_row * class_row) * 0.125
    parts = parts + rest
    for lane in range(0, D, 128):
        wide = wide + parts[:, lane : lane + 128]
    wide = wide + exchanged[...]
    sum_squares = jnp.sum(jnp.sum(wide, axis=1, keepdims=True), axis=0, keepdims=True)
    inv_count = 1.0 / vec[used + 1 : used + 2, 0:1]
    grad_norm = jnp.sqrt(sum_squares) * inv_count
    norm_out[...] = grad_norm
    loss_out[...] = vec[used : used + 1, 0:1] * inv_count
    scale = jnp.minimum(1.0, CLIP_NORM / grad_norm) * inv_count * (1.0 - BETA_FIRST)

    def apply(array, where, grad, rate):
        refs = [buffers[3 * array + kind] for kind in range(3)]
        made = adam(refs[0][where], refs[1][where], refs[2][where], grad, scale, rate)
        for kind, value in enumerate(made):
            results[3 * array + kind][where] = value

    def begin(array, layer=None):
        for move in moves(array, layer):
            move.wait()

    def finish(array, layer=None):
        for move in moves(array, layer, out=True):
            move.start()

    def loop(count, body):
        def one(index, nothing):
            body(index)
            return nothing

        lax.fori_loop(0, count, one, 0)

    step = 32 if rows_in % 32 == 0 else 16
    for layer in range(LAYERS):
        begin(1, layer)

        def column_of(column):
            lanes = pl.ds(pl.multiple_of(column * D, 128), D)
            for at in range(0, rows_in, step):
                if layer < keep:
                    k = 3 * (keep - 1 - layer) + jnp.where(column < 4, 2, 1)
                    row = pl.multiple_of(lax.rem(column, 4) * rows_in + at, 16)
                    grad = res[k, pl.ds(row, step), :].astype(F32)
                else:
                    grad = last_in[at : at + step, lanes]
                apply(1, (layer, slice(at, at + step), lanes), grad, LEARNING_RATE)

        loop(8, column_of)
        finish(1, layer)
    for layer in range(LAYERS):
        begin(2, layer)

        def rows_of(index):
            for part in range(3):
                at = pl.multiple_of(index * 96 + part * 32, 16)
                if layer < keep:
                    grad = res[3 * (keep - 1 - layer), pl.ds(at, 32), :].astype(F32)
                else:
                    grad = last_down[pl.ds(at, 32), :]
                apply(2, (layer, pl.ds(at, 32), slice(0, D)), grad, LEARNING_RATE)

        loop(rows_down // 96, rows_of)
        finish(2, layer)
    begin(0)

    def patch_rows(index):
        for part in range(3):
            at = pl.multiple_of(index * 96 + part * 32, 16)
            grad = small[1, pl.ds(at, 32), :].astype(F32)
            apply(0, (pl.ds(at, 32), slice(0, D)), grad, LEARNING_RATE)

    loop(PATCH_DIM // n_shard // 96, patch_rows)
    finish(0)
    begin(6)

    def head_rows(index):
        for part in range(3):
            rows = pl.ds(pl.multiple_of(index * 48 + part * 16, 16), 16)
            apply(6, (rows, slice(0, NCLS)), grad_head[rows, 0:NCLS], LEARNING_RATE)

    loop(D // 48, head_rows)
    apply(6, (slice(D, D + 1), slice(0, NCLS)), grad_head[D : D + 1, 0:NCLS], LEARNING_RATE)
    finish(6)
    begin(5)
    apply(5, (slice(0, 1), slice(0, D)), class_row, VECTOR_RATE)
    for at in range(0, PATCHES, 28):
        apply(
            5, (slice(1 + at, 29 + at), slice(0, D)), vec[at : at + 28, 0:D], VECTOR_RATE
        )
    finish(5)
    begin(3)
    for layer in range(LAYERS):
        for piece in range(12):
            row = VEC_AT + 12 * layer + piece
            where = (slice(layer, layer + 1), slice(piece * D, (piece + 1) * D))
            apply(3, where, vec[row : row + 1, 0:D], VECTOR_RATE)
    finish(3)
    begin(4)
    rows = [patch_bias, class_row, vec[used - 2 : used - 1, 0:D], vec[used - 1 : used, 0:D]]
    for index, row in enumerate(rows):
        apply(4, (slice(index, index + 1), slice(0, D)), row, VECTOR_RATE)
    finish(4)
    for array, layer in order:
        for move in moves(array, layer, out=True):
            move.wait()


def run_update(n_rep, n_shard, res, small, vec, squares, factors, arrays):
    whole = pl.BlockSpec(memory_space=pltpu.VMEM)
    there = pl.BlockSpec(memory_space=pl.ANY)
    one = jax.ShapeDtypeStruct((1, 1), F32)
    made = pl.pallas_call(
        functools.partial(update, n_rep, n_shard),
        out_shape=[one, one] + [jax.ShapeDtypeStruct(a.shape, F32) for a in arrays],
        in_specs=[whole] * 5 + [there] * 21,
        out_specs=[whole] * 2 + [there] * 21,
        scratch_shapes=[pltpu.VMEM(a.shape, F32) for a in (*arrays, *arrays)]
        + [
            pltpu.VMEM((D // n_shard, 4 * D + FF), F32),
            pltpu.VMEM((FF // n_shard, D), F32),
            pltpu.VMEM((2, D, D), F32),
            pltpu.VMEM((D + 8, CPAD), F32),
            pltpu.SemaphoreType.DMA((21, LAYERS)),
            pltpu.SemaphoreType.DMA((21, LAYERS)),
        ],
        compiler_params=pltpu.CompilerParams(vmem_limit_bytes=62 * 1024 * 1024),
        cost_estimate=pl.CostEstimate(
            flops=200_000_000, bytes_accessed=50_000_000, transcendentals=4_000_000
        ),
        name="adamw",
    )(res, small, vec, squares, factors, *arrays)
    return made[0].reshape(()), made[1].reshape(()), made[2:]


def shards(
    n_rep, n_shard,
    patches, labels, counts, patch_w, layer_in, layer_down, layer_vecs, glob_vecs, pos_embed, head,
    m_patch, v_patch, m_in, v_in, m_down, v_down, m_vecs, v_vecs, m_glob, v_glob, m_pos, v_pos,
    m_head, v_head,
):
    ends = jnp.pad(patches[:, TAIL:], ((0, 0), (0, BLK - PATCHES), (0, 0)))
    res, small, vec, squares, factors = run_train(
        n_rep, n_shard, patches, ends, labels, counts, patch_w, layer_in, layer_down, layer_vecs,
        glob_vecs, pos_embed, head,
    )
    arrays = [
        patch_w, m_patch, v_patch, layer_in, m_in, v_in, layer_down, m_down, v_down,
        layer_vecs, m_vecs, v_vecs, glob_vecs, m_glob, v_glob, pos_embed, m_pos, v_pos,
        head, m_head, v_head,
    ]
    loss, grad_norm, new = run_update(n_rep, n_shard, res, small, vec, squares, factors, arrays)
    return (loss, grad_norm, *new)


def solution(mesh):
    everywhere = P()
    rows = P("shard", None)
    middle = P(None, "shard", None)
    return jax.shard_map(
        functools.partial(shards, mesh.shape["rep"], mesh.shape["shard"]),
        mesh=mesh,
        in_specs=(
            P(("rep", "shard"), None, None),
            P(("rep", "shard")),
            P(("rep", "shard")),
            rows,
            middle,
            middle,
            *(everywhere,) * 4,
            *(rows,) * 2,
            *(middle,) * 4,
            *(everywhere,) * 8,
        ),
        out_specs=(
            *(everywhere,) * 2,
            *(rows,) * 3,
            *(middle,) * 6,
            *(everywhere,) * 12,
        ),
        check_vma=False,
    )
```

```python
import functools

import jax
import jax.numpy as jnp
from jax import lax
from jax.experimental import pallas as pl
from jax.experimental.pallas import tpu as pltpu
from jax.sharding import PartitionSpec as P

D = 384
HEADS = 6
HEAD_DIM = 64
FF = 1536
PATCH_DIM = 768
PATCHES = 196
NCLS = 1000
LAYERS = 3
SEQ = 197

BLK = 208
CLS = 200
TAIL = 192
KEPT = 4
ROWS = KEPT * BLK
HALF = 2 * BLK
CROWS = KEPT * 16
CPAD = 1024
WIDE = 8 * D + FF

NORM_EPS = 1e-06
SMOOTHING = 0.1
CLIP_NORM = 0.05
LEARNING_RATE = 0.05
VECTOR_RATE = 0.5
BETA_FIRST = 0.9
BETA_SECOND = 0.999
ADAM_EPS = 1e-08
WEIGHT_DECAY = 0.05
ADAM_STEP = 10
GELU_SCALE = 0.7978845608028654
GELU_CUBIC = 0.044715

F32 = jnp.float32
BF = jnp.bfloat16


def mm(left, right):
    return jnp.dot(left, right, preferred_element_type=F32)


def mm_nt(left, right):
    return lax.dot_general(left, right, (((1,), (1,)), ((), ())), preferred_element_type=F32)


def mm_tn(left, right):
    return lax.dot_general(left, right, (((0,), (0,)), ((), ())), preferred_element_type=F32)


def fold(values):
    return jnp.sum(values.reshape(-1, 8, values.shape[-1]), axis=0)


def down_sum(values):
    return jnp.sum(values, axis=0, keepdims=True)


def norm(values):
    centre = values - jnp.mean(values, axis=-1, keepdims=True)
    inverse = lax.rsqrt(jnp.mean(centre * centre, axis=-1, keepdims=True) + NORM_EPS)
    return centre * inverse, inverse


def norm_back(upstream, normed, inverse, gain):
    scaled = upstream * gain
    first = jnp.mean(scaled, axis=-1, keepdims=True)
    second = jnp.mean(scaled * normed, axis=-1, keepdims=True)
    return inverse * (scaled - first - normed * second)


def gelu_parts(hidden):
    bent = hidden * (GELU_SCALE + (GELU_SCALE * GELU_CUBIC) * (hidden * hidden))
    tangent = jnp.tanh(bent)
    share = 0.5 + 0.5 * tangent
    slope = share + (1.0 - tangent * tangent) * (1.5 * bent - GELU_SCALE * hidden)
    return hidden * share, slope


def lane_mask(width, low, high):
    lane = lax.broadcasted_iota(jnp.int32, (1, width), 1)
    return jnp.where((lane >= low) & (lane < high), 1.0, 0.0).astype(BF)


STEP = 16


def pieces(total):
    return [(at, min(STEP, total - at)) for at in range(0, total, STEP)]


SCHEDULE = {
    ("cast", 0): ("ws0",),
    ("cast", 1): ("ws1",),
    ("cast", 2): ("ws2",),
    ("cast", 8): ("wf0", "ws3",),
    ("b_start",): ("wr0", "wf1", "ws4", "we0",),
    ("b_norm", 0, 0): ("wf2", "ws5", "wr1", "wf3", "ws6", "we1",),
    ("norm", 0, 0): ("wr2",),
    ("att", 0, 0, 0): ("wf4", "ws7",),
    ("att", 0, 0, 1): ("wr3",),
    ("b_up", 0, 0): ("we2",),
    ("up", 0, 0): ("wr4", "wf5", "ws8",),
    ("b_down", 0, 0): ("we3",),
    ("down", 0, 0): ("wf6", "ws9",),
    ("b_norm", 0, 1): ("we4",),
    ("att", 0, 1, 0): ("wr5", "wf7",),
    ("mid", 0, 1): ("wr6", "wf8",),
    ("b_up", 0, 1): ("we5",),
    ("b_down", 0, 1): ("we6",),
    ("down", 0, 1): ("wr7", "wf9",),
    ("norm", 1, 0): ("wr8",),
    ("mid", 1, 0): ("wr9",),
    ("b_last",): ("we7", "we8", "we9",),
    ("class",): ("fc",),
    ("kv",): ("core6",),
    ("lb", 0): ("fy",),
    ("round", 1): ("y6",),
    ("dn", 1): ("fz", "core0",),
    ("ups", 1): ("y0", "x6", "core1",),
    ("mlpb", 1, 0): ("fx",),
    ("out", 1): ("y1", "z6",),
    ("attb", 1, 2): ("x0", "gz6",),
    ("qkv", 1): ("core2",),
    ("fb", 1, 0): ("gx6",),
    ("fb", 1, 1): ("z0", "x1",),
    ("round", 0): ("y2",),
    ("dn", 0): ("gd6", "core3",),
    ("act", 0, 1): ("z1", "gz0",),
    ("mlpb", 0, 0): ("x2", "y3", "core4",),
    ("mlpb", 0, 1): ("gz1",),
    ("attb", 0, 0): ("gx0",),
    ("attb", 0, 1): ("z2",),
    ("attb", 0, 3): ("x3", "y4", "gx1", "gd0",),
    ("qkv", 0): ("gz2", "core5",),
    ("fb", 0, 1): ("z3",),
    ("emb",): ("vc",),
    ("patch",): ("gx2", "core7",),
    ("tail",): ("vy", "gd1", "x4", "y5", "y7", "fv", "gz3", "vx", "gd2", "z4", "gx3", "vz", "x5", "gz4", "gd3", "vgz", "x7", "z5", "gx4", "vgx", "z7", "gz5", "gd4", "vgy", "gz7", "qz", "fm", "gx5", "vgc", "gx7", "qp", "fd", "vd", "gd5", "gd7", "qd",),
}


WFAC = FF + 5 * D + 128
VEC_ROWS = 256
VEC_AT = BLK
VEC_WIDE = D
MESH = pl.DeviceIdType.MESH
CHUNKS = 6


class Place:
    def __init__(self, n_rep, n_shard):
        self.n_rep, self.n_shard = n_rep, n_shard
        self.n_x = 2 ** ((n_rep.bit_length() - 2) // 2)
        self.n_z = n_rep // self.n_x
        self.n_y = n_shard // 2
        rep, shard = lax.axis_index("rep"), lax.axis_index("shard")
        self.rep, self.shard = rep, shard
        self.z, self.x = rep // self.n_x, rep % self.n_x
        self.y, self.c = shard // 2, shard % 2

    def to(self, x=None, y=None, z=None, c=None):
        x = self.x if x is None else x
        y = self.y if y is None else y
        z = self.z if z is None else z
        c = self.c if c is None else c
        return {"rep": z * self.n_x + x, "shard": y * 2 + c}


def cut(rows, parts, unit):
    return parts if rows % (parts * unit) == 0 else 1


def small_rows(rows, n_x, n_z):
    unit = 16 * n_x * n_z
    padded = -(-rows // unit) * unit
    return padded if 2 * padded <= 3 * rows else rows


def aligned(value, unit):
    return pl.multiple_of(value, unit)


def train(
    n_rep, n_shard,
    patches, patch_ends, labels, counts, own_patch, own_in, own_down, vecs, glob, pos, head,
    res_out, small_out, vec_out, square_out, all_factors,
    X, N1, I1, QKV, ATT, N2, I2, ACT, SLOPE, DXB, DMB, DA, DH,
    pix, lab, lab_given, wp, win, wdn, low_head, head_bias,
    G, RC, RY, RX, RZ, RES, GS, SC, SY, SX, SZ, SRES,
    FAC, FC, FY, V, VC, VY, VX, VZ, VF, SQ, SQZ, SQP, square_sum,
    ag_send, ag_recv, ag_local, rs_send, rs_recv, f_send, f_recv, v_send, v_recv,
    q_send, q_recv,
    img_send, img_recv, img_local, out_local,
):
    here = Place(n_rep, n_shard)
    n_x, n_y, n_z = here.n_x, here.n_y, here.n_z
    x, y, z, c = here.x, here.y, here.z, here.c
    rows_in, rows_down, rows_patch = D // n_shard, FF // n_shard, PATCH_DIM // n_shard
    block = 4 * rows_in
    small_block = small_rows(block // 2, n_x, n_z)
    mate = here.to(c=1 - c)

    def push(src, dst, send, recv, device):
        pltpu.make_async_remote_copy(
            src_ref=src, dst_ref=dst, send_sem=send, recv_sem=recv,
            device_id=device, device_id_type=MESH,
        ).start()

    def arrived(dst, recv, send):
        pltpu.make_async_remote_copy(
            src_ref=dst, dst_ref=dst, send_sem=send, recv_sem=recv,
            device_id=mate, device_id_type=MESH,
        ).wait_recv()

    def left_here(src, recv, send):
        pltpu.make_async_remote_copy(
            src_ref=src, dst_ref=src, send_sem=send, recv_sem=recv,
            device_id=mate, device_id_type=MESH,
        ).wait_send()

    sent = {}

    def go(source, dst, sems, index, device):
        name, send, recv = sems
        push(source(), dst, send.at[index], recv.at[index], device)
        sent[name, index] = (source, send, recv, index)

    def gone(sems, index):
        source, send, recv, at = sent.pop((sems[0], index))
        left_here(source(), recv.at[at], send.at[at])

    def turn(at, by, size):
        return lax.rem(at + by, size)

    barrier = pltpu.get_barrier_semaphore()
    plane = [
        (i, j, k) for i in range(n_x) for j in range(n_y) for k in range(2) if i or j or k
    ]

    def in_plane(step):
        i, j, k = step
        return here.to(x=turn(x, i, n_x), y=turn(y, j, n_y), c=lax.rem(c + k, 2))

    others = [in_plane(step) for step in plane]
    others += [here.to(z=turn(z, o, n_z)) for o in range(1, n_z)]
    for other in others:
        pl.semaphore_signal(barrier, inc=1, device_id=other, device_id_type=MESH)
    pl.semaphore_wait(barrier, len(others))

    def weight(kind, layer, shard, part=None):
        if kind == "patch":
            parts = cut(rows_patch, n_x, 16)
            rows = rows_patch // parts
            if part is None:
                return wp.at[pl.ds(aligned(shard * rows_patch, 16), rows_patch), :]
            return wp.at[pl.ds(aligned(shard * rows_patch + part * rows, 16), rows), :]
        if kind == "down":
            parts = cut(rows_down, n_x, 16)
            rows = rows_down // parts
            if part is None:
                return wdn.at[layer, pl.ds(aligned(shard * rows_down, 16), rows_down), :]
            return wdn.at[layer, pl.ds(aligned(shard * rows_down + part * rows, 16), rows), :]
        base = 0 if kind == "attn" else 4 * D
        rows = pl.ds(aligned(shard * rows_in, 16), rows_in)
        if part is None:
            return win.at[layer, rows, pl.ds(base, 4 * D)]
        wide = 4 * D // n_x
        return win.at[layer, rows, pl.ds(aligned(base + part * wide, 128), wide)]

    units = [("patch", 0)] + [
        (kind, layer) for layer in range(LAYERS) for kind in ("attn", "up", "down")
    ]

    def parts_of(kind):
        if kind == "patch":
            return cut(rows_patch, n_x, 16)
        if kind == "down":
            return cut(rows_down, n_x, 16)
        return n_x

    ag = ("ag", ag_send, ag_recv)
    base_x = n_y
    base_my = base_x + (n_y - 1) * (n_x - 1)
    base_mx = base_my + (n_y - 1)

    stage = 4 * rows_in

    def weights_copies(unit):
        kind, layer = units[unit]
        base = (unit % 2) * stage
        if kind == "patch":
            pairs = [(own_patch, X.at[pl.ds(base, rows_patch)])]
        elif kind == "down":
            pairs = [(own_down.at[layer], X.at[pl.ds(base, rows_down)])]
        else:
            start = 0 if kind == "attn" else 4 * D
            pairs = [
                (
                    own_in.at[layer, :, pl.ds(start + tile * D, D)],
                    X.at[pl.ds(base + tile * rows_in, rows_in)],
                )
                for tile in range(4)
            ]
        return [
            pltpu.make_async_copy(src, dst, ag_local.at[unit, index])
            for index, (src, dst) in enumerate(pairs)
        ]

    def weights_cast(unit):
        kind, layer = units[unit]
        base = (unit % 2) * stage
        for copy in weights_copies(unit):
            copy.wait()
        if kind == "patch":
            rows = pl.ds(aligned(here.shard * rows_patch, 16), rows_patch)
            wp[rows, :] = X[base : base + rows_patch, :].astype(BF)
        elif kind == "down":
            rows = pl.ds(aligned(here.shard * rows_down, 16), rows_down)
            wdn[layer, rows, :] = X[base : base + rows_down, :].astype(BF)
        else:
            start = 0 if kind == "attn" else 4 * D
            rows = pl.ds(aligned(here.shard * rows_in, 16), rows_in)
            for tile in range(4):
                win[layer, rows, start + tile * D : start + (tile + 1) * D] = X[
                    base + tile * rows_in : base + (tile + 1) * rows_in, :
                ].astype(BF)
        if unit + 2 < len(units):
            for copy in weights_copies(unit + 2):
                copy.start()

    def weights_start(unit):
        kind, layer = units[unit]
        part = x if parts_of(kind) > 1 else 0
        for o in range(1, n_y):
            go(
                lambda: weight(kind, layer, here.shard, part),
                weight(kind, layer, here.shard, part), ag, (unit, o),
                here.to(y=turn(y, o, n_y)),
            )
        go(
            lambda: weight(kind, layer, here.shard), weight(kind, layer, here.shard), ag,
            (unit, 0), mate,
        )

    def weights_forward(unit):
        kind, layer = units[unit]
        split = parts_of(kind) > 1
        part = x if split else 0
        for o in range(1, n_y):
            def make(o=o):
                return weight(kind, layer, turn(y, n_y - o, n_y) * 2 + c, part)

            arrived(make(), ag_recv.at[unit, o], ag_send.at[unit, o])
            if split:
                for p in range(1, n_x):
                    index = base_x + (o - 1) * (n_x - 1) + p - 1
                    go(make, make(), ag, (unit, index), here.to(x=turn(x, p, n_x)))
            go(make, make(), ag, (unit, base_my + o - 1), mate)

    def weights_pass(unit):
        kind, layer = units[unit]
        split = parts_of(kind) > 1
        part = x if split else 0
        if split:
            for o in range(1, n_y):
                for p in range(1, n_x):
                    index = (o - 1) * (n_x - 1) + p - 1

                    def make(o=o, p=p):
                        shard = turn(y, n_y - o, n_y) * 2 + c
                        return weight(kind, layer, shard, turn(x, n_x - p, n_x))

                    arrived(
                        make(), ag_recv.at[unit, base_x + index], ag_send.at[unit, base_x + index]
                    )
                    go(make, make(), ag, (unit, base_mx + index), mate)

    def weights_whole(unit):
        kind, layer = units[unit]
        split = parts_of(kind) > 1
        part = x if split else 0
        arrived(weight(kind, layer, y * 2 + 1 - c), ag_recv.at[unit, 0], ag_send.at[unit, 0])
        for o in range(1, n_y):
            shard = turn(y, n_y - o, n_y) * 2 + 1 - c
            index = base_my + o - 1
            arrived(weight(kind, layer, shard, part), ag_recv.at[unit, index], ag_send.at[unit, index])
            if split:
                for p in range(1, n_x):
                    index = base_mx + (o - 1) * (n_x - 1) + p - 1
                    piece = weight(kind, layer, shard, turn(x, n_x - p, n_x))
                    arrived(piece, ag_recv.at[unit, index], ag_send.at[unit, index])

    actions = {}

    def perform(names):
        for name in names:
            actions[name]()

    def at_place(place, *indices):
        for key, names in SCHEDULE.items():
            if key[0] != place:
                continue
            held = None
            for index, value in zip(indices, key[1:], strict=True):
                if not isinstance(index, int):
                    same = index == value
                    held = same if held is None else jnp.logical_and(held, same)
                elif index != value:
                    break
            else:
                if held is None:
                    perform(names)
                else:
                    pl.when(held)(functools.partial(perform, names))

    for unit in range(len(units)):
        actions[f"ws{unit}"] = functools.partial(weights_start, unit)
        actions[f"wf{unit}"] = functools.partial(weights_forward, unit)
        actions[f"wr{unit}"] = functools.partial(weights_pass, unit)
        actions[f"we{unit}"] = functools.partial(weights_whole, unit)

    lower = here.rep < n_rep // 2
    partner = here.to(z=turn(z, n_z // 2, n_z))
    back_parts = (
        pix.at[pl.ds(2, 2), pl.ds(0, TAIL)], pix.at[pl.ds(2, 2), pl.ds(TAIL, BLK - TAIL)]
    )
    given = (patches.at[pl.ds(KEPT, 2), pl.ds(0, TAIL)], patch_ends.at[pl.ds(KEPT, 2)])

    def local_half(half):
        pair = pl.ds(2 * half, 2)
        return (
            pltpu.make_async_copy(
                patches.at[pair, pl.ds(0, TAIL)], pix.at[pair, pl.ds(0, TAIL)],
                img_local.at[half],
            ),
            pltpu.make_async_copy(
                patch_ends.at[pair], pix.at[pair, pl.ds(TAIL, BLK - TAIL)],
                img_local.at[2 + half],
            ),
        )

    def marks(pair):
        row = lax.broadcasted_iota(jnp.int32, (32, 128), 0)
        found = jnp.full((32, 128), -1.0, F32)
        for index in range(2):
            slot = 2 * pair + index
            value = jnp.where(slot < counts[0], labels[slot], -1).astype(F32)
            found = jnp.where(row == CLS - TAIL + 16 * index, value, found)
        return found

    for copy in local_half(0):
        copy.start()
    for unit in range(2):
        for copy in weights_copies(unit):
            copy.start()
    lab[0] = marks(0)
    lab_given[...] = marks(2)

    @pl.when(jnp.logical_not(lower))
    def _():
        for index in range(2):
            push(
                given[index], back_parts[index], img_send.at[index], img_recv.at[index],
                partner,
            )
        push(lab_given, lab.at[1], img_send.at[2], img_recv.at[2], partner)
        for copy in local_half(1):
            copy.start()
        lab[1] = marks(1)

    for unit in range(len(units)):
        weights_cast(unit)
        at_place("cast", unit)

    even = lane_mask(128, 0, 64)
    odd = lane_mask(128, 64, 128)
    low_lane = lax.broadcasted_iota(jnp.int32, (1, 128), 1) < 64
    key_lane = lax.broadcasted_iota(jnp.int32, (1, BLK), 1)
    key_row = jnp.where((key_lane < PATCHES) | (key_lane == CLS), 0.0, -1e30)
    key_sub = lax.broadcasted_iota(jnp.int32, (BLK, 1), 0)
    key_column = jnp.where((key_sub < PATCHES) | (key_sub == CLS), 0.0, -1e30)
    whole_lanes = NCLS // 128 * 128
    low_head[:, 0:whole_lanes] = head[0:D, 0:whole_lanes].astype(BF)
    low_head[:, whole_lanes:] = jnp.zeros((D, CPAD - whole_lanes), BF)
    low_head[:, whole_lanes:NCLS] = head[0:D, whole_lanes:NCLS].astype(BF)
    head_bias[...] = jnp.zeros((1, CPAD), F32)
    head_bias[:, 0:NCLS] = head[D : D + 1, :]
    V[...] = jnp.zeros((VEC_ROWS, VEC_WIDE), F32)
    square_sum[...] = jnp.zeros((8, 128), F32)
    if small_block > block // 2:
        spare = small_block - block // 2
        GS[:, :, :, block // 2 :, :] = jnp.zeros((2, n_y, 2, spare, D), BF)
    zeros = jnp.zeros((8, D), F32)
    patch_bias = glob[0:1, :]

    def whole_lanes_of(tile):
        return jnp.concatenate([tile] * (D // 128), axis=1)

    def vector(layer, at, size):
        return vecs[pl.ds(layer, 1), at : at + size]

    def store_vector(layer, at, row):
        for piece in range(row.shape[-1] // D):
            V[pl.ds(VEC_AT + 12 * layer + at // D + piece, 1), 0:D] = row[
                :, piece * D : (piece + 1) * D
            ]

    def store_sums(layer, parts):
        for at, part in parts:
            store_vector(layer, at, down_sum(part))

    def embed(half):
        made = mm(pix[pl.ds(2 * half, 2)].reshape(HALF, PATCH_DIM), wp[...])
        for image in range(2):
            start = aligned(half * HALF + image * BLK, 16)
            for at, size in pieces(PATCHES - 4):
                X[pl.ds(start + at, size), :] = (
                    made[image * BLK + at : image * BLK + at + size]
                    + pos[1 + at : 1 + at + size, :]
                    + patch_bias
                )
            X[pl.ds(start + TAIL, 16), :] = jnp.zeros((16, D), F32)
            X[pl.ds(start + TAIL, 4), :] = (
                made[image * BLK + TAIL : image * BLK + PATCHES]
                + pos[1 + TAIL : 1 + PATCHES, :]
                + patch_bias
            )
            X[pl.ds(start + CLS, 1), :] = glob[1:2, :] + pos[0:1, :]

    def first_norm(layer, half, columns):
        base = half * HALF
        gain, shift = vector(layer, 0, D), vector(layer, D, D)
        for at, size in pieces(HALF):
            rows = pl.ds(aligned(base + at, 16), size)
            normed, inverse = norm(X[rows, :])
            N1[layer, rows, :] = normed.astype(BF)
            I1[layer, rows, :] = jnp.broadcast_to(inverse, (size, 128))
            DXB[rows, :] = (normed * gain + shift).astype(BF)
        rows = pl.ds(aligned(base, 16), HALF)
        h1 = DXB[rows, :]
        if len(columns) == 3:
            made = mm(h1, win[layer, :, 0 : 2 * D])
            QKV[layer, rows, 0:D] = (made[:, 0:D] + vector(layer, 2 * D, D)).astype(BF)
            QKV[layer, rows, D : 2 * D] = made[:, D:].astype(BF)
            made = mm(h1, win[layer, :, 2 * D : 3 * D])
            QKV[layer, rows, 2 * D :] = (made + vector(layer, 3 * D, D)).astype(BF)
        else:
            made = mm(h1, win[layer, :, D : 3 * D])
            DMB[rows, :] = made[:, 0:D].astype(BF)
            DA[rows, :] = (made[:, D:] + vector(layer, 3 * D, D)).astype(BF)

    lanes = 256
    fill = jnp.zeros((lanes - BLK, 128), BF)
    ones = jnp.full((lanes, 128), 1.0, BF)
    wide_lane = lax.broadcasted_iota(jnp.int32, (1, lanes), 1)
    wide_key_row = jnp.where((wide_lane < PATCHES) | (wide_lane == CLS), 0.0, -1e30)

    def fill_up(values):
        return jnp.concatenate([jnp.concatenate([values, fill], axis=0), ones], axis=1)

    def attend(layer, image):
        rows = pl.ds(aligned(image * BLK, 16), BLK)
        for pair in range(3):
            at = pair * 128
            query = QKV[layer, rows, at : at + 128] * BF(0.125)
            keys = QKV[layer, rows, D + at : D + at + 128]
            values = QKV[layer, rows, 2 * D + at : 2 * D + at + 128]
            both = jnp.concatenate([query * even, query * odd], axis=0)
            scores = mm_nt(both, jnp.concatenate([keys, fill], axis=0))
            probs = []
            for row, size in pieces(HALF):
                part = scores[row : row + size] + wide_key_row
                probs.append(jnp.exp(part - jnp.max(part, axis=-1, keepdims=True)).astype(BF))
            probs = jnp.concatenate(probs, axis=0)
            first = mm(probs[:BLK], fill_up(values * even))
            second = mm(probs[BLK:], fill_up(values * odd))
            made = first[:, :128] * (1.0 / first[:, 128:])
            made = made + second[:, :128] * (1.0 / second[:, 128:])
            ATT[layer, rows, at : at + 128] = made.astype(BF)

    def mlp(layer, half):
        base = half * HALF
        whole = pl.ds(aligned(base, 16), HALF)
        made = mm(ATT[layer, whole, :], win[layer, :, 3 * D : 4 * D])
        bias_out = vector(layer, 4 * D, D)
        gain, shift = vector(layer, 5 * D, D), vector(layer, 6 * D, D)
        for at, size in pieces(HALF):
            rows = pl.ds(aligned(base + at, 16), size)
            middle = X[rows, :] + made[at : at + size] + bias_out
            X[rows, :] = middle
            normed, inverse = norm(middle)
            N2[layer, rows, :] = normed.astype(BF)
            I2[layer, rows, :] = jnp.broadcast_to(inverse, (size, 128))
            DXB[rows, :] = (normed * gain + shift).astype(BF)
        at_place("mid", half, layer)
        at_place("b_up", half, layer)
        h2 = DXB[whole, :]
        for pair in range(2):
            made = mm(h2, win[layer, :, (4 + 2 * pair) * D : (6 + 2 * pair) * D])
            for tile in range(2):
                start = (2 * pair + tile) * D
                columns = slice(start, start + D)
                bias = vector(layer, 7 * D + start, D)
                for at, size in pieces(HALF):
                    rows = pl.ds(aligned(base + at, 16), size)
                    active, slope = gelu_parts(
                        made[at : at + size, tile * D : (tile + 1) * D] + bias
                    )
                    ACT[layer, rows, columns] = active.astype(BF)
                    SLOPE[layer, rows, columns] = slope.astype(BF)
        at_place("up", half, layer)
        at_place("b_down", half, layer)
        made = mm(ACT[layer, whole, :], wdn[layer])
        bias = vector(layer, 7 * D + FF, D)
        for at, size in pieces(HALF):
            rows = pl.ds(aligned(base + at, 16), size)
            X[rows, :] = X[rows, :] + made[at : at + size] + bias
        at_place("down", half, layer)

    at_place("b_start")

    def forward_half(half, carry):
        @pl.when(half == 0)
        def _():
            for copy in local_half(0):
                copy.wait()

        @pl.when(jnp.logical_and(half == 1, lower))
        def _():
            for index in range(2):
                arrived(back_parts[index], img_recv.at[index], img_send.at[index])

        @pl.when(jnp.logical_and(half == 1, jnp.logical_not(lower)))
        def _():
            for copy in local_half(1):
                copy.wait()

        embed(half)
        at_place("embed", half)

        def forward_layer(layer, inner):
            at_place("b_norm", half, layer)
            first_norm(layer, half, (0, 1, 2))
            at_place("norm", half, layer)

            def attend_one(index, nothing):
                attend(layer, 2 * half + index)
                at_place("att", half, layer, index)
                return nothing

            lax.fori_loop(0, 2, attend_one, 0)
            mlp(layer, half)
            return inner

        return lax.fori_loop(0, LAYERS - 1, forward_layer, carry)

    lax.fori_loop(0, 2, forward_half, 0)
    at_place("b_last")

    last = LAYERS - 1

    def last_norm(half, nothing):
        first_norm(last, half, (1, 2))
        at_place("ln", half)
        return nothing

    lax.fori_loop(0, 2, last_norm, 0)

    fac = ("f", f_send, f_recv)
    f_y, f_z = 1, n_y
    f_x = f_z + n_z - 1
    f_v = f_x + n_x - 1
    f_m = f_v + n_y - 1
    part_wide = WFAC // n_y
    group = KEPT * n_shard

    def factors_core():
        go(lambda: FAC.at[1 - c], FC, fac, 0, mate)

    def factors_y():
        arrived(FC, f_recv.at[0], f_send.at[0])
        FAC[c] = FAC[c] + FC[...]
        for o in range(1, n_y):
            go(
                lambda o=o: FAC.at[c, turn(y, o, n_y)], FY.at[o - 1], fac, f_y + o - 1,
                here.to(y=turn(y, o, n_y)),
            )

    def line_factors(z_at, x_at):
        return all_factors.at[c, y, x_at, z_at]

    def factors_z():
        total = FAC[c, y]
        for o in range(1, n_y):
            arrived(FY.at[o - 1], f_recv.at[f_y + o - 1], f_send.at[f_y + o - 1])
            total = total + FY[o - 1]
        FC[0] = total
        pltpu.make_async_copy(FC.at[0], line_factors(z, x), out_local.at[0]).start()
        for o in range(1, n_z):
            go(
                lambda: FC.at[0], line_factors(z, x), fac, f_z + o - 1,
                here.to(z=turn(z, o, n_z)),
            )

    def factors_x():
        for o in range(1, n_z):
            index = f_z + o - 1
            arrived(line_factors(turn(z, n_z - o, n_z), x), f_recv.at[index], f_send.at[index])
        pltpu.make_async_copy(FC.at[0], line_factors(z, x), out_local.at[0]).wait()
        for o in range(1, n_x):
            go(
                lambda: all_factors.at[c, y, x], all_factors.at[c, y, x], fac, f_x + o - 1,
                here.to(x=turn(x, o, n_x)),
            )

    def factors_side():
        for o in range(1, n_x):
            index = f_x + o - 1
            came = all_factors.at[c, y, turn(x, n_x - o, n_x)]
            arrived(came, f_recv.at[index], f_send.at[index])
        for o in range(1, n_y):
            go(
                lambda: all_factors.at[c, y], all_factors.at[c, y], fac, f_v + o - 1,
                here.to(y=turn(y, o, n_y)),
            )

    def factors_mate():
        for o in range(1, n_y):
            index = f_v + o - 1
            came = all_factors.at[c, turn(y, n_y - o, n_y)]
            arrived(came, f_recv.at[index], f_send.at[index])
        go(lambda: all_factors.at[c], all_factors.at[c], fac, f_m, mate)

    def factors_done():
        arrived(all_factors.at[1 - c], f_recv.at[f_m], f_send.at[f_m])

    rs = ("rs", rs_send, rs_recv)
    r_y, r_x = 1, n_y
    r_z = r_x + n_x - 1
    r_gz = r_z + n_z - 1
    r_gx = r_gz + n_z - 1

    def chunk(k):
        if k < CHUNKS:
            slot = k % 3
            return (
                G.at[k], RC.at[slot], RY.at[slot], RX.at[slot], RZ.at[slot], RES.at[k], block
            )
        k = k - CHUNKS
        return GS.at[k], SC.at[0], SY.at[0], SX.at[0], SZ.at[0], SRES.at[k], small_block

    def splits(rows):
        by_x = cut(rows, n_x, 16)
        by_z = cut(rows // by_x, n_z, 16)
        return by_x, rows // by_x, by_z, rows // by_x // by_z

    def step_of(rows, most=192):
        return max(step for step in range(16, most + 1, 16) if rows % step == 0)

    def add_rows(rows, target, target_at, sources):
        step = step_of(rows)

        def one(index, nothing):
            at = index * step
            to = pl.ds(aligned(target_at + at, 16), step)
            total = target[to, :]
            if len(sources) == 1:
                total = total + sources[0][pl.ds(aligned(at, 16), step), :]
            else:
                total = total.astype(F32)
                for source in sources:
                    total = total + source[pl.ds(aligned(at, 16), step), :].astype(F32)
                total = total.astype(BF)
            target[to, :] = total
            return nothing

        lax.fori_loop(0, rows // step, one, 0)

    def reduce_core(k):
        g, rc = chunk(k)[0:2]
        go(lambda: chunk(k)[0].at[:, 1 - c], rc, rs, (k, 0), mate)

    def reduce_y(k):
        g, rc, ry, _, _, _, rows = chunk(k)
        arrived(rc, rs_recv.at[k, 0], rs_send.at[k, 0])
        for o in list(range(1, n_y)) + [0]:
            at = turn(y, o, n_y)
            add_rows(rows, g.at[at, c], 0, [rc.at[at]])
            if o:
                go(
                    lambda o=o: chunk(k)[0].at[turn(y, o, n_y), c], ry.at[o - 1], rs,
                    (k, r_y + o - 1), here.to(y=at),
                )

    def total_of(slots, count, at, step):
        total = None
        for index in range(count):
            value = slots[index, pl.ds(aligned(at, 16), step), :].astype(F32)
            total = value if total is None else total + value
        return total

    def reduce_x(k):
        g, _, ry, rx, _, _, rows = chunk(k)
        by_x, rows_x = splits(rows)[0:2]
        for o in range(1, n_y):
            arrived(ry.at[o - 1], rs_recv.at[k, r_y + o - 1], rs_send.at[k, r_y + o - 1])
        mine = g.at[y, c]
        add_rows(rows, mine, 0, [ry.at[o - 1] for o in range(1, n_y)])
        for o in range(1, n_x):
            to = turn(x, o, n_x)
            if by_x > 1:

                def make(o=o):
                    at = turn(x, o, n_x) * rows_x
                    return chunk(k)[0].at[y, c, pl.ds(aligned(at, 16), rows_x), :]

                go(make, rx.at[o - 1], rs, (k, r_x + o - 1), here.to(x=to))
            else:
                go(lambda: chunk(k)[0].at[y, c], rx.at[x], rs, (k, r_x + o - 1), here.to(x=to))

    def reduce_z(k):
        g, _, _, rx, rz, _, rows = chunk(k)
        by_x, rows_x, by_z, rows_z = splits(rows)
        mine = g.at[y, c]
        for o in range(1, n_x):
            slot = rx.at[o - 1] if by_x > 1 else rx.at[turn(x, n_x - o, n_x)]
            arrived(slot, rs_recv.at[k, r_x + o - 1], rs_send.at[k, r_x + o - 1])
        if by_x > 1:
            start = x * rows_x
            add_rows(rows_x, mine, start, [rx.at[o - 1] for o in range(1, n_x)])
        else:
            start = 0
            rx[x] = mine[...]
            for o in range(1, n_x):
                gone(rs, (k, r_x + o - 1))
            step = step_of(rows)

            def one(index, nothing):
                at = pl.ds(aligned(index * step, 16), step)
                g[y, c, at, :] = total_of(rx, n_x, index * step, step).astype(BF)
                return nothing

            lax.fori_loop(0, rows // step, one, 0)
        for o in range(1, n_z):

            def make(o=o):
                at = x * rows_x if by_x > 1 else 0
                if by_z > 1:
                    at = at + turn(z, o, n_z) * rows_z
                return chunk(k)[0].at[y, c, pl.ds(aligned(at, 16), rows_z), :]

            slot = rz.at[o - 1] if by_z > 1 else rz.at[z]
            go(make, slot, rs, (k, r_z + o - 1), here.to(z=turn(z, o, n_z)))

    def gather_z(k):
        g, _, _, _, rz, res, rows = chunk(k)
        by_x, rows_x, by_z, rows_z = splits(rows)
        start = x * rows_x if by_x > 1 else 0
        if by_z > 1:
            start = start + z * rows_z
        for o in range(1, n_z):
            slot = rz.at[o - 1] if by_z > 1 else rz.at[turn(z, n_z - o, n_z)]
            arrived(slot, rs_recv.at[k, r_z + o - 1], rs_send.at[k, r_z + o - 1])
        own_slot = n_z - 1 if by_z > 1 else z
        rz[own_slot] = g[y, c, pl.ds(aligned(start, 16), rows_z), :]
        share = 1.0 / ((1 if by_x > 1 else n_x) * (1 if by_z > 1 else n_z))
        step = step_of(rows_z, 96)

        def one(index, total):
            low = total_of(rz, n_z, index * step, step).astype(BF)
            res[pl.ds(aligned(start + index * step, 16), step), :] = low
            wide = low.astype(F32)
            return total + fold(wide * wide)

        total = lax.fori_loop(0, rows_z // step, one, zeros) * share
        for at in range(0, D, 128):
            square_sum[...] = square_sum[...] + total[:, at : at + 128]
        if by_z > 1:

            def make():
                at = x * rows_x if by_x > 1 else 0
                return chunk(k)[5].at[pl.ds(aligned(at + z * rows_z, 16), rows_z), :]

            for o in range(1, n_z):
                go(make, make(), rs, (k, r_gz + o - 1), here.to(z=turn(z, o, n_z)))

    def gather_x(k):
        res, rows = chunk(k)[5:7]
        by_x, rows_x, by_z, rows_z = splits(rows)
        if by_z > 1:
            for o in range(1, n_z):
                start = turn(z, n_z - o, n_z) * rows_z
                if by_x > 1:
                    start = start + x * rows_x
                arrived(
                    res.at[pl.ds(aligned(start, 16), rows_z), :],
                    rs_recv.at[k, r_gz + o - 1], rs_send.at[k, r_gz + o - 1],
                )
        if by_x > 1:

            def make():
                return chunk(k)[5].at[pl.ds(aligned(x * rows_x, 16), rows_x), :]

            for o in range(1, n_x):
                go(make, make(), rs, (k, r_gx + o - 1), here.to(x=turn(x, o, n_x)))

    def result(k):
        if k < CHUNKS:
            return pltpu.make_async_copy(RES.at[k], res_out.at[k], out_local.at[1 + k])
        return pltpu.make_async_copy(
            SRES.at[k - CHUNKS], small_out.at[k - CHUNKS], out_local.at[1 + k]
        )

    def gather_done(k):
        res, rows = chunk(k)[5:7]
        by_x, rows_x = splits(rows)[0:2]
        if by_x > 1:
            for o in range(1, n_x):
                start = turn(x, n_x - o, n_x) * rows_x
                arrived(
                    res.at[pl.ds(aligned(start, 16), rows_x), :],
                    rs_recv.at[k, r_gx + o - 1], rs_send.at[k, r_gx + o - 1],
                )
        result(k).start()

    for k in range(CHUNKS + 2):
        actions[f"core{k}"] = functools.partial(reduce_core, k)
        actions[f"y{k}"] = functools.partial(reduce_y, k)
        actions[f"x{k}"] = functools.partial(reduce_x, k)
        actions[f"z{k}"] = functools.partial(reduce_z, k)
        actions[f"gz{k}"] = functools.partial(gather_z, k)
        actions[f"gx{k}"] = functools.partial(gather_x, k)
        actions[f"gd{k}"] = functools.partial(gather_done, k)
    actions.update(
        fc=factors_core, fy=factors_y, fz=factors_z, fx=factors_x, fv=factors_side,
        fm=factors_mate, fd=factors_done,
    )

    def tails(ref, layer=None):
        found = []
        for image in range(KEPT):
            rows = slice(image * BLK + TAIL, (image + 1) * BLK)
            found.append(ref[rows, :] if layer is None else ref[layer, rows, :])
        return jnp.concatenate(found, axis=0)

    @pl.when(lower)
    def _():
        arrived(lab.at[1], img_recv.at[2], img_send.at[2])

    marked = lab[...].reshape(CROWS, 128)[:, 0:1]

    h1 = tails(DXB)
    stream = tails(X)
    query = ((mm(h1, win[last, :, 0:D]) + vector(last, 2 * D, D)).astype(BF)) * BF(0.125)
    head_masks = [lane_mask(D, index * 64, (index + 1) * 64) for index in range(HEADS)]

    def spread(values):
        return jnp.concatenate([values * mask for mask in head_masks], axis=0)

    def gather_heads(values):
        total = None
        for index in range(HEADS):
            part = values[index * 16 : (index + 1) * 16] * head_masks[index].astype(F32)
            total = part if total is None else total + part
        return total

    spread_queries, probabilities, outs = [], [], []
    for image in range(KEPT):
        rows = slice(image * BLK, (image + 1) * BLK)
        queries = spread(query[image * 16 : (image + 1) * 16])
        scores = mm_nt(queries, DMB[rows, :]) + key_row
        raw = jnp.exp(scores - jnp.max(scores, axis=-1, keepdims=True))
        probs = raw * (1.0 / jnp.sum(raw, axis=-1, keepdims=True))
        spread_queries.append(queries)
        probabilities.append(probs)
        outs.append(gather_heads(mm(probs.astype(BF), DA[rows, :])))
    attended = jnp.concatenate(outs, axis=0).astype(BF)
    middle = stream + mm(attended, win[last, :, 3 * D : 4 * D]) + vector(last, 4 * D, D)
    n2, i2 = norm(middle)
    h2 = (n2 * vector(last, 5 * D, D) + vector(last, 6 * D, D)).astype(BF)
    active, slope = gelu_parts(mm(h2, win[last, :, 4 * D :]) + vector(last, 7 * D, FF))
    active = active.astype(BF)
    top = middle + mm(active, wdn[last]) + vector(last, 7 * D + FF, D)
    gain_final = glob[2:3, :]
    nf, inf = norm(top)
    final = (nf * gain_final + glob[3:4, :]).astype(BF)
    class_lane = lax.broadcasted_iota(jnp.int32, (1, CPAD), 1)
    logits = mm(final, low_head[...]) + head_bias[...]
    logits = jnp.where(class_lane < NCLS, logits, -1e30)
    peak = jnp.max(logits, axis=-1, keepdims=True)
    shifted = logits - peak
    raw = jnp.exp(shifted)
    total = jnp.sum(raw, axis=-1, keepdims=True)
    alive = jnp.where(marked >= 0.0, 1.0, 0.0)
    target = jnp.where(class_lane.astype(F32) == marked, 1.0 - SMOOTHING, 0.0) + jnp.where(
        class_lane < NCLS, SMOOTHING / NCLS, 0.0
    )
    log_probs = jnp.where(class_lane < NCLS, shifted - jnp.log(total), 0.0)
    losses = -jnp.sum(target * log_probs, axis=-1, keepdims=True) * alive
    d_logits = ((raw * (1.0 / total) - target) * alive).astype(BF)
    d_final = mm_nt(d_logits, low_head[...])
    last_row = VEC_AT + 12 * LAYERS
    V[last_row : last_row + 1, 0:D] = down_sum(d_final * nf)
    V[last_row + 1 : last_row + 2, 0:D] = down_sum(d_final)
    V[last_row + 2 : last_row + 3, 0:128] = jnp.broadcast_to(down_sum(losses), (1, 128))
    V[last_row + 3 : last_row + 4, 0:128] = jnp.full((1, 128), counts[0].astype(F32), F32)
    d_top = norm_back(d_final, nf, inf, gain_final)
    low_top = d_top.astype(BF)
    store_vector(last, 7 * D + FF, down_sum(d_top))
    d_up = (mm_nt(low_top, wdn[last]) * slope).astype(BF)
    store_vector(last, 7 * D, down_sum(d_up.astype(F32)))
    d_h2 = mm_nt(d_up, win[last, :, 4 * D :])
    store_vector(last, 5 * D, down_sum(d_h2 * n2))
    store_vector(last, 6 * D, down_sum(d_h2))
    d_middle = d_top + norm_back(d_h2, n2, i2, vector(last, 5 * D, D))
    low_middle = d_middle.astype(BF)
    store_vector(last, 4 * D, down_sum(d_middle))
    d_heads = mm_nt(low_middle, win[last, :, 3 * D : 4 * D]).astype(BF)
    d_queries = []
    for image in range(KEPT):
        rows = slice(image * BLK, (image + 1) * BLK)
        ups = spread(d_heads[image * 16 : (image + 1) * 16])
        probs = probabilities[image]
        d_probs = mm_nt(ups, DA[rows, :])
        inner = jnp.sum(d_probs * probs, axis=-1, keepdims=True)
        d_scores = (probs * (d_probs - inner)).astype(BF)
        d_queries.append(gather_heads(mm(d_scores, DMB[rows, :])) * 0.125)
        DMB[rows, :] = mm_tn(d_scores, spread_queries[image]).astype(BF)
        DA[rows, :] = mm_tn(probs.astype(BF), ups).astype(BF)
    d_query = jnp.concatenate(d_queries, axis=0).astype(BF)
    store_vector(last, 2 * D, down_sum(d_query.astype(F32)))
    from_query = mm_nt(d_query, win[last, :, 0:D])

    pick_row = lax.broadcasted_iota(jnp.int32, (group, CROWS), 0)
    pick_lane = lax.broadcasted_iota(jnp.int32, (group, CROWS), 1)
    pick = jnp.where(
        ((pick_row - KEPT * here.shard) * 16 + (CLS - TAIL)) == pick_lane, 1.0, 0.0
    ).astype(BF)
    def keep_factors(half, pieces_of):
        at = 0
        for piece in pieces_of:
            made = None if piece is None else mm(pick, piece).astype(BF)
            for lane in range(0, WFAC - at if made is None else made.shape[-1], 128):
                part, column = divmod(at + lane, part_wide)
                FAC[half, part, :, column : column + 128] = (
                    jnp.zeros((group, 128), BF) if made is None else made[:, lane : lane + 128]
                )
            at += 0 if made is None else made.shape[-1]

    keep_factors(0, (active, h2, attended, h1, final, low_top, None))
    keep_factors(1, (d_up, low_middle, d_query, d_logits, None))
    at_place("class")

    turned = DXB[...].T
    for tile, grads in enumerate((DMB, DA)):
        made = mm(turned, grads[...]).astype(BF)
        for shard in range(n_shard):
            GS[0, shard // 2, shard % 2, tile * rows_in : (tile + 1) * rows_in, :] = made[
                shard * rows_in : (shard + 1) * rows_in
            ]
    at_place("kv")
    store_sums(last, [(3 * D, fold(DA[...].astype(F32)))])

    X[...] = jnp.zeros((ROWS, D), F32)
    gain = vector(last, 0, D)
    gain_sum, shift_sum = zeros, zeros
    for image in range(KEPT):
        rows = slice(image * BLK + TAIL, (image + 1) * BLK)
        part = from_query[image * 16 : (image + 1) * 16]
        normed = N1[last, rows, :].astype(F32)
        gain_sum = gain_sum + fold(part * normed)
        shift_sum = shift_sum + fold(part)
        X[rows, :] = d_middle[image * 16 : (image + 1) * 16] + norm_back(
            part, normed, whole_lanes_of(I1[last, rows, :]), gain
        )

    def first_back(layer, half, made, sums):
        base = half * HALF
        gain = vector(layer, 0, D)
        gain_sum, shift_sum = sums
        for at, size in pieces(HALF):
            rows = pl.ds(aligned(base + at, 16), size)
            part = made[at : at + size]
            normed = N1[layer, rows, :].astype(F32)
            inverse = whole_lanes_of(I1[layer, rows, :])
            gain_sum = gain_sum + fold(part * normed)
            shift_sum = shift_sum + fold(part)
            X[rows, :] = X[rows, :] + norm_back(part, normed, inverse, gain)
        return gain_sum, shift_sum

    def last_back(half, sums):
        rows = pl.ds(aligned(half * HALF, 16), HALF)
        made = mm_nt(DMB[rows, :], win[last, :, D : 2 * D])
        made = made + mm_nt(DA[rows, :], win[last, :, 2 * D : 3 * D])
        sums = first_back(last, half, made, sums)
        at_place("lb", half)
        return sums

    gain_sum, shift_sum = lax.fori_loop(0, 2, last_back, (gain_sum, shift_sum))
    store_sums(last, [(0, gain_sum), (D, shift_sum)])

    def round_up(half, total):
        for at, size in pieces(HALF):
            rows = pl.ds(aligned(half * HALF + at, 16), size)
            up = X[rows, :]
            DXB[rows, :] = up.astype(BF)
            total = total + fold(up)
        return total

    def act_back(layer, half, totals):
        base = half * HALF
        low = DXB[pl.ds(aligned(base, 16), HALF), :]
        ups = []
        for pair in range(2):
            made = mm_nt(low, wdn[layer, 2 * pair * D : 2 * (pair + 1) * D, :])
            for tile in range(2):
                start = (2 * pair + tile) * D
                columns = slice(start, start + D)
                total = totals[2 * pair + tile]
                for at, size in pieces(HALF):
                    rows = pl.ds(aligned(base + at, 16), size)
                    part = made[at : at + size, tile * D : (tile + 1) * D]
                    grad = (part * SLOPE[layer, rows, columns].astype(F32)).astype(BF)
                    DH[rows, columns] = grad
                    total = total + fold(grad.astype(F32))
                ups.append(total)
        return tuple(ups)

    def mlp_back(layer, half, sums):
        base = half * HALF
        whole = pl.ds(aligned(base, 16), HALF)
        gain_sum, shift_sum, bias_out = sums
        made = mm_nt(DH[whole, :], win[layer, :, 4 * D :])
        gain = vector(layer, 5 * D, D)
        for at, size in pieces(HALF):
            rows = pl.ds(aligned(base + at, 16), size)
            part = made[at : at + size]
            normed = N2[layer, rows, :].astype(F32)
            inverse = whole_lanes_of(I2[layer, rows, :])
            gain_sum = gain_sum + fold(part * normed)
            shift_sum = shift_sum + fold(part)
            grad = X[rows, :] + norm_back(part, normed, inverse, gain)
            X[rows, :] = grad
            DMB[rows, :] = grad.astype(BF)
            bias_out = bias_out + fold(grad)
        DA[whole, :] = mm_nt(DMB[whole, :], win[layer, :, 3 * D : 4 * D]).astype(BF)
        return gain_sum, shift_sum, bias_out

    def attend_back(layer, image):
        rows = pl.ds(aligned(image * BLK, 16), BLK)
        for pair in range(3):
            at = pair * 128
            query = QKV[layer, rows, at : at + 128] * BF(0.125)
            keys = QKV[layer, rows, D + at : D + at + 128]
            values = QKV[layer, rows, 2 * D + at : 2 * D + at + 128]
            ups = DA[rows, at : at + 128]
            keys_both = jnp.concatenate([keys * even, keys * odd], axis=0)
            values_both = jnp.concatenate([values * even, values * odd], axis=0)
            query = jnp.concatenate([query, fill], axis=0)
            ups = jnp.concatenate([ups, fill], axis=0)
            scores = mm_nt(keys_both, query)
            d_probs = mm_nt(values_both, ups)
            probs, d_scores = [], []
            for base in (0, BLK):
                low_probs, low_grads = [], []
                for first, end in ((0, 128), (128, lanes)):
                    part = jnp.concatenate(
                        [
                            scores[base : base + TAIL, first:end],
                            scores[base + TAIL : base + BLK, first:end] + key_column[TAIL:],
                        ],
                        axis=0,
                    )
                    raw = jnp.exp(part - jnp.max(part, axis=0, keepdims=True))
                    prob = raw * (1.0 / jnp.sum(raw, axis=0, keepdims=True))
                    grad = d_probs[base : base + BLK, first:end]
                    inner = jnp.sum(grad * prob, axis=0, keepdims=True)
                    low_grads.append((prob * (grad - inner)).astype(BF))
                    low_probs.append(prob.astype(BF))
                probs.append(jnp.concatenate(low_probs, axis=1))
                d_scores.append(jnp.concatenate(low_grads, axis=1))
            probs = jnp.concatenate(probs, axis=0)
            d_scores = jnp.concatenate(d_scores, axis=0)
            d_values = mm(probs, ups)
            d_keys = mm(d_scores, query)
            d_query = mm_tn(d_scores, keys_both)[:BLK] * 0.125
            DH[rows, at : at + 128] = d_query.astype(BF)
            DH[rows, D + at : D + at + 128] = jnp.where(
                low_lane, d_keys[:BLK], d_keys[BLK:]
            ).astype(BF)
            DH[rows, 2 * D + at : 2 * D + at + 128] = jnp.where(
                low_lane, d_values[:BLK], d_values[BLK:]
            ).astype(BF)

    def renew(ref, layer, at):
        gain, shift = vector(layer, at, D), vector(layer, at + D, D)

        def one(index, nothing):
            for at, size in pieces(BLK):
                rows = pl.ds(aligned(index * BLK + at, 16), size)
                DXB[rows, :] = (ref[layer, rows, :].astype(F32) * gain + shift).astype(BF)
            return nothing

        lax.fori_loop(0, KEPT, one, 0)
        return DXB[...].T

    def keep_in(k, tile, made):
        for shard in range(n_shard):
            G[k, shard // 2, shard % 2, tile * rows_in : (tile + 1) * rows_in, :] = made[
                shard * rows_in : (shard + 1) * rows_in
            ]

    def backward(step, carry):
        layer = LAYERS - 2 - step
        kd, ku, kq = 3 * step, 3 * step + 1, 3 * step + 2
        bias_down = lax.fori_loop(0, 2, round_up, zeros)
        at_place("round", layer)
        turned = DXB[...].T
        per = min(rows_down, D)
        for pair in range(2):
            start = 2 * pair * D
            wide = mm(turned, ACT[layer, :, start : start + 2 * D]).astype(BF)
            for tile in range(2):
                made = wide[:, tile * D : (tile + 1) * D].T
                for piece in range(D // per):
                    shard, at = divmod(start + tile * D + piece * per, rows_down)
                    G[kd, shard // 2, shard % 2, at : at + per, :] = made[
                        piece * per : (piece + 1) * per
                    ]
        at_place("dn", layer)

        def one(half, totals):
            totals = act_back(layer, half, totals)
            at_place("act", layer, half)
            return totals

        bias_up = lax.fori_loop(0, 2, one, (zeros,) * 4)
        turned = renew(N2, layer, 5 * D)
        for pair in range(2):
            made = mm(turned, DH[:, 2 * pair * D : 2 * (pair + 1) * D]).astype(BF)
            keep_in(ku, 2 * pair, made[:, :D])
            keep_in(ku, 2 * pair + 1, made[:, D:])
        at_place("ups", layer)

        def one_more(half, sums):
            sums = mlp_back(layer, half, sums)
            at_place("mlpb", layer, half)
            return sums

        gain_sum, shift_sum, bias_out = lax.fori_loop(0, 2, one_more, (zeros, zeros, zeros))
        store_sums(
            layer,
            [(7 * D + FF, bias_down), (5 * D, gain_sum), (6 * D, shift_sum), (4 * D, bias_out)]
            + [(7 * D + tile * D, bias_up[tile]) for tile in range(4)],
        )
        keep_in(kq, 3, mm(ATT[layer].T, DMB[...]).astype(BF))
        at_place("out", layer)

        def two(image, nothing):
            attend_back(layer, image)
            at_place("attb", layer, image)
            return nothing

        lax.fori_loop(0, KEPT, two, 0)
        turned = renew(N1, layer, 0)
        made = mm(turned, DH[:, 0 : 2 * D]).astype(BF)
        keep_in(kq, 0, made[:, :D])
        keep_in(kq, 1, made[:, D:])
        keep_in(kq, 2, mm(turned, DH[:, 2 * D : 3 * D]).astype(BF))
        at_place("qkv", layer)
        store_sums(
            layer,
            [
                (2 * D, fold(DH[:, 0:D].astype(F32))),
                (3 * D, fold(DH[:, 2 * D : 3 * D].astype(F32))),
            ],
        )

        def three(half, sums):
            rows = pl.ds(aligned(half * HALF, 16), HALF)
            made = mm_nt(DH[rows, 0 : 3 * D], win[layer, :, 0 : 3 * D])
            sums = first_back(layer, half, made, sums)
            at_place("fb", layer, half)
            return sums

        gain_sum, shift_sum = lax.fori_loop(0, 2, three, (zeros, zeros))
        store_sums(layer, [(0, gain_sum), (D, shift_sum)])
        return carry

    lax.fori_loop(0, LAYERS - 1, backward, 0)

    for at, size in pieces(BLK):
        total = None
        for image in range(KEPT):
            part = X[image * BLK + at : image * BLK + at + size, :]
            DXB[image * BLK + at : image * BLK + at + size, :] = part.astype(BF)
            total = part if total is None else total + part
        V[at : at + size, 0:D] = total

    vec = ("v", v_send, v_recv)
    v_y, v_x = 1, n_y
    v_z = v_x + n_x - 1
    v_gz = v_z + n_z - 1
    v_gx = v_gz + n_z - 1
    v_gy = v_gx + n_x - 1
    v_gc = v_gy + n_y - 1
    rows_c = VEC_ROWS // 2
    rows_y = rows_c // n_y
    rows_x = rows_y // n_x
    split_z = cut(rows_x, n_z, 8)
    rows_z = rows_x // split_z
    at_c = c * rows_c
    at_y = at_c + y * rows_y
    at_x = at_y + x * rows_x
    at_z = at_x + z * rows_z if split_z > 1 else at_x

    def vrows(ref, at, rows):
        return ref.at[pl.ds(aligned(at, 8), rows), :]

    def vadd(at, rows, sources):
        target = pl.ds(aligned(at, 8), rows)
        total = V[target, :]
        for source in sources:
            total = total + source
        V[target, :] = total

    def vectors_core():
        go(lambda: vrows(V, (1 - c) * rows_c, rows_c), VC, vec, 0, mate)

    def vectors_y():
        arrived(VC, v_recv.at[0], v_send.at[0])
        vadd(at_c, rows_c, [VC[...]])
        for o in range(1, n_y):
            to = turn(y, o, n_y)
            go(
                lambda o=o: vrows(V, at_c + turn(y, o, n_y) * rows_y, rows_y), VY.at[o - 1],
                vec, v_y + o - 1, here.to(y=to),
            )

    def vectors_x():
        for o in range(1, n_y):
            arrived(VY.at[o - 1], v_recv.at[v_y + o - 1], v_send.at[v_y + o - 1])
        vadd(at_y, rows_y, [VY[o - 1] for o in range(1, n_y)])
        for o in range(1, n_x):
            to = turn(x, o, n_x)
            go(
                lambda o=o: vrows(V, at_y + turn(x, o, n_x) * rows_x, rows_x), VX.at[o - 1],
                vec, v_x + o - 1, here.to(x=to),
            )

    def vectors_z():
        for o in range(1, n_x):
            arrived(VX.at[o - 1], v_recv.at[v_x + o - 1], v_send.at[v_x + o - 1])
        vadd(at_x, rows_x, [VX[o - 1] for o in range(1, n_x)])
        for o in range(1, n_z):

            def make(o=o):
                at = at_x + turn(z, o, n_z) * rows_z if split_z > 1 else at_x
                return vrows(V, at, rows_z)

            go(make, VZ.at[z], vec, v_z + o - 1, here.to(z=turn(z, o, n_z)))

    def vectors_gather_z():
        for o in range(1, n_z):
            arrived(
                VZ.at[turn(z, n_z - o, n_z)], v_recv.at[v_z + o - 1], v_send.at[v_z + o - 1]
            )
        target = pl.ds(aligned(at_z, 8), rows_z)
        VZ[z] = V[target, :]
        total = VZ[0]
        for index in range(1, n_z):
            total = total + VZ[index]
        VF[target, :] = total
        if split_z > 1:
            for o in range(1, n_z):
                go(
                    lambda: vrows(VF, at_z, rows_z), vrows(VF, at_z, rows_z), vec, v_gz + o - 1,
                    here.to(z=turn(z, o, n_z)),
                )

    def vectors_gather_x():
        if split_z > 1:
            for o in range(1, n_z):
                came = turn(z, n_z - o, n_z)
                arrived(
                    vrows(VF, at_x + came * rows_z, rows_z), v_recv.at[v_gz + o - 1],
                    v_send.at[v_gz + o - 1],
                )
        for o in range(1, n_x):
            go(
                lambda: vrows(VF, at_x, rows_x), vrows(VF, at_x, rows_x), vec, v_gx + o - 1,
                here.to(x=turn(x, o, n_x)),
            )

    sq = ("q", q_send, q_recv)

    def squares_z():
        SQ[0] = square_sum[...]
        SQZ[z] = square_sum[...]
        for o in range(1, n_z):
            go(lambda: SQ.at[0], SQZ.at[z], sq, o - 1, here.to(z=turn(z, o, n_z)))

    def slot_of(i, j, k):
        return (i * n_y + j) * 2 + k

    def squares_plane():
        for o in range(1, n_z):
            arrived(SQZ.at[turn(z, n_z - o, n_z)], q_recv.at[o - 1], q_send.at[o - 1])
        total = SQZ[0]
        for index in range(1, n_z):
            total = total + SQZ[index]
        SQ[1] = total
        SQP[slot_of(x, y, c)] = total
        for index, step in enumerate(plane):
            go(
                lambda: SQ.at[1], SQP.at[slot_of(x, y, c)], sq, n_z - 1 + index,
                in_plane(step),
            )

    def squares_done():
        for index, (i, j, k) in enumerate(plane):
            slot = slot_of(
                turn(x, n_x - i, n_x), turn(y, n_y - j, n_y), lax.rem(c + k, 2)
            )
            arrived(SQP.at[slot], q_recv.at[n_z - 1 + index], q_send.at[n_z - 1 + index])
        total = SQP[0]
        for index in range(1, 2 * n_x * n_y):
            total = total + SQP[index]
        SQ[2] = total

    def vectors_gather_y():
        for o in range(1, n_x):
            at = at_y + turn(x, n_x - o, n_x) * rows_x
            arrived(vrows(VF, at, rows_x), v_recv.at[v_gx + o - 1], v_send.at[v_gx + o - 1])
        for o in range(1, n_y):
            go(
                lambda: vrows(VF, at_y, rows_y), vrows(VF, at_y, rows_y), vec, v_gy + o - 1,
                here.to(y=turn(y, o, n_y)),
            )

    def vectors_gather_core():
        for o in range(1, n_y):
            at = at_c + turn(y, n_y - o, n_y) * rows_y
            arrived(vrows(VF, at, rows_y), v_recv.at[v_gy + o - 1], v_send.at[v_gy + o - 1])
        go(lambda: vrows(VF, at_c, rows_c), vrows(VF, at_c, rows_c), vec, v_gc, mate)

    def vectors_done():
        arrived(vrows(VF, (1 - c) * rows_c, rows_c), v_recv.at[v_gc], v_send.at[v_gc])

    actions.update(
        vc=vectors_core, vy=vectors_y, vx=vectors_x, vz=vectors_z, vgz=vectors_gather_z,
        vgx=vectors_gather_x, vgy=vectors_gather_y, vgc=vectors_gather_core, vd=vectors_done,
        qz=squares_z, qp=squares_plane, qd=squares_done,
    )
    at_place("emb")
    low = DXB[...]
    for tile in range(2):
        made = mm_tn(pix[:, :, tile * D : (tile + 1) * D].reshape(ROWS, D), low).astype(BF)
        for piece in range(D // rows_patch):
            shard = tile * (D // rows_patch) + piece
            GS[1, shard // 2, shard % 2, 0:rows_patch, :] = made[piece * rows_patch : (piece + 1) * rows_patch]

    at_place("patch")
    ending = SCHEDULE["tail",]
    perform(ending[:-6])
    early = [
        key for key in sent
        if key[0] == "ag" or (key[0] == "rs" and key[1][0] not in (4, 5, 7))
    ]
    for key in early:
        source, send, recv, at = sent.pop(key)
        left_here(source(), recv.at[at], send.at[at])
    perform(ending[-6:])
    last_copies = [
        pltpu.make_async_copy(VF, vec_out, out_local.at[1 + CHUNKS + 2]),
        pltpu.make_async_copy(SQ.at[2], square_out, out_local.at[2 + CHUNKS + 2]),
    ]
    for copy in last_copies:
        copy.start()
    for source, send, recv, at in list(sent.values()):
        left_here(source(), recv.at[at], send.at[at])
    for k in range(CHUNKS + 2):
        result(k).wait()
    for copy in last_copies:
        copy.wait()

    @pl.when(jnp.logical_not(lower))
    def _():
        for index in range(2):
            left_here(given[index], img_recv.at[index], img_send.at[index])
        left_here(lab_given, img_recv.at[2], img_send.at[2])


def run_train(
    n_rep, n_shard, patches, patch_ends, labels, counts, own_patch, own_in, own_down, vecs, glob, pos, head
):
    n_x = 2 ** ((n_rep.bit_length() - 2) // 2)
    n_z, n_y = n_rep // n_x, n_shard // 2
    block = 4 * (D // n_shard)
    small_block = small_rows(block // 2, n_x, n_z)
    group = KEPT * n_shard
    keep = LAYERS - 1
    units = 1 + 3 * LAYERS
    chunks = CHUNKS + 2

    def buf(*shape, dtype=BF):
        return pltpu.VMEM(shape, dtype)

    def sems(*shape):
        return pltpu.SemaphoreType.DMA(shape)

    def reduction(count, slots, rows):
        by_x = cut(rows, n_x, 16)
        by_z = cut(rows // by_x, n_z, 16)
        return [
            buf(count, n_y, 2, rows, D),
            buf(slots, n_y, rows, D),
            buf(slots, n_y - 1, rows, D),
            buf(slots, n_x - 1 if by_x > 1 else n_x, rows // by_x, D),
            buf(slots, n_z, rows // by_x // by_z, D),
            buf(count, rows, D),
        ]

    rows_y = VEC_ROWS // 2 // n_y
    rows_x = rows_y // n_x
    rows_z = rows_x // cut(rows_x, n_z, 8)
    ag_count = n_y + (n_y - 1) * (n_x - 1) * 2 + n_y - 1
    rs_count = 1 + (n_y - 1) + 2 * (n_x - 1) + 2 * (n_z - 1)
    f_count = 1 + 2 * (n_y - 1) + (n_x - 1) + (n_z - 1) + 1
    v_count = 1 + 2 * (n_y - 1) + 2 * (n_x - 1) + 2 * (n_z - 1) + 1
    q_count = n_z - 1 + 2 * n_x * n_y - 1
    whole = pl.BlockSpec(memory_space=pltpu.VMEM)
    there = pl.BlockSpec(memory_space=pl.ANY)
    return pl.pallas_call(
        functools.partial(train, n_rep, n_shard),
        out_shape=[
            jax.ShapeDtypeStruct((CHUNKS, block, D), BF),
            jax.ShapeDtypeStruct((2, small_block, D), BF),
            jax.ShapeDtypeStruct((VEC_ROWS, VEC_WIDE), F32),
            jax.ShapeDtypeStruct((8, 128), F32),
            jax.ShapeDtypeStruct((2, n_y, n_x, n_z, group, WFAC // n_y), BF),
        ],
        in_specs=[there] * 2 + [pl.BlockSpec(memory_space=pltpu.SMEM)] * 2 + [there] * 3 + [whole] * 4,
        out_specs=[there] * 5,
        scratch_shapes=[
            buf(ROWS, D, dtype=F32),
            buf(LAYERS, ROWS, D),
            buf(LAYERS, ROWS, 128, dtype=F32),
            buf(keep, ROWS, 3 * D),
            buf(keep, ROWS, D),
            buf(keep, ROWS, D),
            buf(keep, ROWS, 128, dtype=F32),
            buf(keep, ROWS, FF),
            buf(keep, ROWS, FF),
            buf(ROWS, D),
            buf(ROWS, D),
            buf(ROWS, D),
            buf(ROWS, FF),
            buf(KEPT, BLK, PATCH_DIM),
            buf(2, 32, 128, dtype=F32),
            buf(32, 128, dtype=F32),
            buf(PATCH_DIM, D),
            buf(LAYERS, D, 4 * D + FF),
            buf(LAYERS, FF, D),
            buf(D, CPAD),
            buf(1, CPAD, dtype=F32),
            *reduction(CHUNKS, 3, block),
            *reduction(2, 1, small_block),
            buf(2, n_y, group, WFAC // n_y),
            buf(n_y, group, WFAC // n_y),
            buf(n_y - 1, group, WFAC // n_y),
            buf(VEC_ROWS, VEC_WIDE, dtype=F32),
            buf(VEC_ROWS // 2, VEC_WIDE, dtype=F32),
            buf(n_y - 1, rows_y, VEC_WIDE, dtype=F32),
            buf(n_x - 1, rows_x, VEC_WIDE, dtype=F32),
            buf(n_z, rows_z, VEC_WIDE, dtype=F32),
            buf(VEC_ROWS, VEC_WIDE, dtype=F32),
            buf(3, 8, 128, dtype=F32),
            buf(n_z, 8, 128, dtype=F32),
            buf(2 * n_x * n_y, 8, 128, dtype=F32),
            buf(8, 128, dtype=F32),
            sems(units, ag_count),
            sems(units, ag_count),
            sems(units, 4),
            sems(chunks, rs_count),
            sems(chunks, rs_count),
            sems(f_count),
            sems(f_count),
            sems(v_count),
            sems(v_count),
            sems(q_count),
            sems(q_count),
            sems(3),
            sems(3),
            sems(4),
            sems(3 + chunks),
        ],
        compiler_params=pltpu.CompilerParams(
            vmem_limit_bytes=65400 * 1024, collective_id=0, has_side_effects=True
        ),
        cost_estimate=pl.CostEstimate(
            flops=24_000_000_000, bytes_accessed=30_000_000, transcendentals=10_000_000
        ),
        name="train_step",
    )(patches, patch_ends, labels, counts, own_patch, own_in, own_down, vecs, glob, pos, head)


def adam(weight, first, second, grad, factor, rate):
    share = grad * factor
    first = BETA_FIRST * first + share
    square_scale = (1.0 - BETA_SECOND) / (1.0 - BETA_FIRST) ** 2
    second = BETA_SECOND * second + square_scale * (share * share)
    root_scale = (1.0 / (1.0 - BETA_SECOND**ADAM_STEP)) ** 0.5
    step_scale = rate / (1.0 - BETA_FIRST**ADAM_STEP) / root_scale
    bottom = second * lax.rsqrt(second) + ADAM_EPS / root_scale
    step = first * lax.rsqrt(bottom * bottom)
    return weight * (1.0 - rate * WEIGHT_DECAY) - step * step_scale, first, second


def update(n_rep, n_shard, *refs):
    res_there, small_there, vec, exchanged, factors = refs[0:5]
    sources = refs[5:26]
    loss_out, norm_out = refs[26:28]
    targets = refs[28:49]
    buffers = refs[49:70]
    results = refs[70:91]
    last_in, last_down, passing, grad_head, res, small, in_sems, out_sems, grad_sems = refs[91:]
    shard = lax.axis_index("shard")
    rows_in = D // n_shard
    rows_down = FF // n_shard
    keep = LAYERS - 1

    def moves(array, layer=None, out=False):
        found = []
        for kind in range(3):
            index = 3 * array + kind
            if out:
                src, dst, sem = results[index], targets[index], out_sems
            else:
                src, dst, sem = sources[index], buffers[index], in_sems
            slot = 0 if layer is None else layer
            if layer is not None:
                src, dst = src.at[layer], dst.at[layer]
            found.append(pltpu.make_async_copy(src, dst, sem.at[index, slot]))
        return found

    layered = [(1, layer) for layer in range(LAYERS)] + [(2, layer) for layer in range(LAYERS)]
    order = [(4, None), (3, None), (5, None), (6, None)] + layered + [(0, None)]
    res_copy = pltpu.make_async_copy(res_there, res, grad_sems.at[0])
    small_copy = pltpu.make_async_copy(small_there, small, grad_sems.at[1])
    small_copy.start()
    for array, layer in order:
        for move in moves(array, layer):
            move.start()
        if array == 6:
            res_copy.start()

    n_rows = factors.shape[2] * factors.shape[3] * factors.shape[4]
    part_wide = factors.shape[5]

    def factor(half, at, size):
        found = []
        while size:
            part, column = divmod(at, part_wide)
            wide = min(size, part_wide - column)
            piece = factors[half, part, :, :, :, column : column + wide]
            found.append(piece.reshape(n_rows, wide))
            at, size = at + wide, size - wide
        return found[0] if len(found) == 1 else jnp.concatenate(found, axis=1)

    def squares(values):
        return fold(values * values)

    total = jnp.zeros((8, D), F32)
    own_rows = pl.multiple_of(shard * rows_in, 8)

    def keep_in(column, made):
        slot = column % 2
        passing[slot] = made
        last_in[:, column * D : (column + 1) * D] = passing[slot, pl.ds(own_rows, rows_in), :]

    h2 = factor(0, FF, D)
    for tile in range(4):
        made = mm_tn(h2, factor(1, tile * D, D))
        keep_in(4 + tile, made)
        total = total + squares(made)
    small_copy.wait()
    for tile in range(2):
        last_in[:, (1 + tile) * D : (2 + tile) * D] = small[
            0, tile * rows_in : (tile + 1) * rows_in, :
        ].astype(F32)
    made = mm_tn(factor(0, FF + 2 * D, D), factor(1, FF + D, D))
    keep_in(0, made)
    total = total + squares(made)
    made = mm_tn(factor(0, FF + D, D), factor(1, FF, D))
    keep_in(3, made)
    total = total + squares(made)
    d_top = factor(0, FF + 4 * D, D)
    per = min(rows_down, D)
    for tile in range(4):
        made = mm_tn(factor(0, tile * D, D), d_top)
        total = total + squares(made)
        for piece in range(D // per):
            owner, at = divmod(tile * D + piece * per, rows_down)

            def keep_down(made=made, piece=piece, at=at):
                last_down[at : at + per, :] = made[piece * per : (piece + 1) * per]

            pl.when(shard == owner)(keep_down)
    final = factor(0, FF + 3 * D, D)
    wide = jnp.zeros((8, 128), F32)
    for at in range(0, CPAD, 512):
        d_logits = factor(1, FF + 2 * D + at, 512)
        made = mm_tn(final, d_logits)
        grad_head[0:D, at : at + 512] = made
        bias = down_sum(d_logits.astype(F32))
        grad_head[D : D + 1, at : at + 512] = bias
        sums = squares(made)
        for lane in range(0, 512, 128):
            wide = wide + sums[:, lane : lane + 128]
            row = bias[:, lane : lane + 128]
            wide = wide + (row * row) * 0.125
    for lane in range(0, D, 128):
        wide = wide + total[:, lane : lane + 128]
    used = VEC_AT + 12 * LAYERS + 2
    parts = jnp.zeros((8, D), F32)
    kept_rows = lax.broadcasted_iota(jnp.int32, (8, 1), 0)
    for at in range(0, used, 8):
        value = vec[at : at + 8, 0:D]
        if at + 8 > used:
            value = jnp.where(kept_rows + at < used, value, 0.0)
        parts = parts + value * value
    patch_bias = down_sum(vec[0:PATCHES, 0:D])
    class_row = vec[CLS : CLS + 1, 0:D]
    rest = (patch_bias * patch_bias + class_row * class_row) * 0.125
    parts = parts + rest
    for lane in range(0, D, 128):
        wide = wide + parts[:, lane : lane + 128]
    wide = wide + exchanged[...]
    sum_squares = jnp.sum(jnp.sum(wide, axis=1, keepdims=True), axis=0, keepdims=True)
    inv_count = 1.0 / vec[used + 1 : used + 2, 0:1]
    grad_norm = jnp.sqrt(sum_squares) * inv_count
    norm_out[...] = grad_norm
    loss_out[...] = vec[used : used + 1, 0:1] * inv_count
    scale = jnp.minimum(1.0, CLIP_NORM / grad_norm) * inv_count * (1.0 - BETA_FIRST)

    def apply(array, where, grad, rate):
        refs = [buffers[3 * array + kind] for kind in range(3)]
        made = adam(refs[0][where], refs[1][where], refs[2][where], grad, scale, rate)
        for kind, value in enumerate(made):
            results[3 * array + kind][where] = value

    def begin(array, layer=None):
        for move in moves(array, layer):
            move.wait()

    def finish(array, layer=None):
        for move in moves(array, layer, out=True):
            move.start()

    def loop(count, body):
        def one(index, nothing):
            body(index)
            return nothing

        lax.fori_loop(0, count, one, 0)

    begin(4)
    rows = [patch_bias, class_row, vec[used - 2 : used - 1, 0:D], vec[used - 1 : used, 0:D]]
    for index, row in enumerate(rows):
        apply(4, (slice(index, index + 1), slice(0, D)), row, VECTOR_RATE)
    finish(4)
    begin(3)
    for layer in range(LAYERS):
        for piece in range(12):
            row = VEC_AT + 12 * layer + piece
            where = (slice(layer, layer + 1), slice(piece * D, (piece + 1) * D))
            apply(3, where, vec[row : row + 1, 0:D], VECTOR_RATE)
    finish(3)
    begin(5)
    apply(5, (slice(0, 1), slice(0, D)), class_row, VECTOR_RATE)
    for at in range(0, PATCHES, 28):
        apply(
            5, (slice(1 + at, 29 + at), slice(0, D)), vec[at : at + 28, 0:D], VECTOR_RATE
        )
    finish(5)
    begin(6)

    def head_rows(index):
        for part in range(3):
            rows = pl.ds(pl.multiple_of(index * 48 + part * 16, 16), 16)
            apply(6, (rows, slice(0, NCLS)), grad_head[rows, 0:NCLS], LEARNING_RATE)

    loop(D // 48, head_rows)
    apply(6, (slice(D, D + 1), slice(0, NCLS)), grad_head[D : D + 1, 0:NCLS], LEARNING_RATE)
    finish(6)
    res_copy.wait()
    step = 32 if rows_in % 32 == 0 else 16
    for layer in range(LAYERS):
        begin(1, layer)

        def column_of(column):
            lanes = pl.ds(pl.multiple_of(column * D, 128), D)
            for at in range(0, rows_in, step):
                if layer < keep:
                    k = 3 * (keep - 1 - layer) + jnp.where(column < 4, 2, 1)
                    row = pl.multiple_of(lax.rem(column, 4) * rows_in + at, 16)
                    grad = res[k, pl.ds(row, step), :].astype(F32)
                else:
                    grad = last_in[at : at + step, lanes]
                apply(1, (layer, slice(at, at + step), lanes), grad, LEARNING_RATE)

        loop(8, column_of)
        finish(1, layer)
    for layer in range(LAYERS):
        begin(2, layer)

        def rows_of(index):
            for part in range(3):
                at = pl.multiple_of(index * 96 + part * 32, 16)
                if layer < keep:
                    grad = res[3 * (keep - 1 - layer), pl.ds(at, 32), :].astype(F32)
                else:
                    grad = last_down[pl.ds(at, 32), :]
                apply(2, (layer, pl.ds(at, 32), slice(0, D)), grad, LEARNING_RATE)

        loop(rows_down // 96, rows_of)
        finish(2, layer)
    begin(0)

    def patch_rows(index):
        for part in range(3):
            at = pl.multiple_of(index * 96 + part * 32, 16)
            grad = small[1, pl.ds(at, 32), :].astype(F32)
            apply(0, (pl.ds(at, 32), slice(0, D)), grad, LEARNING_RATE)

    loop(PATCH_DIM // n_shard // 96, patch_rows)
    finish(0)
    for array, layer in order:
        for move in moves(array, layer, out=True):
            move.wait()


def run_update(n_rep, n_shard, res, small, vec, squares, factors, arrays):
    whole = pl.BlockSpec(memory_space=pltpu.VMEM)
    there = pl.BlockSpec(memory_space=pl.ANY)
    one = jax.ShapeDtypeStruct((1, 1), F32)
    made = pl.pallas_call(
        functools.partial(update, n_rep, n_shard),
        out_shape=[one, one] + [jax.ShapeDtypeStruct(a.shape, F32) for a in arrays],
        in_specs=[there] * 2 + [whole] * 3 + [there] * 21,
        out_specs=[whole] * 2 + [there] * 21,
        scratch_shapes=[pltpu.VMEM(a.shape, F32) for a in (*arrays, *arrays)]
        + [
            pltpu.VMEM((D // n_shard, 4 * D + FF), F32),
            pltpu.VMEM((FF // n_shard, D), F32),
            pltpu.VMEM((2, D, D), F32),
            pltpu.VMEM((D + 8, CPAD), F32),
            pltpu.VMEM(res.shape, BF),
            pltpu.VMEM(small.shape, BF),
            pltpu.SemaphoreType.DMA((21, LAYERS)),
            pltpu.SemaphoreType.DMA((21, LAYERS)),
            pltpu.SemaphoreType.DMA((2,)),
        ],
        compiler_params=pltpu.CompilerParams(vmem_limit_bytes=62 * 1024 * 1024),
        cost_estimate=pl.CostEstimate(
            flops=200_000_000, bytes_accessed=50_000_000, transcendentals=4_000_000
        ),
        name="adamw",
    )(res, small, vec, squares, factors, *arrays)
    return made[0].reshape(()), made[1].reshape(()), made[2:]


def shards(
    n_rep, n_shard,
    patches, labels, counts, patch_w, layer_in, layer_down, layer_vecs, glob_vecs, pos_embed, head,
    m_patch, v_patch, m_in, v_in, m_down, v_down, m_vecs, v_vecs, m_glob, v_glob, m_pos, v_pos,
    m_head, v_head,
):
    ends = jnp.pad(patches[:, TAIL:], ((0, 0), (0, BLK - PATCHES), (0, 0)))
    res, small, vec, squares, factors = run_train(
        n_rep, n_shard, patches, ends, labels, counts, patch_w, layer_in, layer_down, layer_vecs,
        glob_vecs, pos_embed, head,
    )
    arrays = [
        patch_w, m_patch, v_patch, layer_in, m_in, v_in, layer_down, m_down, v_down,
        layer_vecs, m_vecs, v_vecs, glob_vecs, m_glob, v_glob, pos_embed, m_pos, v_pos,
        head, m_head, v_head,
    ]
    loss, grad_norm, new = run_update(n_rep, n_shard, res, small, vec, squares, factors, arrays)
    return (loss, grad_norm, *new)


def solution(mesh):
    everywhere = P()
    rows = P("shard", None)
    middle = P(None, "shard", None)
    return jax.shard_map(
        functools.partial(shards, mesh.shape["rep"], mesh.shape["shard"]),
        mesh=mesh,
        in_specs=(
            P(("rep", "shard"), None, None),
            P(("rep", "shard")),
            P(("rep", "shard")),
            rows,
            middle,
            middle,
            *(everywhere,) * 4,
            *(rows,) * 2,
            *(middle,) * 4,
            *(everywhere,) * 8,
        ),
        out_specs=(
            *(everywhere,) * 2,
            *(rows,) * 3,
            *(middle,) * 6,
            *(everywhere,) * 12,
        ),
        check_vma=False,
    )
```

```python
import functools

import jax
import jax.numpy as jnp
from jax import lax
from jax.experimental import pallas as pl
from jax.experimental.pallas import tpu as pltpu
from jax.sharding import PartitionSpec as P

D = 384
HEADS = 6
HEAD_DIM = 64
FF = 1536
PATCH_DIM = 768
PATCHES = 196
NCLS = 1000
LAYERS = 3
SEQ = 197

BLK = 208
CLS = 200
TAIL = 192
KEPT = 4
ROWS = KEPT * BLK
HALF = 2 * BLK
CROWS = KEPT * 16
CPAD = 1024
WIDE = 8 * D + FF

NORM_EPS = 1e-06
SMOOTHING = 0.1
CLIP_NORM = 0.05
LEARNING_RATE = 0.05
VECTOR_RATE = 0.5
BETA_FIRST = 0.9
BETA_SECOND = 0.999
ADAM_EPS = 1e-08
WEIGHT_DECAY = 0.05
ADAM_STEP = 10
GELU_SCALE = 0.7978845608028654
GELU_CUBIC = 0.044715

F32 = jnp.float32
BF = jnp.bfloat16


def mm(left, right):
    return jnp.dot(left, right, preferred_element_type=F32)


def mm_nt(left, right):
    return lax.dot_general(left, right, (((1,), (1,)), ((), ())), preferred_element_type=F32)


def mm_tn(left, right):
    return lax.dot_general(left, right, (((0,), (0,)), ((), ())), preferred_element_type=F32)


def fold(values):
    return jnp.sum(values.reshape(-1, 8, values.shape[-1]), axis=0)


def down_sum(values):
    return jnp.sum(values, axis=0, keepdims=True)


def norm(values):
    centre = values - jnp.mean(values, axis=-1, keepdims=True)
    inverse = lax.rsqrt(jnp.mean(centre * centre, axis=-1, keepdims=True) + NORM_EPS)
    return centre * inverse, inverse


def norm_back(upstream, normed, inverse, gain):
    scaled = upstream * gain
    first = jnp.mean(scaled, axis=-1, keepdims=True)
    second = jnp.mean(scaled * normed, axis=-1, keepdims=True)
    return inverse * (scaled - first - normed * second)


def gelu_parts(hidden):
    bent = hidden * (GELU_SCALE + (GELU_SCALE * GELU_CUBIC) * (hidden * hidden))
    tangent = jnp.tanh(bent)
    share = 0.5 + 0.5 * tangent
    slope = share + (1.0 - tangent * tangent) * (1.5 * bent - GELU_SCALE * hidden)
    return hidden * share, slope


def lane_mask(width, low, high):
    lane = lax.broadcasted_iota(jnp.int32, (1, width), 1)
    return jnp.where((lane >= low) & (lane < high), 1.0, 0.0).astype(BF)


STEP = 16


def pieces(total):
    return [(at, min(STEP, total - at)) for at in range(0, total, STEP)]


SCHEDULE = {
    ("cast", 0): ("ws0",),
    ("cast", 1): ("ws1",),
    ("cast", 2): ("ws2",),
    ("cast", 8): ("wf0", "ws3",),
    ("b_start",): ("wr0", "wf1", "ws4", "we0",),
    ("b_norm", 0, 0): ("wf2", "ws5", "wr1", "wf3", "ws6", "we1",),
    ("norm", 0, 0): ("wr2",),
    ("att", 0, 0, 0): ("wf4", "ws7",),
    ("att", 0, 0, 1): ("wr3",),
    ("b_up", 0, 0): ("we2",),
    ("up", 0, 0): ("wr4", "wf5", "ws8",),
    ("b_down", 0, 0): ("we3",),
    ("down", 0, 0): ("wf6", "ws9",),
    ("b_norm", 0, 1): ("we4",),
    ("att", 0, 1, 0): ("wr5", "wf7",),
    ("mid", 0, 1): ("wr6", "wf8",),
    ("b_up", 0, 1): ("we5",),
    ("b_down", 0, 1): ("we6",),
    ("down", 0, 1): ("wr7", "wf9",),
    ("norm", 1, 0): ("wr8",),
    ("mid", 1, 0): ("wr9",),
    ("b_last",): ("we7", "we8", "we9",),
    ("class",): ("fc",),
    ("kv",): ("core6",),
    ("lb", 0): ("fy",),
    ("round", 1): ("y6",),
    ("dn", 1): ("fz", "core0",),
    ("ups", 1): ("y0", "x6", "core1",),
    ("mlpb", 1, 0): ("fx",),
    ("out", 1): ("y1", "z6",),
    ("attb", 1, 2): ("x0", "gz6",),
    ("qkv", 1): ("core2",),
    ("fb", 1, 0): ("gx6",),
    ("fb", 1, 1): ("z0", "x1",),
    ("round", 0): ("y2",),
    ("dn", 0): ("gd6", "core3",),
    ("act", 0, 1): ("z1", "gz0",),
    ("mlpb", 0, 0): ("x2", "y3", "core4",),
    ("mlpb", 0, 1): ("gz1",),
    ("attb", 0, 0): ("gx0",),
    ("attb", 0, 1): ("z2",),
    ("attb", 0, 3): ("x3", "y4", "gx1", "gd0",),
    ("qkv", 0): ("gz2", "core5",),
    ("fb", 0, 1): ("z3",),
    ("emb",): ("vc",),
    ("patch",): ("gx2", "core7",),
    ("tail",): ("vy", "gd1", "x4", "y5", "y7", "fv", "gz3", "vx", "gd2", "z4", "gx3", "vz", "x5", "gz4", "gd3", "vgz", "x7", "z5", "gx4", "vgx", "z7", "gz5", "gd4", "vgy", "gz7", "qz", "fm", "gx5", "vgc", "gx7", "qp", "fd", "vd", "gd5", "gd7", "qd",),
}


WFAC = FF + 5 * D + 128
VEC_ROWS = 256
VEC_AT = BLK
VEC_WIDE = D
MESH = pl.DeviceIdType.MESH
CHUNKS = 6


class Place:
    def __init__(self, n_rep, n_shard):
        self.n_rep, self.n_shard = n_rep, n_shard
        self.n_x = 2 ** ((n_rep.bit_length() - 2) // 2)
        self.n_z = n_rep // self.n_x
        self.n_y = n_shard // 2
        rep, shard = lax.axis_index("rep"), lax.axis_index("shard")
        self.rep, self.shard = rep, shard
        self.z, self.x = rep // self.n_x, rep % self.n_x
        self.y, self.c = shard // 2, shard % 2

    def to(self, x=None, y=None, z=None, c=None):
        x = self.x if x is None else x
        y = self.y if y is None else y
        z = self.z if z is None else z
        c = self.c if c is None else c
        return {"rep": z * self.n_x + x, "shard": y * 2 + c}


def cut(rows, parts, unit):
    return parts if rows % (parts * unit) == 0 else 1


def small_rows(rows, n_x, n_z):
    unit = 16 * n_x * n_z
    padded = -(-rows // unit) * unit
    return padded if 2 * padded <= 3 * rows else rows


def aligned(value, unit):
    return pl.multiple_of(value, unit)


def train(
    n_rep, n_shard,
    patches, patch_ends, labels, counts, own_patch, own_in, own_down, vecs, glob, pos, head,
    res_out, small_out, vec_out, square_out, all_factors,
    X, N1, I1, QKV, ATT, N2, I2, ACT, SLOPE, DXB, DMB, DA, DH,
    pix, lab, lab_given, wp, win, wdn, low_head, head_bias,
    G, RC, RY, RX, RZ, RES, GS, SC, SY, SX, SZ, SRES,
    FAC, FC, FY, V, VC, VY, VX, VZ, VF, SQ, SQZ, SQP, square_sum,
    ag_send, ag_recv, ag_local, rs_send, rs_recv, f_send, f_recv, v_send, v_recv,
    q_send, q_recv,
    img_send, img_recv, img_local, out_local,
):
    here = Place(n_rep, n_shard)
    n_x, n_y, n_z = here.n_x, here.n_y, here.n_z
    x, y, z, c = here.x, here.y, here.z, here.c
    rows_in, rows_down, rows_patch = D // n_shard, FF // n_shard, PATCH_DIM // n_shard
    block = 4 * rows_in
    small_block = small_rows(block // 2, n_x, n_z)
    mate = here.to(c=1 - c)

    def push(src, dst, send, recv, device):
        pltpu.make_async_remote_copy(
            src_ref=src, dst_ref=dst, send_sem=send, recv_sem=recv,
            device_id=device, device_id_type=MESH,
        ).start()

    def arrived(dst, recv, send):
        pltpu.make_async_remote_copy(
            src_ref=dst, dst_ref=dst, send_sem=send, recv_sem=recv,
            device_id=mate, device_id_type=MESH,
        ).wait_recv()

    def left_here(src, recv, send):
        pltpu.make_async_remote_copy(
            src_ref=src, dst_ref=src, send_sem=send, recv_sem=recv,
            device_id=mate, device_id_type=MESH,
        ).wait_send()

    sent = {}

    def go(source, dst, sems, index, device):
        name, send, recv = sems
        push(source(), dst, send.at[index], recv.at[index], device)
        sent[name, index] = (source, send, recv, index)

    def gone(sems, index):
        source, send, recv, at = sent.pop((sems[0], index))
        left_here(source(), recv.at[at], send.at[at])

    def turn(at, by, size):
        return lax.rem(at + by, size)

    barrier = pltpu.get_barrier_semaphore()
    plane = [
        (i, j, k) for i in range(n_x) for j in range(n_y) for k in range(2) if i or j or k
    ]

    def in_plane(step):
        i, j, k = step
        return here.to(x=turn(x, i, n_x), y=turn(y, j, n_y), c=lax.rem(c + k, 2))

    others = [in_plane(step) for step in plane]
    others += [here.to(z=turn(z, o, n_z)) for o in range(1, n_z)]
    for other in others:
        pl.semaphore_signal(barrier, inc=1, device_id=other, device_id_type=MESH)
    pl.semaphore_wait(barrier, len(others))

    def weight(kind, layer, shard, part=None):
        if kind == "patch":
            parts = cut(rows_patch, n_x, 16)
            rows = rows_patch // parts
            if part is None:
                return wp.at[pl.ds(aligned(shard * rows_patch, 16), rows_patch), :]
            return wp.at[pl.ds(aligned(shard * rows_patch + part * rows, 16), rows), :]
        if kind == "down":
            parts = cut(rows_down, n_x, 16)
            rows = rows_down // parts
            if part is None:
                return wdn.at[layer, pl.ds(aligned(shard * rows_down, 16), rows_down), :]
            return wdn.at[layer, pl.ds(aligned(shard * rows_down + part * rows, 16), rows), :]
        base = 0 if kind == "attn" else 4 * D
        rows = pl.ds(aligned(shard * rows_in, 16), rows_in)
        if part is None:
            return win.at[layer, rows, pl.ds(base, 4 * D)]
        wide = 4 * D // n_x
        return win.at[layer, rows, pl.ds(aligned(base + part * wide, 128), wide)]

    units = [("patch", 0)] + [
        (kind, layer) for layer in range(LAYERS) for kind in ("attn", "up", "down")
    ]

    def parts_of(kind):
        if kind == "patch":
            return cut(rows_patch, n_x, 16)
        if kind == "down":
            return cut(rows_down, n_x, 16)
        return n_x

    ag = ("ag", ag_send, ag_recv)
    base_x = n_y
    base_my = base_x + (n_y - 1) * (n_x - 1)
    base_mx = base_my + (n_y - 1)

    stage = 4 * rows_in

    def weights_copies(unit):
        kind, layer = units[unit]
        base = (unit % 2) * stage
        if kind == "patch":
            pairs = [(own_patch, X.at[pl.ds(base, rows_patch)])]
        elif kind == "down":
            pairs = [(own_down.at[layer], X.at[pl.ds(base, rows_down)])]
        else:
            start = 0 if kind == "attn" else 4 * D
            pairs = [
                (
                    own_in.at[layer, :, pl.ds(start + tile * D, D)],
                    X.at[pl.ds(base + tile * rows_in, rows_in)],
                )
                for tile in range(4)
            ]
        return [
            pltpu.make_async_copy(src, dst, ag_local.at[unit, index])
            for index, (src, dst) in enumerate(pairs)
        ]

    def weights_cast(unit):
        kind, layer = units[unit]
        base = (unit % 2) * stage
        for copy in weights_copies(unit):
            copy.wait()
        if kind == "patch":
            rows = pl.ds(aligned(here.shard * rows_patch, 16), rows_patch)
            wp[rows, :] = X[base : base + rows_patch, :].astype(BF)
        elif kind == "down":
            rows = pl.ds(aligned(here.shard * rows_down, 16), rows_down)
            wdn[layer, rows, :] = X[base : base + rows_down, :].astype(BF)
        else:
            start = 0 if kind == "attn" else 4 * D
            rows = pl.ds(aligned(here.shard * rows_in, 16), rows_in)
            for tile in range(4):
                win[layer, rows, start + tile * D : start + (tile + 1) * D] = X[
                    base + tile * rows_in : base + (tile + 1) * rows_in, :
                ].astype(BF)
        if unit + 2 < len(units):
            for copy in weights_copies(unit + 2):
                copy.start()

    def weights_start(unit):
        kind, layer = units[unit]
        part = x if parts_of(kind) > 1 else 0
        for o in range(1, n_y):
            go(
                lambda: weight(kind, layer, here.shard, part),
                weight(kind, layer, here.shard, part), ag, (unit, o),
                here.to(y=turn(y, o, n_y)),
            )
        go(
            lambda: weight(kind, layer, here.shard), weight(kind, layer, here.shard), ag,
            (unit, 0), mate,
        )

    def weights_forward(unit):
        kind, layer = units[unit]
        split = parts_of(kind) > 1
        part = x if split else 0
        for o in range(1, n_y):
            def make(o=o):
                return weight(kind, layer, turn(y, n_y - o, n_y) * 2 + c, part)

            arrived(make(), ag_recv.at[unit, o], ag_send.at[unit, o])
            if split:
                for p in range(1, n_x):
                    index = base_x + (o - 1) * (n_x - 1) + p - 1
                    go(make, make(), ag, (unit, index), here.to(x=turn(x, p, n_x)))
            go(make, make(), ag, (unit, base_my + o - 1), mate)

    def weights_pass(unit):
        kind, layer = units[unit]
        split = parts_of(kind) > 1
        part = x if split else 0
        if split:
            for o in range(1, n_y):
                for p in range(1, n_x):
                    index = (o - 1) * (n_x - 1) + p - 1

                    def make(o=o, p=p):
                        shard = turn(y, n_y - o, n_y) * 2 + c
                        return weight(kind, layer, shard, turn(x, n_x - p, n_x))

                    arrived(
                        make(), ag_recv.at[unit, base_x + index], ag_send.at[unit, base_x + index]
                    )
                    go(make, make(), ag, (unit, base_mx + index), mate)

    def weights_whole(unit):
        kind, layer = units[unit]
        split = parts_of(kind) > 1
        part = x if split else 0
        arrived(weight(kind, layer, y * 2 + 1 - c), ag_recv.at[unit, 0], ag_send.at[unit, 0])
        for o in range(1, n_y):
            shard = turn(y, n_y - o, n_y) * 2 + 1 - c
            index = base_my + o - 1
            arrived(weight(kind, layer, shard, part), ag_recv.at[unit, index], ag_send.at[unit, index])
            if split:
                for p in range(1, n_x):
                    index = base_mx + (o - 1) * (n_x - 1) + p - 1
                    piece = weight(kind, layer, shard, turn(x, n_x - p, n_x))
                    arrived(piece, ag_recv.at[unit, index], ag_send.at[unit, index])

    actions = {}

    def perform(names):
        for name in names:
            actions[name]()

    def at_place(place, *indices):
        for key, names in SCHEDULE.items():
            if key[0] != place:
                continue
            held = None
            for index, value in zip(indices, key[1:], strict=True):
                if not isinstance(index, int):
                    same = index == value
                    held = same if held is None else jnp.logical_and(held, same)
                elif index != value:
                    break
            else:
                if held is None:
                    perform(names)
                else:
                    pl.when(held)(functools.partial(perform, names))

    for unit in range(len(units)):
        actions[f"ws{unit}"] = functools.partial(weights_start, unit)
        actions[f"wf{unit}"] = functools.partial(weights_forward, unit)
        actions[f"wr{unit}"] = functools.partial(weights_pass, unit)
        actions[f"we{unit}"] = functools.partial(weights_whole, unit)

    lower = here.rep < n_rep // 2
    partner = here.to(z=turn(z, n_z // 2, n_z))
    back_parts = (
        pix.at[pl.ds(2, 2), pl.ds(0, TAIL)], pix.at[pl.ds(2, 2), pl.ds(TAIL, BLK - TAIL)]
    )
    given = (patches.at[pl.ds(KEPT, 2), pl.ds(0, TAIL)], patch_ends.at[pl.ds(KEPT, 2)])

    def local_half(half):
        pair = pl.ds(2 * half, 2)
        return (
            pltpu.make_async_copy(
                patches.at[pair, pl.ds(0, TAIL)], pix.at[pair, pl.ds(0, TAIL)],
                img_local.at[half],
            ),
            pltpu.make_async_copy(
                patch_ends.at[pair], pix.at[pair, pl.ds(TAIL, BLK - TAIL)],
                img_local.at[2 + half],
            ),
        )

    def marks(pair):
        row = lax.broadcasted_iota(jnp.int32, (32, 128), 0)
        found = jnp.full((32, 128), -1.0, F32)
        for index in range(2):
            slot = 2 * pair + index
            value = jnp.where(slot < counts[0], labels[slot], -1).astype(F32)
            found = jnp.where(row == CLS - TAIL + 16 * index, value, found)
        return found

    for copy in local_half(0):
        copy.start()
    for unit in range(2):
        for copy in weights_copies(unit):
            copy.start()
    lab[0] = marks(0)
    lab_given[...] = marks(2)

    @pl.when(jnp.logical_not(lower))
    def _():
        for index in range(2):
            push(
                given[index], back_parts[index], img_send.at[index], img_recv.at[index],
                partner,
            )
        push(lab_given, lab.at[1], img_send.at[2], img_recv.at[2], partner)
        for copy in local_half(1):
            copy.start()
        lab[1] = marks(1)

    for unit in range(len(units)):
        weights_cast(unit)
        at_place("cast", unit)

    even = lane_mask(128, 0, 64)
    odd = lane_mask(128, 64, 128)
    low_lane = lax.broadcasted_iota(jnp.int32, (1, 128), 1) < 64
    key_lane = lax.broadcasted_iota(jnp.int32, (1, BLK), 1)
    key_row = jnp.where((key_lane < PATCHES) | (key_lane == CLS), 0.0, -1e30)
    key_sub = lax.broadcasted_iota(jnp.int32, (BLK, 1), 0)
    key_column = jnp.where((key_sub < PATCHES) | (key_sub == CLS), 0.0, -1e30)
    whole_lanes = NCLS // 128 * 128
    low_head[:, 0:whole_lanes] = head[0:D, 0:whole_lanes].astype(BF)
    low_head[:, whole_lanes:] = jnp.zeros((D, CPAD - whole_lanes), BF)
    low_head[:, whole_lanes:NCLS] = head[0:D, whole_lanes:NCLS].astype(BF)
    head_bias[...] = jnp.zeros((1, CPAD), F32)
    head_bias[:, 0:NCLS] = head[D : D + 1, :]
    V[...] = jnp.zeros((VEC_ROWS, VEC_WIDE), F32)
    square_sum[...] = jnp.zeros((8, 128), F32)
    if small_block > block // 2:
        spare = small_block - block // 2
        GS[:, :, :, block // 2 :, :] = jnp.zeros((2, n_y, 2, spare, D), BF)
    zeros = jnp.zeros((8, D), F32)
    patch_bias = glob[0:1, :]

    def whole_lanes_of(tile):
        return jnp.concatenate([tile] * (D // 128), axis=1)

    def vector(layer, at, size):
        return vecs[pl.ds(layer, 1), at : at + size]

    def store_vector(layer, at, row):
        for piece in range(row.shape[-1] // D):
            V[pl.ds(VEC_AT + 12 * layer + at // D + piece, 1), 0:D] = row[
                :, piece * D : (piece + 1) * D
            ]

    def store_sums(layer, parts):
        for at, part in parts:
            store_vector(layer, at, down_sum(part))

    def embed(half):
        made = mm(pix[pl.ds(2 * half, 2)].reshape(HALF, PATCH_DIM), wp[...])
        for image in range(2):
            start = aligned(half * HALF + image * BLK, 16)
            for at, size in pieces(PATCHES - 4):
                X[pl.ds(start + at, size), :] = (
                    made[image * BLK + at : image * BLK + at + size]
                    + pos[1 + at : 1 + at + size, :]
                    + patch_bias
                )
            X[pl.ds(start + TAIL, 16), :] = jnp.zeros((16, D), F32)
            X[pl.ds(start + TAIL, 4), :] = (
                made[image * BLK + TAIL : image * BLK + PATCHES]
                + pos[1 + TAIL : 1 + PATCHES, :]
                + patch_bias
            )
            X[pl.ds(start + CLS, 1), :] = glob[1:2, :] + pos[0:1, :]

    def first_norm(layer, half, columns):
        base = half * HALF
        gain, shift = vector(layer, 0, D), vector(layer, D, D)
        for at, size in pieces(HALF):
            rows = pl.ds(aligned(base + at, 16), size)
            normed, inverse = norm(X[rows, :])
            N1[layer, rows, :] = normed.astype(BF)
            I1[layer, rows, :] = jnp.broadcast_to(inverse, (size, 128))
            DXB[rows, :] = (normed * gain + shift).astype(BF)
        rows = pl.ds(aligned(base, 16), HALF)
        h1 = DXB[rows, :]
        if len(columns) == 3:
            made = mm(h1, win[layer, :, 0 : 2 * D])
            QKV[layer, rows, 0:D] = (made[:, 0:D] + vector(layer, 2 * D, D)).astype(BF)
            QKV[layer, rows, D : 2 * D] = made[:, D:].astype(BF)
            made = mm(h1, win[layer, :, 2 * D : 3 * D])
            QKV[layer, rows, 2 * D :] = (made + vector(layer, 3 * D, D)).astype(BF)
        else:
            made = mm(h1, win[layer, :, D : 3 * D])
            DMB[rows, :] = made[:, 0:D].astype(BF)
            DA[rows, :] = (made[:, D:] + vector(layer, 3 * D, D)).astype(BF)

    lanes = 256
    fill = jnp.zeros((lanes - BLK, 128), BF)
    ones = jnp.full((lanes, 128), 1.0, BF)
    wide_lane = lax.broadcasted_iota(jnp.int32, (1, lanes), 1)
    wide_key_row = jnp.where((wide_lane < PATCHES) | (wide_lane == CLS), 0.0, -1e30)

    def fill_up(values):
        return jnp.concatenate([jnp.concatenate([values, fill], axis=0), ones], axis=1)

    def attend(layer, image):
        rows = pl.ds(aligned(image * BLK, 16), BLK)
        for pair in range(3):
            at = pair * 128
            query = QKV[layer, rows, at : at + 128] * BF(0.125)
            keys = QKV[layer, rows, D + at : D + at + 128]
            values = QKV[layer, rows, 2 * D + at : 2 * D + at + 128]
            both = jnp.concatenate([query * even, query * odd], axis=0)
            scores = mm_nt(both, jnp.concatenate([keys, fill], axis=0))
            probs = []
            for row, size in pieces(HALF):
                part = scores[row : row + size] + wide_key_row
                probs.append(jnp.exp(part - jnp.max(part, axis=-1, keepdims=True)).astype(BF))
            probs = jnp.concatenate(probs, axis=0)
            first = mm(probs[:BLK], fill_up(values * even))
            second = mm(probs[BLK:], fill_up(values * odd))
            made = first[:, :128] * (1.0 / first[:, 128:])
            made = made + second[:, :128] * (1.0 / second[:, 128:])
            ATT[layer, rows, at : at + 128] = made.astype(BF)

    def mlp(layer, half):
        base = half * HALF
        whole = pl.ds(aligned(base, 16), HALF)
        made = mm(ATT[layer, whole, :], win[layer, :, 3 * D : 4 * D])
        bias_out = vector(layer, 4 * D, D)
        gain, shift = vector(layer, 5 * D, D), vector(layer, 6 * D, D)
        for at, size in pieces(HALF):
            rows = pl.ds(aligned(base + at, 16), size)
            middle = X[rows, :] + made[at : at + size] + bias_out
            X[rows, :] = middle
            normed, inverse = norm(middle)
            N2[layer, rows, :] = normed.astype(BF)
            I2[layer, rows, :] = jnp.broadcast_to(inverse, (size, 128))
            DXB[rows, :] = (normed * gain + shift).astype(BF)
        at_place("mid", half, layer)
        at_place("b_up", half, layer)
        h2 = DXB[whole, :]
        for pair in range(2):
            made = mm(h2, win[layer, :, (4 + 2 * pair) * D : (6 + 2 * pair) * D])
            for tile in range(2):
                start = (2 * pair + tile) * D
                columns = slice(start, start + D)
                bias = vector(layer, 7 * D + start, D)
                for at, size in pieces(HALF):
                    rows = pl.ds(aligned(base + at, 16), size)
                    active, slope = gelu_parts(
                        made[at : at + size, tile * D : (tile + 1) * D] + bias
                    )
                    ACT[layer, rows, columns] = active.astype(BF)
                    SLOPE[layer, rows, columns] = slope.astype(BF)
        at_place("up", half, layer)
        at_place("b_down", half, layer)
        made = mm(ACT[layer, whole, :], wdn[layer])
        bias = vector(layer, 7 * D + FF, D)
        for at, size in pieces(HALF):
            rows = pl.ds(aligned(base + at, 16), size)
            X[rows, :] = X[rows, :] + made[at : at + size] + bias
        at_place("down", half, layer)

    at_place("b_start")

    def forward_half(half, carry):
        @pl.when(half == 0)
        def _():
            for copy in local_half(0):
                copy.wait()

        @pl.when(jnp.logical_and(half == 1, lower))
        def _():
            for index in range(2):
                arrived(back_parts[index], img_recv.at[index], img_send.at[index])

        @pl.when(jnp.logical_and(half == 1, jnp.logical_not(lower)))
        def _():
            for copy in local_half(1):
                copy.wait()

        embed(half)
        at_place("embed", half)

        def forward_layer(layer, inner):
            at_place("b_norm", half, layer)
            first_norm(layer, half, (0, 1, 2))
            at_place("norm", half, layer)

            def attend_one(index, nothing):
                attend(layer, 2 * half + index)
                at_place("att", half, layer, index)
                return nothing

            lax.fori_loop(0, 2, attend_one, 0)
            mlp(layer, half)
            return inner

        return lax.fori_loop(0, LAYERS - 1, forward_layer, carry)

    lax.fori_loop(0, 2, forward_half, 0)
    at_place("b_last")

    last = LAYERS - 1

    def last_norm(half, nothing):
        first_norm(last, half, (1, 2))
        at_place("ln", half)
        return nothing

    lax.fori_loop(0, 2, last_norm, 0)

    fac = ("f", f_send, f_recv)
    f_y, f_z = 1, n_y
    f_x = f_z + n_z - 1
    f_v = f_x + n_x - 1
    f_m = f_v + n_y - 1
    part_wide = WFAC // n_y
    group = KEPT * n_shard

    def factors_core():
        go(lambda: FAC.at[1 - c], FC, fac, 0, mate)

    def factors_y():
        arrived(FC, f_recv.at[0], f_send.at[0])
        FAC[c] = FAC[c] + FC[...]
        for o in range(1, n_y):
            go(
                lambda o=o: FAC.at[c, turn(y, o, n_y)], FY.at[o - 1], fac, f_y + o - 1,
                here.to(y=turn(y, o, n_y)),
            )

    def line_factors(z_at, x_at):
        return all_factors.at[c, y, x_at, z_at]

    def factors_z():
        total = FAC[c, y]
        for o in range(1, n_y):
            arrived(FY.at[o - 1], f_recv.at[f_y + o - 1], f_send.at[f_y + o - 1])
            total = total + FY[o - 1]
        FC[0] = total
        pltpu.make_async_copy(FC.at[0], line_factors(z, x), out_local.at[0]).start()
        for o in range(1, n_z):
            go(
                lambda: FC.at[0], line_factors(z, x), fac, f_z + o - 1,
                here.to(z=turn(z, o, n_z)),
            )

    def factors_x():
        for o in range(1, n_z):
            index = f_z + o - 1
            arrived(line_factors(turn(z, n_z - o, n_z), x), f_recv.at[index], f_send.at[index])
        pltpu.make_async_copy(FC.at[0], line_factors(z, x), out_local.at[0]).wait()
        for o in range(1, n_x):
            go(
                lambda: all_factors.at[c, y, x], all_factors.at[c, y, x], fac, f_x + o - 1,
                here.to(x=turn(x, o, n_x)),
            )

    def factors_side():
        for o in range(1, n_x):
            index = f_x + o - 1
            came = all_factors.at[c, y, turn(x, n_x - o, n_x)]
            arrived(came, f_recv.at[index], f_send.at[index])
        for o in range(1, n_y):
            go(
                lambda: all_factors.at[c, y], all_factors.at[c, y], fac, f_v + o - 1,
                here.to(y=turn(y, o, n_y)),
            )

    def factors_mate():
        for o in range(1, n_y):
            index = f_v + o - 1
            came = all_factors.at[c, turn(y, n_y - o, n_y)]
            arrived(came, f_recv.at[index], f_send.at[index])
        go(lambda: all_factors.at[c], all_factors.at[c], fac, f_m, mate)

    def factors_done():
        arrived(all_factors.at[1 - c], f_recv.at[f_m], f_send.at[f_m])

    rs = ("rs", rs_send, rs_recv)
    r_y, r_x = 1, n_y
    r_z = r_x + n_x - 1
    r_gz = r_z + n_z - 1
    r_gx = r_gz + n_z - 1

    def chunk(k):
        if k < CHUNKS:
            slot = k % 3
            return (
                G.at[k], RC.at[slot], RY.at[slot], RX.at[slot], RZ.at[slot], RES.at[k], block
            )
        k = k - CHUNKS
        return GS.at[k], SC.at[0], SY.at[0], SX.at[0], SZ.at[0], SRES.at[k], small_block

    def splits(rows):
        by_x = cut(rows, n_x, 16)
        by_z = cut(rows // by_x, n_z, 16)
        return by_x, rows // by_x, by_z, rows // by_x // by_z

    def step_of(rows, most=192):
        return max(step for step in range(16, most + 1, 16) if rows % step == 0)

    def add_rows(rows, target, target_at, sources):
        step = step_of(rows)

        def one(index, nothing):
            at = index * step
            to = pl.ds(aligned(target_at + at, 16), step)
            total = target[to, :]
            if len(sources) == 1:
                total = total + sources[0][pl.ds(aligned(at, 16), step), :]
            else:
                total = total.astype(F32)
                for source in sources:
                    total = total + source[pl.ds(aligned(at, 16), step), :].astype(F32)
                total = total.astype(BF)
            target[to, :] = total
            return nothing

        lax.fori_loop(0, rows // step, one, 0)

    def reduce_core(k):
        g, rc = chunk(k)[0:2]
        go(lambda: chunk(k)[0].at[:, 1 - c], rc, rs, (k, 0), mate)

    def reduce_y(k):
        g, rc, ry, _, _, _, rows = chunk(k)
        arrived(rc, rs_recv.at[k, 0], rs_send.at[k, 0])
        for o in list(range(1, n_y)) + [0]:
            at = turn(y, o, n_y)
            add_rows(rows, g.at[at, c], 0, [rc.at[at]])
            if o:
                go(
                    lambda o=o: chunk(k)[0].at[turn(y, o, n_y), c], ry.at[o - 1], rs,
                    (k, r_y + o - 1), here.to(y=at),
                )

    def total_of(slots, count, at, step):
        total = None
        for index in range(count):
            value = slots[index, pl.ds(aligned(at, 16), step), :].astype(F32)
            total = value if total is None else total + value
        return total

    def reduce_x(k):
        g, _, ry, rx, _, _, rows = chunk(k)
        by_x, rows_x = splits(rows)[0:2]
        for o in range(1, n_y):
            arrived(ry.at[o - 1], rs_recv.at[k, r_y + o - 1], rs_send.at[k, r_y + o - 1])
        mine = g.at[y, c]
        add_rows(rows, mine, 0, [ry.at[o - 1] for o in range(1, n_y)])
        for o in range(1, n_x):
            to = turn(x, o, n_x)
            if by_x > 1:

                def make(o=o):
                    at = turn(x, o, n_x) * rows_x
                    return chunk(k)[0].at[y, c, pl.ds(aligned(at, 16), rows_x), :]

                go(make, rx.at[o - 1], rs, (k, r_x + o - 1), here.to(x=to))
            else:
                go(lambda: chunk(k)[0].at[y, c], rx.at[x], rs, (k, r_x + o - 1), here.to(x=to))

    def reduce_z(k):
        g, _, _, rx, rz, _, rows = chunk(k)
        by_x, rows_x, by_z, rows_z = splits(rows)
        mine = g.at[y, c]
        for o in range(1, n_x):
            slot = rx.at[o - 1] if by_x > 1 else rx.at[turn(x, n_x - o, n_x)]
            arrived(slot, rs_recv.at[k, r_x + o - 1], rs_send.at[k, r_x + o - 1])
        if by_x > 1:
            start = x * rows_x
            add_rows(rows_x, mine, start, [rx.at[o - 1] for o in range(1, n_x)])
        else:
            start = 0
            rx[x] = mine[...]
            for o in range(1, n_x):
                gone(rs, (k, r_x + o - 1))
            step = step_of(rows)

            def one(index, nothing):
                at = pl.ds(aligned(index * step, 16), step)
                g[y, c, at, :] = total_of(rx, n_x, index * step, step).astype(BF)
                return nothing

            lax.fori_loop(0, rows // step, one, 0)
        for o in range(1, n_z):

            def make(o=o):
                at = x * rows_x if by_x > 1 else 0
                if by_z > 1:
                    at = at + turn(z, o, n_z) * rows_z
                return chunk(k)[0].at[y, c, pl.ds(aligned(at, 16), rows_z), :]

            slot = rz.at[o - 1] if by_z > 1 else rz.at[z]
            go(make, slot, rs, (k, r_z + o - 1), here.to(z=turn(z, o, n_z)))

    def gather_z(k):
        g, _, _, _, rz, res, rows = chunk(k)
        by_x, rows_x, by_z, rows_z = splits(rows)
        start = x * rows_x if by_x > 1 else 0
        if by_z > 1:
            start = start + z * rows_z
        for o in range(1, n_z):
            slot = rz.at[o - 1] if by_z > 1 else rz.at[turn(z, n_z - o, n_z)]
            arrived(slot, rs_recv.at[k, r_z + o - 1], rs_send.at[k, r_z + o - 1])
        own_slot = n_z - 1 if by_z > 1 else z
        rz[own_slot] = g[y, c, pl.ds(aligned(start, 16), rows_z), :]
        share = 1.0 / ((1 if by_x > 1 else n_x) * (1 if by_z > 1 else n_z))
        step = step_of(rows_z, 96)

        def one(index, total):
            low = total_of(rz, n_z, index * step, step).astype(BF)
            res[pl.ds(aligned(start + index * step, 16), step), :] = low
            wide = low.astype(F32)
            return total + fold(wide * wide)

        total = lax.fori_loop(0, rows_z // step, one, zeros) * share
        for at in range(0, D, 128):
            square_sum[...] = square_sum[...] + total[:, at : at + 128]
        if by_z > 1:

            def make():
                at = x * rows_x if by_x > 1 else 0
                return chunk(k)[5].at[pl.ds(aligned(at + z * rows_z, 16), rows_z), :]

            for o in range(1, n_z):
                go(make, make(), rs, (k, r_gz + o - 1), here.to(z=turn(z, o, n_z)))

    def gather_x(k):
        res, rows = chunk(k)[5:7]
        by_x, rows_x, by_z, rows_z = splits(rows)
        if by_z > 1:
            for o in range(1, n_z):
                start = turn(z, n_z - o, n_z) * rows_z
                if by_x > 1:
                    start = start + x * rows_x
                arrived(
                    res.at[pl.ds(aligned(start, 16), rows_z), :],
                    rs_recv.at[k, r_gz + o - 1], rs_send.at[k, r_gz + o - 1],
                )
        if by_x > 1:

            def make():
                return chunk(k)[5].at[pl.ds(aligned(x * rows_x, 16), rows_x), :]

            for o in range(1, n_x):
                go(make, make(), rs, (k, r_gx + o - 1), here.to(x=turn(x, o, n_x)))

    def result(k):
        if k < CHUNKS:
            return pltpu.make_async_copy(RES.at[k], res_out.at[k], out_local.at[1 + k])
        return pltpu.make_async_copy(
            SRES.at[k - CHUNKS], small_out.at[k - CHUNKS], out_local.at[1 + k]
        )

    def gather_done(k):
        res, rows = chunk(k)[5:7]
        by_x, rows_x = splits(rows)[0:2]
        if by_x > 1:
            for o in range(1, n_x):
                start = turn(x, n_x - o, n_x) * rows_x
                arrived(
                    res.at[pl.ds(aligned(start, 16), rows_x), :],
                    rs_recv.at[k, r_gx + o - 1], rs_send.at[k, r_gx + o - 1],
                )
        result(k).start()

    for k in range(CHUNKS + 2):
        actions[f"core{k}"] = functools.partial(reduce_core, k)
        actions[f"y{k}"] = functools.partial(reduce_y, k)
        actions[f"x{k}"] = functools.partial(reduce_x, k)
        actions[f"z{k}"] = functools.partial(reduce_z, k)
        actions[f"gz{k}"] = functools.partial(gather_z, k)
        actions[f"gx{k}"] = functools.partial(gather_x, k)
        actions[f"gd{k}"] = functools.partial(gather_done, k)
    actions.update(
        fc=factors_core, fy=factors_y, fz=factors_z, fx=factors_x, fv=factors_side,
        fm=factors_mate, fd=factors_done,
    )

    def tails(ref, layer=None):
        found = []
        for image in range(KEPT):
            rows = slice(image * BLK + TAIL, (image + 1) * BLK)
            found.append(ref[rows, :] if layer is None else ref[layer, rows, :])
        return jnp.concatenate(found, axis=0)

    @pl.when(lower)
    def _():
        arrived(lab.at[1], img_recv.at[2], img_send.at[2])

    marked = lab[...].reshape(CROWS, 128)[:, 0:1]

    h1 = tails(DXB)
    stream = tails(X)
    query = ((mm(h1, win[last, :, 0:D]) + vector(last, 2 * D, D)).astype(BF)) * BF(0.125)
    head_masks = [lane_mask(D, index * 64, (index + 1) * 64) for index in range(HEADS)]

    def spread(values):
        return jnp.concatenate([values * mask for mask in head_masks], axis=0)

    def gather_heads(values):
        total = None
        for index in range(HEADS):
            part = values[index * 16 : (index + 1) * 16] * head_masks[index].astype(F32)
            total = part if total is None else total + part
        return total

    spread_queries, probabilities, outs = [], [], []
    for image in range(KEPT):
        rows = slice(image * BLK, (image + 1) * BLK)
        queries = spread(query[image * 16 : (image + 1) * 16])
        scores = mm_nt(queries, DMB[rows, :]) + key_row
        raw = jnp.exp(scores - jnp.max(scores, axis=-1, keepdims=True))
        probs = raw * (1.0 / jnp.sum(raw, axis=-1, keepdims=True))
        spread_queries.append(queries)
        probabilities.append(probs)
        outs.append(gather_heads(mm(probs.astype(BF), DA[rows, :])))
    attended = jnp.concatenate(outs, axis=0).astype(BF)
    middle = stream + mm(attended, win[last, :, 3 * D : 4 * D]) + vector(last, 4 * D, D)
    n2, i2 = norm(middle)
    h2 = (n2 * vector(last, 5 * D, D) + vector(last, 6 * D, D)).astype(BF)
    active, slope = gelu_parts(mm(h2, win[last, :, 4 * D :]) + vector(last, 7 * D, FF))
    active = active.astype(BF)
    top = middle + mm(active, wdn[last]) + vector(last, 7 * D + FF, D)
    gain_final = glob[2:3, :]
    nf, inf = norm(top)
    final = (nf * gain_final + glob[3:4, :]).astype(BF)
    class_lane = lax.broadcasted_iota(jnp.int32, (1, CPAD), 1)
    logits = mm(final, low_head[...]) + head_bias[...]
    logits = jnp.where(class_lane < NCLS, logits, -1e30)
    peak = jnp.max(logits, axis=-1, keepdims=True)
    shifted = logits - peak
    raw = jnp.exp(shifted)
    total = jnp.sum(raw, axis=-1, keepdims=True)
    alive = jnp.where(marked >= 0.0, 1.0, 0.0)
    target = jnp.where(class_lane.astype(F32) == marked, 1.0 - SMOOTHING, 0.0) + jnp.where(
        class_lane < NCLS, SMOOTHING / NCLS, 0.0
    )
    log_probs = jnp.where(class_lane < NCLS, shifted - jnp.log(total), 0.0)
    losses = -jnp.sum(target * log_probs, axis=-1, keepdims=True) * alive
    d_logits = ((raw * (1.0 / total) - target) * alive).astype(BF)
    d_final = mm_nt(d_logits, low_head[...])
    last_row = VEC_AT + 12 * LAYERS
    V[last_row : last_row + 1, 0:D] = down_sum(d_final * nf)
    V[last_row + 1 : last_row + 2, 0:D] = down_sum(d_final)
    V[last_row + 2 : last_row + 3, 0:128] = jnp.broadcast_to(down_sum(losses), (1, 128))
    V[last_row + 3 : last_row + 4, 0:128] = jnp.full((1, 128), counts[0].astype(F32), F32)
    d_top = norm_back(d_final, nf, inf, gain_final)
    low_top = d_top.astype(BF)
    store_vector(last, 7 * D + FF, down_sum(d_top))
    d_up = (mm_nt(low_top, wdn[last]) * slope).astype(BF)
    store_vector(last, 7 * D, down_sum(d_up.astype(F32)))
    d_h2 = mm_nt(d_up, win[last, :, 4 * D :])
    store_vector(last, 5 * D, down_sum(d_h2 * n2))
    store_vector(last, 6 * D, down_sum(d_h2))
    d_middle = d_top + norm_back(d_h2, n2, i2, vector(last, 5 * D, D))
    low_middle = d_middle.astype(BF)
    store_vector(last, 4 * D, down_sum(d_middle))
    d_heads = mm_nt(low_middle, win[last, :, 3 * D : 4 * D]).astype(BF)
    d_queries = []
    for image in range(KEPT):
        rows = slice(image * BLK, (image + 1) * BLK)
        ups = spread(d_heads[image * 16 : (image + 1) * 16])
        probs = probabilities[image]
        d_probs = mm_nt(ups, DA[rows, :])
        inner = jnp.sum(d_probs * probs, axis=-1, keepdims=True)
        d_scores = (probs * (d_probs - inner)).astype(BF)
        d_queries.append(gather_heads(mm(d_scores, DMB[rows, :])) * 0.125)
        DMB[rows, :] = mm_tn(d_scores, spread_queries[image]).astype(BF)
        DA[rows, :] = mm_tn(probs.astype(BF), ups).astype(BF)
    d_query = jnp.concatenate(d_queries, axis=0).astype(BF)
    store_vector(last, 2 * D, down_sum(d_query.astype(F32)))
    from_query = mm_nt(d_query, win[last, :, 0:D])

    pick_row = lax.broadcasted_iota(jnp.int32, (group, CROWS), 0)
    pick_lane = lax.broadcasted_iota(jnp.int32, (group, CROWS), 1)
    pick = jnp.where(
        ((pick_row - KEPT * here.shard) * 16 + (CLS - TAIL)) == pick_lane, 1.0, 0.0
    ).astype(BF)
    def keep_factors(half, pieces_of):
        at = 0
        for piece in pieces_of:
            made = None if piece is None else mm(pick, piece).astype(BF)
            for lane in range(0, WFAC - at if made is None else made.shape[-1], 128):
                part, column = divmod(at + lane, part_wide)
                FAC[half, part, :, column : column + 128] = (
                    jnp.zeros((group, 128), BF) if made is None else made[:, lane : lane + 128]
                )
            at += 0 if made is None else made.shape[-1]

    keep_factors(0, (active, h2, attended, h1, final, low_top, None))
    keep_factors(1, (d_up, low_middle, d_query, d_logits, None))
    at_place("class")

    turned = DXB[...].T
    for tile, grads in enumerate((DMB, DA)):
        made = mm(turned, grads[...]).astype(BF)
        for shard in range(n_shard):
            GS[0, shard // 2, shard % 2, tile * rows_in : (tile + 1) * rows_in, :] = made[
                shard * rows_in : (shard + 1) * rows_in
            ]
    at_place("kv")
    store_sums(last, [(3 * D, fold(DA[...].astype(F32)))])

    X[...] = jnp.zeros((ROWS, D), F32)
    gain = vector(last, 0, D)
    gain_sum, shift_sum = zeros, zeros
    for image in range(KEPT):
        rows = slice(image * BLK + TAIL, (image + 1) * BLK)
        part = from_query[image * 16 : (image + 1) * 16]
        normed = N1[last, rows, :].astype(F32)
        gain_sum = gain_sum + fold(part * normed)
        shift_sum = shift_sum + fold(part)
        X[rows, :] = d_middle[image * 16 : (image + 1) * 16] + norm_back(
            part, normed, whole_lanes_of(I1[last, rows, :]), gain
        )

    def first_back(layer, half, made, sums):
        base = half * HALF
        gain = vector(layer, 0, D)
        gain_sum, shift_sum = sums
        for at, size in pieces(HALF):
            rows = pl.ds(aligned(base + at, 16), size)
            part = made[at : at + size]
            normed = N1[layer, rows, :].astype(F32)
            inverse = whole_lanes_of(I1[layer, rows, :])
            gain_sum = gain_sum + fold(part * normed)
            shift_sum = shift_sum + fold(part)
            X[rows, :] = X[rows, :] + norm_back(part, normed, inverse, gain)
        return gain_sum, shift_sum

    def last_back(half, sums):
        rows = pl.ds(aligned(half * HALF, 16), HALF)
        made = mm_nt(DMB[rows, :], win[last, :, D : 2 * D])
        made = made + mm_nt(DA[rows, :], win[last, :, 2 * D : 3 * D])
        sums = first_back(last, half, made, sums)
        at_place("lb", half)
        return sums

    gain_sum, shift_sum = lax.fori_loop(0, 2, last_back, (gain_sum, shift_sum))
    store_sums(last, [(0, gain_sum), (D, shift_sum)])

    def round_up(half, total):
        for at, size in pieces(HALF):
            rows = pl.ds(aligned(half * HALF + at, 16), size)
            up = X[rows, :]
            DXB[rows, :] = up.astype(BF)
            total = total + fold(up)
        return total

    def act_back(layer, half, totals):
        base = half * HALF
        low = DXB[pl.ds(aligned(base, 16), HALF), :]
        ups = []
        for pair in range(2):
            made = mm_nt(low, wdn[layer, 2 * pair * D : 2 * (pair + 1) * D, :])
            for tile in range(2):
                start = (2 * pair + tile) * D
                columns = slice(start, start + D)
                total = totals[2 * pair + tile]
                for at, size in pieces(HALF):
                    rows = pl.ds(aligned(base + at, 16), size)
                    part = made[at : at + size, tile * D : (tile + 1) * D]
                    grad = (part * SLOPE[layer, rows, columns].astype(F32)).astype(BF)
                    DH[rows, columns] = grad
                    total = total + fold(grad.astype(F32))
                ups.append(total)
        return tuple(ups)

    def mlp_back(layer, half, sums):
        base = half * HALF
        whole = pl.ds(aligned(base, 16), HALF)
        gain_sum, shift_sum, bias_out = sums
        made = mm_nt(DH[whole, :], win[layer, :, 4 * D :])
        gain = vector(layer, 5 * D, D)
        for at, size in pieces(HALF):
            rows = pl.ds(aligned(base + at, 16), size)
            part = made[at : at + size]
            normed = N2[layer, rows, :].astype(F32)
            inverse = whole_lanes_of(I2[layer, rows, :])
            gain_sum = gain_sum + fold(part * normed)
            shift_sum = shift_sum + fold(part)
            grad = X[rows, :] + norm_back(part, normed, inverse, gain)
            X[rows, :] = grad
            DMB[rows, :] = grad.astype(BF)
            bias_out = bias_out + fold(grad)
        DA[whole, :] = mm_nt(DMB[whole, :], win[layer, :, 3 * D : 4 * D]).astype(BF)
        return gain_sum, shift_sum, bias_out

    def attend_back(layer, image):
        rows = pl.ds(aligned(image * BLK, 16), BLK)
        for pair in range(3):
            at = pair * 128
            query = QKV[layer, rows, at : at + 128] * BF(0.125)
            keys = QKV[layer, rows, D + at : D + at + 128]
            values = QKV[layer, rows, 2 * D + at : 2 * D + at + 128]
            ups = DA[rows, at : at + 128]
            keys_both = jnp.concatenate([keys * even, keys * odd], axis=0)
            values_both = jnp.concatenate([values * even, values * odd], axis=0)
            query = jnp.concatenate([query, fill], axis=0)
            ups = jnp.concatenate([ups, fill], axis=0)
            scores = mm_nt(keys_both, query)
            d_probs = mm_nt(values_both, ups)
            probs, d_scores = [], []
            for base in (0, BLK):
                low_probs, low_grads = [], []
                for first, end in ((0, 128), (128, lanes)):
                    part = jnp.concatenate(
                        [
                            scores[base : base + TAIL, first:end],
                            scores[base + TAIL : base + BLK, first:end] + key_column[TAIL:],
                        ],
                        axis=0,
                    )
                    raw = jnp.exp(part - jnp.max(part, axis=0, keepdims=True))
                    prob = raw * (1.0 / jnp.sum(raw, axis=0, keepdims=True))
                    grad = d_probs[base : base + BLK, first:end]
                    inner = jnp.sum(grad * prob, axis=0, keepdims=True)
                    low_grads.append((prob * (grad - inner)).astype(BF))
                    low_probs.append(prob.astype(BF))
                probs.append(jnp.concatenate(low_probs, axis=1))
                d_scores.append(jnp.concatenate(low_grads, axis=1))
            probs = jnp.concatenate(probs, axis=0)
            d_scores = jnp.concatenate(d_scores, axis=0)
            d_values = mm(probs, ups)
            d_keys = mm(d_scores, query)
            d_query = mm_tn(d_scores, keys_both)[:BLK] * 0.125
            DH[rows, at : at + 128] = d_query.astype(BF)
            DH[rows, D + at : D + at + 128] = jnp.where(
                low_lane, d_keys[:BLK], d_keys[BLK:]
            ).astype(BF)
            DH[rows, 2 * D + at : 2 * D + at + 128] = jnp.where(
                low_lane, d_values[:BLK], d_values[BLK:]
            ).astype(BF)

    def renew(ref, layer, at):
        gain, shift = vector(layer, at, D), vector(layer, at + D, D)

        def one(index, nothing):
            for at, size in pieces(BLK):
                rows = pl.ds(aligned(index * BLK + at, 16), size)
                DXB[rows, :] = (ref[layer, rows, :].astype(F32) * gain + shift).astype(BF)
            return nothing

        lax.fori_loop(0, KEPT, one, 0)
        return DXB[...].T

    def keep_in(k, tile, made):
        for shard in range(n_shard):
            G[k, shard // 2, shard % 2, tile * rows_in : (tile + 1) * rows_in, :] = made[
                shard * rows_in : (shard + 1) * rows_in
            ]

    def backward(step, carry):
        layer = LAYERS - 2 - step
        kd, ku, kq = 3 * step, 3 * step + 1, 3 * step + 2
        bias_down = lax.fori_loop(0, 2, round_up, zeros)
        at_place("round", layer)
        turned = DXB[...].T
        per = min(rows_down, D)
        for pair in range(2):
            start = 2 * pair * D
            wide = mm(turned, ACT[layer, :, start : start + 2 * D]).astype(BF)
            for tile in range(2):
                made = wide[:, tile * D : (tile + 1) * D].T
                for piece in range(D // per):
                    shard, at = divmod(start + tile * D + piece * per, rows_down)
                    G[kd, shard // 2, shard % 2, at : at + per, :] = made[
                        piece * per : (piece + 1) * per
                    ]
        at_place("dn", layer)

        def one(half, totals):
            totals = act_back(layer, half, totals)
            at_place("act", layer, half)
            return totals

        bias_up = lax.fori_loop(0, 2, one, (zeros,) * 4)
        turned = renew(N2, layer, 5 * D)
        for pair in range(2):
            made = mm(turned, DH[:, 2 * pair * D : 2 * (pair + 1) * D]).astype(BF)
            keep_in(ku, 2 * pair, made[:, :D])
            keep_in(ku, 2 * pair + 1, made[:, D:])
        at_place("ups", layer)

        def one_more(half, sums):
            sums = mlp_back(layer, half, sums)
            at_place("mlpb", layer, half)
            return sums

        gain_sum, shift_sum, bias_out = lax.fori_loop(0, 2, one_more, (zeros, zeros, zeros))
        store_sums(
            layer,
            [(7 * D + FF, bias_down), (5 * D, gain_sum), (6 * D, shift_sum), (4 * D, bias_out)]
            + [(7 * D + tile * D, bias_up[tile]) for tile in range(4)],
        )
        keep_in(kq, 3, mm(ATT[layer].T, DMB[...]).astype(BF))
        at_place("out", layer)

        def two(image, nothing):
            attend_back(layer, image)
            at_place("attb", layer, image)
            return nothing

        lax.fori_loop(0, KEPT, two, 0)
        turned = renew(N1, layer, 0)
        made = mm(turned, DH[:, 0 : 2 * D]).astype(BF)
        keep_in(kq, 0, made[:, :D])
        keep_in(kq, 1, made[:, D:])
        keep_in(kq, 2, mm(turned, DH[:, 2 * D : 3 * D]).astype(BF))
        at_place("qkv", layer)
        store_sums(
            layer,
            [
                (2 * D, fold(DH[:, 0:D].astype(F32))),
                (3 * D, fold(DH[:, 2 * D : 3 * D].astype(F32))),
            ],
        )

        def three(half, sums):
            rows = pl.ds(aligned(half * HALF, 16), HALF)
            made = mm_nt(DH[rows, 0 : 3 * D], win[layer, :, 0 : 3 * D])
            sums = first_back(layer, half, made, sums)
            at_place("fb", layer, half)
            return sums

        gain_sum, shift_sum = lax.fori_loop(0, 2, three, (zeros, zeros))
        store_sums(layer, [(0, gain_sum), (D, shift_sum)])
        return carry

    lax.fori_loop(0, LAYERS - 1, backward, 0)

    for at, size in pieces(BLK):
        total = None
        for image in range(KEPT):
            part = X[image * BLK + at : image * BLK + at + size, :]
            DXB[image * BLK + at : image * BLK + at + size, :] = part.astype(BF)
            total = part if total is None else total + part
        V[at : at + size, 0:D] = total

    vec = ("v", v_send, v_recv)
    v_y, v_x = 1, n_y
    v_z = v_x + n_x - 1
    v_gz = v_z + n_z - 1
    v_gx = v_gz + n_z - 1
    v_gy = v_gx + n_x - 1
    v_gc = v_gy + n_y - 1
    rows_c = VEC_ROWS // 2
    rows_y = rows_c // n_y
    rows_x = rows_y // n_x
    split_z = cut(rows_x, n_z, 8)
    rows_z = rows_x // split_z
    at_c = c * rows_c
    at_y = at_c + y * rows_y
    at_x = at_y + x * rows_x
    at_z = at_x + z * rows_z if split_z > 1 else at_x

    def vrows(ref, at, rows):
        return ref.at[pl.ds(aligned(at, 8), rows), :]

    def vadd(at, rows, sources):
        target = pl.ds(aligned(at, 8), rows)
        total = V[target, :]
        for source in sources:
            total = total + source
        V[target, :] = total

    def vectors_core():
        go(lambda: vrows(V, (1 - c) * rows_c, rows_c), VC, vec, 0, mate)

    def vectors_y():
        arrived(VC, v_recv.at[0], v_send.at[0])
        vadd(at_c, rows_c, [VC[...]])
        for o in range(1, n_y):
            to = turn(y, o, n_y)
            go(
                lambda o=o: vrows(V, at_c + turn(y, o, n_y) * rows_y, rows_y), VY.at[o - 1],
                vec, v_y + o - 1, here.to(y=to),
            )

    def vectors_x():
        for o in range(1, n_y):
            arrived(VY.at[o - 1], v_recv.at[v_y + o - 1], v_send.at[v_y + o - 1])
        vadd(at_y, rows_y, [VY[o - 1] for o in range(1, n_y)])
        for o in range(1, n_x):
            to = turn(x, o, n_x)
            go(
                lambda o=o: vrows(V, at_y + turn(x, o, n_x) * rows_x, rows_x), VX.at[o - 1],
                vec, v_x + o - 1, here.to(x=to),
            )

    def vectors_z():
        for o in range(1, n_x):
            arrived(VX.at[o - 1], v_recv.at[v_x + o - 1], v_send.at[v_x + o - 1])
        vadd(at_x, rows_x, [VX[o - 1] for o in range(1, n_x)])
        for o in range(1, n_z):

            def make(o=o):
                at = at_x + turn(z, o, n_z) * rows_z if split_z > 1 else at_x
                return vrows(V, at, rows_z)

            go(make, VZ.at[z], vec, v_z + o - 1, here.to(z=turn(z, o, n_z)))

    def vectors_gather_z():
        for o in range(1, n_z):
            arrived(
                VZ.at[turn(z, n_z - o, n_z)], v_recv.at[v_z + o - 1], v_send.at[v_z + o - 1]
            )
        target = pl.ds(aligned(at_z, 8), rows_z)
        VZ[z] = V[target, :]
        total = VZ[0]
        for index in range(1, n_z):
            total = total + VZ[index]
        VF[target, :] = total
        if split_z > 1:
            for o in range(1, n_z):
                go(
                    lambda: vrows(VF, at_z, rows_z), vrows(VF, at_z, rows_z), vec, v_gz + o - 1,
                    here.to(z=turn(z, o, n_z)),
                )

    def vectors_gather_x():
        if split_z > 1:
            for o in range(1, n_z):
                came = turn(z, n_z - o, n_z)
                arrived(
                    vrows(VF, at_x + came * rows_z, rows_z), v_recv.at[v_gz + o - 1],
                    v_send.at[v_gz + o - 1],
                )
        for o in range(1, n_x):
            go(
                lambda: vrows(VF, at_x, rows_x), vrows(VF, at_x, rows_x), vec, v_gx + o - 1,
                here.to(x=turn(x, o, n_x)),
            )

    sq = ("q", q_send, q_recv)

    def squares_z():
        SQ[0] = square_sum[...]
        SQZ[z] = square_sum[...]
        for o in range(1, n_z):
            go(lambda: SQ.at[0], SQZ.at[z], sq, o - 1, here.to(z=turn(z, o, n_z)))

    def slot_of(i, j, k):
        return (i * n_y + j) * 2 + k

    def squares_plane():
        for o in range(1, n_z):
            arrived(SQZ.at[turn(z, n_z - o, n_z)], q_recv.at[o - 1], q_send.at[o - 1])
        total = SQZ[0]
        for index in range(1, n_z):
            total = total + SQZ[index]
        SQ[1] = total
        SQP[slot_of(x, y, c)] = total
        for index, step in enumerate(plane):
            go(
                lambda: SQ.at[1], SQP.at[slot_of(x, y, c)], sq, n_z - 1 + index,
                in_plane(step),
            )

    def squares_done():
        for index, (i, j, k) in enumerate(plane):
            slot = slot_of(
                turn(x, n_x - i, n_x), turn(y, n_y - j, n_y), lax.rem(c + k, 2)
            )
            arrived(SQP.at[slot], q_recv.at[n_z - 1 + index], q_send.at[n_z - 1 + index])
        total = SQP[0]
        for index in range(1, 2 * n_x * n_y):
            total = total + SQP[index]
        SQ[2] = total

    def vectors_gather_y():
        for o in range(1, n_x):
            at = at_y + turn(x, n_x - o, n_x) * rows_x
            arrived(vrows(VF, at, rows_x), v_recv.at[v_gx + o - 1], v_send.at[v_gx + o - 1])
        for o in range(1, n_y):
            go(
                lambda: vrows(VF, at_y, rows_y), vrows(VF, at_y, rows_y), vec, v_gy + o - 1,
                here.to(y=turn(y, o, n_y)),
            )

    def vectors_gather_core():
        for o in range(1, n_y):
            at = at_c + turn(y, n_y - o, n_y) * rows_y
            arrived(vrows(VF, at, rows_y), v_recv.at[v_gy + o - 1], v_send.at[v_gy + o - 1])
        go(lambda: vrows(VF, at_c, rows_c), vrows(VF, at_c, rows_c), vec, v_gc, mate)

    def vectors_done():
        arrived(vrows(VF, (1 - c) * rows_c, rows_c), v_recv.at[v_gc], v_send.at[v_gc])

    actions.update(
        vc=vectors_core, vy=vectors_y, vx=vectors_x, vz=vectors_z, vgz=vectors_gather_z,
        vgx=vectors_gather_x, vgy=vectors_gather_y, vgc=vectors_gather_core, vd=vectors_done,
        qz=squares_z, qp=squares_plane, qd=squares_done,
    )
    at_place("emb")
    low = DXB[...]
    for tile in range(2):
        made = mm_tn(pix[:, :, tile * D : (tile + 1) * D].reshape(ROWS, D), low).astype(BF)
        for piece in range(D // rows_patch):
            shard = tile * (D // rows_patch) + piece
            GS[1, shard // 2, shard % 2, 0:rows_patch, :] = made[piece * rows_patch : (piece + 1) * rows_patch]

    at_place("patch")
    ending = SCHEDULE["tail",]
    perform(ending[:-6])
    early = [
        key for key in sent
        if key[0] == "ag" or (key[0] == "rs" and key[1][0] not in (4, 5, 7))
    ]
    for key in early:
        source, send, recv, at = sent.pop(key)
        left_here(source(), recv.at[at], send.at[at])
    perform(ending[-6:])
    last_copies = [
        pltpu.make_async_copy(VF, vec_out, out_local.at[1 + CHUNKS + 2]),
        pltpu.make_async_copy(SQ.at[2], square_out, out_local.at[2 + CHUNKS + 2]),
    ]
    for copy in last_copies:
        copy.start()
    for source, send, recv, at in list(sent.values()):
        left_here(source(), recv.at[at], send.at[at])
    for k in range(CHUNKS + 2):
        result(k).wait()
    for copy in last_copies:
        copy.wait()

    @pl.when(jnp.logical_not(lower))
    def _():
        for index in range(2):
            left_here(given[index], img_recv.at[index], img_send.at[index])
        left_here(lab_given, img_recv.at[2], img_send.at[2])


def run_train(
    n_rep, n_shard, patches, patch_ends, labels, counts, own_patch, own_in, own_down, vecs, glob, pos, head
):
    n_x = 2 ** ((n_rep.bit_length() - 2) // 2)
    n_z, n_y = n_rep // n_x, n_shard // 2
    block = 4 * (D // n_shard)
    small_block = small_rows(block // 2, n_x, n_z)
    group = KEPT * n_shard
    keep = LAYERS - 1
    units = 1 + 3 * LAYERS
    chunks = CHUNKS + 2

    def buf(*shape, dtype=BF):
        return pltpu.VMEM(shape, dtype)

    def sems(*shape):
        return pltpu.SemaphoreType.DMA(shape)

    def reduction(count, slots, rows):
        by_x = cut(rows, n_x, 16)
        by_z = cut(rows // by_x, n_z, 16)
        return [
            buf(count, n_y, 2, rows, D),
            buf(slots, n_y, rows, D),
            buf(slots, n_y - 1, rows, D),
            buf(slots, n_x - 1 if by_x > 1 else n_x, rows // by_x, D),
            buf(slots, n_z, rows // by_x // by_z, D),
            buf(count, rows, D),
        ]

    rows_y = VEC_ROWS // 2 // n_y
    rows_x = rows_y // n_x
    rows_z = rows_x // cut(rows_x, n_z, 8)
    ag_count = n_y + (n_y - 1) * (n_x - 1) * 2 + n_y - 1
    rs_count = 1 + (n_y - 1) + 2 * (n_x - 1) + 2 * (n_z - 1)
    f_count = 1 + 2 * (n_y - 1) + (n_x - 1) + (n_z - 1) + 1
    v_count = 1 + 2 * (n_y - 1) + 2 * (n_x - 1) + 2 * (n_z - 1) + 1
    q_count = n_z - 1 + 2 * n_x * n_y - 1
    whole = pl.BlockSpec(memory_space=pltpu.VMEM)
    there = pl.BlockSpec(memory_space=pl.ANY)
    return pl.pallas_call(
        functools.partial(train, n_rep, n_shard),
        out_shape=[
            jax.ShapeDtypeStruct((CHUNKS, block, D), BF),
            jax.ShapeDtypeStruct((2, small_block, D), BF),
            jax.ShapeDtypeStruct((VEC_ROWS, VEC_WIDE), F32),
            jax.ShapeDtypeStruct((8, 128), F32),
            jax.ShapeDtypeStruct((2, n_y, n_x, n_z, group, WFAC // n_y), BF),
        ],
        in_specs=[there] * 2 + [pl.BlockSpec(memory_space=pltpu.SMEM)] * 2 + [there] * 3 + [whole] * 4,
        out_specs=[there] * 5,
        scratch_shapes=[
            buf(ROWS, D, dtype=F32),
            buf(LAYERS, ROWS, D),
            buf(LAYERS, ROWS, 128, dtype=F32),
            buf(keep, ROWS, 3 * D),
            buf(keep, ROWS, D),
            buf(keep, ROWS, D),
            buf(keep, ROWS, 128, dtype=F32),
            buf(keep, ROWS, FF),
            buf(keep, ROWS, FF),
            buf(ROWS, D),
            buf(ROWS, D),
            buf(ROWS, D),
            buf(ROWS, FF),
            buf(KEPT, BLK, PATCH_DIM),
            buf(2, 32, 128, dtype=F32),
            buf(32, 128, dtype=F32),
            buf(PATCH_DIM, D),
            buf(LAYERS, D, 4 * D + FF),
            buf(LAYERS, FF, D),
            buf(D, CPAD),
            buf(1, CPAD, dtype=F32),
            *reduction(CHUNKS, 3, block),
            *reduction(2, 1, small_block),
            buf(2, n_y, group, WFAC // n_y),
            buf(n_y, group, WFAC // n_y),
            buf(n_y - 1, group, WFAC // n_y),
            buf(VEC_ROWS, VEC_WIDE, dtype=F32),
            buf(VEC_ROWS // 2, VEC_WIDE, dtype=F32),
            buf(n_y - 1, rows_y, VEC_WIDE, dtype=F32),
            buf(n_x - 1, rows_x, VEC_WIDE, dtype=F32),
            buf(n_z, rows_z, VEC_WIDE, dtype=F32),
            buf(VEC_ROWS, VEC_WIDE, dtype=F32),
            buf(3, 8, 128, dtype=F32),
            buf(n_z, 8, 128, dtype=F32),
            buf(2 * n_x * n_y, 8, 128, dtype=F32),
            buf(8, 128, dtype=F32),
            sems(units, ag_count),
            sems(units, ag_count),
            sems(units, 4),
            sems(chunks, rs_count),
            sems(chunks, rs_count),
            sems(f_count),
            sems(f_count),
            sems(v_count),
            sems(v_count),
            sems(q_count),
            sems(q_count),
            sems(3),
            sems(3),
            sems(4),
            sems(3 + chunks),
        ],
        compiler_params=pltpu.CompilerParams(
            vmem_limit_bytes=65400 * 1024, collective_id=0, has_side_effects=True
        ),
        cost_estimate=pl.CostEstimate(
            flops=24_000_000_000, bytes_accessed=30_000_000, transcendentals=10_000_000
        ),
        name="train_step",
    )(patches, patch_ends, labels, counts, own_patch, own_in, own_down, vecs, glob, pos, head)


def adam(weight, first, second, grad, factor, rate):
    share = grad * factor
    first = BETA_FIRST * first + share
    square_scale = (1.0 - BETA_SECOND) / (1.0 - BETA_FIRST) ** 2
    second = BETA_SECOND * second + square_scale * (share * share)
    root_scale = (1.0 / (1.0 - BETA_SECOND**ADAM_STEP)) ** 0.5
    step_scale = rate / (1.0 - BETA_FIRST**ADAM_STEP) / root_scale
    bottom = second * lax.rsqrt(second) + ADAM_EPS / root_scale
    step = first * lax.rsqrt(bottom * bottom)
    return weight * (1.0 - rate * WEIGHT_DECAY) - step * step_scale, first, second


def update(n_rep, n_shard, *refs):
    res_there, small_there, vec, exchanged, factors = refs[0:5]
    sources = refs[5:26]
    loss_out, norm_out = refs[26:28]
    targets = refs[28:49]
    buffers = refs[49:70]
    results = refs[70:91]
    last_in, last_down, passing, grad_head, res, small, in_sems, out_sems, grad_sems = refs[91:]
    shard = lax.axis_index("shard")
    rows_in = D // n_shard
    rows_down = FF // n_shard
    keep = LAYERS - 1

    def moves(array, layer=None, out=False):
        found = []
        for kind in range(3):
            index = 3 * array + kind
            if out:
                src, dst, sem = results[index], targets[index], out_sems
            else:
                src, dst, sem = sources[index], buffers[index], in_sems
            slot = 0 if layer is None else layer
            if layer is not None:
                src, dst = src.at[layer], dst.at[layer]
            found.append(pltpu.make_async_copy(src, dst, sem.at[index, slot]))
        return found

    order = [(array, layer) for layer in range(keep) for array in (1, 2)]
    order += [(array, None) for array in (0, 4, 3, 5, 6)] + [(1, keep), (2, keep)]
    res_copy = pltpu.make_async_copy(res_there, res, grad_sems.at[0])
    small_copy = pltpu.make_async_copy(small_there, small, grad_sems.at[1])
    res_copy.start()
    small_copy.start()
    for array, layer in order:
        for move in moves(array, layer):
            move.start()

    n_rows = factors.shape[2] * factors.shape[3] * factors.shape[4]
    part_wide = factors.shape[5]

    def factor(half, at, size):
        found = []
        while size:
            part, column = divmod(at, part_wide)
            wide = min(size, part_wide - column)
            piece = factors[half, part, :, :, :, column : column + wide]
            found.append(piece.reshape(n_rows, wide))
            at, size = at + wide, size - wide
        return found[0] if len(found) == 1 else jnp.concatenate(found, axis=1)

    def gram_squares(left, right):
        total = jnp.zeros((8, 128), F32)
        for row in range(0, n_rows, 128):
            both = mm_nt(left[row : row + 128], left) * mm_nt(right[row : row + 128], right)
            both = fold(both)
            for lane in range(0, n_rows, 128):
                total = total + both[:, lane : lane + 128]
        return total

    d_logits = factor(1, FF + 2 * D, CPAD)
    head_bias = down_sum(d_logits.astype(F32))
    wide = gram_squares(factor(0, 0, FF), factor(0, FF + 4 * D, D))
    wide = wide + gram_squares(factor(0, FF, D), factor(1, 0, FF))
    wide = wide + gram_squares(factor(0, FF + D, D), factor(1, FF, D))
    wide = wide + gram_squares(factor(0, FF + 2 * D, D), factor(1, FF + D, D))
    wide = wide + gram_squares(factor(0, FF + 3 * D, D), d_logits)
    for lane in range(0, CPAD, 128):
        row = head_bias[:, lane : lane + 128]
        wide = wide + (row * row) * 0.125
    used = VEC_AT + 12 * LAYERS + 2
    parts = jnp.zeros((8, D), F32)
    kept_rows = lax.broadcasted_iota(jnp.int32, (8, 1), 0)
    for at in range(0, used, 8):
        value = vec[at : at + 8, 0:D]
        if at + 8 > used:
            value = jnp.where(kept_rows + at < used, value, 0.0)
        parts = parts + value * value
    patch_bias = down_sum(vec[0:PATCHES, 0:D])
    class_row = vec[CLS : CLS + 1, 0:D]
    rest = (patch_bias * patch_bias + class_row * class_row) * 0.125
    parts = parts + rest
    for lane in range(0, D, 128):
        wide = wide + parts[:, lane : lane + 128]
    wide = wide + exchanged[...]
    sum_squares = jnp.sum(jnp.sum(wide, axis=1, keepdims=True), axis=0, keepdims=True)
    inv_count = 1.0 / vec[used + 1 : used + 2, 0:1]
    grad_norm = jnp.sqrt(sum_squares) * inv_count
    norm_out[...] = grad_norm
    loss_out[...] = vec[used : used + 1, 0:1] * inv_count
    scale = jnp.minimum(1.0, CLIP_NORM / grad_norm) * inv_count * (1.0 - BETA_FIRST)

    def apply(array, where, grad, rate):
        refs = [buffers[3 * array + kind] for kind in range(3)]
        made = adam(refs[0][where], refs[1][where], refs[2][where], grad, scale, rate)
        for kind, value in enumerate(made):
            results[3 * array + kind][where] = value

    def begin(array, layer=None):
        for move in moves(array, layer):
            move.wait()

    def finish(array, layer=None):
        for move in moves(array, layer, out=True):
            move.start()

    def loop(count, body):
        def one(index, nothing):
            body(index)
            return nothing

        lax.fori_loop(0, count, one, 0)

    step = 32 if rows_in % 32 == 0 else 16

    def update_in(layer):
        begin(1, layer)

        def column_of(column):
            lanes = pl.ds(pl.multiple_of(column * D, 128), D)
            for at in range(0, rows_in, step):
                if layer < keep:
                    k = 3 * (keep - 1 - layer) + jnp.where(column < 4, 2, 1)
                    row = pl.multiple_of(lax.rem(column, 4) * rows_in + at, 16)
                    grad = res[k, pl.ds(row, step), :].astype(F32)
                else:
                    grad = last_in[at : at + step, lanes]
                apply(1, (layer, slice(at, at + step), lanes), grad, LEARNING_RATE)

        loop(8, column_of)
        finish(1, layer)

    def update_down(layer):
        begin(2, layer)

        def rows_of(index):
            for part in range(3):
                at = pl.multiple_of(index * 96 + part * 32, 16)
                if layer < keep:
                    grad = res[3 * (keep - 1 - layer), pl.ds(at, 32), :].astype(F32)
                else:
                    grad = last_down[pl.ds(at, 32), :]
                apply(2, (layer, pl.ds(at, 32), slice(0, D)), grad, LEARNING_RATE)

        loop(rows_down // 96, rows_of)
        finish(2, layer)

    res_copy.wait()
    for layer in range(keep):
        update_in(layer)
        update_down(layer)
    small_copy.wait()
    begin(0)

    def patch_rows(index):
        for part in range(3):
            at = pl.multiple_of(index * 96 + part * 32, 16)
            grad = small[1, pl.ds(at, 32), :].astype(F32)
            apply(0, (pl.ds(at, 32), slice(0, D)), grad, LEARNING_RATE)

    loop(PATCH_DIM // n_shard // 96, patch_rows)
    finish(0)
    begin(4)
    rows = [patch_bias, class_row, vec[used - 2 : used - 1, 0:D], vec[used - 1 : used, 0:D]]
    for index, row in enumerate(rows):
        apply(4, (slice(index, index + 1), slice(0, D)), row, VECTOR_RATE)
    finish(4)
    begin(3)
    for layer in range(LAYERS):
        for piece in range(12):
            row = VEC_AT + 12 * layer + piece
            where = (slice(layer, layer + 1), slice(piece * D, (piece + 1) * D))
            apply(3, where, vec[row : row + 1, 0:D], VECTOR_RATE)
    finish(3)
    begin(5)
    apply(5, (slice(0, 1), slice(0, D)), class_row, VECTOR_RATE)
    for at in range(0, PATCHES, 28):
        apply(
            5, (slice(1 + at, 29 + at), slice(0, D)), vec[at : at + 28, 0:D], VECTOR_RATE
        )
    finish(5)
    final = factor(0, FF + 3 * D, D)
    for at in range(0, CPAD, 512):
        grad_head[0:D, at : at + 512] = mm_tn(final, d_logits[:, at : at + 512])
    grad_head[D : D + 1, :] = head_bias
    begin(6)

    def head_rows(index):
        for part in range(3):
            rows = pl.ds(pl.multiple_of(index * 48 + part * 16, 16), 16)
            apply(6, (rows, slice(0, NCLS)), grad_head[rows, 0:NCLS], LEARNING_RATE)

    loop(D // 48, head_rows)
    apply(6, (slice(D, D + 1), slice(0, NCLS)), grad_head[D : D + 1, 0:NCLS], LEARNING_RATE)
    finish(6)
    own_rows = pl.multiple_of(shard * rows_in, 8)

    def keep_in(column, made):
        slot = column % 2
        passing[slot] = made
        last_in[:, column * D : (column + 1) * D] = passing[slot, pl.ds(own_rows, rows_in), :]

    h2 = factor(0, FF, D)
    for tile in range(4):
        made = mm_tn(h2, factor(1, tile * D, D))
        keep_in(4 + tile, made)
    for tile in range(2):
        last_in[:, (1 + tile) * D : (2 + tile) * D] = small[
            0, tile * rows_in : (tile + 1) * rows_in, :
        ].astype(F32)
    made = mm_tn(factor(0, FF + 2 * D, D), factor(1, FF + D, D))
    keep_in(0, made)
    made = mm_tn(factor(0, FF + D, D), factor(1, FF, D))
    keep_in(3, made)
    d_top = factor(0, FF + 4 * D, D)
    per = min(rows_down, D)
    for tile in range(4):
        made = mm_tn(factor(0, tile * D, D), d_top)
        for piece in range(D // per):
            owner, at = divmod(tile * D + piece * per, rows_down)

            def keep_down(made=made, piece=piece, at=at):
                last_down[at : at + per, :] = made[piece * per : (piece + 1) * per]

            pl.when(shard == owner)(keep_down)
    update_in(keep)
    update_down(keep)
    for array, layer in order:
        for move in moves(array, layer, out=True):
            move.wait()


def run_update(n_rep, n_shard, res, small, vec, squares, factors, arrays):
    whole = pl.BlockSpec(memory_space=pltpu.VMEM)
    there = pl.BlockSpec(memory_space=pl.ANY)
    one = jax.ShapeDtypeStruct((1, 1), F32)
    made = pl.pallas_call(
        functools.partial(update, n_rep, n_shard),
        out_shape=[one, one] + [jax.ShapeDtypeStruct(a.shape, F32) for a in arrays],
        in_specs=[there] * 2 + [whole] * 3 + [there] * 21,
        out_specs=[whole] * 2 + [there] * 21,
        scratch_shapes=[pltpu.VMEM(a.shape, F32) for a in (*arrays, *arrays)]
        + [
            pltpu.VMEM((D // n_shard, 4 * D + FF), F32),
            pltpu.VMEM((FF // n_shard, D), F32),
            pltpu.VMEM((2, D, D), F32),
            pltpu.VMEM((D + 8, CPAD), F32),
            pltpu.VMEM(res.shape, BF),
            pltpu.VMEM(small.shape, BF),
            pltpu.SemaphoreType.DMA((21, LAYERS)),
            pltpu.SemaphoreType.DMA((21, LAYERS)),
            pltpu.SemaphoreType.DMA((2,)),
        ],
        compiler_params=pltpu.CompilerParams(vmem_limit_bytes=62 * 1024 * 1024),
        cost_estimate=pl.CostEstimate(
            flops=200_000_000, bytes_accessed=50_000_000, transcendentals=4_000_000
        ),
        name="adamw",
    )(res, small, vec, squares, factors, *arrays)
    return made[0].reshape(()), made[1].reshape(()), made[2:]


def shards(
    n_rep, n_shard,
    patches, labels, counts, patch_w, layer_in, layer_down, layer_vecs, glob_vecs, pos_embed, head,
    m_patch, v_patch, m_in, v_in, m_down, v_down, m_vecs, v_vecs, m_glob, v_glob, m_pos, v_pos,
    m_head, v_head,
):
    ends = jnp.pad(patches[:, TAIL:], ((0, 0), (0, BLK - PATCHES), (0, 0)))
    res, small, vec, squares, factors = run_train(
        n_rep, n_shard, patches, ends, labels, counts, patch_w, layer_in, layer_down, layer_vecs,
        glob_vecs, pos_embed, head,
    )
    arrays = [
        patch_w, m_patch, v_patch, layer_in, m_in, v_in, layer_down, m_down, v_down,
        layer_vecs, m_vecs, v_vecs, glob_vecs, m_glob, v_glob, pos_embed, m_pos, v_pos,
        head, m_head, v_head,
    ]
    loss, grad_norm, new = run_update(n_rep, n_shard, res, small, vec, squares, factors, arrays)
    return (loss, grad_norm, *new)


def solution(mesh):
    everywhere = P()
    rows = P("shard", None)
    middle = P(None, "shard", None)
    return jax.shard_map(
        functools.partial(shards, mesh.shape["rep"], mesh.shape["shard"]),
        mesh=mesh,
        in_specs=(
            P(("rep", "shard"), None, None),
            P(("rep", "shard")),
            P(("rep", "shard")),
            rows,
            middle,
            middle,
            *(everywhere,) * 4,
            *(rows,) * 2,
            *(middle,) * 4,
            *(everywhere,) * 8,
        ),
        out_specs=(
            *(everywhere,) * 2,
            *(rows,) * 3,
            *(middle,) * 6,
            *(everywhere,) * 12,
        ),
        check_vma=False,
    )
```

```python
import functools

import jax
import jax.numpy as jnp
from jax import lax
from jax.experimental import pallas as pl
from jax.experimental.pallas import tpu as pltpu
from jax.sharding import PartitionSpec as P

D = 384
HEADS = 6
HEAD_DIM = 64
FF = 1536
PATCH_DIM = 768
PATCHES = 196
NCLS = 1000
LAYERS = 3
SEQ = 197

BLK = 208
CLS = 200
TAIL = 192
KEPT = 4
ROWS = KEPT * BLK
HALF = 2 * BLK
CROWS = KEPT * 16
CPAD = 1024
WIDE = 8 * D + FF

NORM_EPS = 1e-06
SMOOTHING = 0.1
CLIP_NORM = 0.05
LEARNING_RATE = 0.05
VECTOR_RATE = 0.5
BETA_FIRST = 0.9
BETA_SECOND = 0.999
ADAM_EPS = 1e-08
WEIGHT_DECAY = 0.05
ADAM_STEP = 10
GELU_SCALE = 0.7978845608028654
GELU_CUBIC = 0.044715

F32 = jnp.float32
BF = jnp.bfloat16


def mm(left, right):
    return jnp.dot(left, right, preferred_element_type=F32)


def mm_nt(left, right):
    return lax.dot_general(left, right, (((1,), (1,)), ((), ())), preferred_element_type=F32)


def mm_tn(left, right):
    return lax.dot_general(left, right, (((0,), (0,)), ((), ())), preferred_element_type=F32)


def fold(values):
    return jnp.sum(values.reshape(-1, 8, values.shape[-1]), axis=0)


def down_sum(values):
    return jnp.sum(values, axis=0, keepdims=True)


def norm(values):
    centre = values - jnp.mean(values, axis=-1, keepdims=True)
    inverse = lax.rsqrt(jnp.mean(centre * centre, axis=-1, keepdims=True) + NORM_EPS)
    return centre * inverse, inverse


def norm_back(upstream, normed, inverse, gain):
    scaled = upstream * gain
    first = jnp.mean(scaled, axis=-1, keepdims=True)
    second = jnp.mean(scaled * normed, axis=-1, keepdims=True)
    return inverse * (scaled - first - normed * second)


def gelu_parts(hidden):
    bent = hidden * (GELU_SCALE + (GELU_SCALE * GELU_CUBIC) * (hidden * hidden))
    tangent = jnp.tanh(bent)
    share = 0.5 + 0.5 * tangent
    slope = share + (1.0 - tangent * tangent) * (1.5 * bent - GELU_SCALE * hidden)
    return hidden * share, slope


def lane_mask(width, low, high):
    lane = lax.broadcasted_iota(jnp.int32, (1, width), 1)
    return jnp.where((lane >= low) & (lane < high), 1.0, 0.0).astype(BF)


STEP = 16


def pieces(total):
    return [(at, min(STEP, total - at)) for at in range(0, total, STEP)]


SCHEDULE = {
    ("cast", 0): ("ws0",),
    ("cast", 1): ("ws1",),
    ("cast", 2): ("ws2",),
    ("cast", 8): ("wf0", "ws3",),
    ("b_start",): ("wr0", "wf1", "ws4", "we0",),
    ("b_norm", 0, 0): ("wf2", "ws5", "wr1", "wf3", "ws6", "we1",),
    ("norm", 0, 0): ("wr2",),
    ("att", 0, 0, 0): ("wf4", "ws7",),
    ("att", 0, 0, 1): ("wr3",),
    ("b_up", 0, 0): ("we2",),
    ("up", 0, 0): ("wr4", "wf5", "ws8",),
    ("b_down", 0, 0): ("we3",),
    ("down", 0, 0): ("wf6", "ws9",),
    ("b_norm", 0, 1): ("we4",),
    ("att", 0, 1, 0): ("wr5", "wf7",),
    ("mid", 0, 1): ("wr6", "wf8",),
    ("b_up", 0, 1): ("we5",),
    ("b_down", 0, 1): ("we6",),
    ("down", 0, 1): ("wr7", "wf9",),
    ("norm", 1, 0): ("wr8",),
    ("mid", 1, 0): ("wr9",),
    ("b_last",): ("we7", "we8", "we9",),
    ("class",): ("fc",),
    ("kv",): ("core6",),
    ("lb", 0): ("fy",),
    ("round", 1): ("y6",),
    ("dn", 1): ("fz", "core0",),
    ("ups", 1): ("y0", "x6", "core1",),
    ("mlpb", 1, 0): ("fx",),
    ("out", 1): ("y1", "z6",),
    ("attb", 1, 2): ("x0", "gz6",),
    ("qkv", 1): ("core2",),
    ("fb", 1, 0): ("gx6",),
    ("fb", 1, 1): ("z0", "x1",),
    ("round", 0): ("y2",),
    ("dn", 0): ("gd6", "core3",),
    ("act", 0, 1): ("z1", "gz0",),
    ("mlpb", 0, 0): ("x2", "y3", "core4",),
    ("mlpb", 0, 1): ("gz1",),
    ("attb", 0, 0): ("gx0",),
    ("attb", 0, 1): ("z2",),
    ("attb", 0, 3): ("x3", "y4", "gx1", "gd0",),
    ("qkv", 0): ("gz2", "core5",),
    ("fb", 0, 1): ("z3",),
    ("emb",): ("vc",),
    ("patch",): ("gx2", "core7",),
    ("tail",): ("vy", "gd1", "x4", "y5", "y7", "fv", "gz3", "vx", "gd2", "z4", "gx3", "vz", "x5", "gz4", "gd3", "vgz", "x7", "z5", "gx4", "vgx", "z7", "gz5", "gd4", "vgy", "gz7", "qz", "fm", "gx5", "vgc", "gx7", "qp", "fd", "vd", "gd5", "gd7", "qd",),
}


WFAC = FF + 5 * D + 128
VEC_ROWS = 256
VEC_AT = BLK
VEC_WIDE = D
MESH = pl.DeviceIdType.MESH
CHUNKS = 6


class Place:
    def __init__(self, n_rep, n_shard):
        self.n_rep, self.n_shard = n_rep, n_shard
        self.n_x = 2 ** ((n_rep.bit_length() - 2) // 2)
        self.n_z = n_rep // self.n_x
        self.n_y = n_shard // 2
        rep, shard = lax.axis_index("rep"), lax.axis_index("shard")
        self.rep, self.shard = rep, shard
        self.z, self.x = rep // self.n_x, rep % self.n_x
        self.y, self.c = shard // 2, shard % 2

    def to(self, x=None, y=None, z=None, c=None):
        x = self.x if x is None else x
        y = self.y if y is None else y
        z = self.z if z is None else z
        c = self.c if c is None else c
        return {"rep": z * self.n_x + x, "shard": y * 2 + c}


def cut(rows, parts, unit):
    return parts if rows % (parts * unit) == 0 else 1


def small_rows(rows, n_x, n_z):
    unit = 16 * n_x * n_z
    padded = -(-rows // unit) * unit
    return padded if 2 * padded <= 3 * rows else rows


def aligned(value, unit):
    return pl.multiple_of(value, unit)


def train(
    n_rep, n_shard,
    patches, patch_ends, labels, counts, own_patch, own_in, own_down, vecs, glob, pos_there, head_there,
    res_out, small_out, vec_out, square_out, all_factors,
    X, N1, I1, QKV, ATT, N2, I2, ACT, SLOPE, DXB, DMB, DA, DH,
    pos, head, pix, lab, lab_given, wp, win, wdn, low_head, head_bias,
    G, RC, RY, RX, RZ, RES, GS, SC, SY, SX, SZ, SRES,
    FAC, FC, FY, V, VC, VY, VX, VZ, VF, SQ, SQZ, SQP, square_sum,
    ag_send, ag_recv, ag_local, rs_send, rs_recv, f_send, f_recv, v_send, v_recv,
    q_send, q_recv,
    img_send, img_recv, img_local, own_local, out_local,
):
    here = Place(n_rep, n_shard)
    n_x, n_y, n_z = here.n_x, here.n_y, here.n_z
    x, y, z, c = here.x, here.y, here.z, here.c
    rows_in, rows_down, rows_patch = D // n_shard, FF // n_shard, PATCH_DIM // n_shard
    block = 4 * rows_in
    small_block = small_rows(block // 2, n_x, n_z)
    mate = here.to(c=1 - c)

    def push(src, dst, send, recv, device):
        pltpu.make_async_remote_copy(
            src_ref=src, dst_ref=dst, send_sem=send, recv_sem=recv,
            device_id=device, device_id_type=MESH,
        ).start()

    def arrived(dst, recv, send):
        pltpu.make_async_remote_copy(
            src_ref=dst, dst_ref=dst, send_sem=send, recv_sem=recv,
            device_id=mate, device_id_type=MESH,
        ).wait_recv()

    def left_here(src, recv, send):
        pltpu.make_async_remote_copy(
            src_ref=src, dst_ref=src, send_sem=send, recv_sem=recv,
            device_id=mate, device_id_type=MESH,
        ).wait_send()

    sent = {}

    def go(source, dst, sems, index, device):
        name, send, recv = sems
        push(source(), dst, send.at[index], recv.at[index], device)
        sent[name, index] = (source, send, recv, index)

    def gone(sems, index):
        source, send, recv, at = sent.pop((sems[0], index))
        left_here(source(), recv.at[at], send.at[at])

    def turn(at, by, size):
        return lax.rem(at + by, size)

    barrier = pltpu.get_barrier_semaphore()
    plane = [
        (i, j, k) for i in range(n_x) for j in range(n_y) for k in range(2) if i or j or k
    ]

    def in_plane(step):
        i, j, k = step
        return here.to(x=turn(x, i, n_x), y=turn(y, j, n_y), c=lax.rem(c + k, 2))

    others = [in_plane(step) for step in plane]
    others += [here.to(z=turn(z, o, n_z)) for o in range(1, n_z)]
    for other in others:
        pl.semaphore_signal(barrier, inc=1, device_id=other, device_id_type=MESH)

    def weight(kind, layer, shard, part=None):
        if kind == "patch":
            parts = cut(rows_patch, n_x, 16)
            rows = rows_patch // parts
            if part is None:
                return wp.at[pl.ds(aligned(shard * rows_patch, 16), rows_patch), :]
            return wp.at[pl.ds(aligned(shard * rows_patch + part * rows, 16), rows), :]
        if kind == "down":
            parts = cut(rows_down, n_x, 16)
            rows = rows_down // parts
            if part is None:
                return wdn.at[layer, pl.ds(aligned(shard * rows_down, 16), rows_down), :]
            return wdn.at[layer, pl.ds(aligned(shard * rows_down + part * rows, 16), rows), :]
        base = 0 if kind == "attn" else 4 * D
        rows = pl.ds(aligned(shard * rows_in, 16), rows_in)
        if part is None:
            return win.at[layer, rows, pl.ds(base, 4 * D)]
        wide = 4 * D // n_x
        return win.at[layer, rows, pl.ds(aligned(base + part * wide, 128), wide)]

    units = [("patch", 0)] + [
        (kind, layer) for layer in range(LAYERS) for kind in ("attn", "up", "down")
    ]

    def parts_of(kind):
        if kind == "patch":
            return cut(rows_patch, n_x, 16)
        if kind == "down":
            return cut(rows_down, n_x, 16)
        return n_x

    ag = ("ag", ag_send, ag_recv)
    base_x = n_y
    base_my = base_x + (n_y - 1) * (n_x - 1)
    base_mx = base_my + (n_y - 1)

    stage = 4 * rows_in

    def weights_copies(unit):
        kind, layer = units[unit]
        base = (unit % 2) * stage
        if kind == "patch":
            pairs = [(own_patch, X.at[pl.ds(base, rows_patch)])]
        elif kind == "down":
            pairs = [(own_down.at[layer], X.at[pl.ds(base, rows_down)])]
        else:
            start = 0 if kind == "attn" else 4 * D
            pairs = [
                (
                    own_in.at[layer, :, pl.ds(start + tile * D, D)],
                    X.at[pl.ds(base + tile * rows_in, rows_in)],
                )
                for tile in range(4)
            ]
        return [
            pltpu.make_async_copy(src, dst, ag_local.at[unit, index])
            for index, (src, dst) in enumerate(pairs)
        ]

    def weights_cast(unit):
        kind, layer = units[unit]
        base = (unit % 2) * stage
        for copy in weights_copies(unit):
            copy.wait()
        if kind == "patch":
            rows = pl.ds(aligned(here.shard * rows_patch, 16), rows_patch)
            wp[rows, :] = X[base : base + rows_patch, :].astype(BF)
        elif kind == "down":
            rows = pl.ds(aligned(here.shard * rows_down, 16), rows_down)
            wdn[layer, rows, :] = X[base : base + rows_down, :].astype(BF)
        else:
            start = 0 if kind == "attn" else 4 * D
            rows = pl.ds(aligned(here.shard * rows_in, 16), rows_in)
            for tile in range(4):
                win[layer, rows, start + tile * D : start + (tile + 1) * D] = X[
                    base + tile * rows_in : base + (tile + 1) * rows_in, :
                ].astype(BF)
        if unit + 2 < len(units):
            for copy in weights_copies(unit + 2):
                copy.start()

    def weights_start(unit):
        kind, layer = units[unit]
        part = x if parts_of(kind) > 1 else 0
        for o in range(1, n_y):
            go(
                lambda: weight(kind, layer, here.shard, part),
                weight(kind, layer, here.shard, part), ag, (unit, o),
                here.to(y=turn(y, o, n_y)),
            )
        go(
            lambda: weight(kind, layer, here.shard), weight(kind, layer, here.shard), ag,
            (unit, 0), mate,
        )

    def weights_forward(unit):
        kind, layer = units[unit]
        split = parts_of(kind) > 1
        part = x if split else 0
        for o in range(1, n_y):
            def make(o=o):
                return weight(kind, layer, turn(y, n_y - o, n_y) * 2 + c, part)

            arrived(make(), ag_recv.at[unit, o], ag_send.at[unit, o])
            if split:
                for p in range(1, n_x):
                    index = base_x + (o - 1) * (n_x - 1) + p - 1
                    go(make, make(), ag, (unit, index), here.to(x=turn(x, p, n_x)))
            go(make, make(), ag, (unit, base_my + o - 1), mate)

    def weights_pass(unit):
        kind, layer = units[unit]
        split = parts_of(kind) > 1
        part = x if split else 0
        if split:
            for o in range(1, n_y):
                for p in range(1, n_x):
                    index = (o - 1) * (n_x - 1) + p - 1

                    def make(o=o, p=p):
                        shard = turn(y, n_y - o, n_y) * 2 + c
                        return weight(kind, layer, shard, turn(x, n_x - p, n_x))

                    arrived(
                        make(), ag_recv.at[unit, base_x + index], ag_send.at[unit, base_x + index]
                    )
                    go(make, make(), ag, (unit, base_mx + index), mate)

    def weights_whole(unit):
        kind, layer = units[unit]
        split = parts_of(kind) > 1
        part = x if split else 0
        arrived(weight(kind, layer, y * 2 + 1 - c), ag_recv.at[unit, 0], ag_send.at[unit, 0])
        for o in range(1, n_y):
            shard = turn(y, n_y - o, n_y) * 2 + 1 - c
            index = base_my + o - 1
            arrived(weight(kind, layer, shard, part), ag_recv.at[unit, index], ag_send.at[unit, index])
            if split:
                for p in range(1, n_x):
                    index = base_mx + (o - 1) * (n_x - 1) + p - 1
                    piece = weight(kind, layer, shard, turn(x, n_x - p, n_x))
                    arrived(piece, ag_recv.at[unit, index], ag_send.at[unit, index])

    actions = {}

    def perform(names):
        for name in names:
            actions[name]()

    def at_place(place, *indices):
        for key, names in SCHEDULE.items():
            if key[0] != place:
                continue
            held = None
            for index, value in zip(indices, key[1:], strict=True):
                if not isinstance(index, int):
                    same = index == value
                    held = same if held is None else jnp.logical_and(held, same)
                elif index != value:
                    break
            else:
                if held is None:
                    perform(names)
                else:
                    pl.when(held)(functools.partial(perform, names))

    for unit in range(len(units)):
        actions[f"ws{unit}"] = functools.partial(weights_start, unit)
        actions[f"wf{unit}"] = functools.partial(weights_forward, unit)
        actions[f"wr{unit}"] = functools.partial(weights_pass, unit)
        actions[f"we{unit}"] = functools.partial(weights_whole, unit)

    lower = here.rep < n_rep // 2
    partner = here.to(z=turn(z, n_z // 2, n_z))
    back_parts = (
        pix.at[pl.ds(2, 2), pl.ds(0, TAIL)], pix.at[pl.ds(2, 2), pl.ds(TAIL, BLK - TAIL)]
    )
    given = (patches.at[pl.ds(KEPT, 2), pl.ds(0, TAIL)], patch_ends.at[pl.ds(KEPT, 2)])

    def local_half(half):
        pair = pl.ds(2 * half, 2)
        return (
            pltpu.make_async_copy(
                patches.at[pair, pl.ds(0, TAIL)], pix.at[pair, pl.ds(0, TAIL)],
                img_local.at[half],
            ),
            pltpu.make_async_copy(
                patch_ends.at[pair], pix.at[pair, pl.ds(TAIL, BLK - TAIL)],
                img_local.at[2 + half],
            ),
        )

    def marks(pair):
        row = lax.broadcasted_iota(jnp.int32, (32, 128), 0)
        found = jnp.full((32, 128), -1.0, F32)
        for index in range(2):
            slot = 2 * pair + index
            value = jnp.where(slot < counts[0], labels[slot], -1).astype(F32)
            found = jnp.where(row == CLS - TAIL + 16 * index, value, found)
        return found

    for unit in range(2):
        for copy in weights_copies(unit):
            copy.start()
    for copy in local_half(0):
        copy.start()
    pos_copy = pltpu.make_async_copy(pos_there, pos, own_local.at[0])
    head_copy = pltpu.make_async_copy(head_there, head, own_local.at[1])
    pos_copy.start()
    head_copy.start()
    lab[0] = marks(0)
    lab_given[...] = marks(2)
    weights_cast(0)
    pl.semaphore_wait(barrier, len(others))
    at_place("cast", 0)

    @pl.when(jnp.logical_not(lower))
    def _():
        for index in range(2):
            push(
                given[index], back_parts[index], img_send.at[index], img_recv.at[index],
                partner,
            )
        push(lab_given, lab.at[1], img_send.at[2], img_recv.at[2], partner)
        for copy in local_half(1):
            copy.start()
        lab[1] = marks(1)

    for unit in range(1, len(units)):
        weights_cast(unit)
        at_place("cast", unit)

    even = lane_mask(128, 0, 64)
    odd = lane_mask(128, 64, 128)
    low_lane = lax.broadcasted_iota(jnp.int32, (1, 128), 1) < 64
    key_lane = lax.broadcasted_iota(jnp.int32, (1, BLK), 1)
    key_row = jnp.where((key_lane < PATCHES) | (key_lane == CLS), 0.0, -1e30)
    key_sub = lax.broadcasted_iota(jnp.int32, (BLK, 1), 0)
    key_column = jnp.where((key_sub < PATCHES) | (key_sub == CLS), 0.0, -1e30)
    whole_lanes = NCLS // 128 * 128
    head_copy.wait()
    pos_copy.wait()
    low_head[:, 0:whole_lanes] = head[0:D, 0:whole_lanes].astype(BF)
    low_head[:, whole_lanes:] = jnp.zeros((D, CPAD - whole_lanes), BF)
    low_head[:, whole_lanes:NCLS] = head[0:D, whole_lanes:NCLS].astype(BF)
    head_bias[...] = jnp.zeros((1, CPAD), F32)
    head_bias[:, 0:NCLS] = head[D : D + 1, :]
    V[...] = jnp.zeros((VEC_ROWS, VEC_WIDE), F32)
    square_sum[...] = jnp.zeros((8, 128), F32)
    if small_block > block // 2:
        spare = small_block - block // 2
        GS[:, :, :, block // 2 :, :] = jnp.zeros((2, n_y, 2, spare, D), BF)
    zeros = jnp.zeros((8, D), F32)
    patch_bias = glob[0:1, :]

    def whole_lanes_of(tile):
        return jnp.concatenate([tile] * (D // 128), axis=1)

    def vector(layer, at, size):
        return vecs[pl.ds(layer, 1), at : at + size]

    def store_vector(layer, at, row):
        for piece in range(row.shape[-1] // D):
            V[pl.ds(VEC_AT + 12 * layer + at // D + piece, 1), 0:D] = row[
                :, piece * D : (piece + 1) * D
            ]

    def store_sums(layer, parts):
        for at, part in parts:
            store_vector(layer, at, down_sum(part))

    def embed(half):
        made = mm(pix[pl.ds(2 * half, 2)].reshape(HALF, PATCH_DIM), wp[...])
        for image in range(2):
            start = aligned(half * HALF + image * BLK, 16)
            for at, size in pieces(PATCHES - 4):
                X[pl.ds(start + at, size), :] = (
                    made[image * BLK + at : image * BLK + at + size]
                    + pos[1 + at : 1 + at + size, :]
                    + patch_bias
                )
            X[pl.ds(start + TAIL, 16), :] = jnp.zeros((16, D), F32)
            X[pl.ds(start + TAIL, 4), :] = (
                made[image * BLK + TAIL : image * BLK + PATCHES]
                + pos[1 + TAIL : 1 + PATCHES, :]
                + patch_bias
            )
            X[pl.ds(start + CLS, 1), :] = glob[1:2, :] + pos[0:1, :]

    def first_norm(layer, half, columns):
        base = half * HALF
        gain, shift = vector(layer, 0, D), vector(layer, D, D)
        for at, size in pieces(HALF):
            rows = pl.ds(aligned(base + at, 16), size)
            normed, inverse = norm(X[rows, :])
            N1[layer, rows, :] = normed.astype(BF)
            I1[layer, rows, :] = jnp.broadcast_to(inverse, (size, 128))
            DXB[rows, :] = (normed * gain + shift).astype(BF)
        rows = pl.ds(aligned(base, 16), HALF)
        h1 = DXB[rows, :]
        if len(columns) == 3:
            made = mm(h1, win[layer, :, 0 : 2 * D])
            QKV[layer, rows, 0:D] = (made[:, 0:D] + vector(layer, 2 * D, D)).astype(BF)
            QKV[layer, rows, D : 2 * D] = made[:, D:].astype(BF)
            made = mm(h1, win[layer, :, 2 * D : 3 * D])
            QKV[layer, rows, 2 * D :] = (made + vector(layer, 3 * D, D)).astype(BF)
        else:
            made = mm(h1, win[layer, :, D : 3 * D])
            DMB[rows, :] = made[:, 0:D].astype(BF)
            DA[rows, :] = (made[:, D:] + vector(layer, 3 * D, D)).astype(BF)

    lanes = 256
    fill = jnp.zeros((lanes - BLK, 128), BF)
    ones = jnp.full((lanes, 128), 1.0, BF)
    wide_lane = lax.broadcasted_iota(jnp.int32, (1, lanes), 1)
    wide_key_row = jnp.where((wide_lane < PATCHES) | (wide_lane == CLS), 0.0, -1e30)

    def fill_up(values):
        return jnp.concatenate([jnp.concatenate([values, fill], axis=0), ones], axis=1)

    def attend(layer, image):
        rows = pl.ds(aligned(image * BLK, 16), BLK)
        for pair in range(3):
            at = pair * 128
            query = QKV[layer, rows, at : at + 128] * BF(0.125)
            keys = QKV[layer, rows, D + at : D + at + 128]
            values = QKV[layer, rows, 2 * D + at : 2 * D + at + 128]
            both = jnp.concatenate([query * even, query * odd], axis=0)
            scores = mm_nt(both, jnp.concatenate([keys, fill], axis=0))
            probs = []
            for row, size in pieces(HALF):
                part = scores[row : row + size] + wide_key_row
                probs.append(jnp.exp(part - jnp.max(part, axis=-1, keepdims=True)).astype(BF))
            probs = jnp.concatenate(probs, axis=0)
            first = mm(probs[:BLK], fill_up(values * even))
            second = mm(probs[BLK:], fill_up(values * odd))
            made = first[:, :128] * (1.0 / first[:, 128:])
            made = made + second[:, :128] * (1.0 / second[:, 128:])
            ATT[layer, rows, at : at + 128] = made.astype(BF)

    def mlp(layer, half):
        base = half * HALF
        whole = pl.ds(aligned(base, 16), HALF)
        made = mm(ATT[layer, whole, :], win[layer, :, 3 * D : 4 * D])
        bias_out = vector(layer, 4 * D, D)
        gain, shift = vector(layer, 5 * D, D), vector(layer, 6 * D, D)
        for at, size in pieces(HALF):
            rows = pl.ds(aligned(base + at, 16), size)
            middle = X[rows, :] + made[at : at + size] + bias_out
            X[rows, :] = middle
            normed, inverse = norm(middle)
            N2[layer, rows, :] = normed.astype(BF)
            I2[layer, rows, :] = jnp.broadcast_to(inverse, (size, 128))
            DXB[rows, :] = (normed * gain + shift).astype(BF)
        at_place("mid", half, layer)
        at_place("b_up", half, layer)
        h2 = DXB[whole, :]
        for pair in range(2):
            made = mm(h2, win[layer, :, (4 + 2 * pair) * D : (6 + 2 * pair) * D])
            for tile in range(2):
                start = (2 * pair + tile) * D
                columns = slice(start, start + D)
                bias = vector(layer, 7 * D + start, D)
                for at, size in pieces(HALF):
                    rows = pl.ds(aligned(base + at, 16), size)
                    active, slope = gelu_parts(
                        made[at : at + size, tile * D : (tile + 1) * D] + bias
                    )
                    ACT[layer, rows, columns] = active.astype(BF)
                    SLOPE[layer, rows, columns] = slope.astype(BF)
        at_place("up", half, layer)
        at_place("b_down", half, layer)
        made = mm(ACT[layer, whole, :], wdn[layer])
        bias = vector(layer, 7 * D + FF, D)
        for at, size in pieces(HALF):
            rows = pl.ds(aligned(base + at, 16), size)
            X[rows, :] = X[rows, :] + made[at : at + size] + bias
        at_place("down", half, layer)

    at_place("b_start")

    def forward_half(half, carry):
        @pl.when(half == 0)
        def _():
            for copy in local_half(0):
                copy.wait()

        @pl.when(jnp.logical_and(half == 1, lower))
        def _():
            for index in range(2):
                arrived(back_parts[index], img_recv.at[index], img_send.at[index])

        @pl.when(jnp.logical_and(half == 1, jnp.logical_not(lower)))
        def _():
            for copy in local_half(1):
                copy.wait()

        embed(half)
        at_place("embed", half)

        def forward_layer(layer, inner):
            at_place("b_norm", half, layer)
            first_norm(layer, half, (0, 1, 2))
            at_place("norm", half, layer)

            def attend_one(index, nothing):
                attend(layer, 2 * half + index)
                at_place("att", half, layer, index)
                return nothing

            lax.fori_loop(0, 2, attend_one, 0)
            mlp(layer, half)
            return inner

        return lax.fori_loop(0, LAYERS - 1, forward_layer, carry)

    lax.fori_loop(0, 2, forward_half, 0)
    at_place("b_last")

    last = LAYERS - 1

    def last_norm(half, nothing):
        first_norm(last, half, (1, 2))
        at_place("ln", half)
        return nothing

    lax.fori_loop(0, 2, last_norm, 0)

    fac = ("f", f_send, f_recv)
    f_y, f_z = 1, n_y
    f_x = f_z + n_z - 1
    f_v = f_x + n_x - 1
    f_m = f_v + n_y - 1
    part_wide = WFAC // n_y
    group = KEPT * n_shard

    def factors_core():
        go(lambda: FAC.at[1 - c], FC, fac, 0, mate)

    def factors_y():
        arrived(FC, f_recv.at[0], f_send.at[0])
        FAC[c] = FAC[c] + FC[...]
        for o in range(1, n_y):
            go(
                lambda o=o: FAC.at[c, turn(y, o, n_y)], FY.at[o - 1], fac, f_y + o - 1,
                here.to(y=turn(y, o, n_y)),
            )

    def line_factors(z_at, x_at):
        return all_factors.at[c, y, x_at, z_at]

    def factors_z():
        total = FAC[c, y]
        for o in range(1, n_y):
            arrived(FY.at[o - 1], f_recv.at[f_y + o - 1], f_send.at[f_y + o - 1])
            total = total + FY[o - 1]
        FC[0] = total
        pltpu.make_async_copy(FC.at[0], line_factors(z, x), out_local.at[0]).start()
        for o in range(1, n_z):
            go(
                lambda: FC.at[0], line_factors(z, x), fac, f_z + o - 1,
                here.to(z=turn(z, o, n_z)),
            )

    def factors_x():
        for o in range(1, n_z):
            index = f_z + o - 1
            arrived(line_factors(turn(z, n_z - o, n_z), x), f_recv.at[index], f_send.at[index])
        pltpu.make_async_copy(FC.at[0], line_factors(z, x), out_local.at[0]).wait()
        for o in range(1, n_x):
            go(
                lambda: all_factors.at[c, y, x], all_factors.at[c, y, x], fac, f_x + o - 1,
                here.to(x=turn(x, o, n_x)),
            )

    def factors_side():
        for o in range(1, n_x):
            index = f_x + o - 1
            came = all_factors.at[c, y, turn(x, n_x - o, n_x)]
            arrived(came, f_recv.at[index], f_send.at[index])
        for o in range(1, n_y):
            go(
                lambda: all_factors.at[c, y], all_factors.at[c, y], fac, f_v + o - 1,
                here.to(y=turn(y, o, n_y)),
            )

    def factors_mate():
        for o in range(1, n_y):
            index = f_v + o - 1
            came = all_factors.at[c, turn(y, n_y - o, n_y)]
            arrived(came, f_recv.at[index], f_send.at[index])
        go(lambda: all_factors.at[c], all_factors.at[c], fac, f_m, mate)

    def factors_done():
        arrived(all_factors.at[1 - c], f_recv.at[f_m], f_send.at[f_m])

    rs = ("rs", rs_send, rs_recv)
    r_y, r_x = 1, n_y
    r_z = r_x + n_x - 1
    r_gz = r_z + n_z - 1
    r_gx = r_gz + n_z - 1

    def chunk(k):
        if k < CHUNKS:
            slot = k % 3
            return (
                G.at[k], RC.at[slot], RY.at[slot], RX.at[slot], RZ.at[slot], RES.at[k], block
            )
        k = k - CHUNKS
        return GS.at[k], SC.at[0], SY.at[0], SX.at[0], SZ.at[0], SRES.at[k], small_block

    def splits(rows):
        by_x = cut(rows, n_x, 16)
        by_z = cut(rows // by_x, n_z, 16)
        return by_x, rows // by_x, by_z, rows // by_x // by_z

    def step_of(rows, most=192):
        return max(step for step in range(16, most + 1, 16) if rows % step == 0)

    def add_rows(rows, target, target_at, sources):
        step = step_of(rows)

        def one(index, nothing):
            at = index * step
            to = pl.ds(aligned(target_at + at, 16), step)
            total = target[to, :]
            if len(sources) == 1:
                total = total + sources[0][pl.ds(aligned(at, 16), step), :]
            else:
                total = total.astype(F32)
                for source in sources:
                    total = total + source[pl.ds(aligned(at, 16), step), :].astype(F32)
                total = total.astype(BF)
            target[to, :] = total
            return nothing

        lax.fori_loop(0, rows // step, one, 0)

    def reduce_core(k):
        g, rc = chunk(k)[0:2]
        go(lambda: chunk(k)[0].at[:, 1 - c], rc, rs, (k, 0), mate)

    def reduce_y(k):
        g, rc, ry, _, _, _, rows = chunk(k)
        arrived(rc, rs_recv.at[k, 0], rs_send.at[k, 0])
        for o in list(range(1, n_y)) + [0]:
            at = turn(y, o, n_y)
            add_rows(rows, g.at[at, c], 0, [rc.at[at]])
            if o:
                go(
                    lambda o=o: chunk(k)[0].at[turn(y, o, n_y), c], ry.at[o - 1], rs,
                    (k, r_y + o - 1), here.to(y=at),
                )

    def total_of(slots, count, at, step):
        total = None
        for index in range(count):
            value = slots[index, pl.ds(aligned(at, 16), step), :].astype(F32)
            total = value if total is None else total + value
        return total

    def reduce_x(k):
        g, _, ry, rx, _, _, rows = chunk(k)
        by_x, rows_x = splits(rows)[0:2]
        for o in range(1, n_y):
            arrived(ry.at[o - 1], rs_recv.at[k, r_y + o - 1], rs_send.at[k, r_y + o - 1])
        mine = g.at[y, c]
        add_rows(rows, mine, 0, [ry.at[o - 1] for o in range(1, n_y)])
        for o in range(1, n_x):
            to = turn(x, o, n_x)
            if by_x > 1:

                def make(o=o):
                    at = turn(x, o, n_x) * rows_x
                    return chunk(k)[0].at[y, c, pl.ds(aligned(at, 16), rows_x), :]

                go(make, rx.at[o - 1], rs, (k, r_x + o - 1), here.to(x=to))
            else:
                go(lambda: chunk(k)[0].at[y, c], rx.at[x], rs, (k, r_x + o - 1), here.to(x=to))

    def reduce_z(k):
        g, _, _, rx, rz, _, rows = chunk(k)
        by_x, rows_x, by_z, rows_z = splits(rows)
        mine = g.at[y, c]
        for o in range(1, n_x):
            slot = rx.at[o - 1] if by_x > 1 else rx.at[turn(x, n_x - o, n_x)]
            arrived(slot, rs_recv.at[k, r_x + o - 1], rs_send.at[k, r_x + o - 1])
        if by_x > 1:
            start = x * rows_x
            add_rows(rows_x, mine, start, [rx.at[o - 1] for o in range(1, n_x)])
        else:
            start = 0
            rx[x] = mine[...]
            for o in range(1, n_x):
                gone(rs, (k, r_x + o - 1))
            step = step_of(rows)

            def one(index, nothing):
                at = pl.ds(aligned(index * step, 16), step)
                g[y, c, at, :] = total_of(rx, n_x, index * step, step).astype(BF)
                return nothing

            lax.fori_loop(0, rows // step, one, 0)
        for o in range(1, n_z):

            def make(o=o):
                at = x * rows_x if by_x > 1 else 0
                if by_z > 1:
                    at = at + turn(z, o, n_z) * rows_z
                return chunk(k)[0].at[y, c, pl.ds(aligned(at, 16), rows_z), :]

            slot = rz.at[o - 1] if by_z > 1 else rz.at[z]
            go(make, slot, rs, (k, r_z + o - 1), here.to(z=turn(z, o, n_z)))

    def gather_z(k):
        g, _, _, _, rz, res, rows = chunk(k)
        by_x, rows_x, by_z, rows_z = splits(rows)
        start = x * rows_x if by_x > 1 else 0
        if by_z > 1:
            start = start + z * rows_z
        for o in range(1, n_z):
            slot = rz.at[o - 1] if by_z > 1 else rz.at[turn(z, n_z - o, n_z)]
            arrived(slot, rs_recv.at[k, r_z + o - 1], rs_send.at[k, r_z + o - 1])
        own_slot = n_z - 1 if by_z > 1 else z
        rz[own_slot] = g[y, c, pl.ds(aligned(start, 16), rows_z), :]
        share = 1.0 / ((1 if by_x > 1 else n_x) * (1 if by_z > 1 else n_z))
        step = step_of(rows_z, 96)

        def one(index, total):
            low = total_of(rz, n_z, index * step, step).astype(BF)
            res[pl.ds(aligned(start + index * step, 16), step), :] = low
            wide = low.astype(F32)
            return total + fold(wide * wide)

        total = lax.fori_loop(0, rows_z // step, one, zeros) * share
        for at in range(0, D, 128):
            square_sum[...] = square_sum[...] + total[:, at : at + 128]
        if by_z > 1:

            def make():
                at = x * rows_x if by_x > 1 else 0
                return chunk(k)[5].at[pl.ds(aligned(at + z * rows_z, 16), rows_z), :]

            for o in range(1, n_z):
                go(make, make(), rs, (k, r_gz + o - 1), here.to(z=turn(z, o, n_z)))

    def gather_x(k):
        res, rows = chunk(k)[5:7]
        by_x, rows_x, by_z, rows_z = splits(rows)
        if by_z > 1:
            for o in range(1, n_z):
                start = turn(z, n_z - o, n_z) * rows_z
                if by_x > 1:
                    start = start + x * rows_x
                arrived(
                    res.at[pl.ds(aligned(start, 16), rows_z), :],
                    rs_recv.at[k, r_gz + o - 1], rs_send.at[k, r_gz + o - 1],
                )
        if by_x > 1:

            def make():
                return chunk(k)[5].at[pl.ds(aligned(x * rows_x, 16), rows_x), :]

            for o in range(1, n_x):
                go(make, make(), rs, (k, r_gx + o - 1), here.to(x=turn(x, o, n_x)))

    def result(k):
        if k < CHUNKS:
            return pltpu.make_async_copy(RES.at[k], res_out.at[k], out_local.at[1 + k])
        return pltpu.make_async_copy(
            SRES.at[k - CHUNKS], small_out.at[k - CHUNKS], out_local.at[1 + k]
        )

    def gather_done(k):
        res, rows = chunk(k)[5:7]
        by_x, rows_x = splits(rows)[0:2]
        if by_x > 1:
            for o in range(1, n_x):
                start = turn(x, n_x - o, n_x) * rows_x
                arrived(
                    res.at[pl.ds(aligned(start, 16), rows_x), :],
                    rs_recv.at[k, r_gx + o - 1], rs_send.at[k, r_gx + o - 1],
                )
        result(k).start()

    for k in range(CHUNKS + 2):
        actions[f"core{k}"] = functools.partial(reduce_core, k)
        actions[f"y{k}"] = functools.partial(reduce_y, k)
        actions[f"x{k}"] = functools.partial(reduce_x, k)
        actions[f"z{k}"] = functools.partial(reduce_z, k)
        actions[f"gz{k}"] = functools.partial(gather_z, k)
        actions[f"gx{k}"] = functools.partial(gather_x, k)
        actions[f"gd{k}"] = functools.partial(gather_done, k)
    actions.update(
        fc=factors_core, fy=factors_y, fz=factors_z, fx=factors_x, fv=factors_side,
        fm=factors_mate, fd=factors_done,
    )

    def tails(ref, layer=None):
        found = []
        for image in range(KEPT):
            rows = slice(image * BLK + TAIL, (image + 1) * BLK)
            found.append(ref[rows, :] if layer is None else ref[layer, rows, :])
        return jnp.concatenate(found, axis=0)

    @pl.when(lower)
    def _():
        arrived(lab.at[1], img_recv.at[2], img_send.at[2])

    marked = lab[...].reshape(CROWS, 128)[:, 0:1]

    h1 = tails(DXB)
    stream = tails(X)
    query = ((mm(h1, win[last, :, 0:D]) + vector(last, 2 * D, D)).astype(BF)) * BF(0.125)
    head_masks = [lane_mask(D, index * 64, (index + 1) * 64) for index in range(HEADS)]

    def spread(values):
        return jnp.concatenate([values * mask for mask in head_masks], axis=0)

    def gather_heads(values):
        total = None
        for index in range(HEADS):
            part = values[index * 16 : (index + 1) * 16] * head_masks[index].astype(F32)
            total = part if total is None else total + part
        return total

    spread_queries, probabilities, outs = [], [], []
    for image in range(KEPT):
        rows = slice(image * BLK, (image + 1) * BLK)
        queries = spread(query[image * 16 : (image + 1) * 16])
        scores = mm_nt(queries, DMB[rows, :]) + key_row
        raw = jnp.exp(scores - jnp.max(scores, axis=-1, keepdims=True))
        probs = raw * (1.0 / jnp.sum(raw, axis=-1, keepdims=True))
        spread_queries.append(queries)
        probabilities.append(probs)
        outs.append(gather_heads(mm(probs.astype(BF), DA[rows, :])))
    attended = jnp.concatenate(outs, axis=0).astype(BF)
    middle = stream + mm(attended, win[last, :, 3 * D : 4 * D]) + vector(last, 4 * D, D)
    n2, i2 = norm(middle)
    h2 = (n2 * vector(last, 5 * D, D) + vector(last, 6 * D, D)).astype(BF)
    active, slope = gelu_parts(mm(h2, win[last, :, 4 * D :]) + vector(last, 7 * D, FF))
    active = active.astype(BF)
    top = middle + mm(active, wdn[last]) + vector(last, 7 * D + FF, D)
    gain_final = glob[2:3, :]
    nf, inf = norm(top)
    final = (nf * gain_final + glob[3:4, :]).astype(BF)
    class_lane = lax.broadcasted_iota(jnp.int32, (1, CPAD), 1)
    logits = mm(final, low_head[...]) + head_bias[...]
    logits = jnp.where(class_lane < NCLS, logits, -1e30)
    peak = jnp.max(logits, axis=-1, keepdims=True)
    shifted = logits - peak
    raw = jnp.exp(shifted)
    total = jnp.sum(raw, axis=-1, keepdims=True)
    alive = jnp.where(marked >= 0.0, 1.0, 0.0)
    target = jnp.where(class_lane.astype(F32) == marked, 1.0 - SMOOTHING, 0.0) + jnp.where(
        class_lane < NCLS, SMOOTHING / NCLS, 0.0
    )
    log_probs = jnp.where(class_lane < NCLS, shifted - jnp.log(total), 0.0)
    losses = -jnp.sum(target * log_probs, axis=-1, keepdims=True) * alive
    d_logits = ((raw * (1.0 / total) - target) * alive).astype(BF)
    d_final = mm_nt(d_logits, low_head[...])
    last_row = VEC_AT + 12 * LAYERS
    V[last_row : last_row + 1, 0:D] = down_sum(d_final * nf)
    V[last_row + 1 : last_row + 2, 0:D] = down_sum(d_final)
    V[last_row + 2 : last_row + 3, 0:128] = jnp.broadcast_to(down_sum(losses), (1, 128))
    V[last_row + 3 : last_row + 4, 0:128] = jnp.full((1, 128), counts[0].astype(F32), F32)
    d_top = norm_back(d_final, nf, inf, gain_final)
    low_top = d_top.astype(BF)
    store_vector(last, 7 * D + FF, down_sum(d_top))
    d_up = (mm_nt(low_top, wdn[last]) * slope).astype(BF)
    store_vector(last, 7 * D, down_sum(d_up.astype(F32)))
    d_h2 = mm_nt(d_up, win[last, :, 4 * D :])
    store_vector(last, 5 * D, down_sum(d_h2 * n2))
    store_vector(last, 6 * D, down_sum(d_h2))
    d_middle = d_top + norm_back(d_h2, n2, i2, vector(last, 5 * D, D))
    low_middle = d_middle.astype(BF)
    store_vector(last, 4 * D, down_sum(d_middle))
    d_heads = mm_nt(low_middle, win[last, :, 3 * D : 4 * D]).astype(BF)
    d_queries = []
    for image in range(KEPT):
        rows = slice(image * BLK, (image + 1) * BLK)
        ups = spread(d_heads[image * 16 : (image + 1) * 16])
        probs = probabilities[image]
        d_probs = mm_nt(ups, DA[rows, :])
        inner = jnp.sum(d_probs * probs, axis=-1, keepdims=True)
        d_scores = (probs * (d_probs - inner)).astype(BF)
        d_queries.append(gather_heads(mm(d_scores, DMB[rows, :])) * 0.125)
        DMB[rows, :] = mm_tn(d_scores, spread_queries[image]).astype(BF)
        DA[rows, :] = mm_tn(probs.astype(BF), ups).astype(BF)
    d_query = jnp.concatenate(d_queries, axis=0).astype(BF)
    store_vector(last, 2 * D, down_sum(d_query.astype(F32)))
    from_query = mm_nt(d_query, win[last, :, 0:D])

    pick_row = lax.broadcasted_iota(jnp.int32, (group, CROWS), 0)
    pick_lane = lax.broadcasted_iota(jnp.int32, (group, CROWS), 1)
    pick = jnp.where(
        ((pick_row - KEPT * here.shard) * 16 + (CLS - TAIL)) == pick_lane, 1.0, 0.0
    ).astype(BF)
    def keep_factors(half, pieces_of):
        at = 0
        for piece in pieces_of:
            made = None if piece is None else mm(pick, piece).astype(BF)
            for lane in range(0, WFAC - at if made is None else made.shape[-1], 128):
                part, column = divmod(at + lane, part_wide)
                FAC[half, part, :, column : column + 128] = (
                    jnp.zeros((group, 128), BF) if made is None else made[:, lane : lane + 128]
                )
            at += 0 if made is None else made.shape[-1]

    keep_factors(0, (active, h2, attended, h1, final, low_top, None))
    keep_factors(1, (d_up, low_middle, d_query, d_logits, None))
    at_place("class")

    turned = DXB[...].T
    for tile, grads in enumerate((DMB, DA)):
        made = mm(turned, grads[...]).astype(BF)
        for shard in range(n_shard):
            GS[0, shard // 2, shard % 2, tile * rows_in : (tile + 1) * rows_in, :] = made[
                shard * rows_in : (shard + 1) * rows_in
            ]
    at_place("kv")
    store_sums(last, [(3 * D, fold(DA[...].astype(F32)))])

    X[...] = jnp.zeros((ROWS, D), F32)
    gain = vector(last, 0, D)
    gain_sum, shift_sum = zeros, zeros
    for image in range(KEPT):
        rows = slice(image * BLK + TAIL, (image + 1) * BLK)
        part = from_query[image * 16 : (image + 1) * 16]
        normed = N1[last, rows, :].astype(F32)
        gain_sum = gain_sum + fold(part * normed)
        shift_sum = shift_sum + fold(part)
        X[rows, :] = d_middle[image * 16 : (image + 1) * 16] + norm_back(
            part, normed, whole_lanes_of(I1[last, rows, :]), gain
        )

    def first_back(layer, half, made, sums):
        base = half * HALF
        gain = vector(layer, 0, D)
        gain_sum, shift_sum = sums
        for at, size in pieces(HALF):
            rows = pl.ds(aligned(base + at, 16), size)
            part = made[at : at + size]
            normed = N1[layer, rows, :].astype(F32)
            inverse = whole_lanes_of(I1[layer, rows, :])
            gain_sum = gain_sum + fold(part * normed)
            shift_sum = shift_sum + fold(part)
            X[rows, :] = X[rows, :] + norm_back(part, normed, inverse, gain)
        return gain_sum, shift_sum

    def last_back(half, sums):
        rows = pl.ds(aligned(half * HALF, 16), HALF)
        made = mm_nt(DMB[rows, :], win[last, :, D : 2 * D])
        made = made + mm_nt(DA[rows, :], win[last, :, 2 * D : 3 * D])
        sums = first_back(last, half, made, sums)
        at_place("lb", half)
        return sums

    gain_sum, shift_sum = lax.fori_loop(0, 2, last_back, (gain_sum, shift_sum))
    store_sums(last, [(0, gain_sum), (D, shift_sum)])

    def round_up(half, total):
        for at, size in pieces(HALF):
            rows = pl.ds(aligned(half * HALF + at, 16), size)
            up = X[rows, :]
            DXB[rows, :] = up.astype(BF)
            total = total + fold(up)
        return total

    def act_back(layer, half, totals):
        base = half * HALF
        low = DXB[pl.ds(aligned(base, 16), HALF), :]
        ups = []
        for pair in range(2):
            made = mm_nt(low, wdn[layer, 2 * pair * D : 2 * (pair + 1) * D, :])
            for tile in range(2):
                start = (2 * pair + tile) * D
                columns = slice(start, start + D)
                total = totals[2 * pair + tile]
                for at, size in pieces(HALF):
                    rows = pl.ds(aligned(base + at, 16), size)
                    part = made[at : at + size, tile * D : (tile + 1) * D]
                    grad = (part * SLOPE[layer, rows, columns].astype(F32)).astype(BF)
                    DH[rows, columns] = grad
                    total = total + fold(grad.astype(F32))
                ups.append(total)
        return tuple(ups)

    def mlp_back(layer, half, sums):
        base = half * HALF
        whole = pl.ds(aligned(base, 16), HALF)
        gain_sum, shift_sum, bias_out = sums
        made = mm_nt(DH[whole, :], win[layer, :, 4 * D :])
        gain = vector(layer, 5 * D, D)
        for at, size in pieces(HALF):
            rows = pl.ds(aligned(base + at, 16), size)
            part = made[at : at + size]
            normed = N2[layer, rows, :].astype(F32)
            inverse = whole_lanes_of(I2[layer, rows, :])
            gain_sum = gain_sum + fold(part * normed)
            shift_sum = shift_sum + fold(part)
            grad = X[rows, :] + norm_back(part, normed, inverse, gain)
            X[rows, :] = grad
            DMB[rows, :] = grad.astype(BF)
            bias_out = bias_out + fold(grad)
        DA[whole, :] = mm_nt(DMB[whole, :], win[layer, :, 3 * D : 4 * D]).astype(BF)
        return gain_sum, shift_sum, bias_out

    def attend_back(layer, image):
        rows = pl.ds(aligned(image * BLK, 16), BLK)
        for pair in range(3):
            at = pair * 128
            query = QKV[layer, rows, at : at + 128] * BF(0.125)
            keys = QKV[layer, rows, D + at : D + at + 128]
            values = QKV[layer, rows, 2 * D + at : 2 * D + at + 128]
            ups = DA[rows, at : at + 128]
            keys_both = jnp.concatenate([keys * even, keys * odd], axis=0)
            values_both = jnp.concatenate([values * even, values * odd], axis=0)
            query = jnp.concatenate([query, fill], axis=0)
            ups = jnp.concatenate([ups, fill], axis=0)
            scores = mm_nt(keys_both, query)
            d_probs = mm_nt(values_both, ups)
            probs, d_scores = [], []
            for base in (0, BLK):
                low_probs, low_grads = [], []
                for first, end in ((0, 128), (128, lanes)):
                    part = jnp.concatenate(
                        [
                            scores[base : base + TAIL, first:end],
                            scores[base + TAIL : base + BLK, first:end] + key_column[TAIL:],
                        ],
                        axis=0,
                    )
                    raw = jnp.exp(part - jnp.max(part, axis=0, keepdims=True))
                    prob = raw * (1.0 / jnp.sum(raw, axis=0, keepdims=True))
                    grad = d_probs[base : base + BLK, first:end]
                    inner = jnp.sum(grad * prob, axis=0, keepdims=True)
                    low_grads.append((prob * (grad - inner)).astype(BF))
                    low_probs.append(prob.astype(BF))
                probs.append(jnp.concatenate(low_probs, axis=1))
                d_scores.append(jnp.concatenate(low_grads, axis=1))
            probs = jnp.concatenate(probs, axis=0)
            d_scores = jnp.concatenate(d_scores, axis=0)
            d_values = mm(probs, ups)
            d_keys = mm(d_scores, query)
            d_query = mm_tn(d_scores, keys_both)[:BLK] * 0.125
            DH[rows, at : at + 128] = d_query.astype(BF)
            DH[rows, D + at : D + at + 128] = jnp.where(
                low_lane, d_keys[:BLK], d_keys[BLK:]
            ).astype(BF)
            DH[rows, 2 * D + at : 2 * D + at + 128] = jnp.where(
                low_lane, d_values[:BLK], d_values[BLK:]
            ).astype(BF)

    def renew(ref, layer, at):
        gain, shift = vector(layer, at, D), vector(layer, at + D, D)

        def one(index, nothing):
            for at, size in pieces(BLK):
                rows = pl.ds(aligned(index * BLK + at, 16), size)
                DXB[rows, :] = (ref[layer, rows, :].astype(F32) * gain + shift).astype(BF)
            return nothing

        lax.fori_loop(0, KEPT, one, 0)
        return DXB[...].T

    def keep_in(k, tile, made):
        for shard in range(n_shard):
            G[k, shard // 2, shard % 2, tile * rows_in : (tile + 1) * rows_in, :] = made[
                shard * rows_in : (shard + 1) * rows_in
            ]

    def backward(step, carry):
        layer = LAYERS - 2 - step
        kd, ku, kq = 3 * step, 3 * step + 1, 3 * step + 2
        bias_down = lax.fori_loop(0, 2, round_up, zeros)
        at_place("round", layer)
        turned = DXB[...].T
        per = min(rows_down, D)
        for pair in range(2):
            start = 2 * pair * D
            wide = mm(turned, ACT[layer, :, start : start + 2 * D]).astype(BF)
            for tile in range(2):
                made = wide[:, tile * D : (tile + 1) * D].T
                for piece in range(D // per):
                    shard, at = divmod(start + tile * D + piece * per, rows_down)
                    G[kd, shard // 2, shard % 2, at : at + per, :] = made[
                        piece * per : (piece + 1) * per
                    ]
        at_place("dn", layer)

        def one(half, totals):
            totals = act_back(layer, half, totals)
            at_place("act", layer, half)
            return totals

        bias_up = lax.fori_loop(0, 2, one, (zeros,) * 4)
        turned = renew(N2, layer, 5 * D)
        for pair in range(2):
            made = mm(turned, DH[:, 2 * pair * D : 2 * (pair + 1) * D]).astype(BF)
            keep_in(ku, 2 * pair, made[:, :D])
            keep_in(ku, 2 * pair + 1, made[:, D:])
        at_place("ups", layer)

        def one_more(half, sums):
            sums = mlp_back(layer, half, sums)
            at_place("mlpb", layer, half)
            return sums

        gain_sum, shift_sum, bias_out = lax.fori_loop(0, 2, one_more, (zeros, zeros, zeros))
        store_sums(
            layer,
            [(7 * D + FF, bias_down), (5 * D, gain_sum), (6 * D, shift_sum), (4 * D, bias_out)]
            + [(7 * D + tile * D, bias_up[tile]) for tile in range(4)],
        )
        keep_in(kq, 3, mm(ATT[layer].T, DMB[...]).astype(BF))
        at_place("out", layer)

        def two(image, nothing):
            attend_back(layer, image)
            at_place("attb", layer, image)
            return nothing

        lax.fori_loop(0, KEPT, two, 0)
        turned = renew(N1, layer, 0)
        made = mm(turned, DH[:, 0 : 2 * D]).astype(BF)
        keep_in(kq, 0, made[:, :D])
        keep_in(kq, 1, made[:, D:])
        keep_in(kq, 2, mm(turned, DH[:, 2 * D : 3 * D]).astype(BF))
        at_place("qkv", layer)
        store_sums(
            layer,
            [
                (2 * D, fold(DH[:, 0:D].astype(F32))),
                (3 * D, fold(DH[:, 2 * D : 3 * D].astype(F32))),
            ],
        )

        def three(half, sums):
            rows = pl.ds(aligned(half * HALF, 16), HALF)
            made = mm_nt(DH[rows, 0 : 3 * D], win[layer, :, 0 : 3 * D])
            sums = first_back(layer, half, made, sums)
            at_place("fb", layer, half)
            return sums

        gain_sum, shift_sum = lax.fori_loop(0, 2, three, (zeros, zeros))
        store_sums(layer, [(0, gain_sum), (D, shift_sum)])
        return carry

    lax.fori_loop(0, LAYERS - 1, backward, 0)

    for at, size in pieces(BLK):
        total = None
        for image in range(KEPT):
            part = X[image * BLK + at : image * BLK + at + size, :]
            DXB[image * BLK + at : image * BLK + at + size, :] = part.astype(BF)
            total = part if total is None else total + part
        V[at : at + size, 0:D] = total

    vec = ("v", v_send, v_recv)
    v_y, v_x = 1, n_y
    v_z = v_x + n_x - 1
    v_gz = v_z + n_z - 1
    v_gx = v_gz + n_z - 1
    v_gy = v_gx + n_x - 1
    v_gc = v_gy + n_y - 1
    rows_c = VEC_ROWS // 2
    rows_y = rows_c // n_y
    rows_x = rows_y // n_x
    split_z = cut(rows_x, n_z, 8)
    rows_z = rows_x // split_z
    at_c = c * rows_c
    at_y = at_c + y * rows_y
    at_x = at_y + x * rows_x
    at_z = at_x + z * rows_z if split_z > 1 else at_x

    def vrows(ref, at, rows):
        return ref.at[pl.ds(aligned(at, 8), rows), :]

    def vadd(at, rows, sources):
        target = pl.ds(aligned(at, 8), rows)
        total = V[target, :]
        for source in sources:
            total = total + source
        V[target, :] = total

    def vectors_core():
        go(lambda: vrows(V, (1 - c) * rows_c, rows_c), VC, vec, 0, mate)

    def vectors_y():
        arrived(VC, v_recv.at[0], v_send.at[0])
        vadd(at_c, rows_c, [VC[...]])
        for o in range(1, n_y):
            to = turn(y, o, n_y)
            go(
                lambda o=o: vrows(V, at_c + turn(y, o, n_y) * rows_y, rows_y), VY.at[o - 1],
                vec, v_y + o - 1, here.to(y=to),
            )

    def vectors_x():
        for o in range(1, n_y):
            arrived(VY.at[o - 1], v_recv.at[v_y + o - 1], v_send.at[v_y + o - 1])
        vadd(at_y, rows_y, [VY[o - 1] for o in range(1, n_y)])
        for o in range(1, n_x):
            to = turn(x, o, n_x)
            go(
                lambda o=o: vrows(V, at_y + turn(x, o, n_x) * rows_x, rows_x), VX.at[o - 1],
                vec, v_x + o - 1, here.to(x=to),
            )

    def vectors_z():
        for o in range(1, n_x):
            arrived(VX.at[o - 1], v_recv.at[v_x + o - 1], v_send.at[v_x + o - 1])
        vadd(at_x, rows_x, [VX[o - 1] for o in range(1, n_x)])
        for o in range(1, n_z):

            def make(o=o):
                at = at_x + turn(z, o, n_z) * rows_z if split_z > 1 else at_x
                return vrows(V, at, rows_z)

            go(make, VZ.at[z], vec, v_z + o - 1, here.to(z=turn(z, o, n_z)))

    def vectors_gather_z():
        for o in range(1, n_z):
            arrived(
                VZ.at[turn(z, n_z - o, n_z)], v_recv.at[v_z + o - 1], v_send.at[v_z + o - 1]
            )
        target = pl.ds(aligned(at_z, 8), rows_z)
        VZ[z] = V[target, :]
        total = VZ[0]
        for index in range(1, n_z):
            total = total + VZ[index]
        VF[target, :] = total
        if split_z > 1:
            for o in range(1, n_z):
                go(
                    lambda: vrows(VF, at_z, rows_z), vrows(VF, at_z, rows_z), vec, v_gz + o - 1,
                    here.to(z=turn(z, o, n_z)),
                )

    def vectors_gather_x():
        if split_z > 1:
            for o in range(1, n_z):
                came = turn(z, n_z - o, n_z)
                arrived(
                    vrows(VF, at_x + came * rows_z, rows_z), v_recv.at[v_gz + o - 1],
                    v_send.at[v_gz + o - 1],
                )
        for o in range(1, n_x):
            go(
                lambda: vrows(VF, at_x, rows_x), vrows(VF, at_x, rows_x), vec, v_gx + o - 1,
                here.to(x=turn(x, o, n_x)),
            )

    sq = ("q", q_send, q_recv)

    def squares_z():
        SQ[0] = square_sum[...]
        SQZ[z] = square_sum[...]
        for o in range(1, n_z):
            go(lambda: SQ.at[0], SQZ.at[z], sq, o - 1, here.to(z=turn(z, o, n_z)))

    def slot_of(i, j, k):
        return (i * n_y + j) * 2 + k

    def squares_plane():
        for o in range(1, n_z):
            arrived(SQZ.at[turn(z, n_z - o, n_z)], q_recv.at[o - 1], q_send.at[o - 1])
        total = SQZ[0]
        for index in range(1, n_z):
            total = total + SQZ[index]
        SQ[1] = total
        SQP[slot_of(x, y, c)] = total
        for index, step in enumerate(plane):
            go(
                lambda: SQ.at[1], SQP.at[slot_of(x, y, c)], sq, n_z - 1 + index,
                in_plane(step),
            )

    def squares_done():
        for index, (i, j, k) in enumerate(plane):
            slot = slot_of(
                turn(x, n_x - i, n_x), turn(y, n_y - j, n_y), lax.rem(c + k, 2)
            )
            arrived(SQP.at[slot], q_recv.at[n_z - 1 + index], q_send.at[n_z - 1 + index])
        total = SQP[0]
        for index in range(1, 2 * n_x * n_y):
            total = total + SQP[index]
        SQ[2] = total

    def vectors_gather_y():
        for o in range(1, n_x):
            at = at_y + turn(x, n_x - o, n_x) * rows_x
            arrived(vrows(VF, at, rows_x), v_recv.at[v_gx + o - 1], v_send.at[v_gx + o - 1])
        for o in range(1, n_y):
            go(
                lambda: vrows(VF, at_y, rows_y), vrows(VF, at_y, rows_y), vec, v_gy + o - 1,
                here.to(y=turn(y, o, n_y)),
            )

    def vectors_gather_core():
        for o in range(1, n_y):
            at = at_c + turn(y, n_y - o, n_y) * rows_y
            arrived(vrows(VF, at, rows_y), v_recv.at[v_gy + o - 1], v_send.at[v_gy + o - 1])
        go(lambda: vrows(VF, at_c, rows_c), vrows(VF, at_c, rows_c), vec, v_gc, mate)

    def vectors_done():
        arrived(vrows(VF, (1 - c) * rows_c, rows_c), v_recv.at[v_gc], v_send.at[v_gc])

    actions.update(
        vc=vectors_core, vy=vectors_y, vx=vectors_x, vz=vectors_z, vgz=vectors_gather_z,
        vgx=vectors_gather_x, vgy=vectors_gather_y, vgc=vectors_gather_core, vd=vectors_done,
        qz=squares_z, qp=squares_plane, qd=squares_done,
    )
    at_place("emb")
    low = DXB[...]
    for tile in range(2):
        made = mm_tn(pix[:, :, tile * D : (tile + 1) * D].reshape(ROWS, D), low).astype(BF)
        for piece in range(D // rows_patch):
            shard = tile * (D // rows_patch) + piece
            GS[1, shard // 2, shard % 2, 0:rows_patch, :] = made[piece * rows_patch : (piece + 1) * rows_patch]

    at_place("patch")
    ending = SCHEDULE["tail",]
    perform(ending[:-6])
    early = [
        key for key in sent
        if key[0] == "ag" or (key[0] == "rs" and key[1][0] not in (4, 5, 7))
    ]
    for key in early:
        source, send, recv, at = sent.pop(key)
        left_here(source(), recv.at[at], send.at[at])
    perform(ending[-6:])
    last_copies = [
        pltpu.make_async_copy(VF, vec_out, out_local.at[1 + CHUNKS + 2]),
        pltpu.make_async_copy(SQ.at[2], square_out, out_local.at[2 + CHUNKS + 2]),
    ]
    for copy in last_copies:
        copy.start()
    for source, send, recv, at in list(sent.values()):
        left_here(source(), recv.at[at], send.at[at])
    for k in range(CHUNKS + 2):
        result(k).wait()
    for copy in last_copies:
        copy.wait()

    @pl.when(jnp.logical_not(lower))
    def _():
        for index in range(2):
            left_here(given[index], img_recv.at[index], img_send.at[index])
        left_here(lab_given, img_recv.at[2], img_send.at[2])


def run_train(
    n_rep, n_shard, patches, patch_ends, labels, counts, own_patch, own_in, own_down, vecs, glob, pos, head
):
    n_x = 2 ** ((n_rep.bit_length() - 2) // 2)
    n_z, n_y = n_rep // n_x, n_shard // 2
    block = 4 * (D // n_shard)
    small_block = small_rows(block // 2, n_x, n_z)
    group = KEPT * n_shard
    keep = LAYERS - 1
    units = 1 + 3 * LAYERS
    chunks = CHUNKS + 2

    def buf(*shape, dtype=BF):
        return pltpu.VMEM(shape, dtype)

    def sems(*shape):
        return pltpu.SemaphoreType.DMA(shape)

    def reduction(count, slots, rows):
        by_x = cut(rows, n_x, 16)
        by_z = cut(rows // by_x, n_z, 16)
        return [
            buf(count, n_y, 2, rows, D),
            buf(slots, n_y, rows, D),
            buf(slots, n_y - 1, rows, D),
            buf(slots, n_x - 1 if by_x > 1 else n_x, rows // by_x, D),
            buf(slots, n_z, rows // by_x // by_z, D),
            buf(count, rows, D),
        ]

    rows_y = VEC_ROWS // 2 // n_y
    rows_x = rows_y // n_x
    rows_z = rows_x // cut(rows_x, n_z, 8)
    ag_count = n_y + (n_y - 1) * (n_x - 1) * 2 + n_y - 1
    rs_count = 1 + (n_y - 1) + 2 * (n_x - 1) + 2 * (n_z - 1)
    f_count = 1 + 2 * (n_y - 1) + (n_x - 1) + (n_z - 1) + 1
    v_count = 1 + 2 * (n_y - 1) + 2 * (n_x - 1) + 2 * (n_z - 1) + 1
    q_count = n_z - 1 + 2 * n_x * n_y - 1
    whole = pl.BlockSpec(memory_space=pltpu.VMEM)
    there = pl.BlockSpec(memory_space=pl.ANY)
    return pl.pallas_call(
        functools.partial(train, n_rep, n_shard),
        out_shape=[
            jax.ShapeDtypeStruct((CHUNKS, block, D), BF),
            jax.ShapeDtypeStruct((2, small_block, D), BF),
            jax.ShapeDtypeStruct((VEC_ROWS, VEC_WIDE), F32),
            jax.ShapeDtypeStruct((8, 128), F32),
            jax.ShapeDtypeStruct((2, n_y, n_x, n_z, group, WFAC // n_y), BF),
        ],
        in_specs=[there] * 2 + [pl.BlockSpec(memory_space=pltpu.SMEM)] * 2 + [there] * 3 + [whole] * 2 + [there] * 2,
        out_specs=[there] * 5,
        scratch_shapes=[
            buf(ROWS, D, dtype=F32),
            buf(LAYERS, ROWS, D),
            buf(LAYERS, ROWS, 128, dtype=F32),
            buf(keep, ROWS, 3 * D),
            buf(keep, ROWS, D),
            buf(keep, ROWS, D),
            buf(keep, ROWS, 128, dtype=F32),
            buf(keep, ROWS, FF),
            buf(keep, ROWS, FF),
            buf(ROWS, D),
            buf(ROWS, D),
            buf(ROWS, D),
            buf(ROWS, FF),
            pltpu.VMEM(pos.shape, F32),
            pltpu.VMEM(head.shape, F32),
            buf(KEPT, BLK, PATCH_DIM),
            buf(2, 32, 128, dtype=F32),
            buf(32, 128, dtype=F32),
            buf(PATCH_DIM, D),
            buf(LAYERS, D, 4 * D + FF),
            buf(LAYERS, FF, D),
            buf(D, CPAD),
            buf(1, CPAD, dtype=F32),
            *reduction(CHUNKS, 3, block),
            *reduction(2, 1, small_block),
            buf(2, n_y, group, WFAC // n_y),
            buf(n_y, group, WFAC // n_y),
            buf(n_y - 1, group, WFAC // n_y),
            buf(VEC_ROWS, VEC_WIDE, dtype=F32),
            buf(VEC_ROWS // 2, VEC_WIDE, dtype=F32),
            buf(n_y - 1, rows_y, VEC_WIDE, dtype=F32),
            buf(n_x - 1, rows_x, VEC_WIDE, dtype=F32),
            buf(n_z, rows_z, VEC_WIDE, dtype=F32),
            buf(VEC_ROWS, VEC_WIDE, dtype=F32),
            buf(3, 8, 128, dtype=F32),
            buf(n_z, 8, 128, dtype=F32),
            buf(2 * n_x * n_y, 8, 128, dtype=F32),
            buf(8, 128, dtype=F32),
            sems(units, ag_count),
            sems(units, ag_count),
            sems(units, 4),
            sems(chunks, rs_count),
            sems(chunks, rs_count),
            sems(f_count),
            sems(f_count),
            sems(v_count),
            sems(v_count),
            sems(q_count),
            sems(q_count),
            sems(3),
            sems(3),
            sems(4),
            sems(2),
            sems(3 + chunks),
        ],
        compiler_params=pltpu.CompilerParams(
            vmem_limit_bytes=65400 * 1024, collective_id=0, has_side_effects=True
        ),
        cost_estimate=pl.CostEstimate(
            flops=24_000_000_000, bytes_accessed=30_000_000, transcendentals=10_000_000
        ),
        name="train_step",
    )(patches, patch_ends, labels, counts, own_patch, own_in, own_down, vecs, glob, pos, head)


def adam(weight, first, second, grad, factor, rate):
    share = grad * factor
    first = BETA_FIRST * first + share
    square_scale = (1.0 - BETA_SECOND) / (1.0 - BETA_FIRST) ** 2
    second = BETA_SECOND * second + square_scale * (share * share)
    root_scale = (1.0 / (1.0 - BETA_SECOND**ADAM_STEP)) ** 0.5
    step_scale = rate / (1.0 - BETA_FIRST**ADAM_STEP) / root_scale
    bottom = second * lax.rsqrt(second) + ADAM_EPS / root_scale
    step = first * lax.rsqrt(bottom * bottom)
    return weight * (1.0 - rate * WEIGHT_DECAY) - step * step_scale, first, second


def update(n_rep, n_shard, *refs):
    res_there, small_there, vec, exchanged, factors = refs[0:5]
    sources = refs[5:26]
    loss_out, norm_out = refs[26:28]
    targets = refs[28:49]
    buffers = refs[49:70]
    results = refs[70:91]
    last_in, last_down, passing, grad_head, res, small, in_sems, out_sems, grad_sems = refs[91:]
    shard = lax.axis_index("shard")
    rows_in = D // n_shard
    rows_down = FF // n_shard
    keep = LAYERS - 1

    def moves(array, layer=None, out=False):
        found = []
        for kind in range(3):
            index = 3 * array + kind
            if out:
                src, dst, sem = results[index], targets[index], out_sems
            else:
                src, dst, sem = sources[index], buffers[index], in_sems
            slot = 0 if layer is None else layer
            if layer is not None:
                src, dst = src.at[layer], dst.at[layer]
            found.append(pltpu.make_async_copy(src, dst, sem.at[index, slot]))
        return found

    order = [(array, layer) for layer in range(keep) for array in (1, 2)]
    order += [(array, None) for array in (0, 4, 3, 5, 6)] + [(1, keep), (2, keep)]
    res_copy = pltpu.make_async_copy(res_there, res, grad_sems.at[0])
    small_copy = pltpu.make_async_copy(small_there, small, grad_sems.at[1])
    res_copy.start()
    small_copy.start()
    for array, layer in order:
        for move in moves(array, layer):
            move.start()

    n_rows = factors.shape[2] * factors.shape[3] * factors.shape[4]
    part_wide = factors.shape[5]

    def factor(half, at, size):
        found = []
        while size:
            part, column = divmod(at, part_wide)
            wide = min(size, part_wide - column)
            piece = factors[half, part, :, :, :, column : column + wide]
            found.append(piece.reshape(n_rows, wide))
            at, size = at + wide, size - wide
        return found[0] if len(found) == 1 else jnp.concatenate(found, axis=1)

    def gram_squares(left, right):
        total = jnp.zeros((8, 128), F32)
        for row in range(0, n_rows, 128):
            both = mm_nt(left[row : row + 128], left) * mm_nt(right[row : row + 128], right)
            both = fold(both)
            for lane in range(0, n_rows, 128):
                total = total + both[:, lane : lane + 128]
        return total

    d_logits = factor(1, FF + 2 * D, CPAD)
    head_bias = down_sum(d_logits.astype(F32))
    wide = gram_squares(factor(0, 0, FF), factor(0, FF + 4 * D, D))
    wide = wide + gram_squares(factor(0, FF, D), factor(1, 0, FF))
    wide = wide + gram_squares(factor(0, FF + D, D), factor(1, FF, D))
    wide = wide + gram_squares(factor(0, FF + 2 * D, D), factor(1, FF + D, D))
    wide = wide + gram_squares(factor(0, FF + 3 * D, D), d_logits)
    for lane in range(0, CPAD, 128):
        row = head_bias[:, lane : lane + 128]
        wide = wide + (row * row) * 0.125
    used = VEC_AT + 12 * LAYERS + 2
    parts = jnp.zeros((8, D), F32)
    kept_rows = lax.broadcasted_iota(jnp.int32, (8, 1), 0)
    for at in range(0, used, 8):
        value = vec[at : at + 8, 0:D]
        if at + 8 > used:
            value = jnp.where(kept_rows + at < used, value, 0.0)
        parts = parts + value * value
    patch_bias = down_sum(vec[0:PATCHES, 0:D])
    class_row = vec[CLS : CLS + 1, 0:D]
    rest = (patch_bias * patch_bias + class_row * class_row) * 0.125
    parts = parts + rest
    for lane in range(0, D, 128):
        wide = wide + parts[:, lane : lane + 128]
    wide = wide + exchanged[...]
    sum_squares = jnp.sum(jnp.sum(wide, axis=1, keepdims=True), axis=0, keepdims=True)
    inv_count = 1.0 / vec[used + 1 : used + 2, 0:1]
    grad_norm = jnp.sqrt(sum_squares) * inv_count
    norm_out[...] = grad_norm
    loss_out[...] = vec[used : used + 1, 0:1] * inv_count
    scale = jnp.minimum(1.0, CLIP_NORM / grad_norm) * inv_count * (1.0 - BETA_FIRST)

    def apply(array, where, grad, rate):
        refs = [buffers[3 * array + kind] for kind in range(3)]
        made = adam(refs[0][where], refs[1][where], refs[2][where], grad, scale, rate)
        for kind, value in enumerate(made):
            results[3 * array + kind][where] = value

    def begin(array, layer=None):
        for move in moves(array, layer):
            move.wait()

    def finish(array, layer=None):
        for move in moves(array, layer, out=True):
            move.start()

    def loop(count, body):
        def one(index, nothing):
            body(index)
            return nothing

        lax.fori_loop(0, count, one, 0)

    step = 32 if rows_in % 32 == 0 else 16

    def update_in(layer):
        begin(1, layer)

        def column_of(column):
            lanes = pl.ds(pl.multiple_of(column * D, 128), D)
            for at in range(0, rows_in, step):
                if layer < keep:
                    k = 3 * (keep - 1 - layer) + jnp.where(column < 4, 2, 1)
                    row = pl.multiple_of(lax.rem(column, 4) * rows_in + at, 16)
                    grad = res[k, pl.ds(row, step), :].astype(F32)
                else:
                    grad = last_in[at : at + step, lanes]
                apply(1, (layer, slice(at, at + step), lanes), grad, LEARNING_RATE)

        loop(8, column_of)
        finish(1, layer)

    def update_down(layer):
        begin(2, layer)

        def rows_of(index):
            for part in range(3):
                at = pl.multiple_of(index * 96 + part * 32, 16)
                if layer < keep:
                    grad = res[3 * (keep - 1 - layer), pl.ds(at, 32), :].astype(F32)
                else:
                    grad = last_down[pl.ds(at, 32), :]
                apply(2, (layer, pl.ds(at, 32), slice(0, D)), grad, LEARNING_RATE)

        loop(rows_down // 96, rows_of)
        finish(2, layer)

    res_copy.wait()
    for layer in range(keep):
        update_in(layer)
        update_down(layer)
    small_copy.wait()
    begin(0)

    def patch_rows(index):
        for part in range(3):
            at = pl.multiple_of(index * 96 + part * 32, 16)
            grad = small[1, pl.ds(at, 32), :].astype(F32)
            apply(0, (pl.ds(at, 32), slice(0, D)), grad, LEARNING_RATE)

    loop(PATCH_DIM // n_shard // 96, patch_rows)
    finish(0)
    begin(4)
    rows = [patch_bias, class_row, vec[used - 2 : used - 1, 0:D], vec[used - 1 : used, 0:D]]
    for index, row in enumerate(rows):
        apply(4, (slice(index, index + 1), slice(0, D)), row, VECTOR_RATE)
    finish(4)
    begin(3)
    for layer in range(LAYERS):
        for piece in range(12):
            row = VEC_AT + 12 * layer + piece
            where = (slice(layer, layer + 1), slice(piece * D, (piece + 1) * D))
            apply(3, where, vec[row : row + 1, 0:D], VECTOR_RATE)
    finish(3)
    begin(5)
    apply(5, (slice(0, 1), slice(0, D)), class_row, VECTOR_RATE)
    for at in range(0, PATCHES, 28):
        apply(
            5, (slice(1 + at, 29 + at), slice(0, D)), vec[at : at + 28, 0:D], VECTOR_RATE
        )
    finish(5)
    final = factor(0, FF + 3 * D, D)
    for at in range(0, CPAD, 512):
        grad_head[0:D, at : at + 512] = mm_tn(final, d_logits[:, at : at + 512])
    grad_head[D : D + 1, :] = head_bias
    begin(6)

    def head_rows(index):
        for part in range(3):
            rows = pl.ds(pl.multiple_of(index * 48 + part * 16, 16), 16)
            apply(6, (rows, slice(0, NCLS)), grad_head[rows, 0:NCLS], LEARNING_RATE)

    loop(D // 48, head_rows)
    apply(6, (slice(D, D + 1), slice(0, NCLS)), grad_head[D : D + 1, 0:NCLS], LEARNING_RATE)
    finish(6)
    own_rows = pl.multiple_of(shard * rows_in, 8)

    def keep_in(column, made):
        slot = column % 2
        passing[slot] = made
        last_in[:, column * D : (column + 1) * D] = passing[slot, pl.ds(own_rows, rows_in), :]

    h2 = factor(0, FF, D)
    for tile in range(4):
        made = mm_tn(h2, factor(1, tile * D, D))
        keep_in(4 + tile, made)
    for tile in range(2):
        last_in[:, (1 + tile) * D : (2 + tile) * D] = small[
            0, tile * rows_in : (tile + 1) * rows_in, :
        ].astype(F32)
    made = mm_tn(factor(0, FF + 2 * D, D), factor(1, FF + D, D))
    keep_in(0, made)
    made = mm_tn(factor(0, FF + D, D), factor(1, FF, D))
    keep_in(3, made)
    d_top = factor(0, FF + 4 * D, D)
    per = min(rows_down, D)
    for tile in range(4):
        made = mm_tn(factor(0, tile * D, D), d_top)
        for piece in range(D // per):
            owner, at = divmod(tile * D + piece * per, rows_down)

            def keep_down(made=made, piece=piece, at=at):
                last_down[at : at + per, :] = made[piece * per : (piece + 1) * per]

            pl.when(shard == owner)(keep_down)
    update_in(keep)
    update_down(keep)
    for array, layer in order:
        for move in moves(array, layer, out=True):
            move.wait()


def run_update(n_rep, n_shard, res, small, vec, squares, factors, arrays):
    whole = pl.BlockSpec(memory_space=pltpu.VMEM)
    there = pl.BlockSpec(memory_space=pl.ANY)
    one = jax.ShapeDtypeStruct((1, 1), F32)
    made = pl.pallas_call(
        functools.partial(update, n_rep, n_shard),
        out_shape=[one, one] + [jax.ShapeDtypeStruct(a.shape, F32) for a in arrays],
        in_specs=[there] * 2 + [whole] * 3 + [there] * 21,
        out_specs=[whole] * 2 + [there] * 21,
        scratch_shapes=[pltpu.VMEM(a.shape, F32) for a in (*arrays, *arrays)]
        + [
            pltpu.VMEM((D // n_shard, 4 * D + FF), F32),
            pltpu.VMEM((FF // n_shard, D), F32),
            pltpu.VMEM((2, D, D), F32),
            pltpu.VMEM((D + 8, CPAD), F32),
            pltpu.VMEM(res.shape, BF),
            pltpu.VMEM(small.shape, BF),
            pltpu.SemaphoreType.DMA((21, LAYERS)),
            pltpu.SemaphoreType.DMA((21, LAYERS)),
            pltpu.SemaphoreType.DMA((2,)),
        ],
        compiler_params=pltpu.CompilerParams(vmem_limit_bytes=62 * 1024 * 1024),
        cost_estimate=pl.CostEstimate(
            flops=200_000_000, bytes_accessed=50_000_000, transcendentals=4_000_000
        ),
        name="adamw",
    )(res, small, vec, squares, factors, *arrays)
    return made[0].reshape(()), made[1].reshape(()), made[2:]


def shards(
    n_rep, n_shard,
    patches, labels, counts, patch_w, layer_in, layer_down, layer_vecs, glob_vecs, pos_embed, head,
    m_patch, v_patch, m_in, v_in, m_down, v_down, m_vecs, v_vecs, m_glob, v_glob, m_pos, v_pos,
    m_head, v_head,
):
    ends = lax.pad(patches, BF(0), ((0, 0, 0), (-TAIL, BLK - PATCHES, 0), (0, 0, 0)))
    res, small, vec, squares, factors = run_train(
        n_rep, n_shard, patches, ends, labels, counts, patch_w, layer_in, layer_down, layer_vecs,
        glob_vecs, pos_embed, head,
    )
    arrays = [
        patch_w, m_patch, v_patch, layer_in, m_in, v_in, layer_down, m_down, v_down,
        layer_vecs, m_vecs, v_vecs, glob_vecs, m_glob, v_glob, pos_embed, m_pos, v_pos,
        head, m_head, v_head,
    ]
    loss, grad_norm, new = run_update(n_rep, n_shard, res, small, vec, squares, factors, arrays)
    return (loss, grad_norm, *new)


def solution(mesh):
    everywhere = P()
    rows = P("shard", None)
    middle = P(None, "shard", None)
    return jax.shard_map(
        functools.partial(shards, mesh.shape["rep"], mesh.shape["shard"]),
        mesh=mesh,
        in_specs=(
            P(("rep", "shard"), None, None),
            P(("rep", "shard")),
            P(("rep", "shard")),
            rows,
            middle,
            middle,
            *(everywhere,) * 4,
            *(rows,) * 2,
            *(middle,) * 4,
            *(everywhere,) * 8,
        ),
        out_specs=(
            *(everywhere,) * 2,
            *(rows,) * 3,
            *(middle,) * 6,
            *(everywhere,) * 12,
        ),
        check_vma=False,
    )
```

```python
import functools

import jax
import jax.numpy as jnp
from jax import lax
from jax.experimental import pallas as pl
from jax.experimental.pallas import tpu as pltpu
from jax.sharding import PartitionSpec as P

D = 384
HEADS = 6
HEAD_DIM = 64
FF = 1536
PATCH_DIM = 768
PATCHES = 196
NCLS = 1000
LAYERS = 3
SEQ = 197

BLK = 208
CLS = 200
TAIL = 192
KEPT = 4
ROWS = KEPT * BLK
HALF = 2 * BLK
CROWS = KEPT * 16
CPAD = 1024
WIDE = 8 * D + FF

NORM_EPS = 1e-06
SMOOTHING = 0.1
CLIP_NORM = 0.05
LEARNING_RATE = 0.05
VECTOR_RATE = 0.5
BETA_FIRST = 0.9
BETA_SECOND = 0.999
ADAM_EPS = 1e-08
WEIGHT_DECAY = 0.05
ADAM_STEP = 10
GELU_SCALE = 0.7978845608028654
GELU_CUBIC = 0.044715

F32 = jnp.float32
BF = jnp.bfloat16


def mm(left, right):
    return jnp.dot(left, right, preferred_element_type=F32)


def mm_nt(left, right):
    return lax.dot_general(left, right, (((1,), (1,)), ((), ())), preferred_element_type=F32)


def mm_tn(left, right):
    return lax.dot_general(left, right, (((0,), (0,)), ((), ())), preferred_element_type=F32)


def fold(values):
    return jnp.sum(values.reshape(-1, 8, values.shape[-1]), axis=0)


def down_sum(values):
    return jnp.sum(values, axis=0, keepdims=True)


def norm(values):
    centre = values - jnp.mean(values, axis=-1, keepdims=True)
    inverse = lax.rsqrt(jnp.mean(centre * centre, axis=-1, keepdims=True) + NORM_EPS)
    return centre * inverse, inverse


def norm_back(upstream, normed, inverse, gain):
    scaled = upstream * gain
    first = jnp.mean(scaled, axis=-1, keepdims=True)
    second = jnp.mean(scaled * normed, axis=-1, keepdims=True)
    return inverse * (scaled - first - normed * second)


def gelu_parts(hidden):
    bent = hidden * (GELU_SCALE + (GELU_SCALE * GELU_CUBIC) * (hidden * hidden))
    tangent = jnp.tanh(bent)
    share = 0.5 + 0.5 * tangent
    slope = share + (1.0 - tangent * tangent) * (1.5 * bent - GELU_SCALE * hidden)
    return hidden * share, slope


def lane_mask(width, low, high):
    lane = lax.broadcasted_iota(jnp.int32, (1, width), 1)
    return jnp.where((lane >= low) & (lane < high), 1.0, 0.0).astype(BF)


STEP = 16


def pieces(total):
    return [(at, min(STEP, total - at)) for at in range(0, total, STEP)]


SCHEDULE = {
    ("cast", 0): ("ws0",),
    ("cast", 1): ("ws1",),
    ("cast", 2): ("ws2",),
    ("cast", 8): ("wf0", "ws3",),
    ("b_start",): ("wr0", "wf1", "ws4", "we0",),
    ("b_norm", 0, 0): ("wf2", "ws5", "wr1", "wf3", "ws6", "we1",),
    ("norm", 0, 0): ("wr2",),
    ("att", 0, 0, 0): ("wf4", "ws7",),
    ("att", 0, 0, 1): ("wr3",),
    ("b_up", 0, 0): ("we2",),
    ("up", 0, 0): ("wr4", "wf5", "ws8",),
    ("b_down", 0, 0): ("we3",),
    ("down", 0, 0): ("wf6", "ws9",),
    ("b_norm", 0, 1): ("we4",),
    ("att", 0, 1, 0): ("wr5", "wf7",),
    ("mid", 0, 1): ("wr6", "wf8",),
    ("b_up", 0, 1): ("we5",),
    ("b_down", 0, 1): ("we6",),
    ("down", 0, 1): ("wr7", "wf9",),
    ("norm", 1, 0): ("wr8",),
    ("mid", 1, 0): ("wr9",),
    ("b_last",): ("we7", "we8", "we9",),
    ("class",): ("fc",),
    ("kv",): ("core6",),
    ("lb", 0): ("fy",),
    ("round", 1): ("y6",),
    ("dn", 1): ("fz", "core0",),
    ("ups", 1): ("y0", "x6", "core1",),
    ("mlpb", 1, 0): ("fx",),
    ("out", 1): ("y1", "z6",),
    ("attb", 1, 2): ("x0", "gz6",),
    ("qkv", 1): ("core2",),
    ("fb", 1, 0): ("gx6",),
    ("fb", 1, 1): ("z0", "x1",),
    ("round", 0): ("y2",),
    ("dn", 0): ("gd6", "core3",),
    ("act", 0, 1): ("z1", "gz0",),
    ("mlpb", 0, 0): ("x2", "y3", "core4",),
    ("mlpb", 0, 1): ("gz1",),
    ("attb", 0, 0): ("gx0",),
    ("attb", 0, 1): ("z2",),
    ("attb", 0, 3): ("x3", "y4", "gx1", "gd0",),
    ("qkv", 0): ("gz2", "core5",),
    ("fb", 0, 1): ("z3",),
    ("emb",): ("vc",),
    ("patch",): ("gx2", "core7",),
    ("tail",): ("vy", "gd1", "x4", "y5", "y7", "fv", "gz3", "vx", "gd2", "z4", "gx3", "vz", "x5", "gz4", "gd3", "vgz", "x7", "z5", "gx4", "vgx", "z7", "gz5", "gd4", "vgy", "gz7", "qz", "fm", "gx5", "vgc", "gx7", "qp", "fd", "vd", "gd5", "gd7", "qd",),
}


WFAC = FF + 5 * D + 128
VEC_ROWS = 256
VEC_AT = BLK
VEC_WIDE = D
MESH = pl.DeviceIdType.MESH
CHUNKS = 6


class Place:
    def __init__(self, n_rep, n_shard):
        self.n_rep, self.n_shard = n_rep, n_shard
        self.n_x = 2 ** ((n_rep.bit_length() - 2) // 2)
        self.n_z = n_rep // self.n_x
        self.n_y = n_shard // 2
        rep, shard = lax.axis_index("rep"), lax.axis_index("shard")
        self.rep, self.shard = rep, shard
        self.z, self.x = rep // self.n_x, rep % self.n_x
        self.y, self.c = shard // 2, shard % 2

    def to(self, x=None, y=None, z=None, c=None):
        x = self.x if x is None else x
        y = self.y if y is None else y
        z = self.z if z is None else z
        c = self.c if c is None else c
        return {"rep": z * self.n_x + x, "shard": y * 2 + c}


def cut(rows, parts, unit):
    return parts if rows % (parts * unit) == 0 else 1


def small_rows(rows, n_x, n_z):
    unit = 16 * n_x * n_z
    padded = -(-rows // unit) * unit
    return padded if 2 * padded <= 3 * rows else rows


def aligned(value, unit):
    return pl.multiple_of(value, unit)


def train(
    n_rep, n_shard,
    patches, patch_ends, labels, counts, own_patch, own_in, own_down, vecs, glob, pos_there, head_there,
    res_out, small_out, vec_out, square_out, all_factors,
    X, N1, I1, QKV, ATT, N2, I2, ACT, SLOPE, DXB, DMB, DA, DH,
    pos, head, pix, lab, lab_given, wp, win, wdn, low_head, head_bias,
    G, RC, RY, RX, RZ, RES, GS, SC, SY, SX, SZ, SRES,
    FAC, FC, FY, V, VC, VY, VX, VZ, VF, SQ, SQZ, SQP, square_sum,
    ag_send, ag_recv, ag_local, rs_send, rs_recv, f_send, f_recv, v_send, v_recv,
    q_send, q_recv,
    img_send, img_recv, img_local, own_local, out_local,
):
    here = Place(n_rep, n_shard)
    n_x, n_y, n_z = here.n_x, here.n_y, here.n_z
    x, y, z, c = here.x, here.y, here.z, here.c
    rows_in, rows_down, rows_patch = D // n_shard, FF // n_shard, PATCH_DIM // n_shard
    block = 4 * rows_in
    small_block = small_rows(block // 2, n_x, n_z)
    mate = here.to(c=1 - c)

    def push(src, dst, send, recv, device):
        pltpu.make_async_remote_copy(
            src_ref=src, dst_ref=dst, send_sem=send, recv_sem=recv,
            device_id=device, device_id_type=MESH,
        ).start()

    def arrived(dst, recv, send):
        pltpu.make_async_remote_copy(
            src_ref=dst, dst_ref=dst, send_sem=send, recv_sem=recv,
            device_id=mate, device_id_type=MESH,
        ).wait_recv()

    def left_here(src, recv, send):
        pltpu.make_async_remote_copy(
            src_ref=src, dst_ref=src, send_sem=send, recv_sem=recv,
            device_id=mate, device_id_type=MESH,
        ).wait_send()

    sent = {}

    def go(source, dst, sems, index, device):
        name, send, recv = sems
        push(source(), dst, send.at[index], recv.at[index], device)
        sent[name, index] = (source, send, recv, index)

    def gone(sems, index):
        source, send, recv, at = sent.pop((sems[0], index))
        left_here(source(), recv.at[at], send.at[at])

    def turn(at, by, size):
        return lax.rem(at + by, size)

    barrier = pltpu.get_barrier_semaphore()
    plane = [
        (i, j, k) for i in range(n_x) for j in range(n_y) for k in range(2) if i or j or k
    ]

    def in_plane(step):
        i, j, k = step
        return here.to(x=turn(x, i, n_x), y=turn(y, j, n_y), c=lax.rem(c + k, 2))

    others = [in_plane(step) for step in plane]
    others += [here.to(z=turn(z, o, n_z)) for o in range(1, n_z)]
    for other in others:
        pl.semaphore_signal(barrier, inc=1, device_id=other, device_id_type=MESH)

    def weight(kind, layer, shard, part=None):
        if kind == "patch":
            parts = cut(rows_patch, n_x, 16)
            rows = rows_patch // parts
            if part is None:
                return wp.at[pl.ds(aligned(shard * rows_patch, 16), rows_patch), :]
            return wp.at[pl.ds(aligned(shard * rows_patch + part * rows, 16), rows), :]
        if kind == "down":
            parts = cut(rows_down, n_x, 16)
            rows = rows_down // parts
            if part is None:
                return wdn.at[layer, pl.ds(aligned(shard * rows_down, 16), rows_down), :]
            return wdn.at[layer, pl.ds(aligned(shard * rows_down + part * rows, 16), rows), :]
        base = 0 if kind == "attn" else 4 * D
        rows = pl.ds(aligned(shard * rows_in, 16), rows_in)
        if part is None:
            return win.at[layer, rows, pl.ds(base, 4 * D)]
        wide = 4 * D // n_x
        return win.at[layer, rows, pl.ds(aligned(base + part * wide, 128), wide)]

    units = [("patch", 0)] + [
        (kind, layer) for layer in range(LAYERS) for kind in ("attn", "up", "down")
    ]

    def parts_of(kind):
        if kind == "patch":
            return cut(rows_patch, n_x, 16)
        if kind == "down":
            return cut(rows_down, n_x, 16)
        return n_x

    ag = ("ag", ag_send, ag_recv)
    base_x = n_y
    base_my = base_x + (n_y - 1) * (n_x - 1)
    base_mx = base_my + (n_y - 1)

    stage = 4 * rows_in

    def weights_copies(unit):
        kind, layer = units[unit]
        base = (unit % 2) * stage
        if kind == "patch":
            pairs = [(own_patch, X.at[pl.ds(base, rows_patch)])]
        elif kind == "down":
            pairs = [(own_down.at[layer], X.at[pl.ds(base, rows_down)])]
        else:
            start = 0 if kind == "attn" else 4 * D
            pairs = [
                (
                    own_in.at[layer, :, pl.ds(start + tile * D, D)],
                    X.at[pl.ds(base + tile * rows_in, rows_in)],
                )
                for tile in range(4)
            ]
        return [
            pltpu.make_async_copy(src, dst, ag_local.at[unit, index])
            for index, (src, dst) in enumerate(pairs)
        ]

    def weights_cast(unit):
        kind, layer = units[unit]
        base = (unit % 2) * stage
        for copy in weights_copies(unit):
            copy.wait()
        if kind == "patch":
            rows = pl.ds(aligned(here.shard * rows_patch, 16), rows_patch)
            wp[rows, :] = X[base : base + rows_patch, :].astype(BF)
        elif kind == "down":
            rows = pl.ds(aligned(here.shard * rows_down, 16), rows_down)
            wdn[layer, rows, :] = X[base : base + rows_down, :].astype(BF)
        else:
            start = 0 if kind == "attn" else 4 * D
            rows = pl.ds(aligned(here.shard * rows_in, 16), rows_in)
            for tile in range(4):
                win[layer, rows, start + tile * D : start + (tile + 1) * D] = X[
                    base + tile * rows_in : base + (tile + 1) * rows_in, :
                ].astype(BF)
        if unit + 2 < len(units):
            for copy in weights_copies(unit + 2):
                copy.start()

    def weights_start(unit):
        kind, layer = units[unit]
        part = x if parts_of(kind) > 1 else 0
        for o in range(1, n_y):
            go(
                lambda: weight(kind, layer, here.shard, part),
                weight(kind, layer, here.shard, part), ag, (unit, o),
                here.to(y=turn(y, o, n_y)),
            )
        go(
            lambda: weight(kind, layer, here.shard), weight(kind, layer, here.shard), ag,
            (unit, 0), mate,
        )

    def weights_forward(unit):
        kind, layer = units[unit]
        split = parts_of(kind) > 1
        part = x if split else 0
        for o in range(1, n_y):
            def make(o=o):
                return weight(kind, layer, turn(y, n_y - o, n_y) * 2 + c, part)

            arrived(make(), ag_recv.at[unit, o], ag_send.at[unit, o])
            if split:
                for p in range(1, n_x):
                    index = base_x + (o - 1) * (n_x - 1) + p - 1
                    go(make, make(), ag, (unit, index), here.to(x=turn(x, p, n_x)))
            go(make, make(), ag, (unit, base_my + o - 1), mate)

    def weights_pass(unit):
        kind, layer = units[unit]
        split = parts_of(kind) > 1
        part = x if split else 0
        if split:
            for o in range(1, n_y):
                for p in range(1, n_x):
                    index = (o - 1) * (n_x - 1) + p - 1

                    def make(o=o, p=p):
                        shard = turn(y, n_y - o, n_y) * 2 + c
                        return weight(kind, layer, shard, turn(x, n_x - p, n_x))

                    arrived(
                        make(), ag_recv.at[unit, base_x + index], ag_send.at[unit, base_x + index]
                    )
                    go(make, make(), ag, (unit, base_mx + index), mate)

    def weights_whole(unit):
        kind, layer = units[unit]
        split = parts_of(kind) > 1
        part = x if split else 0
        arrived(weight(kind, layer, y * 2 + 1 - c), ag_recv.at[unit, 0], ag_send.at[unit, 0])
        for o in range(1, n_y):
            shard = turn(y, n_y - o, n_y) * 2 + 1 - c
            index = base_my + o - 1
            arrived(weight(kind, layer, shard, part), ag_recv.at[unit, index], ag_send.at[unit, index])
            if split:
                for p in range(1, n_x):
                    index = base_mx + (o - 1) * (n_x - 1) + p - 1
                    piece = weight(kind, layer, shard, turn(x, n_x - p, n_x))
                    arrived(piece, ag_recv.at[unit, index], ag_send.at[unit, index])

    actions = {}

    def perform(names):
        for name in names:
            actions[name]()

    def at_place(place, *indices):
        for key, names in SCHEDULE.items():
            if key[0] != place:
                continue
            held = None
            for index, value in zip(indices, key[1:], strict=True):
                if not isinstance(index, int):
                    same = index == value
                    held = same if held is None else jnp.logical_and(held, same)
                elif index != value:
                    break
            else:
                if held is None:
                    perform(names)
                else:
                    pl.when(held)(functools.partial(perform, names))

    for unit in range(len(units)):
        actions[f"ws{unit}"] = functools.partial(weights_start, unit)
        actions[f"wf{unit}"] = functools.partial(weights_forward, unit)
        actions[f"wr{unit}"] = functools.partial(weights_pass, unit)
        actions[f"we{unit}"] = functools.partial(weights_whole, unit)

    lower = here.rep < n_rep // 2
    partner = here.to(z=turn(z, n_z // 2, n_z))
    back_parts = (
        pix.at[pl.ds(2, 2), pl.ds(0, TAIL)], pix.at[pl.ds(2, 2), pl.ds(TAIL, BLK - TAIL)]
    )
    given = (patches.at[pl.ds(KEPT, 2), pl.ds(0, TAIL)], patch_ends.at[pl.ds(KEPT, 2)])

    def local_half(half):
        pair = pl.ds(2 * half, 2)
        return (
            pltpu.make_async_copy(
                patches.at[pair, pl.ds(0, TAIL)], pix.at[pair, pl.ds(0, TAIL)],
                img_local.at[half],
            ),
            pltpu.make_async_copy(
                patch_ends.at[pair], pix.at[pair, pl.ds(TAIL, BLK - TAIL)],
                img_local.at[2 + half],
            ),
        )

    def marks(pair):
        row = lax.broadcasted_iota(jnp.int32, (32, 128), 0)
        found = jnp.full((32, 128), -1.0, F32)
        for index in range(2):
            slot = 2 * pair + index
            value = jnp.where(slot < counts[0], labels[slot], -1).astype(F32)
            found = jnp.where(row == CLS - TAIL + 16 * index, value, found)
        return found

    for unit in range(2):
        for copy in weights_copies(unit):
            copy.start()
    for copy in local_half(0):
        copy.start()
    pos_copy = pltpu.make_async_copy(pos_there, pos, own_local.at[0])
    head_copy = pltpu.make_async_copy(head_there, head, own_local.at[1])
    pos_copy.start()
    head_copy.start()
    lab[0] = marks(0)
    lab_given[...] = marks(2)
    weights_cast(0)
    pl.semaphore_wait(barrier, len(others))
    at_place("cast", 0)

    @pl.when(jnp.logical_not(lower))
    def _():
        for index in range(2):
            push(
                given[index], back_parts[index], img_send.at[index], img_recv.at[index],
                partner,
            )
        push(lab_given, lab.at[1], img_send.at[2], img_recv.at[2], partner)
        for copy in local_half(1):
            copy.start()
        lab[1] = marks(1)

    for unit in range(1, len(units)):
        weights_cast(unit)
        at_place("cast", unit)

    even = lane_mask(128, 0, 64)
    odd = lane_mask(128, 64, 128)
    low_lane = lax.broadcasted_iota(jnp.int32, (1, 128), 1) < 64
    key_lane = lax.broadcasted_iota(jnp.int32, (1, BLK), 1)
    key_row = jnp.where((key_lane < PATCHES) | (key_lane == CLS), 0.0, -1e30)
    key_sub = lax.broadcasted_iota(jnp.int32, (BLK, 1), 0)
    key_column = jnp.where((key_sub < PATCHES) | (key_sub == CLS), 0.0, -1e30)
    whole_lanes = NCLS // 128 * 128
    head_copy.wait()
    pos_copy.wait()
    low_head[:, 0:whole_lanes] = head[0:D, 0:whole_lanes].astype(BF)
    low_head[:, whole_lanes:] = jnp.zeros((D, CPAD - whole_lanes), BF)
    low_head[:, whole_lanes:NCLS] = head[0:D, whole_lanes:NCLS].astype(BF)
    head_bias[...] = jnp.zeros((1, CPAD), F32)
    head_bias[:, 0:NCLS] = head[D : D + 1, :]
    V[...] = jnp.zeros((VEC_ROWS, VEC_WIDE), F32)
    square_sum[...] = jnp.zeros((8, 128), F32)
    if small_block > block // 2:
        spare = small_block - block // 2
        GS[:, :, :, block // 2 :, :] = jnp.zeros((2, n_y, 2, spare, D), BF)
    zeros = jnp.zeros((8, D), F32)
    patch_bias = glob[0:1, :]

    def whole_lanes_of(tile):
        return jnp.concatenate([tile] * (D // 128), axis=1)

    def vector(layer, at, size):
        return vecs[pl.ds(layer, 1), at : at + size]

    def store_vector(layer, at, row):
        for piece in range(row.shape[-1] // D):
            V[pl.ds(VEC_AT + 12 * layer + at // D + piece, 1), 0:D] = row[
                :, piece * D : (piece + 1) * D
            ]

    def store_sums(layer, parts):
        for at, part in parts:
            store_vector(layer, at, down_sum(part))

    def embed(half):
        made = mm(pix[pl.ds(2 * half, 2)].reshape(HALF, PATCH_DIM), wp[...])
        for image in range(2):
            start = aligned(half * HALF + image * BLK, 16)
            for at, size in pieces(PATCHES - 4):
                X[pl.ds(start + at, size), :] = (
                    made[image * BLK + at : image * BLK + at + size]
                    + pos[1 + at : 1 + at + size, :]
                    + patch_bias
                )
            X[pl.ds(start + TAIL, 16), :] = jnp.zeros((16, D), F32)
            X[pl.ds(start + TAIL, 4), :] = (
                made[image * BLK + TAIL : image * BLK + PATCHES]
                + pos[1 + TAIL : 1 + PATCHES, :]
                + patch_bias
            )
            X[pl.ds(start + CLS, 1), :] = glob[1:2, :] + pos[0:1, :]

    def first_norm(layer, half, columns):
        base = half * HALF
        gain, shift = vector(layer, 0, D), vector(layer, D, D)
        for at, size in pieces(HALF):
            rows = pl.ds(aligned(base + at, 16), size)
            normed, inverse = norm(X[rows, :])
            N1[layer, rows, :] = normed.astype(BF)
            I1[layer, rows, :] = jnp.broadcast_to(inverse, (size, 128))
            DXB[rows, :] = (normed * gain + shift).astype(BF)
        rows = pl.ds(aligned(base, 16), HALF)
        h1 = DXB[rows, :]
        if len(columns) == 3:
            made = mm(h1, win[layer, :, 0 : 2 * D])
            QKV[layer, rows, 0:D] = (made[:, 0:D] + vector(layer, 2 * D, D)).astype(BF)
            QKV[layer, rows, D : 2 * D] = made[:, D:].astype(BF)
            made = mm(h1, win[layer, :, 2 * D : 3 * D])
            QKV[layer, rows, 2 * D :] = (made + vector(layer, 3 * D, D)).astype(BF)
        else:
            made = mm(h1, win[layer, :, D : 3 * D])
            DMB[rows, :] = made[:, 0:D].astype(BF)
            DA[rows, :] = (made[:, D:] + vector(layer, 3 * D, D)).astype(BF)

    lanes = 256
    fill = jnp.zeros((lanes - BLK, 128), BF)
    ones = jnp.full((lanes, 128), 1.0, BF)
    wide_lane = lax.broadcasted_iota(jnp.int32, (1, lanes), 1)
    wide_key_row = jnp.where((wide_lane < PATCHES) | (wide_lane == CLS), 0.0, -1e30)

    def fill_up(values):
        return jnp.concatenate([jnp.concatenate([values, fill], axis=0), ones], axis=1)

    def attend(layer, image):
        rows = pl.ds(aligned(image * BLK, 16), BLK)
        for pair in range(3):
            at = pair * 128
            query = QKV[layer, rows, at : at + 128] * BF(0.125)
            keys = QKV[layer, rows, D + at : D + at + 128]
            values = QKV[layer, rows, 2 * D + at : 2 * D + at + 128]
            both = jnp.concatenate([query * even, query * odd], axis=0)
            scores = mm_nt(both, jnp.concatenate([keys, fill], axis=0))
            probs = []
            for row, size in pieces(HALF):
                part = scores[row : row + size] + wide_key_row
                probs.append(jnp.exp(part - jnp.max(part, axis=-1, keepdims=True)).astype(BF))
            probs = jnp.concatenate(probs, axis=0)
            first = mm(probs[:BLK], fill_up(values * even))
            second = mm(probs[BLK:], fill_up(values * odd))
            made = first[:, :128] * (1.0 / first[:, 128:])
            made = made + second[:, :128] * (1.0 / second[:, 128:])
            ATT[layer, rows, at : at + 128] = made.astype(BF)

    def mlp(layer, half):
        base = half * HALF
        whole = pl.ds(aligned(base, 16), HALF)
        made = mm(ATT[layer, whole, :], win[layer, :, 3 * D : 4 * D])
        bias_out = vector(layer, 4 * D, D)
        gain, shift = vector(layer, 5 * D, D), vector(layer, 6 * D, D)
        for at, size in pieces(HALF):
            rows = pl.ds(aligned(base + at, 16), size)
            middle = X[rows, :] + made[at : at + size] + bias_out
            X[rows, :] = middle
            normed, inverse = norm(middle)
            N2[layer, rows, :] = normed.astype(BF)
            I2[layer, rows, :] = jnp.broadcast_to(inverse, (size, 128))
            DXB[rows, :] = (normed * gain + shift).astype(BF)
        at_place("mid", half, layer)
        at_place("b_up", half, layer)
        h2 = DXB[whole, :]
        for pair in range(2):
            made = mm(h2, win[layer, :, (4 + 2 * pair) * D : (6 + 2 * pair) * D])
            for tile in range(2):
                start = (2 * pair + tile) * D
                columns = slice(start, start + D)
                bias = vector(layer, 7 * D + start, D)
                for at, size in pieces(HALF):
                    rows = pl.ds(aligned(base + at, 16), size)
                    active, slope = gelu_parts(
                        made[at : at + size, tile * D : (tile + 1) * D] + bias
                    )
                    ACT[layer, rows, columns] = active.astype(BF)
                    SLOPE[layer, rows, columns] = slope.astype(BF)
        at_place("up", half, layer)
        at_place("b_down", half, layer)
        made = mm(ACT[layer, whole, :], wdn[layer])
        bias = vector(layer, 7 * D + FF, D)
        for at, size in pieces(HALF):
            rows = pl.ds(aligned(base + at, 16), size)
            X[rows, :] = X[rows, :] + made[at : at + size] + bias
        at_place("down", half, layer)

    at_place("b_start")

    def forward_half(half, carry):
        @pl.when(half == 0)
        def _():
            for copy in local_half(0):
                copy.wait()

        @pl.when(jnp.logical_and(half == 1, lower))
        def _():
            for index in range(2):
                arrived(back_parts[index], img_recv.at[index], img_send.at[index])

        @pl.when(jnp.logical_and(half == 1, jnp.logical_not(lower)))
        def _():
            for copy in local_half(1):
                copy.wait()

        embed(half)
        at_place("embed", half)

        def forward_layer(layer, inner):
            at_place("b_norm", half, layer)
            first_norm(layer, half, (0, 1, 2))
            at_place("norm", half, layer)

            for index in range(2):
                attend(layer, 2 * half + index)
            for index in range(2):
                at_place("att", half, layer, index)
            mlp(layer, half)
            return inner

        return lax.fori_loop(0, LAYERS - 1, forward_layer, carry)

    lax.fori_loop(0, 2, forward_half, 0)
    at_place("b_last")

    last = LAYERS - 1

    def last_norm(half, nothing):
        first_norm(last, half, (1, 2))
        at_place("ln", half)
        return nothing

    lax.fori_loop(0, 2, last_norm, 0)

    fac = ("f", f_send, f_recv)
    f_y, f_z = 1, n_y
    f_x = f_z + n_z - 1
    f_v = f_x + n_x - 1
    f_m = f_v + n_y - 1
    part_wide = WFAC // n_y
    group = KEPT * n_shard

    def factors_core():
        go(lambda: FAC.at[1 - c], FC, fac, 0, mate)

    def factors_y():
        arrived(FC, f_recv.at[0], f_send.at[0])
        FAC[c] = FAC[c] + FC[...]
        for o in range(1, n_y):
            go(
                lambda o=o: FAC.at[c, turn(y, o, n_y)], FY.at[o - 1], fac, f_y + o - 1,
                here.to(y=turn(y, o, n_y)),
            )

    def line_factors(z_at, x_at):
        return all_factors.at[c, y, x_at, z_at]

    def factors_z():
        total = FAC[c, y]
        for o in range(1, n_y):
            arrived(FY.at[o - 1], f_recv.at[f_y + o - 1], f_send.at[f_y + o - 1])
            total = total + FY[o - 1]
        FC[0] = total
        pltpu.make_async_copy(FC.at[0], line_factors(z, x), out_local.at[0]).start()
        for o in range(1, n_z):
            go(
                lambda: FC.at[0], line_factors(z, x), fac, f_z + o - 1,
                here.to(z=turn(z, o, n_z)),
            )

    def factors_x():
        for o in range(1, n_z):
            index = f_z + o - 1
            arrived(line_factors(turn(z, n_z - o, n_z), x), f_recv.at[index], f_send.at[index])
        pltpu.make_async_copy(FC.at[0], line_factors(z, x), out_local.at[0]).wait()
        for o in range(1, n_x):
            go(
                lambda: all_factors.at[c, y, x], all_factors.at[c, y, x], fac, f_x + o - 1,
                here.to(x=turn(x, o, n_x)),
            )

    def factors_side():
        for o in range(1, n_x):
            index = f_x + o - 1
            came = all_factors.at[c, y, turn(x, n_x - o, n_x)]
            arrived(came, f_recv.at[index], f_send.at[index])
        for o in range(1, n_y):
            go(
                lambda: all_factors.at[c, y], all_factors.at[c, y], fac, f_v + o - 1,
                here.to(y=turn(y, o, n_y)),
            )

    def factors_mate():
        for o in range(1, n_y):
            index = f_v + o - 1
            came = all_factors.at[c, turn(y, n_y - o, n_y)]
            arrived(came, f_recv.at[index], f_send.at[index])
        go(lambda: all_factors.at[c], all_factors.at[c], fac, f_m, mate)

    def factors_done():
        arrived(all_factors.at[1 - c], f_recv.at[f_m], f_send.at[f_m])

    rs = ("rs", rs_send, rs_recv)
    r_y, r_x = 1, n_y
    r_z = r_x + n_x - 1
    r_gz = r_z + n_z - 1
    r_gx = r_gz + n_z - 1

    def chunk(k):
        if k < CHUNKS:
            slot = k % 3
            return (
                G.at[k], RC.at[slot], RY.at[slot], RX.at[slot], RZ.at[slot], RES.at[k], block
            )
        k = k - CHUNKS
        return GS.at[k], SC.at[0], SY.at[0], SX.at[0], SZ.at[0], SRES.at[k], small_block

    def splits(rows):
        by_x = cut(rows, n_x, 16)
        by_z = cut(rows // by_x, n_z, 16)
        return by_x, rows // by_x, by_z, rows // by_x // by_z

    def step_of(rows, most=192):
        return max(step for step in range(16, most + 1, 16) if rows % step == 0)

    def add_rows(rows, target, target_at, sources):
        step = step_of(rows)

        def one(index, nothing):
            at = index * step
            to = pl.ds(aligned(target_at + at, 16), step)
            total = target[to, :]
            if len(sources) == 1:
                total = total + sources[0][pl.ds(aligned(at, 16), step), :]
            else:
                total = total.astype(F32)
                for source in sources:
                    total = total + source[pl.ds(aligned(at, 16), step), :].astype(F32)
                total = total.astype(BF)
            target[to, :] = total
            return nothing

        lax.fori_loop(0, rows // step, one, 0)

    def reduce_core(k):
        g, rc = chunk(k)[0:2]
        go(lambda: chunk(k)[0].at[:, 1 - c], rc, rs, (k, 0), mate)

    def reduce_y(k):
        g, rc, ry, _, _, _, rows = chunk(k)
        arrived(rc, rs_recv.at[k, 0], rs_send.at[k, 0])
        for o in list(range(1, n_y)) + [0]:
            at = turn(y, o, n_y)
            add_rows(rows, g.at[at, c], 0, [rc.at[at]])
            if o:
                go(
                    lambda o=o: chunk(k)[0].at[turn(y, o, n_y), c], ry.at[o - 1], rs,
                    (k, r_y + o - 1), here.to(y=at),
                )

    def total_of(slots, count, at, step):
        total = None
        for index in range(count):
            value = slots[index, pl.ds(aligned(at, 16), step), :].astype(F32)
            total = value if total is None else total + value
        return total

    def reduce_x(k):
        g, _, ry, rx, _, _, rows = chunk(k)
        by_x, rows_x = splits(rows)[0:2]
        for o in range(1, n_y):
            arrived(ry.at[o - 1], rs_recv.at[k, r_y + o - 1], rs_send.at[k, r_y + o - 1])
        mine = g.at[y, c]
        add_rows(rows, mine, 0, [ry.at[o - 1] for o in range(1, n_y)])
        for o in range(1, n_x):
            to = turn(x, o, n_x)
            if by_x > 1:

                def make(o=o):
                    at = turn(x, o, n_x) * rows_x
                    return chunk(k)[0].at[y, c, pl.ds(aligned(at, 16), rows_x), :]

                go(make, rx.at[o - 1], rs, (k, r_x + o - 1), here.to(x=to))
            else:
                go(lambda: chunk(k)[0].at[y, c], rx.at[x], rs, (k, r_x + o - 1), here.to(x=to))

    def reduce_z(k):
        g, _, _, rx, rz, _, rows = chunk(k)
        by_x, rows_x, by_z, rows_z = splits(rows)
        mine = g.at[y, c]
        for o in range(1, n_x):
            slot = rx.at[o - 1] if by_x > 1 else rx.at[turn(x, n_x - o, n_x)]
            arrived(slot, rs_recv.at[k, r_x + o - 1], rs_send.at[k, r_x + o - 1])
        if by_x > 1:
            start = x * rows_x
            add_rows(rows_x, mine, start, [rx.at[o - 1] for o in range(1, n_x)])
        else:
            start = 0
            rx[x] = mine[...]
            for o in range(1, n_x):
                gone(rs, (k, r_x + o - 1))
            step = step_of(rows)

            def one(index, nothing):
                at = pl.ds(aligned(index * step, 16), step)
                g[y, c, at, :] = total_of(rx, n_x, index * step, step).astype(BF)
                return nothing

            lax.fori_loop(0, rows // step, one, 0)
        for o in range(1, n_z):

            def make(o=o):
                at = x * rows_x if by_x > 1 else 0
                if by_z > 1:
                    at = at + turn(z, o, n_z) * rows_z
                return chunk(k)[0].at[y, c, pl.ds(aligned(at, 16), rows_z), :]

            slot = rz.at[o - 1] if by_z > 1 else rz.at[z]
            go(make, slot, rs, (k, r_z + o - 1), here.to(z=turn(z, o, n_z)))

    def gather_z(k):
        g, _, _, _, rz, res, rows = chunk(k)
        by_x, rows_x, by_z, rows_z = splits(rows)
        start = x * rows_x if by_x > 1 else 0
        if by_z > 1:
            start = start + z * rows_z
        for o in range(1, n_z):
            slot = rz.at[o - 1] if by_z > 1 else rz.at[turn(z, n_z - o, n_z)]
            arrived(slot, rs_recv.at[k, r_z + o - 1], rs_send.at[k, r_z + o - 1])
        own_slot = n_z - 1 if by_z > 1 else z
        rz[own_slot] = g[y, c, pl.ds(aligned(start, 16), rows_z), :]
        share = 1.0 / ((1 if by_x > 1 else n_x) * (1 if by_z > 1 else n_z))
        step = step_of(rows_z, 96)

        def one(index, total):
            low = total_of(rz, n_z, index * step, step).astype(BF)
            res[pl.ds(aligned(start + index * step, 16), step), :] = low
            wide = low.astype(F32)
            return total + fold(wide * wide)

        total = lax.fori_loop(0, rows_z // step, one, zeros) * share
        for at in range(0, D, 128):
            square_sum[...] = square_sum[...] + total[:, at : at + 128]
        if by_z > 1:

            def make():
                at = x * rows_x if by_x > 1 else 0
                return chunk(k)[5].at[pl.ds(aligned(at + z * rows_z, 16), rows_z), :]

            for o in range(1, n_z):
                go(make, make(), rs, (k, r_gz + o - 1), here.to(z=turn(z, o, n_z)))

    def gather_x(k):
        res, rows = chunk(k)[5:7]
        by_x, rows_x, by_z, rows_z = splits(rows)
        if by_z > 1:
            for o in range(1, n_z):
                start = turn(z, n_z - o, n_z) * rows_z
                if by_x > 1:
                    start = start + x * rows_x
                arrived(
                    res.at[pl.ds(aligned(start, 16), rows_z), :],
                    rs_recv.at[k, r_gz + o - 1], rs_send.at[k, r_gz + o - 1],
                )
        if by_x > 1:

            def make():
                return chunk(k)[5].at[pl.ds(aligned(x * rows_x, 16), rows_x), :]

            for o in range(1, n_x):
                go(make, make(), rs, (k, r_gx + o - 1), here.to(x=turn(x, o, n_x)))

    def result(k):
        if k < CHUNKS:
            return pltpu.make_async_copy(RES.at[k], res_out.at[k], out_local.at[1 + k])
        return pltpu.make_async_copy(
            SRES.at[k - CHUNKS], small_out.at[k - CHUNKS], out_local.at[1 + k]
        )

    def gather_done(k):
        res, rows = chunk(k)[5:7]
        by_x, rows_x = splits(rows)[0:2]
        if by_x > 1:
            for o in range(1, n_x):
                start = turn(x, n_x - o, n_x) * rows_x
                arrived(
                    res.at[pl.ds(aligned(start, 16), rows_x), :],
                    rs_recv.at[k, r_gx + o - 1], rs_send.at[k, r_gx + o - 1],
                )
        result(k).start()

    for k in range(CHUNKS + 2):
        actions[f"core{k}"] = functools.partial(reduce_core, k)
        actions[f"y{k}"] = functools.partial(reduce_y, k)
        actions[f"x{k}"] = functools.partial(reduce_x, k)
        actions[f"z{k}"] = functools.partial(reduce_z, k)
        actions[f"gz{k}"] = functools.partial(gather_z, k)
        actions[f"gx{k}"] = functools.partial(gather_x, k)
        actions[f"gd{k}"] = functools.partial(gather_done, k)
    actions.update(
        fc=factors_core, fy=factors_y, fz=factors_z, fx=factors_x, fv=factors_side,
        fm=factors_mate, fd=factors_done,
    )

    def tails(ref, layer=None):
        found = []
        for image in range(KEPT):
            rows = slice(image * BLK + TAIL, (image + 1) * BLK)
            found.append(ref[rows, :] if layer is None else ref[layer, rows, :])
        return jnp.concatenate(found, axis=0)

    @pl.when(lower)
    def _():
        arrived(lab.at[1], img_recv.at[2], img_send.at[2])

    marked = lab[...].reshape(CROWS, 128)[:, 0:1]

    h1 = tails(DXB)
    stream = tails(X)
    query = ((mm(h1, win[last, :, 0:D]) + vector(last, 2 * D, D)).astype(BF)) * BF(0.125)
    head_masks = [lane_mask(D, index * 64, (index + 1) * 64) for index in range(HEADS)]

    def spread(values):
        return jnp.concatenate([values * mask for mask in head_masks], axis=0)

    def gather_heads(values):
        total = None
        for index in range(HEADS):
            part = values[index * 16 : (index + 1) * 16] * head_masks[index].astype(F32)
            total = part if total is None else total + part
        return total

    spread_queries, probabilities, outs = [], [], []
    for image in range(KEPT):
        rows = slice(image * BLK, (image + 1) * BLK)
        queries = spread(query[image * 16 : (image + 1) * 16])
        scores = mm_nt(queries, DMB[rows, :]) + key_row
        raw = jnp.exp(scores - jnp.max(scores, axis=-1, keepdims=True))
        probs = raw * (1.0 / jnp.sum(raw, axis=-1, keepdims=True))
        spread_queries.append(queries)
        probabilities.append(probs)
        outs.append(gather_heads(mm(probs.astype(BF), DA[rows, :])))
    attended = jnp.concatenate(outs, axis=0).astype(BF)
    middle = stream + mm(attended, win[last, :, 3 * D : 4 * D]) + vector(last, 4 * D, D)
    n2, i2 = norm(middle)
    h2 = (n2 * vector(last, 5 * D, D) + vector(last, 6 * D, D)).astype(BF)
    active, slope = gelu_parts(mm(h2, win[last, :, 4 * D :]) + vector(last, 7 * D, FF))
    active = active.astype(BF)
    top = middle + mm(active, wdn[last]) + vector(last, 7 * D + FF, D)
    gain_final = glob[2:3, :]
    nf, inf = norm(top)
    final = (nf * gain_final + glob[3:4, :]).astype(BF)
    class_lane = lax.broadcasted_iota(jnp.int32, (1, CPAD), 1)
    logits = mm(final, low_head[...]) + head_bias[...]
    logits = jnp.where(class_lane < NCLS, logits, -1e30)
    peak = jnp.max(logits, axis=-1, keepdims=True)
    shifted = logits - peak
    raw = jnp.exp(shifted)
    total = jnp.sum(raw, axis=-1, keepdims=True)
    alive = jnp.where(marked >= 0.0, 1.0, 0.0)
    target = jnp.where(class_lane.astype(F32) == marked, 1.0 - SMOOTHING, 0.0) + jnp.where(
        class_lane < NCLS, SMOOTHING / NCLS, 0.0
    )
    log_probs = jnp.where(class_lane < NCLS, shifted - jnp.log(total), 0.0)
    losses = -jnp.sum(target * log_probs, axis=-1, keepdims=True) * alive
    d_logits = ((raw * (1.0 / total) - target) * alive).astype(BF)
    d_final = mm_nt(d_logits, low_head[...])
    last_row = VEC_AT + 12 * LAYERS
    V[last_row : last_row + 1, 0:D] = down_sum(d_final * nf)
    V[last_row + 1 : last_row + 2, 0:D] = down_sum(d_final)
    V[last_row + 2 : last_row + 3, 0:128] = jnp.broadcast_to(down_sum(losses), (1, 128))
    V[last_row + 3 : last_row + 4, 0:128] = jnp.full((1, 128), counts[0].astype(F32), F32)
    d_top = norm_back(d_final, nf, inf, gain_final)
    low_top = d_top.astype(BF)
    store_vector(last, 7 * D + FF, down_sum(d_top))
    d_up = (mm_nt(low_top, wdn[last]) * slope).astype(BF)
    store_vector(last, 7 * D, down_sum(d_up.astype(F32)))
    d_h2 = mm_nt(d_up, win[last, :, 4 * D :])
    store_vector(last, 5 * D, down_sum(d_h2 * n2))
    store_vector(last, 6 * D, down_sum(d_h2))
    d_middle = d_top + norm_back(d_h2, n2, i2, vector(last, 5 * D, D))
    low_middle = d_middle.astype(BF)
    store_vector(last, 4 * D, down_sum(d_middle))
    d_heads = mm_nt(low_middle, win[last, :, 3 * D : 4 * D]).astype(BF)
    d_queries = []
    for image in range(KEPT):
        rows = slice(image * BLK, (image + 1) * BLK)
        ups = spread(d_heads[image * 16 : (image + 1) * 16])
        probs = probabilities[image]
        d_probs = mm_nt(ups, DA[rows, :])
        inner = jnp.sum(d_probs * probs, axis=-1, keepdims=True)
        d_scores = (probs * (d_probs - inner)).astype(BF)
        d_queries.append(gather_heads(mm(d_scores, DMB[rows, :])) * 0.125)
        DMB[rows, :] = mm_tn(d_scores, spread_queries[image]).astype(BF)
        DA[rows, :] = mm_tn(probs.astype(BF), ups).astype(BF)
    d_query = jnp.concatenate(d_queries, axis=0).astype(BF)
    store_vector(last, 2 * D, down_sum(d_query.astype(F32)))
    from_query = mm_nt(d_query, win[last, :, 0:D])

    pick_row = lax.broadcasted_iota(jnp.int32, (group, CROWS), 0)
    pick_lane = lax.broadcasted_iota(jnp.int32, (group, CROWS), 1)
    pick = jnp.where(
        ((pick_row - KEPT * here.shard) * 16 + (CLS - TAIL)) == pick_lane, 1.0, 0.0
    ).astype(BF)
    def keep_factors(half, pieces_of):
        at = 0
        for piece in pieces_of:
            made = None if piece is None else mm(pick, piece).astype(BF)
            for lane in range(0, WFAC - at if made is None else made.shape[-1], 128):
                part, column = divmod(at + lane, part_wide)
                FAC[half, part, :, column : column + 128] = (
                    jnp.zeros((group, 128), BF) if made is None else made[:, lane : lane + 128]
                )
            at += 0 if made is None else made.shape[-1]

    keep_factors(0, (active, h2, attended, h1, final, low_top, None))
    keep_factors(1, (d_up, low_middle, d_query, d_logits, None))
    at_place("class")

    turned = DXB[...].T
    for tile, grads in enumerate((DMB, DA)):
        made = mm(turned, grads[...]).astype(BF)
        for shard in range(n_shard):
            GS[0, shard // 2, shard % 2, tile * rows_in : (tile + 1) * rows_in, :] = made[
                shard * rows_in : (shard + 1) * rows_in
            ]
    at_place("kv")
    store_sums(last, [(3 * D, fold(DA[...].astype(F32)))])

    X[...] = jnp.zeros((ROWS, D), F32)
    gain = vector(last, 0, D)
    gain_sum, shift_sum = zeros, zeros
    for image in range(KEPT):
        rows = slice(image * BLK + TAIL, (image + 1) * BLK)
        part = from_query[image * 16 : (image + 1) * 16]
        normed = N1[last, rows, :].astype(F32)
        gain_sum = gain_sum + fold(part * normed)
        shift_sum = shift_sum + fold(part)
        X[rows, :] = d_middle[image * 16 : (image + 1) * 16] + norm_back(
            part, normed, whole_lanes_of(I1[last, rows, :]), gain
        )

    def first_back(layer, half, made, sums):
        base = half * HALF
        gain = vector(layer, 0, D)
        gain_sum, shift_sum = sums
        for at, size in pieces(HALF):
            rows = pl.ds(aligned(base + at, 16), size)
            part = made[at : at + size]
            normed = N1[layer, rows, :].astype(F32)
            inverse = whole_lanes_of(I1[layer, rows, :])
            gain_sum = gain_sum + fold(part * normed)
            shift_sum = shift_sum + fold(part)
            X[rows, :] = X[rows, :] + norm_back(part, normed, inverse, gain)
        return gain_sum, shift_sum

    def last_back(half, sums):
        rows = pl.ds(aligned(half * HALF, 16), HALF)
        made = mm_nt(DMB[rows, :], win[last, :, D : 2 * D])
        made = made + mm_nt(DA[rows, :], win[last, :, 2 * D : 3 * D])
        sums = first_back(last, half, made, sums)
        at_place("lb", half)
        return sums

    gain_sum, shift_sum = lax.fori_loop(0, 2, last_back, (gain_sum, shift_sum))
    store_sums(last, [(0, gain_sum), (D, shift_sum)])

    def round_up(half, total):
        for at, size in pieces(HALF):
            rows = pl.ds(aligned(half * HALF + at, 16), size)
            up = X[rows, :]
            DXB[rows, :] = up.astype(BF)
            total = total + fold(up)
        return total

    def act_back(layer, half, totals):
        base = half * HALF
        low = DXB[pl.ds(aligned(base, 16), HALF), :]
        ups = []
        for pair in range(2):
            made = mm_nt(low, wdn[layer, 2 * pair * D : 2 * (pair + 1) * D, :])
            for tile in range(2):
                start = (2 * pair + tile) * D
                columns = slice(start, start + D)
                total = totals[2 * pair + tile]
                for at, size in pieces(HALF):
                    rows = pl.ds(aligned(base + at, 16), size)
                    part = made[at : at + size, tile * D : (tile + 1) * D]
                    grad = (part * SLOPE[layer, rows, columns].astype(F32)).astype(BF)
                    DH[rows, columns] = grad
                    total = total + fold(grad.astype(F32))
                ups.append(total)
        return tuple(ups)

    def mlp_back(layer, half, sums):
        base = half * HALF
        whole = pl.ds(aligned(base, 16), HALF)
        gain_sum, shift_sum, bias_out = sums
        made = mm_nt(DH[whole, :], win[layer, :, 4 * D :])
        gain = vector(layer, 5 * D, D)
        for at, size in pieces(HALF):
            rows = pl.ds(aligned(base + at, 16), size)
            part = made[at : at + size]
            normed = N2[layer, rows, :].astype(F32)
            inverse = whole_lanes_of(I2[layer, rows, :])
            gain_sum = gain_sum + fold(part * normed)
            shift_sum = shift_sum + fold(part)
            grad = X[rows, :] + norm_back(part, normed, inverse, gain)
            X[rows, :] = grad
            DMB[rows, :] = grad.astype(BF)
            bias_out = bias_out + fold(grad)
        DA[whole, :] = mm_nt(DMB[whole, :], win[layer, :, 3 * D : 4 * D]).astype(BF)
        return gain_sum, shift_sum, bias_out

    def attend_back(layer, image):
        rows = pl.ds(aligned(image * BLK, 16), BLK)
        for pair in range(3):
            at = pair * 128
            query = QKV[layer, rows, at : at + 128] * BF(0.125)
            keys = QKV[layer, rows, D + at : D + at + 128]
            values = QKV[layer, rows, 2 * D + at : 2 * D + at + 128]
            ups = DA[rows, at : at + 128]
            keys_both = jnp.concatenate([keys * even, keys * odd], axis=0)
            values_both = jnp.concatenate([values * even, values * odd], axis=0)
            query = jnp.concatenate([query, fill], axis=0)
            ups = jnp.concatenate([ups, fill], axis=0)
            scores = mm_nt(keys_both, query)
            d_probs = mm_nt(values_both, ups)
            probs, d_scores = [], []
            for base in (0, BLK):
                low_probs, low_grads = [], []
                for first, end in ((0, 128), (128, lanes)):
                    part = jnp.concatenate(
                        [
                            scores[base : base + TAIL, first:end],
                            scores[base + TAIL : base + BLK, first:end] + key_column[TAIL:],
                        ],
                        axis=0,
                    )
                    raw = jnp.exp(part - jnp.max(part, axis=0, keepdims=True))
                    prob = raw * (1.0 / jnp.sum(raw, axis=0, keepdims=True))
                    grad = d_probs[base : base + BLK, first:end]
                    inner = jnp.sum(grad * prob, axis=0, keepdims=True)
                    low_grads.append((prob * (grad - inner)).astype(BF))
                    low_probs.append(prob.astype(BF))
                probs.append(jnp.concatenate(low_probs, axis=1))
                d_scores.append(jnp.concatenate(low_grads, axis=1))
            probs = jnp.concatenate(probs, axis=0)
            d_scores = jnp.concatenate(d_scores, axis=0)
            d_values = mm(probs, ups)
            d_keys = mm(d_scores, query)
            d_query = mm_tn(d_scores, keys_both)[:BLK] * 0.125
            DH[rows, at : at + 128] = d_query.astype(BF)
            DH[rows, D + at : D + at + 128] = jnp.where(
                low_lane, d_keys[:BLK], d_keys[BLK:]
            ).astype(BF)
            DH[rows, 2 * D + at : 2 * D + at + 128] = jnp.where(
                low_lane, d_values[:BLK], d_values[BLK:]
            ).astype(BF)

    def renew(ref, layer, at):
        gain, shift = vector(layer, at, D), vector(layer, at + D, D)

        def one(index, nothing):
            for at, size in pieces(BLK):
                rows = pl.ds(aligned(index * BLK + at, 16), size)
                DXB[rows, :] = (ref[layer, rows, :].astype(F32) * gain + shift).astype(BF)
            return nothing

        lax.fori_loop(0, KEPT, one, 0)
        return DXB[...].T

    def keep_in(k, tile, made):
        for shard in range(n_shard):
            G[k, shard // 2, shard % 2, tile * rows_in : (tile + 1) * rows_in, :] = made[
                shard * rows_in : (shard + 1) * rows_in
            ]

    def backward(step, carry):
        layer = LAYERS - 2 - step
        kd, ku, kq = 3 * step, 3 * step + 1, 3 * step + 2
        bias_down = lax.fori_loop(0, 2, round_up, zeros)
        at_place("round", layer)
        turned = DXB[...].T
        per = min(rows_down, D)
        for pair in range(2):
            start = 2 * pair * D
            wide = mm(turned, ACT[layer, :, start : start + 2 * D]).astype(BF)
            for tile in range(2):
                made = wide[:, tile * D : (tile + 1) * D].T
                for piece in range(D // per):
                    shard, at = divmod(start + tile * D + piece * per, rows_down)
                    G[kd, shard // 2, shard % 2, at : at + per, :] = made[
                        piece * per : (piece + 1) * per
                    ]
        at_place("dn", layer)

        def one(half, totals):
            totals = act_back(layer, half, totals)
            at_place("act", layer, half)
            return totals

        bias_up = lax.fori_loop(0, 2, one, (zeros,) * 4)
        turned = renew(N2, layer, 5 * D)
        for pair in range(2):
            made = mm(turned, DH[:, 2 * pair * D : 2 * (pair + 1) * D]).astype(BF)
            keep_in(ku, 2 * pair, made[:, :D])
            keep_in(ku, 2 * pair + 1, made[:, D:])
        at_place("ups", layer)

        def one_more(half, sums):
            sums = mlp_back(layer, half, sums)
            at_place("mlpb", layer, half)
            return sums

        gain_sum, shift_sum, bias_out = lax.fori_loop(0, 2, one_more, (zeros, zeros, zeros))
        store_sums(
            layer,
            [(7 * D + FF, bias_down), (5 * D, gain_sum), (6 * D, shift_sum), (4 * D, bias_out)]
            + [(7 * D + tile * D, bias_up[tile]) for tile in range(4)],
        )
        keep_in(kq, 3, mm(ATT[layer].T, DMB[...]).astype(BF))
        at_place("out", layer)

        def two(image, nothing):
            attend_back(layer, image)
            at_place("attb", layer, image)
            return nothing

        lax.fori_loop(0, KEPT, two, 0)
        turned = renew(N1, layer, 0)
        made = mm(turned, DH[:, 0 : 2 * D]).astype(BF)
        keep_in(kq, 0, made[:, :D])
        keep_in(kq, 1, made[:, D:])
        keep_in(kq, 2, mm(turned, DH[:, 2 * D : 3 * D]).astype(BF))
        at_place("qkv", layer)
        store_sums(
            layer,
            [
                (2 * D, fold(DH[:, 0:D].astype(F32))),
                (3 * D, fold(DH[:, 2 * D : 3 * D].astype(F32))),
            ],
        )

        def three(half, sums):
            rows = pl.ds(aligned(half * HALF, 16), HALF)
            made = mm_nt(DH[rows, 0 : 3 * D], win[layer, :, 0 : 3 * D])
            sums = first_back(layer, half, made, sums)
            at_place("fb", layer, half)
            return sums

        gain_sum, shift_sum = lax.fori_loop(0, 2, three, (zeros, zeros))
        store_sums(layer, [(0, gain_sum), (D, shift_sum)])
        return carry

    lax.fori_loop(0, LAYERS - 1, backward, 0)

    for at, size in pieces(BLK):
        total = None
        for image in range(KEPT):
            part = X[image * BLK + at : image * BLK + at + size, :]
            DXB[image * BLK + at : image * BLK + at + size, :] = part.astype(BF)
            total = part if total is None else total + part
        V[at : at + size, 0:D] = total

    vec = ("v", v_send, v_recv)
    v_y, v_x = 1, n_y
    v_z = v_x + n_x - 1
    v_gz = v_z + n_z - 1
    v_gx = v_gz + n_z - 1
    v_gy = v_gx + n_x - 1
    v_gc = v_gy + n_y - 1
    rows_c = VEC_ROWS // 2
    rows_y = rows_c // n_y
    rows_x = rows_y // n_x
    split_z = cut(rows_x, n_z, 8)
    rows_z = rows_x // split_z
    at_c = c * rows_c
    at_y = at_c + y * rows_y
    at_x = at_y + x * rows_x
    at_z = at_x + z * rows_z if split_z > 1 else at_x

    def vrows(ref, at, rows):
        return ref.at[pl.ds(aligned(at, 8), rows), :]

    def vadd(at, rows, sources):
        target = pl.ds(aligned(at, 8), rows)
        total = V[target, :]
        for source in sources:
            total = total + source
        V[target, :] = total

    def vectors_core():
        go(lambda: vrows(V, (1 - c) * rows_c, rows_c), VC, vec, 0, mate)

    def vectors_y():
        arrived(VC, v_recv.at[0], v_send.at[0])
        vadd(at_c, rows_c, [VC[...]])
        for o in range(1, n_y):
            to = turn(y, o, n_y)
            go(
                lambda o=o: vrows(V, at_c + turn(y, o, n_y) * rows_y, rows_y), VY.at[o - 1],
                vec, v_y + o - 1, here.to(y=to),
            )

    def vectors_x():
        for o in range(1, n_y):
            arrived(VY.at[o - 1], v_recv.at[v_y + o - 1], v_send.at[v_y + o - 1])
        vadd(at_y, rows_y, [VY[o - 1] for o in range(1, n_y)])
        for o in range(1, n_x):
            to = turn(x, o, n_x)
            go(
                lambda o=o: vrows(V, at_y + turn(x, o, n_x) * rows_x, rows_x), VX.at[o - 1],
                vec, v_x + o - 1, here.to(x=to),
            )

    def vectors_z():
        for o in range(1, n_x):
            arrived(VX.at[o - 1], v_recv.at[v_x + o - 1], v_send.at[v_x + o - 1])
        vadd(at_x, rows_x, [VX[o - 1] for o in range(1, n_x)])
        for o in range(1, n_z):

            def make(o=o):
                at = at_x + turn(z, o, n_z) * rows_z if split_z > 1 else at_x
                return vrows(V, at, rows_z)

            go(make, VZ.at[z], vec, v_z + o - 1, here.to(z=turn(z, o, n_z)))

    def vectors_gather_z():
        for o in range(1, n_z):
            arrived(
                VZ.at[turn(z, n_z - o, n_z)], v_recv.at[v_z + o - 1], v_send.at[v_z + o - 1]
            )
        target = pl.ds(aligned(at_z, 8), rows_z)
        VZ[z] = V[target, :]
        total = VZ[0]
        for index in range(1, n_z):
            total = total + VZ[index]
        VF[target, :] = total
        if split_z > 1:
            for o in range(1, n_z):
                go(
                    lambda: vrows(VF, at_z, rows_z), vrows(VF, at_z, rows_z), vec, v_gz + o - 1,
                    here.to(z=turn(z, o, n_z)),
                )

    def vectors_gather_x():
        if split_z > 1:
            for o in range(1, n_z):
                came = turn(z, n_z - o, n_z)
                arrived(
                    vrows(VF, at_x + came * rows_z, rows_z), v_recv.at[v_gz + o - 1],
                    v_send.at[v_gz + o - 1],
                )
        for o in range(1, n_x):
            go(
                lambda: vrows(VF, at_x, rows_x), vrows(VF, at_x, rows_x), vec, v_gx + o - 1,
                here.to(x=turn(x, o, n_x)),
            )

    sq = ("q", q_send, q_recv)

    def squares_z():
        SQ[0] = square_sum[...]
        SQZ[z] = square_sum[...]
        for o in range(1, n_z):
            go(lambda: SQ.at[0], SQZ.at[z], sq, o - 1, here.to(z=turn(z, o, n_z)))

    def slot_of(i, j, k):
        return (i * n_y + j) * 2 + k

    def squares_plane():
        for o in range(1, n_z):
            arrived(SQZ.at[turn(z, n_z - o, n_z)], q_recv.at[o - 1], q_send.at[o - 1])
        total = SQZ[0]
        for index in range(1, n_z):
            total = total + SQZ[index]
        SQ[1] = total
        SQP[slot_of(x, y, c)] = total
        for index, step in enumerate(plane):
            go(
                lambda: SQ.at[1], SQP.at[slot_of(x, y, c)], sq, n_z - 1 + index,
                in_plane(step),
            )

    def squares_done():
        for index, (i, j, k) in enumerate(plane):
            slot = slot_of(
                turn(x, n_x - i, n_x), turn(y, n_y - j, n_y), lax.rem(c + k, 2)
            )
            arrived(SQP.at[slot], q_recv.at[n_z - 1 + index], q_send.at[n_z - 1 + index])
        total = SQP[0]
        for index in range(1, 2 * n_x * n_y):
            total = total + SQP[index]
        SQ[2] = total

    def vectors_gather_y():
        for o in range(1, n_x):
            at = at_y + turn(x, n_x - o, n_x) * rows_x
            arrived(vrows(VF, at, rows_x), v_recv.at[v_gx + o - 1], v_send.at[v_gx + o - 1])
        for o in range(1, n_y):
            go(
                lambda: vrows(VF, at_y, rows_y), vrows(VF, at_y, rows_y), vec, v_gy + o - 1,
                here.to(y=turn(y, o, n_y)),
            )

    def vectors_gather_core():
        for o in range(1, n_y):
            at = at_c + turn(y, n_y - o, n_y) * rows_y
            arrived(vrows(VF, at, rows_y), v_recv.at[v_gy + o - 1], v_send.at[v_gy + o - 1])
        go(lambda: vrows(VF, at_c, rows_c), vrows(VF, at_c, rows_c), vec, v_gc, mate)

    def vectors_done():
        arrived(vrows(VF, (1 - c) * rows_c, rows_c), v_recv.at[v_gc], v_send.at[v_gc])

    actions.update(
        vc=vectors_core, vy=vectors_y, vx=vectors_x, vz=vectors_z, vgz=vectors_gather_z,
        vgx=vectors_gather_x, vgy=vectors_gather_y, vgc=vectors_gather_core, vd=vectors_done,
        qz=squares_z, qp=squares_plane, qd=squares_done,
    )
    at_place("emb")
    low = DXB[...]
    for tile in range(2):
        made = mm_tn(pix[:, :, tile * D : (tile + 1) * D].reshape(ROWS, D), low).astype(BF)
        for piece in range(D // rows_patch):
            shard = tile * (D // rows_patch) + piece
            GS[1, shard // 2, shard % 2, 0:rows_patch, :] = made[piece * rows_patch : (piece + 1) * rows_patch]

    at_place("patch")
    ending = SCHEDULE["tail",]
    perform(ending[:-6])
    early = [
        key for key in sent
        if key[0] == "ag" or (key[0] == "rs" and key[1][0] not in (4, 5, 7))
    ]
    for key in early:
        source, send, recv, at = sent.pop(key)
        left_here(source(), recv.at[at], send.at[at])
    perform(ending[-6:])
    last_copies = [
        pltpu.make_async_copy(VF, vec_out, out_local.at[1 + CHUNKS + 2]),
        pltpu.make_async_copy(SQ.at[2], square_out, out_local.at[2 + CHUNKS + 2]),
    ]
    for copy in last_copies:
        copy.start()
    for source, send, recv, at in list(sent.values()):
        left_here(source(), recv.at[at], send.at[at])
    for k in range(CHUNKS + 2):
        result(k).wait()
    for copy in last_copies:
        copy.wait()

    @pl.when(jnp.logical_not(lower))
    def _():
        for index in range(2):
            left_here(given[index], img_recv.at[index], img_send.at[index])
        left_here(lab_given, img_recv.at[2], img_send.at[2])


def run_train(
    n_rep, n_shard, patches, patch_ends, labels, counts, own_patch, own_in, own_down, vecs, glob, pos, head
):
    n_x = 2 ** ((n_rep.bit_length() - 2) // 2)
    n_z, n_y = n_rep // n_x, n_shard // 2
    block = 4 * (D // n_shard)
    small_block = small_rows(block // 2, n_x, n_z)
    group = KEPT * n_shard
    keep = LAYERS - 1
    units = 1 + 3 * LAYERS
    chunks = CHUNKS + 2

    def buf(*shape, dtype=BF):
        return pltpu.VMEM(shape, dtype)

    def sems(*shape):
        return pltpu.SemaphoreType.DMA(shape)

    def reduction(count, slots, rows):
        by_x = cut(rows, n_x, 16)
        by_z = cut(rows // by_x, n_z, 16)
        return [
            buf(count, n_y, 2, rows, D),
            buf(slots, n_y, rows, D),
            buf(slots, n_y - 1, rows, D),
            buf(slots, n_x - 1 if by_x > 1 else n_x, rows // by_x, D),
            buf(slots, n_z, rows // by_x // by_z, D),
            buf(count, rows, D),
        ]

    rows_y = VEC_ROWS // 2 // n_y
    rows_x = rows_y // n_x
    rows_z = rows_x // cut(rows_x, n_z, 8)
    ag_count = n_y + (n_y - 1) * (n_x - 1) * 2 + n_y - 1
    rs_count = 1 + (n_y - 1) + 2 * (n_x - 1) + 2 * (n_z - 1)
    f_count = 1 + 2 * (n_y - 1) + (n_x - 1) + (n_z - 1) + 1
    v_count = 1 + 2 * (n_y - 1) + 2 * (n_x - 1) + 2 * (n_z - 1) + 1
    q_count = n_z - 1 + 2 * n_x * n_y - 1
    whole = pl.BlockSpec(memory_space=pltpu.VMEM)
    there = pl.BlockSpec(memory_space=pl.ANY)
    return pl.pallas_call(
        functools.partial(train, n_rep, n_shard),
        out_shape=[
            jax.ShapeDtypeStruct((CHUNKS, block, D), BF),
            jax.ShapeDtypeStruct((2, small_block, D), BF),
            jax.ShapeDtypeStruct((VEC_ROWS, VEC_WIDE), F32),
            jax.ShapeDtypeStruct((8, 128), F32),
            jax.ShapeDtypeStruct((2, n_y, n_x, n_z, group, WFAC // n_y), BF),
        ],
        in_specs=[there] * 2 + [pl.BlockSpec(memory_space=pltpu.SMEM)] * 2 + [there] * 3 + [whole] * 2 + [there] * 2,
        out_specs=[there] * 5,
        scratch_shapes=[
            buf(ROWS, D, dtype=F32),
            buf(LAYERS, ROWS, D),
            buf(LAYERS, ROWS, 128, dtype=F32),
            buf(keep, ROWS, 3 * D),
            buf(keep, ROWS, D),
            buf(keep, ROWS, D),
            buf(keep, ROWS, 128, dtype=F32),
            buf(keep, ROWS, FF),
            buf(keep, ROWS, FF),
            buf(ROWS, D),
            buf(ROWS, D),
            buf(ROWS, D),
            buf(ROWS, FF),
            pltpu.VMEM(pos.shape, F32),
            pltpu.VMEM(head.shape, F32),
            buf(KEPT, BLK, PATCH_DIM),
            buf(2, 32, 128, dtype=F32),
            buf(32, 128, dtype=F32),
            buf(PATCH_DIM, D),
            buf(LAYERS, D, 4 * D + FF),
            buf(LAYERS, FF, D),
            buf(D, CPAD),
            buf(1, CPAD, dtype=F32),
            *reduction(CHUNKS, 3, block),
            *reduction(2, 1, small_block),
            buf(2, n_y, group, WFAC // n_y),
            buf(n_y, group, WFAC // n_y),
            buf(n_y - 1, group, WFAC // n_y),
            buf(VEC_ROWS, VEC_WIDE, dtype=F32),
            buf(VEC_ROWS // 2, VEC_WIDE, dtype=F32),
            buf(n_y - 1, rows_y, VEC_WIDE, dtype=F32),
            buf(n_x - 1, rows_x, VEC_WIDE, dtype=F32),
            buf(n_z, rows_z, VEC_WIDE, dtype=F32),
            buf(VEC_ROWS, VEC_WIDE, dtype=F32),
            buf(3, 8, 128, dtype=F32),
            buf(n_z, 8, 128, dtype=F32),
            buf(2 * n_x * n_y, 8, 128, dtype=F32),
            buf(8, 128, dtype=F32),
            sems(units, ag_count),
            sems(units, ag_count),
            sems(units, 4),
            sems(chunks, rs_count),
            sems(chunks, rs_count),
            sems(f_count),
            sems(f_count),
            sems(v_count),
            sems(v_count),
            sems(q_count),
            sems(q_count),
            sems(3),
            sems(3),
            sems(4),
            sems(2),
            sems(3 + chunks),
        ],
        compiler_params=pltpu.CompilerParams(
            vmem_limit_bytes=65400 * 1024, collective_id=0, has_side_effects=True
        ),
        cost_estimate=pl.CostEstimate(
            flops=24_000_000_000, bytes_accessed=30_000_000, transcendentals=10_000_000
        ),
        name="train_step",
    )(patches, patch_ends, labels, counts, own_patch, own_in, own_down, vecs, glob, pos, head)


def adam(weight, first, second, grad, factor, rate):
    share = grad * factor
    first = BETA_FIRST * first + share
    square_scale = (1.0 - BETA_SECOND) / (1.0 - BETA_FIRST) ** 2
    second = BETA_SECOND * second + square_scale * (share * share)
    root_scale = (1.0 / (1.0 - BETA_SECOND**ADAM_STEP)) ** 0.5
    step_scale = rate / (1.0 - BETA_FIRST**ADAM_STEP) / root_scale
    bottom = second * lax.rsqrt(second) + ADAM_EPS / root_scale
    step = first * lax.rsqrt(bottom * bottom)
    return weight * (1.0 - rate * WEIGHT_DECAY) - step * step_scale, first, second


def update(n_rep, n_shard, *refs):
    res_there, small_there, vec, exchanged, factors = refs[0:5]
    sources = refs[5:26]
    loss_out, norm_out = refs[26:28]
    targets = refs[28:49]
    buffers = refs[49:70]
    results = refs[70:91]
    last_in, last_down, passing, grad_head, res, small, in_sems, out_sems, grad_sems = refs[91:]
    shard = lax.axis_index("shard")
    rows_in = D // n_shard
    rows_down = FF // n_shard
    keep = LAYERS - 1

    def moves(array, layer=None, out=False):
        found = []
        for kind in range(3):
            index = 3 * array + kind
            if out:
                src, dst, sem = results[index], targets[index], out_sems
            else:
                src, dst, sem = sources[index], buffers[index], in_sems
            slot = 0 if layer is None else layer
            if layer is not None:
                src, dst = src.at[layer], dst.at[layer]
            found.append(pltpu.make_async_copy(src, dst, sem.at[index, slot]))
        return found

    order = [(array, layer) for layer in range(keep) for array in (1, 2)]
    order += [(array, None) for array in (0, 4, 3, 5, 6)] + [(1, keep), (2, keep)]
    res_copy = pltpu.make_async_copy(res_there, res, grad_sems.at[0])
    small_copy = pltpu.make_async_copy(small_there, small, grad_sems.at[1])
    res_copy.start()
    small_copy.start()
    for array, layer in order:
        for move in moves(array, layer):
            move.start()

    n_rows = factors.shape[2] * factors.shape[3] * factors.shape[4]
    part_wide = factors.shape[5]

    def factor(half, at, size):
        found = []
        while size:
            part, column = divmod(at, part_wide)
            wide = min(size, part_wide - column)
            piece = factors[half, part, :, :, :, column : column + wide]
            found.append(piece.reshape(n_rows, wide))
            at, size = at + wide, size - wide
        return found[0] if len(found) == 1 else jnp.concatenate(found, axis=1)

    def gram_squares(left, right):
        total = jnp.zeros((8, 128), F32)
        for row in range(0, n_rows, 128):
            both = mm_nt(left[row : row + 128], left) * mm_nt(right[row : row + 128], right)
            both = fold(both)
            for lane in range(0, n_rows, 128):
                total = total + both[:, lane : lane + 128]
        return total

    d_logits = factor(1, FF + 2 * D, CPAD)
    head_bias = down_sum(d_logits.astype(F32))
    wide = gram_squares(factor(0, 0, FF), factor(0, FF + 4 * D, D))
    wide = wide + gram_squares(factor(0, FF, D), factor(1, 0, FF))
    wide = wide + gram_squares(factor(0, FF + D, D), factor(1, FF, D))
    wide = wide + gram_squares(factor(0, FF + 2 * D, D), factor(1, FF + D, D))
    wide = wide + gram_squares(factor(0, FF + 3 * D, D), d_logits)
    for lane in range(0, CPAD, 128):
        row = head_bias[:, lane : lane + 128]
        wide = wide + (row * row) * 0.125
    used = VEC_AT + 12 * LAYERS + 2
    parts = jnp.zeros((8, D), F32)
    kept_rows = lax.broadcasted_iota(jnp.int32, (8, 1), 0)
    for at in range(0, used, 8):
        value = vec[at : at + 8, 0:D]
        if at + 8 > used:
            value = jnp.where(kept_rows + at < used, value, 0.0)
        parts = parts + value * value
    patch_bias = down_sum(vec[0:PATCHES, 0:D])
    class_row = vec[CLS : CLS + 1, 0:D]
    rest = (patch_bias * patch_bias + class_row * class_row) * 0.125
    parts = parts + rest
    for lane in range(0, D, 128):
        wide = wide + parts[:, lane : lane + 128]
    wide = wide + exchanged[...]
    sum_squares = jnp.sum(jnp.sum(wide, axis=1, keepdims=True), axis=0, keepdims=True)
    inv_count = 1.0 / vec[used + 1 : used + 2, 0:1]
    grad_norm = jnp.sqrt(sum_squares) * inv_count
    norm_out[...] = grad_norm
    loss_out[...] = vec[used : used + 1, 0:1] * inv_count
    scale = jnp.minimum(1.0, CLIP_NORM / grad_norm) * inv_count * (1.0 - BETA_FIRST)

    def apply(array, where, grad, rate):
        refs = [buffers[3 * array + kind] for kind in range(3)]
        made = adam(refs[0][where], refs[1][where], refs[2][where], grad, scale, rate)
        for kind, value in enumerate(made):
            results[3 * array + kind][where] = value

    def begin(array, layer=None):
        for move in moves(array, layer):
            move.wait()

    def finish(array, layer=None):
        for move in moves(array, layer, out=True):
            move.start()

    def loop(count, body):
        def one(index, nothing):
            body(index)
            return nothing

        lax.fori_loop(0, count, one, 0)

    step = 32 if rows_in % 32 == 0 else 16

    def update_in(layer):
        begin(1, layer)

        def column_of(column):
            lanes = pl.ds(pl.multiple_of(column * D, 128), D)
            for at in range(0, rows_in, step):
                if layer < keep:
                    k = 3 * (keep - 1 - layer) + jnp.where(column < 4, 2, 1)
                    row = pl.multiple_of(lax.rem(column, 4) * rows_in + at, 16)
                    grad = res[k, pl.ds(row, step), :].astype(F32)
                else:
                    grad = last_in[at : at + step, lanes]
                apply(1, (layer, slice(at, at + step), lanes), grad, LEARNING_RATE)

        loop(8, column_of)
        finish(1, layer)

    def update_down(layer):
        begin(2, layer)

        def rows_of(index):
            for part in range(3):
                at = pl.multiple_of(index * 96 + part * 32, 16)
                if layer < keep:
                    grad = res[3 * (keep - 1 - layer), pl.ds(at, 32), :].astype(F32)
                else:
                    grad = last_down[pl.ds(at, 32), :]
                apply(2, (layer, pl.ds(at, 32), slice(0, D)), grad, LEARNING_RATE)

        loop(rows_down // 96, rows_of)
        finish(2, layer)

    res_copy.wait()
    for layer in range(keep):
        update_in(layer)
        update_down(layer)
    small_copy.wait()
    begin(0)

    def patch_rows(index):
        for part in range(3):
            at = pl.multiple_of(index * 96 + part * 32, 16)
            grad = small[1, pl.ds(at, 32), :].astype(F32)
            apply(0, (pl.ds(at, 32), slice(0, D)), grad, LEARNING_RATE)

    loop(PATCH_DIM // n_shard // 96, patch_rows)
    finish(0)
    begin(4)
    rows = [patch_bias, class_row, vec[used - 2 : used - 1, 0:D], vec[used - 1 : used, 0:D]]
    for index, row in enumerate(rows):
        apply(4, (slice(index, index + 1), slice(0, D)), row, VECTOR_RATE)
    finish(4)
    begin(3)
    for layer in range(LAYERS):
        for piece in range(12):
            row = VEC_AT + 12 * layer + piece
            where = (slice(layer, layer + 1), slice(piece * D, (piece + 1) * D))
            apply(3, where, vec[row : row + 1, 0:D], VECTOR_RATE)
    finish(3)
    begin(5)
    apply(5, (slice(0, 1), slice(0, D)), class_row, VECTOR_RATE)
    for at in range(0, PATCHES, 28):
        apply(
            5, (slice(1 + at, 29 + at), slice(0, D)), vec[at : at + 28, 0:D], VECTOR_RATE
        )
    finish(5)
    final = factor(0, FF + 3 * D, D)
    for at in range(0, CPAD, 512):
        grad_head[0:D, at : at + 512] = mm_tn(final, d_logits[:, at : at + 512])
    grad_head[D : D + 1, :] = head_bias
    begin(6)

    def head_rows(index):
        for part in range(3):
            rows = pl.ds(pl.multiple_of(index * 48 + part * 16, 16), 16)
            apply(6, (rows, slice(0, NCLS)), grad_head[rows, 0:NCLS], LEARNING_RATE)

    loop(D // 48, head_rows)
    apply(6, (slice(D, D + 1), slice(0, NCLS)), grad_head[D : D + 1, 0:NCLS], LEARNING_RATE)
    finish(6)
    own_rows = pl.multiple_of(shard * rows_in, 8)

    def keep_in(column, made):
        slot = column % 2
        passing[slot] = made
        last_in[:, column * D : (column + 1) * D] = passing[slot, pl.ds(own_rows, rows_in), :]

    h2 = factor(0, FF, D)
    for tile in range(4):
        made = mm_tn(h2, factor(1, tile * D, D))
        keep_in(4 + tile, made)
    for tile in range(2):
        last_in[:, (1 + tile) * D : (2 + tile) * D] = small[
            0, tile * rows_in : (tile + 1) * rows_in, :
        ].astype(F32)
    made = mm_tn(factor(0, FF + 2 * D, D), factor(1, FF + D, D))
    keep_in(0, made)
    made = mm_tn(factor(0, FF + D, D), factor(1, FF, D))
    keep_in(3, made)
    d_top = factor(0, FF + 4 * D, D)
    per = min(rows_down, D)
    for tile in range(4):
        made = mm_tn(factor(0, tile * D, D), d_top)
        for piece in range(D // per):
            owner, at = divmod(tile * D + piece * per, rows_down)

            def keep_down(made=made, piece=piece, at=at):
                last_down[at : at + per, :] = made[piece * per : (piece + 1) * per]

            pl.when(shard == owner)(keep_down)
    update_in(keep)
    update_down(keep)
    for array, layer in order:
        for move in moves(array, layer, out=True):
            move.wait()


def run_update(n_rep, n_shard, res, small, vec, squares, factors, arrays):
    whole = pl.BlockSpec(memory_space=pltpu.VMEM)
    there = pl.BlockSpec(memory_space=pl.ANY)
    one = jax.ShapeDtypeStruct((1, 1), F32)
    made = pl.pallas_call(
        functools.partial(update, n_rep, n_shard),
        out_shape=[one, one] + [jax.ShapeDtypeStruct(a.shape, F32) for a in arrays],
        in_specs=[there] * 2 + [whole] * 3 + [there] * 21,
        out_specs=[whole] * 2 + [there] * 21,
        scratch_shapes=[pltpu.VMEM(a.shape, F32) for a in (*arrays, *arrays)]
        + [
            pltpu.VMEM((D // n_shard, 4 * D + FF), F32),
            pltpu.VMEM((FF // n_shard, D), F32),
            pltpu.VMEM((2, D, D), F32),
            pltpu.VMEM((D + 8, CPAD), F32),
            pltpu.VMEM(res.shape, BF),
            pltpu.VMEM(small.shape, BF),
            pltpu.SemaphoreType.DMA((21, LAYERS)),
            pltpu.SemaphoreType.DMA((21, LAYERS)),
            pltpu.SemaphoreType.DMA((2,)),
        ],
        compiler_params=pltpu.CompilerParams(vmem_limit_bytes=62 * 1024 * 1024),
        cost_estimate=pl.CostEstimate(
            flops=200_000_000, bytes_accessed=50_000_000, transcendentals=4_000_000
        ),
        name="adamw",
    )(res, small, vec, squares, factors, *arrays)
    return made[0].reshape(()), made[1].reshape(()), made[2:]


def shards(
    n_rep, n_shard,
    patches, labels, counts, patch_w, layer_in, layer_down, layer_vecs, glob_vecs, pos_embed, head,
    m_patch, v_patch, m_in, v_in, m_down, v_down, m_vecs, v_vecs, m_glob, v_glob, m_pos, v_pos,
    m_head, v_head,
):
    ends = lax.pad(patches, BF(0), ((0, 0, 0), (-TAIL, BLK - PATCHES, 0), (0, 0, 0)))
    res, small, vec, squares, factors = run_train(
        n_rep, n_shard, patches, ends, labels, counts, patch_w, layer_in, layer_down, layer_vecs,
        glob_vecs, pos_embed, head,
    )
    arrays = [
        patch_w, m_patch, v_patch, layer_in, m_in, v_in, layer_down, m_down, v_down,
        layer_vecs, m_vecs, v_vecs, glob_vecs, m_glob, v_glob, pos_embed, m_pos, v_pos,
        head, m_head, v_head,
    ]
    loss, grad_norm, new = run_update(n_rep, n_shard, res, small, vec, squares, factors, arrays)
    return (loss, grad_norm, *new)


def solution(mesh):
    everywhere = P()
    rows = P("shard", None)
    middle = P(None, "shard", None)
    return jax.shard_map(
        functools.partial(shards, mesh.shape["rep"], mesh.shape["shard"]),
        mesh=mesh,
        in_specs=(
            P(("rep", "shard"), None, None),
            P(("rep", "shard")),
            P(("rep", "shard")),
            rows,
            middle,
            middle,
            *(everywhere,) * 4,
            *(rows,) * 2,
            *(middle,) * 4,
            *(everywhere,) * 8,
        ),
        out_specs=(
            *(everywhere,) * 2,
            *(rows,) * 3,
            *(middle,) * 6,
            *(everywhere,) * 12,
        ),
        check_vma=False,
    )
```
